32 devices in a mesh: section: 2 (over core), dp: 4 (over y, x), seq: 4 (over z).
Axes of the slice: x: 2, y: 2, z: 4, core: 2. Of those that a mesh axis runs over, the one named last changes fastest.
Arguments:
- block_input: bfloat16 [4, 4, 1024, 768], P(None, 'dp', 'seq'), may hold values from -6 to 6
- cotangent: bfloat16 [4, 4, 1024, 768], P(None, 'dp', 'seq'), may hold values from -6 to 6
- random_ids: int32 [4, 4, 16, 12, 3], P(None, 'dp'), may hold values from 0 to 15, as said below
- segment_ids: int32 [4, 4, 1024], P(None, 'dp'), may hold values from 0 to 2, as said below
- global_ids: int32 [4, 4, 2], P(None, 'dp'), may hold values from 0 to 15, as said below
- w_rows: float32 [2, 768, 6144], P('section', None, ('dp', 'seq'))
- w_rows_first: float32 [2, 768, 6144], P('section', None, ('dp', 'seq')), may hold values from -768 to 768
- w_rows_second: float32 [2, 768, 6144], P('section', None, ('dp', 'seq')), may hold values from 49152 to 196608
- w_down: float32 [2, 3072, 768], P('section', ('dp', 'seq')), may hold values from -0.109375 to 0.109375
- w_down_first: float32 [2, 3072, 768], P('section', ('dp', 'seq')), may hold values from -384 to 384
- w_down_second: float32 [2, 3072, 768], P('section', ('dp', 'seq')), may hold values from 1966.08 to 16384
- vectors: float32 [2, 9216], P('section', ('dp', 'seq'))
- vectors_first: float32 [2, 9216], P('section', ('dp', 'seq')), may hold values from -1536 to 1536
- vectors_second: float32 [2, 9216], P('section', ('dp', 'seq')), may hold values from 98304 to 589824
Outputs:
- section_result: float32 [2, 4, 4, 1024, 768], P('section', None, 'dp', 'seq')
- new_rows: float32 [2, 768, 6144], P('section', None, ('dp', 'seq'))
- new_rows_first: float32 [2, 768, 6144], P('section', None, ('dp', 'seq'))
- new_rows_second: float32 [2, 768, 6144], P('section', None, ('dp', 'seq'))
- new_down: float32 [2, 3072, 768], P('section', ('dp', 'seq'))
- new_down_first: float32 [2, 3072, 768], P('section', ('dp', 'seq'))
- new_down_second: float32 [2, 3072, 768], P('section', ('dp', 'seq'))
- new_vectors: float32 [2, 9216], P('section', ('dp', 'seq'))
- new_vectors_first: float32 [2, 9216], P('section', ('dp', 'seq'))
- new_vectors_second: float32 [2, 9216], P('section', ('dp', 'seq'))
The draws below stay inside these ranges and needn't reach their ends.
Inputs may be any that keep to these rules, and one draw needn't show every extreme that they name: `random_ids`: the 3 blocks of one query block and head are different. The 144 random blocks named by the 4 query blocks of one index of seq in a window (all heads and picks) lie at most 36 on any one index of seq, and exactly 36 on some index, in every window. `segment_ids`: segment numbers never fall along a window; segment 0 ends within the window's first 256 tokens and segment 2 begins within its last 256 tokens. `global_ids`: the 2 global blocks of a window are different.
All inputs are finite; a program needn't handle non-finite values.
Results may differ from the reference program's by a relative error of at most 0.011.
Values may be sent and summed in bfloat16 or wider, within the bound.
A program may use at most 512 MiB of HBM per device.

```python
import math
import jax
import jax.numpy as jnp
from jax import lax

D = 768
FF = 3072
HEADS = 12
HEAD_DIM = 64
BLOCK = 64
RAND = 3
GLOB = 2
MICRO = 4
STEP = 5
LENGTH = 1024
NB = 16
BLK_DEV = 4
REQ = 144
WINDOWS = 4
SUMMED = 16384
ROWCOLS = 6144
VEC = 9216


def draw_random_ids(key, part):
    key = jax.random.fold_in(key, 11)
    groups = NB // BLK_DEV
    count = MICRO * WINDOWS * groups
    order_keys = jax.random.split(jax.random.fold_in(key, 1), count)
    orders = jax.vmap(lambda single: jax.random.permutation(single, groups))(order_keys)
    positions = jnp.arange(REQ) % groups
    owners = orders[:, positions]
    inside = jax.random.randint(jax.random.fold_in(key, 2), (count, REQ), 0, BLK_DEV)
    chosen = owners * BLK_DEV + inside
    return chosen.reshape(MICRO, WINDOWS, NB, HEADS, RAND).astype(jnp.int32)


def draw_segment_ids(key, part):
    key = jax.random.fold_in(key, 12)
    device_tokens = BLK_DEV * BLOCK
    first_end = jax.random.randint(jax.random.fold_in(key, 1), (MICRO, WINDOWS, 1), 1, device_tokens)
    last_start = LENGTH - jax.random.randint(jax.random.fold_in(key, 2), (MICRO, WINDOWS, 1), 1, device_tokens)
    positions = jnp.arange(LENGTH)
    segments = (positions >= first_end).astype(jnp.int32) + (positions >= last_start).astype(jnp.int32)
    return segments.astype(jnp.int32)


def draw_global_ids(key, part):
    key = jax.random.fold_in(key, 13)
    columns = []
    for which in range(GLOB):
        lower = which * NB // GLOB
        upper = (which + 1) * NB // GLOB
        columns.append(jax.random.randint(jax.random.fold_in(key, which), (MICRO, WINDOWS), lower, upper))
    return jnp.stack(columns, axis=-1).astype(jnp.int32)


def draw_w_rows(key, part):
    key = jax.random.fold_in(key, 14)
    values = jax.random.normal(key, (2, D, 4 * D + FF), jnp.float32)
    column = jnp.arange(4 * D + FF)
    factor = jnp.where((column >= 3 * D) & (column < 4 * D), 4.0, 1.0) / math.sqrt(D)
    return values * factor


def draw_vectors(key, part):
    key = jax.random.fold_in(key, 15)
    values = jax.random.normal(key, (2, 8 * D + FF), jnp.float32)
    entry = jnp.arange(8 * D + FF)
    is_gain = (entry < D) | (entry >= 5 * D) & (entry < 6 * D)
    return jnp.where(is_gain, 1.0 + 0.1 * values, 0.2 * values)


def block_levels(rng, dims, cuts, least, largest):
    def one(dim, blocks):
        steps = jax.random.uniform(jax.random.fold_in(jax.random.fold_in(rng, 6), dim), (blocks,), jnp.float32, least / len(cuts), largest / len(cuts))
        return jnp.repeat(jnp.exp(steps), dims[dim] // blocks).reshape((-1,) + (1,) * (len(dims) - dim - 1))

    factor_of = one(*cuts[0])
    for cut in cuts[1:]:
        factor_of = factor_of * one(*cut)
    return factor_of


def bell_draw(rng, extent, scale, reach, shards=(), dtype=jnp.bfloat16):
    values = scale * jax.random.normal(rng, extent, jnp.float32)
    if shards:
        values = values * block_levels(rng, extent, shards, -0.22, 0.18)
    return jnp.clip(values, -reach, reach).astype(dtype)


def setup_inputs(seed: int = 0) -> dict:
    key_list = jax.random.split(jax.random.key(seed), 15)
    block_input = bell_draw(key_list[0], (MICRO, WINDOWS, LENGTH, D), 1.0, 6.0, ((1, 4), (2, 4)))
    cotangent = bell_draw(key_list[1], (MICRO, WINDOWS, LENGTH, D), 1.0, 6.0, ((1, 4), (2, 4)))
    random_ids = draw_random_ids(jax.random.fold_in(key_list[14], 71), 0)
    segment_ids = draw_segment_ids(jax.random.fold_in(key_list[14], 71), 0)
    global_ids = draw_global_ids(jax.random.fold_in(key_list[14], 71), 0)
    w_rows = draw_w_rows(jax.random.fold_in(key_list[14], 71), 0)
    w_rows_first = bell_draw(key_list[6], (2, D, ROWCOLS), (1.0 * SUMMED ** 0.5), 768.0, ((0, 2), (2, 16)), jnp.float32)
    w_rows_second = jnp.clip(jnp.exp(math.log(196608.0) - 1.3862944 * jax.random.uniform(key_list[7], (2, D, ROWCOLS), jnp.float32) ** block_levels(key_list[7], (2, D, ROWCOLS), ((0, 2), (2, 16)), -0.2, 0.2)), 49152.0, 196608.0)
    w_down = bell_draw(key_list[8], (2, FF, D), FF ** -0.5, 0.109375, ((0, 2), (1, 16)), jnp.float32)
    w_down_first = bell_draw(key_list[9], (2, FF, D), (0.5 * SUMMED ** 0.5), 384.0, ((0, 2), (1, 16)), jnp.float32)
    w_down_second = jnp.clip(jnp.exp(math.log(16384.0) - 2.1202636 * jax.random.uniform(key_list[10], (2, FF, D), jnp.float32) ** block_levels(key_list[10], (2, FF, D), ((0, 2), (1, 16)), -0.2, 0.2)), 1966.08, 16384.0)
    vectors = draw_vectors(jax.random.fold_in(key_list[14], 71), 0)
    vectors_first = bell_draw(key_list[12], (2, VEC), (2.0 * SUMMED ** 0.5), 1536.0, ((0, 2), (1, 16)), jnp.float32)
    vectors_second = jnp.clip(jnp.exp(math.log(589824.0) - 1.7917595 * jax.random.uniform(key_list[13], (2, VEC), jnp.float32) ** block_levels(key_list[13], (2, VEC), ((0, 2), (1, 16)), -0.2, 0.2)), 98304.0, 589824.0)
    return {"block_input": block_input, "cotangent": cotangent, "random_ids": random_ids, "segment_ids": segment_ids, "global_ids": global_ids, "w_rows": w_rows, "w_rows_first": w_rows_first, "w_rows_second": w_rows_second, "w_down": w_down, "w_down_first": w_down_first, "w_down_second": w_down_second, "vectors": vectors, "vectors_first": vectors_first, "vectors_second": vectors_second}


@jax.custom_vjp
def low(v):
    return lax.optimization_barrier(v.astype(jnp.bfloat16)).astype(jnp.float32)

@jax.custom_vjp
def low_back(v):
    return v

def low_keep(v):
    return (low(v), None)

def low_pass(kept, grad):
    return (grad,)

def back_keep(v):
    return (v, None)

def back_low(kept, grad):
    return (low(grad),)
low.defvjp(low_keep, low_pass)
low_back.defvjp(back_keep, back_low)
epsilon = 1e-05
masked = -1e+30
rate_matrix = 0.02
rate_vector = 0.2
decay_matrix = 0.01

def exact_two(form, left, right):
    return jnp.einsum(form, left, right, precision=lax.Precision.HIGHEST)

def norm_rows(values_in, gain_vec, shift_vec):
    row_mean = lax.optimization_barrier(jnp.mean(values_in, axis=-1, keepdims=True))
    centred = values_in - row_mean
    spread = lax.optimization_barrier(jnp.mean(centred * centred, axis=-1, keepdims=True))
    return centred * lax.rsqrt(spread + epsilon) * gain_vec + shift_vec

def attend(queries, key_part, value_part, random_rows, segments, global_rows):
    length = queries.shape[0]
    blocks = length // BLOCK
    query_blocks = queries.reshape(blocks, BLOCK, HEADS, HEAD_DIM)
    paired = jnp.concatenate([key_part.reshape(blocks, BLOCK, HEADS, HEAD_DIM), value_part.reshape(blocks, BLOCK, HEADS, HEAD_DIM)], axis=-1)
    padded = jnp.pad(paired, ((1, 1), (0, 0), (0, 0), (0, 0)))
    sliding = jnp.concatenate([padded[:-2], padded[1:-1], padded[2:]], axis=1)
    global_kv = paired[global_rows].reshape(GLOB * BLOCK, HEADS, 2 * HEAD_DIM)
    by_head = jnp.transpose(paired, (2, 0, 1, 3))
    far_kv = by_head[jnp.arange(HEADS)[None, :, None], random_rows]
    seg_blocks = segments.reshape(blocks, BLOCK)
    seg_pad = jnp.pad(seg_blocks, ((1, 1), (0, 0)), constant_values=-1)
    slide_seg = jnp.concatenate([seg_pad[:-2], seg_pad[1:-1], seg_pad[2:]], axis=1)
    global_seg = seg_blocks[global_rows].reshape(-1)
    far_seg = seg_blocks[random_rows].reshape(blocks, HEADS, -1)
    key_seg = jnp.concatenate([jnp.broadcast_to(slide_seg[:, None, :], (blocks, HEADS, slide_seg.shape[1])), jnp.broadcast_to(global_seg[None, None, :], (blocks, HEADS, global_seg.shape[0])), far_seg], axis=-1)
    key_mask = seg_blocks[:, None, :, None] == key_seg[:, :, None, :]
    raw_scores = jnp.concatenate([exact_two('bqhd,bkhd->bhqk', query_blocks, sliding[..., :HEAD_DIM]), exact_two('bqhd,khd->bhqk', query_blocks, global_kv[..., :HEAD_DIM]), exact_two('bqhd,bhrkd->bhqrk', query_blocks, far_kv[..., :HEAD_DIM]).reshape(blocks, HEADS, BLOCK, -1)], axis=-1)
    scores = low_back(HEAD_DIM ** (-0.5) * raw_scores)
    scores = jnp.where(key_mask, scores, masked)
    row_top = lax.optimization_barrier(jnp.max(scores, axis=-1, keepdims=True))
    weight = jnp.exp(scores - row_top)
    probabilities = low(weight / lax.optimization_barrier(jnp.sum(weight, axis=-1, keepdims=True)))
    near_keys = 3 * BLOCK
    global_keys = GLOB * BLOCK
    attended = exact_two('bhqk,bkhd->bqhd', probabilities[..., :near_keys], sliding[..., HEAD_DIM:])
    attended = attended + exact_two('bhqk,khd->bqhd', probabilities[..., near_keys:near_keys + global_keys], global_kv[..., HEAD_DIM:])
    far_probs = probabilities[..., near_keys + global_keys:].reshape(blocks, HEADS, BLOCK, RAND, BLOCK)
    attended = attended + exact_two('bhqrk,bhrkd->bqhd', far_probs, far_kv[..., HEAD_DIM:])
    global_queries = query_blocks[global_rows].reshape(GLOB * BLOCK, HEADS, HEAD_DIM)
    full_keys = key_part.reshape(length, HEADS, HEAD_DIM)
    full_values = value_part.reshape(length, HEADS, HEAD_DIM)
    full_scores = low_back(HEAD_DIM ** (-0.5) * exact_two('qhd,khd->hqk', global_queries, full_keys))
    full_mask = global_seg[:, None] == segments[None, :]
    full_scores = jnp.where(full_mask[None], full_scores, masked)
    full_top = lax.optimization_barrier(jnp.max(full_scores, axis=-1, keepdims=True))
    full_weight = jnp.exp(full_scores - full_top)
    full_probs = low(full_weight / lax.optimization_barrier(jnp.sum(full_weight, axis=-1, keepdims=True)))
    full_out = exact_two('hqk,khd->qhd', full_probs, full_values).reshape(GLOB, BLOCK, HEADS, HEAD_DIM)
    global_hot = (global_rows[:, None] == jnp.arange(blocks)[None, :]).astype(jnp.float32)
    placed = exact_two('gb,gqhd->bqhd', global_hot, full_out)
    is_global = lax.optimization_barrier(jnp.sum(global_hot, axis=0)) > 0
    attended = jnp.where(is_global[:, None, None, None], placed, attended)
    return attended.reshape(length, HEADS * HEAD_DIM)

def layer_apply(hidden, row_weights, down_weights, vector_weights, random_rows, segments, global_rows):
    row_weights = low(row_weights)
    down_weights = low(down_weights)
    vector_weights = low(vector_weights)
    pieces = [vector_weights[piece_index * D:(piece_index + 1) * D] for piece_index in range(8)]
    gain_one, shift_one, bias_query, bias_value, bias_out, gain_two, shift_two, bias_down = pieces
    bias_up = vector_weights[8 * D:]
    normed = low(norm_rows(hidden, gain_one, shift_one))
    projected = jnp.dot(normed, row_weights[:, :3 * D], precision=lax.Precision.HIGHEST)
    projected = projected + jnp.concatenate([bias_query, jnp.zeros_like(bias_query), bias_value])
    projected = low_back(low(projected))
    attended = attend(projected[:, :D], projected[:, D:2 * D], projected[:, 2 * D:], random_rows, segments, global_rows)
    attended = low_back(low(attended))
    branch = low_back(jnp.dot(attended, row_weights[:, 3 * D:4 * D], precision=lax.Precision.HIGHEST) + bias_out)
    middle = hidden + branch
    normed_two = low(norm_rows(middle, gain_two, shift_two))
    up_value = low_back(jnp.dot(normed_two, row_weights[:, 4 * D:], precision=lax.Precision.HIGHEST) + bias_up)
    active = low(jax.nn.gelu(up_value, approximate=False))
    return middle + low_back(jnp.dot(active, down_weights, precision=lax.Precision.HIGHEST) + bias_down)

def adam_update(master, first_old, second_old, gradient, step_rate, decay_rate):
    first_new = 0.5 * first_old + 0.5 * gradient
    second_new = 0.5 * second_old + 0.5 * gradient * gradient
    first_hat = first_new / (1.0 - 0.5 ** STEP)
    second_hat = second_new / (1.0 - 0.5 ** STEP)
    master_new = master - step_rate * (first_hat / (jnp.sqrt(second_hat) + 1e-08) + decay_rate * master)
    return (master_new, first_new, second_new)

def reference(block_input, cotangent, random_ids, segment_ids, global_ids, w_rows, w_rows_first, w_rows_second, w_down, w_down_first, w_down_second, vectors, vectors_first, vectors_second):
    masters = (w_rows, w_down, vectors)
    count = MICRO * WINDOWS
    inputs = block_input.reshape(count, LENGTH, D).astype(jnp.float32)
    backs = cotangent.reshape(count, LENGTH, D).astype(jnp.float32)
    randoms = random_ids.reshape(count, NB, HEADS, RAND)
    segments_all = segment_ids.reshape(count, LENGTH)
    globals_all = global_ids.reshape(count, GLOB)

    def one_window(totals, window_items):
        hidden, back_grad, random_rows, segments, global_rows = window_items

        def two_layers(params, values_in):
            for section_index in range(2):
                values_in = layer_apply(values_in, params[0][section_index], params[1][section_index], params[2][section_index], random_rows, segments, global_rows)
                if section_index == 0:
                    values_in = low_back(low(values_in))
            return values_in
        output, pullback = jax.vjp(two_layers, masters, hidden)
        gradients, grad_input = pullback(back_grad)
        totals = jax.tree.map(lambda left, right: left + right, totals, gradients)
        return (totals, (output, grad_input))
    zero_grads = jax.tree.map(jnp.zeros_like, masters)
    totals, (outputs, grad_inputs) = lax.scan(one_window, zero_grads, (inputs, backs, randoms, segments_all, globals_all))
    section_result = jnp.stack([grad_inputs.reshape(MICRO, WINDOWS, LENGTH, D), outputs.reshape(MICRO, WINDOWS, LENGTH, D)])
    new_rows, new_rows_first, new_rows_second = adam_update(w_rows, w_rows_first, w_rows_second, totals[0], rate_matrix, decay_matrix)
    new_down, new_down_first, new_down_second = adam_update(w_down, w_down_first, w_down_second, totals[1], rate_matrix, decay_matrix)
    new_vectors, new_vectors_first, new_vectors_second = adam_update(vectors, vectors_first, vectors_second, totals[2], rate_vector, 0.0)
    return (section_result, new_rows, new_rows_first, new_rows_second, new_down, new_down_first, new_down_second, new_vectors, new_vectors_first, new_vectors_second)
```

```python
import math
from functools import partial

import jax
import jax.numpy as jnp
import ml_dtypes
import numpy as np
from jax import lax
from jax.experimental import pallas as pl
from jax.experimental.pallas import tpu as pltpu
from jax.sharding import PartitionSpec as P

HEADS = 12
BLOCK = 64
STEP = 5


epsilon = 1e-05
masked = -1e30
rate_matrix = 0.02
rate_vector = 0.2
decay_matrix = 0.01


def with_halo(x, sides, width):
    for axis, dim in sides:
        devices, length = (lax.axis_size(axis), x.shape[dim])
        up = [(i, (i + 1) % devices) for i in range(devices - 1)]
        down = [(j, i) for i, j in up]
        last = lax.slice_in_dim(x, length - width, length, axis=dim)
        initial = lax.slice_in_dim(x, 0, width, axis=dim)
        before = lax.ppermute(last, axis, up)
        after = lax.ppermute(initial, axis, down)
        x = jnp.concatenate([before, x, after], axis=dim)
    return x


def merged(value, axis, join):
    pieces = jax.tree.map(lambda part: lax.all_gather(part, axis), value)
    head = jax.tree.map(lambda part: part[0], pieces)
    tail = jax.tree.map(lambda part: part[1:], pieces)
    subtotal, _ = lax.scan(lambda subtotal, share: (join(subtotal, share), None), head, tail)
    return subtotal


def from_behind(x, axis, by):
    devices = lax.axis_size(axis)
    pairs = [(i, i + by) for i in range(devices) if 0 <= i + by < devices]
    return lax.ppermute(x, axis, pairs)


def partner(value, axis, bit):
    mask = 2**bit
    pairs = [(source, source ^ mask) for source in range(lax.axis_size(axis))]
    return lax.ppermute(value, axis, pairs)


def mixed_sum(form, left, right):
    return jnp.einsum(form, left, right, preferred_element_type=jnp.float32)


def exact_two(form, left, right):
    return jnp.einsum(
        form, left, right, precision=lax.Precision.HIGHEST, preferred_element_type=jnp.float32
    )


def norm_rows(values_in, gain_vec, shift_vec):
    row_mean = jnp.mean(values_in, axis=-1, keepdims=True)
    centred = values_in - row_mean
    spread = jnp.mean(centred * centred, axis=-1, keepdims=True)
    return centred * lax.rsqrt(spread + epsilon) * gain_vec + shift_vec


def split_vectors(vector_weights, model_width):
    pieces = [
        vector_weights[piece_index * model_width : (piece_index + 1) * model_width]
        for piece_index in range(8)
    ]
    return pieces + [vector_weights[8 * model_width :]]


def route_tables(random_rows, segments, global_rows, seq_place, groups):
    windows, blocks, head_count, pick_count = random_rows.shape
    blocks_dev = blocks // groups
    request_count = blocks_dev * head_count * pick_count
    capacity = -(-request_count // groups)
    requests = random_rows.reshape(windows, groups, request_count)
    owners = requests // blocks_dev
    inside = requests % blocks_dev
    head_of = jnp.arange(request_count) // pick_count % head_count
    is_mine = owners == seq_place
    slot_index = jnp.cumsum(is_mine.astype(jnp.int32), axis=2) - 1
    slot_hot = ((slot_index[..., None] == jnp.arange(capacity)) & is_mine[..., None]).astype(
        jnp.float32
    )
    inside_hot = (inside[..., None] == jnp.arange(blocks_dev)).astype(jnp.float32)
    head_hot = (head_of[:, None] == jnp.arange(head_count)).astype(jnp.float32)
    sender = jnp.einsum(
        "wqsc,wqsb,sh->wqcbh", slot_hot, inside_hot, head_hot, precision=lax.Precision.HIGHEST
    )
    my_owners = lax.dynamic_index_in_dim(owners, seq_place, axis=1, keepdims=False)
    earlier = jnp.arange(request_count)[None, :] < jnp.arange(request_count)[:, None]
    same_owner = my_owners[:, :, None] == my_owners[:, None, :]
    rank_index = jnp.sum((same_owner & earlier[None]).astype(jnp.int32), axis=2)
    picker = (
        (my_owners[..., None, None] == jnp.arange(groups)[:, None])
        & (rank_index[..., None, None] == jnp.arange(capacity)[None, :])
    ).astype(jnp.float32)
    first_block = seq_place * blocks_dev
    owned_hot = (global_rows[:, :, None] == first_block + jnp.arange(blocks_dev)).astype(
        jnp.float32
    )
    length = segments.shape[1]
    block_len = length // blocks
    seg_blocks = segments.reshape(windows, blocks, block_len)
    seg_pad = jnp.pad(seg_blocks, ((0, 0), (1, 1), (0, 0)), constant_values=-1)
    near_segs = lax.dynamic_slice_in_dim(seg_pad, first_block, blocks_dev + 2, axis=1)
    slide_seg = jnp.concatenate([near_segs[:, :-2], near_segs[:, 1:-1], near_segs[:, 2:]], axis=2)
    query_seg = near_segs[:, 1:-1]
    rows_index = jnp.arange(windows)
    global_seg = seg_blocks[rows_index[:, None], global_rows].reshape(windows, -1)
    chosen = lax.dynamic_slice_in_dim(random_rows, first_block, blocks_dev, axis=1)
    far_seg = seg_blocks[rows_index[:, None, None, None], chosen].reshape(
        windows, blocks_dev, head_count, -1
    )
    key_seg = jnp.concatenate(
        [
            jnp.broadcast_to(
                slide_seg[:, :, None, :], (windows, blocks_dev, head_count, slide_seg.shape[2])
            ),
            jnp.broadcast_to(
                global_seg[:, None, None, :], (windows, blocks_dev, head_count, global_seg.shape[1])
            ),
            far_seg,
        ],
        axis=3,
    )
    key_mask = query_seg[:, :, None, :, None] == key_seg[:, :, :, None, :]
    local_seg = query_seg.reshape(windows, -1)
    full_mask = global_seg[:, None, :, None] == local_seg[:, None, None, :]
    return (sender, picker, owned_hot, key_mask, full_mask)


def fetch_blocks(paired, queries, sender, picker, owned_hot):
    windows, tokens, head_count, doubled = paired.shape
    head_dim = queries.shape[-1]
    blocks_dev = tokens // BLOCK
    flattened = paired.reshape(windows, tokens, head_count * doubled)
    padded = with_halo(flattened, (("seq", 1),), BLOCK)
    framed = padded.reshape(windows, blocks_dev + 2, BLOCK, head_count, doubled)
    sliding = jnp.concatenate([framed[:, :-2], framed[:, 1:-1], framed[:, 2:]], axis=2)
    local_blocks = paired.reshape(windows, blocks_dev, BLOCK, head_count, doubled)
    owned_low = owned_hot.astype(jnp.bfloat16)
    offered = mixed_sum("wgb,wbthe->wgthe", owned_low, local_blocks)
    offered_queries = mixed_sum("wgb,wbqhd->wgqhd", owned_low, queries)
    global_kv, global_queries = (
        lax.psum(offered.astype(jnp.bfloat16), "seq").astype(jnp.float32),
        lax.psum(offered_queries.astype(jnp.bfloat16), "seq").astype(jnp.float32),
    )
    global_kv = global_kv.astype(jnp.bfloat16).reshape(windows, -1, head_count, doubled)
    global_queries = global_queries.astype(jnp.bfloat16).reshape(windows, -1, head_count, head_dim)
    outgoing = mixed_sum("wqcbh,wbthe->qwcte", sender.astype(jnp.bfloat16), local_blocks).astype(
        jnp.bfloat16
    )
    incoming = lax.all_to_all(outgoing, "seq", split_axis=0, concat_axis=0, tiled=True)
    distant = mixed_sum("wspc,pwcte->wste", picker.astype(jnp.bfloat16), incoming).astype(
        jnp.bfloat16
    )
    pick_count = picker.shape[1] // (blocks_dev * head_count)
    distant = distant.reshape(windows, blocks_dev, head_count, pick_count, BLOCK, doubled)
    return (sliding, global_kv, distant, global_queries)


def combine_stats(earlier, later):
    top = jnp.maximum(earlier[0], later[0])
    return (top, earlier[1] * jnp.exp(earlier[0] - top) + later[1] * jnp.exp(later[0] - top))


def full_forward(global_queries, key_part, value_part, full_mask, head_dim):
    scores = mixed_sum("wqhd,wkhd->whqk", global_queries, key_part) * head_dim ** (-0.5)
    scores = jnp.where(full_mask, scores, masked)
    local_top = jnp.max(scores, axis=3, keepdims=True)
    local_sum = jnp.sum(
        jnp.where(full_mask, jnp.exp(scores - local_top), 0.0), axis=3, keepdims=True
    )
    row_top, row_sum = merged((local_top, local_sum), "seq", combine_stats)
    full_probs = jnp.where(full_mask, jnp.exp(scores - row_top), 0.0) / row_sum
    partial_out = mixed_sum("whqk,wkhd->wqhd", full_probs.astype(jnp.bfloat16), value_part)
    full_out = lax.psum(partial_out.astype(jnp.bfloat16), "seq").astype(jnp.float32)
    return (full_out, full_probs)


def attention_weights(queries, sliding, global_kv, distant, key_mask):
    head_dim = queries.shape[-1]
    windows, blocks_dev, _, head_count, _ = queries.shape
    near_scores = mixed_sum("wbqhd,wbkhd->wbhqk", queries, sliding[..., :head_dim])
    global_scores = mixed_sum("wbqhd,wkhd->wbhqk", queries, global_kv[..., :head_dim])
    far_scores = mixed_sum("wbqhd,wbhrkd->wbhqrk", queries, distant[..., :head_dim])
    far_scores = far_scores.reshape(windows, blocks_dev, head_count, BLOCK, -1)
    scores = jnp.concatenate([near_scores, global_scores, far_scores], axis=4) * head_dim ** (-0.5)
    scores = jnp.where(key_mask, scores, masked)
    row_top = jnp.max(scores, axis=4, keepdims=True)
    weight = jnp.exp(scores - row_top)
    return weight / jnp.sum(weight, axis=4, keepdims=True)


def split_keys(scores_like, sliding, global_kv, distant):
    near_keys = sliding.shape[2]
    global_keys = global_kv.shape[1]
    windows, blocks_dev, head_count, pick_count, _, _ = distant.shape
    near_part = scores_like[..., :near_keys]
    global_part = scores_like[..., near_keys : near_keys + global_keys]
    far_part = scores_like[..., near_keys + global_keys :].reshape(
        windows, blocks_dev, head_count, BLOCK, pick_count, BLOCK
    )
    return (near_part, global_part, far_part)


def attention_values(low_probs, sliding, global_kv, distant, head_dim):
    near_part, global_part, far_part = split_keys(low_probs, sliding, global_kv, distant)
    attended = mixed_sum("wbhqk,wbkhd->wbqhd", near_part, sliding[..., head_dim:])
    attended = attended + mixed_sum("wbhqk,wkhd->wbqhd", global_part, global_kv[..., head_dim:])
    return attended + mixed_sum("wbhqrk,wbhrkd->wbqhd", far_part, distant[..., head_dim:])


def layer_forward(hidden, weights, tables):
    row_weights, down_weights, vector_weights = weights
    sender, picker, owned_hot, key_mask, full_mask = tables
    model_width = row_weights.shape[0]
    windows, tokens, _ = hidden.shape
    blocks_dev = tokens // BLOCK
    head_dim = model_width // HEADS
    (
        gain_one,
        shift_one,
        bias_query,
        bias_value,
        bias_out,
        gain_two,
        shift_two,
        bias_down,
        bias_up,
    ) = split_vectors(vector_weights, model_width)
    normed = norm_rows(hidden, gain_one, shift_one).astype(jnp.bfloat16)
    projected = mixed_sum("wtd,de->wte", normed, row_weights[:, : 3 * model_width])
    projected = (
        projected + jnp.concatenate([bias_query, jnp.zeros_like(bias_query), bias_value])
    ).astype(jnp.bfloat16)
    queries = projected[..., :model_width].reshape(windows, blocks_dev, BLOCK, HEADS, head_dim)
    key_part = projected[..., model_width : 2 * model_width].reshape(
        windows, tokens, HEADS, head_dim
    )
    value_part = projected[..., 2 * model_width :].reshape(windows, tokens, HEADS, head_dim)
    paired = jnp.concatenate([key_part, value_part], axis=3)
    sliding, global_kv, distant, global_queries = fetch_blocks(
        paired, queries, sender, picker, owned_hot
    )
    probabilities = attention_weights(queries, sliding, global_kv, distant, key_mask)
    attended = attention_values(
        probabilities.astype(jnp.bfloat16), sliding, global_kv, distant, head_dim
    )
    full_out, full_probs = full_forward(global_queries, key_part, value_part, full_mask, head_dim)
    placed = exact_two(
        "wgb,wgqhd->wbqhd", owned_hot, full_out.reshape(windows, -1, BLOCK, HEADS, head_dim)
    )
    on_global = jnp.sum(owned_hot, axis=1)[:, :, None, None, None] > 0
    attended = jnp.where(on_global, placed, attended)
    mixed_low = attended.reshape(windows, tokens, model_width).astype(jnp.bfloat16)
    middle = (
        hidden
        + mixed_sum("wtd,de->wte", mixed_low, row_weights[:, 3 * model_width : 4 * model_width])
        + bias_out
    )
    normed_two = norm_rows(middle, gain_two, shift_two).astype(jnp.bfloat16)
    up_value = mixed_sum("wtd,df->wtf", normed_two, row_weights[:, 4 * model_width :]) + bias_up
    active = jax.nn.gelu(up_value, approximate=False).astype(jnp.bfloat16)
    output = middle + mixed_sum("wtf,fd->wtd", active, down_weights) + bias_down
    stored = (
        hidden,
        normed,
        queries,
        sliding,
        global_kv,
        distant,
        probabilities,
        mixed_low,
        middle,
        normed_two,
        up_value,
        active,
        key_part,
        value_part,
        global_queries,
        full_probs,
    )
    return (output, stored)


def return_blocks(near_back, global_back, far_back, query_part, sender, picker, owned_hot):
    windows, blocks_dev, _, head_count, doubled = near_back.shape
    first_third = near_back[:, :, :BLOCK]
    centre_third = near_back[:, :, BLOCK : 2 * BLOCK]
    last_third = near_back[:, :, 2 * BLOCK :]
    framed = jnp.pad(first_third, ((0, 0), (0, 2), (0, 0), (0, 0), (0, 0)))
    framed = framed + jnp.pad(centre_third, ((0, 0), (1, 1), (0, 0), (0, 0), (0, 0)))
    framed = framed + jnp.pad(last_third, ((0, 0), (2, 0), (0, 0), (0, 0), (0, 0)))
    own_grad = framed[:, 1:-1]
    for direction in (1, -1):
        rim_grad = framed[:, -1] if direction == 1 else framed[:, 0]
        arrived = from_behind(rim_grad.astype(jnp.bfloat16), "seq", direction).astype(
            rim_grad.dtype
        )
        if direction == 1:
            own_grad = jnp.concatenate(
                [own_grad[:, :1] + arrived[:, None], own_grad[:, 1:]], axis=1
            )
        else:
            own_grad = jnp.concatenate(
                [own_grad[:, :-1], own_grad[:, -1:] + arrived[:, None]], axis=1
            )
    global_total, query_total = (
        lax.psum(
            global_back.reshape(windows, -1, BLOCK, head_count, doubled).astype(jnp.bfloat16), "seq"
        ).astype(jnp.float32),
        lax.psum(query_part.astype(jnp.bfloat16), "seq").astype(jnp.float32),
    )
    own_grad = own_grad + exact_two("wgb,wgthe->wbthe", owned_hot, global_total)
    far_flat = far_back.reshape(windows, -1, BLOCK, doubled)
    returning = exact_two("wspc,wste->pwcte", picker, far_flat)
    arrived_far = lax.all_to_all(
        returning.astype(jnp.bfloat16), "seq", split_axis=0, concat_axis=0, tiled=True
    ).astype(returning.dtype)
    own_grad = own_grad + exact_two("wqcbh,qwcte->wbthe", sender, arrived_far)
    return (own_grad.reshape(windows, blocks_dev * BLOCK, head_count, doubled), query_total)


def attention_back(
    grad_attended,
    queries,
    sliding,
    global_kv,
    distant,
    probabilities,
    key_part,
    value_part,
    global_queries,
    full_probs,
    sender,
    picker,
    owned_hot,
):
    head_dim = queries.shape[-1]
    score_scale = head_dim ** (-0.5)
    windows, blocks_dev, _, head_count, _ = queries.shape
    on_global = jnp.sum(owned_hot, axis=1)[:, :, None, None, None] > 0
    selected = mixed_sum("wgb,wbqhd->wgqhd", owned_hot.astype(jnp.bfloat16), grad_attended)
    rows_grad = lax.psum(selected.astype(jnp.bfloat16), "seq").reshape(
        windows, -1, head_count, head_dim
    )
    grad_attended = jnp.where(on_global, jnp.zeros_like(grad_attended), grad_attended)
    low_probs = probabilities.astype(jnp.bfloat16)
    near_grad = mixed_sum("wbqhd,wbkhd->wbhqk", grad_attended, sliding[..., head_dim:])
    global_grad = mixed_sum("wbqhd,wkhd->wbhqk", grad_attended, global_kv[..., head_dim:])
    far_grad = mixed_sum("wbqhd,wbhrkd->wbhqrk", grad_attended, distant[..., head_dim:])
    far_grad = far_grad.reshape(windows, blocks_dev, head_count, BLOCK, -1)
    grad_probs = jnp.concatenate([near_grad, global_grad, far_grad], axis=4)
    grad_scores = probabilities * (
        grad_probs - jnp.sum(probabilities * grad_probs, axis=4, keepdims=True)
    )
    grad_scores = grad_scores.astype(jnp.bfloat16)
    near_split, global_split, far_split = split_keys(grad_scores, sliding, global_kv, distant)
    near_probs, global_probs, far_probs = split_keys(low_probs, sliding, global_kv, distant)
    grad_query = mixed_sum("wbhqk,wbkhd->wbqhd", near_split, sliding[..., :head_dim])
    grad_query = grad_query + mixed_sum(
        "wbhqk,wkhd->wbqhd", global_split, global_kv[..., :head_dim]
    )
    grad_query = (
        grad_query + mixed_sum("wbhqrk,wbhrkd->wbqhd", far_split, distant[..., :head_dim])
    ) * score_scale
    near_back = jnp.concatenate(
        [
            mixed_sum("wbhqk,wbqhd->wbkhd", near_split, queries) * score_scale,
            mixed_sum("wbhqk,wbqhd->wbkhd", near_probs, grad_attended),
        ],
        axis=4,
    )
    global_back = jnp.concatenate(
        [
            mixed_sum("wbhqk,wbqhd->wkhd", global_split, queries) * score_scale,
            mixed_sum("wbhqk,wbqhd->wkhd", global_probs, grad_attended),
        ],
        axis=3,
    )
    far_back = jnp.concatenate(
        [
            mixed_sum("wbhqrk,wbqhd->wbhrkd", far_split, queries) * score_scale,
            mixed_sum("wbhqrk,wbqhd->wbhrkd", far_probs, grad_attended),
        ],
        axis=5,
    )
    full_grad_probs = mixed_sum("wqhd,wkhd->whqk", rows_grad, value_part)
    partial_dot = jnp.sum(full_probs * full_grad_probs, axis=3, keepdims=True)
    row_dot = lax.psum(partial_dot, "seq")
    full_grad_scores = (full_probs * (full_grad_probs - row_dot)).astype(jnp.bfloat16)
    query_part = mixed_sum("whqk,wkhd->wqhd", full_grad_scores, key_part) * score_scale
    full_key_grad = mixed_sum("whqk,wqhd->wkhd", full_grad_scores, global_queries) * score_scale
    full_value_grad = mixed_sum("whqk,wqhd->wkhd", full_probs.astype(jnp.bfloat16), rows_grad)
    grad_paired, query_total = return_blocks(
        near_back, global_back, far_back, query_part, sender, picker, owned_hot
    )
    grad_query = grad_query + exact_two(
        "wgb,wgqhd->wbqhd", owned_hot, query_total.reshape(windows, -1, BLOCK, head_count, head_dim)
    )
    grad_paired = grad_paired + jnp.concatenate([full_key_grad, full_value_grad], axis=3)
    return (grad_query, grad_paired)


def layer_backward(stored, grad_output, weights, tables):
    row_weights, down_weights, vector_weights = weights
    sender, picker, owned_hot, key_mask, full_mask = tables
    (
        hidden,
        normed,
        queries,
        sliding,
        global_kv,
        distant,
        probabilities,
        mixed_low,
        middle,
        normed_two,
        up_value,
        active,
        key_part,
        value_part,
        global_queries,
        full_probs,
    ) = stored
    model_width = row_weights.shape[0]
    windows, tokens, _ = hidden.shape
    blocks_dev = tokens // BLOCK
    head_dim = model_width // HEADS
    (
        gain_one,
        shift_one,
        bias_query,
        bias_value,
        bias_out,
        gain_two,
        shift_two,
        bias_down,
        bias_up,
    ) = split_vectors(vector_weights, model_width)
    grad_ffn = grad_output.astype(jnp.bfloat16)
    grad_bias_down = jnp.sum(grad_ffn.astype(jnp.float32), axis=(0, 1))
    grad_down = mixed_sum("wtf,wtd->fd", active, grad_ffn)
    grad_active = mixed_sum("wtd,fd->wtf", grad_ffn, down_weights)
    gelu_pull = jax.vjp(partial(jax.nn.gelu, approximate=False), up_value)[1]
    grad_up = gelu_pull(grad_active)[0].astype(jnp.bfloat16)
    grad_bias_up = jnp.sum(grad_up.astype(jnp.float32), axis=(0, 1))
    grad_in = mixed_sum("wtd,wtf->df", normed_two, grad_up)
    grad_normed_two = mixed_sum("wtf,df->wtd", grad_up, row_weights[:, 4 * model_width :])
    norm_pull_two = jax.vjp(norm_rows, middle, gain_two, shift_two)[1]
    grad_middle_norm, grad_gain_two, grad_shift_two = norm_pull_two(grad_normed_two)
    grad_middle = grad_output + grad_middle_norm
    grad_branch = grad_middle.astype(jnp.bfloat16)
    grad_bias_out = jnp.sum(grad_branch.astype(jnp.float32), axis=(0, 1))
    grad_out_weight = mixed_sum("wtd,wte->de", mixed_low, grad_branch)
    grad_attended = mixed_sum(
        "wte,de->wtd", grad_branch, row_weights[:, 3 * model_width : 4 * model_width]
    ).astype(jnp.bfloat16)
    grad_attended = grad_attended.reshape(windows, blocks_dev, BLOCK, HEADS, head_dim)
    grad_query, grad_paired = attention_back(
        grad_attended,
        queries,
        sliding,
        global_kv,
        distant,
        probabilities,
        key_part,
        value_part,
        global_queries,
        full_probs,
        sender,
        picker,
        owned_hot,
    )
    grad_projected = jnp.concatenate(
        [
            grad_query.reshape(windows, tokens, model_width),
            grad_paired[..., :head_dim].reshape(windows, tokens, model_width),
            grad_paired[..., head_dim:].reshape(windows, tokens, model_width),
        ],
        axis=2,
    ).astype(jnp.bfloat16)
    summed = jnp.sum(grad_projected.astype(jnp.float32), axis=(0, 1))
    grad_bias_query = summed[:model_width]
    grad_bias_value = summed[2 * model_width :]
    grad_projection = mixed_sum("wtd,wte->de", normed, grad_projected)
    grad_normed = mixed_sum("wte,de->wtd", grad_projected, row_weights[:, : 3 * model_width])
    norm_pull_one = jax.vjp(norm_rows, hidden, gain_one, shift_one)[1]
    grad_hidden_norm, grad_gain_one, grad_shift_one = norm_pull_one(grad_normed)
    grad_hidden = grad_middle + grad_hidden_norm
    grad_rows = jnp.concatenate([grad_projection, grad_out_weight, grad_in], axis=1)
    grad_vectors = jnp.concatenate(
        [
            grad_gain_one,
            grad_shift_one,
            grad_bias_query,
            grad_bias_value,
            grad_bias_out,
            grad_gain_two,
            grad_shift_two,
            grad_bias_down,
            grad_bias_up,
        ]
    )
    return (grad_hidden, (grad_rows, grad_down, grad_vectors))


def adam_update(master, first_old, second_old, gradient, step_rate, decay_rate):
    first_new = 0.5 * first_old + 0.5 * gradient
    second_new = 0.5 * second_old + 0.5 * gradient * gradient
    first_hat = first_new / (1.0 - 0.5**STEP)
    second_hat = second_new / (1.0 - 0.5**STEP)
    master_new = master - step_rate * (
        first_hat / (jnp.sqrt(second_hat) + 1e-08) + decay_rate * master
    )
    return (master_new, first_new, second_new)


def general_shards(
    block_input,
    cotangent,
    random_ids,
    segment_ids,
    global_ids,
    w_rows,
    w_rows_first,
    w_rows_second,
    w_down,
    w_down_first,
    w_down_second,
    vectors,
    vectors_first,
    vectors_second,
):
    section_index = lax.axis_index("section")
    seq_place = lax.axis_index("seq")
    groups = lax.axis_size("seq")
    row_weights, down_weights, vector_low = (
        lax.all_gather(w_rows[0].astype(jnp.bfloat16), ("dp", "seq"), axis=1, tiled=True),
        lax.all_gather(w_down[0].astype(jnp.bfloat16), ("dp", "seq"), axis=0, tiled=True),
        lax.all_gather(vectors[0].astype(jnp.bfloat16), ("dp", "seq"), axis=0, tiled=True),
    )
    weights = (row_weights, down_weights, vector_low.astype(jnp.float32))
    micro_count, windows, tokens, model_width = block_input.shape
    received = jnp.zeros((windows, tokens, model_width), jnp.bfloat16)
    results = jnp.zeros(block_input.shape, jnp.float32)
    full_totals = (
        jnp.zeros(row_weights.shape, jnp.float32),
        jnp.zeros(down_weights.shape, jnp.float32),
        jnp.zeros(vector_low.shape, jnp.float32),
    )

    def tick(tick_index, carry):
        received, results, full_totals = carry
        forward_mb = jnp.clip(tick_index - section_index, 0, micro_count - 1)
        behind_raw = tick_index - 2 + section_index
        behind = jnp.clip(behind_raw, 0, micro_count - 1)
        live_mask = ((behind_raw >= 0) & (behind_raw < micro_count)).astype(jnp.float32)
        tables_forward = route_tables(
            lax.dynamic_index_in_dim(random_ids, forward_mb, 0, keepdims=False),
            lax.dynamic_index_in_dim(segment_ids, forward_mb, 0, keepdims=False),
            lax.dynamic_index_in_dim(global_ids, forward_mb, 0, keepdims=False),
            seq_place,
            groups,
        )
        tables_behind = route_tables(
            lax.dynamic_index_in_dim(random_ids, behind, 0, keepdims=False),
            lax.dynamic_index_in_dim(segment_ids, behind, 0, keepdims=False),
            lax.dynamic_index_in_dim(global_ids, behind, 0, keepdims=False),
            seq_place,
            groups,
        )
        incoming_values = received.astype(jnp.float32)
        first_input = lax.dynamic_index_in_dim(block_input, forward_mb, 0, keepdims=False).astype(
            jnp.float32
        )
        forward_input = jnp.where(section_index == 0, first_input, incoming_values)
        forward_output = layer_forward(forward_input, weights, tables_forward)[0]
        back_source = lax.dynamic_index_in_dim(block_input, behind, 0, keepdims=False).astype(
            jnp.float32
        )
        back_input = jnp.where(section_index == 0, back_source, incoming_values)
        given_grad = lax.dynamic_index_in_dim(cotangent, behind, 0, keepdims=False).astype(
            jnp.float32
        )
        back_grad = jnp.where(section_index == 0, incoming_values, given_grad) * live_mask
        stored = layer_forward(back_input, weights, tables_behind)[1]
        grad_input, gradients = layer_backward(stored, back_grad, weights, tables_behind)
        outgoing = jnp.where(section_index == 0, forward_output, grad_input).astype(jnp.bfloat16)
        finished = jnp.where(section_index == 0, grad_input, forward_output)
        updated = lax.dynamic_update_index_in_dim(results, finished, behind, 0)
        results = jnp.where(live_mask > 0, updated, results)
        full_totals = tuple(
            (total_part + grad_part for total_part, grad_part in zip(full_totals, gradients))
        )
        return (partner(outgoing, "section", 0), results, full_totals)

    received, results, full_totals = lax.fori_loop(
        0, micro_count + 2, tick, (received, results, full_totals)
    )
    shard_totals = (
        lax.psum_scatter(full_totals[0], ("dp", "seq"), scatter_dimension=1, tiled=True),
        lax.psum_scatter(full_totals[1], ("dp", "seq"), scatter_dimension=0, tiled=True),
        lax.psum_scatter(full_totals[2], ("dp", "seq"), scatter_dimension=0, tiled=True),
    )
    new_rows, new_rows_first, new_rows_second = adam_update(
        w_rows[0], w_rows_first[0], w_rows_second[0], shard_totals[0], rate_matrix, decay_matrix
    )
    new_down, new_down_first, new_down_second = adam_update(
        w_down[0], w_down_first[0], w_down_second[0], shard_totals[1], rate_matrix, decay_matrix
    )
    new_vectors, new_vectors_first, new_vectors_second = adam_update(
        vectors[0], vectors_first[0], vectors_second[0], shard_totals[2], rate_vector, 0.0
    )
    return (
        results[None],
        new_rows[None],
        new_rows_first[None],
        new_rows_second[None],
        new_down[None],
        new_down_first[None],
        new_down_second[None],
        new_vectors[None],
        new_vectors_first[None],
        new_vectors_second[None],
    )


LOW = jnp.bfloat16
LOG_HIGH = [float(np.log(c).astype(ml_dtypes.bfloat16)) for c in (1.0, 2.0, 3.0)]
LOG_LOW = [float(np.log(c)) - high for c, high in zip((1.0, 2.0, 3.0), LOG_HIGH)]
CHUNK = 256
VMEM_BYTES = 48 * 1024 * 1024


def dot_rows(left, right):
    return lax.dot_general(left, right, (((1,), (1,)), ((), ())), preferred_element_type=jnp.float32)


def dot_plain(left, right):
    return lax.dot_general(left, right, (((1,), (0,)), ((), ())), preferred_element_type=jnp.float32)


def dot_tokens(left, right):
    return lax.dot_general(left, right, (((0,), (0,)), ((), ())), preferred_element_type=jnp.float32)


def key_features(random_rows, segments, global_rows):
    blocks, head_count, _ = random_rows.shape
    index = jnp.arange(blocks)
    near = (jnp.abs(index[:, None] - index[None, :]) <= 1).astype(jnp.int32)
    named = jnp.sum((global_rows[:, None] == index[None, :]).astype(jnp.int32), axis=0)
    far = jnp.sum((random_rows[..., None] == index).astype(jnp.int32), axis=2)
    count = near[:, None, :] + named[None, None, :] + far
    count = jnp.where(named[:, None, None] > 0, 1, count)
    high = jnp.where(count == 0, masked, 0.0)
    low = jnp.zeros_like(high)
    for times in (2, 3):
        high = jnp.where(count == times, LOG_HIGH[times - 1], high)
        low = jnp.where(count == times, LOG_LOW[times - 1], low)
    width = -(-(2 * blocks + 6) // 128) * 128
    tokens = segments.shape[0]
    segment_hot = (segments[:, None] == jnp.arange(3)).astype(jnp.float32)
    table = jnp.concatenate([high, low], axis=2).transpose(1, 0, 2)
    spread = jnp.broadcast_to(
        table[:, :, None, :], (head_count, blocks, BLOCK, 2 * blocks)
    ).reshape(head_count, tokens, 2 * blocks)
    query_side = jnp.concatenate(
        [
            spread,
            jnp.broadcast_to(segment_hot, (head_count, tokens, 3)),
            jnp.zeros((head_count, tokens, width - 2 * blocks - 3), jnp.float32),
        ],
        axis=2,
    ).astype(LOW)
    block_hot = (jnp.arange(tokens)[:, None] // BLOCK == index).astype(jnp.float32)
    key_side = jnp.concatenate(
        [
            block_hot,
            block_hot,
            masked * (1.0 - segment_hot),
            jnp.ones((tokens, 3), jnp.float32),
            jnp.zeros((tokens, width - 2 * blocks - 6), jnp.float32),
        ],
        axis=1,
    ).astype(LOW)
    return query_side, key_side


def attend_kernel(q_ref, k_ref, v_ref, qa_ref, ka_ref, out_ref, lse_ref):
    tokens, pair = q_ref.shape
    left = lax.broadcasted_iota(jnp.int32, (CHUNK, pair), 1) < pair // 2
    keys = jnp.concatenate([k_ref[...], ka_ref[...]], axis=1)
    values = v_ref[...]

    def step(index, carry):
        rows = pl.ds(pl.multiple_of(index * CHUNK, CHUNK), CHUNK)
        queries = q_ref[rows, :] * 0.125
        outs, tops = [], []
        for head in range(2):
            mine = left if head == 0 else jnp.logical_not(left)
            side = jnp.where(mine, queries, jnp.zeros_like(queries))
            scores = dot_rows(jnp.concatenate([side, qa_ref[head, rows, :]], axis=1), keys)
            top = jnp.max(scores, axis=1, keepdims=True)
            weight = jnp.exp(scores - top)
            total = jnp.sum(weight, axis=1, keepdims=True)
            outs.append(dot_plain(weight.astype(LOW), values) / total)
            tops.append(top + jnp.log(total))
        out_ref[rows, :] = jnp.where(left, outs[0], outs[1]).astype(LOW)
        lse_ref[rows, :] = jnp.where(left, tops[0], tops[1])
        return carry

    lax.fori_loop(0, tokens // CHUNK, step, 0)


def attend(projected, query_side, key_side, width):
    tokens = projected.shape[0]
    pairs = width // 128
    features = key_side.shape[1]
    return pl.pallas_call(
        attend_kernel,
        grid=(pairs,),
        in_specs=[
            pl.BlockSpec((tokens, 128), lambda p: (0, p)),
            pl.BlockSpec((tokens, 128), lambda p: (0, pairs + p)),
            pl.BlockSpec((tokens, 128), lambda p: (0, 2 * pairs + p)),
            pl.BlockSpec((2, tokens, features), lambda p: (p, 0, 0)),
            pl.BlockSpec((tokens, features), lambda p: (0, 0)),
        ],
        out_specs=[
            pl.BlockSpec((tokens, 128), lambda p: (0, p)),
            pl.BlockSpec((tokens, 128), lambda p: (0, p)),
        ],
        out_shape=[
            jax.ShapeDtypeStruct((tokens, width), LOW),
            jax.ShapeDtypeStruct((tokens, width), jnp.float32),
        ],
        compiler_params=pltpu.CompilerParams(vmem_limit_bytes=VMEM_BYTES),
        cost_estimate=pl.CostEstimate(
            flops=16 * pairs * tokens * tokens * 128,
            bytes_accessed=tokens * width * 16,
            transcendentals=2 * pairs * tokens * tokens,
        ),
    )(projected, projected, projected, query_side, key_side)


def three_terms(values):
    high = values.astype(LOW).astype(jnp.float32)
    rest = values - high
    middle = rest.astype(LOW).astype(jnp.float32)
    return high, middle, rest - middle


def attend_back_kernel(
    q_ref, k_ref, v_ref, do_ref, o_ref, lse_ref, qa_ref, ka_ref, grad_ref, dk_acc, dv_acc
):
    tokens, pair = q_ref.shape
    features = ka_ref.shape[1]
    pairs = pl.num_programs(0)
    place = pl.program_id(0)
    blocks = tokens // BLOCK
    first = 2 * blocks + 3
    left = lax.broadcasted_iota(jnp.int32, (CHUNK, pair), 1) < pair // 2
    lane = lax.broadcasted_iota(jnp.int32, (CHUNK, features), 1)
    lane_pair = lax.broadcasted_iota(jnp.int32, (CHUNK, pair), 1)
    keys = jnp.concatenate([k_ref[...], ka_ref[...]], axis=1)
    turned = jnp.transpose(k_ref[...].astype(jnp.float32)).astype(LOW)
    ones = (lax.broadcasted_iota(jnp.int32, (tokens, pair), 1) < 3).astype(jnp.float32).astype(LOW)
    values = jnp.concatenate([v_ref[...], ones], axis=1)
    dk_acc[...] = jnp.zeros_like(dk_acc)
    dv_acc[...] = jnp.zeros_like(dv_acc)
    column = pl.multiple_of(place * 128, 128)

    def step(index, carry):
        rows = pl.ds(pl.multiple_of(index * CHUNK, CHUNK), CHUNK)
        queries = q_ref[rows, :] * 0.125
        grads = do_ref[rows, :]
        product = grads.astype(jnp.float32) * o_ref[rows, :].astype(jnp.float32)
        parts = []
        for head in range(2):
            mine = left if head == 0 else jnp.logical_not(left)
            level = lse_ref[rows, head * 64 : head * 64 + 1]
            inner = jnp.sum(jnp.where(mine, product, 0.0), axis=1, keepdims=True)
            side = qa_ref[head, rows, :].astype(jnp.float32)
            for spot, term in enumerate(three_terms(level)):
                side = jnp.where(lane == first + spot, -term, side)
            query_side = jnp.where(mine, queries, jnp.zeros_like(queries))
            grad_side = jnp.where(mine, grads, jnp.zeros_like(grads))
            tail = jnp.zeros((CHUNK, pair), jnp.float32)
            for spot, term in enumerate(three_terms(inner)):
                tail = jnp.where(lane_pair == spot, -term, tail)
            probs = jnp.exp(
                dot_rows(keys, jnp.concatenate([query_side, side.astype(LOW)], axis=1))
            )
            change = dot_rows(values, jnp.concatenate([grad_side, tail.astype(LOW)], axis=1))
            grad_scores = (probs * change).astype(LOW)
            dv_acc[...] += dot_plain(probs.astype(LOW), grad_side)
            dk_acc[...] += dot_plain(grad_scores, query_side)
            parts.append(dot_plain(turned, grad_scores))
        half = pair // 2
        joined = jnp.concatenate([parts[0][:half], parts[1][half:]], axis=0)
        grad_ref[rows, pl.ds(column, 128)] = (jnp.transpose(joined) * 0.125).astype(LOW)
        return carry

    lax.fori_loop(0, tokens // CHUNK, step, 0)
    key_column = pl.multiple_of((pairs + place) * 128, 128)
    value_column = pl.multiple_of((2 * pairs + place) * 128, 128)
    grad_ref[:, pl.ds(key_column, 128)] = dk_acc[...].astype(LOW)
    grad_ref[:, pl.ds(value_column, 128)] = dv_acc[...].astype(LOW)


def attend_back(projected, grad_attended, attended, levels, query_side, key_side):
    tokens, width = attended.shape
    pairs = width // 128
    features = key_side.shape[1]
    return pl.pallas_call(
        attend_back_kernel,
        grid=(pairs,),
        in_specs=[
            pl.BlockSpec((tokens, 128), lambda p: (0, p)),
            pl.BlockSpec((tokens, 128), lambda p: (0, pairs + p)),
            pl.BlockSpec((tokens, 128), lambda p: (0, 2 * pairs + p)),
            pl.BlockSpec((tokens, 128), lambda p: (0, p)),
            pl.BlockSpec((tokens, 128), lambda p: (0, p)),
            pl.BlockSpec((tokens, 128), lambda p: (0, p)),
            pl.BlockSpec((2, tokens, features), lambda p: (p, 0, 0)),
            pl.BlockSpec((tokens, features), lambda p: (0, 0)),
        ],
        out_specs=pl.BlockSpec((tokens, 3 * width), lambda p: (0, 0)),
        out_shape=jax.ShapeDtypeStruct((tokens, 3 * width), LOW),
        scratch_shapes=[
            pltpu.VMEM((tokens, 128), jnp.float32),
            pltpu.VMEM((tokens, 128), jnp.float32),
        ],
        compiler_params=pltpu.CompilerParams(vmem_limit_bytes=VMEM_BYTES),
        cost_estimate=pl.CostEstimate(
            flops=40 * pairs * tokens * tokens * 128,
            bytes_accessed=tokens * width * 24,
            transcendentals=2 * pairs * tokens * tokens,
        ),
    )(projected, projected, projected, grad_attended, attended, levels, query_side, key_side)


def swap(value):
    return lax.ppermute(value, "section", [(0, 1), (1, 0)])


def normalized(values_in):
    row_mean = jnp.mean(values_in, axis=-1, keepdims=True)
    centred = values_in - row_mean
    spread = jnp.mean(centred * centred, axis=-1, keepdims=True)
    scale = lax.rsqrt(spread + epsilon)
    return centred * scale, scale


def norm_back(values_in, incoming, gain_vec):
    unit, scale = normalized(values_in)
    grad_gain = jnp.sum(incoming * unit, axis=0)
    grad_shift = jnp.sum(incoming, axis=0)
    p = incoming * gain_vec
    mean_p = jnp.mean(p, axis=-1, keepdims=True)
    mean_pn = jnp.mean(p * unit, axis=-1, keepdims=True)
    return scale * (p - mean_p - unit * mean_pn), grad_gain, grad_shift


class Shares:
    def __init__(self, width, columns, depth, vector_len):
        self.width = width
        self.columns = columns
        self.depth = depth
        self.vector_len = vector_len
        self.half = columns // 2
        self.per = width // columns
        self.groups = columns // depth
        self.rows = self.half + depth // 2 + 16

    def row_half(self, turned, core, kind):
        half, per = self.half, self.per
        plain = lax.dynamic_slice_in_dim(turned, core * half, half, axis=0)
        inner = turned.reshape(self.columns, per, 2, half)
        inner = lax.dynamic_index_in_dim(inner, core, 2, keepdims=False)
        inner = inner.reshape(2, half, per * half).transpose(1, 0, 2).reshape(half, self.width)
        hidden = turned.reshape(self.groups, 2, self.depth // 2, self.width)
        hidden = lax.dynamic_index_in_dim(hidden, core, 1, keepdims=False)
        hidden = hidden.reshape(half, self.width)
        return jnp.where(kind == 1, inner, jnp.where(kind == 2, hidden, plain))

    def row_whole(self, halves, kind):
        half, per = self.half, self.per
        plain = jnp.concatenate(halves, axis=0)
        inner = jnp.stack(
            [
                piece.reshape(half, 2, per * half)
                .transpose(1, 0, 2)
                .reshape(self.columns, per, half)
                for piece in halves
            ],
            axis=2,
        ).reshape(self.columns, self.width)
        hidden = jnp.stack(
            [piece.reshape(self.groups, self.depth // 2, self.width) for piece in halves], axis=1
        ).reshape(self.columns, self.width)
        return jnp.where(kind == 1, inner, jnp.where(kind == 2, hidden, plain))

    def payload(self, turned, down, vector_row, core, kind):
        mine = self.row_half(turned, core, kind)
        below = lax.dynamic_slice_in_dim(down, core * (self.depth // 2), self.depth // 2, axis=0)
        return jnp.concatenate([mine, below, vector_row], axis=0)

    def unpack(self, gathered, core):
        half, per, width = self.half, self.per, self.width
        rows = gathered[:, :half]
        proj = rows[: 3 * per].reshape(3 * per * half, width)
        out = (
            rows[3 * per : 4 * per]
            .reshape(per, half, 2, per * half)
            .transpose(0, 2, 1, 3)
            .reshape(width, per * half)
        )
        up = rows[4 * per :].reshape(-1, width)
        down = gathered[:, half : half + self.depth // 2].reshape(-1, width)
        vec = gathered[:, half + self.depth // 2, : self.vector_len].reshape(-1)
        pieces = split_vectors(vec.astype(jnp.float32), width)
        bias_query, bias_value = self.vector_half(pieces[2], core), self.vector_half(pieces[3], core)
        bias_up = lax.dynamic_index_in_dim(
            pieces[8].reshape(-1, 2, self.depth // 2), core, 1, keepdims=False
        ).reshape(-1)
        return (
            (proj, out, up, down),
            (pieces[0], pieces[1], bias_query, bias_value, pieces[4], pieces[5], pieces[6])
            + (pieces[7], bias_up),
        )

    def vector_half(self, vec, core):
        return lax.dynamic_index_in_dim(
            vec.reshape(self.per, 2, self.half), core, 1, keepdims=False
        ).reshape(-1)

    def pack_grads(self, grads, vector_grads, core):
        proj, out, up, down = grads
        half, per, width = self.half, self.per, self.width
        out = (
            out.reshape(per, 2, half, per * half).transpose(0, 2, 1, 3).reshape(per, half, width)
        )
        rows = jnp.concatenate(
            [proj.reshape(-1, half, width), out, up.reshape(-1, half, width)], axis=0
        )
        shards = rows.shape[0]
        below = down.reshape(shards, self.depth // 2, width)
        hot = (jnp.arange(2) == core).astype(jnp.float32)
        first = hot[0]
        spread = list(vector_grads)
        for index in (2, 3):
            spread[index] = (
                spread[index].reshape(per, 1, half) * hot[None, :, None]
            ).reshape(-1)
        spread[8] = (spread[8].reshape(-1, 1, self.depth // 2) * hot[None, :, None]).reshape(-1)
        for index in (0, 1, 4, 5, 6, 7):
            spread[index] = spread[index] * first
        vec = jnp.concatenate(spread).reshape(shards, 1, self.vector_len)
        vec = jnp.pad(vec, ((0, 0), (0, 15), (0, width - self.vector_len)))
        return jnp.concatenate([rows, below, vec.astype(LOW)], axis=1)


def window_forward(hidden, weights, biases, features):
    proj, out, up, down = weights
    gain_one, shift_one, bias_query, bias_value, bias_out = biases[:5]
    gain_two, shift_two, bias_down, bias_up = biases[5:]
    unit, _ = normalized(hidden)
    normed = (unit * gain_one + shift_one).astype(LOW)
    bias = jnp.concatenate([bias_query, jnp.zeros_like(bias_query), bias_value])
    projected = (dot_rows(normed, proj) + bias).astype(LOW)
    attended, levels = attend(projected, *features, bias_query.shape[0])
    branch = dot_rows(attended, out)
    middle = hidden + (branch + swap(branch.astype(LOW)).astype(jnp.float32) + bias_out)
    unit_two, _ = normalized(middle)
    normed_two = (unit_two * gain_two + shift_two).astype(LOW)
    up_value = dot_rows(normed_two, up) + bias_up
    cdf = 0.5 * (1.0 + lax.erf(up_value * 0.5**0.5))
    active = (up_value * cdf).astype(LOW)
    slope = cdf + up_value * jnp.exp(-0.5 * up_value * up_value) * (0.5 / math.pi) ** 0.5
    part = dot_plain(active, down)
    output = middle + (part + swap(part.astype(LOW)).astype(jnp.float32) + bias_down)
    return output, (hidden, normed, projected, attended, levels, middle, normed_two, slope, active)


def window_backward(stored, grad_output, weights, biases, features):
    hidden, normed, projected, attended, levels, middle, normed_two, slope, active = stored
    proj, out, up, down = weights
    gain_one, gain_two = biases[0], biases[5]
    grad_ffn = grad_output.astype(LOW)
    grad_bias_down = jnp.sum(grad_ffn.astype(jnp.float32), axis=0)
    grad_up = (dot_rows(grad_ffn, down) * slope).astype(LOW)
    grad_bias_up = jnp.sum(grad_up.astype(jnp.float32), axis=0)
    part = dot_plain(grad_up, up)
    arrived = swap(part.astype(LOW)).astype(jnp.float32)
    down_grad = dot_tokens(active, grad_ffn).astype(LOW)
    up_grad = dot_tokens(grad_up, normed_two).astype(LOW)
    grad_norm, grad_gain_two, grad_shift_two = norm_back(middle, part + arrived, gain_two)
    grad_middle = grad_output + grad_norm
    grad_branch = grad_middle.astype(LOW)
    grad_bias_out = jnp.sum(grad_branch.astype(jnp.float32), axis=0)
    out_grad = dot_tokens(grad_branch, attended).astype(LOW)
    grad_attended = dot_plain(grad_branch, out).astype(LOW)
    grad_proj = attend_back(projected, grad_attended, attended, levels, *features)
    summed = jnp.sum(grad_proj.astype(jnp.float32), axis=0)
    width = attended.shape[1]
    part = dot_plain(grad_proj, proj)
    arrived = swap(part.astype(LOW)).astype(jnp.float32)
    proj_grad = dot_tokens(grad_proj, normed).astype(LOW)
    grad_norm, grad_gain_one, grad_shift_one = norm_back(hidden, part + arrived, gain_one)
    vector_grads = (
        grad_gain_one,
        grad_shift_one,
        summed[:width],
        summed[2 * width :],
        grad_bias_out,
        grad_gain_two,
        grad_shift_two,
        grad_bias_down,
        grad_bias_up,
    )
    return grad_middle + grad_norm, (proj_grad, out_grad, up_grad, down_grad), vector_grads


def window_shards(
    block_input,
    cotangent,
    random_ids,
    segment_ids,
    global_ids,
    w_rows,
    w_rows_first,
    w_rows_second,
    w_down,
    w_down_first,
    w_down_second,
    vectors,
    vectors_first,
    vectors_second,
):
    core = lax.axis_index("section")
    place = lax.axis_index("seq")
    shard = lax.axis_index(("dp", "seq"))
    micro, _, tokens, width = block_input.shape
    half = tokens // 2
    _, _, columns = w_rows.shape
    shares = Shares(width, columns, w_down.shape[1], vectors.shape[1])
    offset = shard * columns
    kind = jnp.where(offset < 3 * width, 0, jnp.where(offset < 4 * width, 1, 2))

    def by_core(mine, other):
        return jnp.where(core == 0, mine, other), jnp.where(core == 0, other, mine)

    def window_of(array):
        piece = lax.dynamic_slice_in_dim(array[:, 0], core * half, half, axis=1)
        mine = lax.all_to_all(piece, "seq", 0, 0, tiled=True)
        low, high = by_core(mine, swap(mine))
        return jnp.stack([low, high], axis=1).reshape(micro * tokens, width)

    turned = w_rows[0].astype(LOW).T
    below = w_down[0].astype(LOW)
    vector_row = jnp.pad(
        vectors[0].astype(LOW)[None], ((0, 15), (0, width - shares.vector_len))
    )
    kept = shares.payload(turned, below, vector_row, core, kind)
    given = shares.payload(turned, below, vector_row, 1 - core, kind)
    layers = by_core(kept, swap(given))
    gathered = [lax.all_gather(layer, ("dp", "seq"), axis=0) for layer in layers]

    head_half = shares.half // (width // HEADS)
    random_rows = lax.dynamic_index_in_dim(random_ids[:, 0], place, 0, keepdims=False)
    random_rows = random_rows.reshape(random_rows.shape[0], shares.per, 2, head_half, -1)
    random_rows = lax.dynamic_index_in_dim(random_rows, core, 2, keepdims=False)
    random_rows = random_rows.reshape(random_rows.shape[0], shares.per * head_half, -1)
    segments = lax.dynamic_index_in_dim(segment_ids[:, 0], place, 0, keepdims=False)
    global_rows = lax.dynamic_index_in_dim(global_ids[:, 0], place, 0, keepdims=False)
    features = key_features(random_rows, segments, global_rows)

    params = [shares.unpack(piece, core) for piece in gathered]
    hidden = window_of(block_input).astype(jnp.float32)
    output, stored_zero = window_forward(hidden, *params[0], features)
    hidden = output.astype(LOW).astype(jnp.float32)
    final, stored_one = window_forward(hidden, *params[1], features)

    def back_to_slices(array):
        pieces = array.astype(LOW).reshape(micro, 2, half, width)
        piece = lax.dynamic_index_in_dim(pieces, core, 1, keepdims=False)
        return lax.all_to_all(piece, "seq", 0, 0, tiled=True)

    final_slices = back_to_slices(final)
    grad = window_of(cotangent).astype(jnp.float32)
    grad, grads_one, vector_one = window_backward(stored_one, grad, *params[1], features)
    packed_one = shares.pack_grads(grads_one, vector_one, core)
    reduced_one = lax.psum_scatter(packed_one, ("dp", "seq"), scatter_dimension=0)
    grad = grad.astype(LOW).astype(jnp.float32)
    grad, grads_zero, vector_zero = window_backward(stored_zero, grad, *params[0], features)
    packed_zero = shares.pack_grads(grads_zero, vector_zero, core)
    reduced_zero = lax.psum_scatter(packed_zero, ("dp", "seq"), scatter_dimension=0)
    grad_slices = back_to_slices(grad)

    kept, given = by_core(grad_slices, final_slices)
    low, high = by_core(kept, swap(given))
    section_result = jnp.stack([low, high], axis=1).reshape(micro, 1, tokens, width)

    kept, given = by_core(reduced_zero, reduced_one)
    halves = by_core(kept, swap(given))
    halves = [piece.astype(jnp.float32) for piece in halves]
    split, end = shares.half, shares.half + shares.depth // 2
    grad_rows = shares.row_whole([piece[:split] for piece in halves], kind).T
    grad_down = jnp.concatenate([piece[split:end] for piece in halves], axis=0)
    grad_vector = (halves[0][end] + halves[1][end])[: shares.vector_len]
    new_rows = adam_update(
        w_rows[0], w_rows_first[0], w_rows_second[0], grad_rows, rate_matrix, decay_matrix
    )
    new_down = adam_update(
        w_down[0], w_down_first[0], w_down_second[0], grad_down, rate_matrix, decay_matrix
    )
    new_vectors = adam_update(
        vectors[0], vectors_first[0], vectors_second[0], grad_vector, rate_vector, 0.0
    )
    updated = [piece[None] for piece in new_rows + new_down + new_vectors]
    return (section_result[None].astype(jnp.float32), *updated)


def one_window_each(mesh, block_input, w_rows, w_down, vectors):
    micro, windows, length, width = block_input.shape
    shards = mesh.shape["dp"] * mesh.shape["seq"]
    columns, depth = w_rows.shape[2] // shards, w_down.shape[1] // shards
    head_dim = width // HEADS
    tokens = length // mesh.shape["seq"]
    return (
        mesh.shape["section"] == 2
        and mesh.shape["seq"] == micro
        and mesh.shape["dp"] == windows
        and tokens % (2 * BLOCK) == 0
        and length % CHUNK == 0
        and head_dim == 64
        and width % columns == 0
        and columns % (2 * head_dim) == 0
        and columns % depth == 0
        and width // columns * (columns // 2) % 128 == 0
        and depth % 32 == 0
        and vectors.shape[1] // shards <= width
    )


def solution(mesh):
    in_specs = (
        P(None, "dp", "seq", None),
        P(None, "dp", "seq", None),
        P(None, "dp", None, None, None),
        P(None, "dp", None),
        P(None, "dp", None),
        P("section", None, ("dp", "seq")),
        P("section", None, ("dp", "seq")),
        P("section", None, ("dp", "seq")),
        P("section", ("dp", "seq"), None),
        P("section", ("dp", "seq"), None),
        P("section", ("dp", "seq"), None),
        P("section", ("dp", "seq")),
        P("section", ("dp", "seq")),
        P("section", ("dp", "seq")),
    )
    out_specs = (
        P("section", None, "dp", "seq", None),
        P("section", None, ("dp", "seq")),
        P("section", None, ("dp", "seq")),
        P("section", None, ("dp", "seq")),
        P("section", ("dp", "seq"), None),
        P("section", ("dp", "seq"), None),
        P("section", ("dp", "seq"), None),
        P("section", ("dp", "seq")),
        P("section", ("dp", "seq")),
        P("section", ("dp", "seq")),
    )

    def step(*arrays):
        chosen = general_shards
        if one_window_each(mesh, arrays[0], arrays[5], arrays[8], arrays[11]):
            chosen = window_shards
        return jax.shard_map(
            chosen, mesh=mesh, in_specs=in_specs, out_specs=out_specs, check_vma=False
        )(*arrays)

    return step
```

```python
import math
from functools import partial

import jax
import jax.numpy as jnp
import ml_dtypes
import numpy as np
from jax import lax
from jax.experimental import pallas as pl
from jax.experimental.pallas import tpu as pltpu
from jax.sharding import PartitionSpec as P

SECTION, DP, SEQ = "section", "dp", "seq"
HEADS = 12
BLOCK = 64
STEP = 5


epsilon = 1e-05
masked = -1e30
rate_matrix = 0.02
rate_vector = 0.2
decay_matrix = 0.01


def with_halo(x, sides, width):
    for axis, dim in sides:
        devices, length = (lax.axis_size(axis), x.shape[dim])
        up = [(i, (i + 1) % devices) for i in range(devices - 1)]
        down = [(j, i) for i, j in up]
        last = lax.slice_in_dim(x, length - width, length, axis=dim)
        initial = lax.slice_in_dim(x, 0, width, axis=dim)
        before = lax.ppermute(last, axis, up)
        after = lax.ppermute(initial, axis, down)
        x = jnp.concatenate([before, x, after], axis=dim)
    return x


def merged(value, axis, join):
    pieces = jax.tree.map(lambda part: lax.all_gather(part, axis), value)
    head = jax.tree.map(lambda part: part[0], pieces)
    tail = jax.tree.map(lambda part: part[1:], pieces)
    subtotal, _ = lax.scan(lambda subtotal, share: (join(subtotal, share), None), head, tail)
    return subtotal


def from_behind(x, axis, by):
    devices = lax.axis_size(axis)
    pairs = [(i, i + by) for i in range(devices) if 0 <= i + by < devices]
    return lax.ppermute(x, axis, pairs)


def partner(value, axis, bit):
    mask = 2**bit
    pairs = [(source, source ^ mask) for source in range(lax.axis_size(axis))]
    return lax.ppermute(value, axis, pairs)


def mixed_sum(form, left, right):
    return jnp.einsum(form, left, right, preferred_element_type=jnp.float32)


def exact_two(form, left, right):
    return jnp.einsum(
        form, left, right, precision=lax.Precision.HIGHEST, preferred_element_type=jnp.float32
    )


def norm_rows(values_in, gain_vec, shift_vec):
    row_mean = jnp.mean(values_in, axis=-1, keepdims=True)
    centred = values_in - row_mean
    spread = jnp.mean(centred * centred, axis=-1, keepdims=True)
    return centred * lax.rsqrt(spread + epsilon) * gain_vec + shift_vec


def split_vectors(vector_weights, model_width):
    pieces = [
        vector_weights[piece_index * model_width : (piece_index + 1) * model_width]
        for piece_index in range(8)
    ]
    return pieces + [vector_weights[8 * model_width :]]


def route_tables(random_rows, segments, global_rows, seq_place, groups):
    windows, blocks, head_count, pick_count = random_rows.shape
    blocks_dev = blocks // groups
    request_count = blocks_dev * head_count * pick_count
    capacity = -(-request_count // groups)
    requests = random_rows.reshape(windows, groups, request_count)
    owners = requests // blocks_dev
    inside = requests % blocks_dev
    head_of = jnp.arange(request_count) // pick_count % head_count
    is_mine = owners == seq_place
    slot_index = jnp.cumsum(is_mine.astype(jnp.int32), axis=2) - 1
    slot_hot = ((slot_index[..., None] == jnp.arange(capacity)) & is_mine[..., None]).astype(
        jnp.float32
    )
    inside_hot = (inside[..., None] == jnp.arange(blocks_dev)).astype(jnp.float32)
    head_hot = (head_of[:, None] == jnp.arange(head_count)).astype(jnp.float32)
    sender = jnp.einsum(
        "wqsc,wqsb,sh->wqcbh", slot_hot, inside_hot, head_hot, precision=lax.Precision.HIGHEST
    )
    my_owners = lax.dynamic_index_in_dim(owners, seq_place, axis=1, keepdims=False)
    earlier = jnp.arange(request_count)[None, :] < jnp.arange(request_count)[:, None]
    same_owner = my_owners[:, :, None] == my_owners[:, None, :]
    rank_index = jnp.sum((same_owner & earlier[None]).astype(jnp.int32), axis=2)
    picker = (
        (my_owners[..., None, None] == jnp.arange(groups)[:, None])
        & (rank_index[..., None, None] == jnp.arange(capacity)[None, :])
    ).astype(jnp.float32)
    first_block = seq_place * blocks_dev
    owned_hot = (global_rows[:, :, None] == first_block + jnp.arange(blocks_dev)).astype(
        jnp.float32
    )
    length = segments.shape[1]
    block_len = length // blocks
    seg_blocks = segments.reshape(windows, blocks, block_len)
    seg_pad = jnp.pad(seg_blocks, ((0, 0), (1, 1), (0, 0)), constant_values=-1)
    near_segs = lax.dynamic_slice_in_dim(seg_pad, first_block, blocks_dev + 2, axis=1)
    slide_seg = jnp.concatenate([near_segs[:, :-2], near_segs[:, 1:-1], near_segs[:, 2:]], axis=2)
    query_seg = near_segs[:, 1:-1]
    rows_index = jnp.arange(windows)
    global_seg = seg_blocks[rows_index[:, None], global_rows].reshape(windows, -1)
    chosen = lax.dynamic_slice_in_dim(random_rows, first_block, blocks_dev, axis=1)
    far_seg = seg_blocks[rows_index[:, None, None, None], chosen].reshape(
        windows, blocks_dev, head_count, -1
    )
    key_seg = jnp.concatenate(
        [
            jnp.broadcast_to(
                slide_seg[:, :, None, :], (windows, blocks_dev, head_count, slide_seg.shape[2])
            ),
            jnp.broadcast_to(
                global_seg[:, None, None, :], (windows, blocks_dev, head_count, global_seg.shape[1])
            ),
            far_seg,
        ],
        axis=3,
    )
    key_mask = query_seg[:, :, None, :, None] == key_seg[:, :, :, None, :]
    local_seg = query_seg.reshape(windows, -1)
    full_mask = global_seg[:, None, :, None] == local_seg[:, None, None, :]
    return (sender, picker, owned_hot, key_mask, full_mask)


def fetch_blocks(paired, queries, sender, picker, owned_hot):
    windows, tokens, head_count, doubled = paired.shape
    head_dim = queries.shape[-1]
    blocks_dev = tokens // BLOCK
    flattened = paired.reshape(windows, tokens, head_count * doubled)
    padded = with_halo(flattened, ((SEQ, 1),), BLOCK)
    framed = padded.reshape(windows, blocks_dev + 2, BLOCK, head_count, doubled)
    sliding = jnp.concatenate([framed[:, :-2], framed[:, 1:-1], framed[:, 2:]], axis=2)
    local_blocks = paired.reshape(windows, blocks_dev, BLOCK, head_count, doubled)
    owned_low = owned_hot.astype(jnp.bfloat16)
    offered = mixed_sum("wgb,wbthe->wgthe", owned_low, local_blocks)
    offered_queries = mixed_sum("wgb,wbqhd->wgqhd", owned_low, queries)
    global_kv, global_queries = (
        lax.psum(offered.astype(jnp.bfloat16), SEQ).astype(jnp.float32),
        lax.psum(offered_queries.astype(jnp.bfloat16), SEQ).astype(jnp.float32),
    )
    global_kv = global_kv.astype(jnp.bfloat16).reshape(windows, -1, head_count, doubled)
    global_queries = global_queries.astype(jnp.bfloat16).reshape(windows, -1, head_count, head_dim)
    outgoing = mixed_sum("wqcbh,wbthe->qwcte", sender.astype(jnp.bfloat16), local_blocks).astype(
        jnp.bfloat16
    )
    incoming = lax.all_to_all(outgoing, SEQ, split_axis=0, concat_axis=0, tiled=True)
    distant = mixed_sum("wspc,pwcte->wste", picker.astype(jnp.bfloat16), incoming).astype(
        jnp.bfloat16
    )
    pick_count = picker.shape[1] // (blocks_dev * head_count)
    distant = distant.reshape(windows, blocks_dev, head_count, pick_count, BLOCK, doubled)
    return (sliding, global_kv, distant, global_queries)


def combine_stats(earlier, later):
    top = jnp.maximum(earlier[0], later[0])
    return (top, earlier[1] * jnp.exp(earlier[0] - top) + later[1] * jnp.exp(later[0] - top))


def full_forward(global_queries, key_part, value_part, full_mask, head_dim):
    scores = mixed_sum("wqhd,wkhd->whqk", global_queries, key_part) * head_dim ** (-0.5)
    scores = jnp.where(full_mask, scores, masked)
    local_top = jnp.max(scores, axis=3, keepdims=True)
    local_sum = jnp.sum(
        jnp.where(full_mask, jnp.exp(scores - local_top), 0.0), axis=3, keepdims=True
    )
    row_top, row_sum = merged((local_top, local_sum), SEQ, combine_stats)
    full_probs = jnp.where(full_mask, jnp.exp(scores - row_top), 0.0) / row_sum
    partial_out = mixed_sum("whqk,wkhd->wqhd", full_probs.astype(jnp.bfloat16), value_part)
    full_out = lax.psum(partial_out.astype(jnp.bfloat16), SEQ).astype(jnp.float32)
    return (full_out, full_probs)


def attention_weights(queries, sliding, global_kv, distant, key_mask):
    head_dim = queries.shape[-1]
    windows, blocks_dev, _, head_count, _ = queries.shape
    near_scores = mixed_sum("wbqhd,wbkhd->wbhqk", queries, sliding[..., :head_dim])
    global_scores = mixed_sum("wbqhd,wkhd->wbhqk", queries, global_kv[..., :head_dim])
    far_scores = mixed_sum("wbqhd,wbhrkd->wbhqrk", queries, distant[..., :head_dim])
    far_scores = far_scores.reshape(windows, blocks_dev, head_count, BLOCK, -1)
    scores = jnp.concatenate([near_scores, global_scores, far_scores], axis=4) * head_dim ** (-0.5)
    scores = jnp.where(key_mask, scores, masked)
    row_top = jnp.max(scores, axis=4, keepdims=True)
    weight = jnp.exp(scores - row_top)
    return weight / jnp.sum(weight, axis=4, keepdims=True)


def split_keys(scores_like, sliding, global_kv, distant):
    near_keys = sliding.shape[2]
    global_keys = global_kv.shape[1]
    windows, blocks_dev, head_count, pick_count, _, _ = distant.shape
    near_part = scores_like[..., :near_keys]
    global_part = scores_like[..., near_keys : near_keys + global_keys]
    far_part = scores_like[..., near_keys + global_keys :].reshape(
        windows, blocks_dev, head_count, BLOCK, pick_count, BLOCK
    )
    return (near_part, global_part, far_part)


def attention_values(low_probs, sliding, global_kv, distant, head_dim):
    near_part, global_part, far_part = split_keys(low_probs, sliding, global_kv, distant)
    attended = mixed_sum("wbhqk,wbkhd->wbqhd", near_part, sliding[..., head_dim:])
    attended = attended + mixed_sum("wbhqk,wkhd->wbqhd", global_part, global_kv[..., head_dim:])
    return attended + mixed_sum("wbhqrk,wbhrkd->wbqhd", far_part, distant[..., head_dim:])


def layer_forward(hidden, weights, tables):
    row_weights, down_weights, vector_weights = weights
    sender, picker, owned_hot, key_mask, full_mask = tables
    model_width = row_weights.shape[0]
    windows, tokens, _ = hidden.shape
    blocks_dev = tokens // BLOCK
    head_dim = model_width // HEADS
    (
        gain_one,
        shift_one,
        bias_query,
        bias_value,
        bias_out,
        gain_two,
        shift_two,
        bias_down,
        bias_up,
    ) = split_vectors(vector_weights, model_width)
    normed = norm_rows(hidden, gain_one, shift_one).astype(jnp.bfloat16)
    projected = mixed_sum("wtd,de->wte", normed, row_weights[:, : 3 * model_width])
    projected = (
        projected + jnp.concatenate([bias_query, jnp.zeros_like(bias_query), bias_value])
    ).astype(jnp.bfloat16)
    queries = projected[..., :model_width].reshape(windows, blocks_dev, BLOCK, HEADS, head_dim)
    key_part = projected[..., model_width : 2 * model_width].reshape(
        windows, tokens, HEADS, head_dim
    )
    value_part = projected[..., 2 * model_width :].reshape(windows, tokens, HEADS, head_dim)
    paired = jnp.concatenate([key_part, value_part], axis=3)
    sliding, global_kv, distant, global_queries = fetch_blocks(
        paired, queries, sender, picker, owned_hot
    )
    probabilities = attention_weights(queries, sliding, global_kv, distant, key_mask)
    attended = attention_values(
        probabilities.astype(jnp.bfloat16), sliding, global_kv, distant, head_dim
    )
    full_out, full_probs = full_forward(global_queries, key_part, value_part, full_mask, head_dim)
    placed = exact_two(
        "wgb,wgqhd->wbqhd", owned_hot, full_out.reshape(windows, -1, BLOCK, HEADS, head_dim)
    )
    on_global = jnp.sum(owned_hot, axis=1)[:, :, None, None, None] > 0
    attended = jnp.where(on_global, placed, attended)
    mixed_low = attended.reshape(windows, tokens, model_width).astype(jnp.bfloat16)
    middle = (
        hidden
        + mixed_sum("wtd,de->wte", mixed_low, row_weights[:, 3 * model_width : 4 * model_width])
        + bias_out
    )
    normed_two = norm_rows(middle, gain_two, shift_two).astype(jnp.bfloat16)
    up_value = mixed_sum("wtd,df->wtf", normed_two, row_weights[:, 4 * model_width :]) + bias_up
    active = jax.nn.gelu(up_value, approximate=False).astype(jnp.bfloat16)
    output = middle + mixed_sum("wtf,fd->wtd", active, down_weights) + bias_down
    stored = (
        hidden,
        normed,
        queries,
        sliding,
        global_kv,
        distant,
        probabilities,
        mixed_low,
        middle,
        normed_two,
        up_value,
        active,
        key_part,
        value_part,
        global_queries,
        full_probs,
    )
    return (output, stored)


def return_blocks(near_back, global_back, far_back, query_part, sender, picker, owned_hot):
    windows, blocks_dev, _, head_count, doubled = near_back.shape
    first_third = near_back[:, :, :BLOCK]
    centre_third = near_back[:, :, BLOCK : 2 * BLOCK]
    last_third = near_back[:, :, 2 * BLOCK :]
    framed = jnp.pad(first_third, ((0, 0), (0, 2), (0, 0), (0, 0), (0, 0)))
    framed = framed + jnp.pad(centre_third, ((0, 0), (1, 1), (0, 0), (0, 0), (0, 0)))
    framed = framed + jnp.pad(last_third, ((0, 0), (2, 0), (0, 0), (0, 0), (0, 0)))
    own_grad = framed[:, 1:-1]
    for direction in (1, -1):
        rim_grad = framed[:, -1] if direction == 1 else framed[:, 0]
        arrived = from_behind(rim_grad.astype(jnp.bfloat16), SEQ, direction).astype(
            rim_grad.dtype
        )
        if direction == 1:
            own_grad = jnp.concatenate(
                [own_grad[:, :1] + arrived[:, None], own_grad[:, 1:]], axis=1
            )
        else:
            own_grad = jnp.concatenate(
                [own_grad[:, :-1], own_grad[:, -1:] + arrived[:, None]], axis=1
            )
    global_total, query_total = (
        lax.psum(
            global_back.reshape(windows, -1, BLOCK, head_count, doubled).astype(jnp.bfloat16), SEQ
        ).astype(jnp.float32),
        lax.psum(query_part.astype(jnp.bfloat16), SEQ).astype(jnp.float32),
    )
    own_grad = own_grad + exact_two("wgb,wgthe->wbthe", owned_hot, global_total)
    far_flat = far_back.reshape(windows, -1, BLOCK, doubled)
    returning = exact_two("wspc,wste->pwcte", picker, far_flat)
    arrived_far = lax.all_to_all(
        returning.astype(jnp.bfloat16), SEQ, split_axis=0, concat_axis=0, tiled=True
    ).astype(returning.dtype)
    own_grad = own_grad + exact_two("wqcbh,qwcte->wbthe", sender, arrived_far)
    return (own_grad.reshape(windows, blocks_dev * BLOCK, head_count, doubled), query_total)


def attention_back(
    grad_attended,
    queries,
    sliding,
    global_kv,
    distant,
    probabilities,
    key_part,
    value_part,
    global_queries,
    full_probs,
    sender,
    picker,
    owned_hot,
):
    head_dim = queries.shape[-1]
    score_scale = head_dim ** (-0.5)
    windows, blocks_dev, _, head_count, _ = queries.shape
    on_global = jnp.sum(owned_hot, axis=1)[:, :, None, None, None] > 0
    selected = mixed_sum("wgb,wbqhd->wgqhd", owned_hot.astype(jnp.bfloat16), grad_attended)
    rows_grad = lax.psum(selected.astype(jnp.bfloat16), SEQ).reshape(
        windows, -1, head_count, head_dim
    )
    grad_attended = jnp.where(on_global, jnp.zeros_like(grad_attended), grad_attended)
    low_probs = probabilities.astype(jnp.bfloat16)
    near_grad = mixed_sum("wbqhd,wbkhd->wbhqk", grad_attended, sliding[..., head_dim:])
    global_grad = mixed_sum("wbqhd,wkhd->wbhqk", grad_attended, global_kv[..., head_dim:])
    far_grad = mixed_sum("wbqhd,wbhrkd->wbhqrk", grad_attended, distant[..., head_dim:])
    far_grad = far_grad.reshape(windows, blocks_dev, head_count, BLOCK, -1)
    grad_probs = jnp.concatenate([near_grad, global_grad, far_grad], axis=4)
    grad_scores = probabilities * (
        grad_probs - jnp.sum(probabilities * grad_probs, axis=4, keepdims=True)
    )
    grad_scores = grad_scores.astype(jnp.bfloat16)
    near_split, global_split, far_split = split_keys(grad_scores, sliding, global_kv, distant)
    near_probs, global_probs, far_probs = split_keys(low_probs, sliding, global_kv, distant)
    grad_query = mixed_sum("wbhqk,wbkhd->wbqhd", near_split, sliding[..., :head_dim])
    grad_query = grad_query + mixed_sum(
        "wbhqk,wkhd->wbqhd", global_split, global_kv[..., :head_dim]
    )
    grad_query = (
        grad_query + mixed_sum("wbhqrk,wbhrkd->wbqhd", far_split, distant[..., :head_dim])
    ) * score_scale
    near_back = jnp.concatenate(
        [
            mixed_sum("wbhqk,wbqhd->wbkhd", near_split, queries) * score_scale,
            mixed_sum("wbhqk,wbqhd->wbkhd", near_probs, grad_attended),
        ],
        axis=4,
    )
    global_back = jnp.concatenate(
        [
            mixed_sum("wbhqk,wbqhd->wkhd", global_split, queries) * score_scale,
            mixed_sum("wbhqk,wbqhd->wkhd", global_probs, grad_attended),
        ],
        axis=3,
    )
    far_back = jnp.concatenate(
        [
            mixed_sum("wbhqrk,wbqhd->wbhrkd", far_split, queries) * score_scale,
            mixed_sum("wbhqrk,wbqhd->wbhrkd", far_probs, grad_attended),
        ],
        axis=5,
    )
    full_grad_probs = mixed_sum("wqhd,wkhd->whqk", rows_grad, value_part)
    partial_dot = jnp.sum(full_probs * full_grad_probs, axis=3, keepdims=True)
    row_dot = lax.psum(partial_dot, SEQ)
    full_grad_scores = (full_probs * (full_grad_probs - row_dot)).astype(jnp.bfloat16)
    query_part = mixed_sum("whqk,wkhd->wqhd", full_grad_scores, key_part) * score_scale
    full_key_grad = mixed_sum("whqk,wqhd->wkhd", full_grad_scores, global_queries) * score_scale
    full_value_grad = mixed_sum("whqk,wqhd->wkhd", full_probs.astype(jnp.bfloat16), rows_grad)
    grad_paired, query_total = return_blocks(
        near_back, global_back, far_back, query_part, sender, picker, owned_hot
    )
    grad_query = grad_query + exact_two(
        "wgb,wgqhd->wbqhd", owned_hot, query_total.reshape(windows, -1, BLOCK, head_count, head_dim)
    )
    grad_paired = grad_paired + jnp.concatenate([full_key_grad, full_value_grad], axis=3)
    return (grad_query, grad_paired)


def layer_backward(stored, grad_output, weights, tables):
    row_weights, down_weights, vector_weights = weights
    sender, picker, owned_hot, key_mask, full_mask = tables
    (
        hidden,
        normed,
        queries,
        sliding,
        global_kv,
        distant,
        probabilities,
        mixed_low,
        middle,
        normed_two,
        up_value,
        active,
        key_part,
        value_part,
        global_queries,
        full_probs,
    ) = stored
    model_width = row_weights.shape[0]
    windows, tokens, _ = hidden.shape
    blocks_dev = tokens // BLOCK
    head_dim = model_width // HEADS
    (
        gain_one,
        shift_one,
        bias_query,
        bias_value,
        bias_out,
        gain_two,
        shift_two,
        bias_down,
        bias_up,
    ) = split_vectors(vector_weights, model_width)
    grad_ffn = grad_output.astype(jnp.bfloat16)
    grad_bias_down = jnp.sum(grad_ffn.astype(jnp.float32), axis=(0, 1))
    grad_down = mixed_sum("wtf,wtd->fd", active, grad_ffn)
    grad_active = mixed_sum("wtd,fd->wtf", grad_ffn, down_weights)
    gelu_pull = jax.vjp(partial(jax.nn.gelu, approximate=False), up_value)[1]
    grad_up = gelu_pull(grad_active)[0].astype(jnp.bfloat16)
    grad_bias_up = jnp.sum(grad_up.astype(jnp.float32), axis=(0, 1))
    grad_in = mixed_sum("wtd,wtf->df", normed_two, grad_up)
    grad_normed_two = mixed_sum("wtf,df->wtd", grad_up, row_weights[:, 4 * model_width :])
    norm_pull_two = jax.vjp(norm_rows, middle, gain_two, shift_two)[1]
    grad_middle_norm, grad_gain_two, grad_shift_two = norm_pull_two(grad_normed_two)
    grad_middle = grad_output + grad_middle_norm
    grad_branch = grad_middle.astype(jnp.bfloat16)
    grad_bias_out = jnp.sum(grad_branch.astype(jnp.float32), axis=(0, 1))
    grad_out_weight = mixed_sum("wtd,wte->de", mixed_low, grad_branch)
    grad_attended = mixed_sum(
        "wte,de->wtd", grad_branch, row_weights[:, 3 * model_width : 4 * model_width]
    ).astype(jnp.bfloat16)
    grad_attended = grad_attended.reshape(windows, blocks_dev, BLOCK, HEADS, head_dim)
    grad_query, grad_paired = attention_back(
        grad_attended,
        queries,
        sliding,
        global_kv,
        distant,
        probabilities,
        key_part,
        value_part,
        global_queries,
        full_probs,
        sender,
        picker,
        owned_hot,
    )
    grad_projected = jnp.concatenate(
        [
            grad_query.reshape(windows, tokens, model_width),
            grad_paired[..., :head_dim].reshape(windows, tokens, model_width),
            grad_paired[..., head_dim:].reshape(windows, tokens, model_width),
        ],
        axis=2,
    ).astype(jnp.bfloat16)
    summed = jnp.sum(grad_projected.astype(jnp.float32), axis=(0, 1))
    grad_bias_query = summed[:model_width]
    grad_bias_value = summed[2 * model_width :]
    grad_projection = mixed_sum("wtd,wte->de", normed, grad_projected)
    grad_normed = mixed_sum("wte,de->wtd", grad_projected, row_weights[:, : 3 * model_width])
    norm_pull_one = jax.vjp(norm_rows, hidden, gain_one, shift_one)[1]
    grad_hidden_norm, grad_gain_one, grad_shift_one = norm_pull_one(grad_normed)
    grad_hidden = grad_middle + grad_hidden_norm
    grad_rows = jnp.concatenate([grad_projection, grad_out_weight, grad_in], axis=1)
    grad_vectors = jnp.concatenate(
        [
            grad_gain_one,
            grad_shift_one,
            grad_bias_query,
            grad_bias_value,
            grad_bias_out,
            grad_gain_two,
            grad_shift_two,
            grad_bias_down,
            grad_bias_up,
        ]
    )
    return (grad_hidden, (grad_rows, grad_down, grad_vectors))


def adam_update(master, first_old, second_old, gradient, step_rate, decay_rate):
    first_new = 0.5 * first_old + 0.5 * gradient
    second_new = 0.5 * second_old + 0.5 * gradient * gradient
    first_hat = first_new / (1.0 - 0.5**STEP)
    second_hat = second_new / (1.0 - 0.5**STEP)
    master_new = master - step_rate * (
        first_hat / (jnp.sqrt(second_hat) + 1e-08) + decay_rate * master
    )
    return (master_new, first_new, second_new)


def general_shards(
    block_input,
    cotangent,
    random_ids,
    segment_ids,
    global_ids,
    w_rows,
    w_rows_first,
    w_rows_second,
    w_down,
    w_down_first,
    w_down_second,
    vectors,
    vectors_first,
    vectors_second,
):
    section_index = lax.axis_index(SECTION)
    seq_place = lax.axis_index(SEQ)
    groups = lax.axis_size(SEQ)
    row_weights, down_weights, vector_low = (
        lax.all_gather(w_rows[0].astype(jnp.bfloat16), (DP, SEQ), axis=1, tiled=True),
        lax.all_gather(w_down[0].astype(jnp.bfloat16), (DP, SEQ), axis=0, tiled=True),
        lax.all_gather(vectors[0].astype(jnp.bfloat16), (DP, SEQ), axis=0, tiled=True),
    )
    weights = (row_weights, down_weights, vector_low.astype(jnp.float32))
    micro_count, windows, tokens, model_width = block_input.shape
    received = jnp.zeros((windows, tokens, model_width), jnp.bfloat16)
    results = jnp.zeros(block_input.shape, jnp.float32)
    full_totals = (
        jnp.zeros(row_weights.shape, jnp.float32),
        jnp.zeros(down_weights.shape, jnp.float32),
        jnp.zeros(vector_low.shape, jnp.float32),
    )

    def tick(tick_index, carry):
        received, results, full_totals = carry
        forward_mb = jnp.clip(tick_index - section_index, 0, micro_count - 1)
        behind_raw = tick_index - 2 + section_index
        behind = jnp.clip(behind_raw, 0, micro_count - 1)
        live_mask = ((behind_raw >= 0) & (behind_raw < micro_count)).astype(jnp.float32)
        tables_forward = route_tables(
            lax.dynamic_index_in_dim(random_ids, forward_mb, 0, keepdims=False),
            lax.dynamic_index_in_dim(segment_ids, forward_mb, 0, keepdims=False),
            lax.dynamic_index_in_dim(global_ids, forward_mb, 0, keepdims=False),
            seq_place,
            groups,
        )
        tables_behind = route_tables(
            lax.dynamic_index_in_dim(random_ids, behind, 0, keepdims=False),
            lax.dynamic_index_in_dim(segment_ids, behind, 0, keepdims=False),
            lax.dynamic_index_in_dim(global_ids, behind, 0, keepdims=False),
            seq_place,
            groups,
        )
        incoming_values = received.astype(jnp.float32)
        first_input = lax.dynamic_index_in_dim(block_input, forward_mb, 0, keepdims=False).astype(
            jnp.float32
        )
        forward_input = jnp.where(section_index == 0, first_input, incoming_values)
        forward_output = layer_forward(forward_input, weights, tables_forward)[0]
        back_source = lax.dynamic_index_in_dim(block_input, behind, 0, keepdims=False).astype(
            jnp.float32
        )
        back_input = jnp.where(section_index == 0, back_source, incoming_values)
        given_grad = lax.dynamic_index_in_dim(cotangent, behind, 0, keepdims=False).astype(
            jnp.float32
        )
        back_grad = jnp.where(section_index == 0, incoming_values, given_grad) * live_mask
        stored = layer_forward(back_input, weights, tables_behind)[1]
        grad_input, gradients = layer_backward(stored, back_grad, weights, tables_behind)
        outgoing = jnp.where(section_index == 0, forward_output, grad_input).astype(jnp.bfloat16)
        finished = jnp.where(section_index == 0, grad_input, forward_output)
        updated = lax.dynamic_update_index_in_dim(results, finished, behind, 0)
        results = jnp.where(live_mask > 0, updated, results)
        full_totals = tuple(
            (total_part + grad_part for total_part, grad_part in zip(full_totals, gradients))
        )
        return (partner(outgoing, SECTION, 0), results, full_totals)

    received, results, full_totals = lax.fori_loop(
        0, micro_count + 2, tick, (received, results, full_totals)
    )
    shard_totals = (
        lax.psum_scatter(full_totals[0], (DP, SEQ), scatter_dimension=1, tiled=True),
        lax.psum_scatter(full_totals[1], (DP, SEQ), scatter_dimension=0, tiled=True),
        lax.psum_scatter(full_totals[2], (DP, SEQ), scatter_dimension=0, tiled=True),
    )
    new_rows, new_rows_first, new_rows_second = adam_update(
        w_rows[0], w_rows_first[0], w_rows_second[0], shard_totals[0], rate_matrix, decay_matrix
    )
    new_down, new_down_first, new_down_second = adam_update(
        w_down[0], w_down_first[0], w_down_second[0], shard_totals[1], rate_matrix, decay_matrix
    )
    new_vectors, new_vectors_first, new_vectors_second = adam_update(
        vectors[0], vectors_first[0], vectors_second[0], shard_totals[2], rate_vector, 0.0
    )
    return (
        results[None],
        new_rows[None],
        new_rows_first[None],
        new_rows_second[None],
        new_down[None],
        new_down_first[None],
        new_down_second[None],
        new_vectors[None],
        new_vectors_first[None],
        new_vectors_second[None],
    )


LOW = jnp.bfloat16
LOG_HIGH = [float(np.log(c).astype(ml_dtypes.bfloat16)) for c in (1.0, 2.0, 3.0)]
LOG_LOW = [float(np.log(c)) - high for c, high in zip((1.0, 2.0, 3.0), LOG_HIGH)]
CHUNK = 256
VMEM_BYTES = 48 * 1024 * 1024


def dot_rows(left, right):
    return lax.dot_general(left, right, (((1,), (1,)), ((), ())), preferred_element_type=jnp.float32)


def dot_plain(left, right):
    return lax.dot_general(left, right, (((1,), (0,)), ((), ())), preferred_element_type=jnp.float32)


def dot_tokens(left, right):
    return lax.dot_general(left, right, (((0,), (0,)), ((), ())), preferred_element_type=jnp.float32)


def key_features(random_rows, segments, global_rows):
    blocks, head_count, _ = random_rows.shape
    index = jnp.arange(blocks)
    near = (jnp.abs(index[:, None] - index[None, :]) <= 1).astype(jnp.int32)
    named = jnp.sum((global_rows[:, None] == index[None, :]).astype(jnp.int32), axis=0)
    far = jnp.sum((random_rows[..., None] == index).astype(jnp.int32), axis=2)
    count = near[:, None, :] + named[None, None, :] + far
    count = jnp.where(named[:, None, None] > 0, 1, count)
    high = jnp.where(count == 0, masked, 0.0)
    low = jnp.zeros_like(high)
    for times in (2, 3):
        high = jnp.where(count == times, LOG_HIGH[times - 1], high)
        low = jnp.where(count == times, LOG_LOW[times - 1], low)
    width = -(-(2 * blocks + 6) // 128) * 128
    tokens = segments.shape[0]
    segment_hot = (segments[:, None] == jnp.arange(3)).astype(jnp.float32)
    table = jnp.concatenate([high, low], axis=2).transpose(1, 0, 2)
    spread = jnp.broadcast_to(
        table[:, :, None, :], (head_count, blocks, BLOCK, 2 * blocks)
    ).reshape(head_count, tokens, 2 * blocks)
    query_side = jnp.concatenate(
        [
            spread,
            jnp.broadcast_to(segment_hot, (head_count, tokens, 3)),
            jnp.zeros((head_count, tokens, width - 2 * blocks - 3), jnp.float32),
        ],
        axis=2,
    ).astype(LOW)
    block_hot = (jnp.arange(tokens)[:, None] // BLOCK == index).astype(jnp.float32)
    key_side = jnp.concatenate(
        [
            block_hot,
            block_hot,
            masked * (1.0 - segment_hot),
            jnp.ones((tokens, 3), jnp.float32),
            jnp.zeros((tokens, width - 2 * blocks - 6), jnp.float32),
        ],
        axis=1,
    ).astype(LOW)
    return query_side, key_side


def attend_kernel(q_ref, k_ref, v_ref, qa_ref, ka_ref, out_ref, lse_ref):
    tokens, pair = q_ref.shape
    left = lax.broadcasted_iota(jnp.int32, (CHUNK, pair), 1) < pair // 2
    keys = jnp.concatenate([k_ref[...], ka_ref[...]], axis=1)
    values = v_ref[...]

    def step(index, carry):
        rows = pl.ds(pl.multiple_of(index * CHUNK, CHUNK), CHUNK)
        queries = q_ref[rows, :] * 0.125
        outs, tops = [], []
        for head in range(2):
            mine = left if head == 0 else jnp.logical_not(left)
            side = jnp.where(mine, queries, jnp.zeros_like(queries))
            scores = dot_rows(jnp.concatenate([side, qa_ref[head, rows, :]], axis=1), keys)
            top = jnp.max(scores, axis=1, keepdims=True)
            weight = jnp.exp(scores - top)
            total = jnp.sum(weight, axis=1, keepdims=True)
            outs.append(dot_plain(weight.astype(LOW), values) / total)
            tops.append(top + jnp.log(total))
        out_ref[rows, :] = jnp.where(left, outs[0], outs[1]).astype(LOW)
        lse_ref[rows, :] = jnp.where(left, tops[0], tops[1])
        return carry

    lax.fori_loop(0, tokens // CHUNK, step, 0)


def attend(projected, query_side, key_side, width):
    tokens = projected.shape[0]
    pairs = width // 128
    features = key_side.shape[1]
    return pl.pallas_call(
        attend_kernel,
        grid=(pairs,),
        in_specs=[
            pl.BlockSpec((tokens, 128), lambda p: (0, p)),
            pl.BlockSpec((tokens, 128), lambda p: (0, pairs + p)),
            pl.BlockSpec((tokens, 128), lambda p: (0, 2 * pairs + p)),
            pl.BlockSpec((2, tokens, features), lambda p: (p, 0, 0)),
            pl.BlockSpec((tokens, features), lambda p: (0, 0)),
        ],
        out_specs=[
            pl.BlockSpec((tokens, 128), lambda p: (0, p)),
            pl.BlockSpec((tokens, 128), lambda p: (0, p)),
        ],
        out_shape=[
            jax.ShapeDtypeStruct((tokens, width), LOW),
            jax.ShapeDtypeStruct((tokens, width), jnp.float32),
        ],
        compiler_params=pltpu.CompilerParams(vmem_limit_bytes=VMEM_BYTES),
        cost_estimate=pl.CostEstimate(
            flops=16 * pairs * tokens * tokens * 128,
            bytes_accessed=tokens * width * 16,
            transcendentals=2 * pairs * tokens * tokens,
        ),
    )(projected, projected, projected, query_side, key_side)


def three_terms(values):
    high = values.astype(LOW).astype(jnp.float32)
    rest = values - high
    middle = rest.astype(LOW).astype(jnp.float32)
    return high, middle, rest - middle


def attend_back_kernel(
    q_ref, k_ref, v_ref, do_ref, o_ref, lse_ref, qa_ref, ka_ref, grad_ref, dk_acc, dv_acc
):
    tokens, pair = q_ref.shape
    features = ka_ref.shape[1]
    pairs = pl.num_programs(0)
    place = pl.program_id(0)
    blocks = tokens // BLOCK
    first = 2 * blocks + 3
    left = lax.broadcasted_iota(jnp.int32, (CHUNK, pair), 1) < pair // 2
    lane = lax.broadcasted_iota(jnp.int32, (CHUNK, features), 1)
    lane_pair = lax.broadcasted_iota(jnp.int32, (CHUNK, pair), 1)
    keys = jnp.concatenate([k_ref[...], ka_ref[...]], axis=1)
    turned = jnp.transpose(k_ref[...].astype(jnp.float32)).astype(LOW)
    ones = (lax.broadcasted_iota(jnp.int32, (tokens, pair), 1) < 3).astype(jnp.float32).astype(LOW)
    values = jnp.concatenate([v_ref[...], ones], axis=1)
    dk_acc[...] = jnp.zeros_like(dk_acc)
    dv_acc[...] = jnp.zeros_like(dv_acc)
    column = pl.multiple_of(place * 128, 128)

    def step(index, carry):
        rows = pl.ds(pl.multiple_of(index * CHUNK, CHUNK), CHUNK)
        queries = q_ref[rows, :] * 0.125
        grads = do_ref[rows, :]
        product = grads.astype(jnp.float32) * o_ref[rows, :].astype(jnp.float32)
        parts = []
        for head in range(2):
            mine = left if head == 0 else jnp.logical_not(left)
            level = lse_ref[rows, head * 64 : head * 64 + 1]
            inner = jnp.sum(jnp.where(mine, product, 0.0), axis=1, keepdims=True)
            side = qa_ref[head, rows, :].astype(jnp.float32)
            for spot, term in enumerate(three_terms(level)):
                side = jnp.where(lane == first + spot, -term, side)
            query_side = jnp.where(mine, queries, jnp.zeros_like(queries))
            grad_side = jnp.where(mine, grads, jnp.zeros_like(grads))
            tail = jnp.zeros((CHUNK, pair), jnp.float32)
            for spot, term in enumerate(three_terms(inner)):
                tail = jnp.where(lane_pair == spot, -term, tail)
            probs = jnp.exp(
                dot_rows(keys, jnp.concatenate([query_side, side.astype(LOW)], axis=1))
            )
            change = dot_rows(values, jnp.concatenate([grad_side, tail.astype(LOW)], axis=1))
            grad_scores = (probs * change).astype(LOW)
            dv_acc[...] += dot_plain(probs.astype(LOW), grad_side)
            dk_acc[...] += dot_plain(grad_scores, query_side)
            parts.append(dot_plain(turned, grad_scores))
        half = pair // 2
        joined = jnp.concatenate([parts[0][:half], parts[1][half:]], axis=0)
        grad_ref[rows, pl.ds(column, 128)] = (jnp.transpose(joined) * 0.125).astype(LOW)
        return carry

    lax.fori_loop(0, tokens // CHUNK, step, 0)
    key_column = pl.multiple_of((pairs + place) * 128, 128)
    value_column = pl.multiple_of((2 * pairs + place) * 128, 128)
    grad_ref[:, pl.ds(key_column, 128)] = dk_acc[...].astype(LOW)
    grad_ref[:, pl.ds(value_column, 128)] = dv_acc[...].astype(LOW)


def attend_back(projected, grad_attended, attended, levels, query_side, key_side):
    tokens, width = attended.shape
    pairs = width // 128
    features = key_side.shape[1]
    return pl.pallas_call(
        attend_back_kernel,
        grid=(pairs,),
        in_specs=[
            pl.BlockSpec((tokens, 128), lambda p: (0, p)),
            pl.BlockSpec((tokens, 128), lambda p: (0, pairs + p)),
            pl.BlockSpec((tokens, 128), lambda p: (0, 2 * pairs + p)),
            pl.BlockSpec((tokens, 128), lambda p: (0, p)),
            pl.BlockSpec((tokens, 128), lambda p: (0, p)),
            pl.BlockSpec((tokens, 128), lambda p: (0, p)),
            pl.BlockSpec((2, tokens, features), lambda p: (p, 0, 0)),
            pl.BlockSpec((tokens, features), lambda p: (0, 0)),
        ],
        out_specs=pl.BlockSpec((tokens, 3 * width), lambda p: (0, 0)),
        out_shape=jax.ShapeDtypeStruct((tokens, 3 * width), LOW),
        scratch_shapes=[
            pltpu.VMEM((tokens, 128), jnp.float32),
            pltpu.VMEM((tokens, 128), jnp.float32),
        ],
        compiler_params=pltpu.CompilerParams(vmem_limit_bytes=VMEM_BYTES),
        cost_estimate=pl.CostEstimate(
            flops=40 * pairs * tokens * tokens * 128,
            bytes_accessed=tokens * width * 24,
            transcendentals=2 * pairs * tokens * tokens,
        ),
    )(projected, projected, projected, grad_attended, attended, levels, query_side, key_side)


def swap(value):
    return lax.ppermute(value, SECTION, [(0, 1), (1, 0)])


def normalized(values_in):
    row_mean = jnp.mean(values_in, axis=-1, keepdims=True)
    centred = values_in - row_mean
    spread = jnp.mean(centred * centred, axis=-1, keepdims=True)
    scale = lax.rsqrt(spread + epsilon)
    return centred * scale, scale


def norm_back(values_in, incoming, gain_vec):
    unit, scale = normalized(values_in)
    grad_gain = jnp.sum(incoming * unit, axis=0)
    grad_shift = jnp.sum(incoming, axis=0)
    p = incoming * gain_vec
    mean_p = jnp.mean(p, axis=-1, keepdims=True)
    mean_pn = jnp.mean(p * unit, axis=-1, keepdims=True)
    return scale * (p - mean_p - unit * mean_pn), grad_gain, grad_shift


class Shares:
    def __init__(self, width, columns, depth, vector_len):
        self.width = width
        self.columns = columns
        self.depth = depth
        self.vector_len = vector_len
        self.half = columns // 2
        self.per = width // columns
        self.groups = columns // depth

    def unpack(self, gathered, core):
        half, per, width = self.half, self.per, self.width
        rows = gathered[0].reshape(-1, half, width)
        proj = rows[: 3 * per].reshape(3 * per * half, width)
        out = (
            rows[3 * per : 4 * per]
            .reshape(per, half, 2, per * half)
            .transpose(0, 2, 1, 3)
            .reshape(width, per * half)
        )
        up = rows[4 * per :].reshape(-1, width)
        down = gathered[1].reshape(-1, width)
        vec = gathered[2].reshape(-1, TAIL, width)[:, 0, : self.vector_len].reshape(-1)
        pieces = split_vectors(vec.astype(jnp.float32), width)
        bias_query, bias_value = self.vector_half(pieces[2], core), self.vector_half(pieces[3], core)
        bias_up = lax.dynamic_index_in_dim(
            pieces[8].reshape(-1, 2, self.depth // 2), core, 1, keepdims=False
        ).reshape(-1)
        return (
            (proj, out, up, down),
            (pieces[0], pieces[1], bias_query, bias_value, pieces[4], pieces[5], pieces[6])
            + (pieces[7], bias_up),
        )

    def vector_half(self, vec, core):
        return lax.dynamic_index_in_dim(
            vec.reshape(self.per, 2, self.half), core, 1, keepdims=False
        ).reshape(-1)

    def by_shard(self, grads, vector_grads, core):
        proj, out, up, down = grads
        half, per, width = self.half, self.per, self.width
        out = (
            out.reshape(per, 2, half, per * half).transpose(0, 2, 1, 3).reshape(per, half, width)
        )
        hot = (jnp.arange(2) == core).astype(jnp.float32)
        spread = list(vector_grads)
        for index in (2, 3):
            spread[index] = (
                spread[index].reshape(per, 1, half) * hot[None, :, None]
            ).reshape(-1)
        spread[8] = (spread[8].reshape(-1, 1, self.depth // 2) * hot[None, :, None]).reshape(-1)
        for index in (0, 1, 4, 5, 6, 7):
            spread[index] = spread[index] * hot[0]
        vec = jnp.concatenate(spread).reshape(-1, 1, self.vector_len)
        vec = jnp.pad(vec, ((0, 0), (0, TAIL - 1), (0, width - self.vector_len))).astype(LOW)
        return (
            proj.reshape(-1, half, width),
            out,
            up.reshape(2, 4, half, width),
            down.reshape(2, 2, 4, self.depth // 2, width),
            vec.reshape(2, 2, 4, TAIL, width),
        )


MESH = pl.DeviceIdType.MESH
PIECE = 48
TAIL = 16


def prepare_kernel(shares, rows_ref, down_ref, vector_ref, rows_out, down_out, vector_out):
    core = lax.axis_index(SECTION)
    offset = lax.axis_index((DP, SEQ)) * shares.columns
    half, per, width, depth = shares.half, shares.per, shares.width, shares.depth // 2
    is_inner = (offset >= 3 * width) & (offset < 4 * width)
    is_hidden = offset >= 4 * width

    @pl.when(is_inner)
    def _():
        for which in range(2):
            side = core if which == 0 else 1 - core
            held = [rows_ref[pl.ds((2 * j + side) * half, half), :] for j in range(per)]
            turned = jnp.transpose(jnp.concatenate(held, axis=0))
            rows_out[which] = jnp.concatenate([turned[:half], turned[half:]], axis=1).astype(LOW)

    @pl.when(jnp.logical_not(is_inner))
    def _():
        turned = jnp.transpose(rows_ref[...]).astype(LOW)
        plain = [turned[:half], turned[half:]]
        hidden = [
            jnp.concatenate(
                [turned[(2 * j + side) * depth :][:depth] for j in range(shares.groups)], axis=0
            )
            for side in range(2)
        ]
        halves = [jnp.where(is_hidden, b, a) for a, b in zip(plain, hidden)]
        rows_out[0] = jnp.where(core == 0, halves[0], halves[1])
        rows_out[1] = jnp.where(core == 0, halves[1], halves[0])

    down = down_ref[...].astype(LOW)
    down_out[0] = jnp.where(core == 0, down[:depth], down[depth:])
    down_out[1] = jnp.where(core == 0, down[depth:], down[:depth])
    vector_out[...] = jnp.zeros_like(vector_out)
    vector_out[0:1, : shares.vector_len] = vector_ref[...].astype(LOW)


def prepare(shares, rows, down, vector):
    return pl.pallas_call(
        partial(prepare_kernel, shares),
        out_shape=[
            jax.ShapeDtypeStruct((2, shares.half, shares.width), LOW),
            jax.ShapeDtypeStruct((2, shares.depth // 2, shares.width), LOW),
            jax.ShapeDtypeStruct((TAIL, shares.width), LOW),
        ],
        compiler_params=pltpu.CompilerParams(vmem_limit_bytes=VMEM_BYTES),
    )(rows, down, vector)


class Place:
    def __init__(self):
        self.core = lax.axis_index(SECTION)
        self.dp = lax.axis_index(DP)
        self.z = lax.axis_index(SEQ)
        self.y, self.x = self.dp // 2, self.dp % 2
        self.high, self.low = self.z // 2, self.z % 2
        self.partner = {SECTION: 1 - self.core}
        self.along_x = {DP: 2 * self.y + 1 - self.x}
        self.along_y = {DP: 2 * (1 - self.y) + self.x}
        self.along_high = {SEQ: 2 * (1 - self.high) + self.low}
        self.along_low = {SEQ: 2 * self.high + 1 - self.low}
        self.others = [{SEQ: (self.z + by) % 4} for by in (1, 2, 3)]

    def greet(self):
        barrier = pltpu.get_barrier_semaphore()
        everyone = [self.partner, self.along_x, self.along_y] + self.others
        for device in everyone:
            pl.semaphore_signal(barrier, inc=1, device_id=device, device_id_type=MESH)
        pl.semaphore_wait(barrier, len(everyone))


def remote(src, dst, sems, spot, device):
    return pltpu.make_async_remote_copy(
        src_ref=src,
        dst_ref=dst,
        send_sem=sems[0].at[spot],
        recv_sem=sems[1].at[spot],
        device_id=device,
        device_id_type=MESH,
    )


def chunk_pairs(shares):
    pairs = []
    for array, length in ((0, shares.half), (1, shares.depth // 2)):
        for start in range(0, length, 2 * PIECE):
            pairs.append([(array, start, PIECE, 0), (array, start + PIECE, PIECE, 1)])
    pairs[0].append((2, 0, TAIL, 0))
    return pairs


def gather_kernel(shares, micro, *refs):
    (rows_in, down_in, vector_in, x_in, cot_in), refs = refs[:5], refs[5:]
    outs, refs = [refs[0:3], refs[3:6]], refs[6:]
    (x_out, cot_out), refs = refs[:2], refs[2:]
    local, swap_send, swap_recv, z_send, z_recv, send, recv = refs
    here = Place()
    core, y, x, z = here.core, here.y, here.x, here.z
    half = x_in.shape[2] // 2
    here.greet()

    kept = [rows_in.at[0], down_in.at[0], vector_in]
    given = [rows_in.at[1], down_in.at[1], vector_in]

    def slices(source, target, base):
        mine = pl.ds(pl.multiple_of(core * half, half), half)
        own = pltpu.make_async_copy(
            source.at[z, 0, mine], target.at[z, core], local.at[6 + base // 4]
        )
        sends = [
            remote(
                source.at[(z + by) % 4, 0, mine],
                target.at[z, core],
                (z_send, z_recv),
                base + by - 1,
                here.others[by - 1],
            )
            for by in (1, 2, 3)
        ]
        arrivals = [
            remote(
                source.at[z, 0, mine],
                target.at[(z + 4 - by) % 4, core],
                (z_send, z_recv),
                base + by - 1,
                here.others[by - 1],
            )
            for by in (1, 2, 3)
        ]
        forward = remote(
            target.at[:, core], target.at[:, core], (z_send, z_recv), base + 3, here.partner
        )
        arrived = remote(
            target.at[:, 1 - core], target.at[:, 1 - core], (z_send, z_recv), base + 3, here.partner
        )
        return own, sends, arrivals, forward, arrived

    x_moves = slices(x_in, x_out, 0)
    cot_moves = slices(cot_in, cot_out, 4)

    def open_slices(moves):
        moves[0].start()
        for copy in moves[1]:
            copy.start()

    def pass_slices(moves):
        moves[0].wait()
        for copy in moves[2]:
            copy.wait_recv()
        moves[3].start()

    def close_slices(moves):
        for copy in moves[1]:
            copy.wait_send()
        moves[3].wait_send()
        moves[4].wait_recv()

    for layer in range(2):

        @pl.when(core == layer)
        def _():
            own, across = [], []
            for index in range(3):
                spot = outs[layer][index].at[y, x, z]
                own.append(pltpu.make_async_copy(kept[index], spot, local.at[index]))
                across.append(
                    remote(given[index], spot, (swap_send, swap_recv), index, here.partner)
                )
            for copy in across + own:
                copy.start()
            for index in range(3):
                own[index].wait()
                across[index].wait_send()
                spot = outs[1 - layer][index].at[y, x, z]
                remote(given[index], spot, (swap_send, swap_recv), index, here.partner).wait_recv()

    open_slices(x_moves)

    phases = {}
    pairs = []
    for layer in range(2):
        for pair in chunk_pairs(shares):
            entry = []
            for array, start, length, order in pair:
                ref = outs[layer][array]
                rows = pl.ds(start, length)
                number = len(phases)
                steps = [
                    (ref.at[y, x, pl.ds(z, 1), rows], here.along_low),
                    (ref.at[y, x, pl.ds(2 * here.high, 2), rows], here.along_high),
                ]
                arrive = [
                    ref.at[y, x, pl.ds(2 * here.high + 1 - here.low, 1), rows],
                    ref.at[y, x, pl.ds(2 * (1 - here.high), 2), rows],
                ]
                if order == 0:
                    steps.append((ref.at[y, x, :, rows], here.along_y))
                    steps.append((ref.at[:, x, :, rows], here.along_x))
                    arrive.append(ref.at[1 - y, x, :, rows])
                    arrive.append(ref.at[:, 1 - x, :, rows])
                else:
                    steps.append((ref.at[y, x, :, rows], here.along_x))
                    steps.append((ref.at[y, :, :, rows], here.along_y))
                    arrive.append(ref.at[y, 1 - x, :, rows])
                    arrive.append(ref.at[1 - y, :, :, rows])
                phases[number] = [
                    (
                        remote(piece, piece, (send, recv), (number, phase), device),
                        remote(landing, landing, (send, recv), (number, phase), device),
                    )
                    for phase, ((piece, device), landing) in enumerate(zip(steps, arrive))
                ]
                entry.append(number)
            pairs.append(entry)

    for tick in range(len(pairs) + 3):
        for phase in (3, 2, 1, 0):
            if 0 <= tick - phase < len(pairs):
                for number in pairs[tick - phase]:
                    if phase:
                        phases[number][phase - 1][1].wait_recv()
                    phases[number][phase][0].start()
        if tick == 1:
            pass_slices(x_moves)
            open_slices(cot_moves)
        if tick == 5:
            pass_slices(cot_moves)
    for entry in pairs:
        for number in entry:
            phases[number][3][1].wait_recv()
            for phase in range(4):
                phases[number][phase][0].wait_send()
    close_slices(x_moves)
    close_slices(cot_moves)


def gather(shares, prepared, block_input, cotangent):
    micro, _, tokens, width = block_input.shape
    chunks = 2 * sum(len(pair) for pair in chunk_pairs(shares))
    lengths = (shares.half, shares.depth // 2, TAIL)
    layer = [jax.ShapeDtypeStruct((2, 2, 4, rows, width), LOW) for rows in lengths]
    window = jax.ShapeDtypeStruct((micro, 2, tokens // 2, width), LOW)
    anywhere = pl.BlockSpec(memory_space=pl.ANY)
    results = pl.pallas_call(
        partial(gather_kernel, shares, micro),
        in_specs=[anywhere] * 5,
        out_specs=[anywhere] * 8,
        out_shape=layer + layer + [window, window],
        scratch_shapes=[
            pltpu.SemaphoreType.DMA((8,)),
            pltpu.SemaphoreType.DMA((3,)),
            pltpu.SemaphoreType.DMA((3,)),
            pltpu.SemaphoreType.DMA((8,)),
            pltpu.SemaphoreType.DMA((8,)),
            pltpu.SemaphoreType.DMA((chunks, 4)),
            pltpu.SemaphoreType.DMA((chunks, 4)),
        ],
        compiler_params=pltpu.CompilerParams(collective_id=0, has_side_effects=True),
    )(*prepared, block_input, cotangent)
    return results[0:3], results[3:6], results[6], results[7]


def scatter_kernel(shares, *refs):
    layers, refs = [refs[0:5], refs[5:10]], refs[10:]
    (dx_ref, final_ref, halves, slices), refs = refs[:4], refs[4:]
    work, refs = [refs[0:3], refs[3:6]], refs[6:]
    (got_one, got_two, got_three, got_four, total), refs = refs[:5], refs[5:]
    load, local, swap_send, swap_recv, z_send, z_recv, send, recv = refs
    here = Place()
    core, y, x, z = here.core, here.y, here.x, here.z
    lengths = (shares.half, shares.depth // 2, TAIL)
    bases = (0, shares.half, shares.half + shares.depth // 2)

    loads = []
    for layer in range(2):
        proj, out, up, down, vec = layers[layer]
        rows = work[layer][0]
        moves = [
            (proj.at[pl.ds(0, 4)], rows.at[0, 0]),
            (proj.at[pl.ds(4, 2)], rows.at[0, 1, pl.ds(0, 2)]),
            (out, rows.at[0, 1, pl.ds(2, 2)]),
            (up, rows.at[1]),
            (down, work[layer][1]),
            (vec, work[layer][2]),
        ]
        loads.append(
            [
                pltpu.make_async_copy(src, dst, load.at[layer, index])
                for index, (src, dst) in enumerate(moves)
            ]
        )
    for layer in (1, 0):
        for copy in loads[layer]:
            copy.start()
    here.greet()

    for section, source in ((0, dx_ref), (1, final_ref)):

        @pl.when(core == section)
        def _():
            pltpu.make_async_copy(source.at[z], slices.at[z], local.at[0]).start()
            for by in (1, 2, 3):
                remote(
                    source.at[(z + by) % 4],
                    slices.at[z],
                    (z_send, z_recv),
                    by - 1,
                    here.others[by - 1],
                ).start()

    pairs, chunks = [], []
    counts = 0
    for layer in (1, 0):
        for pair in chunk_pairs(shares):
            entry = []
            for array, start, length, order in pair:
                entry.append((len(chunks), layer, array, start, length, order))
                chunks.append(entry[-1])
            pairs.append(entry)

    def pieces(chunk):
        number, layer, array, start, length, order = chunk
        ref = work[layer][array]
        rows = pl.ds(start, length)
        own_pair = pl.ds(2 * here.high, 2)
        other_pair = pl.ds(2 * (1 - here.high), 2)
        other = pl.ds(2 * here.high + 1 - here.low, 1)
        if order == 0:
            moves = [
                (ref.at[:, 1 - x, :, rows], here.along_x, ref.at[:, x, :, rows]),
                (ref.at[1 - y, x, :, rows], here.along_y, ref.at[y, x, :, rows]),
            ]
        else:
            moves = [
                (ref.at[1 - y, :, :, rows], here.along_y, ref.at[y, :, :, rows]),
                (ref.at[y, 1 - x, :, rows], here.along_x, ref.at[y, x, :, rows]),
            ]
        moves.append((ref.at[y, x, other_pair, rows], here.along_high, ref.at[y, x, own_pair, rows]))
        moves.append((ref.at[y, x, other, rows], here.along_low, ref.at[y, x, pl.ds(z, 1), rows]))
        slots = [got.at[number, ..., pl.ds(0, length), :] for got in (got_one, got_two)]
        slots += [got.at[number, ..., pl.ds(0, length), :] for got in (got_three, got_four)]
        copies = [
            remote(src, slot, (send, recv), (number, phase), device)
            for phase, ((src, device, _), slot) in enumerate(zip(moves, slots))
        ]
        return copies, [keep for _, _, keep in moves], slots

    built = [pieces(chunk) for chunk in chunks]
    loaded = set()
    for tick in range(len(pairs) + 4):
        for phase in (4, 3, 2, 1, 0):
            if not 0 <= tick - phase < len(pairs):
                continue
            for chunk in pairs[tick - phase]:
                number, layer, array, start, length, _ = chunk
                copies, keeps, slots = built[number]
                if phase == 0 and (layer, array) not in loaded:
                    loaded.add((layer, array))
                    spots = ((0, 1, 2, 3), (4,), (5,))[array]
                    for spot in spots:
                        loads[layer][spot].wait()
                if phase:
                    copies[phase - 1].wait_recv()
                    keep, slot = keeps[phase - 1], slots[phase - 1]
                    if phase == 4:
                        spot = pl.ds(bases[array] + start, length)
                        total[layer, spot, :] = (keep[...] + slot[...])[0]
                    else:
                        keep[...] = keep[...] + slot[...]
                if phase < 4:
                    copies[phase].start()
    for copies, _, _ in built:
        for copy in copies:
            copy.wait_send()
    across = remote(total.at[1 - core], halves.at[core], (swap_send, swap_recv), 0, here.partner)
    across.start()
    own = pltpu.make_async_copy(total.at[core], halves.at[core], local.at[1])
    own.start()
    own.wait()
    across.wait_send()
    remote(
        total.at[1 - core], halves.at[1 - core], (swap_send, swap_recv), 0, here.partner
    ).wait_recv()
    pltpu.make_async_copy(dx_ref.at[z], slices.at[z], local.at[0]).wait()
    for by in (1, 2, 3):
        copy = remote(
            dx_ref.at[z], slices.at[(z + 4 - by) % 4], (z_send, z_recv), by - 1, here.others[by - 1]
        )
        copy.wait_send()
        copy.wait_recv()


def scatter(shares, layers, grad, final):
    micro, tokens, width = grad.shape
    lengths = (shares.half, shares.depth // 2, TAIL)
    chunks = 2 * sum(len(pair) for pair in chunk_pairs(shares))
    rows = sum(lengths)
    anywhere = pl.BlockSpec(memory_space=pl.ANY)
    work = [pltpu.VMEM((2, 2, 4, length, width), LOW) for length in lengths]
    return pl.pallas_call(
        partial(scatter_kernel, shares),
        in_specs=[anywhere] * 12,
        out_specs=[anywhere] * 2,
        out_shape=[
            jax.ShapeDtypeStruct((2, rows, width), LOW),
            jax.ShapeDtypeStruct((micro, tokens, width), LOW),
        ],
        scratch_shapes=work
        + work
        + [
            pltpu.VMEM((chunks, 2, 4, PIECE, width), LOW),
            pltpu.VMEM((chunks, 4, PIECE, width), LOW),
            pltpu.VMEM((chunks, 2, PIECE, width), LOW),
            pltpu.VMEM((chunks, 1, PIECE, width), LOW),
            pltpu.VMEM((2, rows, width), LOW),
            pltpu.SemaphoreType.DMA((2, 6)),
            pltpu.SemaphoreType.DMA((2,)),
            pltpu.SemaphoreType.DMA((1,)),
            pltpu.SemaphoreType.DMA((1,)),
            pltpu.SemaphoreType.DMA((3,)),
            pltpu.SemaphoreType.DMA((3,)),
            pltpu.SemaphoreType.DMA((chunks, 4)),
            pltpu.SemaphoreType.DMA((chunks, 4)),
        ],
        compiler_params=pltpu.CompilerParams(
            collective_id=1, has_side_effects=True, vmem_limit_bytes=VMEM_BYTES
        ),
    )(*layers[0], *layers[1], grad, final)


def update_kernel(shares, halves_ref, *refs):
    old, new, turned = refs[:9], refs[9:18], refs[18]
    offset = lax.axis_index((DP, SEQ)) * shares.columns
    half, per, width, depth = shares.half, shares.per, shares.width, shares.depth // 2
    is_inner = (offset >= 3 * width) & (offset < 4 * width)
    is_hidden = offset >= 4 * width

    @pl.when(is_inner)
    def _():
        for side in range(2):
            piece = halves_ref[side, :half, :].astype(jnp.float32)
            wide = per * half
            back = jnp.transpose(jnp.concatenate([piece[:, :wide], piece[:, wide:]], axis=0))
            for j in range(per):
                turned[(2 * j + side) * half : (2 * j + side + 1) * half, :] = back[
                    j * half : (j + 1) * half
                ]

    @pl.when(jnp.logical_not(is_inner))
    def _():
        pair = [halves_ref[side, :half, :].astype(jnp.float32) for side in range(2)]
        plain = jnp.concatenate(pair, axis=0)
        hidden = jnp.concatenate(
            [pair[side][j * depth :][:depth] for j in range(shares.groups) for side in range(2)],
            axis=0,
        )
        turned[...] = jnp.transpose(jnp.where(is_hidden, hidden, plain))

    def store(first, gradient, rate, decay):
        results = adam_update(*[ref[...] for ref in old[first : first + 3]], gradient, rate, decay)
        for ref, result in zip(new[first : first + 3], results):
            ref[...] = result

    store(0, turned[...], rate_matrix, decay_matrix)
    down = [halves_ref[side, half : half + depth, :] for side in range(2)]
    store(3, jnp.concatenate(down, axis=0).astype(jnp.float32), rate_matrix, decay_matrix)
    tails = [halves_ref[side, half + depth :, :].astype(jnp.float32) for side in range(2)]
    store(6, (tails[0] + tails[1])[0:1, : shares.vector_len], rate_vector, 0.0)


def update(shares, halves, old):
    return pl.pallas_call(
        partial(update_kernel, shares),
        out_shape=[jax.ShapeDtypeStruct(piece.shape, jnp.float32) for piece in old],
        scratch_shapes=[pltpu.VMEM((shares.width, shares.columns), jnp.float32)],
        compiler_params=pltpu.CompilerParams(vmem_limit_bytes=VMEM_BYTES),
    )(halves, *old)


def window_forward(hidden, weights, biases, features):
    proj, out, up, down = weights
    gain_one, shift_one, bias_query, bias_value, bias_out = biases[:5]
    gain_two, shift_two, bias_down, bias_up = biases[5:]
    unit, _ = normalized(hidden)
    normed = (unit * gain_one + shift_one).astype(LOW)
    bias = jnp.concatenate([bias_query, jnp.zeros_like(bias_query), bias_value])
    projected = (dot_rows(normed, proj) + bias).astype(LOW)
    attended, levels = attend(projected, *features, bias_query.shape[0])
    branch = dot_rows(attended, out)
    middle = hidden + (branch + swap(branch.astype(LOW)).astype(jnp.float32) + bias_out)
    unit_two, _ = normalized(middle)
    normed_two = (unit_two * gain_two + shift_two).astype(LOW)
    up_value = dot_rows(normed_two, up) + bias_up
    cdf = 0.5 * (1.0 + lax.erf(up_value * 0.5**0.5))
    active = (up_value * cdf).astype(LOW)
    slope = cdf + up_value * jnp.exp(-0.5 * up_value * up_value) * (0.5 / math.pi) ** 0.5
    part = dot_plain(active, down)
    output = middle + (part + swap(part.astype(LOW)).astype(jnp.float32) + bias_down)
    return output, (hidden, normed, projected, attended, levels, middle, normed_two, slope, active)


def window_backward(stored, grad_output, weights, biases, features):
    hidden, normed, projected, attended, levels, middle, normed_two, slope, active = stored
    proj, out, up, down = weights
    gain_one, gain_two = biases[0], biases[5]
    grad_ffn = grad_output.astype(LOW)
    grad_bias_down = jnp.sum(grad_ffn.astype(jnp.float32), axis=0)
    grad_up = (dot_rows(grad_ffn, down) * slope).astype(LOW)
    grad_bias_up = jnp.sum(grad_up.astype(jnp.float32), axis=0)
    part = dot_plain(grad_up, up)
    arrived = swap(part.astype(LOW)).astype(jnp.float32)
    down_grad = dot_tokens(active, grad_ffn).astype(LOW)
    up_grad = dot_tokens(grad_up, normed_two).astype(LOW)
    grad_norm, grad_gain_two, grad_shift_two = norm_back(middle, part + arrived, gain_two)
    grad_middle = grad_output + grad_norm
    grad_branch = grad_middle.astype(LOW)
    grad_bias_out = jnp.sum(grad_branch.astype(jnp.float32), axis=0)
    out_grad = dot_tokens(grad_branch, attended).astype(LOW)
    grad_attended = dot_plain(grad_branch, out).astype(LOW)
    grad_proj = attend_back(projected, grad_attended, attended, levels, *features)
    summed = jnp.sum(grad_proj.astype(jnp.float32), axis=0)
    width = attended.shape[1]
    part = dot_plain(grad_proj, proj)
    arrived = swap(part.astype(LOW)).astype(jnp.float32)
    proj_grad = dot_tokens(grad_proj, normed).astype(LOW)
    grad_norm, grad_gain_one, grad_shift_one = norm_back(hidden, part + arrived, gain_one)
    vector_grads = (
        grad_gain_one,
        grad_shift_one,
        summed[:width],
        summed[2 * width :],
        grad_bias_out,
        grad_gain_two,
        grad_shift_two,
        grad_bias_down,
        grad_bias_up,
    )
    return grad_middle + grad_norm, (proj_grad, out_grad, up_grad, down_grad), vector_grads


def window_shards(
    block_input,
    cotangent,
    random_ids,
    segment_ids,
    global_ids,
    w_rows,
    w_rows_first,
    w_rows_second,
    w_down,
    w_down_first,
    w_down_second,
    vectors,
    vectors_first,
    vectors_second,
):
    core = lax.axis_index(SECTION)
    place = lax.axis_index(SEQ)
    micro, _, tokens, width = block_input.shape
    _, _, columns = w_rows.shape
    shares = Shares(width, columns, w_down.shape[1], vectors.shape[1])
    prepared = prepare(shares, w_rows[0], w_down[0], vectors)
    gathered_zero, gathered_one, hidden, grad = gather(shares, prepared, block_input, cotangent)

    head_half = shares.half // (width // HEADS)
    random_rows = lax.dynamic_index_in_dim(random_ids[:, 0], place, 0, keepdims=False)
    random_rows = random_rows.reshape(random_rows.shape[0], shares.per, 2, head_half, -1)
    random_rows = lax.dynamic_index_in_dim(random_rows, core, 2, keepdims=False)
    random_rows = random_rows.reshape(random_rows.shape[0], shares.per * head_half, -1)
    segments = lax.dynamic_index_in_dim(segment_ids[:, 0], place, 0, keepdims=False)
    global_rows = lax.dynamic_index_in_dim(global_ids[:, 0], place, 0, keepdims=False)
    features = key_features(random_rows, segments, global_rows)

    params = [shares.unpack(piece, core) for piece in (gathered_zero, gathered_one)]
    hidden = hidden.reshape(-1, width).astype(jnp.float32)
    output, stored_zero = window_forward(hidden, *params[0], features)
    hidden = output.astype(LOW).astype(jnp.float32)
    final, stored_one = window_forward(hidden, *params[1], features)
    final = final.astype(LOW).reshape(micro, tokens, width)

    grad = grad.reshape(-1, width).astype(jnp.float32)
    grad, *grads_one = window_backward(stored_one, grad, *params[1], features)
    grad = grad.astype(LOW).astype(jnp.float32)
    grad, *grads_zero = window_backward(stored_zero, grad, *params[0], features)
    grad = grad.astype(LOW).reshape(micro, tokens, width)
    layers = [shares.by_shard(*grads, core) for grads in (grads_zero, grads_one)]
    halves, slices = scatter(shares, layers, grad, final)
    section_result = slices.astype(jnp.float32)[None, :, None]
    old = [
        w_rows[0],
        w_rows_first[0],
        w_rows_second[0],
        w_down[0],
        w_down_first[0],
        w_down_second[0],
        vectors,
        vectors_first,
        vectors_second,
    ]
    new = update(shares, halves, old)
    return (section_result, *[piece[None] for piece in new[:6]], *new[6:])


def one_window_each(mesh, block_input, w_rows, w_down, vectors):
    micro, windows, length, width = block_input.shape
    shards = mesh.shape[DP] * mesh.shape[SEQ]
    columns, depth = w_rows.shape[2] // shards, w_down.shape[1] // shards
    head_dim = width // HEADS
    tokens = length // mesh.shape[SEQ]
    return (
        mesh.shape[SECTION] == 2
        and mesh.shape[SEQ] == micro
        and mesh.shape[DP] == windows
        and tokens % (2 * BLOCK) == 0
        and length % CHUNK == 0
        and head_dim == 64
        and width % columns == 0
        and columns % (2 * head_dim) == 0
        and columns % depth == 0
        and width // columns * (columns // 2) % 128 == 0
        and depth % 32 == 0
        and vectors.shape[1] // shards <= width
        and mesh.shape[DP] == 4
        and micro == 4
        and width == 2 * columns
        and (columns // 2) % (2 * PIECE) == 0
        and (depth // 2) % (2 * PIECE) == 0
    )


def solution(mesh):
    in_specs = (
        P(None, DP, SEQ, None),
        P(None, DP, SEQ, None),
        P(None, DP, None, None, None),
        P(None, DP, None),
        P(None, DP, None),
        P(SECTION, None, (DP, SEQ)),
        P(SECTION, None, (DP, SEQ)),
        P(SECTION, None, (DP, SEQ)),
        P(SECTION, (DP, SEQ), None),
        P(SECTION, (DP, SEQ), None),
        P(SECTION, (DP, SEQ), None),
        P(SECTION, (DP, SEQ)),
        P(SECTION, (DP, SEQ)),
        P(SECTION, (DP, SEQ)),
    )
    out_specs = (
        P(SECTION, None, DP, SEQ, None),
        P(SECTION, None, (DP, SEQ)),
        P(SECTION, None, (DP, SEQ)),
        P(SECTION, None, (DP, SEQ)),
        P(SECTION, (DP, SEQ), None),
        P(SECTION, (DP, SEQ), None),
        P(SECTION, (DP, SEQ), None),
        P(SECTION, (DP, SEQ)),
        P(SECTION, (DP, SEQ)),
        P(SECTION, (DP, SEQ)),
    )

    def step(*arrays):
        chosen = general_shards
        if one_window_each(mesh, arrays[0], arrays[5], arrays[8], arrays[11]):
            chosen = window_shards
        return jax.shard_map(
            chosen, mesh=mesh, in_specs=in_specs, out_specs=out_specs, check_vma=False
        )(*arrays)

    return step
```

```python
import math
from functools import partial

import jax
import jax.numpy as jnp
import ml_dtypes
import numpy as np
from jax import lax
from jax.experimental import pallas as pl
from jax.experimental.pallas import tpu as pltpu
from jax.sharding import PartitionSpec as P

SECTION, DP, SEQ = "section", "dp", "seq"
HEADS = 12
BLOCK = 64
STEP = 5


epsilon = 1e-05
masked = -1e30
rate_matrix = 0.02
rate_vector = 0.2
decay_matrix = 0.01


def with_halo(x, sides, width):
    for axis, dim in sides:
        devices, length = (lax.axis_size(axis), x.shape[dim])
        up = [(i, (i + 1) % devices) for i in range(devices - 1)]
        down = [(j, i) for i, j in up]
        last = lax.slice_in_dim(x, length - width, length, axis=dim)
        initial = lax.slice_in_dim(x, 0, width, axis=dim)
        before = lax.ppermute(last, axis, up)
        after = lax.ppermute(initial, axis, down)
        x = jnp.concatenate([before, x, after], axis=dim)
    return x


def merged(value, axis, join):
    pieces = jax.tree.map(lambda part: lax.all_gather(part, axis), value)
    head = jax.tree.map(lambda part: part[0], pieces)
    tail = jax.tree.map(lambda part: part[1:], pieces)
    subtotal, _ = lax.scan(lambda subtotal, share: (join(subtotal, share), None), head, tail)
    return subtotal


def from_behind(x, axis, by):
    devices = lax.axis_size(axis)
    pairs = [(i, i + by) for i in range(devices) if 0 <= i + by < devices]
    return lax.ppermute(x, axis, pairs)


def partner(value, axis, bit):
    mask = 2**bit
    pairs = [(source, source ^ mask) for source in range(lax.axis_size(axis))]
    return lax.ppermute(value, axis, pairs)


def mixed_sum(form, left, right):
    return jnp.einsum(form, left, right, preferred_element_type=jnp.float32)


def exact_two(form, left, right):
    return jnp.einsum(
        form, left, right, precision=lax.Precision.HIGHEST, preferred_element_type=jnp.float32
    )


def norm_rows(values_in, gain_vec, shift_vec):
    row_mean = jnp.mean(values_in, axis=-1, keepdims=True)
    centred = values_in - row_mean
    spread = jnp.mean(centred * centred, axis=-1, keepdims=True)
    return centred * lax.rsqrt(spread + epsilon) * gain_vec + shift_vec


def split_vectors(vector_weights, model_width):
    pieces = [
        vector_weights[piece_index * model_width : (piece_index + 1) * model_width]
        for piece_index in range(8)
    ]
    return pieces + [vector_weights[8 * model_width :]]


def route_tables(random_rows, segments, global_rows, seq_place, groups):
    windows, blocks, head_count, pick_count = random_rows.shape
    blocks_dev = blocks // groups
    request_count = blocks_dev * head_count * pick_count
    capacity = -(-request_count // groups)
    requests = random_rows.reshape(windows, groups, request_count)
    owners = requests // blocks_dev
    inside = requests % blocks_dev
    head_of = jnp.arange(request_count) // pick_count % head_count
    is_mine = owners == seq_place
    slot_index = jnp.cumsum(is_mine.astype(jnp.int32), axis=2) - 1
    slot_hot = ((slot_index[..., None] == jnp.arange(capacity)) & is_mine[..., None]).astype(
        jnp.float32
    )
    inside_hot = (inside[..., None] == jnp.arange(blocks_dev)).astype(jnp.float32)
    head_hot = (head_of[:, None] == jnp.arange(head_count)).astype(jnp.float32)
    sender = jnp.einsum(
        "wqsc,wqsb,sh->wqcbh", slot_hot, inside_hot, head_hot, precision=lax.Precision.HIGHEST
    )
    my_owners = lax.dynamic_index_in_dim(owners, seq_place, axis=1, keepdims=False)
    earlier = jnp.arange(request_count)[None, :] < jnp.arange(request_count)[:, None]
    same_owner = my_owners[:, :, None] == my_owners[:, None, :]
    rank_index = jnp.sum((same_owner & earlier[None]).astype(jnp.int32), axis=2)
    picker = (
        (my_owners[..., None, None] == jnp.arange(groups)[:, None])
        & (rank_index[..., None, None] == jnp.arange(capacity)[None, :])
    ).astype(jnp.float32)
    first_block = seq_place * blocks_dev
    owned_hot = (global_rows[:, :, None] == first_block + jnp.arange(blocks_dev)).astype(
        jnp.float32
    )
    length = segments.shape[1]
    block_len = length // blocks
    seg_blocks = segments.reshape(windows, blocks, block_len)
    seg_pad = jnp.pad(seg_blocks, ((0, 0), (1, 1), (0, 0)), constant_values=-1)
    near_segs = lax.dynamic_slice_in_dim(seg_pad, first_block, blocks_dev + 2, axis=1)
    slide_seg = jnp.concatenate([near_segs[:, :-2], near_segs[:, 1:-1], near_segs[:, 2:]], axis=2)
    query_seg = near_segs[:, 1:-1]
    rows_index = jnp.arange(windows)
    global_seg = seg_blocks[rows_index[:, None], global_rows].reshape(windows, -1)
    chosen = lax.dynamic_slice_in_dim(random_rows, first_block, blocks_dev, axis=1)
    far_seg = seg_blocks[rows_index[:, None, None, None], chosen].reshape(
        windows, blocks_dev, head_count, -1
    )
    key_seg = jnp.concatenate(
        [
            jnp.broadcast_to(
                slide_seg[:, :, None, :], (windows, blocks_dev, head_count, slide_seg.shape[2])
            ),
            jnp.broadcast_to(
                global_seg[:, None, None, :], (windows, blocks_dev, head_count, global_seg.shape[1])
            ),
            far_seg,
        ],
        axis=3,
    )
    key_mask = query_seg[:, :, None, :, None] == key_seg[:, :, :, None, :]
    local_seg = query_seg.reshape(windows, -1)
    full_mask = global_seg[:, None, :, None] == local_seg[:, None, None, :]
    return (sender, picker, owned_hot, key_mask, full_mask)


def fetch_blocks(paired, queries, sender, picker, owned_hot):
    windows, tokens, head_count, doubled = paired.shape
    head_dim = queries.shape[-1]
    blocks_dev = tokens // BLOCK
    flattened = paired.reshape(windows, tokens, head_count * doubled)
    padded = with_halo(flattened, ((SEQ, 1),), BLOCK)
    framed = padded.reshape(windows, blocks_dev + 2, BLOCK, head_count, doubled)
    sliding = jnp.concatenate([framed[:, :-2], framed[:, 1:-1], framed[:, 2:]], axis=2)
    local_blocks = paired.reshape(windows, blocks_dev, BLOCK, head_count, doubled)
    owned_low = owned_hot.astype(jnp.bfloat16)
    offered = mixed_sum("wgb,wbthe->wgthe", owned_low, local_blocks)
    offered_queries = mixed_sum("wgb,wbqhd->wgqhd", owned_low, queries)
    global_kv, global_queries = (
        lax.psum(offered.astype(jnp.bfloat16), SEQ).astype(jnp.float32),
        lax.psum(offered_queries.astype(jnp.bfloat16), SEQ).astype(jnp.float32),
    )
    global_kv = global_kv.astype(jnp.bfloat16).reshape(windows, -1, head_count, doubled)
    global_queries = global_queries.astype(jnp.bfloat16).reshape(windows, -1, head_count, head_dim)
    outgoing = mixed_sum("wqcbh,wbthe->qwcte", sender.astype(jnp.bfloat16), local_blocks).astype(
        jnp.bfloat16
    )
    incoming = lax.all_to_all(outgoing, SEQ, split_axis=0, concat_axis=0, tiled=True)
    distant = mixed_sum("wspc,pwcte->wste", picker.astype(jnp.bfloat16), incoming).astype(
        jnp.bfloat16
    )
    pick_count = picker.shape[1] // (blocks_dev * head_count)
    distant = distant.reshape(windows, blocks_dev, head_count, pick_count, BLOCK, doubled)
    return (sliding, global_kv, distant, global_queries)


def combine_stats(earlier, later):
    top = jnp.maximum(earlier[0], later[0])
    return (top, earlier[1] * jnp.exp(earlier[0] - top) + later[1] * jnp.exp(later[0] - top))


def full_forward(global_queries, key_part, value_part, full_mask, head_dim):
    scores = mixed_sum("wqhd,wkhd->whqk", global_queries, key_part) * head_dim ** (-0.5)
    scores = jnp.where(full_mask, scores, masked)
    local_top = jnp.max(scores, axis=3, keepdims=True)
    local_sum = jnp.sum(
        jnp.where(full_mask, jnp.exp(scores - local_top), 0.0), axis=3, keepdims=True
    )
    row_top, row_sum = merged((local_top, local_sum), SEQ, combine_stats)
    full_probs = jnp.where(full_mask, jnp.exp(scores - row_top), 0.0) / row_sum
    partial_out = mixed_sum("whqk,wkhd->wqhd", full_probs.astype(jnp.bfloat16), value_part)
    full_out = lax.psum(partial_out.astype(jnp.bfloat16), SEQ).astype(jnp.float32)
    return (full_out, full_probs)


def attention_weights(queries, sliding, global_kv, distant, key_mask):
    head_dim = queries.shape[-1]
    windows, blocks_dev, _, head_count, _ = queries.shape
    near_scores = mixed_sum("wbqhd,wbkhd->wbhqk", queries, sliding[..., :head_dim])
    global_scores = mixed_sum("wbqhd,wkhd->wbhqk", queries, global_kv[..., :head_dim])
    far_scores = mixed_sum("wbqhd,wbhrkd->wbhqrk", queries, distant[..., :head_dim])
    far_scores = far_scores.reshape(windows, blocks_dev, head_count, BLOCK, -1)
    scores = jnp.concatenate([near_scores, global_scores, far_scores], axis=4) * head_dim ** (-0.5)
    scores = jnp.where(key_mask, scores, masked)
    row_top = jnp.max(scores, axis=4, keepdims=True)
    weight = jnp.exp(scores - row_top)
    return weight / jnp.sum(weight, axis=4, keepdims=True)


def split_keys(scores_like, sliding, global_kv, distant):
    near_keys = sliding.shape[2]
    global_keys = global_kv.shape[1]
    windows, blocks_dev, head_count, pick_count, _, _ = distant.shape
    near_part = scores_like[..., :near_keys]
    global_part = scores_like[..., near_keys : near_keys + global_keys]
    far_part = scores_like[..., near_keys + global_keys :].reshape(
        windows, blocks_dev, head_count, BLOCK, pick_count, BLOCK
    )
    return (near_part, global_part, far_part)


def attention_values(low_probs, sliding, global_kv, distant, head_dim):
    near_part, global_part, far_part = split_keys(low_probs, sliding, global_kv, distant)
    attended = mixed_sum("wbhqk,wbkhd->wbqhd", near_part, sliding[..., head_dim:])
    attended = attended + mixed_sum("wbhqk,wkhd->wbqhd", global_part, global_kv[..., head_dim:])
    return attended + mixed_sum("wbhqrk,wbhrkd->wbqhd", far_part, distant[..., head_dim:])


def layer_forward(hidden, weights, tables):
    row_weights, down_weights, vector_weights = weights
    sender, picker, owned_hot, key_mask, full_mask = tables
    model_width = row_weights.shape[0]
    windows, tokens, _ = hidden.shape
    blocks_dev = tokens // BLOCK
    head_dim = model_width // HEADS
    (
        gain_one,
        shift_one,
        bias_query,
        bias_value,
        bias_out,
        gain_two,
        shift_two,
        bias_down,
        bias_up,
    ) = split_vectors(vector_weights, model_width)
    normed = norm_rows(hidden, gain_one, shift_one).astype(jnp.bfloat16)
    projected = mixed_sum("wtd,de->wte", normed, row_weights[:, : 3 * model_width])
    projected = (
        projected + jnp.concatenate([bias_query, jnp.zeros_like(bias_query), bias_value])
    ).astype(jnp.bfloat16)
    queries = projected[..., :model_width].reshape(windows, blocks_dev, BLOCK, HEADS, head_dim)
    key_part = projected[..., model_width : 2 * model_width].reshape(
        windows, tokens, HEADS, head_dim
    )
    value_part = projected[..., 2 * model_width :].reshape(windows, tokens, HEADS, head_dim)
    paired = jnp.concatenate([key_part, value_part], axis=3)
    sliding, global_kv, distant, global_queries = fetch_blocks(
        paired, queries, sender, picker, owned_hot
    )
    probabilities = attention_weights(queries, sliding, global_kv, distant, key_mask)
    attended = attention_values(
        probabilities.astype(jnp.bfloat16), sliding, global_kv, distant, head_dim
    )
    full_out, full_probs = full_forward(global_queries, key_part, value_part, full_mask, head_dim)
    placed = exact_two(
        "wgb,wgqhd->wbqhd", owned_hot, full_out.reshape(windows, -1, BLOCK, HEADS, head_dim)
    )
    on_global = jnp.sum(owned_hot, axis=1)[:, :, None, None, None] > 0
    attended = jnp.where(on_global, placed, attended)
    mixed_low = attended.reshape(windows, tokens, model_width).astype(jnp.bfloat16)
    middle = (
        hidden
        + mixed_sum("wtd,de->wte", mixed_low, row_weights[:, 3 * model_width : 4 * model_width])
        + bias_out
    )
    normed_two = norm_rows(middle, gain_two, shift_two).astype(jnp.bfloat16)
    up_value = mixed_sum("wtd,df->wtf", normed_two, row_weights[:, 4 * model_width :]) + bias_up
    active = jax.nn.gelu(up_value, approximate=False).astype(jnp.bfloat16)
    output = middle + mixed_sum("wtf,fd->wtd", active, down_weights) + bias_down
    stored = (
        hidden,
        normed,
        queries,
        sliding,
        global_kv,
        distant,
        probabilities,
        mixed_low,
        middle,
        normed_two,
        up_value,
        active,
        key_part,
        value_part,
        global_queries,
        full_probs,
    )
    return (output, stored)


def return_blocks(near_back, global_back, far_back, query_part, sender, picker, owned_hot):
    windows, blocks_dev, _, head_count, doubled = near_back.shape
    first_third = near_back[:, :, :BLOCK]
    centre_third = near_back[:, :, BLOCK : 2 * BLOCK]
    last_third = near_back[:, :, 2 * BLOCK :]
    framed = jnp.pad(first_third, ((0, 0), (0, 2), (0, 0), (0, 0), (0, 0)))
    framed = framed + jnp.pad(centre_third, ((0, 0), (1, 1), (0, 0), (0, 0), (0, 0)))
    framed = framed + jnp.pad(last_third, ((0, 0), (2, 0), (0, 0), (0, 0), (0, 0)))
    own_grad = framed[:, 1:-1]
    for direction in (1, -1):
        rim_grad = framed[:, -1] if direction == 1 else framed[:, 0]
        arrived = from_behind(rim_grad.astype(jnp.bfloat16), SEQ, direction).astype(
            rim_grad.dtype
        )
        if direction == 1:
            own_grad = jnp.concatenate(
                [own_grad[:, :1] + arrived[:, None], own_grad[:, 1:]], axis=1
            )
        else:
            own_grad = jnp.concatenate(
                [own_grad[:, :-1], own_grad[:, -1:] + arrived[:, None]], axis=1
            )
    global_total, query_total = (
        lax.psum(
            global_back.reshape(windows, -1, BLOCK, head_count, doubled).astype(jnp.bfloat16), SEQ
        ).astype(jnp.float32),
        lax.psum(query_part.astype(jnp.bfloat16), SEQ).astype(jnp.float32),
    )
    own_grad = own_grad + exact_two("wgb,wgthe->wbthe", owned_hot, global_total)
    far_flat = far_back.reshape(windows, -1, BLOCK, doubled)
    returning = exact_two("wspc,wste->pwcte", picker, far_flat)
    arrived_far = lax.all_to_all(
        returning.astype(jnp.bfloat16), SEQ, split_axis=0, concat_axis=0, tiled=True
    ).astype(returning.dtype)
    own_grad = own_grad + exact_two("wqcbh,qwcte->wbthe", sender, arrived_far)
    return (own_grad.reshape(windows, blocks_dev * BLOCK, head_count, doubled), query_total)


def attention_back(
    grad_attended,
    queries,
    sliding,
    global_kv,
    distant,
    probabilities,
    key_part,
    value_part,
    global_queries,
    full_probs,
    sender,
    picker,
    owned_hot,
):
    head_dim = queries.shape[-1]
    score_scale = head_dim ** (-0.5)
    windows, blocks_dev, _, head_count, _ = queries.shape
    on_global = jnp.sum(owned_hot, axis=1)[:, :, None, None, None] > 0
    selected = mixed_sum("wgb,wbqhd->wgqhd", owned_hot.astype(jnp.bfloat16), grad_attended)
    rows_grad = lax.psum(selected.astype(jnp.bfloat16), SEQ).reshape(
        windows, -1, head_count, head_dim
    )
    grad_attended = jnp.where(on_global, jnp.zeros_like(grad_attended), grad_attended)
    low_probs = probabilities.astype(jnp.bfloat16)
    near_grad = mixed_sum("wbqhd,wbkhd->wbhqk", grad_attended, sliding[..., head_dim:])
    global_grad = mixed_sum("wbqhd,wkhd->wbhqk", grad_attended, global_kv[..., head_dim:])
    far_grad = mixed_sum("wbqhd,wbhrkd->wbhqrk", grad_attended, distant[..., head_dim:])
    far_grad = far_grad.reshape(windows, blocks_dev, head_count, BLOCK, -1)
    grad_probs = jnp.concatenate([near_grad, global_grad, far_grad], axis=4)
    grad_scores = probabilities * (
        grad_probs - jnp.sum(probabilities * grad_probs, axis=4, keepdims=True)
    )
    grad_scores = grad_scores.astype(jnp.bfloat16)
    near_split, global_split, far_split = split_keys(grad_scores, sliding, global_kv, distant)
    near_probs, global_probs, far_probs = split_keys(low_probs, sliding, global_kv, distant)
    grad_query = mixed_sum("wbhqk,wbkhd->wbqhd", near_split, sliding[..., :head_dim])
    grad_query = grad_query + mixed_sum(
        "wbhqk,wkhd->wbqhd", global_split, global_kv[..., :head_dim]
    )
    grad_query = (
        grad_query + mixed_sum("wbhqrk,wbhrkd->wbqhd", far_split, distant[..., :head_dim])
    ) * score_scale
    near_back = jnp.concatenate(
        [
            mixed_sum("wbhqk,wbqhd->wbkhd", near_split, queries) * score_scale,
            mixed_sum("wbhqk,wbqhd->wbkhd", near_probs, grad_attended),
        ],
        axis=4,
    )
    global_back = jnp.concatenate(
        [
            mixed_sum("wbhqk,wbqhd->wkhd", global_split, queries) * score_scale,
            mixed_sum("wbhqk,wbqhd->wkhd", global_probs, grad_attended),
        ],
        axis=3,
    )
    far_back = jnp.concatenate(
        [
            mixed_sum("wbhqrk,wbqhd->wbhrkd", far_split, queries) * score_scale,
            mixed_sum("wbhqrk,wbqhd->wbhrkd", far_probs, grad_attended),
        ],
        axis=5,
    )
    full_grad_probs = mixed_sum("wqhd,wkhd->whqk", rows_grad, value_part)
    partial_dot = jnp.sum(full_probs * full_grad_probs, axis=3, keepdims=True)
    row_dot = lax.psum(partial_dot, SEQ)
    full_grad_scores = (full_probs * (full_grad_probs - row_dot)).astype(jnp.bfloat16)
    query_part = mixed_sum("whqk,wkhd->wqhd", full_grad_scores, key_part) * score_scale
    full_key_grad = mixed_sum("whqk,wqhd->wkhd", full_grad_scores, global_queries) * score_scale
    full_value_grad = mixed_sum("whqk,wqhd->wkhd", full_probs.astype(jnp.bfloat16), rows_grad)
    grad_paired, query_total = return_blocks(
        near_back, global_back, far_back, query_part, sender, picker, owned_hot
    )
    grad_query = grad_query + exact_two(
        "wgb,wgqhd->wbqhd", owned_hot, query_total.reshape(windows, -1, BLOCK, head_count, head_dim)
    )
    grad_paired = grad_paired + jnp.concatenate([full_key_grad, full_value_grad], axis=3)
    return (grad_query, grad_paired)


def layer_backward(stored, grad_output, weights, tables):
    row_weights, down_weights, vector_weights = weights
    sender, picker, owned_hot, key_mask, full_mask = tables
    (
        hidden,
        normed,
        queries,
        sliding,
        global_kv,
        distant,
        probabilities,
        mixed_low,
        middle,
        normed_two,
        up_value,
        active,
        key_part,
        value_part,
        global_queries,
        full_probs,
    ) = stored
    model_width = row_weights.shape[0]
    windows, tokens, _ = hidden.shape
    blocks_dev = tokens // BLOCK
    head_dim = model_width // HEADS
    (
        gain_one,
        shift_one,
        bias_query,
        bias_value,
        bias_out,
        gain_two,
        shift_two,
        bias_down,
        bias_up,
    ) = split_vectors(vector_weights, model_width)
    grad_ffn = grad_output.astype(jnp.bfloat16)
    grad_bias_down = jnp.sum(grad_ffn.astype(jnp.float32), axis=(0, 1))
    grad_down = mixed_sum("wtf,wtd->fd", active, grad_ffn)
    grad_active = mixed_sum("wtd,fd->wtf", grad_ffn, down_weights)
    gelu_pull = jax.vjp(partial(jax.nn.gelu, approximate=False), up_value)[1]
    grad_up = gelu_pull(grad_active)[0].astype(jnp.bfloat16)
    grad_bias_up = jnp.sum(grad_up.astype(jnp.float32), axis=(0, 1))
    grad_in = mixed_sum("wtd,wtf->df", normed_two, grad_up)
    grad_normed_two = mixed_sum("wtf,df->wtd", grad_up, row_weights[:, 4 * model_width :])
    norm_pull_two = jax.vjp(norm_rows, middle, gain_two, shift_two)[1]
    grad_middle_norm, grad_gain_two, grad_shift_two = norm_pull_two(grad_normed_two)
    grad_middle = grad_output + grad_middle_norm
    grad_branch = grad_middle.astype(jnp.bfloat16)
    grad_bias_out = jnp.sum(grad_branch.astype(jnp.float32), axis=(0, 1))
    grad_out_weight = mixed_sum("wtd,wte->de", mixed_low, grad_branch)
    grad_attended = mixed_sum(
        "wte,de->wtd", grad_branch, row_weights[:, 3 * model_width : 4 * model_width]
    ).astype(jnp.bfloat16)
    grad_attended = grad_attended.reshape(windows, blocks_dev, BLOCK, HEADS, head_dim)
    grad_query, grad_paired = attention_back(
        grad_attended,
        queries,
        sliding,
        global_kv,
        distant,
        probabilities,
        key_part,
        value_part,
        global_queries,
        full_probs,
        sender,
        picker,
        owned_hot,
    )
    grad_projected = jnp.concatenate(
        [
            grad_query.reshape(windows, tokens, model_width),
            grad_paired[..., :head_dim].reshape(windows, tokens, model_width),
            grad_paired[..., head_dim:].reshape(windows, tokens, model_width),
        ],
        axis=2,
    ).astype(jnp.bfloat16)
    summed = jnp.sum(grad_projected.astype(jnp.float32), axis=(0, 1))
    grad_bias_query = summed[:model_width]
    grad_bias_value = summed[2 * model_width :]
    grad_projection = mixed_sum("wtd,wte->de", normed, grad_projected)
    grad_normed = mixed_sum("wte,de->wtd", grad_projected, row_weights[:, : 3 * model_width])
    norm_pull_one = jax.vjp(norm_rows, hidden, gain_one, shift_one)[1]
    grad_hidden_norm, grad_gain_one, grad_shift_one = norm_pull_one(grad_normed)
    grad_hidden = grad_middle + grad_hidden_norm
    grad_rows = jnp.concatenate([grad_projection, grad_out_weight, grad_in], axis=1)
    grad_vectors = jnp.concatenate(
        [
            grad_gain_one,
            grad_shift_one,
            grad_bias_query,
            grad_bias_value,
            grad_bias_out,
            grad_gain_two,
            grad_shift_two,
            grad_bias_down,
            grad_bias_up,
        ]
    )
    return (grad_hidden, (grad_rows, grad_down, grad_vectors))


def adam_update(master, first_old, second_old, gradient, step_rate, decay_rate):
    first_new = 0.5 * first_old + 0.5 * gradient
    second_new = 0.5 * second_old + 0.5 * gradient * gradient
    first_hat = first_new / (1.0 - 0.5**STEP)
    second_hat = second_new / (1.0 - 0.5**STEP)
    master_new = master - step_rate * (
        first_hat / (jnp.sqrt(second_hat) + 1e-08) + decay_rate * master
    )
    return (master_new, first_new, second_new)


def general_shards(
    block_input,
    cotangent,
    random_ids,
    segment_ids,
    global_ids,
    w_rows,
    w_rows_first,
    w_rows_second,
    w_down,
    w_down_first,
    w_down_second,
    vectors,
    vectors_first,
    vectors_second,
):
    section_index = lax.axis_index(SECTION)
    seq_place = lax.axis_index(SEQ)
    groups = lax.axis_size(SEQ)
    row_weights, down_weights, vector_low = (
        lax.all_gather(w_rows[0].astype(jnp.bfloat16), (DP, SEQ), axis=1, tiled=True),
        lax.all_gather(w_down[0].astype(jnp.bfloat16), (DP, SEQ), axis=0, tiled=True),
        lax.all_gather(vectors[0].astype(jnp.bfloat16), (DP, SEQ), axis=0, tiled=True),
    )
    weights = (row_weights, down_weights, vector_low.astype(jnp.float32))
    micro_count, windows, tokens, model_width = block_input.shape
    received = jnp.zeros((windows, tokens, model_width), jnp.bfloat16)
    results = jnp.zeros(block_input.shape, jnp.float32)
    full_totals = (
        jnp.zeros(row_weights.shape, jnp.float32),
        jnp.zeros(down_weights.shape, jnp.float32),
        jnp.zeros(vector_low.shape, jnp.float32),
    )

    def tick(tick_index, carry):
        received, results, full_totals = carry
        forward_mb = jnp.clip(tick_index - section_index, 0, micro_count - 1)
        behind_raw = tick_index - 2 + section_index
        behind = jnp.clip(behind_raw, 0, micro_count - 1)
        live_mask = ((behind_raw >= 0) & (behind_raw < micro_count)).astype(jnp.float32)
        tables_forward = route_tables(
            lax.dynamic_index_in_dim(random_ids, forward_mb, 0, keepdims=False),
            lax.dynamic_index_in_dim(segment_ids, forward_mb, 0, keepdims=False),
            lax.dynamic_index_in_dim(global_ids, forward_mb, 0, keepdims=False),
            seq_place,
            groups,
        )
        tables_behind = route_tables(
            lax.dynamic_index_in_dim(random_ids, behind, 0, keepdims=False),
            lax.dynamic_index_in_dim(segment_ids, behind, 0, keepdims=False),
            lax.dynamic_index_in_dim(global_ids, behind, 0, keepdims=False),
            seq_place,
            groups,
        )
        incoming_values = received.astype(jnp.float32)
        first_input = lax.dynamic_index_in_dim(block_input, forward_mb, 0, keepdims=False).astype(
            jnp.float32
        )
        forward_input = jnp.where(section_index == 0, first_input, incoming_values)
        forward_output = layer_forward(forward_input, weights, tables_forward)[0]
        back_source = lax.dynamic_index_in_dim(block_input, behind, 0, keepdims=False).astype(
            jnp.float32
        )
        back_input = jnp.where(section_index == 0, back_source, incoming_values)
        given_grad = lax.dynamic_index_in_dim(cotangent, behind, 0, keepdims=False).astype(
            jnp.float32
        )
        back_grad = jnp.where(section_index == 0, incoming_values, given_grad) * live_mask
        stored = layer_forward(back_input, weights, tables_behind)[1]
        grad_input, gradients = layer_backward(stored, back_grad, weights, tables_behind)
        outgoing = jnp.where(section_index == 0, forward_output, grad_input).astype(jnp.bfloat16)
        finished = jnp.where(section_index == 0, grad_input, forward_output)
        updated = lax.dynamic_update_index_in_dim(results, finished, behind, 0)
        results = jnp.where(live_mask > 0, updated, results)
        full_totals = tuple(
            (total_part + grad_part for total_part, grad_part in zip(full_totals, gradients))
        )
        return (partner(outgoing, SECTION, 0), results, full_totals)

    received, results, full_totals = lax.fori_loop(
        0, micro_count + 2, tick, (received, results, full_totals)
    )
    shard_totals = (
        lax.psum_scatter(full_totals[0], (DP, SEQ), scatter_dimension=1, tiled=True),
        lax.psum_scatter(full_totals[1], (DP, SEQ), scatter_dimension=0, tiled=True),
        lax.psum_scatter(full_totals[2], (DP, SEQ), scatter_dimension=0, tiled=True),
    )
    new_rows, new_rows_first, new_rows_second = adam_update(
        w_rows[0], w_rows_first[0], w_rows_second[0], shard_totals[0], rate_matrix, decay_matrix
    )
    new_down, new_down_first, new_down_second = adam_update(
        w_down[0], w_down_first[0], w_down_second[0], shard_totals[1], rate_matrix, decay_matrix
    )
    new_vectors, new_vectors_first, new_vectors_second = adam_update(
        vectors[0], vectors_first[0], vectors_second[0], shard_totals[2], rate_vector, 0.0
    )
    return (
        results[None],
        new_rows[None],
        new_rows_first[None],
        new_rows_second[None],
        new_down[None],
        new_down_first[None],
        new_down_second[None],
        new_vectors[None],
        new_vectors_first[None],
        new_vectors_second[None],
    )


LOW = jnp.bfloat16
LOG_HIGH = [float(np.log(c).astype(ml_dtypes.bfloat16)) for c in (1.0, 2.0, 3.0)]
LOG_LOW = [float(np.log(c)) - high for c, high in zip((1.0, 2.0, 3.0), LOG_HIGH)]
CHUNK = 256
VMEM_BYTES = 48 * 1024 * 1024


def dot_rows(left, right):
    return lax.dot_general(left, right, (((1,), (1,)), ((), ())), preferred_element_type=jnp.float32)


def dot_plain(left, right):
    return lax.dot_general(left, right, (((1,), (0,)), ((), ())), preferred_element_type=jnp.float32)


def dot_tokens(left, right):
    return lax.dot_general(left, right, (((0,), (0,)), ((), ())), preferred_element_type=jnp.float32)


def key_features(random_rows, segments, global_rows):
    blocks, head_count, _ = random_rows.shape
    index = jnp.arange(blocks)
    near = (jnp.abs(index[:, None] - index[None, :]) <= 1).astype(jnp.int32)
    named = jnp.sum((global_rows[:, None] == index[None, :]).astype(jnp.int32), axis=0)
    far = jnp.sum((random_rows[..., None] == index).astype(jnp.int32), axis=2)
    count = near[:, None, :] + named[None, None, :] + far
    count = jnp.where(named[:, None, None] > 0, 1, count)
    high = jnp.where(count == 0, masked, 0.0)
    low = jnp.zeros_like(high)
    for times in (2, 3):
        high = jnp.where(count == times, LOG_HIGH[times - 1], high)
        low = jnp.where(count == times, LOG_LOW[times - 1], low)
    width = -(-(2 * blocks + 6) // 128) * 128
    tokens = segments.shape[0]
    segment_hot = (segments[:, None] == jnp.arange(3)).astype(jnp.float32)
    table = jnp.concatenate([high, low], axis=2).transpose(1, 0, 2)
    spread = jnp.broadcast_to(
        table[:, :, None, :], (head_count, blocks, BLOCK, 2 * blocks)
    ).reshape(head_count, tokens, 2 * blocks)
    query_side = jnp.concatenate(
        [
            spread,
            jnp.broadcast_to(segment_hot, (head_count, tokens, 3)),
            jnp.zeros((head_count, tokens, width - 2 * blocks - 3), jnp.float32),
        ],
        axis=2,
    ).astype(LOW)
    block_hot = (jnp.arange(tokens)[:, None] // BLOCK == index).astype(jnp.float32)
    key_side = jnp.concatenate(
        [
            block_hot,
            block_hot,
            masked * (1.0 - segment_hot),
            jnp.ones((tokens, 3), jnp.float32),
            jnp.zeros((tokens, width - 2 * blocks - 6), jnp.float32),
        ],
        axis=1,
    ).astype(LOW)
    return query_side, key_side


def attend_kernel(q_ref, k_ref, v_ref, qa_ref, ka_ref, out_ref, lse_ref):
    tokens, pair = q_ref.shape
    left = lax.broadcasted_iota(jnp.int32, (CHUNK, pair), 1) < pair // 2
    keys = jnp.concatenate([k_ref[...], ka_ref[...]], axis=1)
    values = v_ref[...]

    def step(index, carry):
        rows = pl.ds(pl.multiple_of(index * CHUNK, CHUNK), CHUNK)
        queries = q_ref[rows, :] * 0.125
        outs, tops = [], []
        for head in range(2):
            mine = left if head == 0 else jnp.logical_not(left)
            side = jnp.where(mine, queries, jnp.zeros_like(queries))
            scores = dot_rows(jnp.concatenate([side, qa_ref[head, rows, :]], axis=1), keys)
            top = jnp.max(scores, axis=1, keepdims=True)
            weight = jnp.exp(scores - top)
            total = jnp.sum(weight, axis=1, keepdims=True)
            outs.append(dot_plain(weight.astype(LOW), values) / total)
            tops.append(top + jnp.log(total))
        out_ref[rows, :] = jnp.where(left, outs[0], outs[1]).astype(LOW)
        lse_ref[rows, :] = jnp.where(left, tops[0], tops[1])
        return carry

    lax.fori_loop(0, tokens // CHUNK, step, 0)


def attend(projected, query_side, key_side, width):
    tokens = projected.shape[0]
    pairs = width // 128
    features = key_side.shape[1]
    return pl.pallas_call(
        attend_kernel,
        grid=(pairs,),
        in_specs=[
            pl.BlockSpec((tokens, 128), lambda p: (0, p)),
            pl.BlockSpec((tokens, 128), lambda p: (0, pairs + p)),
            pl.BlockSpec((tokens, 128), lambda p: (0, 2 * pairs + p)),
            pl.BlockSpec((2, tokens, features), lambda p: (p, 0, 0)),
            pl.BlockSpec((tokens, features), lambda p: (0, 0)),
        ],
        out_specs=[
            pl.BlockSpec((tokens, 128), lambda p: (0, p)),
            pl.BlockSpec((tokens, 128), lambda p: (0, p)),
        ],
        out_shape=[
            jax.ShapeDtypeStruct((tokens, width), LOW),
            jax.ShapeDtypeStruct((tokens, width), jnp.float32),
        ],
        compiler_params=pltpu.CompilerParams(vmem_limit_bytes=VMEM_BYTES),
        cost_estimate=pl.CostEstimate(
            flops=16 * pairs * tokens * tokens * 128,
            bytes_accessed=tokens * width * 16,
            transcendentals=2 * pairs * tokens * tokens,
        ),
    )(projected, projected, projected, query_side, key_side)


def three_terms(values):
    high = values.astype(LOW).astype(jnp.float32)
    rest = values - high
    middle = rest.astype(LOW).astype(jnp.float32)
    return high, middle, rest - middle


def attend_back_kernel(
    q_ref, k_ref, v_ref, do_ref, o_ref, lse_ref, qa_ref, ka_ref, grad_ref, dk_acc, dv_acc
):
    tokens, pair = q_ref.shape
    features = ka_ref.shape[1]
    pairs = pl.num_programs(0)
    place = pl.program_id(0)
    blocks = tokens // BLOCK
    first = 2 * blocks + 3
    left = lax.broadcasted_iota(jnp.int32, (CHUNK, pair), 1) < pair // 2
    lane = lax.broadcasted_iota(jnp.int32, (CHUNK, features), 1)
    lane_pair = lax.broadcasted_iota(jnp.int32, (CHUNK, pair), 1)
    keys = jnp.concatenate([k_ref[...], ka_ref[...]], axis=1)
    turned = jnp.transpose(k_ref[...].astype(jnp.float32)).astype(LOW)
    ones = (lax.broadcasted_iota(jnp.int32, (tokens, pair), 1) < 3).astype(jnp.float32).astype(LOW)
    values = jnp.concatenate([v_ref[...], ones], axis=1)
    dk_acc[...] = jnp.zeros_like(dk_acc)
    dv_acc[...] = jnp.zeros_like(dv_acc)
    column = pl.multiple_of(place * 128, 128)

    def step(index, carry):
        rows = pl.ds(pl.multiple_of(index * CHUNK, CHUNK), CHUNK)
        queries = q_ref[rows, :] * 0.125
        grads = do_ref[rows, :]
        product = grads.astype(jnp.float32) * o_ref[rows, :].astype(jnp.float32)
        parts = []
        for head in range(2):
            mine = left if head == 0 else jnp.logical_not(left)
            level = lse_ref[rows, head * 64 : head * 64 + 1]
            inner = jnp.sum(jnp.where(mine, product, 0.0), axis=1, keepdims=True)
            side = qa_ref[head, rows, :].astype(jnp.float32)
            for spot, term in enumerate(three_terms(level)):
                side = jnp.where(lane == first + spot, -term, side)
            query_side = jnp.where(mine, queries, jnp.zeros_like(queries))
            grad_side = jnp.where(mine, grads, jnp.zeros_like(grads))
            tail = jnp.zeros((CHUNK, pair), jnp.float32)
            for spot, term in enumerate(three_terms(inner)):
                tail = jnp.where(lane_pair == spot, -term, tail)
            probs = jnp.exp(
                dot_rows(keys, jnp.concatenate([query_side, side.astype(LOW)], axis=1))
            )
            change = dot_rows(values, jnp.concatenate([grad_side, tail.astype(LOW)], axis=1))
            grad_scores = (probs * change).astype(LOW)
            dv_acc[...] += dot_plain(probs.astype(LOW), grad_side)
            dk_acc[...] += dot_plain(grad_scores, query_side)
            parts.append(dot_plain(turned, grad_scores))
        half = pair // 2
        joined = jnp.concatenate([parts[0][:half], parts[1][half:]], axis=0)
        grad_ref[rows, pl.ds(column, 128)] = (jnp.transpose(joined) * 0.125).astype(LOW)
        return carry

    lax.fori_loop(0, tokens // CHUNK, step, 0)
    key_column = pl.multiple_of((pairs + place) * 128, 128)
    value_column = pl.multiple_of((2 * pairs + place) * 128, 128)
    grad_ref[:, pl.ds(key_column, 128)] = dk_acc[...].astype(LOW)
    grad_ref[:, pl.ds(value_column, 128)] = dv_acc[...].astype(LOW)


def attend_back(projected, grad_attended, attended, levels, query_side, key_side):
    tokens, width = attended.shape
    pairs = width // 128
    features = key_side.shape[1]
    return pl.pallas_call(
        attend_back_kernel,
        grid=(pairs,),
        in_specs=[
            pl.BlockSpec((tokens, 128), lambda p: (0, p)),
            pl.BlockSpec((tokens, 128), lambda p: (0, pairs + p)),
            pl.BlockSpec((tokens, 128), lambda p: (0, 2 * pairs + p)),
            pl.BlockSpec((tokens, 128), lambda p: (0, p)),
            pl.BlockSpec((tokens, 128), lambda p: (0, p)),
            pl.BlockSpec((tokens, 128), lambda p: (0, p)),
            pl.BlockSpec((2, tokens, features), lambda p: (p, 0, 0)),
            pl.BlockSpec((tokens, features), lambda p: (0, 0)),
        ],
        out_specs=pl.BlockSpec((tokens, 3 * width), lambda p: (0, 0)),
        out_shape=jax.ShapeDtypeStruct((tokens, 3 * width), LOW),
        scratch_shapes=[
            pltpu.VMEM((tokens, 128), jnp.float32),
            pltpu.VMEM((tokens, 128), jnp.float32),
        ],
        compiler_params=pltpu.CompilerParams(vmem_limit_bytes=VMEM_BYTES),
        cost_estimate=pl.CostEstimate(
            flops=40 * pairs * tokens * tokens * 128,
            bytes_accessed=tokens * width * 24,
            transcendentals=2 * pairs * tokens * tokens,
        ),
    )(projected, projected, projected, grad_attended, attended, levels, query_side, key_side)


def swap(value):
    return lax.ppermute(value, SECTION, [(0, 1), (1, 0)])


def normalized(values_in):
    row_mean = jnp.mean(values_in, axis=-1, keepdims=True)
    centred = values_in - row_mean
    spread = jnp.mean(centred * centred, axis=-1, keepdims=True)
    scale = lax.rsqrt(spread + epsilon)
    return centred * scale, scale


def norm_back(values_in, incoming, gain_vec):
    unit, scale = normalized(values_in)
    grad_gain = jnp.sum(incoming * unit, axis=0)
    grad_shift = jnp.sum(incoming, axis=0)
    p = incoming * gain_vec
    mean_p = jnp.mean(p, axis=-1, keepdims=True)
    mean_pn = jnp.mean(p * unit, axis=-1, keepdims=True)
    return scale * (p - mean_p - unit * mean_pn), grad_gain, grad_shift


class Shares:
    def __init__(self, width, columns, depth, vector_len):
        self.width = width
        self.columns = columns
        self.depth = depth
        self.vector_len = vector_len
        self.half = columns // 2
        self.per = width // columns
        self.groups = columns // depth

    def unpack(self, gathered, core):
        half, per, width = self.half, self.per, self.width
        if len(gathered) == 3:
            rows = gathered[0].reshape(-1, half, width)
            gathered = (
                rows[: 3 * per],
                rows[3 * per : 4 * per],
                rows[4 * per :],
                gathered[1],
                gathered[2],
            )
        proj, out, up, down, vec = gathered
        proj, up, down = [piece.reshape(-1, width) for piece in (proj, up, down)]
        out = (
            out.reshape(per, half, 2, per * half)
            .transpose(0, 2, 1, 3)
            .reshape(width, per * half)
        )
        vec = vec.reshape(-1, TAIL, width)[:, 0, : self.vector_len].reshape(-1)
        pieces = split_vectors(vec.astype(jnp.float32), width)
        bias_query, bias_value = self.vector_half(pieces[2], core), self.vector_half(pieces[3], core)
        bias_up = lax.dynamic_index_in_dim(
            pieces[8].reshape(-1, 2, self.depth // 2), core, 1, keepdims=False
        ).reshape(-1)
        return (
            (proj, out, up, down),
            (pieces[0], pieces[1], bias_query, bias_value, pieces[4], pieces[5], pieces[6])
            + (pieces[7], bias_up),
        )

    def vector_half(self, vec, core):
        return lax.dynamic_index_in_dim(
            vec.reshape(self.per, 2, self.half), core, 1, keepdims=False
        ).reshape(-1)

    def by_shard(self, grads, vector_grads, core):
        proj, out, up, down = grads
        half, per, width = self.half, self.per, self.width
        out = (
            out.reshape(per, 2, half, per * half).transpose(0, 2, 1, 3).reshape(per, half, width)
        )
        hot = (jnp.arange(2) == core).astype(jnp.float32)
        spread = list(vector_grads)
        for index in (2, 3):
            spread[index] = (
                spread[index].reshape(per, 1, half) * hot[None, :, None]
            ).reshape(-1)
        spread[8] = (spread[8].reshape(-1, 1, self.depth // 2) * hot[None, :, None]).reshape(-1)
        for index in (0, 1, 4, 5, 6, 7):
            spread[index] = spread[index] * hot[0]
        vec = jnp.concatenate(spread).reshape(-1, 1, self.vector_len)
        vec = jnp.pad(vec, ((0, 0), (0, TAIL - 1), (0, width - self.vector_len))).astype(LOW)
        return (
            proj.reshape(-1, half, width),
            out,
            up.reshape(2, 4, half, width),
            down.reshape(2, 2, 4, self.depth // 2, width),
            vec.reshape(2, 2, 4, TAIL, width),
        )


MESH = pl.DeviceIdType.MESH
PIECE = 48
TAIL = 16


def prepare_kernel(shares, rows_ref, down_ref, vector_ref, rows_out, down_out, vector_out):
    core = lax.axis_index(SECTION)
    offset = lax.axis_index((DP, SEQ)) * shares.columns
    half, per, width, depth = shares.half, shares.per, shares.width, shares.depth // 2
    is_inner = (offset >= 3 * width) & (offset < 4 * width)
    is_hidden = offset >= 4 * width

    @pl.when(is_inner)
    def _():
        for which in range(2):
            side = core if which == 0 else 1 - core
            held = [rows_ref[pl.ds((2 * j + side) * half, half), :] for j in range(per)]
            turned = jnp.transpose(jnp.concatenate(held, axis=0))
            rows_out[which] = jnp.concatenate([turned[:half], turned[half:]], axis=1).astype(LOW)

    @pl.when(jnp.logical_not(is_inner))
    def _():
        turned = jnp.transpose(rows_ref[...]).astype(LOW)
        plain = [turned[:half], turned[half:]]
        hidden = [
            jnp.concatenate(
                [turned[(2 * j + side) * depth :][:depth] for j in range(shares.groups)], axis=0
            )
            for side in range(2)
        ]
        halves = [jnp.where(is_hidden, b, a) for a, b in zip(plain, hidden)]
        rows_out[0] = jnp.where(core == 0, halves[0], halves[1])
        rows_out[1] = jnp.where(core == 0, halves[1], halves[0])

    down = down_ref[...].astype(LOW)
    down_out[0] = jnp.where(core == 0, down[:depth], down[depth:])
    down_out[1] = jnp.where(core == 0, down[depth:], down[:depth])
    vector_out[...] = jnp.zeros_like(vector_out)
    vector_out[0:1, : shares.vector_len] = vector_ref[...].astype(LOW)


def prepare(shares, rows, down, vector):
    return pl.pallas_call(
        partial(prepare_kernel, shares),
        out_shape=[
            jax.ShapeDtypeStruct((2, shares.half, shares.width), LOW),
            jax.ShapeDtypeStruct((2, shares.depth // 2, shares.width), LOW),
            jax.ShapeDtypeStruct((TAIL, shares.width), LOW),
        ],
        compiler_params=pltpu.CompilerParams(vmem_limit_bytes=VMEM_BYTES),
    )(rows, down, vector)


class Place:
    def __init__(self):
        self.core = lax.axis_index(SECTION)
        self.dp = lax.axis_index(DP)
        self.z = lax.axis_index(SEQ)
        self.y, self.x = self.dp // 2, self.dp % 2
        self.high, self.low = self.z // 2, self.z % 2
        self.inner = self.high + self.low == 1
        self.outer = self.high + self.low != 1
        self.partner = {SECTION: 1 - self.core}
        self.along_x = {DP: 2 * self.y + 1 - self.x}
        self.along_y = {DP: 2 * (1 - self.y) + self.x}
        self.across = {SEQ: 3 - self.z}
        self.beside = {SEQ: 2 * self.high + 1 - self.low}
        self.others = [{SEQ: (self.z + by) % 4} for by in (1, 2, 3)]
        self.own = pl.ds(self.z, 1)
        self.next = pl.ds(2 * self.high + 1 - self.low, 1)
        self.near = pl.ds(2 * self.high, 2)
        self.far = pl.ds(2 * (1 - self.high), 2)

    def greet(self):
        barrier = pltpu.get_barrier_semaphore()
        everyone = [self.partner, self.along_x, self.along_y] + self.others
        for device in everyone:
            pl.semaphore_signal(barrier, inc=1, device_id=device, device_id_type=MESH)
        pl.semaphore_wait(barrier, len(everyone))


def remote(src, dst, sems, spots, device):
    return pltpu.make_async_remote_copy(
        src_ref=src,
        dst_ref=dst,
        send_sem=sems[0].at[spots[0]],
        recv_sem=sems[1].at[spots[1]],
        device_id=device,
        device_id_type=MESH,
    )


def chunk_pairs(shares):
    pairs = []
    for array, length in ((0, shares.half), (1, shares.depth // 2)):
        for start in range(0, length, 2 * PIECE):
            pairs.append([(array, start, PIECE, 0), (array, start + PIECE, PIECE, 1)])
    pairs[0].append((2, 0, TAIL, 0))
    return pairs


def quad_pairs(shares):
    length = (shares.half + shares.depth // 2) // 2
    pairs = [
        [(0, start, PIECE, None), (1, start, PIECE, None)] for start in range(0, length, PIECE)
    ]
    pairs[0].append((2, 0, TAIL, 0))
    return pairs


def gather_kernel(shares, *refs):
    (rows_in, down_in, vector_in, x_in, cot_in), refs = refs[:5], refs[5:]
    outs, refs = [refs[0:3], refs[3:6]], refs[6:]
    (x_out, cot_out), refs = refs[:2], refs[2:]
    local, swap_send, swap_recv, z_send, z_recv, send, recv = refs
    here = Place()
    core, y, x, z = here.core, here.y, here.x, here.z
    half = x_in.shape[2] // 2
    rows_half, down_half = shares.half // 2, shares.depth // 4
    here.greet()

    def slices(source, target, base):
        mine = pl.ds(pl.multiple_of(core * half, half), half)
        sems = (z_send, z_recv)
        own = pltpu.make_async_copy(
            source.at[z, 0, mine], target.at[z, core], local.at[8 + base // 4]
        )
        sends, arrivals = [], []
        for by in (1, 2, 3):
            spots = (base + by - 1, base + by - 1)
            device = here.others[by - 1]
            sends.append(
                remote(source.at[(z + by) % 4, 0, mine], target.at[z, core], sems, spots, device)
            )
            arrivals.append(
                remote(
                    source.at[z, 0, mine], target.at[(z + 4 - by) % 4, core], sems, spots, device
                )
            )
        spots = (base + 3, base + 3)
        forward = remote(target.at[:, core], target.at[:, core], sems, spots, here.partner)
        arrived = remote(target.at[:, 1 - core], target.at[:, 1 - core], sems, spots, here.partner)
        return own, sends, arrivals, forward, arrived

    x_moves = slices(x_in, x_out, 0)
    cot_moves = slices(cot_in, cot_out, 4)

    def open_slices(moves):
        moves[0].start()
        for copy in moves[1]:
            copy.start()

    def pass_slices(moves):
        moves[0].wait()
        for copy in moves[2]:
            copy.wait_recv()
        moves[3].start()

    def close_slices(moves):
        for copy in moves[1]:
            copy.wait_send()
        moves[3].wait_send()
        moves[4].wait_recv()

    def first_moves(layer, which):
        down = down_in.at[which]
        rows = rows_in.at[which]
        if layer == 0:
            return [
                (0, rows, outs[0][0].at[y, x, z]),
                (1, down, outs[0][1].at[y, x, z]),
                (2, vector_in, outs[0][2].at[y, x, z]),
            ]
        moves = [(7, vector_in, outs[1][2].at[y, x, z])]
        for part in range(2):
            target = outs[1][part]
            moves.append(
                (
                    3 + 2 * part,
                    rows.at[pl.ds(part * rows_half, rows_half)],
                    target.at[z, pl.ds(0, rows_half)],
                )
            )
            moves.append(
                (
                    4 + 2 * part,
                    down.at[pl.ds(part * down_half, down_half)],
                    target.at[z, pl.ds(rows_half, down_half)],
                )
            )
        return moves

    swaps = (swap_send, swap_recv)
    for layer in range(2):

        @pl.when(core == layer)
        def _():
            across = [
                remote(src, dst, swaps, (spot, spot), here.partner)
                for spot, src, dst in first_moves(layer, 1)
            ]
            own = [
                pltpu.make_async_copy(src, dst, local.at[spot])
                for spot, src, dst in first_moves(layer, 0)
            ]
            for copy in across + own:
                copy.start()
            for copy in own:
                copy.wait()
            for copy in across:
                copy.wait_send()
            for spot, src, dst in first_moves(1 - layer, 0):
                remote(src, dst, swaps, (spot, spot), here.partner).wait_recv()

    numbers, pairs = {}, []
    for layer in range(2):
        for pair in chunk_pairs(shares) if layer == 0 else quad_pairs(shares):
            entry = []
            for array, start, length, order in pair:
                ref = outs[layer][array]
                rows = pl.ds(start, length)
                flat = order is None
                number = len(numbers)
                sems = (send, recv)

                def part(which):
                    return ref.at[which, rows] if flat else ref.at[y, x, which, rows]

                def copy(piece, spots, device):
                    return remote(piece, piece, sems, ((number, spots[0]), (number, spots[1])), device)

                steps = {
                    "z": copy(part(here.own), (0, 0), here.beside),
                    "across": copy(part(here.near), (1, 1), here.across),
                    "on": copy(part(here.far), (4, 1), here.beside),
                }
                arrive = [
                    copy(part(here.next), (0, 0), here.beside),
                    copy(part(here.far), (1, 1), here.across),
                ]
                if order == 0:
                    steps["one"] = copy(ref.at[y, x, :, rows], (2, 2), here.along_y)
                    steps["two"] = copy(ref.at[:, x, :, rows], (3, 3), here.along_x)
                    arrive.append(copy(ref.at[1 - y, x, :, rows], (2, 2), here.along_y))
                    arrive.append(copy(ref.at[:, 1 - x, :, rows], (3, 3), here.along_x))
                elif order == 1:
                    steps["one"] = copy(ref.at[y, x, :, rows], (2, 2), here.along_x)
                    steps["two"] = copy(ref.at[y, :, :, rows], (3, 3), here.along_y)
                    arrive.append(copy(ref.at[y, 1 - x, :, rows], (2, 2), here.along_x))
                    arrive.append(copy(ref.at[1 - y, :, :, rows], (3, 3), here.along_y))
                numbers[number] = (steps, arrive)
                entry.append(number)
            pairs.append(entry)

    for tick in range(len(pairs) + 3):
        for phase in (3, 2, 1, 0):
            if not 0 <= tick - phase < len(pairs):
                continue
            entry = pairs[tick - phase]
            for number in entry:
                steps, arrive = numbers[number]
                if phase and phase <= len(arrive):
                    arrive[phase - 1].wait_recv()
            if phase == 0:
                for number in entry:
                    numbers[number][0]["z"].start()
            elif phase == 3:
                for number in entry:
                    if "two" in numbers[number][0]:
                        numbers[number][0]["two"].start()
            else:

                @pl.when(here.inner)
                def _():
                    for number in entry:
                        numbers[number][0]["across" if phase == 1 else "on"].start()

                if phase == 2:
                    for number in entry:
                        if "one" in numbers[number][0]:
                            numbers[number][0]["one"].start()
        if tick == 1:
            open_slices(x_moves)
        if tick == 4:
            pass_slices(x_moves)
            open_slices(cot_moves)
        if tick == 7:
            pass_slices(cot_moves)
    for steps, arrive in numbers.values():
        if len(arrive) == 4:
            arrive[3].wait_recv()
        for name in steps:
            if name not in ("across", "on"):
                steps[name].wait_send()

    @pl.when(here.inner)
    def _():
        for steps, _ in numbers.values():
            steps["across"].wait_send()
            steps["on"].wait_send()

    close_slices(x_moves)
    close_slices(cot_moves)


def gather(shares, prepared, block_input, cotangent):
    micro, _, tokens, width = block_input.shape
    chunks = sum(len(pair) for pair in chunk_pairs(shares) + quad_pairs(shares))
    lengths = (shares.half, shares.depth // 2, TAIL)
    layer = [jax.ShapeDtypeStruct((2, 2, 4, rows, width), LOW) for rows in lengths]
    quad = jax.ShapeDtypeStruct((4, (lengths[0] + lengths[1]) // 2, width), LOW)
    window = jax.ShapeDtypeStruct((micro, 2, tokens // 2, width), LOW)
    anywhere = pl.BlockSpec(memory_space=pl.ANY)
    results = pl.pallas_call(
        partial(gather_kernel, shares),
        in_specs=[anywhere] * 5,
        out_specs=[anywhere] * 8,
        out_shape=layer + [quad, quad, layer[2]] + [window, window],
        scratch_shapes=[
            pltpu.SemaphoreType.DMA((10,)),
            pltpu.SemaphoreType.DMA((8,)),
            pltpu.SemaphoreType.DMA((8,)),
            pltpu.SemaphoreType.DMA((8,)),
            pltpu.SemaphoreType.DMA((8,)),
            pltpu.SemaphoreType.DMA((chunks, 5)),
            pltpu.SemaphoreType.DMA((chunks, 4)),
        ],
        compiler_params=pltpu.CompilerParams(collective_id=0, has_side_effects=True),
    )(*prepared, block_input, cotangent)
    return results[0:3], results[3:6], results[6], results[7]


def over(value, bit):
    return lax.ppermute(value, DP, [(i, i ^ bit) for i in range(4)])


def layout_moves(shares, y, x, pieces, arrays):
    proj, out, up, down = arrays
    rows_half, down_half = shares.half // 2, shares.depth // 4
    moves = []
    for part in range(2):
        rows = pl.ds(part * rows_half, rows_half)
        for index, (by_y, by_x) in enumerate(((0, 0), (1, 0), (0, 1), (1, 1))):
            piece = pieces[part][index]
            at_y, at_x = y ^ by_y, x ^ by_x
            top = pl.ds(0, rows_half)
            if at_y == 1:
                moves.append((piece.at[:, top], up.at[at_x, :, rows]))
            elif at_x == 0:
                moves.append((piece.at[:, top], proj.at[pl.ds(0, 4), rows]))
            else:
                moves.append((piece.at[pl.ds(0, 2), top], proj.at[pl.ds(4, 2), rows]))
                moves.append((piece.at[pl.ds(2, 2), top], out.at[:, rows]))
            moves.append(
                (
                    piece.at[:, pl.ds(rows_half, down_half)],
                    down.at[at_y, at_x, :, pl.ds(part * down_half, down_half)],
                )
            )
    return moves


def layout_kernel(shares, joins, *refs):
    sem = refs[-1]
    dp = lax.axis_index(DP)
    if joins:
        pieces, arrays = [refs[0:4], refs[4:8]], refs[8:12]
    else:
        arrays, pieces = refs[0:4], [refs[4:8], refs[8:12]]
    for spot in range(4):

        @pl.when(dp == spot)
        def _():
            copies = []
            for piece, place in layout_moves(shares, spot // 2, spot % 2, pieces, arrays):
                src, dst = (piece, place) if joins else (place, piece)
                copies.append(pltpu.make_async_copy(src, dst, sem.at[len(copies)]))
            for copy in copies:
                copy.start()
            for copy in copies:
                copy.wait()


def layout(shares, joins, *arrays):
    half, depth, width = shares.half, shares.depth // 2, shares.width
    if joins:
        shapes = [
            (6, half, width),
            (2, half, width),
            (2, 4, half, width),
            (2, 2, 4, depth, width),
        ]
    else:
        shapes = [(4, (half + depth) // 2, width)] * 8
    anywhere = pl.BlockSpec(memory_space=pl.ANY)
    return pl.pallas_call(
        partial(layout_kernel, shares, joins),
        in_specs=[anywhere] * len(arrays),
        out_specs=[anywhere] * len(shapes),
        out_shape=[jax.ShapeDtypeStruct(shape, LOW) for shape in shapes],
        scratch_shapes=[pltpu.SemaphoreType.DMA((18,))],
        cost_estimate=pl.CostEstimate(
            flops=0, bytes_accessed=64 * (half + depth) * width, transcendentals=0
        ),
    )(*arrays)


def spread_quads(shares, quads):
    low, high = quads
    low_y, low_x, high_y, high_x = over(low, 2), over(low, 1), over(high, 2), over(high, 1)
    return layout(shares, True, low, low_y, low_x, over(low_y, 1), high, high_y, high_x, over(high_x, 2))


def sum_quads(shares, arrays):
    pieces = layout(shares, False, *arrays)

    def total(*terms):
        return sum(term.astype(jnp.float32) for term in terms).astype(LOW)

    own, by_y, by_x, both = pieces[:4]
    low = total(own, over(by_x, 1), over(total(by_y, over(both, 1)), 2))
    own, by_y, by_x, both = pieces[4:]
    high = total(own, over(by_y, 2), over(total(by_x, over(both, 2)), 1))
    return low, high


def scatter_kernel(shares, *refs):
    (proj, out, up, down, vec_zero, low, high, vec_one), refs = refs[:8], refs[8:]
    (dx_ref, final_ref, halves, slices), refs = refs[:4], refs[4:]
    work, refs = [refs[0:3], refs[3:6]], refs[6:]
    (got_one, got_two, got_far, got_across, got_near, total), refs = refs[:6], refs[6:]
    load, local, swap_send, swap_recv, z_send, z_recv, send, recv = refs
    here = Place()
    core, y, x, z = here.core, here.y, here.x, here.z
    rows_half, down_half = shares.half // 2, shares.depth // 4
    down_base = shares.half
    tail_base = shares.half + shares.depth // 2

    rows = work[0][0]
    moves = [
        [
            (proj.at[pl.ds(0, 4)], rows.at[0, 0]),
            (proj.at[pl.ds(4, 2)], rows.at[0, 1, pl.ds(0, 2)]),
            (out, rows.at[0, 1, pl.ds(2, 2)]),
            (up, rows.at[1]),
            (down, work[0][1]),
            (vec_zero, work[0][2]),
        ],
        [(low, work[1][0]), (high, work[1][1]), (vec_one, work[1][2])],
    ]
    loads = [
        [
            pltpu.make_async_copy(src, dst, load.at[layer, index])
            for index, (src, dst) in enumerate(moves[layer])
        ]
        for layer in range(2)
    ]
    for layer in (1, 0):
        for copy in loads[layer]:
            copy.start()
    here.greet()

    def place_of(layer, array, start):
        if array == 2:
            return tail_base
        if layer == 0:
            return (0, down_base)[array] + start
        if start < rows_half:
            return array * rows_half + start
        return down_base + array * down_half + start - rows_half

    pairs, chunks = [], []
    for layer in (1, 0):
        for index, pair in enumerate(quad_pairs(shares) if layer else chunk_pairs(shares)):
            entry = []
            for array, start, length, order in pair:
                entry.append((len(chunks), layer, array, start, length, order))
                chunks.append(entry[-1])
            pairs.append((index, entry))

    def pieces(chunk):
        number, layer, array, start, length, order = chunk
        ref = work[layer][array]
        rows = pl.ds(start, length)
        sems = (send, recv)
        keeps, slots, copies = [], [], []

        def part(which):
            return ref.at[which, rows] if order is None else ref.at[y, x, which, rows]

        def add(src, slot, device, keep):
            spots = (number, len(copies))
            copies.append(remote(src, slot, sems, (spots, spots), device))
            slots.append(slot)
            keeps.append(keep)

        room = pl.ds(0, length)
        if order == 0:
            add(ref.at[:, 1 - x, :, rows], got_one.at[number, :, :, room], here.along_x, ref.at[:, x, :, rows])
            add(ref.at[1 - y, x, :, rows], got_two.at[number, :, room], here.along_y, ref.at[y, x, :, rows])
        elif order == 1:
            add(ref.at[1 - y, :, :, rows], got_one.at[number, :, :, room], here.along_y, ref.at[y, :, :, rows])
            add(ref.at[y, 1 - x, :, rows], got_two.at[number, :, room], here.along_x, ref.at[y, x, :, rows])
        else:
            copies, slots, keeps = [None] * 2, [None] * 2, [None] * 2
        add(part(here.far), got_far.at[number, :, room], here.beside, part(here.far))
        add(part(here.far), got_across.at[number, :, room], here.across, part(here.near))
        add(part(here.next), got_near.at[number, :, room], here.beside, part(here.own))
        return copies, keeps, slots

    built = [pieces(chunk) for chunk in chunks]
    loaded = set()

    def land(number, phase):
        copies, keeps, slots = built[number]
        copies[phase].wait_recv()
        keep, slot = keeps[phase], slots[phase]
        keep[...] = keep[...] + slot[...]

    def run(chunk, phase):
        number, layer, array, start, length, order = chunk
        copies, keeps, slots = built[number]
        if (layer, array) not in loaded:
            loaded.add((layer, array))
            spots = ((0, 1, 2, 3), (4,), (5,))[array] if layer == 0 else (array,)
            for spot in spots:
                loads[layer][spot].wait()
        if phase < 2:
            if order is not None:
                if phase:
                    land(number, 0)
                copies[phase].start()
        elif phase == 2:
            if order is not None:
                land(number, 1)

            @pl.when(here.outer)
            def _():
                copies[2].start()
                copies[4].start()

        elif phase == 3:

            @pl.when(here.inner)
            def _():
                land(number, 2)
                copies[3].start()

        elif phase == 4:

            @pl.when(here.inner)
            def _():
                land(number, 3)
                copies[4].start()

        else:
            copies[4].wait_recv()
            spot = pl.ds(place_of(layer, array, start), length)
            total[layer, spot, :] = (keeps[4][...] + slots[4][...])[0]

    for tick in range(len(pairs) + 6):
        for phase in (5, 4, 3, 2, 1, 0):
            for index, entry in pairs:
                for chunk in entry:
                    first = 2 if chunk[5] is None else 0
                    if first <= phase and index + phase - first == tick:
                        run(chunk, phase)
        if tick == 0:
            for section, source in ((0, dx_ref), (1, final_ref)):

                @pl.when(core == section)
                def _():
                    pltpu.make_async_copy(source.at[z], slices.at[z], local.at[0]).start()
                    for by in (1, 2, 3):
                        remote(
                            source.at[(z + by) % 4],
                            slices.at[z],
                            (z_send, z_recv),
                            (by - 1, by - 1),
                            here.others[by - 1],
                        ).start()

    for copies, _, _ in built:
        for index in (0, 1, 4):
            if copies[index] is not None:
                copies[index].wait_send()
    for section, index in ((here.outer, 2), (here.inner, 3)):

        @pl.when(section)
        def _():
            for copies, _, _ in built:
                copies[index].wait_send()

    swaps = (swap_send, swap_recv)
    across = remote(total.at[1 - core], halves.at[core], swaps, (0, 0), here.partner)
    across.start()
    own = pltpu.make_async_copy(total.at[core], halves.at[core], local.at[1])
    own.start()
    own.wait()
    across.wait_send()
    remote(total.at[1 - core], halves.at[1 - core], swaps, (0, 0), here.partner).wait_recv()
    pltpu.make_async_copy(dx_ref.at[z], slices.at[z], local.at[0]).wait()
    for by in (1, 2, 3):
        copy = remote(
            dx_ref.at[z],
            slices.at[(z + 4 - by) % 4],
            (z_send, z_recv),
            (by - 1, by - 1),
            here.others[by - 1],
        )
        copy.wait_send()
        copy.wait_recv()


def scatter(shares, arrays, vec_zero, quads, vec_one, grad, final):
    micro, tokens, width = grad.shape
    lengths = (shares.half, shares.depth // 2, TAIL)
    chunks = sum(len(pair) for pair in chunk_pairs(shares) + quad_pairs(shares))
    rows = sum(lengths)
    anywhere = pl.BlockSpec(memory_space=pl.ANY)
    work = [pltpu.VMEM((2, 2, 4, length, width), LOW) for length in lengths]
    quad = pltpu.VMEM((4, (lengths[0] + lengths[1]) // 2, width), LOW)
    return pl.pallas_call(
        partial(scatter_kernel, shares),
        in_specs=[anywhere] * 10,
        out_specs=[anywhere] * 2,
        out_shape=[
            jax.ShapeDtypeStruct((2, rows, width), LOW),
            jax.ShapeDtypeStruct((micro, tokens, width), LOW),
        ],
        scratch_shapes=work
        + [quad, quad, work[2]]
        + [
            pltpu.VMEM((chunks, 2, 4, PIECE, width), LOW),
            pltpu.VMEM((chunks, 4, PIECE, width), LOW),
            pltpu.VMEM((chunks, 2, PIECE, width), LOW),
            pltpu.VMEM((chunks, 2, PIECE, width), LOW),
            pltpu.VMEM((chunks, 1, PIECE, width), LOW),
            pltpu.VMEM((2, rows, width), LOW),
            pltpu.SemaphoreType.DMA((2, 6)),
            pltpu.SemaphoreType.DMA((2,)),
            pltpu.SemaphoreType.DMA((1,)),
            pltpu.SemaphoreType.DMA((1,)),
            pltpu.SemaphoreType.DMA((3,)),
            pltpu.SemaphoreType.DMA((3,)),
            pltpu.SemaphoreType.DMA((chunks, 5)),
            pltpu.SemaphoreType.DMA((chunks, 5)),
        ],
        compiler_params=pltpu.CompilerParams(
            collective_id=1, has_side_effects=True, vmem_limit_bytes=VMEM_BYTES
        ),
    )(*arrays, vec_zero, *quads, vec_one, grad, final)


def update_kernel(shares, halves_ref, *refs):
    old, new, turned = refs[:9], refs[9:18], refs[18]
    offset = lax.axis_index((DP, SEQ)) * shares.columns
    half, per, width, depth = shares.half, shares.per, shares.width, shares.depth // 2
    is_inner = (offset >= 3 * width) & (offset < 4 * width)
    is_hidden = offset >= 4 * width

    @pl.when(is_inner)
    def _():
        for side in range(2):
            piece = halves_ref[side, :half, :].astype(jnp.float32)
            wide = per * half
            back = jnp.transpose(jnp.concatenate([piece[:, :wide], piece[:, wide:]], axis=0))
            for j in range(per):
                turned[(2 * j + side) * half : (2 * j + side + 1) * half, :] = back[
                    j * half : (j + 1) * half
                ]

    @pl.when(jnp.logical_not(is_inner))
    def _():
        pair = [halves_ref[side, :half, :].astype(jnp.float32) for side in range(2)]
        plain = jnp.concatenate(pair, axis=0)
        hidden = jnp.concatenate(
            [pair[side][j * depth :][:depth] for j in range(shares.groups) for side in range(2)],
            axis=0,
        )
        turned[...] = jnp.transpose(jnp.where(is_hidden, hidden, plain))

    def store(first, gradient, rate, decay):
        results = adam_update(*[ref[...] for ref in old[first : first + 3]], gradient, rate, decay)
        for ref, result in zip(new[first : first + 3], results):
            ref[...] = result

    store(0, turned[...], rate_matrix, decay_matrix)
    down = [halves_ref[side, half : half + depth, :] for side in range(2)]
    store(3, jnp.concatenate(down, axis=0).astype(jnp.float32), rate_matrix, decay_matrix)
    tails = [halves_ref[side, half + depth :, :].astype(jnp.float32) for side in range(2)]
    store(6, (tails[0] + tails[1])[0:1, : shares.vector_len], rate_vector, 0.0)


def update(shares, halves, old):
    return pl.pallas_call(
        partial(update_kernel, shares),
        out_shape=[jax.ShapeDtypeStruct(piece.shape, jnp.float32) for piece in old],
        scratch_shapes=[pltpu.VMEM((shares.width, shares.columns), jnp.float32)],
        compiler_params=pltpu.CompilerParams(vmem_limit_bytes=VMEM_BYTES),
    )(halves, *old)


def window_forward(hidden, weights, biases, features):
    proj, out, up, down = weights
    gain_one, shift_one, bias_query, bias_value, bias_out = biases[:5]
    gain_two, shift_two, bias_down, bias_up = biases[5:]
    unit, _ = normalized(hidden)
    normed = (unit * gain_one + shift_one).astype(LOW)
    bias = jnp.concatenate([bias_query, jnp.zeros_like(bias_query), bias_value])
    projected = (dot_rows(normed, proj) + bias).astype(LOW)
    attended, levels = attend(projected, *features, bias_query.shape[0])
    branch = dot_rows(attended, out)
    middle = hidden + (branch + swap(branch.astype(LOW)).astype(jnp.float32) + bias_out)
    unit_two, _ = normalized(middle)
    normed_two = (unit_two * gain_two + shift_two).astype(LOW)
    up_value = dot_rows(normed_two, up) + bias_up
    cdf = 0.5 * (1.0 + lax.erf(up_value * 0.5**0.5))
    active = (up_value * cdf).astype(LOW)
    slope = cdf + up_value * jnp.exp(-0.5 * up_value * up_value) * (0.5 / math.pi) ** 0.5
    part = dot_plain(active, down)
    output = middle + (part + swap(part.astype(LOW)).astype(jnp.float32) + bias_down)
    return output, (hidden, normed, projected, attended, levels, middle, normed_two, slope, active)


def window_backward(stored, grad_output, weights, biases, features):
    hidden, normed, projected, attended, levels, middle, normed_two, slope, active = stored
    proj, out, up, down = weights
    gain_one, gain_two = biases[0], biases[5]
    grad_ffn = grad_output.astype(LOW)
    grad_bias_down = jnp.sum(grad_ffn.astype(jnp.float32), axis=0)
    grad_up = (dot_rows(grad_ffn, down) * slope).astype(LOW)
    grad_bias_up = jnp.sum(grad_up.astype(jnp.float32), axis=0)
    part = dot_plain(grad_up, up)
    arrived = swap(part.astype(LOW)).astype(jnp.float32)
    down_grad = dot_tokens(active, grad_ffn).astype(LOW)
    up_grad = dot_tokens(grad_up, normed_two).astype(LOW)
    grad_norm, grad_gain_two, grad_shift_two = norm_back(middle, part + arrived, gain_two)
    grad_middle = grad_output + grad_norm
    grad_branch = grad_middle.astype(LOW)
    grad_bias_out = jnp.sum(grad_branch.astype(jnp.float32), axis=0)
    out_grad = dot_tokens(grad_branch, attended).astype(LOW)
    grad_attended = dot_plain(grad_branch, out).astype(LOW)
    grad_proj = attend_back(projected, grad_attended, attended, levels, *features)
    summed = jnp.sum(grad_proj.astype(jnp.float32), axis=0)
    width = attended.shape[1]
    part = dot_plain(grad_proj, proj)
    arrived = swap(part.astype(LOW)).astype(jnp.float32)
    proj_grad = dot_tokens(grad_proj, normed).astype(LOW)
    grad_norm, grad_gain_one, grad_shift_one = norm_back(hidden, part + arrived, gain_one)
    vector_grads = (
        grad_gain_one,
        grad_shift_one,
        summed[:width],
        summed[2 * width :],
        grad_bias_out,
        grad_gain_two,
        grad_shift_two,
        grad_bias_down,
        grad_bias_up,
    )
    return grad_middle + grad_norm, (proj_grad, out_grad, up_grad, down_grad), vector_grads


def window_shards(
    block_input,
    cotangent,
    random_ids,
    segment_ids,
    global_ids,
    w_rows,
    w_rows_first,
    w_rows_second,
    w_down,
    w_down_first,
    w_down_second,
    vectors,
    vectors_first,
    vectors_second,
):
    core = lax.axis_index(SECTION)
    place = lax.axis_index(SEQ)
    micro, _, tokens, width = block_input.shape
    _, _, columns = w_rows.shape
    shares = Shares(width, columns, w_down.shape[1], vectors.shape[1])
    prepared = prepare(shares, w_rows[0], w_down[0], vectors)
    gathered_zero, gathered_one, hidden, grad = gather(shares, prepared, block_input, cotangent)

    head_half = shares.half // (width // HEADS)
    random_rows = lax.dynamic_index_in_dim(random_ids[:, 0], place, 0, keepdims=False)
    random_rows = random_rows.reshape(random_rows.shape[0], shares.per, 2, head_half, -1)
    random_rows = lax.dynamic_index_in_dim(random_rows, core, 2, keepdims=False)
    random_rows = random_rows.reshape(random_rows.shape[0], shares.per * head_half, -1)
    segments = lax.dynamic_index_in_dim(segment_ids[:, 0], place, 0, keepdims=False)
    global_rows = lax.dynamic_index_in_dim(global_ids[:, 0], place, 0, keepdims=False)
    features = key_features(random_rows, segments, global_rows)

    gathered_one = (*spread_quads(shares, gathered_one[:2]), gathered_one[2])
    params = [shares.unpack(piece, core) for piece in (gathered_zero, gathered_one)]
    hidden = hidden.reshape(-1, width).astype(jnp.float32)
    output, stored_zero = window_forward(hidden, *params[0], features)
    hidden = output.astype(LOW).astype(jnp.float32)
    final, stored_one = window_forward(hidden, *params[1], features)
    final = final.astype(LOW).reshape(micro, tokens, width)

    grad = grad.reshape(-1, width).astype(jnp.float32)
    grad, *grads_one = window_backward(stored_one, grad, *params[1], features)
    *arrays_one, vec_one = shares.by_shard(*grads_one, core)
    quads_one = sum_quads(shares, arrays_one)
    grad = grad.astype(LOW).astype(jnp.float32)
    grad, *grads_zero = window_backward(stored_zero, grad, *params[0], features)
    grad = grad.astype(LOW).reshape(micro, tokens, width)
    *arrays_zero, vec_zero = shares.by_shard(*grads_zero, core)
    halves, slices = scatter(shares, arrays_zero, vec_zero, quads_one, vec_one, grad, final)
    section_result = slices.astype(jnp.float32)[None, :, None]
    old = [
        w_rows[0],
        w_rows_first[0],
        w_rows_second[0],
        w_down[0],
        w_down_first[0],
        w_down_second[0],
        vectors,
        vectors_first,
        vectors_second,
    ]
    new = update(shares, halves, old)
    return (section_result, *[piece[None] for piece in new[:6]], *new[6:])


def one_window_each(mesh, block_input, w_rows, w_down, vectors):
    micro, windows, length, width = block_input.shape
    shards = mesh.shape[DP] * mesh.shape[SEQ]
    columns, depth = w_rows.shape[2] // shards, w_down.shape[1] // shards
    head_dim = width // HEADS
    tokens = length // mesh.shape[SEQ]
    return (
        mesh.shape[SECTION] == 2
        and mesh.shape[SEQ] == micro
        and mesh.shape[DP] == windows
        and tokens % (2 * BLOCK) == 0
        and length % CHUNK == 0
        and head_dim == 64
        and width % columns == 0
        and columns % (2 * head_dim) == 0
        and columns % depth == 0
        and width // columns * (columns // 2) % 128 == 0
        and depth % 32 == 0
        and vectors.shape[1] // shards <= width
        and mesh.shape[DP] == 4
        and micro == 4
        and width == 2 * columns
        and (columns // 2) % (2 * PIECE) == 0
        and (depth // 2) % (2 * PIECE) == 0
    )


def solution(mesh):
    in_specs = (
        P(None, DP, SEQ, None),
        P(None, DP, SEQ, None),
        P(None, DP, None, None, None),
        P(None, DP, None),
        P(None, DP, None),
        P(SECTION, None, (DP, SEQ)),
        P(SECTION, None, (DP, SEQ)),
        P(SECTION, None, (DP, SEQ)),
        P(SECTION, (DP, SEQ), None),
        P(SECTION, (DP, SEQ), None),
        P(SECTION, (DP, SEQ), None),
        P(SECTION, (DP, SEQ)),
        P(SECTION, (DP, SEQ)),
        P(SECTION, (DP, SEQ)),
    )
    out_specs = (
        P(SECTION, None, DP, SEQ, None),
        P(SECTION, None, (DP, SEQ)),
        P(SECTION, None, (DP, SEQ)),
        P(SECTION, None, (DP, SEQ)),
        P(SECTION, (DP, SEQ), None),
        P(SECTION, (DP, SEQ), None),
        P(SECTION, (DP, SEQ), None),
        P(SECTION, (DP, SEQ)),
        P(SECTION, (DP, SEQ)),
        P(SECTION, (DP, SEQ)),
    )

    def step(*arrays):
        chosen = general_shards
        if one_window_each(mesh, arrays[0], arrays[5], arrays[8], arrays[11]):
            chosen = window_shards
        return jax.shard_map(
            chosen, mesh=mesh, in_specs=in_specs, out_specs=out_specs, check_vma=False
        )(*arrays)

    return step
```

```python
import math
from functools import partial

import jax
import jax.numpy as jnp
import ml_dtypes
import numpy as np
from jax import lax
from jax.experimental import pallas as pl
from jax.experimental.pallas import tpu as pltpu
from jax.sharding import PartitionSpec as P

SECTION, DP, SEQ = "section", "dp", "seq"
HEADS = 12
BLOCK = 64
STEP = 5


epsilon = 1e-05
masked = -1e30
rate_matrix = 0.02
rate_vector = 0.2
decay_matrix = 0.01


def with_halo(x, sides, width):
    for axis, dim in sides:
        devices, length = (lax.axis_size(axis), x.shape[dim])
        up = [(i, (i + 1) % devices) for i in range(devices - 1)]
        down = [(j, i) for i, j in up]
        last = lax.slice_in_dim(x, length - width, length, axis=dim)
        initial = lax.slice_in_dim(x, 0, width, axis=dim)
        before = lax.ppermute(last, axis, up)
        after = lax.ppermute(initial, axis, down)
        x = jnp.concatenate([before, x, after], axis=dim)
    return x


def merged(value, axis, join):
    pieces = jax.tree.map(lambda part: lax.all_gather(part, axis), value)
    head = jax.tree.map(lambda part: part[0], pieces)
    tail = jax.tree.map(lambda part: part[1:], pieces)
    subtotal, _ = lax.scan(lambda subtotal, share: (join(subtotal, share), None), head, tail)
    return subtotal


def from_behind(x, axis, by):
    devices = lax.axis_size(axis)
    pairs = [(i, i + by) for i in range(devices) if 0 <= i + by < devices]
    return lax.ppermute(x, axis, pairs)


def partner(value, axis, bit):
    mask = 2**bit
    pairs = [(source, source ^ mask) for source in range(lax.axis_size(axis))]
    return lax.ppermute(value, axis, pairs)


def mixed_sum(form, left, right):
    return jnp.einsum(form, left, right, preferred_element_type=jnp.float32)


def exact_two(form, left, right):
    return jnp.einsum(
        form, left, right, precision=lax.Precision.HIGHEST, preferred_element_type=jnp.float32
    )


def norm_rows(values_in, gain_vec, shift_vec):
    row_mean = jnp.mean(values_in, axis=-1, keepdims=True)
    centred = values_in - row_mean
    spread = jnp.mean(centred * centred, axis=-1, keepdims=True)
    return centred * lax.rsqrt(spread + epsilon) * gain_vec + shift_vec


def split_vectors(vector_weights, model_width):
    pieces = [
        vector_weights[piece_index * model_width : (piece_index + 1) * model_width]
        for piece_index in range(8)
    ]
    return pieces + [vector_weights[8 * model_width :]]


def route_tables(random_rows, segments, global_rows, seq_place, groups):
    windows, blocks, head_count, pick_count = random_rows.shape
    blocks_dev = blocks // groups
    request_count = blocks_dev * head_count * pick_count
    capacity = -(-request_count // groups)
    requests = random_rows.reshape(windows, groups, request_count)
    owners = requests // blocks_dev
    inside = requests % blocks_dev
    head_of = jnp.arange(request_count) // pick_count % head_count
    is_mine = owners == seq_place
    slot_index = jnp.cumsum(is_mine.astype(jnp.int32), axis=2) - 1
    slot_hot = ((slot_index[..., None] == jnp.arange(capacity)) & is_mine[..., None]).astype(
        jnp.float32
    )
    inside_hot = (inside[..., None] == jnp.arange(blocks_dev)).astype(jnp.float32)
    head_hot = (head_of[:, None] == jnp.arange(head_count)).astype(jnp.float32)
    sender = jnp.einsum(
        "wqsc,wqsb,sh->wqcbh", slot_hot, inside_hot, head_hot, precision=lax.Precision.HIGHEST
    )
    my_owners = lax.dynamic_index_in_dim(owners, seq_place, axis=1, keepdims=False)
    earlier = jnp.arange(request_count)[None, :] < jnp.arange(request_count)[:, None]
    same_owner = my_owners[:, :, None] == my_owners[:, None, :]
    rank_index = jnp.sum((same_owner & earlier[None]).astype(jnp.int32), axis=2)
    picker = (
        (my_owners[..., None, None] == jnp.arange(groups)[:, None])
        & (rank_index[..., None, None] == jnp.arange(capacity)[None, :])
    ).astype(jnp.float32)
    first_block = seq_place * blocks_dev
    owned_hot = (global_rows[:, :, None] == first_block + jnp.arange(blocks_dev)).astype(
        jnp.float32
    )
    length = segments.shape[1]
    block_len = length // blocks
    seg_blocks = segments.reshape(windows, blocks, block_len)
    seg_pad = jnp.pad(seg_blocks, ((0, 0), (1, 1), (0, 0)), constant_values=-1)
    near_segs = lax.dynamic_slice_in_dim(seg_pad, first_block, blocks_dev + 2, axis=1)
    slide_seg = jnp.concatenate([near_segs[:, :-2], near_segs[:, 1:-1], near_segs[:, 2:]], axis=2)
    query_seg = near_segs[:, 1:-1]
    rows_index = jnp.arange(windows)
    global_seg = seg_blocks[rows_index[:, None], global_rows].reshape(windows, -1)
    chosen = lax.dynamic_slice_in_dim(random_rows, first_block, blocks_dev, axis=1)
    far_seg = seg_blocks[rows_index[:, None, None, None], chosen].reshape(
        windows, blocks_dev, head_count, -1
    )
    key_seg = jnp.concatenate(
        [
            jnp.broadcast_to(
                slide_seg[:, :, None, :], (windows, blocks_dev, head_count, slide_seg.shape[2])
            ),
            jnp.broadcast_to(
                global_seg[:, None, None, :], (windows, blocks_dev, head_count, global_seg.shape[1])
            ),
            far_seg,
        ],
        axis=3,
    )
    key_mask = query_seg[:, :, None, :, None] == key_seg[:, :, :, None, :]
    local_seg = query_seg.reshape(windows, -1)
    full_mask = global_seg[:, None, :, None] == local_seg[:, None, None, :]
    return (sender, picker, owned_hot, key_mask, full_mask)


def fetch_blocks(paired, queries, sender, picker, owned_hot):
    windows, tokens, head_count, doubled = paired.shape
    head_dim = queries.shape[-1]
    blocks_dev = tokens // BLOCK
    flattened = paired.reshape(windows, tokens, head_count * doubled)
    padded = with_halo(flattened, ((SEQ, 1),), BLOCK)
    framed = padded.reshape(windows, blocks_dev + 2, BLOCK, head_count, doubled)
    sliding = jnp.concatenate([framed[:, :-2], framed[:, 1:-1], framed[:, 2:]], axis=2)
    local_blocks = paired.reshape(windows, blocks_dev, BLOCK, head_count, doubled)
    owned_low = owned_hot.astype(jnp.bfloat16)
    offered = mixed_sum("wgb,wbthe->wgthe", owned_low, local_blocks)
    offered_queries = mixed_sum("wgb,wbqhd->wgqhd", owned_low, queries)
    global_kv, global_queries = (
        lax.psum(offered.astype(jnp.bfloat16), SEQ).astype(jnp.float32),
        lax.psum(offered_queries.astype(jnp.bfloat16), SEQ).astype(jnp.float32),
    )
    global_kv = global_kv.astype(jnp.bfloat16).reshape(windows, -1, head_count, doubled)
    global_queries = global_queries.astype(jnp.bfloat16).reshape(windows, -1, head_count, head_dim)
    outgoing = mixed_sum("wqcbh,wbthe->qwcte", sender.astype(jnp.bfloat16), local_blocks).astype(
        jnp.bfloat16
    )
    incoming = lax.all_to_all(outgoing, SEQ, split_axis=0, concat_axis=0, tiled=True)
    distant = mixed_sum("wspc,pwcte->wste", picker.astype(jnp.bfloat16), incoming).astype(
        jnp.bfloat16
    )
    pick_count = picker.shape[1] // (blocks_dev * head_count)
    distant = distant.reshape(windows, blocks_dev, head_count, pick_count, BLOCK, doubled)
    return (sliding, global_kv, distant, global_queries)


def combine_stats(earlier, later):
    top = jnp.maximum(earlier[0], later[0])
    return (top, earlier[1] * jnp.exp(earlier[0] - top) + later[1] * jnp.exp(later[0] - top))


def full_forward(global_queries, key_part, value_part, full_mask, head_dim):
    scores = mixed_sum("wqhd,wkhd->whqk", global_queries, key_part) * head_dim ** (-0.5)
    scores = jnp.where(full_mask, scores, masked)
    local_top = jnp.max(scores, axis=3, keepdims=True)
    local_sum = jnp.sum(
        jnp.where(full_mask, jnp.exp(scores - local_top), 0.0), axis=3, keepdims=True
    )
    row_top, row_sum = merged((local_top, local_sum), SEQ, combine_stats)
    full_probs = jnp.where(full_mask, jnp.exp(scores - row_top), 0.0) / row_sum
    partial_out = mixed_sum("whqk,wkhd->wqhd", full_probs.astype(jnp.bfloat16), value_part)
    full_out = lax.psum(partial_out.astype(jnp.bfloat16), SEQ).astype(jnp.float32)
    return (full_out, full_probs)


def attention_weights(queries, sliding, global_kv, distant, key_mask):
    head_dim = queries.shape[-1]
    windows, blocks_dev, _, head_count, _ = queries.shape
    near_scores = mixed_sum("wbqhd,wbkhd->wbhqk", queries, sliding[..., :head_dim])
    global_scores = mixed_sum("wbqhd,wkhd->wbhqk", queries, global_kv[..., :head_dim])
    far_scores = mixed_sum("wbqhd,wbhrkd->wbhqrk", queries, distant[..., :head_dim])
    far_scores = far_scores.reshape(windows, blocks_dev, head_count, BLOCK, -1)
    scores = jnp.concatenate([near_scores, global_scores, far_scores], axis=4) * head_dim ** (-0.5)
    scores = jnp.where(key_mask, scores, masked)
    row_top = jnp.max(scores, axis=4, keepdims=True)
    weight = jnp.exp(scores - row_top)
    return weight / jnp.sum(weight, axis=4, keepdims=True)


def split_keys(scores_like, sliding, global_kv, distant):
    near_keys = sliding.shape[2]
    global_keys = global_kv.shape[1]
    windows, blocks_dev, head_count, pick_count, _, _ = distant.shape
    near_part = scores_like[..., :near_keys]
    global_part = scores_like[..., near_keys : near_keys + global_keys]
    far_part = scores_like[..., near_keys + global_keys :].reshape(
        windows, blocks_dev, head_count, BLOCK, pick_count, BLOCK
    )
    return (near_part, global_part, far_part)


def attention_values(low_probs, sliding, global_kv, distant, head_dim):
    near_part, global_part, far_part = split_keys(low_probs, sliding, global_kv, distant)
    attended = mixed_sum("wbhqk,wbkhd->wbqhd", near_part, sliding[..., head_dim:])
    attended = attended + mixed_sum("wbhqk,wkhd->wbqhd", global_part, global_kv[..., head_dim:])
    return attended + mixed_sum("wbhqrk,wbhrkd->wbqhd", far_part, distant[..., head_dim:])


def layer_forward(hidden, weights, tables):
    row_weights, down_weights, vector_weights = weights
    sender, picker, owned_hot, key_mask, full_mask = tables
    model_width = row_weights.shape[0]
    windows, tokens, _ = hidden.shape
    blocks_dev = tokens // BLOCK
    head_dim = model_width // HEADS
    (
        gain_one,
        shift_one,
        bias_query,
        bias_value,
        bias_out,
        gain_two,
        shift_two,
        bias_down,
        bias_up,
    ) = split_vectors(vector_weights, model_width)
    normed = norm_rows(hidden, gain_one, shift_one).astype(jnp.bfloat16)
    projected = mixed_sum("wtd,de->wte", normed, row_weights[:, : 3 * model_width])
    projected = (
        projected + jnp.concatenate([bias_query, jnp.zeros_like(bias_query), bias_value])
    ).astype(jnp.bfloat16)
    queries = projected[..., :model_width].reshape(windows, blocks_dev, BLOCK, HEADS, head_dim)
    key_part = projected[..., model_width : 2 * model_width].reshape(
        windows, tokens, HEADS, head_dim
    )
    value_part = projected[..., 2 * model_width :].reshape(windows, tokens, HEADS, head_dim)
    paired = jnp.concatenate([key_part, value_part], axis=3)
    sliding, global_kv, distant, global_queries = fetch_blocks(
        paired, queries, sender, picker, owned_hot
    )
    probabilities = attention_weights(queries, sliding, global_kv, distant, key_mask)
    attended = attention_values(
        probabilities.astype(jnp.bfloat16), sliding, global_kv, distant, head_dim
    )
    full_out, full_probs = full_forward(global_queries, key_part, value_part, full_mask, head_dim)
    placed = exact_two(
        "wgb,wgqhd->wbqhd", owned_hot, full_out.reshape(windows, -1, BLOCK, HEADS, head_dim)
    )
    on_global = jnp.sum(owned_hot, axis=1)[:, :, None, None, None] > 0
    attended = jnp.where(on_global, placed, attended)
    mixed_low = attended.reshape(windows, tokens, model_width).astype(jnp.bfloat16)
    middle = (
        hidden
        + mixed_sum("wtd,de->wte", mixed_low, row_weights[:, 3 * model_width : 4 * model_width])
        + bias_out
    )
    normed_two = norm_rows(middle, gain_two, shift_two).astype(jnp.bfloat16)
    up_value = mixed_sum("wtd,df->wtf", normed_two, row_weights[:, 4 * model_width :]) + bias_up
    active = jax.nn.gelu(up_value, approximate=False).astype(jnp.bfloat16)
    output = middle + mixed_sum("wtf,fd->wtd", active, down_weights) + bias_down
    stored = (
        hidden,
        normed,
        queries,
        sliding,
        global_kv,
        distant,
        probabilities,
        mixed_low,
        middle,
        normed_two,
        up_value,
        active,
        key_part,
        value_part,
        global_queries,
        full_probs,
    )
    return (output, stored)


def return_blocks(near_back, global_back, far_back, query_part, sender, picker, owned_hot):
    windows, blocks_dev, _, head_count, doubled = near_back.shape
    first_third = near_back[:, :, :BLOCK]
    centre_third = near_back[:, :, BLOCK : 2 * BLOCK]
    last_third = near_back[:, :, 2 * BLOCK :]
    framed = jnp.pad(first_third, ((0, 0), (0, 2), (0, 0), (0, 0), (0, 0)))
    framed = framed + jnp.pad(centre_third, ((0, 0), (1, 1), (0, 0), (0, 0), (0, 0)))
    framed = framed + jnp.pad(last_third, ((0, 0), (2, 0), (0, 0), (0, 0), (0, 0)))
    own_grad = framed[:, 1:-1]
    for direction in (1, -1):
        rim_grad = framed[:, -1] if direction == 1 else framed[:, 0]
        arrived = from_behind(rim_grad.astype(jnp.bfloat16), SEQ, direction).astype(
            rim_grad.dtype
        )
        if direction == 1:
            own_grad = jnp.concatenate(
                [own_grad[:, :1] + arrived[:, None], own_grad[:, 1:]], axis=1
            )
        else:
            own_grad = jnp.concatenate(
                [own_grad[:, :-1], own_grad[:, -1:] + arrived[:, None]], axis=1
            )
    global_total, query_total = (
        lax.psum(
            global_back.reshape(windows, -1, BLOCK, head_count, doubled).astype(jnp.bfloat16), SEQ
        ).astype(jnp.float32),
        lax.psum(query_part.astype(jnp.bfloat16), SEQ).astype(jnp.float32),
    )
    own_grad = own_grad + exact_two("wgb,wgthe->wbthe", owned_hot, global_total)
    far_flat = far_back.reshape(windows, -1, BLOCK, doubled)
    returning = exact_two("wspc,wste->pwcte", picker, far_flat)
    arrived_far = lax.all_to_all(
        returning.astype(jnp.bfloat16), SEQ, split_axis=0, concat_axis=0, tiled=True
    ).astype(returning.dtype)
    own_grad = own_grad + exact_two("wqcbh,qwcte->wbthe", sender, arrived_far)
    return (own_grad.reshape(windows, blocks_dev * BLOCK, head_count, doubled), query_total)


def attention_back(
    grad_attended,
    queries,
    sliding,
    global_kv,
    distant,
    probabilities,
    key_part,
    value_part,
    global_queries,
    full_probs,
    sender,
    picker,
    owned_hot,
):
    head_dim = queries.shape[-1]
    score_scale = head_dim ** (-0.5)
    windows, blocks_dev, _, head_count, _ = queries.shape
    on_global = jnp.sum(owned_hot, axis=1)[:, :, None, None, None] > 0
    selected = mixed_sum("wgb,wbqhd->wgqhd", owned_hot.astype(jnp.bfloat16), grad_attended)
    rows_grad = lax.psum(selected.astype(jnp.bfloat16), SEQ).reshape(
        windows, -1, head_count, head_dim
    )
    grad_attended = jnp.where(on_global, jnp.zeros_like(grad_attended), grad_attended)
    low_probs = probabilities.astype(jnp.bfloat16)
    near_grad = mixed_sum("wbqhd,wbkhd->wbhqk", grad_attended, sliding[..., head_dim:])
    global_grad = mixed_sum("wbqhd,wkhd->wbhqk", grad_attended, global_kv[..., head_dim:])
    far_grad = mixed_sum("wbqhd,wbhrkd->wbhqrk", grad_attended, distant[..., head_dim:])
    far_grad = far_grad.reshape(windows, blocks_dev, head_count, BLOCK, -1)
    grad_probs = jnp.concatenate([near_grad, global_grad, far_grad], axis=4)
    grad_scores = probabilities * (
        grad_probs - jnp.sum(probabilities * grad_probs, axis=4, keepdims=True)
    )
    grad_scores = grad_scores.astype(jnp.bfloat16)
    near_split, global_split, far_split = split_keys(grad_scores, sliding, global_kv, distant)
    near_probs, global_probs, far_probs = split_keys(low_probs, sliding, global_kv, distant)
    grad_query = mixed_sum("wbhqk,wbkhd->wbqhd", near_split, sliding[..., :head_dim])
    grad_query = grad_query + mixed_sum(
        "wbhqk,wkhd->wbqhd", global_split, global_kv[..., :head_dim]
    )
    grad_query = (
        grad_query + mixed_sum("wbhqrk,wbhrkd->wbqhd", far_split, distant[..., :head_dim])
    ) * score_scale
    near_back = jnp.concatenate(
        [
            mixed_sum("wbhqk,wbqhd->wbkhd", near_split, queries) * score_scale,
            mixed_sum("wbhqk,wbqhd->wbkhd", near_probs, grad_attended),
        ],
        axis=4,
    )
    global_back = jnp.concatenate(
        [
            mixed_sum("wbhqk,wbqhd->wkhd", global_split, queries) * score_scale,
            mixed_sum("wbhqk,wbqhd->wkhd", global_probs, grad_attended),
        ],
        axis=3,
    )
    far_back = jnp.concatenate(
        [
            mixed_sum("wbhqrk,wbqhd->wbhrkd", far_split, queries) * score_scale,
            mixed_sum("wbhqrk,wbqhd->wbhrkd", far_probs, grad_attended),
        ],
        axis=5,
    )
    full_grad_probs = mixed_sum("wqhd,wkhd->whqk", rows_grad, value_part)
    partial_dot = jnp.sum(full_probs * full_grad_probs, axis=3, keepdims=True)
    row_dot = lax.psum(partial_dot, SEQ)
    full_grad_scores = (full_probs * (full_grad_probs - row_dot)).astype(jnp.bfloat16)
    query_part = mixed_sum("whqk,wkhd->wqhd", full_grad_scores, key_part) * score_scale
    full_key_grad = mixed_sum("whqk,wqhd->wkhd", full_grad_scores, global_queries) * score_scale
    full_value_grad = mixed_sum("whqk,wqhd->wkhd", full_probs.astype(jnp.bfloat16), rows_grad)
    grad_paired, query_total = return_blocks(
        near_back, global_back, far_back, query_part, sender, picker, owned_hot
    )
    grad_query = grad_query + exact_two(
        "wgb,wgqhd->wbqhd", owned_hot, query_total.reshape(windows, -1, BLOCK, head_count, head_dim)
    )
    grad_paired = grad_paired + jnp.concatenate([full_key_grad, full_value_grad], axis=3)
    return (grad_query, grad_paired)


def layer_backward(stored, grad_output, weights, tables):
    row_weights, down_weights, vector_weights = weights
    sender, picker, owned_hot, key_mask, full_mask = tables
    (
        hidden,
        normed,
        queries,
        sliding,
        global_kv,
        distant,
        probabilities,
        mixed_low,
        middle,
        normed_two,
        up_value,
        active,
        key_part,
        value_part,
        global_queries,
        full_probs,
    ) = stored
    model_width = row_weights.shape[0]
    windows, tokens, _ = hidden.shape
    blocks_dev = tokens // BLOCK
    head_dim = model_width // HEADS
    (
        gain_one,
        shift_one,
        bias_query,
        bias_value,
        bias_out,
        gain_two,
        shift_two,
        bias_down,
        bias_up,
    ) = split_vectors(vector_weights, model_width)
    grad_ffn = grad_output.astype(jnp.bfloat16)
    grad_bias_down = jnp.sum(grad_ffn.astype(jnp.float32), axis=(0, 1))
    grad_down = mixed_sum("wtf,wtd->fd", active, grad_ffn)
    grad_active = mixed_sum("wtd,fd->wtf", grad_ffn, down_weights)
    gelu_pull = jax.vjp(partial(jax.nn.gelu, approximate=False), up_value)[1]
    grad_up = gelu_pull(grad_active)[0].astype(jnp.bfloat16)
    grad_bias_up = jnp.sum(grad_up.astype(jnp.float32), axis=(0, 1))
    grad_in = mixed_sum("wtd,wtf->df", normed_two, grad_up)
    grad_normed_two = mixed_sum("wtf,df->wtd", grad_up, row_weights[:, 4 * model_width :])
    norm_pull_two = jax.vjp(norm_rows, middle, gain_two, shift_two)[1]
    grad_middle_norm, grad_gain_two, grad_shift_two = norm_pull_two(grad_normed_two)
    grad_middle = grad_output + grad_middle_norm
    grad_branch = grad_middle.astype(jnp.bfloat16)
    grad_bias_out = jnp.sum(grad_branch.astype(jnp.float32), axis=(0, 1))
    grad_out_weight = mixed_sum("wtd,wte->de", mixed_low, grad_branch)
    grad_attended = mixed_sum(
        "wte,de->wtd", grad_branch, row_weights[:, 3 * model_width : 4 * model_width]
    ).astype(jnp.bfloat16)
    grad_attended = grad_attended.reshape(windows, blocks_dev, BLOCK, HEADS, head_dim)
    grad_query, grad_paired = attention_back(
        grad_attended,
        queries,
        sliding,
        global_kv,
        distant,
        probabilities,
        key_part,
        value_part,
        global_queries,
        full_probs,
        sender,
        picker,
        owned_hot,
    )
    grad_projected = jnp.concatenate(
        [
            grad_query.reshape(windows, tokens, model_width),
            grad_paired[..., :head_dim].reshape(windows, tokens, model_width),
            grad_paired[..., head_dim:].reshape(windows, tokens, model_width),
        ],
        axis=2,
    ).astype(jnp.bfloat16)
    summed = jnp.sum(grad_projected.astype(jnp.float32), axis=(0, 1))
    grad_bias_query = summed[:model_width]
    grad_bias_value = summed[2 * model_width :]
    grad_projection = mixed_sum("wtd,wte->de", normed, grad_projected)
    grad_normed = mixed_sum("wte,de->wtd", grad_projected, row_weights[:, : 3 * model_width])
    norm_pull_one = jax.vjp(norm_rows, hidden, gain_one, shift_one)[1]
    grad_hidden_norm, grad_gain_one, grad_shift_one = norm_pull_one(grad_normed)
    grad_hidden = grad_middle + grad_hidden_norm
    grad_rows = jnp.concatenate([grad_projection, grad_out_weight, grad_in], axis=1)
    grad_vectors = jnp.concatenate(
        [
            grad_gain_one,
            grad_shift_one,
            grad_bias_query,
            grad_bias_value,
            grad_bias_out,
            grad_gain_two,
            grad_shift_two,
            grad_bias_down,
            grad_bias_up,
        ]
    )
    return (grad_hidden, (grad_rows, grad_down, grad_vectors))


def adam_update(master, first_old, second_old, gradient, step_rate, decay_rate):
    first_new = 0.5 * first_old + 0.5 * gradient
    second_new = 0.5 * second_old + 0.5 * gradient * gradient
    first_hat = first_new / (1.0 - 0.5**STEP)
    second_hat = second_new / (1.0 - 0.5**STEP)
    master_new = master - step_rate * (
        first_hat / (jnp.sqrt(second_hat) + 1e-08) + decay_rate * master
    )
    return (master_new, first_new, second_new)


def general_shards(
    block_input,
    cotangent,
    random_ids,
    segment_ids,
    global_ids,
    w_rows,
    w_rows_first,
    w_rows_second,
    w_down,
    w_down_first,
    w_down_second,
    vectors,
    vectors_first,
    vectors_second,
):
    section_index = lax.axis_index(SECTION)
    seq_place = lax.axis_index(SEQ)
    groups = lax.axis_size(SEQ)
    row_weights, down_weights, vector_low = (
        lax.all_gather(w_rows[0].astype(jnp.bfloat16), (DP, SEQ), axis=1, tiled=True),
        lax.all_gather(w_down[0].astype(jnp.bfloat16), (DP, SEQ), axis=0, tiled=True),
        lax.all_gather(vectors[0].astype(jnp.bfloat16), (DP, SEQ), axis=0, tiled=True),
    )
    weights = (row_weights, down_weights, vector_low.astype(jnp.float32))
    micro_count, windows, tokens, model_width = block_input.shape
    received = jnp.zeros((windows, tokens, model_width), jnp.bfloat16)
    results = jnp.zeros(block_input.shape, jnp.float32)
    full_totals = (
        jnp.zeros(row_weights.shape, jnp.float32),
        jnp.zeros(down_weights.shape, jnp.float32),
        jnp.zeros(vector_low.shape, jnp.float32),
    )

    def tick(tick_index, carry):
        received, results, full_totals = carry
        forward_mb = jnp.clip(tick_index - section_index, 0, micro_count - 1)
        behind_raw = tick_index - 2 + section_index
        behind = jnp.clip(behind_raw, 0, micro_count - 1)
        live_mask = ((behind_raw >= 0) & (behind_raw < micro_count)).astype(jnp.float32)
        tables_forward = route_tables(
            lax.dynamic_index_in_dim(random_ids, forward_mb, 0, keepdims=False),
            lax.dynamic_index_in_dim(segment_ids, forward_mb, 0, keepdims=False),
            lax.dynamic_index_in_dim(global_ids, forward_mb, 0, keepdims=False),
            seq_place,
            groups,
        )
        tables_behind = route_tables(
            lax.dynamic_index_in_dim(random_ids, behind, 0, keepdims=False),
            lax.dynamic_index_in_dim(segment_ids, behind, 0, keepdims=False),
            lax.dynamic_index_in_dim(global_ids, behind, 0, keepdims=False),
            seq_place,
            groups,
        )
        incoming_values = received.astype(jnp.float32)
        first_input = lax.dynamic_index_in_dim(block_input, forward_mb, 0, keepdims=False).astype(
            jnp.float32
        )
        forward_input = jnp.where(section_index == 0, first_input, incoming_values)
        forward_output = layer_forward(forward_input, weights, tables_forward)[0]
        back_source = lax.dynamic_index_in_dim(block_input, behind, 0, keepdims=False).astype(
            jnp.float32
        )
        back_input = jnp.where(section_index == 0, back_source, incoming_values)
        given_grad = lax.dynamic_index_in_dim(cotangent, behind, 0, keepdims=False).astype(
            jnp.float32
        )
        back_grad = jnp.where(section_index == 0, incoming_values, given_grad) * live_mask
        stored = layer_forward(back_input, weights, tables_behind)[1]
        grad_input, gradients = layer_backward(stored, back_grad, weights, tables_behind)
        outgoing = jnp.where(section_index == 0, forward_output, grad_input).astype(jnp.bfloat16)
        finished = jnp.where(section_index == 0, grad_input, forward_output)
        updated = lax.dynamic_update_index_in_dim(results, finished, behind, 0)
        results = jnp.where(live_mask > 0, updated, results)
        full_totals = tuple(
            (total_part + grad_part for total_part, grad_part in zip(full_totals, gradients))
        )
        return (partner(outgoing, SECTION, 0), results, full_totals)

    received, results, full_totals = lax.fori_loop(
        0, micro_count + 2, tick, (received, results, full_totals)
    )
    shard_totals = (
        lax.psum_scatter(full_totals[0], (DP, SEQ), scatter_dimension=1, tiled=True),
        lax.psum_scatter(full_totals[1], (DP, SEQ), scatter_dimension=0, tiled=True),
        lax.psum_scatter(full_totals[2], (DP, SEQ), scatter_dimension=0, tiled=True),
    )
    new_rows, new_rows_first, new_rows_second = adam_update(
        w_rows[0], w_rows_first[0], w_rows_second[0], shard_totals[0], rate_matrix, decay_matrix
    )
    new_down, new_down_first, new_down_second = adam_update(
        w_down[0], w_down_first[0], w_down_second[0], shard_totals[1], rate_matrix, decay_matrix
    )
    new_vectors, new_vectors_first, new_vectors_second = adam_update(
        vectors[0], vectors_first[0], vectors_second[0], shard_totals[2], rate_vector, 0.0
    )
    return (
        results[None],
        new_rows[None],
        new_rows_first[None],
        new_rows_second[None],
        new_down[None],
        new_down_first[None],
        new_down_second[None],
        new_vectors[None],
        new_vectors_first[None],
        new_vectors_second[None],
    )


LOW = jnp.bfloat16
LOG_HIGH = [float(np.log(c).astype(ml_dtypes.bfloat16)) for c in (1.0, 2.0, 3.0)]
LOG_LOW = [float(np.log(c)) - high for c, high in zip((1.0, 2.0, 3.0), LOG_HIGH)]
CHUNK = 256
VMEM_BYTES = 48 * 1024 * 1024


def dot_rows(left, right):
    return lax.dot_general(left, right, (((1,), (1,)), ((), ())), preferred_element_type=jnp.float32)


def dot_plain(left, right):
    return lax.dot_general(left, right, (((1,), (0,)), ((), ())), preferred_element_type=jnp.float32)


def dot_tokens(left, right):
    return lax.dot_general(left, right, (((0,), (0,)), ((), ())), preferred_element_type=jnp.float32)


def key_features(random_rows, segments, global_rows):
    blocks, head_count, _ = random_rows.shape
    index = jnp.arange(blocks)
    near = (jnp.abs(index[:, None] - index[None, :]) <= 1).astype(jnp.int32)
    named = jnp.sum((global_rows[:, None] == index[None, :]).astype(jnp.int32), axis=0)
    far = jnp.sum((random_rows[..., None] == index).astype(jnp.int32), axis=2)
    count = near[:, None, :] + named[None, None, :] + far
    count = jnp.where(named[:, None, None] > 0, 1, count)
    high = jnp.where(count == 0, masked, 0.0)
    low = jnp.zeros_like(high)
    for times in (2, 3):
        high = jnp.where(count == times, LOG_HIGH[times - 1], high)
        low = jnp.where(count == times, LOG_LOW[times - 1], low)
    width = -(-(2 * blocks + 6) // 128) * 128
    tokens = segments.shape[0]
    segment_hot = (segments[:, None] == jnp.arange(3)).astype(jnp.float32)
    table = jnp.concatenate([high, low], axis=2).transpose(1, 0, 2)
    spread = jnp.broadcast_to(
        table[:, :, None, :], (head_count, blocks, BLOCK, 2 * blocks)
    ).reshape(head_count, tokens, 2 * blocks)
    query_side = jnp.concatenate(
        [
            spread,
            jnp.broadcast_to(segment_hot, (head_count, tokens, 3)),
            jnp.zeros((head_count, tokens, width - 2 * blocks - 3), jnp.float32),
        ],
        axis=2,
    ).astype(LOW)
    block_hot = (jnp.arange(tokens)[:, None] // BLOCK == index).astype(jnp.float32)
    key_side = jnp.concatenate(
        [
            block_hot,
            block_hot,
            masked * (1.0 - segment_hot),
            jnp.ones((tokens, 3), jnp.float32),
            jnp.zeros((tokens, width - 2 * blocks - 6), jnp.float32),
        ],
        axis=1,
    ).astype(LOW)
    return query_side, key_side


def attend_kernel(q_ref, k_ref, v_ref, qa_ref, ka_ref, out_ref, lse_ref):
    tokens, pair = q_ref.shape
    left = lax.broadcasted_iota(jnp.int32, (CHUNK, pair), 1) < pair // 2
    keys = jnp.concatenate([k_ref[...], ka_ref[...]], axis=1)
    values = v_ref[...]

    def step(index, carry):
        rows = pl.ds(pl.multiple_of(index * CHUNK, CHUNK), CHUNK)
        queries = q_ref[rows, :] * 0.125
        outs, tops = [], []
        for head in range(2):
            mine = left if head == 0 else jnp.logical_not(left)
            side = jnp.where(mine, queries, jnp.zeros_like(queries))
            scores = dot_rows(jnp.concatenate([side, qa_ref[head, rows, :]], axis=1), keys)
            top = jnp.max(scores, axis=1, keepdims=True)
            weight = jnp.exp(scores - top)
            total = jnp.sum(weight, axis=1, keepdims=True)
            outs.append(dot_plain(weight.astype(LOW), values) / total)
            tops.append(top + jnp.log(total))
        out_ref[rows, :] = jnp.where(left, outs[0], outs[1]).astype(LOW)
        lse_ref[rows, :] = jnp.where(left, tops[0], tops[1])
        return carry

    lax.fori_loop(0, tokens // CHUNK, step, 0)


def attend(projected, query_side, key_side, width):
    tokens = projected.shape[0]
    pairs = width // 128
    features = key_side.shape[1]
    return pl.pallas_call(
        attend_kernel,
        grid=(pairs,),
        in_specs=[
            pl.BlockSpec((tokens, 128), lambda p: (0, p)),
            pl.BlockSpec((tokens, 128), lambda p: (0, pairs + p)),
            pl.BlockSpec((tokens, 128), lambda p: (0, 2 * pairs + p)),
            pl.BlockSpec((2, tokens, features), lambda p: (p, 0, 0)),
            pl.BlockSpec((tokens, features), lambda p: (0, 0)),
        ],
        out_specs=[
            pl.BlockSpec((tokens, 128), lambda p: (0, p)),
            pl.BlockSpec((tokens, 128), lambda p: (0, p)),
        ],
        out_shape=[
            jax.ShapeDtypeStruct((tokens, width), LOW),
            jax.ShapeDtypeStruct((tokens, width), jnp.float32),
        ],
        compiler_params=pltpu.CompilerParams(vmem_limit_bytes=VMEM_BYTES),
        cost_estimate=pl.CostEstimate(
            flops=16 * pairs * tokens * tokens * 128,
            bytes_accessed=tokens * width * 16,
            transcendentals=2 * pairs * tokens * tokens,
        ),
    )(projected, projected, projected, query_side, key_side)


def three_terms(values):
    high = values.astype(LOW).astype(jnp.float32)
    rest = values - high
    middle = rest.astype(LOW).astype(jnp.float32)
    return high, middle, rest - middle


def attend_back_kernel(
    q_ref, k_ref, v_ref, do_ref, o_ref, lse_ref, qa_ref, ka_ref, grad_ref, dk_acc, dv_acc
):
    tokens, pair = q_ref.shape
    features = ka_ref.shape[1]
    pairs = pl.num_programs(0)
    place = pl.program_id(0)
    blocks = tokens // BLOCK
    first = 2 * blocks + 3
    left = lax.broadcasted_iota(jnp.int32, (CHUNK, pair), 1) < pair // 2
    lane = lax.broadcasted_iota(jnp.int32, (CHUNK, features), 1)
    lane_pair = lax.broadcasted_iota(jnp.int32, (CHUNK, pair), 1)
    keys = jnp.concatenate([k_ref[...], ka_ref[...]], axis=1)
    turned = jnp.transpose(k_ref[...].astype(jnp.float32)).astype(LOW)
    ones = (lax.broadcasted_iota(jnp.int32, (tokens, pair), 1) < 3).astype(jnp.float32).astype(LOW)
    values = jnp.concatenate([v_ref[...], ones], axis=1)
    dk_acc[...] = jnp.zeros_like(dk_acc)
    dv_acc[...] = jnp.zeros_like(dv_acc)
    column = pl.multiple_of(place * 128, 128)

    def step(index, carry):
        rows = pl.ds(pl.multiple_of(index * CHUNK, CHUNK), CHUNK)
        queries = q_ref[rows, :] * 0.125
        grads = do_ref[rows, :]
        product = grads.astype(jnp.float32) * o_ref[rows, :].astype(jnp.float32)
        parts = []
        for head in range(2):
            mine = left if head == 0 else jnp.logical_not(left)
            level = lse_ref[rows, head * 64 : head * 64 + 1]
            inner = jnp.sum(jnp.where(mine, product, 0.0), axis=1, keepdims=True)
            side = qa_ref[head, rows, :].astype(jnp.float32)
            for spot, term in enumerate(three_terms(level)):
                side = jnp.where(lane == first + spot, -term, side)
            query_side = jnp.where(mine, queries, jnp.zeros_like(queries))
            grad_side = jnp.where(mine, grads, jnp.zeros_like(grads))
            tail = jnp.zeros((CHUNK, pair), jnp.float32)
            for spot, term in enumerate(three_terms(inner)):
                tail = jnp.where(lane_pair == spot, -term, tail)
            probs = jnp.exp(
                dot_rows(keys, jnp.concatenate([query_side, side.astype(LOW)], axis=1))
            )
            change = dot_rows(values, jnp.concatenate([grad_side, tail.astype(LOW)], axis=1))
            grad_scores = (probs * change).astype(LOW)
            dv_acc[...] += dot_plain(probs.astype(LOW), grad_side)
            dk_acc[...] += dot_plain(grad_scores, query_side)
            parts.append(dot_plain(turned, grad_scores))
        half = pair // 2
        joined = jnp.concatenate([parts[0][:half], parts[1][half:]], axis=0)
        grad_ref[rows, pl.ds(column, 128)] = (jnp.transpose(joined) * 0.125).astype(LOW)
        return carry

    lax.fori_loop(0, tokens // CHUNK, step, 0)
    key_column = pl.multiple_of((pairs + place) * 128, 128)
    value_column = pl.multiple_of((2 * pairs + place) * 128, 128)
    grad_ref[:, pl.ds(key_column, 128)] = dk_acc[...].astype(LOW)
    grad_ref[:, pl.ds(value_column, 128)] = dv_acc[...].astype(LOW)


def attend_back(projected, grad_attended, attended, levels, query_side, key_side):
    tokens, width = attended.shape
    pairs = width // 128
    features = key_side.shape[1]
    return pl.pallas_call(
        attend_back_kernel,
        grid=(pairs,),
        in_specs=[
            pl.BlockSpec((tokens, 128), lambda p: (0, p)),
            pl.BlockSpec((tokens, 128), lambda p: (0, pairs + p)),
            pl.BlockSpec((tokens, 128), lambda p: (0, 2 * pairs + p)),
            pl.BlockSpec((tokens, 128), lambda p: (0, p)),
            pl.BlockSpec((tokens, 128), lambda p: (0, p)),
            pl.BlockSpec((tokens, 128), lambda p: (0, p)),
            pl.BlockSpec((2, tokens, features), lambda p: (p, 0, 0)),
            pl.BlockSpec((tokens, features), lambda p: (0, 0)),
        ],
        out_specs=pl.BlockSpec((tokens, 3 * width), lambda p: (0, 0)),
        out_shape=jax.ShapeDtypeStruct((tokens, 3 * width), LOW),
        scratch_shapes=[
            pltpu.VMEM((tokens, 128), jnp.float32),
            pltpu.VMEM((tokens, 128), jnp.float32),
        ],
        compiler_params=pltpu.CompilerParams(vmem_limit_bytes=VMEM_BYTES),
        cost_estimate=pl.CostEstimate(
            flops=40 * pairs * tokens * tokens * 128,
            bytes_accessed=tokens * width * 24,
            transcendentals=2 * pairs * tokens * tokens,
        ),
    )(projected, projected, projected, grad_attended, attended, levels, query_side, key_side)


def swap(value):
    return lax.ppermute(value, SECTION, [(0, 1), (1, 0)])


def normalized(values_in):
    row_mean = jnp.mean(values_in, axis=-1, keepdims=True)
    centred = values_in - row_mean
    spread = jnp.mean(centred * centred, axis=-1, keepdims=True)
    scale = lax.rsqrt(spread + epsilon)
    return centred * scale, scale


def norm_back(values_in, incoming, gain_vec):
    unit, scale = normalized(values_in)
    grad_gain = jnp.sum(incoming * unit, axis=0)
    grad_shift = jnp.sum(incoming, axis=0)
    p = incoming * gain_vec
    mean_p = jnp.mean(p, axis=-1, keepdims=True)
    mean_pn = jnp.mean(p * unit, axis=-1, keepdims=True)
    return scale * (p - mean_p - unit * mean_pn), grad_gain, grad_shift


class Shares:
    def __init__(self, width, columns, depth, vector_len):
        self.width = width
        self.columns = columns
        self.depth = depth
        self.vector_len = vector_len
        self.half = columns // 2
        self.per = width // columns
        self.groups = columns // depth

    def unpack(self, gathered, core):
        half, per, width = self.half, self.per, self.width
        if len(gathered) == 3:
            rows = gathered[0].reshape(-1, half, width)
            gathered = (
                rows[: 3 * per],
                rows[3 * per : 4 * per],
                rows[4 * per :],
                gathered[1],
                gathered[2],
            )
        proj, out, up, down, vec = gathered
        proj, up, down = [piece.reshape(-1, width) for piece in (proj, up, down)]
        out = (
            out.reshape(per, half, 2, per * half)
            .transpose(0, 2, 1, 3)
            .reshape(width, per * half)
        )
        vec = vec.reshape(-1, TAIL, width)[:, 0, : self.vector_len].reshape(-1)
        pieces = split_vectors(vec.astype(jnp.float32), width)
        bias_query, bias_value = self.vector_half(pieces[2], core), self.vector_half(pieces[3], core)
        bias_up = lax.dynamic_index_in_dim(
            pieces[8].reshape(-1, 2, self.depth // 2), core, 1, keepdims=False
        ).reshape(-1)
        return (
            (proj, out, up, down),
            (pieces[0], pieces[1], bias_query, bias_value, pieces[4], pieces[5], pieces[6])
            + (pieces[7], bias_up),
        )

    def vector_half(self, vec, core):
        return lax.dynamic_index_in_dim(
            vec.reshape(self.per, 2, self.half), core, 1, keepdims=False
        ).reshape(-1)

    def by_shard(self, grads, vector_grads, core):
        proj, out, up, down = grads
        half, per, width = self.half, self.per, self.width
        out = (
            out.reshape(per, 2, half, per * half).transpose(0, 2, 1, 3).reshape(per, half, width)
        )
        hot = (jnp.arange(2) == core).astype(jnp.float32)
        spread = list(vector_grads)
        for index in (2, 3):
            spread[index] = (
                spread[index].reshape(per, 1, half) * hot[None, :, None]
            ).reshape(-1)
        spread[8] = (spread[8].reshape(-1, 1, self.depth // 2) * hot[None, :, None]).reshape(-1)
        for index in (0, 1, 4, 5, 6, 7):
            spread[index] = spread[index] * hot[0]
        vec = jnp.concatenate(spread).reshape(-1, 1, self.vector_len)
        vec = jnp.pad(vec, ((0, 0), (0, TAIL - 1), (0, width - self.vector_len))).astype(LOW)
        return (
            proj.reshape(-1, half, width),
            out,
            up.reshape(2, 4, half, width),
            down.reshape(2, 2, 4, self.depth // 2, width),
            vec.reshape(2, 2, 4, TAIL, width),
        )


MESH = pl.DeviceIdType.MESH
PIECE = 48
TAIL = 16


def prepare_kernel(shares, rows_ref, down_ref, vector_ref, rows_out, down_out, vector_out):
    core = lax.axis_index(SECTION)
    offset = lax.axis_index((DP, SEQ)) * shares.columns
    half, per, width, depth = shares.half, shares.per, shares.width, shares.depth // 2
    is_inner = (offset >= 3 * width) & (offset < 4 * width)
    is_hidden = offset >= 4 * width

    @pl.when(is_inner)
    def _():
        for which in range(2):
            side = core if which == 0 else 1 - core
            held = [rows_ref[pl.ds((2 * j + side) * half, half), :] for j in range(per)]
            turned = jnp.transpose(jnp.concatenate(held, axis=0))
            rows_out[which] = jnp.concatenate([turned[:half], turned[half:]], axis=1).astype(LOW)

    @pl.when(jnp.logical_not(is_inner))
    def _():
        turned = jnp.transpose(rows_ref[...]).astype(LOW)
        plain = [turned[:half], turned[half:]]
        hidden = [
            jnp.concatenate(
                [turned[(2 * j + side) * depth :][:depth] for j in range(shares.groups)], axis=0
            )
            for side in range(2)
        ]
        halves = [jnp.where(is_hidden, b, a) for a, b in zip(plain, hidden)]
        rows_out[0] = jnp.where(core == 0, halves[0], halves[1])
        rows_out[1] = jnp.where(core == 0, halves[1], halves[0])

    down = down_ref[...].astype(LOW)
    down_out[0] = jnp.where(core == 0, down[:depth], down[depth:])
    down_out[1] = jnp.where(core == 0, down[depth:], down[:depth])
    vector_out[...] = jnp.zeros_like(vector_out)
    vector_out[0:1, : shares.vector_len] = vector_ref[...].astype(LOW)


def prepare(shares, rows, down, vector):
    return pl.pallas_call(
        partial(prepare_kernel, shares),
        out_shape=[
            jax.ShapeDtypeStruct((2, shares.half, shares.width), LOW),
            jax.ShapeDtypeStruct((2, shares.depth // 2, shares.width), LOW),
            jax.ShapeDtypeStruct((TAIL, shares.width), LOW),
        ],
        compiler_params=pltpu.CompilerParams(vmem_limit_bytes=VMEM_BYTES),
    )(rows, down, vector)


class Place:
    def __init__(self):
        self.core = lax.axis_index(SECTION)
        self.dp = lax.axis_index(DP)
        self.z = lax.axis_index(SEQ)
        self.y, self.x = self.dp // 2, self.dp % 2
        self.high, self.low = self.z // 2, self.z % 2
        self.inner = self.high + self.low == 1
        self.outer = self.high + self.low != 1
        self.partner = {SECTION: 1 - self.core}
        self.along_x = {DP: 2 * self.y + 1 - self.x}
        self.along_y = {DP: 2 * (1 - self.y) + self.x}
        self.across = {SEQ: 3 - self.z}
        self.beside = {SEQ: 2 * self.high + 1 - self.low}
        self.others = [{SEQ: (self.z + by) % 4} for by in (1, 2, 3)]
        self.own = pl.ds(self.z, 1)
        self.next = pl.ds(2 * self.high + 1 - self.low, 1)
        self.near = pl.ds(2 * self.high, 2)
        self.far = pl.ds(2 * (1 - self.high), 2)

    def greet(self):
        barrier = pltpu.get_barrier_semaphore()
        everyone = [self.partner, self.along_x, self.along_y] + self.others
        for device in everyone:
            pl.semaphore_signal(barrier, inc=1, device_id=device, device_id_type=MESH)
        pl.semaphore_wait(barrier, len(everyone))


def remote(src, dst, sems, spots, device):
    return pltpu.make_async_remote_copy(
        src_ref=src,
        dst_ref=dst,
        send_sem=sems[0].at[spots[0]],
        recv_sem=sems[1].at[spots[1]],
        device_id=device,
        device_id_type=MESH,
    )


def chunk_pairs(shares):
    pairs = []
    for array, length in ((0, shares.half), (1, shares.depth // 2)):
        for start in range(0, length, 2 * PIECE):
            pairs.append([(array, start, PIECE, 0), (array, start + PIECE, PIECE, 1)])
    pairs[0].append((2, 0, TAIL, 0))
    return pairs


def quad_pairs(shares):
    length = (shares.half + shares.depth // 2) // 2
    pairs = [
        [(0, start, PIECE, None), (1, start, PIECE, None)] for start in range(0, length, PIECE)
    ]
    pairs[0].append((2, 0, TAIL, 0))
    return pairs


def gather_kernel(shares, *refs):
    (rows_in, down_in, vector_in, x_in, cot_in), refs = refs[:5], refs[5:]
    outs, refs = [refs[0:3], refs[3:6]], refs[6:]
    (x_out, cot_out), refs = refs[:2], refs[2:]
    local, swap_send, swap_recv, z_send, z_recv, send, recv = refs
    here = Place()
    core, y, x, z = here.core, here.y, here.x, here.z
    half = x_in.shape[2] // 2
    rows_half, down_half = shares.half // 2, shares.depth // 4
    here.greet()

    def slices(source, target, base):
        mine = pl.ds(pl.multiple_of(core * half, half), half)
        sems = (z_send, z_recv)
        own = pltpu.make_async_copy(
            source.at[z, 0, mine], target.at[z, core], local.at[8 + base // 4]
        )
        sends, arrivals = [], []
        for by in (1, 2, 3):
            spots = (base + by - 1, base + by - 1)
            device = here.others[by - 1]
            sends.append(
                remote(source.at[(z + by) % 4, 0, mine], target.at[z, core], sems, spots, device)
            )
            arrivals.append(
                remote(
                    source.at[z, 0, mine], target.at[(z + 4 - by) % 4, core], sems, spots, device
                )
            )
        spots = (base + 3, base + 3)
        forward = remote(target.at[:, core], target.at[:, core], sems, spots, here.partner)
        arrived = remote(target.at[:, 1 - core], target.at[:, 1 - core], sems, spots, here.partner)
        return own, sends, arrivals, forward, arrived

    x_moves = slices(x_in, x_out, 0)
    cot_moves = slices(cot_in, cot_out, 4)

    def open_slices(moves):
        moves[0].start()
        for copy in moves[1]:
            copy.start()

    def pass_slices(moves):
        moves[0].wait()
        for copy in moves[2]:
            copy.wait_recv()
        moves[3].start()

    def close_slices(moves):
        for copy in moves[1]:
            copy.wait_send()
        moves[3].wait_send()
        moves[4].wait_recv()

    def first_moves(layer, which):
        down = down_in.at[which]
        rows = rows_in.at[which]
        if layer == 0:
            return [
                (0, rows, outs[0][0].at[y, x, z]),
                (1, down, outs[0][1].at[y, x, z]),
                (2, vector_in, outs[0][2].at[y, x, z]),
            ]
        moves = [(7, vector_in, outs[1][2].at[y, x, z])]
        for part in range(2):
            target = outs[1][part]
            moves.append(
                (
                    3 + 2 * part,
                    rows.at[pl.ds(part * rows_half, rows_half)],
                    target.at[z, pl.ds(0, rows_half)],
                )
            )
            moves.append(
                (
                    4 + 2 * part,
                    down.at[pl.ds(part * down_half, down_half)],
                    target.at[z, pl.ds(rows_half, down_half)],
                )
            )
        return moves

    swaps = (swap_send, swap_recv)
    for layer in range(2):

        @pl.when(core == layer)
        def _():
            across = [
                remote(src, dst, swaps, (spot, spot), here.partner)
                for spot, src, dst in first_moves(layer, 1)
            ]
            own = [
                pltpu.make_async_copy(src, dst, local.at[spot])
                for spot, src, dst in first_moves(layer, 0)
            ]
            for copy in across + own:
                copy.start()
            for copy in own:
                copy.wait()
            for copy in across:
                copy.wait_send()
            for spot, src, dst in first_moves(1 - layer, 0):
                remote(src, dst, swaps, (spot, spot), here.partner).wait_recv()

    numbers, pairs = {}, []
    for layer in range(2):
        for pair in chunk_pairs(shares) if layer == 0 else quad_pairs(shares):
            entry = []
            for array, start, length, order in pair:
                ref = outs[layer][array]
                rows = pl.ds(start, length)
                flat = order is None
                number = len(numbers)
                sems = (send, recv)

                def part(which):
                    return ref.at[which, rows] if flat else ref.at[y, x, which, rows]

                def copy(piece, spots, device):
                    return remote(piece, piece, sems, ((number, spots[0]), (number, spots[1])), device)

                steps = {
                    "z": copy(part(here.own), (0, 0), here.beside),
                    "across": copy(part(here.near), (1, 1), here.across),
                    "on": copy(part(here.far), (4, 1), here.beside),
                }
                arrive = [
                    copy(part(here.next), (0, 0), here.beside),
                    copy(part(here.far), (1, 1), here.across),
                ]
                if order == 0:
                    steps["one"] = copy(ref.at[y, x, :, rows], (2, 2), here.along_y)
                    steps["two"] = copy(ref.at[:, x, :, rows], (3, 3), here.along_x)
                    arrive.append(copy(ref.at[1 - y, x, :, rows], (2, 2), here.along_y))
                    arrive.append(copy(ref.at[:, 1 - x, :, rows], (3, 3), here.along_x))
                elif order == 1:
                    steps["one"] = copy(ref.at[y, x, :, rows], (2, 2), here.along_x)
                    steps["two"] = copy(ref.at[y, :, :, rows], (3, 3), here.along_y)
                    arrive.append(copy(ref.at[y, 1 - x, :, rows], (2, 2), here.along_x))
                    arrive.append(copy(ref.at[1 - y, :, :, rows], (3, 3), here.along_y))
                numbers[number] = (steps, arrive)
                entry.append(number)
            pairs.append(entry)

    def issue(name, entry):
        after = {"z": None, "across": 0, "on": 1, "one": 1, "two": 2}[name]

        def start():
            for number in entry:
                steps, arrive = numbers[number]
                if name in steps:
                    if after is not None and not (name == "one"):
                        arrive[after].wait_recv()
                    steps[name].start()

        if name in ("across", "on"):
            pl.when(here.inner)(start)
        else:
            start()

    def arrived(entry, index, where):
        def wait():
            for number in entry:
                numbers[number][1][index].wait_recv()

        pl.when(where)(wait)

    first, second = pairs[: len(chunk_pairs(shares))], pairs[len(chunk_pairs(shares)) :]
    for entry in first:
        issue("z", entry)
    for entry in first:
        issue("across", entry)
        arrived(entry, 0, here.outer)
    for entry in second:
        issue("z", entry)
    open_slices(x_moves)
    for entry in first:
        issue("on", entry)
    for entry in first:
        arrived(entry, 1, here.outer)
        issue("one", entry)
    for entry in second:
        issue("across", entry)
        arrived(entry, 0, here.outer)
    for index in range(max(len(first), len(second))):
        if index < len(first):
            issue("two", first[index])
        if index < len(second):
            issue("on", second[index])
    pass_slices(x_moves)
    open_slices(cot_moves)
    for entry in second:
        arrived(entry, 1, here.outer)
        for number in entry:
            steps, arrive = numbers[number]
            if "one" in steps:
                steps["one"].start()
                arrive[2].wait_recv()
                steps["two"].start()
    pass_slices(cot_moves)
    for steps, arrive in numbers.values():
        if len(arrive) == 4:
            arrive[3].wait_recv()
        for name in steps:
            if name not in ("across", "on"):
                steps[name].wait_send()

    @pl.when(here.inner)
    def _():
        for steps, _ in numbers.values():
            steps["across"].wait_send()
            steps["on"].wait_send()

    close_slices(x_moves)
    close_slices(cot_moves)


def gather(shares, prepared, block_input, cotangent):
    micro, _, tokens, width = block_input.shape
    chunks = sum(len(pair) for pair in chunk_pairs(shares) + quad_pairs(shares))
    lengths = (shares.half, shares.depth // 2, TAIL)
    layer = [jax.ShapeDtypeStruct((2, 2, 4, rows, width), LOW) for rows in lengths]
    quad = jax.ShapeDtypeStruct((4, (lengths[0] + lengths[1]) // 2, width), LOW)
    window = jax.ShapeDtypeStruct((micro, 2, tokens // 2, width), LOW)
    anywhere = pl.BlockSpec(memory_space=pl.ANY)
    results = pl.pallas_call(
        partial(gather_kernel, shares),
        in_specs=[anywhere] * 5,
        out_specs=[anywhere] * 8,
        out_shape=layer + [quad, quad, layer[2]] + [window, window],
        scratch_shapes=[
            pltpu.SemaphoreType.DMA((10,)),
            pltpu.SemaphoreType.DMA((8,)),
            pltpu.SemaphoreType.DMA((8,)),
            pltpu.SemaphoreType.DMA((8,)),
            pltpu.SemaphoreType.DMA((8,)),
            pltpu.SemaphoreType.DMA((chunks, 5)),
            pltpu.SemaphoreType.DMA((chunks, 4)),
        ],
        compiler_params=pltpu.CompilerParams(collective_id=0, has_side_effects=True),
    )(*prepared, block_input, cotangent)
    return results[0:3], results[3:6], results[6], results[7]


def over(value, bit):
    return lax.ppermute(value, DP, [(i, i ^ bit) for i in range(4)])


def layout_moves(shares, y, x, pieces, arrays):
    proj, out, up, down = arrays
    rows_half, down_half = shares.half // 2, shares.depth // 4
    moves = []
    for part in range(2):
        rows = pl.ds(part * rows_half, rows_half)
        for index, (by_y, by_x) in enumerate(((0, 0), (1, 0), (0, 1), (1, 1))):
            piece = pieces[part][index]
            at_y, at_x = y ^ by_y, x ^ by_x
            top = pl.ds(0, rows_half)
            if at_y == 1:
                moves.append((piece.at[:, top], up.at[at_x, :, rows]))
            elif at_x == 0:
                moves.append((piece.at[:, top], proj.at[pl.ds(0, 4), rows]))
            else:
                moves.append((piece.at[pl.ds(0, 2), top], proj.at[pl.ds(4, 2), rows]))
                moves.append((piece.at[pl.ds(2, 2), top], out.at[:, rows]))
            moves.append(
                (
                    piece.at[:, pl.ds(rows_half, down_half)],
                    down.at[at_y, at_x, :, pl.ds(part * down_half, down_half)],
                )
            )
    return moves


def layout_kernel(shares, joins, *refs):
    dp = lax.axis_index(DP)
    if joins:
        pieces, arrays = [refs[0:4], refs[4:8]], refs[8:12]
    else:
        arrays, pieces = refs[0:4], [refs[4:8], refs[8:12]]
    for spot in range(4):

        @pl.when(dp == spot)
        def _():
            for piece, place in layout_moves(shares, spot // 2, spot % 2, pieces, arrays):
                src, dst = (piece, place) if joins else (place, piece)
                dst[...] = src[...]


def layout(shares, joins, *arrays):
    half, depth, width = shares.half, shares.depth // 2, shares.width
    if joins:
        shapes = [
            (6, half, width),
            (2, half, width),
            (2, 4, half, width),
            (2, 2, 4, depth, width),
        ]
    else:
        shapes = [(4, (half + depth) // 2, width)] * 8
    return pl.pallas_call(
        partial(layout_kernel, shares, joins),
        out_shape=[jax.ShapeDtypeStruct(shape, LOW) for shape in shapes],
        compiler_params=pltpu.CompilerParams(vmem_limit_bytes=VMEM_BYTES),
        cost_estimate=pl.CostEstimate(
            flops=0, bytes_accessed=64 * (half + depth) * width, transcendentals=0
        ),
    )(*arrays)


def tied(value, flying):
    return lax.optimization_barrier((value, flying))


def spread_quads(shares, quads):
    low, high = quads
    flying = (low, high, over(low, 2), over(high, 1))
    low, high, low_y, high_x = yield flying
    flying = (low_y, high_x, over(low, 1), over(high, 2))
    low_y, high_x, low_x, high_y = yield flying
    flying = (over(low_y, 1), over(high_x, 2))
    low_both, high_both = yield flying
    yield layout(shares, True, low, low_y, low_x, low_both, high, high_y, high_x, high_both)


def sum_quads(shares, arrays):
    pieces = layout(shares, False, *arrays)

    def total(*terms):
        return sum(term.astype(jnp.float32) for term in terms).astype(LOW)

    low, low_y, low_x, low_both = pieces[:4]
    high, high_y, high_x, high_both = pieces[4:]
    flying = (low_x, high_y, over(low_both, 1), over(high_both, 2))
    low_x, high_y, low_hop, high_hop = yield flying
    low_y, high_x = total(low_y, low_hop), total(high_x, high_hop)
    flying = (low_y, high_x, over(low_x, 1), over(high_y, 2))
    low_y, high_x, low_x, high_y = yield flying
    flying = (over(low_y, 2), over(high_x, 1))
    low_y, high_x = yield flying
    yield (total(low, low_x, low_y), total(high, high_x, high_y))


class Beside:
    def __init__(self, hops=None):
        self.hops = hops
        self.flying = None if hops is None else next(hops)

    def tie(self, value):
        if self.hops is None:
            return value
        value, arrived = tied(value, self.flying)
        self.flying = self.hops.send(arrived)
        return value


def scatter_kernel(shares, *refs):
    (proj, out, up, down, vec_zero, low, high, vec_one), refs = refs[:8], refs[8:]
    (dx_ref, final_ref, halves, slices), refs = refs[:4], refs[4:]
    work, refs = [refs[0:3], refs[3:6]], refs[6:]
    (got_one, got_two, got_far, got_across, got_near, total), refs = refs[:6], refs[6:]
    load, local, swap_send, swap_recv, z_send, z_recv, send, recv = refs
    here = Place()
    core, y, x, z = here.core, here.y, here.x, here.z
    rows_half, down_half = shares.half // 2, shares.depth // 4
    down_base = shares.half
    tail_base = shares.half + shares.depth // 2

    rows = work[0][0]
    moves = [
        [
            (proj.at[pl.ds(0, 4)], rows.at[0, 0]),
            (proj.at[pl.ds(4, 2)], rows.at[0, 1, pl.ds(0, 2)]),
            (out, rows.at[0, 1, pl.ds(2, 2)]),
            (up, rows.at[1]),
            (down, work[0][1]),
            (vec_zero, work[0][2]),
        ],
        [(low, work[1][0]), (high, work[1][1]), (vec_one, work[1][2])],
    ]
    loads = [
        [
            pltpu.make_async_copy(src, dst, load.at[layer, index])
            for index, (src, dst) in enumerate(moves[layer])
        ]
        for layer in range(2)
    ]
    for layer in (1, 0):
        for copy in loads[layer]:
            copy.start()
    here.greet()

    def place_of(layer, array, start):
        if array == 2:
            return tail_base
        if layer == 0:
            return (0, down_base)[array] + start
        if start < rows_half:
            return array * rows_half + start
        return down_base + array * down_half + start - rows_half

    pairs, chunks = [], []
    for layer in (1, 0):
        for index, pair in enumerate(quad_pairs(shares) if layer else chunk_pairs(shares)):
            entry = []
            for array, start, length, order in pair:
                entry.append((len(chunks), layer, array, start, length, order))
                chunks.append(entry[-1])
            pairs.append((index, entry))

    def pieces(chunk):
        number, layer, array, start, length, order = chunk
        ref = work[layer][array]
        rows = pl.ds(start, length)
        sems = (send, recv)
        keeps, slots, copies = [], [], []

        def part(which):
            return ref.at[which, rows] if order is None else ref.at[y, x, which, rows]

        def add(src, slot, device, keep):
            spots = (number, len(copies))
            copies.append(remote(src, slot, sems, (spots, spots), device))
            slots.append(slot)
            keeps.append(keep)

        room = pl.ds(0, length)
        if order == 0:
            add(ref.at[:, 1 - x, :, rows], got_one.at[number, :, :, room], here.along_x, ref.at[:, x, :, rows])
            add(ref.at[1 - y, x, :, rows], got_two.at[number, :, room], here.along_y, ref.at[y, x, :, rows])
        elif order == 1:
            add(ref.at[1 - y, :, :, rows], got_one.at[number, :, :, room], here.along_y, ref.at[y, :, :, rows])
            add(ref.at[y, 1 - x, :, rows], got_two.at[number, :, room], here.along_x, ref.at[y, x, :, rows])
        else:
            copies, slots, keeps = [None] * 2, [None] * 2, [None] * 2
        add(part(here.far), got_far.at[number, :, room], here.beside, part(here.far))
        add(part(here.far), got_across.at[number, :, room], here.across, part(here.near))
        add(part(here.next), got_near.at[number, :, room], here.beside, part(here.own))
        return copies, keeps, slots

    built = [pieces(chunk) for chunk in chunks]
    loaded = set()

    def land(number, phase):
        copies, keeps, slots = built[number]
        copies[phase].wait_recv()
        keep, slot = keeps[phase], slots[phase]
        keep[...] = keep[...] + slot[...]

    def run(chunk, phase):
        number, layer, array, start, length, order = chunk
        copies, keeps, slots = built[number]
        if (layer, array) not in loaded:
            loaded.add((layer, array))
            spots = ((0, 1, 2, 3), (4,), (5,))[array] if layer == 0 else (array,)
            for spot in spots:
                loads[layer][spot].wait()
        if phase < 2:
            if order is not None:
                if phase:
                    land(number, 0)
                copies[phase].start()
        elif phase == 2:
            if order is not None:
                land(number, 1)

            @pl.when(here.outer)
            def _():
                copies[2].start()
                copies[4].start()

        elif phase == 3:

            @pl.when(here.inner)
            def _():
                land(number, 2)
                copies[3].start()

        elif phase == 4:

            @pl.when(here.inner)
            def _():
                land(number, 3)
                copies[4].start()

        else:
            copies[4].wait_recv()
            spot = pl.ds(place_of(layer, array, start), length)
            total[layer, spot, :] = (keeps[4][...] + slots[4][...])[0]

    def step(entry, phase):
        for chunk in entry:
            run(chunk, phase)

    second = [entry for _, entry in pairs[: len(quad_pairs(shares))]]
    first = [entry for _, entry in pairs[len(quad_pairs(shares)) :]]
    tails = [chunk for entry in second for chunk in entry if chunk[5] is not None]
    second = [[chunk for chunk in entry if chunk[5] is None] for entry in second]
    first[0] = first[0] + tails
    for index in range(max(len(first), len(second))):
        if index < len(first):
            step(first[index], 0)
        if index < len(second):
            step(second[index], 2)
    for section, source in ((0, dx_ref), (1, final_ref)):

        @pl.when(core == section)
        def _():
            pltpu.make_async_copy(source.at[z], slices.at[z], local.at[0]).start()
            for by in (1, 2, 3):
                remote(
                    source.at[(z + by) % 4],
                    slices.at[z],
                    (z_send, z_recv),
                    (by - 1, by - 1),
                    here.others[by - 1],
                ).start()

    for entry in second:
        step(entry, 3)
    for index in range(max(len(first), len(second))):
        if index < len(first):
            step(first[index], 1)
        if index < len(second):
            step(second[index], 4)
    for entry in first:
        step(entry, 2)
    for entry in second:
        step(entry, 5)
    for phase in (3, 4, 5):
        for entry in first:
            step(entry, phase)

    for copies, _, _ in built:
        for index in (0, 1, 4):
            if copies[index] is not None:
                copies[index].wait_send()
    for section, index in ((here.outer, 2), (here.inner, 3)):

        @pl.when(section)
        def _():
            for copies, _, _ in built:
                copies[index].wait_send()

    swaps = (swap_send, swap_recv)
    across = remote(total.at[1 - core], halves.at[core], swaps, (0, 0), here.partner)
    across.start()
    own = pltpu.make_async_copy(total.at[core], halves.at[core], local.at[1])
    own.start()
    own.wait()
    across.wait_send()
    remote(total.at[1 - core], halves.at[1 - core], swaps, (0, 0), here.partner).wait_recv()
    pltpu.make_async_copy(dx_ref.at[z], slices.at[z], local.at[0]).wait()
    for by in (1, 2, 3):
        copy = remote(
            dx_ref.at[z],
            slices.at[(z + 4 - by) % 4],
            (z_send, z_recv),
            (by - 1, by - 1),
            here.others[by - 1],
        )
        copy.wait_send()
        copy.wait_recv()


def scatter(shares, arrays, vec_zero, quads, vec_one, grad, final):
    micro, tokens, width = grad.shape
    lengths = (shares.half, shares.depth // 2, TAIL)
    chunks = sum(len(pair) for pair in chunk_pairs(shares) + quad_pairs(shares))
    rows = sum(lengths)
    anywhere = pl.BlockSpec(memory_space=pl.ANY)
    work = [pltpu.VMEM((2, 2, 4, length, width), LOW) for length in lengths]
    quad = pltpu.VMEM((4, (lengths[0] + lengths[1]) // 2, width), LOW)
    return pl.pallas_call(
        partial(scatter_kernel, shares),
        in_specs=[anywhere] * 10,
        out_specs=[anywhere] * 2,
        out_shape=[
            jax.ShapeDtypeStruct((2, rows, width), LOW),
            jax.ShapeDtypeStruct((micro, tokens, width), LOW),
        ],
        scratch_shapes=work
        + [quad, quad, work[2]]
        + [
            pltpu.VMEM((chunks, 2, 4, PIECE, width), LOW),
            pltpu.VMEM((chunks, 4, PIECE, width), LOW),
            pltpu.VMEM((chunks, 2, PIECE, width), LOW),
            pltpu.VMEM((chunks, 2, PIECE, width), LOW),
            pltpu.VMEM((chunks, 1, PIECE, width), LOW),
            pltpu.VMEM((2, rows, width), LOW),
            pltpu.SemaphoreType.DMA((2, 6)),
            pltpu.SemaphoreType.DMA((2,)),
            pltpu.SemaphoreType.DMA((1,)),
            pltpu.SemaphoreType.DMA((1,)),
            pltpu.SemaphoreType.DMA((3,)),
            pltpu.SemaphoreType.DMA((3,)),
            pltpu.SemaphoreType.DMA((chunks, 5)),
            pltpu.SemaphoreType.DMA((chunks, 5)),
        ],
        compiler_params=pltpu.CompilerParams(
            collective_id=1, has_side_effects=True, vmem_limit_bytes=VMEM_BYTES
        ),
    )(*arrays, vec_zero, *quads, vec_one, grad, final)


def update_kernel(shares, halves_ref, *refs):
    old, new, turned = refs[:9], refs[9:18], refs[18]
    offset = lax.axis_index((DP, SEQ)) * shares.columns
    half, per, width, depth = shares.half, shares.per, shares.width, shares.depth // 2
    is_inner = (offset >= 3 * width) & (offset < 4 * width)
    is_hidden = offset >= 4 * width

    @pl.when(is_inner)
    def _():
        for side in range(2):
            piece = halves_ref[side, :half, :].astype(jnp.float32)
            wide = per * half
            back = jnp.transpose(jnp.concatenate([piece[:, :wide], piece[:, wide:]], axis=0))
            for j in range(per):
                turned[(2 * j + side) * half : (2 * j + side + 1) * half, :] = back[
                    j * half : (j + 1) * half
                ]

    @pl.when(jnp.logical_not(is_inner))
    def _():
        pair = [halves_ref[side, :half, :].astype(jnp.float32) for side in range(2)]
        plain = jnp.concatenate(pair, axis=0)
        hidden = jnp.concatenate(
            [pair[side][j * depth :][:depth] for j in range(shares.groups) for side in range(2)],
            axis=0,
        )
        turned[...] = jnp.transpose(jnp.where(is_hidden, hidden, plain))

    def store(first, gradient, rate, decay):
        results = adam_update(*[ref[...] for ref in old[first : first + 3]], gradient, rate, decay)
        for ref, result in zip(new[first : first + 3], results):
            ref[...] = result

    store(0, turned[...], rate_matrix, decay_matrix)
    down = [halves_ref[side, half : half + depth, :] for side in range(2)]
    store(3, jnp.concatenate(down, axis=0).astype(jnp.float32), rate_matrix, decay_matrix)
    tails = [halves_ref[side, half + depth :, :].astype(jnp.float32) for side in range(2)]
    store(6, (tails[0] + tails[1])[0:1, : shares.vector_len], rate_vector, 0.0)


def update(shares, halves, old):
    return pl.pallas_call(
        partial(update_kernel, shares),
        out_shape=[jax.ShapeDtypeStruct(piece.shape, jnp.float32) for piece in old],
        scratch_shapes=[pltpu.VMEM((shares.width, shares.columns), jnp.float32)],
        compiler_params=pltpu.CompilerParams(vmem_limit_bytes=VMEM_BYTES),
    )(halves, *old)


def window_forward(hidden, weights, biases, features, beside):
    proj, out, up, down = weights
    gain_one, shift_one, bias_query, bias_value, bias_out = biases[:5]
    gain_two, shift_two, bias_down, bias_up = biases[5:]
    unit, _ = normalized(hidden)
    normed = (unit * gain_one + shift_one).astype(LOW)
    bias = jnp.concatenate([bias_query, jnp.zeros_like(bias_query), bias_value])
    projected = (dot_rows(normed, proj) + bias).astype(LOW)
    projected = beside.tie(projected)
    attended, levels = attend(projected, *features, bias_query.shape[0])
    attended, levels = beside.tie((attended, levels))
    branch = dot_rows(attended, out)
    middle = hidden + (branch + swap(branch.astype(LOW)).astype(jnp.float32) + bias_out)
    unit_two, _ = normalized(middle)
    normed_two = (unit_two * gain_two + shift_two).astype(LOW)
    up_value = dot_rows(normed_two, up) + bias_up
    cdf = 0.5 * (1.0 + lax.erf(up_value * 0.5**0.5))
    active = (up_value * cdf).astype(LOW)
    slope = cdf + up_value * jnp.exp(-0.5 * up_value * up_value) * (0.5 / math.pi) ** 0.5
    active = beside.tie(active)
    part = dot_plain(active, down)
    output = middle + (part + swap(part.astype(LOW)).astype(jnp.float32) + bias_down)
    return output, (hidden, normed, projected, attended, levels, middle, normed_two, slope, active)


def window_backward(stored, grad_output, weights, biases, features, beside):
    hidden, normed, projected, attended, levels, middle, normed_two, slope, active = stored
    proj, out, up, down = weights
    gain_one, gain_two = biases[0], biases[5]
    grad_ffn = grad_output.astype(LOW)
    grad_bias_down = jnp.sum(grad_ffn.astype(jnp.float32), axis=0)
    grad_up = (dot_rows(grad_ffn, down) * slope).astype(LOW)
    grad_up = beside.tie(grad_up)
    grad_bias_up = jnp.sum(grad_up.astype(jnp.float32), axis=0)
    part = dot_plain(grad_up, up)
    arrived = swap(part.astype(LOW)).astype(jnp.float32)
    down_grad = dot_tokens(active, grad_ffn).astype(LOW)
    up_grad = dot_tokens(grad_up, normed_two).astype(LOW)
    grad_norm, grad_gain_two, grad_shift_two = norm_back(middle, part + arrived, gain_two)
    grad_middle = grad_output + grad_norm
    grad_branch = grad_middle.astype(LOW)
    grad_bias_out = jnp.sum(grad_branch.astype(jnp.float32), axis=0)
    out_grad = dot_tokens(grad_branch, attended).astype(LOW)
    grad_attended = dot_plain(grad_branch, out).astype(LOW)
    grad_attended = beside.tie(grad_attended)
    grad_proj = attend_back(projected, grad_attended, attended, levels, *features)
    grad_proj = beside.tie(grad_proj)
    summed = jnp.sum(grad_proj.astype(jnp.float32), axis=0)
    width = attended.shape[1]
    part = dot_plain(grad_proj, proj)
    arrived = swap(part.astype(LOW)).astype(jnp.float32)
    proj_grad = dot_tokens(grad_proj, normed).astype(LOW)
    grad_norm, grad_gain_one, grad_shift_one = norm_back(hidden, part + arrived, gain_one)
    vector_grads = (
        grad_gain_one,
        grad_shift_one,
        summed[:width],
        summed[2 * width :],
        grad_bias_out,
        grad_gain_two,
        grad_shift_two,
        grad_bias_down,
        grad_bias_up,
    )
    return grad_middle + grad_norm, (proj_grad, out_grad, up_grad, down_grad), vector_grads


def window_shards(
    block_input,
    cotangent,
    random_ids,
    segment_ids,
    global_ids,
    w_rows,
    w_rows_first,
    w_rows_second,
    w_down,
    w_down_first,
    w_down_second,
    vectors,
    vectors_first,
    vectors_second,
):
    core = lax.axis_index(SECTION)
    place = lax.axis_index(SEQ)
    micro, _, tokens, width = block_input.shape
    _, _, columns = w_rows.shape
    shares = Shares(width, columns, w_down.shape[1], vectors.shape[1])
    prepared = prepare(shares, w_rows[0], w_down[0], vectors)
    gathered_zero, gathered_one, hidden, grad = gather(shares, prepared, block_input, cotangent)

    head_half = shares.half // (width // HEADS)
    random_rows = lax.dynamic_index_in_dim(random_ids[:, 0], place, 0, keepdims=False)
    random_rows = random_rows.reshape(random_rows.shape[0], shares.per, 2, head_half, -1)
    random_rows = lax.dynamic_index_in_dim(random_rows, core, 2, keepdims=False)
    random_rows = random_rows.reshape(random_rows.shape[0], shares.per * head_half, -1)
    segments = lax.dynamic_index_in_dim(segment_ids[:, 0], place, 0, keepdims=False)
    global_rows = lax.dynamic_index_in_dim(global_ids[:, 0], place, 0, keepdims=False)
    features = key_features(random_rows, segments, global_rows)

    beside = Beside(spread_quads(shares, gathered_one[:2]))
    params = [shares.unpack(gathered_zero, core)]
    hidden = hidden.reshape(-1, width).astype(jnp.float32)
    output, stored_zero = window_forward(hidden, *params[0], features, beside)
    params.append(shares.unpack((*beside.flying, gathered_one[2]), core))
    hidden = output.astype(LOW).astype(jnp.float32)
    final, stored_one = window_forward(hidden, *params[1], features, Beside())
    final = final.astype(LOW).reshape(micro, tokens, width)

    grad = grad.reshape(-1, width).astype(jnp.float32)
    grad, *grads_one = window_backward(stored_one, grad, *params[1], features, Beside())
    *arrays_one, vec_one = shares.by_shard(*grads_one, core)
    beside = Beside(sum_quads(shares, arrays_one))
    grad = grad.astype(LOW).astype(jnp.float32)
    grad, *grads_zero = window_backward(stored_zero, grad, *params[0], features, beside)
    grad = grad.astype(LOW).reshape(micro, tokens, width)
    *arrays_zero, vec_zero = shares.by_shard(*grads_zero, core)
    halves, slices = scatter(shares, arrays_zero, vec_zero, beside.flying, vec_one, grad, final)
    section_result = slices.astype(jnp.float32)[None, :, None]
    old = [
        w_rows[0],
        w_rows_first[0],
        w_rows_second[0],
        w_down[0],
        w_down_first[0],
        w_down_second[0],
        vectors,
        vectors_first,
        vectors_second,
    ]
    new = update(shares, halves, old)
    return (section_result, *[piece[None] for piece in new[:6]], *new[6:])


def one_window_each(mesh, block_input, w_rows, w_down, vectors):
    micro, windows, length, width = block_input.shape
    shards = mesh.shape[DP] * mesh.shape[SEQ]
    columns, depth = w_rows.shape[2] // shards, w_down.shape[1] // shards
    head_dim = width // HEADS
    tokens = length // mesh.shape[SEQ]
    return (
        mesh.shape[SECTION] == 2
        and mesh.shape[SEQ] == micro
        and mesh.shape[DP] == windows
        and tokens % (2 * BLOCK) == 0
        and length % CHUNK == 0
        and head_dim == 64
        and width % columns == 0
        and columns % (2 * head_dim) == 0
        and columns % depth == 0
        and width // columns * (columns // 2) % 128 == 0
        and depth % 32 == 0
        and vectors.shape[1] // shards <= width
        and mesh.shape[DP] == 4
        and micro == 4
        and width == 2 * columns
        and (columns // 2) % (2 * PIECE) == 0
        and (depth // 2) % (2 * PIECE) == 0
    )


def solution(mesh):
    in_specs = (
        P(None, DP, SEQ, None),
        P(None, DP, SEQ, None),
        P(None, DP, None, None, None),
        P(None, DP, None),
        P(None, DP, None),
        P(SECTION, None, (DP, SEQ)),
        P(SECTION, None, (DP, SEQ)),
        P(SECTION, None, (DP, SEQ)),
        P(SECTION, (DP, SEQ), None),
        P(SECTION, (DP, SEQ), None),
        P(SECTION, (DP, SEQ), None),
        P(SECTION, (DP, SEQ)),
        P(SECTION, (DP, SEQ)),
        P(SECTION, (DP, SEQ)),
    )
    out_specs = (
        P(SECTION, None, DP, SEQ, None),
        P(SECTION, None, (DP, SEQ)),
        P(SECTION, None, (DP, SEQ)),
        P(SECTION, None, (DP, SEQ)),
        P(SECTION, (DP, SEQ), None),
        P(SECTION, (DP, SEQ), None),
        P(SECTION, (DP, SEQ), None),
        P(SECTION, (DP, SEQ)),
        P(SECTION, (DP, SEQ)),
        P(SECTION, (DP, SEQ)),
    )

    def step(*arrays):
        chosen = general_shards
        if one_window_each(mesh, arrays[0], arrays[5], arrays[8], arrays[11]):
            chosen = window_shards
        return jax.shard_map(
            chosen, mesh=mesh, in_specs=in_specs, out_specs=out_specs, check_vma=False
        )(*arrays)

    return step
```

```python
import math
from functools import partial

import jax
import jax.numpy as jnp
import ml_dtypes
import numpy as np
from jax import lax
from jax.experimental import pallas as pl
from jax.experimental.pallas import tpu as pltpu
from jax.sharding import PartitionSpec as P

SECTION, DP, SEQ = "section", "dp", "seq"
HEADS = 12
BLOCK = 64
STEP = 5


epsilon = 1e-05
masked = -1e30
rate_matrix = 0.02
rate_vector = 0.2
decay_matrix = 0.01


def with_halo(x, sides, width):
    for axis, dim in sides:
        devices, length = (lax.axis_size(axis), x.shape[dim])
        up = [(i, (i + 1) % devices) for i in range(devices - 1)]
        down = [(j, i) for i, j in up]
        last = lax.slice_in_dim(x, length - width, length, axis=dim)
        initial = lax.slice_in_dim(x, 0, width, axis=dim)
        before = lax.ppermute(last, axis, up)
        after = lax.ppermute(initial, axis, down)
        x = jnp.concatenate([before, x, after], axis=dim)
    return x


def merged(value, axis, join):
    pieces = jax.tree.map(lambda part: lax.all_gather(part, axis), value)
    head = jax.tree.map(lambda part: part[0], pieces)
    tail = jax.tree.map(lambda part: part[1:], pieces)
    subtotal, _ = lax.scan(lambda subtotal, share: (join(subtotal, share), None), head, tail)
    return subtotal


def from_behind(x, axis, by):
    devices = lax.axis_size(axis)
    pairs = [(i, i + by) for i in range(devices) if 0 <= i + by < devices]
    return lax.ppermute(x, axis, pairs)


def partner(value, axis, bit):
    mask = 2**bit
    pairs = [(source, source ^ mask) for source in range(lax.axis_size(axis))]
    return lax.ppermute(value, axis, pairs)


def mixed_sum(form, left, right):
    return jnp.einsum(form, left, right, preferred_element_type=jnp.float32)


def exact_two(form, left, right):
    return jnp.einsum(
        form, left, right, precision=lax.Precision.HIGHEST, preferred_element_type=jnp.float32
    )


def norm_rows(values_in, gain_vec, shift_vec):
    row_mean = jnp.mean(values_in, axis=-1, keepdims=True)
    centred = values_in - row_mean
    spread = jnp.mean(centred * centred, axis=-1, keepdims=True)
    return centred * lax.rsqrt(spread + epsilon) * gain_vec + shift_vec


def split_vectors(vector_weights, model_width):
    pieces = [
        vector_weights[piece_index * model_width : (piece_index + 1) * model_width]
        for piece_index in range(8)
    ]
    return pieces + [vector_weights[8 * model_width :]]


def route_tables(random_rows, segments, global_rows, seq_place, groups):
    windows, blocks, head_count, pick_count = random_rows.shape
    blocks_dev = blocks // groups
    request_count = blocks_dev * head_count * pick_count
    capacity = -(-request_count // groups)
    requests = random_rows.reshape(windows, groups, request_count)
    owners = requests // blocks_dev
    inside = requests % blocks_dev
    head_of = jnp.arange(request_count) // pick_count % head_count
    is_mine = owners == seq_place
    slot_index = jnp.cumsum(is_mine.astype(jnp.int32), axis=2) - 1
    slot_hot = ((slot_index[..., None] == jnp.arange(capacity)) & is_mine[..., None]).astype(
        jnp.float32
    )
    inside_hot = (inside[..., None] == jnp.arange(blocks_dev)).astype(jnp.float32)
    head_hot = (head_of[:, None] == jnp.arange(head_count)).astype(jnp.float32)
    sender = jnp.einsum(
        "wqsc,wqsb,sh->wqcbh", slot_hot, inside_hot, head_hot, precision=lax.Precision.HIGHEST
    )
    my_owners = lax.dynamic_index_in_dim(owners, seq_place, axis=1, keepdims=False)
    earlier = jnp.arange(request_count)[None, :] < jnp.arange(request_count)[:, None]
    same_owner = my_owners[:, :, None] == my_owners[:, None, :]
    rank_index = jnp.sum((same_owner & earlier[None]).astype(jnp.int32), axis=2)
    picker = (
        (my_owners[..., None, None] == jnp.arange(groups)[:, None])
        & (rank_index[..., None, None] == jnp.arange(capacity)[None, :])
    ).astype(jnp.float32)
    first_block = seq_place * blocks_dev
    owned_hot = (global_rows[:, :, None] == first_block + jnp.arange(blocks_dev)).astype(
        jnp.float32
    )
    length = segments.shape[1]
    block_len = length // blocks
    seg_blocks = segments.reshape(windows, blocks, block_len)
    seg_pad = jnp.pad(seg_blocks, ((0, 0), (1, 1), (0, 0)), constant_values=-1)
    near_segs = lax.dynamic_slice_in_dim(seg_pad, first_block, blocks_dev + 2, axis=1)
    slide_seg = jnp.concatenate([near_segs[:, :-2], near_segs[:, 1:-1], near_segs[:, 2:]], axis=2)
    query_seg = near_segs[:, 1:-1]
    rows_index = jnp.arange(windows)
    global_seg = seg_blocks[rows_index[:, None], global_rows].reshape(windows, -1)
    chosen = lax.dynamic_slice_in_dim(random_rows, first_block, blocks_dev, axis=1)
    far_seg = seg_blocks[rows_index[:, None, None, None], chosen].reshape(
        windows, blocks_dev, head_count, -1
    )
    key_seg = jnp.concatenate(
        [
            jnp.broadcast_to(
                slide_seg[:, :, None, :], (windows, blocks_dev, head_count, slide_seg.shape[2])
            ),
            jnp.broadcast_to(
                global_seg[:, None, None, :], (windows, blocks_dev, head_count, global_seg.shape[1])
            ),
            far_seg,
        ],
        axis=3,
    )
    key_mask = query_seg[:, :, None, :, None] == key_seg[:, :, :, None, :]
    local_seg = query_seg.reshape(windows, -1)
    full_mask = global_seg[:, None, :, None] == local_seg[:, None, None, :]
    return (sender, picker, owned_hot, key_mask, full_mask)


def fetch_blocks(paired, queries, sender, picker, owned_hot):
    windows, tokens, head_count, doubled = paired.shape
    head_dim = queries.shape[-1]
    blocks_dev = tokens // BLOCK
    flattened = paired.reshape(windows, tokens, head_count * doubled)
    padded = with_halo(flattened, ((SEQ, 1),), BLOCK)
    framed = padded.reshape(windows, blocks_dev + 2, BLOCK, head_count, doubled)
    sliding = jnp.concatenate([framed[:, :-2], framed[:, 1:-1], framed[:, 2:]], axis=2)
    local_blocks = paired.reshape(windows, blocks_dev, BLOCK, head_count, doubled)
    owned_low = owned_hot.astype(jnp.bfloat16)
    offered = mixed_sum("wgb,wbthe->wgthe", owned_low, local_blocks)
    offered_queries = mixed_sum("wgb,wbqhd->wgqhd", owned_low, queries)
    global_kv, global_queries = (
        lax.psum(offered.astype(jnp.bfloat16), SEQ).astype(jnp.float32),
        lax.psum(offered_queries.astype(jnp.bfloat16), SEQ).astype(jnp.float32),
    )
    global_kv = global_kv.astype(jnp.bfloat16).reshape(windows, -1, head_count, doubled)
    global_queries = global_queries.astype(jnp.bfloat16).reshape(windows, -1, head_count, head_dim)
    outgoing = mixed_sum("wqcbh,wbthe->qwcte", sender.astype(jnp.bfloat16), local_blocks).astype(
        jnp.bfloat16
    )
    incoming = lax.all_to_all(outgoing, SEQ, split_axis=0, concat_axis=0, tiled=True)
    distant = mixed_sum("wspc,pwcte->wste", picker.astype(jnp.bfloat16), incoming).astype(
        jnp.bfloat16
    )
    pick_count = picker.shape[1] // (blocks_dev * head_count)
    distant = distant.reshape(windows, blocks_dev, head_count, pick_count, BLOCK, doubled)
    return (sliding, global_kv, distant, global_queries)


def combine_stats(earlier, later):
    top = jnp.maximum(earlier[0], later[0])
    return (top, earlier[1] * jnp.exp(earlier[0] - top) + later[1] * jnp.exp(later[0] - top))


def full_forward(global_queries, key_part, value_part, full_mask, head_dim):
    scores = mixed_sum("wqhd,wkhd->whqk", global_queries, key_part) * head_dim ** (-0.5)
    scores = jnp.where(full_mask, scores, masked)
    local_top = jnp.max(scores, axis=3, keepdims=True)
    local_sum = jnp.sum(
        jnp.where(full_mask, jnp.exp(scores - local_top), 0.0), axis=3, keepdims=True
    )
    row_top, row_sum = merged((local_top, local_sum), SEQ, combine_stats)
    full_probs = jnp.where(full_mask, jnp.exp(scores - row_top), 0.0) / row_sum
    partial_out = mixed_sum("whqk,wkhd->wqhd", full_probs.astype(jnp.bfloat16), value_part)
    full_out = lax.psum(partial_out.astype(jnp.bfloat16), SEQ).astype(jnp.float32)
    return (full_out, full_probs)


def attention_weights(queries, sliding, global_kv, distant, key_mask):
    head_dim = queries.shape[-1]
    windows, blocks_dev, _, head_count, _ = queries.shape
    near_scores = mixed_sum("wbqhd,wbkhd->wbhqk", queries, sliding[..., :head_dim])
    global_scores = mixed_sum("wbqhd,wkhd->wbhqk", queries, global_kv[..., :head_dim])
    far_scores = mixed_sum("wbqhd,wbhrkd->wbhqrk", queries, distant[..., :head_dim])
    far_scores = far_scores.reshape(windows, blocks_dev, head_count, BLOCK, -1)
    scores = jnp.concatenate([near_scores, global_scores, far_scores], axis=4) * head_dim ** (-0.5)
    scores = jnp.where(key_mask, scores, masked)
    row_top = jnp.max(scores, axis=4, keepdims=True)
    weight = jnp.exp(scores - row_top)
    return weight / jnp.sum(weight, axis=4, keepdims=True)


def split_keys(scores_like, sliding, global_kv, distant):
    near_keys = sliding.shape[2]
    global_keys = global_kv.shape[1]
    windows, blocks_dev, head_count, pick_count, _, _ = distant.shape
    near_part = scores_like[..., :near_keys]
    global_part = scores_like[..., near_keys : near_keys + global_keys]
    far_part = scores_like[..., near_keys + global_keys :].reshape(
        windows, blocks_dev, head_count, BLOCK, pick_count, BLOCK
    )
    return (near_part, global_part, far_part)


def attention_values(low_probs, sliding, global_kv, distant, head_dim):
    near_part, global_part, far_part = split_keys(low_probs, sliding, global_kv, distant)
    attended = mixed_sum("wbhqk,wbkhd->wbqhd", near_part, sliding[..., head_dim:])
    attended = attended + mixed_sum("wbhqk,wkhd->wbqhd", global_part, global_kv[..., head_dim:])
    return attended + mixed_sum("wbhqrk,wbhrkd->wbqhd", far_part, distant[..., head_dim:])


def layer_forward(hidden, weights, tables):
    row_weights, down_weights, vector_weights = weights
    sender, picker, owned_hot, key_mask, full_mask = tables
    model_width = row_weights.shape[0]
    windows, tokens, _ = hidden.shape
    blocks_dev = tokens // BLOCK
    head_dim = model_width // HEADS
    (
        gain_one,
        shift_one,
        bias_query,
        bias_value,
        bias_out,
        gain_two,
        shift_two,
        bias_down,
        bias_up,
    ) = split_vectors(vector_weights, model_width)
    normed = norm_rows(hidden, gain_one, shift_one).astype(jnp.bfloat16)
    projected = mixed_sum("wtd,de->wte", normed, row_weights[:, : 3 * model_width])
    projected = (
        projected + jnp.concatenate([bias_query, jnp.zeros_like(bias_query), bias_value])
    ).astype(jnp.bfloat16)
    queries = projected[..., :model_width].reshape(windows, blocks_dev, BLOCK, HEADS, head_dim)
    key_part = projected[..., model_width : 2 * model_width].reshape(
        windows, tokens, HEADS, head_dim
    )
    value_part = projected[..., 2 * model_width :].reshape(windows, tokens, HEADS, head_dim)
    paired = jnp.concatenate([key_part, value_part], axis=3)
    sliding, global_kv, distant, global_queries = fetch_blocks(
        paired, queries, sender, picker, owned_hot
    )
    probabilities = attention_weights(queries, sliding, global_kv, distant, key_mask)
    attended = attention_values(
        probabilities.astype(jnp.bfloat16), sliding, global_kv, distant, head_dim
    )
    full_out, full_probs = full_forward(global_queries, key_part, value_part, full_mask, head_dim)
    placed = exact_two(
        "wgb,wgqhd->wbqhd", owned_hot, full_out.reshape(windows, -1, BLOCK, HEADS, head_dim)
    )
    on_global = jnp.sum(owned_hot, axis=1)[:, :, None, None, None] > 0
    attended = jnp.where(on_global, placed, attended)
    mixed_low = attended.reshape(windows, tokens, model_width).astype(jnp.bfloat16)
    middle = (
        hidden
        + mixed_sum("wtd,de->wte", mixed_low, row_weights[:, 3 * model_width : 4 * model_width])
        + bias_out
    )
    normed_two = norm_rows(middle, gain_two, shift_two).astype(jnp.bfloat16)
    up_value = mixed_sum("wtd,df->wtf", normed_two, row_weights[:, 4 * model_width :]) + bias_up
    active = jax.nn.gelu(up_value, approximate=False).astype(jnp.bfloat16)
    output = middle + mixed_sum("wtf,fd->wtd", active, down_weights) + bias_down
    stored = (
        hidden,
        normed,
        queries,
        sliding,
        global_kv,
        distant,
        probabilities,
        mixed_low,
        middle,
        normed_two,
        up_value,
        active,
        key_part,
        value_part,
        global_queries,
        full_probs,
    )
    return (output, stored)


def return_blocks(near_back, global_back, far_back, query_part, sender, picker, owned_hot):
    windows, blocks_dev, _, head_count, doubled = near_back.shape
    first_third = near_back[:, :, :BLOCK]
    centre_third = near_back[:, :, BLOCK : 2 * BLOCK]
    last_third = near_back[:, :, 2 * BLOCK :]
    framed = jnp.pad(first_third, ((0, 0), (0, 2), (0, 0), (0, 0), (0, 0)))
    framed = framed + jnp.pad(centre_third, ((0, 0), (1, 1), (0, 0), (0, 0), (0, 0)))
    framed = framed + jnp.pad(last_third, ((0, 0), (2, 0), (0, 0), (0, 0), (0, 0)))
    own_grad = framed[:, 1:-1]
    for direction in (1, -1):
        rim_grad = framed[:, -1] if direction == 1 else framed[:, 0]
        arrived = from_behind(rim_grad.astype(jnp.bfloat16), SEQ, direction).astype(
            rim_grad.dtype
        )
        if direction == 1:
            own_grad = jnp.concatenate(
                [own_grad[:, :1] + arrived[:, None], own_grad[:, 1:]], axis=1
            )
        else:
            own_grad = jnp.concatenate(
                [own_grad[:, :-1], own_grad[:, -1:] + arrived[:, None]], axis=1
            )
    global_total, query_total = (
        lax.psum(
            global_back.reshape(windows, -1, BLOCK, head_count, doubled).astype(jnp.bfloat16), SEQ
        ).astype(jnp.float32),
        lax.psum(query_part.astype(jnp.bfloat16), SEQ).astype(jnp.float32),
    )
    own_grad = own_grad + exact_two("wgb,wgthe->wbthe", owned_hot, global_total)
    far_flat = far_back.reshape(windows, -1, BLOCK, doubled)
    returning = exact_two("wspc,wste->pwcte", picker, far_flat)
    arrived_far = lax.all_to_all(
        returning.astype(jnp.bfloat16), SEQ, split_axis=0, concat_axis=0, tiled=True
    ).astype(returning.dtype)
    own_grad = own_grad + exact_two("wqcbh,qwcte->wbthe", sender, arrived_far)
    return (own_grad.reshape(windows, blocks_dev * BLOCK, head_count, doubled), query_total)


def attention_back(
    grad_attended,
    queries,
    sliding,
    global_kv,
    distant,
    probabilities,
    key_part,
    value_part,
    global_queries,
    full_probs,
    sender,
    picker,
    owned_hot,
):
    head_dim = queries.shape[-1]
    score_scale = head_dim ** (-0.5)
    windows, blocks_dev, _, head_count, _ = queries.shape
    on_global = jnp.sum(owned_hot, axis=1)[:, :, None, None, None] > 0
    selected = mixed_sum("wgb,wbqhd->wgqhd", owned_hot.astype(jnp.bfloat16), grad_attended)
    rows_grad = lax.psum(selected.astype(jnp.bfloat16), SEQ).reshape(
        windows, -1, head_count, head_dim
    )
    grad_attended = jnp.where(on_global, jnp.zeros_like(grad_attended), grad_attended)
    low_probs = probabilities.astype(jnp.bfloat16)
    near_grad = mixed_sum("wbqhd,wbkhd->wbhqk", grad_attended, sliding[..., head_dim:])
    global_grad = mixed_sum("wbqhd,wkhd->wbhqk", grad_attended, global_kv[..., head_dim:])
    far_grad = mixed_sum("wbqhd,wbhrkd->wbhqrk", grad_attended, distant[..., head_dim:])
    far_grad = far_grad.reshape(windows, blocks_dev, head_count, BLOCK, -1)
    grad_probs = jnp.concatenate([near_grad, global_grad, far_grad], axis=4)
    grad_scores = probabilities * (
        grad_probs - jnp.sum(probabilities * grad_probs, axis=4, keepdims=True)
    )
    grad_scores = grad_scores.astype(jnp.bfloat16)
    near_split, global_split, far_split = split_keys(grad_scores, sliding, global_kv, distant)
    near_probs, global_probs, far_probs = split_keys(low_probs, sliding, global_kv, distant)
    grad_query = mixed_sum("wbhqk,wbkhd->wbqhd", near_split, sliding[..., :head_dim])
    grad_query = grad_query + mixed_sum(
        "wbhqk,wkhd->wbqhd", global_split, global_kv[..., :head_dim]
    )
    grad_query = (
        grad_query + mixed_sum("wbhqrk,wbhrkd->wbqhd", far_split, distant[..., :head_dim])
    ) * score_scale
    near_back = jnp.concatenate(
        [
            mixed_sum("wbhqk,wbqhd->wbkhd", near_split, queries) * score_scale,
            mixed_sum("wbhqk,wbqhd->wbkhd", near_probs, grad_attended),
        ],
        axis=4,
    )
    global_back = jnp.concatenate(
        [
            mixed_sum("wbhqk,wbqhd->wkhd", global_split, queries) * score_scale,
            mixed_sum("wbhqk,wbqhd->wkhd", global_probs, grad_attended),
        ],
        axis=3,
    )
    far_back = jnp.concatenate(
        [
            mixed_sum("wbhqrk,wbqhd->wbhrkd", far_split, queries) * score_scale,
            mixed_sum("wbhqrk,wbqhd->wbhrkd", far_probs, grad_attended),
        ],
        axis=5,
    )
    full_grad_probs = mixed_sum("wqhd,wkhd->whqk", rows_grad, value_part)
    partial_dot = jnp.sum(full_probs * full_grad_probs, axis=3, keepdims=True)
    row_dot = lax.psum(partial_dot, SEQ)
    full_grad_scores = (full_probs * (full_grad_probs - row_dot)).astype(jnp.bfloat16)
    query_part = mixed_sum("whqk,wkhd->wqhd", full_grad_scores, key_part) * score_scale
    full_key_grad = mixed_sum("whqk,wqhd->wkhd", full_grad_scores, global_queries) * score_scale
    full_value_grad = mixed_sum("whqk,wqhd->wkhd", full_probs.astype(jnp.bfloat16), rows_grad)
    grad_paired, query_total = return_blocks(
        near_back, global_back, far_back, query_part, sender, picker, owned_hot
    )
    grad_query = grad_query + exact_two(
        "wgb,wgqhd->wbqhd", owned_hot, query_total.reshape(windows, -1, BLOCK, head_count, head_dim)
    )
    grad_paired = grad_paired + jnp.concatenate([full_key_grad, full_value_grad], axis=3)
    return (grad_query, grad_paired)


def layer_backward(stored, grad_output, weights, tables):
    row_weights, down_weights, vector_weights = weights
    sender, picker, owned_hot, key_mask, full_mask = tables
    (
        hidden,
        normed,
        queries,
        sliding,
        global_kv,
        distant,
        probabilities,
        mixed_low,
        middle,
        normed_two,
        up_value,
        active,
        key_part,
        value_part,
        global_queries,
        full_probs,
    ) = stored
    model_width = row_weights.shape[0]
    windows, tokens, _ = hidden.shape
    blocks_dev = tokens // BLOCK
    head_dim = model_width // HEADS
    (
        gain_one,
        shift_one,
        bias_query,
        bias_value,
        bias_out,
        gain_two,
        shift_two,
        bias_down,
        bias_up,
    ) = split_vectors(vector_weights, model_width)
    grad_ffn = grad_output.astype(jnp.bfloat16)
    grad_bias_down = jnp.sum(grad_ffn.astype(jnp.float32), axis=(0, 1))
    grad_down = mixed_sum("wtf,wtd->fd", active, grad_ffn)
    grad_active = mixed_sum("wtd,fd->wtf", grad_ffn, down_weights)
    gelu_pull = jax.vjp(partial(jax.nn.gelu, approximate=False), up_value)[1]
    grad_up = gelu_pull(grad_active)[0].astype(jnp.bfloat16)
    grad_bias_up = jnp.sum(grad_up.astype(jnp.float32), axis=(0, 1))
    grad_in = mixed_sum("wtd,wtf->df", normed_two, grad_up)
    grad_normed_two = mixed_sum("wtf,df->wtd", grad_up, row_weights[:, 4 * model_width :])
    norm_pull_two = jax.vjp(norm_rows, middle, gain_two, shift_two)[1]
    grad_middle_norm, grad_gain_two, grad_shift_two = norm_pull_two(grad_normed_two)
    grad_middle = grad_output + grad_middle_norm
    grad_branch = grad_middle.astype(jnp.bfloat16)
    grad_bias_out = jnp.sum(grad_branch.astype(jnp.float32), axis=(0, 1))
    grad_out_weight = mixed_sum("wtd,wte->de", mixed_low, grad_branch)
    grad_attended = mixed_sum(
        "wte,de->wtd", grad_branch, row_weights[:, 3 * model_width : 4 * model_width]
    ).astype(jnp.bfloat16)
    grad_attended = grad_attended.reshape(windows, blocks_dev, BLOCK, HEADS, head_dim)
    grad_query, grad_paired = attention_back(
        grad_attended,
        queries,
        sliding,
        global_kv,
        distant,
        probabilities,
        key_part,
        value_part,
        global_queries,
        full_probs,
        sender,
        picker,
        owned_hot,
    )
    grad_projected = jnp.concatenate(
        [
            grad_query.reshape(windows, tokens, model_width),
            grad_paired[..., :head_dim].reshape(windows, tokens, model_width),
            grad_paired[..., head_dim:].reshape(windows, tokens, model_width),
        ],
        axis=2,
    ).astype(jnp.bfloat16)
    summed = jnp.sum(grad_projected.astype(jnp.float32), axis=(0, 1))
    grad_bias_query = summed[:model_width]
    grad_bias_value = summed[2 * model_width :]
    grad_projection = mixed_sum("wtd,wte->de", normed, grad_projected)
    grad_normed = mixed_sum("wte,de->wtd", grad_projected, row_weights[:, : 3 * model_width])
    norm_pull_one = jax.vjp(norm_rows, hidden, gain_one, shift_one)[1]
    grad_hidden_norm, grad_gain_one, grad_shift_one = norm_pull_one(grad_normed)
    grad_hidden = grad_middle + grad_hidden_norm
    grad_rows = jnp.concatenate([grad_projection, grad_out_weight, grad_in], axis=1)
    grad_vectors = jnp.concatenate(
        [
            grad_gain_one,
            grad_shift_one,
            grad_bias_query,
            grad_bias_value,
            grad_bias_out,
            grad_gain_two,
            grad_shift_two,
            grad_bias_down,
            grad_bias_up,
        ]
    )
    return (grad_hidden, (grad_rows, grad_down, grad_vectors))


def adam_update(master, first_old, second_old, gradient, step_rate, decay_rate):
    first_new = 0.5 * first_old + 0.5 * gradient
    second_new = 0.5 * second_old + 0.5 * gradient * gradient
    first_hat = first_new / (1.0 - 0.5**STEP)
    second_hat = second_new / (1.0 - 0.5**STEP)
    master_new = master - step_rate * (
        first_hat / (jnp.sqrt(second_hat) + 1e-08) + decay_rate * master
    )
    return (master_new, first_new, second_new)


def general_shards(
    block_input,
    cotangent,
    random_ids,
    segment_ids,
    global_ids,
    w_rows,
    w_rows_first,
    w_rows_second,
    w_down,
    w_down_first,
    w_down_second,
    vectors,
    vectors_first,
    vectors_second,
):
    section_index = lax.axis_index(SECTION)
    seq_place = lax.axis_index(SEQ)
    groups = lax.axis_size(SEQ)
    row_weights, down_weights, vector_low = (
        lax.all_gather(w_rows[0].astype(jnp.bfloat16), (DP, SEQ), axis=1, tiled=True),
        lax.all_gather(w_down[0].astype(jnp.bfloat16), (DP, SEQ), axis=0, tiled=True),
        lax.all_gather(vectors[0].astype(jnp.bfloat16), (DP, SEQ), axis=0, tiled=True),
    )
    weights = (row_weights, down_weights, vector_low.astype(jnp.float32))
    micro_count, windows, tokens, model_width = block_input.shape
    received = jnp.zeros((windows, tokens, model_width), jnp.bfloat16)
    results = jnp.zeros(block_input.shape, jnp.float32)
    full_totals = (
        jnp.zeros(row_weights.shape, jnp.float32),
        jnp.zeros(down_weights.shape, jnp.float32),
        jnp.zeros(vector_low.shape, jnp.float32),
    )

    def tick(tick_index, carry):
        received, results, full_totals = carry
        forward_mb = jnp.clip(tick_index - section_index, 0, micro_count - 1)
        behind_raw = tick_index - 2 + section_index
        behind = jnp.clip(behind_raw, 0, micro_count - 1)
        live_mask = ((behind_raw >= 0) & (behind_raw < micro_count)).astype(jnp.float32)
        tables_forward = route_tables(
            lax.dynamic_index_in_dim(random_ids, forward_mb, 0, keepdims=False),
            lax.dynamic_index_in_dim(segment_ids, forward_mb, 0, keepdims=False),
            lax.dynamic_index_in_dim(global_ids, forward_mb, 0, keepdims=False),
            seq_place,
            groups,
        )
        tables_behind = route_tables(
            lax.dynamic_index_in_dim(random_ids, behind, 0, keepdims=False),
            lax.dynamic_index_in_dim(segment_ids, behind, 0, keepdims=False),
            lax.dynamic_index_in_dim(global_ids, behind, 0, keepdims=False),
            seq_place,
            groups,
        )
        incoming_values = received.astype(jnp.float32)
        first_input = lax.dynamic_index_in_dim(block_input, forward_mb, 0, keepdims=False).astype(
            jnp.float32
        )
        forward_input = jnp.where(section_index == 0, first_input, incoming_values)
        forward_output = layer_forward(forward_input, weights, tables_forward)[0]
        back_source = lax.dynamic_index_in_dim(block_input, behind, 0, keepdims=False).astype(
            jnp.float32
        )
        back_input = jnp.where(section_index == 0, back_source, incoming_values)
        given_grad = lax.dynamic_index_in_dim(cotangent, behind, 0, keepdims=False).astype(
            jnp.float32
        )
        back_grad = jnp.where(section_index == 0, incoming_values, given_grad) * live_mask
        stored = layer_forward(back_input, weights, tables_behind)[1]
        grad_input, gradients = layer_backward(stored, back_grad, weights, tables_behind)
        outgoing = jnp.where(section_index == 0, forward_output, grad_input).astype(jnp.bfloat16)
        finished = jnp.where(section_index == 0, grad_input, forward_output)
        updated = lax.dynamic_update_index_in_dim(results, finished, behind, 0)
        results = jnp.where(live_mask > 0, updated, results)
        full_totals = tuple(
            (total_part + grad_part for total_part, grad_part in zip(full_totals, gradients))
        )
        return (partner(outgoing, SECTION, 0), results, full_totals)

    received, results, full_totals = lax.fori_loop(
        0, micro_count + 2, tick, (received, results, full_totals)
    )
    shard_totals = (
        lax.psum_scatter(full_totals[0], (DP, SEQ), scatter_dimension=1, tiled=True),
        lax.psum_scatter(full_totals[1], (DP, SEQ), scatter_dimension=0, tiled=True),
        lax.psum_scatter(full_totals[2], (DP, SEQ), scatter_dimension=0, tiled=True),
    )
    new_rows, new_rows_first, new_rows_second = adam_update(
        w_rows[0], w_rows_first[0], w_rows_second[0], shard_totals[0], rate_matrix, decay_matrix
    )
    new_down, new_down_first, new_down_second = adam_update(
        w_down[0], w_down_first[0], w_down_second[0], shard_totals[1], rate_matrix, decay_matrix
    )
    new_vectors, new_vectors_first, new_vectors_second = adam_update(
        vectors[0], vectors_first[0], vectors_second[0], shard_totals[2], rate_vector, 0.0
    )
    return (
        results[None],
        new_rows[None],
        new_rows_first[None],
        new_rows_second[None],
        new_down[None],
        new_down_first[None],
        new_down_second[None],
        new_vectors[None],
        new_vectors_first[None],
        new_vectors_second[None],
    )


LOW = jnp.bfloat16
LOG_HIGH = [float(np.log(c).astype(ml_dtypes.bfloat16)) for c in (1.0, 2.0, 3.0)]
LOG_LOW = [float(np.log(c)) - high for c, high in zip((1.0, 2.0, 3.0), LOG_HIGH)]
CHUNK = 256
VMEM_BYTES = 48 * 1024 * 1024


def dot_rows(left, right):
    return lax.dot_general(left, right, (((1,), (1,)), ((), ())), preferred_element_type=jnp.float32)


def dot_plain(left, right):
    return lax.dot_general(left, right, (((1,), (0,)), ((), ())), preferred_element_type=jnp.float32)


def dot_tokens(left, right):
    return lax.dot_general(left, right, (((0,), (0,)), ((), ())), preferred_element_type=jnp.float32)


def attend_kernel(
    half, q_ref, k_ref, v_ref, qa_ref, ka_ref, packed_ref, out_ref, lse_ref, branch_ref, low_ref
):
    tokens, pair = q_ref.shape
    left = lax.broadcasted_iota(jnp.int32, (CHUNK, pair), 1) < pair // 2
    keys = jnp.concatenate([k_ref[...], ka_ref[...]], axis=1)
    values = v_ref[...]

    def step(index, carry):
        rows = pl.ds(pl.multiple_of(index * CHUNK, CHUNK), CHUNK)
        queries = q_ref[rows, :] * 0.125
        outs, tops = [], []
        for head in range(2):
            mine = left if head == 0 else jnp.logical_not(left)
            side = jnp.where(mine, queries, jnp.zeros_like(queries))
            scores = dot_rows(jnp.concatenate([side, qa_ref[head, rows, :]], axis=1), keys)
            top = jnp.max(scores, axis=1, keepdims=True)
            weight = jnp.exp(scores - top)
            total = jnp.sum(weight, axis=1, keepdims=True)
            outs.append(dot_plain(weight.astype(LOW), values) / total)
            tops.append(top + jnp.log(total))
        out_ref[rows, :] = jnp.where(left, outs[0], outs[1]).astype(LOW)
        lse_ref[rows, :] = jnp.where(left, tops[0], tops[1])
        return carry

    lax.fori_loop(0, tokens // CHUNK, step, 0)
    place = pl.program_id(0)
    wide = packed_ref.shape[1] // 2
    weights = jnp.concatenate(
        [
            packed_ref[
                shard * half : (shard + 1) * half,
                pl.ds(pl.multiple_of(side * wide + place * pair, pair), pair),
            ]
            for shard in range(2)
            for side in range(2)
        ],
        axis=0,
    )

    @pl.when(place == 0)
    def _():
        branch_ref[...] = jnp.zeros_like(branch_ref)

    def project_out(rows):
        branch_ref[rows, :] += dot_rows(out_ref[rows, :], weights)

    by_rows(tokens, project_out)

    @pl.when(place == pl.num_programs(0) - 1)
    def _():
        low_ref[...] = branch_ref[...].astype(LOW)


def attend(projected, query_side, key_side, rows, half):
    tokens = projected.shape[0]
    width = projected.shape[1] // 3
    model = rows.shape[1]
    pairs = width // 128
    features = key_side.shape[1]
    return pl.pallas_call(
        partial(attend_kernel, half),
        grid=(pairs,),
        in_specs=[
            pl.BlockSpec((tokens, 128), lambda p: (0, p)),
            pl.BlockSpec((tokens, 128), lambda p: (0, pairs + p)),
            pl.BlockSpec((tokens, 128), lambda p: (0, 2 * pairs + p)),
            pl.BlockSpec((2, tokens, features), lambda p: (p, 0, 0)),
            whole((tokens, features)),
            pl.BlockSpec((COLS, model), lambda p: (3, 0)),
        ],
        out_specs=[
            pl.BlockSpec((tokens, 128), lambda p: (0, p)),
            pl.BlockSpec((tokens, 128), lambda p: (0, p)),
            whole((tokens, model)),
            whole((tokens, model)),
        ],
        out_shape=[
            jax.ShapeDtypeStruct((tokens, width), LOW),
            jax.ShapeDtypeStruct((tokens, width), jnp.float32),
            jax.ShapeDtypeStruct((tokens, model), jnp.float32),
            jax.ShapeDtypeStruct((tokens, model), LOW),
        ],
        **params_of(
            16 * pairs * tokens * tokens * 128, tokens * width * 16, 2 * pairs * tokens * tokens
        ),
    )(projected, projected, projected, query_side, key_side, rows)


def three_terms(values):
    high = values.astype(LOW).astype(jnp.float32)
    rest = values - high
    middle = rest.astype(LOW).astype(jnp.float32)
    return high, middle, rest - middle


def attend_back_kernel(
    q_ref, k_ref, v_ref, do_ref, o_ref, lse_ref, qa_ref, ka_ref, grad_ref, dk_acc, dv_acc
):
    tokens, pair = q_ref.shape
    features = ka_ref.shape[1]
    pairs = pl.num_programs(0)
    place = pl.program_id(0)
    blocks = tokens // BLOCK
    first = 2 * blocks + 3
    left = lax.broadcasted_iota(jnp.int32, (CHUNK, pair), 1) < pair // 2
    lane = lax.broadcasted_iota(jnp.int32, (CHUNK, features), 1)
    lane_pair = lax.broadcasted_iota(jnp.int32, (CHUNK, pair), 1)
    keys = jnp.concatenate([k_ref[...], ka_ref[...]], axis=1)
    turned = jnp.transpose(k_ref[...].astype(jnp.float32)).astype(LOW)
    ones = (lax.broadcasted_iota(jnp.int32, (tokens, pair), 1) < 3).astype(jnp.float32).astype(LOW)
    values = jnp.concatenate([v_ref[...], ones], axis=1)
    dk_acc[...] = jnp.zeros_like(dk_acc)
    dv_acc[...] = jnp.zeros_like(dv_acc)
    column = pl.multiple_of(place * 128, 128)

    def step(index, carry):
        rows = pl.ds(pl.multiple_of(index * CHUNK, CHUNK), CHUNK)
        queries = q_ref[rows, :] * 0.125
        grads = do_ref[rows, :]
        product = grads.astype(jnp.float32) * o_ref[rows, :].astype(jnp.float32)
        parts = []
        for head in range(2):
            mine = left if head == 0 else jnp.logical_not(left)
            level = lse_ref[rows, head * 64 : head * 64 + 1]
            inner = jnp.sum(jnp.where(mine, product, 0.0), axis=1, keepdims=True)
            side = qa_ref[head, rows, :].astype(jnp.float32)
            for spot, term in enumerate(three_terms(level)):
                side = jnp.where(lane == first + spot, -term, side)
            query_side = jnp.where(mine, queries, jnp.zeros_like(queries))
            grad_side = jnp.where(mine, grads, jnp.zeros_like(grads))
            tail = jnp.zeros((CHUNK, pair), jnp.float32)
            for spot, term in enumerate(three_terms(inner)):
                tail = jnp.where(lane_pair == spot, -term, tail)
            probs = jnp.exp(
                dot_rows(keys, jnp.concatenate([query_side, side.astype(LOW)], axis=1))
            )
            change = dot_rows(values, jnp.concatenate([grad_side, tail.astype(LOW)], axis=1))
            grad_scores = (probs * change).astype(LOW)
            dv_acc[...] += dot_plain(probs.astype(LOW), grad_side)
            dk_acc[...] += dot_plain(grad_scores, query_side)
            parts.append(dot_plain(turned, grad_scores))
        half = pair // 2
        joined = jnp.concatenate([parts[0][:half], parts[1][half:]], axis=0)
        grad_ref[rows, pl.ds(column, 128)] = (jnp.transpose(joined) * 0.125).astype(LOW)
        return carry

    lax.fori_loop(0, tokens // CHUNK, step, 0)
    key_column = pl.multiple_of((pairs + place) * 128, 128)
    value_column = pl.multiple_of((2 * pairs + place) * 128, 128)
    grad_ref[:, pl.ds(key_column, 128)] = dk_acc[...].astype(LOW)
    grad_ref[:, pl.ds(value_column, 128)] = dv_acc[...].astype(LOW)


def attend_back(projected, grad_attended, attended, levels, query_side, key_side):
    tokens, width = attended.shape
    pairs = width // 128
    features = key_side.shape[1]
    return pl.pallas_call(
        attend_back_kernel,
        grid=(pairs,),
        in_specs=[
            pl.BlockSpec((tokens, 128), lambda p: (0, p)),
            pl.BlockSpec((tokens, 128), lambda p: (0, pairs + p)),
            pl.BlockSpec((tokens, 128), lambda p: (0, 2 * pairs + p)),
            pl.BlockSpec((tokens, 128), lambda p: (0, p)),
            pl.BlockSpec((tokens, 128), lambda p: (0, p)),
            pl.BlockSpec((tokens, 128), lambda p: (0, p)),
            pl.BlockSpec((2, tokens, features), lambda p: (p, 0, 0)),
            pl.BlockSpec((tokens, features), lambda p: (0, 0)),
        ],
        out_specs=pl.BlockSpec((tokens, 3 * width), lambda p: (0, 0)),
        out_shape=jax.ShapeDtypeStruct((tokens, 3 * width), LOW),
        scratch_shapes=[
            pltpu.VMEM((tokens, 128), jnp.float32),
            pltpu.VMEM((tokens, 128), jnp.float32),
        ],
        compiler_params=pltpu.CompilerParams(vmem_limit_bytes=VMEM_BYTES),
        cost_estimate=pl.CostEstimate(
            flops=40 * pairs * tokens * tokens * 128,
            bytes_accessed=tokens * width * 24,
            transcendentals=2 * pairs * tokens * tokens,
        ),
    )(projected, projected, projected, grad_attended, attended, levels, query_side, key_side)


def swap(value):
    return lax.ppermute(value, SECTION, [(0, 1), (1, 0)])


def normalized(values_in):
    row_mean = jnp.mean(values_in, axis=-1, keepdims=True)
    centred = values_in - row_mean
    spread = jnp.mean(centred * centred, axis=-1, keepdims=True)
    scale = lax.rsqrt(spread + epsilon)
    return centred * scale, scale


class Shares:
    def __init__(self, width, columns, depth, vector_len):
        self.width = width
        self.columns = columns
        self.depth = depth
        self.vector_len = vector_len
        self.half = columns // 2
        self.per = width // columns
        self.groups = columns // depth

    def unpack(self, gathered, core):
        rows, down, vec = gathered
        vec = vec.reshape(-1, TAIL, self.width)[:, 0, : self.vector_len].reshape(-1)
        pieces = split_vectors(vec.astype(jnp.float32), self.width)
        for index in (2, 3):
            pieces[index] = lax.dynamic_index_in_dim(
                pieces[index].reshape(self.per, 2, self.half), core, 1, keepdims=False
            )
        pieces[8] = lax.dynamic_index_in_dim(
            pieces[8].reshape(-1, 2, self.depth // 2), core, 1, keepdims=False
        )
        return (
            (rows.reshape(-1, self.width), down.reshape(-1, self.width)),
            [piece.reshape(1, -1) for piece in pieces],
        )

    def by_shard(self, grads, vector_grads, core):
        proj, out, up, down = grads
        half, per, width = self.half, self.per, self.width
        hot = (jnp.arange(2) == core).astype(jnp.float32)
        spread = list(vector_grads)
        for index in (2, 3):
            spread[index] = (
                spread[index].reshape(per, 1, half) * hot[None, :, None]
            ).reshape(-1)
        spread[8] = (spread[8].reshape(-1, 1, self.depth // 2) * hot[None, :, None]).reshape(-1)
        for index in (0, 1, 4, 5, 6, 7):
            spread[index] = spread[index] * hot[0]
        vec = jnp.concatenate(spread).reshape(-1, 1, self.vector_len)
        vec = jnp.pad(vec, ((0, 0), (0, TAIL - 1), (0, width - self.vector_len))).astype(LOW)
        return (
            proj.reshape(-1, half, width),
            out.reshape(-1, half, width),
            up.reshape(2, 4, half, width),
            down.reshape(2, 2, 4, self.depth // 2, width),
            vec.reshape(2, 2, 4, TAIL, width),
        )


MESH = pl.DeviceIdType.MESH
PIECE = 48
TAIL = 16


def prepare_kernel(shares, rows_ref, down_ref, vector_ref, rows_out, down_out, vector_out):
    core = lax.axis_index(SECTION)
    offset = lax.axis_index((DP, SEQ)) * shares.columns
    half, per, width, depth = shares.half, shares.per, shares.width, shares.depth // 2
    is_inner = (offset >= 3 * width) & (offset < 4 * width)
    is_hidden = offset >= 4 * width

    @pl.when(is_inner)
    def _():
        for which in range(2):
            side = core if which == 0 else 1 - core
            held = [rows_ref[pl.ds((2 * j + side) * half, half), :] for j in range(per)]
            turned = jnp.transpose(jnp.concatenate(held, axis=0))
            rows_out[which] = jnp.concatenate([turned[:half], turned[half:]], axis=1).astype(LOW)

    @pl.when(jnp.logical_not(is_inner))
    def _():
        turned = jnp.transpose(rows_ref[...]).astype(LOW)
        plain = [turned[:half], turned[half:]]
        hidden = [
            jnp.concatenate(
                [turned[(2 * j + side) * depth :][:depth] for j in range(shares.groups)], axis=0
            )
            for side in range(2)
        ]
        halves = [jnp.where(is_hidden, b, a) for a, b in zip(plain, hidden)]
        rows_out[0] = jnp.where(core == 0, halves[0], halves[1])
        rows_out[1] = jnp.where(core == 0, halves[1], halves[0])

    down = down_ref[...].astype(LOW)
    down_out[0] = jnp.where(core == 0, down[:depth], down[depth:])
    down_out[1] = jnp.where(core == 0, down[depth:], down[:depth])
    vector_out[...] = jnp.zeros_like(vector_out)
    vector_out[0:1, : shares.vector_len] = vector_ref[...].astype(LOW)


def prepare(shares, rows, down, vector):
    return pl.pallas_call(
        partial(prepare_kernel, shares),
        out_shape=[
            jax.ShapeDtypeStruct((2, shares.half, shares.width), LOW),
            jax.ShapeDtypeStruct((2, shares.depth // 2, shares.width), LOW),
            jax.ShapeDtypeStruct((TAIL, shares.width), LOW),
        ],
        compiler_params=pltpu.CompilerParams(vmem_limit_bytes=VMEM_BYTES),
    )(rows, down, vector)


class Place:
    def __init__(self):
        self.core = lax.axis_index(SECTION)
        self.dp = lax.axis_index(DP)
        self.z = lax.axis_index(SEQ)
        self.y, self.x = self.dp // 2, self.dp % 2
        self.high, self.low = self.z // 2, self.z % 2
        self.inner = self.high + self.low == 1
        self.outer = self.high + self.low != 1
        self.partner = {SECTION: 1 - self.core}
        self.along_x = {DP: 2 * self.y + 1 - self.x}
        self.along_y = {DP: 2 * (1 - self.y) + self.x}
        self.across = {SEQ: 3 - self.z}
        self.beside = {SEQ: 2 * self.high + 1 - self.low}
        self.others = [{SEQ: (self.z + by) % 4} for by in (1, 2, 3)]
        self.own = pl.ds(self.z, 1)
        self.next = pl.ds(2 * self.high + 1 - self.low, 1)
        self.near = pl.ds(2 * self.high, 2)
        self.far = pl.ds(2 * (1 - self.high), 2)

    def greet(self):
        barrier = pltpu.get_barrier_semaphore()
        everyone = [self.partner, self.along_x, self.along_y] + self.others
        for device in everyone:
            pl.semaphore_signal(barrier, inc=1, device_id=device, device_id_type=MESH)
        pl.semaphore_wait(barrier, len(everyone))


def remote(src, dst, sems, spots, device):
    return pltpu.make_async_remote_copy(
        src_ref=src,
        dst_ref=dst,
        send_sem=sems[0].at[spots[0]],
        recv_sem=sems[1].at[spots[1]],
        device_id=device,
        device_id_type=MESH,
    )


def chunk_pairs(shares):
    pairs = []
    for array, length in ((0, shares.half), (1, shares.depth // 2)):
        for start in range(0, length, 2 * PIECE):
            pairs.append([(array, start, PIECE, 0), (array, start + PIECE, PIECE, 1)])
    pairs[0].append((2, 0, TAIL, 0))
    return pairs


def quad_pairs(shares):
    length = (shares.half + shares.depth // 2) // 2
    pairs = [
        [(0, start, PIECE, None), (1, start, PIECE, None)] for start in range(0, length, PIECE)
    ]
    pairs[0].append((2, 0, TAIL, 0))
    return pairs


def gather_kernel(shares, *refs):
    (rows_in, down_in, vector_in, x_in, cot_in), refs = refs[:5], refs[5:]
    outs, refs = [refs[0:3], refs[3:6]], refs[6:]
    (x_out, cot_out), refs = refs[:2], refs[2:]
    local, swap_send, swap_recv, z_send, z_recv, send, recv = refs
    here = Place()
    core, y, x, z = here.core, here.y, here.x, here.z
    half = x_in.shape[2] // 2
    rows_half, down_half = shares.half // 2, shares.depth // 4
    here.greet()

    def slices(source, target, base):
        mine = pl.ds(pl.multiple_of(core * half, half), half)
        sems = (z_send, z_recv)
        own = pltpu.make_async_copy(
            source.at[z, 0, mine], target.at[z, core], local.at[8 + base // 4]
        )
        sends, arrivals = [], []
        for by in (1, 2, 3):
            spots = (base + by - 1, base + by - 1)
            device = here.others[by - 1]
            sends.append(
                remote(source.at[(z + by) % 4, 0, mine], target.at[z, core], sems, spots, device)
            )
            arrivals.append(
                remote(
                    source.at[z, 0, mine], target.at[(z + 4 - by) % 4, core], sems, spots, device
                )
            )
        spots = (base + 3, base + 3)
        forward = remote(target.at[:, core], target.at[:, core], sems, spots, here.partner)
        arrived = remote(target.at[:, 1 - core], target.at[:, 1 - core], sems, spots, here.partner)
        return own, sends, arrivals, forward, arrived

    x_moves = slices(x_in, x_out, 0)
    cot_moves = slices(cot_in, cot_out, 4)

    def open_slices(moves):
        moves[0].start()
        for copy in moves[1]:
            copy.start()

    def pass_slices(moves):
        moves[0].wait()
        for copy in moves[2]:
            copy.wait_recv()
        moves[3].start()

    def close_slices(moves):
        for copy in moves[1]:
            copy.wait_send()
        moves[3].wait_send()
        moves[4].wait_recv()

    def first_moves(layer, which):
        down = down_in.at[which]
        rows = rows_in.at[which]
        if layer == 0:
            return [
                (0, rows, outs[0][0].at[y, x, z]),
                (1, down, outs[0][1].at[y, x, z]),
                (2, vector_in, outs[0][2].at[y, x, z]),
            ]
        moves = [(7, vector_in, outs[1][2].at[y, x, z])]
        for part in range(2):
            target = outs[1][part]
            moves.append(
                (
                    3 + 2 * part,
                    rows.at[pl.ds(part * rows_half, rows_half)],
                    target.at[z, pl.ds(0, rows_half)],
                )
            )
            moves.append(
                (
                    4 + 2 * part,
                    down.at[pl.ds(part * down_half, down_half)],
                    target.at[z, pl.ds(rows_half, down_half)],
                )
            )
        return moves

    swaps = (swap_send, swap_recv)
    for layer in range(2):

        @pl.when(core == layer)
        def _():
            across = [
                remote(src, dst, swaps, (spot, spot), here.partner)
                for spot, src, dst in first_moves(layer, 1)
            ]
            own = [
                pltpu.make_async_copy(src, dst, local.at[spot])
                for spot, src, dst in first_moves(layer, 0)
            ]
            for copy in across + own:
                copy.start()
            for copy in own:
                copy.wait()
            for copy in across:
                copy.wait_send()
            for spot, src, dst in first_moves(1 - layer, 0):
                remote(src, dst, swaps, (spot, spot), here.partner).wait_recv()

    numbers, pairs = {}, []
    for layer in range(2):
        for pair in chunk_pairs(shares) if layer == 0 else quad_pairs(shares):
            entry = []
            for array, start, length, order in pair:
                ref = outs[layer][array]
                rows = pl.ds(start, length)
                flat = order is None
                number = len(numbers)
                sems = (send, recv)

                def part(which):
                    return ref.at[which, rows] if flat else ref.at[y, x, which, rows]

                def copy(piece, spots, device):
                    return remote(piece, piece, sems, ((number, spots[0]), (number, spots[1])), device)

                steps = {
                    "z": copy(part(here.own), (0, 0), here.beside),
                    "across": copy(part(here.near), (1, 1), here.across),
                    "on": copy(part(here.far), (4, 1), here.beside),
                }
                arrive = [
                    copy(part(here.next), (0, 0), here.beside),
                    copy(part(here.far), (1, 1), here.across),
                ]
                if order == 0:
                    steps["one"] = copy(ref.at[y, x, :, rows], (2, 2), here.along_y)
                    steps["two"] = copy(ref.at[:, x, :, rows], (3, 3), here.along_x)
                    arrive.append(copy(ref.at[1 - y, x, :, rows], (2, 2), here.along_y))
                    arrive.append(copy(ref.at[:, 1 - x, :, rows], (3, 3), here.along_x))
                elif order == 1:
                    steps["one"] = copy(ref.at[y, x, :, rows], (2, 2), here.along_x)
                    steps["two"] = copy(ref.at[y, :, :, rows], (3, 3), here.along_y)
                    arrive.append(copy(ref.at[y, 1 - x, :, rows], (2, 2), here.along_x))
                    arrive.append(copy(ref.at[1 - y, :, :, rows], (3, 3), here.along_y))
                numbers[number] = (steps, arrive)
                entry.append(number)
            pairs.append(entry)

    def issue(name, entry):
        after = {"z": None, "across": 0, "on": 1, "one": 1, "two": 2}[name]

        def start():
            for number in entry:
                steps, arrive = numbers[number]
                if name in steps:
                    if after is not None and not (name == "one"):
                        arrive[after].wait_recv()
                    steps[name].start()

        if name in ("across", "on"):
            pl.when(here.inner)(start)
        else:
            start()

    def arrived(entry, index, where):
        def wait():
            for number in entry:
                numbers[number][1][index].wait_recv()

        pl.when(where)(wait)

    first, second = pairs[: len(chunk_pairs(shares))], pairs[len(chunk_pairs(shares)) :]
    for entry in first:
        issue("z", entry)
    for entry in first:
        issue("across", entry)
        arrived(entry, 0, here.outer)
    for index, entry in enumerate(first):
        issue("on", entry)
        arrived(entry, 1, here.outer)
        issue("one", entry)
        if index:
            issue("two", first[index - 1])
    open_slices(x_moves)
    for entry in second:
        issue("z", entry)
    for entry in second:
        issue("across", entry)
        arrived(entry, 0, here.outer)
    issue("two", first[-1])
    open_slices(cot_moves)
    for entry in second:
        issue("on", entry)
    pass_slices(x_moves)
    for entry in second:
        arrived(entry, 1, here.outer)
        for number in entry:
            steps, arrive = numbers[number]
            if "one" in steps:
                steps["one"].start()
                arrive[2].wait_recv()
                steps["two"].start()
    pass_slices(cot_moves)
    for steps, arrive in numbers.values():
        if len(arrive) == 4:
            arrive[3].wait_recv()
        for name in steps:
            if name not in ("across", "on"):
                steps[name].wait_send()

    @pl.when(here.inner)
    def _():
        for steps, _ in numbers.values():
            steps["across"].wait_send()
            steps["on"].wait_send()

    close_slices(x_moves)
    close_slices(cot_moves)


def gather(shares, prepared, block_input, cotangent):
    micro, _, tokens, width = block_input.shape
    chunks = sum(len(pair) for pair in chunk_pairs(shares) + quad_pairs(shares))
    lengths = (shares.half, shares.depth // 2, TAIL)
    layer = [jax.ShapeDtypeStruct((2, 2, 4, rows, width), LOW) for rows in lengths]
    quad = jax.ShapeDtypeStruct((4, (lengths[0] + lengths[1]) // 2, width), LOW)
    window = jax.ShapeDtypeStruct((micro, 2, tokens // 2, width), LOW)
    anywhere = pl.BlockSpec(memory_space=pl.ANY)
    results = pl.pallas_call(
        partial(gather_kernel, shares),
        in_specs=[anywhere] * 5,
        out_specs=[anywhere] * 8,
        out_shape=layer + [quad, quad, layer[2]] + [window, window],
        scratch_shapes=[
            pltpu.SemaphoreType.DMA((10,)),
            pltpu.SemaphoreType.DMA((8,)),
            pltpu.SemaphoreType.DMA((8,)),
            pltpu.SemaphoreType.DMA((8,)),
            pltpu.SemaphoreType.DMA((8,)),
            pltpu.SemaphoreType.DMA((chunks, 5)),
            pltpu.SemaphoreType.DMA((chunks, 4)),
        ],
        compiler_params=pltpu.CompilerParams(collective_id=0, has_side_effects=True),
    )(*prepared, block_input, cotangent)
    return results[0:3], results[3:6], results[6], results[7]


def over(value, bit):
    return lax.ppermute(value, DP, [(i, i ^ bit) for i in range(4)])


def layout_moves(shares, y, x, pieces, arrays):
    rows_half, down_half = shares.half // 2, shares.depth // 4
    down = arrays[-1]
    moves = []
    for part in range(2):
        rows = pl.ds(part * rows_half, rows_half)
        for index, (by_y, by_x) in enumerate(((0, 0), (1, 0), (0, 1), (1, 1))):
            piece = pieces[part][index]
            at_y, at_x = y ^ by_y, x ^ by_x
            top = pl.ds(0, rows_half)
            if len(arrays) == 2:
                moves.append((piece.at[:, top], arrays[0].at[at_y, at_x, :, rows]))
            else:
                proj, out, up, _ = arrays
                if at_y == 1:
                    moves.append((piece.at[:, top], up.at[at_x, :, rows]))
                elif at_x == 0:
                    moves.append((piece.at[:, top], proj.at[pl.ds(0, 4), rows]))
                else:
                    moves.append((piece.at[pl.ds(0, 2), top], proj.at[pl.ds(4, 2), rows]))
                    moves.append((piece.at[pl.ds(2, 2), top], out.at[:, rows]))
            moves.append(
                (
                    piece.at[:, pl.ds(rows_half, down_half)],
                    down.at[at_y, at_x, :, pl.ds(part * down_half, down_half)],
                )
            )
    return moves


def layout_kernel(shares, joins, *refs):
    dp = lax.axis_index(DP)
    if joins:
        pieces, arrays = [refs[0:4], refs[4:8]], refs[8:10]
    else:
        arrays, pieces = refs[0:4], [refs[4:8], refs[8:12]]
    for spot in range(4):

        @pl.when(dp == spot)
        def _():
            for piece, place in layout_moves(shares, spot // 2, spot % 2, pieces, arrays):
                src, dst = (piece, place) if joins else (place, piece)
                dst[...] = src[...]


def layout(shares, joins, *arrays):
    half, depth, width = shares.half, shares.depth // 2, shares.width
    if joins:
        shapes = [(2, 2, 4, half, width), (2, 2, 4, depth, width)]
    else:
        shapes = [(4, (half + depth) // 2, width)] * 8
    return pl.pallas_call(
        partial(layout_kernel, shares, joins),
        out_shape=[jax.ShapeDtypeStruct(shape, LOW) for shape in shapes],
        compiler_params=pltpu.CompilerParams(vmem_limit_bytes=VMEM_BYTES),
        cost_estimate=pl.CostEstimate(
            flops=0, bytes_accessed=64 * (half + depth) * width, transcendentals=0
        ),
    )(*arrays)


def tied(value, flying):
    return lax.optimization_barrier((value, flying))


def spread_quads(shares, quads):
    low, high = quads
    flying = (low, high, over(low, 2), over(high, 1))
    low, high, low_y, high_x = yield flying
    flying = (low_y, high_x, over(low, 1), over(high, 2))
    low_y, high_x, low_x, high_y = yield flying
    flying = (over(low_y, 1), over(high_x, 2))
    low_both, high_both = yield flying
    yield layout(shares, True, low, low_y, low_x, low_both, high, high_y, high_x, high_both)


def sum_quads(shares, arrays):
    pieces = layout(shares, False, *arrays)

    def total(*terms):
        return sum(term.astype(jnp.float32) for term in terms).astype(LOW)

    low, low_y, low_x, low_both = pieces[:4]
    high, high_y, high_x, high_both = pieces[4:]
    flying = (low_x, high_y, over(low_both, 1), over(high_both, 2))
    low_x, high_y, low_hop, high_hop = yield flying
    low_y, high_x = total(low_y, low_hop), total(high_x, high_hop)
    flying = (low_y, high_x, over(low_x, 1), over(high_y, 2))
    low_y, high_x, low_x, high_y = yield flying
    flying = (over(low_y, 2), over(high_x, 1))
    low_y, high_x = yield flying
    yield (total(low, low_x, low_y), total(high, high_x, high_y))


class Beside:
    def __init__(self, hops=None):
        self.hops = hops
        self.flying = None if hops is None else next(hops)

    def tie(self, value):
        if self.hops is None:
            return value
        value, arrived = tied(value, self.flying)
        self.flying = self.hops.send(arrived)
        return value


def scatter_kernel(shares, *refs):
    (proj, out, up, down, vec_zero, low, high, vec_one), refs = refs[:8], refs[8:]
    (dx_ref, final_ref, halves, slices), refs = refs[:4], refs[4:]
    work, refs = [refs[0:3], refs[3:6]], refs[6:]
    (got_one, got_two, got_far, got_across, got_near, total), refs = refs[:6], refs[6:]
    load, local, swap_send, swap_recv, z_send, z_recv, send, recv = refs
    here = Place()
    core, y, x, z = here.core, here.y, here.x, here.z
    rows_half, down_half = shares.half // 2, shares.depth // 4
    down_base = shares.half
    tail_base = shares.half + shares.depth // 2

    rows = work[0][0]
    moves = [
        [
            (proj.at[pl.ds(0, 4)], rows.at[0, 0]),
            (proj.at[pl.ds(4, 2)], rows.at[0, 1, pl.ds(0, 2)]),
            (out, rows.at[0, 1, pl.ds(2, 2)]),
            (up, rows.at[1]),
            (down, work[0][1]),
            (vec_zero, work[0][2]),
        ],
        [(low, work[1][0]), (high, work[1][1]), (vec_one, work[1][2])],
    ]
    loads = [
        [
            pltpu.make_async_copy(src, dst, load.at[layer, index])
            for index, (src, dst) in enumerate(moves[layer])
        ]
        for layer in range(2)
    ]
    for layer in (1, 0):
        for copy in loads[layer]:
            copy.start()
    here.greet()

    def place_of(layer, array, start):
        if array == 2:
            return tail_base
        if layer == 0:
            return (0, down_base)[array] + start
        if start < rows_half:
            return array * rows_half + start
        return down_base + array * down_half + start - rows_half

    pairs, chunks = [], []
    for layer in (1, 0):
        for index, pair in enumerate(quad_pairs(shares) if layer else chunk_pairs(shares)):
            entry = []
            for array, start, length, order in pair:
                entry.append((len(chunks), layer, array, start, length, order))
                chunks.append(entry[-1])
            pairs.append((index, entry))

    def pieces(chunk):
        number, layer, array, start, length, order = chunk
        ref = work[layer][array]
        rows = pl.ds(start, length)
        sems = (send, recv)
        keeps, slots, copies = [], [], []

        def part(which):
            return ref.at[which, rows] if order is None else ref.at[y, x, which, rows]

        def add(src, slot, device, keep):
            spots = (number, len(copies))
            copies.append(remote(src, slot, sems, (spots, spots), device))
            slots.append(slot)
            keeps.append(keep)

        room = pl.ds(0, length)
        if order == 0:
            add(ref.at[:, 1 - x, :, rows], got_one.at[number, :, :, room], here.along_x, ref.at[:, x, :, rows])
            add(ref.at[1 - y, x, :, rows], got_two.at[number, :, room], here.along_y, ref.at[y, x, :, rows])
        elif order == 1:
            add(ref.at[1 - y, :, :, rows], got_one.at[number, :, :, room], here.along_y, ref.at[y, :, :, rows])
            add(ref.at[y, 1 - x, :, rows], got_two.at[number, :, room], here.along_x, ref.at[y, x, :, rows])
        else:
            copies, slots, keeps = [None] * 2, [None] * 2, [None] * 2
        add(part(here.far), got_far.at[number, :, room], here.beside, part(here.far))
        add(part(here.far), got_across.at[number, :, room], here.across, part(here.near))
        add(part(here.next), got_near.at[number, :, room], here.beside, part(here.own))
        return copies, keeps, slots

    built = [pieces(chunk) for chunk in chunks]
    loaded = set()

    def land(number, phase):
        copies, keeps, slots = built[number]
        copies[phase].wait_recv()
        keep, slot = keeps[phase], slots[phase]
        keep[...] = keep[...] + slot[...]

    def run(chunk, phase):
        number, layer, array, start, length, order = chunk
        copies, keeps, slots = built[number]
        if (layer, array) not in loaded:
            loaded.add((layer, array))
            spots = ((0, 1, 2, 3), (4,), (5,))[array] if layer == 0 else (array,)
            for spot in spots:
                loads[layer][spot].wait()
        if phase < 2:
            if order is not None:
                if phase:
                    land(number, 0)
                copies[phase].start()
        elif phase == 2:
            if order is not None:
                land(number, 1)

            @pl.when(here.outer)
            def _():
                copies[2].start()
                copies[4].start()

        elif phase == 3:

            @pl.when(here.inner)
            def _():
                land(number, 2)
                copies[3].start()

        elif phase == 4:

            @pl.when(here.inner)
            def _():
                land(number, 3)
                copies[4].start()

        else:
            copies[4].wait_recv()
            spot = pl.ds(place_of(layer, array, start), length)
            total[layer, spot, :] = (keeps[4][...] + slots[4][...])[0]

    def step(entry, phase):
        for chunk in entry:
            run(chunk, phase)

    second = [entry for _, entry in pairs[: len(quad_pairs(shares))]]
    first = [entry for _, entry in pairs[len(quad_pairs(shares)) :]]
    tails = [chunk for entry in second for chunk in entry if chunk[5] is not None]
    second = [[chunk for chunk in entry if chunk[5] is None] for entry in second]
    first[0] = first[0] + tails
    step(first[0], 0)
    step(first[1], 0)
    for entry in second:
        step(entry, 2)
    step(first[0], 1)
    for section, source in ((0, dx_ref), (1, final_ref)):

        @pl.when(core == section)
        def _():
            pltpu.make_async_copy(source.at[z], slices.at[z], local.at[0]).start()
            for by in (1, 2, 3):
                remote(
                    source.at[(z + by) % 4],
                    slices.at[z],
                    (z_send, z_recv),
                    (by - 1, by - 1),
                    here.others[by - 1],
                ).start()

    for entry in second:
        step(entry, 3)
    step(first[2], 0)
    step(first[1], 1)
    for entry in second:
        step(entry, 4)
    step(first[0], 2)
    step(first[2], 1)
    for entry in second:
        step(entry, 5)
    step(first[0], 3)
    step(first[1], 2)
    step(first[0], 4)
    step(first[1], 3)
    step(first[2], 2)
    step(first[1], 4)
    step(first[2], 3)
    step(first[2], 4)
    for entry in first:
        step(entry, 5)

    for copies, _, _ in built:
        for index in (0, 1, 4):
            if copies[index] is not None:
                copies[index].wait_send()
    for section, index in ((here.outer, 2), (here.inner, 3)):

        @pl.when(section)
        def _():
            for copies, _, _ in built:
                copies[index].wait_send()

    swaps = (swap_send, swap_recv)
    across = remote(total.at[1 - core], halves.at[core], swaps, (0, 0), here.partner)
    across.start()
    own = pltpu.make_async_copy(total.at[core], halves.at[core], local.at[1])
    own.start()
    own.wait()
    across.wait_send()
    remote(total.at[1 - core], halves.at[1 - core], swaps, (0, 0), here.partner).wait_recv()
    pltpu.make_async_copy(dx_ref.at[z], slices.at[z], local.at[0]).wait()
    for by in (1, 2, 3):
        copy = remote(
            dx_ref.at[z],
            slices.at[(z + 4 - by) % 4],
            (z_send, z_recv),
            (by - 1, by - 1),
            here.others[by - 1],
        )
        copy.wait_send()
        copy.wait_recv()


def scatter(shares, arrays, vec_zero, quads, vec_one, grad, final):
    micro, tokens, width = grad.shape
    lengths = (shares.half, shares.depth // 2, TAIL)
    chunks = sum(len(pair) for pair in chunk_pairs(shares) + quad_pairs(shares))
    rows = sum(lengths)
    anywhere = pl.BlockSpec(memory_space=pl.ANY)
    work = [pltpu.VMEM((2, 2, 4, length, width), LOW) for length in lengths]
    quad = pltpu.VMEM((4, (lengths[0] + lengths[1]) // 2, width), LOW)
    return pl.pallas_call(
        partial(scatter_kernel, shares),
        in_specs=[anywhere] * 10,
        out_specs=[anywhere] * 2,
        out_shape=[
            jax.ShapeDtypeStruct((2, rows, width), LOW),
            jax.ShapeDtypeStruct((micro, tokens, width), LOW),
        ],
        scratch_shapes=work
        + [quad, quad, work[2]]
        + [
            pltpu.VMEM((chunks, 2, 4, PIECE, width), LOW),
            pltpu.VMEM((chunks, 4, PIECE, width), LOW),
            pltpu.VMEM((chunks, 2, PIECE, width), LOW),
            pltpu.VMEM((chunks, 2, PIECE, width), LOW),
            pltpu.VMEM((chunks, 1, PIECE, width), LOW),
            pltpu.VMEM((2, rows, width), LOW),
            pltpu.SemaphoreType.DMA((2, 6)),
            pltpu.SemaphoreType.DMA((2,)),
            pltpu.SemaphoreType.DMA((1,)),
            pltpu.SemaphoreType.DMA((1,)),
            pltpu.SemaphoreType.DMA((3,)),
            pltpu.SemaphoreType.DMA((3,)),
            pltpu.SemaphoreType.DMA((chunks, 5)),
            pltpu.SemaphoreType.DMA((chunks, 5)),
        ],
        compiler_params=pltpu.CompilerParams(
            collective_id=1, has_side_effects=True, vmem_limit_bytes=VMEM_BYTES
        ),
    )(*arrays, vec_zero, *quads, vec_one, grad, final)


def update_kernel(shares, halves_ref, *refs):
    old, new, turned = refs[:9], refs[9:18], refs[18]
    offset = lax.axis_index((DP, SEQ)) * shares.columns
    half, per, width, depth = shares.half, shares.per, shares.width, shares.depth // 2
    is_inner = (offset >= 3 * width) & (offset < 4 * width)
    is_hidden = offset >= 4 * width

    @pl.when(is_inner)
    def _():
        for side in range(2):
            piece = halves_ref[side, :half, :].astype(jnp.float32)
            wide = per * half
            back = jnp.transpose(jnp.concatenate([piece[:, :wide], piece[:, wide:]], axis=0))
            for j in range(per):
                turned[(2 * j + side) * half : (2 * j + side + 1) * half, :] = back[
                    j * half : (j + 1) * half
                ]

    @pl.when(jnp.logical_not(is_inner))
    def _():
        pair = [halves_ref[side, :half, :].astype(jnp.float32) for side in range(2)]
        plain = jnp.concatenate(pair, axis=0)
        hidden = jnp.concatenate(
            [pair[side][j * depth :][:depth] for j in range(shares.groups) for side in range(2)],
            axis=0,
        )
        turned[...] = jnp.transpose(jnp.where(is_hidden, hidden, plain))

    def store(first, gradient, rate, decay):
        results = adam_update(*[ref[...] for ref in old[first : first + 3]], gradient, rate, decay)
        for ref, result in zip(new[first : first + 3], results):
            ref[...] = result

    store(0, turned[...], rate_matrix, decay_matrix)
    down = [halves_ref[side, half : half + depth, :] for side in range(2)]
    store(3, jnp.concatenate(down, axis=0).astype(jnp.float32), rate_matrix, decay_matrix)
    tails = [halves_ref[side, half + depth :, :].astype(jnp.float32) for side in range(2)]
    store(6, (tails[0] + tails[1])[0:1, : shares.vector_len], rate_vector, 0.0)


def update(shares, halves, old):
    return pl.pallas_call(
        partial(update_kernel, shares),
        out_shape=[jax.ShapeDtypeStruct(piece.shape, jnp.float32) for piece in old],
        scratch_shapes=[pltpu.VMEM((shares.width, shares.columns), jnp.float32)],
        compiler_params=pltpu.CompilerParams(vmem_limit_bytes=VMEM_BYTES),
    )(halves, *old)


ROWS = 256
COLS = 384


def whole(shape):
    return pl.BlockSpec(shape, lambda i: (0,) * len(shape))


def row_block(width):
    return pl.BlockSpec((ROWS, width), lambda i: (i, 0))


def col_block(tokens):
    return pl.BlockSpec((tokens, COLS), lambda i: (0, i))


def weight_block(width, first=0):
    return pl.BlockSpec((COLS, width), lambda i: (first + i, 0))


def params_of(flops, moved, transcendentals=0):
    return {
        "compiler_params": pltpu.CompilerParams(vmem_limit_bytes=VMEM_BYTES),
        "cost_estimate": pl.CostEstimate(
            flops=flops, bytes_accessed=moved, transcendentals=transcendentals
        ),
    }


def by_rows(tokens, body):
    def step(index, carry):
        body(pl.ds(pl.multiple_of(index * ROWS, ROWS), ROWS))
        return carry

    lax.fori_loop(0, tokens // ROWS, step, 0)


def features_kernel(shares, random_ref, segment_ref, global_ref, query_ref, key_ref):
    core = lax.axis_index(SECTION)
    place = lax.axis_index(SEQ)
    blocks = random_ref.shape[1]
    width = key_ref.shape[1]
    heads = query_ref.shape[0]
    per_half = heads // shares.per
    picks = random_ref.shape[2] // (2 * heads)
    tokens = key_ref.shape[0]
    lane = lax.broadcasted_iota(jnp.int32, (blocks, width), 1)
    row = lax.broadcasted_iota(jnp.int32, (blocks, width), 0)
    key = jnp.where(lane < blocks, lane, lane - blocks)
    chosen = random_ref[place]
    named = global_ref[place]
    always = (jnp.abs(row - key) <= 1).astype(jnp.int32)
    is_global = jnp.zeros((blocks, width), jnp.int32)
    for index in range(named.shape[1]):
        spot = named[:, index : index + 1]
        always = always + (key == spot).astype(jnp.int32)
        is_global = is_global + (row == spot).astype(jnp.int32)
    line = segment_ref[place].astype(jnp.float32)
    column = jnp.transpose(jnp.broadcast_to(line, (8, tokens)))[:, 0:1]
    token_lane = lax.broadcasted_iota(jnp.int32, (tokens, width), 1)
    same = column == (token_lane - 2 * blocks).astype(jnp.float32)
    in_segment = (token_lane >= 2 * blocks) & (token_lane < 2 * blocks + 3)
    segment_side = jnp.where(in_segment & same, 1.0, 0.0)
    for head in range(heads):
        count = always
        for pick in range(picks):
            at = [
                (2 * per_half * (head // per_half) + per_half * side + head % per_half) * picks
                + pick
                for side in range(2)
            ]
            spot = jnp.where(core == 0, chosen[:, at[0] : at[0] + 1], chosen[:, at[1] : at[1] + 1])
            count = count + (key == spot).astype(jnp.int32)
        count = jnp.where(is_global > 0, 1, count)
        high = jnp.where(count == 0, masked, 0.0)
        low = jnp.zeros_like(high)
        for times in (2, 3):
            high = jnp.where(count == times, LOG_HIGH[times - 1], high)
            low = jnp.where(count == times, LOG_LOW[times - 1], low)
        table = jnp.where(lane < blocks, high, jnp.where(lane < 2 * blocks, low, 0.0))
        for block in range(blocks):
            rows = slice(block * BLOCK, (block + 1) * BLOCK)
            query_ref[head, rows, :] = (table[block : block + 1] + segment_side[rows]).astype(LOW)
    token_block = lax.shift_right_logical(
        lax.broadcasted_iota(jnp.int32, (tokens, width), 0), BLOCK.bit_length() - 1
    )
    here = (token_block == token_lane) | (token_block == token_lane - blocks)
    side = jnp.where(here & (token_lane < 2 * blocks), 1.0, 0.0)
    side = jnp.where(in_segment & jnp.logical_not(same), masked, side)
    ones = (token_lane >= 2 * blocks + 3) & (token_lane < 2 * blocks + 6)
    key_ref[...] = jnp.where(ones, 1.0, side).astype(LOW)


def key_features(shares, random_ids, segment_ids, global_ids):
    micro, _, blocks, head_count, picks = random_ids.shape
    tokens = segment_ids.shape[2]
    width = -(-(2 * blocks + 6) // 128) * 128
    return pl.pallas_call(
        partial(features_kernel, shares),
        out_shape=[
            jax.ShapeDtypeStruct((head_count // 2, tokens, width), LOW),
            jax.ShapeDtypeStruct((tokens, width), LOW),
        ],
        **params_of(0, head_count * tokens * width),
    )(random_ids.reshape(micro, blocks, head_count * picks), segment_ids, global_ids)


def project_kernel(joins, *refs):
    if joins:
        (middle_ref, part_ref, recv_ref, bias_down_ref), refs = refs[:4], refs[4:]
    else:
        hidden_ref, refs = refs[0], refs[1:]
    (gain_ref, shift_ref, weight_ref, bias_ref), refs = refs[:4], refs[4:]
    if joins:
        hidden_ref, refs = refs[0], refs[1:]
    normed_ref, out_ref = refs
    tokens = normed_ref.shape[0]

    @pl.when(pl.program_id(0) == 0)
    def _():
        def body(rows):
            if joins:
                part = part_ref[rows, :] + recv_ref[rows, :].astype(jnp.float32)
                hidden_ref[rows, :] = (middle_ref[rows, :] + part + bias_down_ref[...]).astype(LOW)
            unit, _ = normalized(hidden_ref[rows, :].astype(jnp.float32))
            normed_ref[rows, :] = (unit * gain_ref[...] + shift_ref[...]).astype(LOW)

        by_rows(tokens, body)

    def body(rows):
        product = dot_rows(normed_ref[rows, :], weight_ref[...])
        out_ref[rows, :] = (product + bias_ref[...]).astype(LOW)

    by_rows(tokens, body)


def project(before, gain, shift, rows, bias):
    joins = len(before) > 1
    tokens, width = before[0].shape
    out_width = bias.shape[1]
    big = whole((tokens, width))
    small = whole((1, width))
    ins = [big] * 3 + [small] if joins else [big]
    outs = [big] * (2 if joins else 1)
    low = jax.ShapeDtypeStruct((tokens, width), LOW)
    return pl.pallas_call(
        partial(project_kernel, joins),
        grid=(out_width // COLS,),
        in_specs=ins
        + [small, small, weight_block(width), pl.BlockSpec((1, COLS), lambda i: (0, i))],
        out_specs=outs + [col_block(tokens)],
        out_shape=[low] * len(outs) + [jax.ShapeDtypeStruct((tokens, out_width), LOW)],
        **params_of(2 * tokens * width * out_width, tokens * width * 16),
    )(*before, gain, shift, rows, bias)


def gelu_parts(value):
    size = jnp.abs(value)
    t = 1.0 / (1.0 + (0.3275911 * 0.5**0.5) * size)
    bell = jnp.exp(-0.5 * value * value)
    poly = 1.061405429
    for coefficient in (-1.453152027, 1.421413741, -0.284496736, 0.254829592):
        poly = poly * t + coefficient
    tail = 0.5 * poly * t * bell
    cdf = jnp.where(value > 0, 1.0 - tail, tail)
    return value * cdf, cdf + value * bell * (0.5 / math.pi) ** 0.5


def expand_kernel(
    hidden_ref,
    branch_ref,
    recv_ref,
    bias_out_ref,
    gain_ref,
    shift_ref,
    up_ref,
    down_ref,
    bias_up_ref,
    middle_ref,
    normed_ref,
    slope_ref,
    active_ref,
    part_ref,
    low_ref,
):
    tokens = middle_ref.shape[0]
    step = pl.program_id(0)

    @pl.when(step == 0)
    def _():
        def body(rows):
            branch = branch_ref[rows, :] + recv_ref[rows, :].astype(jnp.float32)
            middle = hidden_ref[rows, :].astype(jnp.float32) + (branch + bias_out_ref[...])
            middle_ref[rows, :] = middle
            unit, _ = normalized(middle)
            normed_ref[rows, :] = (unit * gain_ref[...] + shift_ref[...]).astype(LOW)
            part_ref[rows, :] = jnp.zeros_like(middle)

        by_rows(tokens, body)

    def body(rows):
        value = dot_rows(normed_ref[rows, :], up_ref[...]) + bias_up_ref[...]
        active, slope = gelu_parts(value)
        active = active.astype(LOW)
        active_ref[rows, :] = active
        slope_ref[rows, :] = slope
        part_ref[rows, :] += dot_plain(active, down_ref[...])

    by_rows(tokens, body)

    @pl.when(step == pl.num_programs(0) - 1)
    def _():
        low_ref[...] = part_ref[...].astype(LOW)


def expand(hidden, branch, recv, bias_out, gain, shift, rows, first, down, bias_up):
    tokens, width = hidden.shape
    inner = down.shape[0]
    big, small = whole((tokens, width)), whole((1, width))
    return pl.pallas_call(
        expand_kernel,
        grid=(inner // COLS,),
        in_specs=[big, big, big, small, small, small]
        + [weight_block(width, first), weight_block(width)]
        + [pl.BlockSpec((1, COLS), lambda i: (0, i))],
        out_specs=[big, big, col_block(tokens), col_block(tokens), big, big],
        out_shape=[
            jax.ShapeDtypeStruct((tokens, width), jnp.float32),
            jax.ShapeDtypeStruct((tokens, width), LOW),
            jax.ShapeDtypeStruct((tokens, inner), jnp.float32),
            jax.ShapeDtypeStruct((tokens, inner), LOW),
            jax.ShapeDtypeStruct((tokens, width), jnp.float32),
            jax.ShapeDtypeStruct((tokens, width), LOW),
        ],
        **params_of(4 * tokens * width * inner, tokens * width * 32, tokens * inner),
    )(hidden, branch, recv, bias_out, gain, shift, rows, down, bias_up)


def expand_back_kernel(
    grad_ref,
    slope_ref,
    active_ref,
    normed_ref,
    up_ref,
    down_ref,
    part_ref,
    low_ref,
    up_grad_ref,
    down_grad_ref,
    bias_up_ref,
    bias_down_ref,
    held,
):
    tokens = grad_ref.shape[0]
    step = pl.program_id(0)

    @pl.when(step == 0)
    def _():
        part_ref[...] = jnp.zeros_like(part_ref)
        bias_down_ref[...] = jnp.sum(grad_ref[...].astype(jnp.float32), axis=0, keepdims=True)

    bias_up_ref[...] = jnp.zeros_like(bias_up_ref)

    def body(rows):
        grad_active = dot_rows(grad_ref[rows, :], down_ref[...])
        grad_up = (grad_active * slope_ref[rows, :]).astype(LOW)
        held[rows, :] = grad_up
        bias_up_ref[...] += jnp.sum(grad_up.astype(jnp.float32), axis=0, keepdims=True)
        part_ref[rows, :] += dot_plain(grad_up, up_ref[...])

    by_rows(tokens, body)
    for first in range(0, COLS, 128):
        cols = slice(first, first + 128)
        down_grad_ref[cols, :] = dot_tokens(active_ref[:, cols], grad_ref[...]).astype(LOW)
        up_grad_ref[cols, :] = dot_tokens(held[:, cols], normed_ref[...]).astype(LOW)

    @pl.when(step == pl.num_programs(0) - 1)
    def _():
        low_ref[...] = part_ref[...].astype(LOW)


def expand_back(grad, slope, active, normed, rows, first, down):
    tokens, width = grad.shape
    inner = down.shape[0]
    big = whole((tokens, width))
    return pl.pallas_call(
        expand_back_kernel,
        grid=(inner // COLS,),
        in_specs=[big, col_block(tokens), col_block(tokens), big]
        + [weight_block(width, first), weight_block(width)],
        out_specs=[big, big, weight_block(width), weight_block(width)]
        + [pl.BlockSpec((1, COLS), lambda i: (0, i)), whole((1, width))],
        out_shape=[
            jax.ShapeDtypeStruct((tokens, width), jnp.float32),
            jax.ShapeDtypeStruct((tokens, width), LOW),
            jax.ShapeDtypeStruct((inner, width), LOW),
            jax.ShapeDtypeStruct((inner, width), LOW),
            jax.ShapeDtypeStruct((1, inner), jnp.float32),
            jax.ShapeDtypeStruct((1, width), jnp.float32),
        ],
        scratch_shapes=[pltpu.VMEM((tokens, COLS), LOW)],
        **params_of(8 * tokens * width * inner, tokens * width * 32),
    )(grad, slope, active, normed, rows, down)


def out_halves(packed, half):
    wide = packed.shape[1] // 2
    return [
        jnp.concatenate([piece[:, :wide], piece[:, wide:]], axis=0)
        for piece in (packed[:half], packed[half:])
    ]


def norm_back_rows(values_in, incoming, gain_vec):
    unit, scale = normalized(values_in)
    p = incoming * gain_vec
    mean_p = jnp.mean(p, axis=-1, keepdims=True)
    mean_pn = jnp.mean(p * unit, axis=-1, keepdims=True)
    grad_gain = jnp.sum(incoming * unit, axis=0, keepdims=True)
    grad_shift = jnp.sum(incoming, axis=0, keepdims=True)
    return scale * (p - mean_p - unit * mean_pn), grad_gain, grad_shift


def branch_back_kernel(
    half,
    middle_ref,
    part_ref,
    recv_ref,
    grad_ref,
    attended_ref,
    gain_ref,
    packed_ref,
    grad_middle_ref,
    grad_attended_ref,
    out_grad_ref,
    gain_grad_ref,
    shift_grad_ref,
    bias_grad_ref,
    total,
):
    step = pl.program_id(0)

    @pl.when(step == 0)
    def _():
        total[...] = jnp.zeros_like(total)
        for ref in (gain_grad_ref, shift_grad_ref, bias_grad_ref):
            ref[...] = jnp.zeros_like(ref)

    incoming = part_ref[...] + recv_ref[...].astype(jnp.float32)
    change, grad_gain, grad_shift = norm_back_rows(middle_ref[...], incoming, gain_ref[...])
    grad_middle = grad_ref[...].astype(jnp.float32) + change
    grad_middle_ref[...] = grad_middle
    low = grad_middle.astype(LOW)
    gain_grad_ref[...] += grad_gain
    shift_grad_ref[...] += grad_shift
    bias_grad_ref[...] += jnp.sum(low.astype(jnp.float32), axis=0, keepdims=True)
    weights = out_halves(packed_ref[...], half)
    wide = weights[0].shape[0]
    attended = attended_ref[...]
    pieces = [low[:, :wide], low[:, wide:]]
    grad_attended_ref[...] = (
        dot_plain(pieces[0], weights[0]) + dot_plain(pieces[1], weights[1])
    ).astype(LOW)
    for index in range(2):
        total[index] += dot_tokens(pieces[index], attended)

    @pl.when(step == pl.num_programs(0) - 1)
    def _():
        for index in range(2):
            joined = jnp.concatenate([total[index, :half, :], total[index, half:, :]], axis=1)
            out_grad_ref[index * half : (index + 1) * half, :] = joined.astype(LOW)


def branch_back(shares, middle, part, recv, grad, attended, gain, rows):
    tokens, width = middle.shape
    wide = attended.shape[1]
    small = whole((1, width))
    one = jax.ShapeDtypeStruct((1, width), jnp.float32)
    return pl.pallas_call(
        partial(branch_back_kernel, shares.half),
        grid=(tokens // ROWS,),
        in_specs=[row_block(width)] * 4
        + [row_block(wide), small, pl.BlockSpec((COLS, width), lambda i: (3, 0))],
        out_specs=[row_block(width), row_block(wide), whole((COLS, width)), small, small, small],
        out_shape=[
            jax.ShapeDtypeStruct((tokens, width), jnp.float32),
            jax.ShapeDtypeStruct((tokens, wide), LOW),
            jax.ShapeDtypeStruct((COLS, width), LOW),
            one,
            one,
            one,
        ],
        scratch_shapes=[pltpu.VMEM((2, width // 2, wide), jnp.float32)],
        **params_of(4 * tokens * width * wide, tokens * width * 20),
    )(middle, part, recv, grad, attended, gain, rows)


def project_back_kernel(
    grad_ref, normed_ref, weight_ref, part_ref, low_ref, weight_grad_ref, bias_ref
):
    tokens = grad_ref.shape[0]
    step = pl.program_id(0)

    @pl.when(step == 0)
    def _():
        part_ref[...] = jnp.zeros_like(part_ref)

    bias_ref[...] = jnp.zeros_like(bias_ref)

    def body(rows):
        grad = grad_ref[rows, :]
        bias_ref[...] += jnp.sum(grad.astype(jnp.float32), axis=0, keepdims=True)
        part_ref[rows, :] += dot_plain(grad, weight_ref[...])

    by_rows(tokens, body)
    for first in range(0, COLS, 128):
        cols = slice(first, first + 128)
        weight_grad_ref[cols, :] = dot_tokens(grad_ref[:, cols], normed_ref[...]).astype(LOW)

    @pl.when(step == pl.num_programs(0) - 1)
    def _():
        low_ref[...] = part_ref[...].astype(LOW)


def project_back(grad_proj, normed, rows):
    tokens, width = normed.shape
    out_width = grad_proj.shape[1]
    big = whole((tokens, width))
    return pl.pallas_call(
        project_back_kernel,
        grid=(out_width // COLS,),
        in_specs=[col_block(tokens), big, weight_block(width)],
        out_specs=[big, big, weight_block(width), pl.BlockSpec((1, COLS), lambda i: (0, i))],
        out_shape=[
            jax.ShapeDtypeStruct((tokens, width), jnp.float32),
            jax.ShapeDtypeStruct((tokens, width), LOW),
            jax.ShapeDtypeStruct((out_width, width), LOW),
            jax.ShapeDtypeStruct((1, out_width), jnp.float32),
        ],
        **params_of(4 * tokens * width * out_width, tokens * width * 16),
    )(grad_proj, normed, rows)


def input_back_kernel(
    hidden_ref, part_ref, recv_ref, grad_ref, gain_ref, out_ref, gain_grad_ref, shift_grad_ref
):
    @pl.when(pl.program_id(0) == 0)
    def _():
        gain_grad_ref[...] = jnp.zeros_like(gain_grad_ref)
        shift_grad_ref[...] = jnp.zeros_like(shift_grad_ref)

    incoming = part_ref[...] + recv_ref[...].astype(jnp.float32)
    hidden = hidden_ref[...].astype(jnp.float32)
    change, grad_gain, grad_shift = norm_back_rows(hidden, incoming, gain_ref[...])
    out_ref[...] = (grad_ref[...] + change).astype(LOW)
    gain_grad_ref[...] += grad_gain
    shift_grad_ref[...] += grad_shift


def input_back(hidden, part, recv, grad_middle, gain):
    tokens, width = hidden.shape
    small = whole((1, width))
    one = jax.ShapeDtypeStruct((1, width), jnp.float32)
    return pl.pallas_call(
        input_back_kernel,
        grid=(tokens // ROWS,),
        in_specs=[row_block(width)] * 4 + [small],
        out_specs=[row_block(width), small, small],
        out_shape=[jax.ShapeDtypeStruct((tokens, width), LOW), one, one],
        **params_of(0, tokens * width * 12),
    )(hidden, part, recv, grad_middle, gain)


def window_forward(shares, before, weights, biases, features, beside):
    rows, down = weights
    gain_one, shift_one, bias_query, bias_value, bias_out = biases[:5]
    gain_two, shift_two, _, bias_up = biases[5:]
    bias = jnp.concatenate([bias_query, jnp.zeros_like(bias_query), bias_value], axis=1)
    results = project(before, gain_one, shift_one, rows, bias)
    hidden = before[0] if len(before) == 1 else results[0]
    normed, projected = results[-2:]
    projected = beside.tie(projected)
    attended, levels, branch, low = attend(projected, *features, rows, shares.half)
    attended, levels, branch, low = beside.tie((attended, levels, branch, low))
    expanded = expand(
        hidden, branch, swap(low), bias_out, gain_two, shift_two, rows, 4, down, bias_up
    )
    middle, normed_two, slope, active, part, low = beside.tie(tuple(expanded))
    stored = (hidden, normed, projected, attended, levels, middle, normed_two, slope, active)
    return (middle, part, swap(low), biases[7]), stored


def window_backward(shares, stored, grad, weights, biases, features, beside):
    hidden, normed, projected, attended, levels, middle, normed_two, slope, active = stored
    rows, down = weights
    part, low, up_grad, down_grad, bias_up, bias_down = beside.tie(
        tuple(expand_back(grad, slope, active, normed_two, rows, 4, down))
    )
    grad_middle, grad_attended, out_grad, gain_two, shift_two, bias_out = branch_back(
        shares, middle, part, swap(low), grad, attended, biases[5], rows
    )
    grad_attended = beside.tie(grad_attended)
    grad_proj = attend_back(projected, grad_attended, attended, levels, *features)
    grad_proj = beside.tie(grad_proj)
    part, low, proj_grad, summed = project_back(grad_proj, normed, rows)
    grad, gain_one, shift_one = input_back(hidden, part, swap(low), grad_middle, biases[0])
    width = attended.shape[1]
    vector_grads = (gain_one, shift_one, summed[:, :width], summed[:, 2 * width :], bias_out)
    vector_grads += (gain_two, shift_two, bias_down, bias_up)
    vector_grads = [piece[0] for piece in vector_grads]
    return grad, (proj_grad, out_grad, up_grad, down_grad), vector_grads


def window_shards(
    block_input,
    cotangent,
    random_ids,
    segment_ids,
    global_ids,
    w_rows,
    w_rows_first,
    w_rows_second,
    w_down,
    w_down_first,
    w_down_second,
    vectors,
    vectors_first,
    vectors_second,
):
    core = lax.axis_index(SECTION)
    micro, _, tokens, width = block_input.shape
    _, _, columns = w_rows.shape
    shares = Shares(width, columns, w_down.shape[1], vectors.shape[1])
    prepared = prepare(shares, w_rows[0], w_down[0], vectors)
    features = key_features(shares, random_ids, segment_ids, global_ids)
    gathered_zero, gathered_one, hidden, grad = gather(shares, prepared, block_input, cotangent)

    beside = Beside(spread_quads(shares, gathered_one[:2]))
    params = [shares.unpack(gathered_zero, core)]
    before = (hidden.reshape(-1, width),)
    before, stored_zero = window_forward(shares, before, *params[0], features, beside)
    params.append(shares.unpack((*beside.flying, gathered_one[2]), core))
    after, stored_one = window_forward(shares, before, *params[1], features, Beside())
    final = (after[0] + (after[1] + after[2].astype(jnp.float32) + after[3])).astype(LOW)

    grad = grad.reshape(-1, width)
    grad, *grads_one = window_backward(shares, stored_one, grad, *params[1], features, Beside())
    *arrays_one, vec_one = shares.by_shard(*grads_one, core)
    beside = Beside(sum_quads(shares, arrays_one))
    grad, *grads_zero = window_backward(shares, stored_zero, grad, *params[0], features, beside)
    *arrays_zero, vec_zero = shares.by_shard(*grads_zero, core)
    grad, final = [piece.reshape(micro, tokens, width) for piece in (grad, final)]
    halves, slices = scatter(shares, arrays_zero, vec_zero, beside.flying, vec_one, grad, final)
    section_result = slices.astype(jnp.float32)[None, :, None]
    old = [
        w_rows[0],
        w_rows_first[0],
        w_rows_second[0],
        w_down[0],
        w_down_first[0],
        w_down_second[0],
        vectors,
        vectors_first,
        vectors_second,
    ]
    new = update(shares, halves, old)
    return (section_result, *[piece[None] for piece in new[:6]], *new[6:])


def one_window_each(mesh, block_input, w_rows, w_down, vectors):
    micro, windows, length, width = block_input.shape
    shards = mesh.shape[DP] * mesh.shape[SEQ]
    columns, depth = w_rows.shape[2] // shards, w_down.shape[1] // shards
    head_dim = width // HEADS
    tokens = length // mesh.shape[SEQ]
    return (
        mesh.shape[SECTION] == 2
        and mesh.shape[SEQ] == micro
        and mesh.shape[DP] == windows
        and tokens % (2 * BLOCK) == 0
        and length % CHUNK == 0
        and head_dim == 64
        and width % columns == 0
        and columns % (2 * head_dim) == 0
        and columns % depth == 0
        and width // columns * (columns // 2) % 128 == 0
        and depth % 32 == 0
        and vectors.shape[1] // shards <= width
        and mesh.shape[DP] == 4
        and micro == 4
        and width == 2 * columns == 2 * COLS
        and w_down.shape[1] == 4 * width
        and (columns // 2) % (2 * PIECE) == 0
        and (depth // 2) % (2 * PIECE) == 0
        and length % (4 * ROWS) == 0
    )


def solution(mesh):
    in_specs = (
        P(None, DP, SEQ, None),
        P(None, DP, SEQ, None),
        P(None, DP, None, None, None),
        P(None, DP, None),
        P(None, DP, None),
        P(SECTION, None, (DP, SEQ)),
        P(SECTION, None, (DP, SEQ)),
        P(SECTION, None, (DP, SEQ)),
        P(SECTION, (DP, SEQ), None),
        P(SECTION, (DP, SEQ), None),
        P(SECTION, (DP, SEQ), None),
        P(SECTION, (DP, SEQ)),
        P(SECTION, (DP, SEQ)),
        P(SECTION, (DP, SEQ)),
    )
    out_specs = (
        P(SECTION, None, DP, SEQ, None),
        P(SECTION, None, (DP, SEQ)),
        P(SECTION, None, (DP, SEQ)),
        P(SECTION, None, (DP, SEQ)),
        P(SECTION, (DP, SEQ), None),
        P(SECTION, (DP, SEQ), None),
        P(SECTION, (DP, SEQ), None),
        P(SECTION, (DP, SEQ)),
        P(SECTION, (DP, SEQ)),
        P(SECTION, (DP, SEQ)),
    )

    def step(*arrays):
        chosen = general_shards
        if one_window_each(mesh, arrays[0], arrays[5], arrays[8], arrays[11]):
            chosen = window_shards
        return jax.shard_map(
            chosen, mesh=mesh, in_specs=in_specs, out_specs=out_specs, check_vma=False
        )(*arrays)

    return step
```

```python
import math
from functools import partial

import jax
import jax.numpy as jnp
import ml_dtypes
import numpy as np
from jax import lax
from jax.experimental import pallas as pl
from jax.experimental.pallas import tpu as pltpu
from jax.sharding import PartitionSpec as P

SECTION, DP, SEQ = "section", "dp", "seq"
HEADS = 12
BLOCK = 64
STEP = 5


epsilon = 1e-05
masked = -1e30
rate_matrix = 0.02
rate_vector = 0.2
decay_matrix = 0.01


def with_halo(x, sides, width):
    for axis, dim in sides:
        devices, length = (lax.axis_size(axis), x.shape[dim])
        up = [(i, (i + 1) % devices) for i in range(devices - 1)]
        down = [(j, i) for i, j in up]
        last = lax.slice_in_dim(x, length - width, length, axis=dim)
        initial = lax.slice_in_dim(x, 0, width, axis=dim)
        before = lax.ppermute(last, axis, up)
        after = lax.ppermute(initial, axis, down)
        x = jnp.concatenate([before, x, after], axis=dim)
    return x


def merged(value, axis, join):
    pieces = jax.tree.map(lambda part: lax.all_gather(part, axis), value)
    head = jax.tree.map(lambda part: part[0], pieces)
    tail = jax.tree.map(lambda part: part[1:], pieces)
    subtotal, _ = lax.scan(lambda subtotal, share: (join(subtotal, share), None), head, tail)
    return subtotal


def from_behind(x, axis, by):
    devices = lax.axis_size(axis)
    pairs = [(i, i + by) for i in range(devices) if 0 <= i + by < devices]
    return lax.ppermute(x, axis, pairs)


def partner(value, axis, bit):
    mask = 2**bit
    pairs = [(source, source ^ mask) for source in range(lax.axis_size(axis))]
    return lax.ppermute(value, axis, pairs)


def mixed_sum(form, left, right):
    return jnp.einsum(form, left, right, preferred_element_type=jnp.float32)


def exact_two(form, left, right):
    return jnp.einsum(
        form, left, right, precision=lax.Precision.HIGHEST, preferred_element_type=jnp.float32
    )


def norm_rows(values_in, gain_vec, shift_vec):
    row_mean = jnp.mean(values_in, axis=-1, keepdims=True)
    centred = values_in - row_mean
    spread = jnp.mean(centred * centred, axis=-1, keepdims=True)
    return centred * lax.rsqrt(spread + epsilon) * gain_vec + shift_vec


def split_vectors(vector_weights, model_width):
    pieces = [
        vector_weights[piece_index * model_width : (piece_index + 1) * model_width]
        for piece_index in range(8)
    ]
    return pieces + [vector_weights[8 * model_width :]]


def route_tables(random_rows, segments, global_rows, seq_place, groups):
    windows, blocks, head_count, pick_count = random_rows.shape
    blocks_dev = blocks // groups
    request_count = blocks_dev * head_count * pick_count
    capacity = -(-request_count // groups)
    requests = random_rows.reshape(windows, groups, request_count)
    owners = requests // blocks_dev
    inside = requests % blocks_dev
    head_of = jnp.arange(request_count) // pick_count % head_count
    is_mine = owners == seq_place
    slot_index = jnp.cumsum(is_mine.astype(jnp.int32), axis=2) - 1
    slot_hot = ((slot_index[..., None] == jnp.arange(capacity)) & is_mine[..., None]).astype(
        jnp.float32
    )
    inside_hot = (inside[..., None] == jnp.arange(blocks_dev)).astype(jnp.float32)
    head_hot = (head_of[:, None] == jnp.arange(head_count)).astype(jnp.float32)
    sender = jnp.einsum(
        "wqsc,wqsb,sh->wqcbh", slot_hot, inside_hot, head_hot, precision=lax.Precision.HIGHEST
    )
    my_owners = lax.dynamic_index_in_dim(owners, seq_place, axis=1, keepdims=False)
    earlier = jnp.arange(request_count)[None, :] < jnp.arange(request_count)[:, None]
    same_owner = my_owners[:, :, None] == my_owners[:, None, :]
    rank_index = jnp.sum((same_owner & earlier[None]).astype(jnp.int32), axis=2)
    picker = (
        (my_owners[..., None, None] == jnp.arange(groups)[:, None])
        & (rank_index[..., None, None] == jnp.arange(capacity)[None, :])
    ).astype(jnp.float32)
    first_block = seq_place * blocks_dev
    owned_hot = (global_rows[:, :, None] == first_block + jnp.arange(blocks_dev)).astype(
        jnp.float32
    )
    length = segments.shape[1]
    block_len = length // blocks
    seg_blocks = segments.reshape(windows, blocks, block_len)
    seg_pad = jnp.pad(seg_blocks, ((0, 0), (1, 1), (0, 0)), constant_values=-1)
    near_segs = lax.dynamic_slice_in_dim(seg_pad, first_block, blocks_dev + 2, axis=1)
    slide_seg = jnp.concatenate([near_segs[:, :-2], near_segs[:, 1:-1], near_segs[:, 2:]], axis=2)
    query_seg = near_segs[:, 1:-1]
    rows_index = jnp.arange(windows)
    global_seg = seg_blocks[rows_index[:, None], global_rows].reshape(windows, -1)
    chosen = lax.dynamic_slice_in_dim(random_rows, first_block, blocks_dev, axis=1)
    far_seg = seg_blocks[rows_index[:, None, None, None], chosen].reshape(
        windows, blocks_dev, head_count, -1
    )
    key_seg = jnp.concatenate(
        [
            jnp.broadcast_to(
                slide_seg[:, :, None, :], (windows, blocks_dev, head_count, slide_seg.shape[2])
            ),
            jnp.broadcast_to(
                global_seg[:, None, None, :], (windows, blocks_dev, head_count, global_seg.shape[1])
            ),
            far_seg,
        ],
        axis=3,
    )
    key_mask = query_seg[:, :, None, :, None] == key_seg[:, :, :, None, :]
    local_seg = query_seg.reshape(windows, -1)
    full_mask = global_seg[:, None, :, None] == local_seg[:, None, None, :]
    return (sender, picker, owned_hot, key_mask, full_mask)


def fetch_blocks(paired, queries, sender, picker, owned_hot):
    windows, tokens, head_count, doubled = paired.shape
    head_dim = queries.shape[-1]
    blocks_dev = tokens // BLOCK
    flattened = paired.reshape(windows, tokens, head_count * doubled)
    padded = with_halo(flattened, ((SEQ, 1),), BLOCK)
    framed = padded.reshape(windows, blocks_dev + 2, BLOCK, head_count, doubled)
    sliding = jnp.concatenate([framed[:, :-2], framed[:, 1:-1], framed[:, 2:]], axis=2)
    local_blocks = paired.reshape(windows, blocks_dev, BLOCK, head_count, doubled)
    owned_low = owned_hot.astype(jnp.bfloat16)
    offered = mixed_sum("wgb,wbthe->wgthe", owned_low, local_blocks)
    offered_queries = mixed_sum("wgb,wbqhd->wgqhd", owned_low, queries)
    global_kv, global_queries = (
        lax.psum(offered.astype(jnp.bfloat16), SEQ).astype(jnp.float32),
        lax.psum(offered_queries.astype(jnp.bfloat16), SEQ).astype(jnp.float32),
    )
    global_kv = global_kv.astype(jnp.bfloat16).reshape(windows, -1, head_count, doubled)
    global_queries = global_queries.astype(jnp.bfloat16).reshape(windows, -1, head_count, head_dim)
    outgoing = mixed_sum("wqcbh,wbthe->qwcte", sender.astype(jnp.bfloat16), local_blocks).astype(
        jnp.bfloat16
    )
    incoming = lax.all_to_all(outgoing, SEQ, split_axis=0, concat_axis=0, tiled=True)
    distant = mixed_sum("wspc,pwcte->wste", picker.astype(jnp.bfloat16), incoming).astype(
        jnp.bfloat16
    )
    pick_count = picker.shape[1] // (blocks_dev * head_count)
    distant = distant.reshape(windows, blocks_dev, head_count, pick_count, BLOCK, doubled)
    return (sliding, global_kv, distant, global_queries)


def combine_stats(earlier, later):
    top = jnp.maximum(earlier[0], later[0])
    return (top, earlier[1] * jnp.exp(earlier[0] - top) + later[1] * jnp.exp(later[0] - top))


def full_forward(global_queries, key_part, value_part, full_mask, head_dim):
    scores = mixed_sum("wqhd,wkhd->whqk", global_queries, key_part) * head_dim ** (-0.5)
    scores = jnp.where(full_mask, scores, masked)
    local_top = jnp.max(scores, axis=3, keepdims=True)
    local_sum = jnp.sum(
        jnp.where(full_mask, jnp.exp(scores - local_top), 0.0), axis=3, keepdims=True
    )
    row_top, row_sum = merged((local_top, local_sum), SEQ, combine_stats)
    full_probs = jnp.where(full_mask, jnp.exp(scores - row_top), 0.0) / row_sum
    partial_out = mixed_sum("whqk,wkhd->wqhd", full_probs.astype(jnp.bfloat16), value_part)
    full_out = lax.psum(partial_out.astype(jnp.bfloat16), SEQ).astype(jnp.float32)
    return (full_out, full_probs)


def attention_weights(queries, sliding, global_kv, distant, key_mask):
    head_dim = queries.shape[-1]
    windows, blocks_dev, _, head_count, _ = queries.shape
    near_scores = mixed_sum("wbqhd,wbkhd->wbhqk", queries, sliding[..., :head_dim])
    global_scores = mixed_sum("wbqhd,wkhd->wbhqk", queries, global_kv[..., :head_dim])
    far_scores = mixed_sum("wbqhd,wbhrkd->wbhqrk", queries, distant[..., :head_dim])
    far_scores = far_scores.reshape(windows, blocks_dev, head_count, BLOCK, -1)
    scores = jnp.concatenate([near_scores, global_scores, far_scores], axis=4) * head_dim ** (-0.5)
    scores = jnp.where(key_mask, scores, masked)
    row_top = jnp.max(scores, axis=4, keepdims=True)
    weight = jnp.exp(scores - row_top)
    return weight / jnp.sum(weight, axis=4, keepdims=True)


def split_keys(scores_like, sliding, global_kv, distant):
    near_keys = sliding.shape[2]
    global_keys = global_kv.shape[1]
    windows, blocks_dev, head_count, pick_count, _, _ = distant.shape
    near_part = scores_like[..., :near_keys]
    global_part = scores_like[..., near_keys : near_keys + global_keys]
    far_part = scores_like[..., near_keys + global_keys :].reshape(
        windows, blocks_dev, head_count, BLOCK, pick_count, BLOCK
    )
    return (near_part, global_part, far_part)


def attention_values(low_probs, sliding, global_kv, distant, head_dim):
    near_part, global_part, far_part = split_keys(low_probs, sliding, global_kv, distant)
    attended = mixed_sum("wbhqk,wbkhd->wbqhd", near_part, sliding[..., head_dim:])
    attended = attended + mixed_sum("wbhqk,wkhd->wbqhd", global_part, global_kv[..., head_dim:])
    return attended + mixed_sum("wbhqrk,wbhrkd->wbqhd", far_part, distant[..., head_dim:])


def layer_forward(hidden, weights, tables):
    row_weights, down_weights, vector_weights = weights
    sender, picker, owned_hot, key_mask, full_mask = tables
    model_width = row_weights.shape[0]
    windows, tokens, _ = hidden.shape
    blocks_dev = tokens // BLOCK
    head_dim = model_width // HEADS
    (
        gain_one,
        shift_one,
        bias_query,
        bias_value,
        bias_out,
        gain_two,
        shift_two,
        bias_down,
        bias_up,
    ) = split_vectors(vector_weights, model_width)
    normed = norm_rows(hidden, gain_one, shift_one).astype(jnp.bfloat16)
    projected = mixed_sum("wtd,de->wte", normed, row_weights[:, : 3 * model_width])
    projected = (
        projected + jnp.concatenate([bias_query, jnp.zeros_like(bias_query), bias_value])
    ).astype(jnp.bfloat16)
    queries = projected[..., :model_width].reshape(windows, blocks_dev, BLOCK, HEADS, head_dim)
    key_part = projected[..., model_width : 2 * model_width].reshape(
        windows, tokens, HEADS, head_dim
    )
    value_part = projected[..., 2 * model_width :].reshape(windows, tokens, HEADS, head_dim)
    paired = jnp.concatenate([key_part, value_part], axis=3)
    sliding, global_kv, distant, global_queries = fetch_blocks(
        paired, queries, sender, picker, owned_hot
    )
    probabilities = attention_weights(queries, sliding, global_kv, distant, key_mask)
    attended = attention_values(
        probabilities.astype(jnp.bfloat16), sliding, global_kv, distant, head_dim
    )
    full_out, full_probs = full_forward(global_queries, key_part, value_part, full_mask, head_dim)
    placed = exact_two(
        "wgb,wgqhd->wbqhd", owned_hot, full_out.reshape(windows, -1, BLOCK, HEADS, head_dim)
    )
    on_global = jnp.sum(owned_hot, axis=1)[:, :, None, None, None] > 0
    attended = jnp.where(on_global, placed, attended)
    mixed_low = attended.reshape(windows, tokens, model_width).astype(jnp.bfloat16)
    middle = (
        hidden
        + mixed_sum("wtd,de->wte", mixed_low, row_weights[:, 3 * model_width : 4 * model_width])
        + bias_out
    )
    normed_two = norm_rows(middle, gain_two, shift_two).astype(jnp.bfloat16)
    up_value = mixed_sum("wtd,df->wtf", normed_two, row_weights[:, 4 * model_width :]) + bias_up
    active = jax.nn.gelu(up_value, approximate=False).astype(jnp.bfloat16)
    output = middle + mixed_sum("wtf,fd->wtd", active, down_weights) + bias_down
    stored = (
        hidden,
        normed,
        queries,
        sliding,
        global_kv,
        distant,
        probabilities,
        mixed_low,
        middle,
        normed_two,
        up_value,
        active,
        key_part,
        value_part,
        global_queries,
        full_probs,
    )
    return (output, stored)


def return_blocks(near_back, global_back, far_back, query_part, sender, picker, owned_hot):
    windows, blocks_dev, _, head_count, doubled = near_back.shape
    first_third = near_back[:, :, :BLOCK]
    centre_third = near_back[:, :, BLOCK : 2 * BLOCK]
    last_third = near_back[:, :, 2 * BLOCK :]
    framed = jnp.pad(first_third, ((0, 0), (0, 2), (0, 0), (0, 0), (0, 0)))
    framed = framed + jnp.pad(centre_third, ((0, 0), (1, 1), (0, 0), (0, 0), (0, 0)))
    framed = framed + jnp.pad(last_third, ((0, 0), (2, 0), (0, 0), (0, 0), (0, 0)))
    own_grad = framed[:, 1:-1]
    for direction in (1, -1):
        rim_grad = framed[:, -1] if direction == 1 else framed[:, 0]
        arrived = from_behind(rim_grad.astype(jnp.bfloat16), SEQ, direction).astype(
            rim_grad.dtype
        )
        if direction == 1:
            own_grad = jnp.concatenate(
                [own_grad[:, :1] + arrived[:, None], own_grad[:, 1:]], axis=1
            )
        else:
            own_grad = jnp.concatenate(
                [own_grad[:, :-1], own_grad[:, -1:] + arrived[:, None]], axis=1
            )
    global_total, query_total = (
        lax.psum(
            global_back.reshape(windows, -1, BLOCK, head_count, doubled).astype(jnp.bfloat16), SEQ
        ).astype(jnp.float32),
        lax.psum(query_part.astype(jnp.bfloat16), SEQ).astype(jnp.float32),
    )
    own_grad = own_grad + exact_two("wgb,wgthe->wbthe", owned_hot, global_total)
    far_flat = far_back.reshape(windows, -1, BLOCK, doubled)
    returning = exact_two("wspc,wste->pwcte", picker, far_flat)
    arrived_far = lax.all_to_all(
        returning.astype(jnp.bfloat16), SEQ, split_axis=0, concat_axis=0, tiled=True
    ).astype(returning.dtype)
    own_grad = own_grad + exact_two("wqcbh,qwcte->wbthe", sender, arrived_far)
    return (own_grad.reshape(windows, blocks_dev * BLOCK, head_count, doubled), query_total)


def attention_back(
    grad_attended,
    queries,
    sliding,
    global_kv,
    distant,
    probabilities,
    key_part,
    value_part,
    global_queries,
    full_probs,
    sender,
    picker,
    owned_hot,
):
    head_dim = queries.shape[-1]
    score_scale = head_dim ** (-0.5)
    windows, blocks_dev, _, head_count, _ = queries.shape
    on_global = jnp.sum(owned_hot, axis=1)[:, :, None, None, None] > 0
    selected = mixed_sum("wgb,wbqhd->wgqhd", owned_hot.astype(jnp.bfloat16), grad_attended)
    rows_grad = lax.psum(selected.astype(jnp.bfloat16), SEQ).reshape(
        windows, -1, head_count, head_dim
    )
    grad_attended = jnp.where(on_global, jnp.zeros_like(grad_attended), grad_attended)
    low_probs = probabilities.astype(jnp.bfloat16)
    near_grad = mixed_sum("wbqhd,wbkhd->wbhqk", grad_attended, sliding[..., head_dim:])
    global_grad = mixed_sum("wbqhd,wkhd->wbhqk", grad_attended, global_kv[..., head_dim:])
    far_grad = mixed_sum("wbqhd,wbhrkd->wbhqrk", grad_attended, distant[..., head_dim:])
    far_grad = far_grad.reshape(windows, blocks_dev, head_count, BLOCK, -1)
    grad_probs = jnp.concatenate([near_grad, global_grad, far_grad], axis=4)
    grad_scores = probabilities * (
        grad_probs - jnp.sum(probabilities * grad_probs, axis=4, keepdims=True)
    )
    grad_scores = grad_scores.astype(jnp.bfloat16)
    near_split, global_split, far_split = split_keys(grad_scores, sliding, global_kv, distant)
    near_probs, global_probs, far_probs = split_keys(low_probs, sliding, global_kv, distant)
    grad_query = mixed_sum("wbhqk,wbkhd->wbqhd", near_split, sliding[..., :head_dim])
    grad_query = grad_query + mixed_sum(
        "wbhqk,wkhd->wbqhd", global_split, global_kv[..., :head_dim]
    )
    grad_query = (
        grad_query + mixed_sum("wbhqrk,wbhrkd->wbqhd", far_split, distant[..., :head_dim])
    ) * score_scale
    near_back = jnp.concatenate(
        [
            mixed_sum("wbhqk,wbqhd->wbkhd", near_split, queries) * score_scale,
            mixed_sum("wbhqk,wbqhd->wbkhd", near_probs, grad_attended),
        ],
        axis=4,
    )
    global_back = jnp.concatenate(
        [
            mixed_sum("wbhqk,wbqhd->wkhd", global_split, queries) * score_scale,
            mixed_sum("wbhqk,wbqhd->wkhd", global_probs, grad_attended),
        ],
        axis=3,
    )
    far_back = jnp.concatenate(
        [
            mixed_sum("wbhqrk,wbqhd->wbhrkd", far_split, queries) * score_scale,
            mixed_sum("wbhqrk,wbqhd->wbhrkd", far_probs, grad_attended),
        ],
        axis=5,
    )
    full_grad_probs = mixed_sum("wqhd,wkhd->whqk", rows_grad, value_part)
    partial_dot = jnp.sum(full_probs * full_grad_probs, axis=3, keepdims=True)
    row_dot = lax.psum(partial_dot, SEQ)
    full_grad_scores = (full_probs * (full_grad_probs - row_dot)).astype(jnp.bfloat16)
    query_part = mixed_sum("whqk,wkhd->wqhd", full_grad_scores, key_part) * score_scale
    full_key_grad = mixed_sum("whqk,wqhd->wkhd", full_grad_scores, global_queries) * score_scale
    full_value_grad = mixed_sum("whqk,wqhd->wkhd", full_probs.astype(jnp.bfloat16), rows_grad)
    grad_paired, query_total = return_blocks(
        near_back, global_back, far_back, query_part, sender, picker, owned_hot
    )
    grad_query = grad_query + exact_two(
        "wgb,wgqhd->wbqhd", owned_hot, query_total.reshape(windows, -1, BLOCK, head_count, head_dim)
    )
    grad_paired = grad_paired + jnp.concatenate([full_key_grad, full_value_grad], axis=3)
    return (grad_query, grad_paired)


def layer_backward(stored, grad_output, weights, tables):
    row_weights, down_weights, vector_weights = weights
    sender, picker, owned_hot, key_mask, full_mask = tables
    (
        hidden,
        normed,
        queries,
        sliding,
        global_kv,
        distant,
        probabilities,
        mixed_low,
        middle,
        normed_two,
        up_value,
        active,
        key_part,
        value_part,
        global_queries,
        full_probs,
    ) = stored
    model_width = row_weights.shape[0]
    windows, tokens, _ = hidden.shape
    blocks_dev = tokens // BLOCK
    head_dim = model_width // HEADS
    (
        gain_one,
        shift_one,
        bias_query,
        bias_value,
        bias_out,
        gain_two,
        shift_two,
        bias_down,
        bias_up,
    ) = split_vectors(vector_weights, model_width)
    grad_ffn = grad_output.astype(jnp.bfloat16)
    grad_bias_down = jnp.sum(grad_ffn.astype(jnp.float32), axis=(0, 1))
    grad_down = mixed_sum("wtf,wtd->fd", active, grad_ffn)
    grad_active = mixed_sum("wtd,fd->wtf", grad_ffn, down_weights)
    gelu_pull = jax.vjp(partial(jax.nn.gelu, approximate=False), up_value)[1]
    grad_up = gelu_pull(grad_active)[0].astype(jnp.bfloat16)
    grad_bias_up = jnp.sum(grad_up.astype(jnp.float32), axis=(0, 1))
    grad_in = mixed_sum("wtd,wtf->df", normed_two, grad_up)
    grad_normed_two = mixed_sum("wtf,df->wtd", grad_up, row_weights[:, 4 * model_width :])
    norm_pull_two = jax.vjp(norm_rows, middle, gain_two, shift_two)[1]
    grad_middle_norm, grad_gain_two, grad_shift_two = norm_pull_two(grad_normed_two)
    grad_middle = grad_output + grad_middle_norm
    grad_branch = grad_middle.astype(jnp.bfloat16)
    grad_bias_out = jnp.sum(grad_branch.astype(jnp.float32), axis=(0, 1))
    grad_out_weight = mixed_sum("wtd,wte->de", mixed_low, grad_branch)
    grad_attended = mixed_sum(
        "wte,de->wtd", grad_branch, row_weights[:, 3 * model_width : 4 * model_width]
    ).astype(jnp.bfloat16)
    grad_attended = grad_attended.reshape(windows, blocks_dev, BLOCK, HEADS, head_dim)
    grad_query, grad_paired = attention_back(
        grad_attended,
        queries,
        sliding,
        global_kv,
        distant,
        probabilities,
        key_part,
        value_part,
        global_queries,
        full_probs,
        sender,
        picker,
        owned_hot,
    )
    grad_projected = jnp.concatenate(
        [
            grad_query.reshape(windows, tokens, model_width),
            grad_paired[..., :head_dim].reshape(windows, tokens, model_width),
            grad_paired[..., head_dim:].reshape(windows, tokens, model_width),
        ],
        axis=2,
    ).astype(jnp.bfloat16)
    summed = jnp.sum(grad_projected.astype(jnp.float32), axis=(0, 1))
    grad_bias_query = summed[:model_width]
    grad_bias_value = summed[2 * model_width :]
    grad_projection = mixed_sum("wtd,wte->de", normed, grad_projected)
    grad_normed = mixed_sum("wte,de->wtd", grad_projected, row_weights[:, : 3 * model_width])
    norm_pull_one = jax.vjp(norm_rows, hidden, gain_one, shift_one)[1]
    grad_hidden_norm, grad_gain_one, grad_shift_one = norm_pull_one(grad_normed)
    grad_hidden = grad_middle + grad_hidden_norm
    grad_rows = jnp.concatenate([grad_projection, grad_out_weight, grad_in], axis=1)
    grad_vectors = jnp.concatenate(
        [
            grad_gain_one,
            grad_shift_one,
            grad_bias_query,
            grad_bias_value,
            grad_bias_out,
            grad_gain_two,
            grad_shift_two,
            grad_bias_down,
            grad_bias_up,
        ]
    )
    return (grad_hidden, (grad_rows, grad_down, grad_vectors))


def adam_update(master, first_old, second_old, gradient, step_rate, decay_rate):
    first_new = 0.5 * first_old + 0.5 * gradient
    second_new = 0.5 * second_old + 0.5 * gradient * gradient
    first_hat = first_new / (1.0 - 0.5**STEP)
    second_hat = second_new / (1.0 - 0.5**STEP)
    master_new = master - step_rate * (
        first_hat / (jnp.sqrt(second_hat) + 1e-08) + decay_rate * master
    )
    return (master_new, first_new, second_new)


def general_shards(
    block_input,
    cotangent,
    random_ids,
    segment_ids,
    global_ids,
    w_rows,
    w_rows_first,
    w_rows_second,
    w_down,
    w_down_first,
    w_down_second,
    vectors,
    vectors_first,
    vectors_second,
):
    section_index = lax.axis_index(SECTION)
    seq_place = lax.axis_index(SEQ)
    groups = lax.axis_size(SEQ)
    row_weights, down_weights, vector_low = (
        lax.all_gather(w_rows[0].astype(jnp.bfloat16), (DP, SEQ), axis=1, tiled=True),
        lax.all_gather(w_down[0].astype(jnp.bfloat16), (DP, SEQ), axis=0, tiled=True),
        lax.all_gather(vectors[0].astype(jnp.bfloat16), (DP, SEQ), axis=0, tiled=True),
    )
    weights = (row_weights, down_weights, vector_low.astype(jnp.float32))
    micro_count, windows, tokens, model_width = block_input.shape
    received = jnp.zeros((windows, tokens, model_width), jnp.bfloat16)
    results = jnp.zeros(block_input.shape, jnp.float32)
    full_totals = (
        jnp.zeros(row_weights.shape, jnp.float32),
        jnp.zeros(down_weights.shape, jnp.float32),
        jnp.zeros(vector_low.shape, jnp.float32),
    )

    def tick(tick_index, carry):
        received, results, full_totals = carry
        forward_mb = jnp.clip(tick_index - section_index, 0, micro_count - 1)
        behind_raw = tick_index - 2 + section_index
        behind = jnp.clip(behind_raw, 0, micro_count - 1)
        live_mask = ((behind_raw >= 0) & (behind_raw < micro_count)).astype(jnp.float32)
        tables_forward = route_tables(
            lax.dynamic_index_in_dim(random_ids, forward_mb, 0, keepdims=False),
            lax.dynamic_index_in_dim(segment_ids, forward_mb, 0, keepdims=False),
            lax.dynamic_index_in_dim(global_ids, forward_mb, 0, keepdims=False),
            seq_place,
            groups,
        )
        tables_behind = route_tables(
            lax.dynamic_index_in_dim(random_ids, behind, 0, keepdims=False),
            lax.dynamic_index_in_dim(segment_ids, behind, 0, keepdims=False),
            lax.dynamic_index_in_dim(global_ids, behind, 0, keepdims=False),
            seq_place,
            groups,
        )
        incoming_values = received.astype(jnp.float32)
        first_input = lax.dynamic_index_in_dim(block_input, forward_mb, 0, keepdims=False).astype(
            jnp.float32
        )
        forward_input = jnp.where(section_index == 0, first_input, incoming_values)
        forward_output = layer_forward(forward_input, weights, tables_forward)[0]
        back_source = lax.dynamic_index_in_dim(block_input, behind, 0, keepdims=False).astype(
            jnp.float32
        )
        back_input = jnp.where(section_index == 0, back_source, incoming_values)
        given_grad = lax.dynamic_index_in_dim(cotangent, behind, 0, keepdims=False).astype(
            jnp.float32
        )
        back_grad = jnp.where(section_index == 0, incoming_values, given_grad) * live_mask
        stored = layer_forward(back_input, weights, tables_behind)[1]
        grad_input, gradients = layer_backward(stored, back_grad, weights, tables_behind)
        outgoing = jnp.where(section_index == 0, forward_output, grad_input).astype(jnp.bfloat16)
        finished = jnp.where(section_index == 0, grad_input, forward_output)
        updated = lax.dynamic_update_index_in_dim(results, finished, behind, 0)
        results = jnp.where(live_mask > 0, updated, results)
        full_totals = tuple(
            (total_part + grad_part for total_part, grad_part in zip(full_totals, gradients))
        )
        return (partner(outgoing, SECTION, 0), results, full_totals)

    received, results, full_totals = lax.fori_loop(
        0, micro_count + 2, tick, (received, results, full_totals)
    )
    shard_totals = (
        lax.psum_scatter(full_totals[0], (DP, SEQ), scatter_dimension=1, tiled=True),
        lax.psum_scatter(full_totals[1], (DP, SEQ), scatter_dimension=0, tiled=True),
        lax.psum_scatter(full_totals[2], (DP, SEQ), scatter_dimension=0, tiled=True),
    )
    new_rows, new_rows_first, new_rows_second = adam_update(
        w_rows[0], w_rows_first[0], w_rows_second[0], shard_totals[0], rate_matrix, decay_matrix
    )
    new_down, new_down_first, new_down_second = adam_update(
        w_down[0], w_down_first[0], w_down_second[0], shard_totals[1], rate_matrix, decay_matrix
    )
    new_vectors, new_vectors_first, new_vectors_second = adam_update(
        vectors[0], vectors_first[0], vectors_second[0], shard_totals[2], rate_vector, 0.0
    )
    return (
        results[None],
        new_rows[None],
        new_rows_first[None],
        new_rows_second[None],
        new_down[None],
        new_down_first[None],
        new_down_second[None],
        new_vectors[None],
        new_vectors_first[None],
        new_vectors_second[None],
    )


LOW = jnp.bfloat16
LOG_HIGH = [float(np.log(c).astype(ml_dtypes.bfloat16)) for c in (1.0, 2.0, 3.0)]
LOG_LOW = [float(np.log(c)) - high for c, high in zip((1.0, 2.0, 3.0), LOG_HIGH)]
CHUNK = 256
VMEM_BYTES = 48 * 1024 * 1024
DENSE_BYTES = 36 * 1024 * 1024


def dot_rows(left, right):
    return lax.dot_general(left, right, (((1,), (1,)), ((), ())), preferred_element_type=jnp.float32)


def dot_plain(left, right):
    return lax.dot_general(left, right, (((1,), (0,)), ((), ())), preferred_element_type=jnp.float32)


def dot_tokens(left, right):
    return lax.dot_general(left, right, (((0,), (0,)), ((), ())), preferred_element_type=jnp.float32)


def swap(value):
    return lax.ppermute(value, SECTION, [(0, 1), (1, 0)])


def normalized(values_in):
    row_mean = jnp.mean(values_in, axis=-1, keepdims=True)
    centred = values_in - row_mean
    spread = jnp.mean(centred * centred, axis=-1, keepdims=True)
    scale = lax.rsqrt(spread + epsilon)
    return centred * scale, scale


class Shares:
    def __init__(self, width, columns, depth, vector_len):
        self.width = width
        self.columns = columns
        self.depth = depth
        self.vector_len = vector_len
        self.half = columns // 2
        self.per = width // columns
        self.groups = columns // depth

    def unpack(self, gathered, core):
        rows, down, vec = gathered
        vec = vec.reshape(-1, TAIL, self.width)[:, 0, : self.vector_len].reshape(-1)
        pieces = split_vectors(vec.astype(jnp.float32), self.width)
        for index in (2, 3):
            pieces[index] = lax.dynamic_index_in_dim(
                pieces[index].reshape(self.per, 2, self.half), core, 1, keepdims=False
            )
        pieces[8] = lax.dynamic_index_in_dim(
            pieces[8].reshape(-1, 2, self.depth // 2), core, 1, keepdims=False
        )
        return (
            (rows.reshape(-1, self.width), down.reshape(-1, self.width)),
            [piece.reshape(1, -1) for piece in pieces],
        )

    def by_shard(self, grads, vector_grads, core):
        proj, out, up, down = grads
        half, per, width = self.half, self.per, self.width
        hot = (jnp.arange(2) == core).astype(jnp.float32)
        spread = list(vector_grads)
        for index in (2, 3):
            spread[index] = (
                spread[index].reshape(per, 1, half) * hot[None, :, None]
            ).reshape(-1)
        spread[8] = (spread[8].reshape(-1, 1, self.depth // 2) * hot[None, :, None]).reshape(-1)
        for index in (0, 1, 4, 5, 6, 7):
            spread[index] = spread[index] * hot[0]
        vec = jnp.concatenate(spread).reshape(-1, 1, self.vector_len)
        vec = jnp.pad(vec, ((0, 0), (0, TAIL - 1), (0, width - self.vector_len))).astype(LOW)
        return (
            proj.reshape(-1, half, width),
            out.reshape(-1, half, width),
            up.reshape(2, 4, half, width),
            down.reshape(2, 2, 4, self.depth // 2, width),
            vec.reshape(2, 2, 4, TAIL, width),
        )


MESH = pl.DeviceIdType.MESH
PIECE = 48
TAIL = 16


def prepare_kernel(shares, rows_ref, down_ref, vector_ref, rows_out, down_out, vector_out):
    core = lax.axis_index(SECTION)
    offset = lax.axis_index((DP, SEQ)) * shares.columns
    half, per, width, depth = shares.half, shares.per, shares.width, shares.depth // 2
    is_inner = (offset >= 3 * width) & (offset < 4 * width)
    is_hidden = offset >= 4 * width

    @pl.when(is_inner)
    def _():
        for which in range(2):
            side = core if which == 0 else 1 - core
            held = [rows_ref[pl.ds((2 * j + side) * half, half), :] for j in range(per)]
            turned = jnp.transpose(jnp.concatenate(held, axis=0))
            rows_out[which] = jnp.concatenate([turned[:half], turned[half:]], axis=1).astype(LOW)

    @pl.when(jnp.logical_not(is_inner))
    def _():
        turned = jnp.transpose(rows_ref[...]).astype(LOW)
        plain = [turned[:half], turned[half:]]
        hidden = [
            jnp.concatenate(
                [turned[(2 * j + side) * depth :][:depth] for j in range(shares.groups)], axis=0
            )
            for side in range(2)
        ]
        halves = [jnp.where(is_hidden, b, a) for a, b in zip(plain, hidden)]
        rows_out[0] = jnp.where(core == 0, halves[0], halves[1])
        rows_out[1] = jnp.where(core == 0, halves[1], halves[0])

    down = down_ref[...].astype(LOW)
    down_out[0] = jnp.where(core == 0, down[:depth], down[depth:])
    down_out[1] = jnp.where(core == 0, down[depth:], down[:depth])
    vector_out[...] = jnp.zeros_like(vector_out)
    vector_out[0:1, : shares.vector_len] = vector_ref[...].astype(LOW)


def prepare(shares, rows, down, vector):
    return pl.pallas_call(
        partial(prepare_kernel, shares),
        out_shape=[
            jax.ShapeDtypeStruct((2, shares.half, shares.width), LOW),
            jax.ShapeDtypeStruct((2, shares.depth // 2, shares.width), LOW),
            jax.ShapeDtypeStruct((TAIL, shares.width), LOW),
        ],
        compiler_params=pltpu.CompilerParams(vmem_limit_bytes=VMEM_BYTES),
    )(rows, down, vector)


class Place:
    def __init__(self):
        self.core = lax.axis_index(SECTION)
        self.dp = lax.axis_index(DP)
        self.z = lax.axis_index(SEQ)
        self.y, self.x = self.dp // 2, self.dp % 2
        self.high, self.low = self.z // 2, self.z % 2
        self.inner = self.high + self.low == 1
        self.outer = self.high + self.low != 1
        self.partner = {SECTION: 1 - self.core}
        self.along_x = {DP: 2 * self.y + 1 - self.x}
        self.along_y = {DP: 2 * (1 - self.y) + self.x}
        self.across = {SEQ: 3 - self.z}
        self.beside = {SEQ: 2 * self.high + 1 - self.low}
        self.others = [{SEQ: (self.z + by) % 4} for by in (1, 2, 3)]
        self.own = pl.ds(self.z, 1)
        self.next = pl.ds(2 * self.high + 1 - self.low, 1)
        self.near = pl.ds(2 * self.high, 2)
        self.far = pl.ds(2 * (1 - self.high), 2)

    def greet(self):
        barrier = pltpu.get_barrier_semaphore()
        everyone = [self.partner, self.along_x, self.along_y] + self.others
        for device in everyone:
            pl.semaphore_signal(barrier, inc=1, device_id=device, device_id_type=MESH)
        pl.semaphore_wait(barrier, len(everyone))


def remote(src, dst, sems, spots, device):
    return pltpu.make_async_remote_copy(
        src_ref=src,
        dst_ref=dst,
        send_sem=sems[0].at[spots[0]],
        recv_sem=sems[1].at[spots[1]],
        device_id=device,
        device_id_type=MESH,
    )


def chunk_pairs(shares):
    pairs = []
    for array, length in ((0, shares.half), (1, shares.depth // 2)):
        for start in range(0, length, 2 * PIECE):
            pairs.append([(array, start, PIECE, 0), (array, start + PIECE, PIECE, 1)])
    pairs[0].append((2, 0, TAIL, 0))
    return pairs


def quad_pairs(shares):
    length = (shares.half + shares.depth // 2) // 2
    pairs = [
        [(0, start, PIECE, None), (1, start, PIECE, None)] for start in range(0, length, PIECE)
    ]
    pairs[0].append((2, 0, TAIL, 0))
    return pairs


def gather_kernel(shares, *refs):
    (rows_in, down_in, vector_in, x_in, cot_in), refs = refs[:5], refs[5:]
    outs, refs = [refs[0:3], refs[3:6]], refs[6:]
    (x_out, cot_out), refs = refs[:2], refs[2:]
    local, swap_send, swap_recv, z_send, z_recv, send, recv = refs
    here = Place()
    core, y, x, z = here.core, here.y, here.x, here.z
    half = x_in.shape[2] // 2
    rows_half, down_half = shares.half // 2, shares.depth // 4
    here.greet()

    def slices(source, target, base):
        mine = pl.ds(pl.multiple_of(core * half, half), half)
        sems = (z_send, z_recv)
        own = pltpu.make_async_copy(
            source.at[z, 0, mine], target.at[z, core], local.at[8 + base // 4]
        )
        sends, arrivals = [], []
        for by in (1, 2, 3):
            spots = (base + by - 1, base + by - 1)
            device = here.others[by - 1]
            sends.append(
                remote(source.at[(z + by) % 4, 0, mine], target.at[z, core], sems, spots, device)
            )
            arrivals.append(
                remote(
                    source.at[z, 0, mine], target.at[(z + 4 - by) % 4, core], sems, spots, device
                )
            )
        spots = (base + 3, base + 3)
        forward = remote(target.at[:, core], target.at[:, core], sems, spots, here.partner)
        arrived = remote(target.at[:, 1 - core], target.at[:, 1 - core], sems, spots, here.partner)
        return own, sends, arrivals, forward, arrived

    x_moves = slices(x_in, x_out, 0)
    cot_moves = slices(cot_in, cot_out, 4)

    def open_slices(moves):
        moves[0].start()
        for copy in moves[1]:
            copy.start()

    def pass_slices(moves):
        moves[0].wait()
        for copy in moves[2]:
            copy.wait_recv()
        moves[3].start()

    def close_slices(moves):
        for copy in moves[1]:
            copy.wait_send()
        moves[3].wait_send()
        moves[4].wait_recv()

    def first_moves(layer, which):
        down = down_in.at[which]
        rows = rows_in.at[which]
        if layer == 0:
            return [
                (0, rows, outs[0][0].at[y, x, z]),
                (1, down, outs[0][1].at[y, x, z]),
                (2, vector_in, outs[0][2].at[y, x, z]),
            ]
        moves = [(7, vector_in, outs[1][2].at[y, x, z])]
        for part in range(2):
            target = outs[1][part]
            moves.append(
                (
                    3 + 2 * part,
                    rows.at[pl.ds(part * rows_half, rows_half)],
                    target.at[z, pl.ds(0, rows_half)],
                )
            )
            moves.append(
                (
                    4 + 2 * part,
                    down.at[pl.ds(part * down_half, down_half)],
                    target.at[z, pl.ds(rows_half, down_half)],
                )
            )
        return moves

    swaps = (swap_send, swap_recv)
    for layer in range(2):

        @pl.when(core == layer)
        def _():
            across = [
                remote(src, dst, swaps, (spot, spot), here.partner)
                for spot, src, dst in first_moves(layer, 1)
            ]
            own = [
                pltpu.make_async_copy(src, dst, local.at[spot])
                for spot, src, dst in first_moves(layer, 0)
            ]
            for copy in across + own:
                copy.start()
            for copy in own:
                copy.wait()
            for copy in across:
                copy.wait_send()
            for spot, src, dst in first_moves(1 - layer, 0):
                remote(src, dst, swaps, (spot, spot), here.partner).wait_recv()

    numbers, pairs = {}, []
    for layer in range(2):
        for pair in chunk_pairs(shares) if layer == 0 else quad_pairs(shares):
            entry = []
            for array, start, length, order in pair:
                ref = outs[layer][array]
                rows = pl.ds(start, length)
                flat = order is None
                number = len(numbers)
                sems = (send, recv)

                def part(which):
                    return ref.at[which, rows] if flat else ref.at[y, x, which, rows]

                def copy(piece, spots, device):
                    return remote(piece, piece, sems, ((number, spots[0]), (number, spots[1])), device)

                steps = {
                    "z": copy(part(here.own), (0, 0), here.beside),
                    "across": copy(part(here.near), (1, 1), here.across),
                    "on": copy(part(here.far), (4, 1), here.beside),
                }
                arrive = [
                    copy(part(here.next), (0, 0), here.beside),
                    copy(part(here.far), (1, 1), here.across),
                ]
                if order == 0:
                    steps["one"] = copy(ref.at[y, x, :, rows], (2, 2), here.along_y)
                    steps["two"] = copy(ref.at[:, x, :, rows], (3, 3), here.along_x)
                    arrive.append(copy(ref.at[1 - y, x, :, rows], (2, 2), here.along_y))
                    arrive.append(copy(ref.at[:, 1 - x, :, rows], (3, 3), here.along_x))
                elif order == 1:
                    steps["one"] = copy(ref.at[y, x, :, rows], (2, 2), here.along_x)
                    steps["two"] = copy(ref.at[y, :, :, rows], (3, 3), here.along_y)
                    arrive.append(copy(ref.at[y, 1 - x, :, rows], (2, 2), here.along_x))
                    arrive.append(copy(ref.at[1 - y, :, :, rows], (3, 3), here.along_y))
                numbers[number] = (steps, arrive)
                entry.append(number)
            pairs.append(entry)

    def issue(name, entry):
        after = {"z": None, "across": 0, "on": 1, "one": 1, "two": 2}[name]

        def start():
            for number in entry:
                steps, arrive = numbers[number]
                if name in steps:
                    if after is not None and not (name == "one"):
                        arrive[after].wait_recv()
                    steps[name].start()

        if name in ("across", "on"):
            pl.when(here.inner)(start)
        else:
            start()

    def arrived(entry, index, where):
        def wait():
            for number in entry:
                numbers[number][1][index].wait_recv()

        pl.when(where)(wait)

    first, second = pairs[: len(chunk_pairs(shares))], pairs[len(chunk_pairs(shares)) :]
    for entry in first:
        issue("z", entry)
    for entry in first:
        issue("across", entry)
        arrived(entry, 0, here.outer)
    for entry in first[:-1]:
        issue("on", entry)
        arrived(entry, 1, here.outer)
        issue("one", entry)
    issue("on", first[-1])
    for entry in second:
        issue("z", entry)
    open_slices(x_moves)
    arrived(first[-1], 1, here.outer)
    issue("one", first[-1])
    issue("two", first[0])
    for entry in second:
        issue("across", entry)
        arrived(entry, 0, here.outer)
    issue("two", first[1])
    open_slices(cot_moves)
    for entry in second:
        issue("on", entry)
    issue("two", first[2])
    pass_slices(x_moves)
    for entry in second:
        arrived(entry, 1, here.outer)
        for number in entry:
            steps, arrive = numbers[number]
            if "one" in steps:
                steps["one"].start()
                arrive[2].wait_recv()
                steps["two"].start()
    pass_slices(cot_moves)
    for steps, arrive in numbers.values():
        if len(arrive) == 4:
            arrive[3].wait_recv()
        for name in steps:
            if name not in ("across", "on"):
                steps[name].wait_send()

    @pl.when(here.inner)
    def _():
        for steps, _ in numbers.values():
            steps["across"].wait_send()
            steps["on"].wait_send()

    close_slices(x_moves)
    close_slices(cot_moves)


def gather(shares, prepared, block_input, cotangent):
    micro, _, tokens, width = block_input.shape
    chunks = sum(len(pair) for pair in chunk_pairs(shares) + quad_pairs(shares))
    lengths = (shares.half, shares.depth // 2, TAIL)
    layer = [jax.ShapeDtypeStruct((2, 2, 4, rows, width), LOW) for rows in lengths]
    quad = jax.ShapeDtypeStruct((4, (lengths[0] + lengths[1]) // 2, width), LOW)
    window = jax.ShapeDtypeStruct((micro, 2, tokens // 2, width), LOW)
    anywhere = pl.BlockSpec(memory_space=pl.ANY)
    results = pl.pallas_call(
        partial(gather_kernel, shares),
        in_specs=[anywhere] * 5,
        out_specs=[anywhere] * 8,
        out_shape=layer + [quad, quad, layer[2]] + [window, window],
        scratch_shapes=[
            pltpu.SemaphoreType.DMA((10,)),
            pltpu.SemaphoreType.DMA((8,)),
            pltpu.SemaphoreType.DMA((8,)),
            pltpu.SemaphoreType.DMA((8,)),
            pltpu.SemaphoreType.DMA((8,)),
            pltpu.SemaphoreType.DMA((chunks, 5)),
            pltpu.SemaphoreType.DMA((chunks, 4)),
        ],
        compiler_params=pltpu.CompilerParams(collective_id=0, has_side_effects=True),
    )(*prepared, block_input, cotangent)
    return results[0:3], results[3:6], results[6], results[7]


def over(value, bit):
    return lax.ppermute(value, DP, [(i, i ^ bit) for i in range(4)])


def layout_moves(shares, y, x, pieces, arrays):
    rows_half, down_half = shares.half // 2, shares.depth // 4
    down = arrays[-1]
    moves = []
    for part in range(2):
        rows = pl.ds(part * rows_half, rows_half)
        for index, (by_y, by_x) in enumerate(((0, 0), (1, 0), (0, 1), (1, 1))):
            piece = pieces[part][index]
            at_y, at_x = y ^ by_y, x ^ by_x
            top = pl.ds(0, rows_half)
            if len(arrays) == 2:
                moves.append((piece.at[:, top], arrays[0].at[at_y, at_x, :, rows]))
            else:
                proj, out, up, _ = arrays
                if at_y == 1:
                    moves.append((piece.at[:, top], up.at[at_x, :, rows]))
                elif at_x == 0:
                    moves.append((piece.at[:, top], proj.at[pl.ds(0, 4), rows]))
                else:
                    moves.append((piece.at[pl.ds(0, 2), top], proj.at[pl.ds(4, 2), rows]))
                    moves.append((piece.at[pl.ds(2, 2), top], out.at[:, rows]))
            moves.append(
                (
                    piece.at[:, pl.ds(rows_half, down_half)],
                    down.at[at_y, at_x, :, pl.ds(part * down_half, down_half)],
                )
            )
    return moves


def layout_kernel(shares, joins, *refs):
    dp = lax.axis_index(DP)
    if joins:
        pieces, arrays = [refs[0:4], refs[4:8]], refs[8:10]
    else:
        arrays, pieces = refs[0:4], [refs[4:8], refs[8:12]]
    for spot in range(4):

        @pl.when(dp == spot)
        def _():
            for piece, place in layout_moves(shares, spot // 2, spot % 2, pieces, arrays):
                src, dst = (piece, place) if joins else (place, piece)
                dst[...] = src[...]


def layout(shares, joins, *arrays):
    half, depth, width = shares.half, shares.depth // 2, shares.width
    if joins:
        shapes = [(2, 2, 4, half, width), (2, 2, 4, depth, width)]
    else:
        shapes = [(4, (half + depth) // 2, width)] * 8
    return pl.pallas_call(
        partial(layout_kernel, shares, joins),
        out_shape=[jax.ShapeDtypeStruct(shape, LOW) for shape in shapes],
        compiler_params=pltpu.CompilerParams(vmem_limit_bytes=VMEM_BYTES),
        cost_estimate=pl.CostEstimate(
            flops=0, bytes_accessed=64 * (half + depth) * width, transcendentals=0
        ),
    )(*arrays)


def tied(value, flying):
    return lax.optimization_barrier((value, flying))


def spread_quads(shares, quads):
    low, high = quads
    flying = (low, high, over(low, 2), over(high, 1))
    low, high, low_y, high_x = yield flying
    flying = (low_y, high_x, over(low, 1), over(high, 2))
    low_y, high_x, low_x, high_y = yield flying
    flying = (over(low_y, 1), over(high_x, 2))
    low_both, high_both = yield flying
    yield layout(shares, True, low, low_y, low_x, low_both, high, high_y, high_x, high_both)


def sum_quads(shares, arrays):
    pieces = layout(shares, False, *arrays)

    def total(*terms):
        return sum(term.astype(jnp.float32) for term in terms).astype(LOW)

    low, low_y, low_x, low_both = pieces[:4]
    high, high_y, high_x, high_both = pieces[4:]
    flying = (low_x, high_y, over(low_both, 1), over(high_both, 2))
    low_x, high_y, low_hop, high_hop = yield flying
    low_y, high_x = total(low_y, low_hop), total(high_x, high_hop)
    flying = (low_y, high_x, over(low_x, 1), over(high_y, 2))
    low_y, high_x, low_x, high_y = yield flying
    flying = (over(low_y, 2), over(high_x, 1))
    low_y, high_x = yield flying
    yield (total(low, low_x, low_y), total(high, high_x, high_y))


class Beside:
    def __init__(self, hops=None):
        self.hops = hops
        self.flying = None if hops is None else next(hops)

    def tie(self, value):
        if self.hops is None:
            return value
        value, arrived = tied(value, self.flying)
        self.flying = self.hops.send(arrived)
        return value


def scatter_kernel(shares, *refs):
    (proj, out, up, down, vec_zero, low, high, vec_one), refs = refs[:8], refs[8:]
    (dx_ref, final_ref, halves, slices), refs = refs[:4], refs[4:]
    work, refs = [refs[0:3], refs[3:6]], refs[6:]
    (got_one, got_two, got_far, got_across, got_near, total), refs = refs[:6], refs[6:]
    load, local, swap_send, swap_recv, z_send, z_recv, send, recv = refs
    here = Place()
    core, y, x, z = here.core, here.y, here.x, here.z
    rows_half, down_half = shares.half // 2, shares.depth // 4
    down_base = shares.half
    tail_base = shares.half + shares.depth // 2

    rows = work[0][0]
    moves = [
        [
            (proj.at[pl.ds(0, 4)], rows.at[0, 0]),
            (proj.at[pl.ds(4, 2)], rows.at[0, 1, pl.ds(0, 2)]),
            (out, rows.at[0, 1, pl.ds(2, 2)]),
            (up, rows.at[1]),
            (down, work[0][1]),
            (vec_zero, work[0][2]),
        ],
        [(low, work[1][0]), (high, work[1][1]), (vec_one, work[1][2])],
    ]
    loads = [
        [
            pltpu.make_async_copy(src, dst, load.at[layer, index])
            for index, (src, dst) in enumerate(moves[layer])
        ]
        for layer in range(2)
    ]
    for layer in (1, 0):
        for copy in loads[layer]:
            copy.start()
    here.greet()

    def place_of(layer, array, start):
        if array == 2:
            return tail_base
        if layer == 0:
            return (0, down_base)[array] + start
        if start < rows_half:
            return array * rows_half + start
        return down_base + array * down_half + start - rows_half

    pairs, chunks = [], []
    for layer in (1, 0):
        for index, pair in enumerate(quad_pairs(shares) if layer else chunk_pairs(shares)):
            entry = []
            for array, start, length, order in pair:
                entry.append((len(chunks), layer, array, start, length, order))
                chunks.append(entry[-1])
            pairs.append((index, entry))

    def pieces(chunk):
        number, layer, array, start, length, order = chunk
        ref = work[layer][array]
        rows = pl.ds(start, length)
        sems = (send, recv)
        keeps, slots, copies = [], [], []

        def part(which):
            return ref.at[which, rows] if order is None else ref.at[y, x, which, rows]

        def add(src, slot, device, keep):
            spots = (number, len(copies))
            copies.append(remote(src, slot, sems, (spots, spots), device))
            slots.append(slot)
            keeps.append(keep)

        room = pl.ds(0, length)
        if order == 0:
            add(ref.at[:, 1 - x, :, rows], got_one.at[number, :, :, room], here.along_x, ref.at[:, x, :, rows])
            add(ref.at[1 - y, x, :, rows], got_two.at[number, :, room], here.along_y, ref.at[y, x, :, rows])
        elif order == 1:
            add(ref.at[1 - y, :, :, rows], got_one.at[number, :, :, room], here.along_y, ref.at[y, :, :, rows])
            add(ref.at[y, 1 - x, :, rows], got_two.at[number, :, room], here.along_x, ref.at[y, x, :, rows])
        else:
            copies, slots, keeps = [None] * 2, [None] * 2, [None] * 2
        add(part(here.far), got_far.at[number, :, room], here.beside, part(here.far))
        add(part(here.far), got_across.at[number, :, room], here.across, part(here.near))
        add(part(here.next), got_near.at[number, :, room], here.beside, part(here.own))
        return copies, keeps, slots

    built = [pieces(chunk) for chunk in chunks]
    loaded = set()

    def land(number, phase):
        copies, keeps, slots = built[number]
        copies[phase].wait_recv()
        keep, slot = keeps[phase], slots[phase]
        keep[...] = keep[...] + slot[...]

    def run(chunk, phase):
        number, layer, array, start, length, order = chunk
        copies, keeps, slots = built[number]
        if (layer, array) not in loaded:
            loaded.add((layer, array))
            spots = ((0, 1, 2, 3), (4,), (5,))[array] if layer == 0 else (array,)
            for spot in spots:
                loads[layer][spot].wait()
        if phase < 2:
            if order is not None:
                if phase:
                    land(number, 0)
                copies[phase].start()
        elif phase == 2:
            if order is not None:
                land(number, 1)

            @pl.when(here.outer)
            def _():
                copies[2].start()
                copies[4].start()

        elif phase == 3:

            @pl.when(here.inner)
            def _():
                land(number, 2)
                copies[3].start()

        elif phase == 4:

            @pl.when(here.inner)
            def _():
                land(number, 3)
                copies[4].start()

        else:
            copies[4].wait_recv()
            spot = pl.ds(place_of(layer, array, start), length)
            total[layer, spot, :] = (keeps[4][...] + slots[4][...])[0]

    def step(entry, phase):
        for chunk in entry:
            run(chunk, phase)

    second = [entry for _, entry in pairs[: len(quad_pairs(shares))]]
    first = [entry for _, entry in pairs[len(quad_pairs(shares)) :]]
    tails = [chunk for entry in second for chunk in entry if chunk[5] is not None]
    second = [[chunk for chunk in entry if chunk[5] is None] for entry in second]
    first[0] = first[0] + tails
    step(first[0], 0)
    step(first[1], 0)
    for entry in second:
        step(entry, 2)
    step(first[0], 1)
    for section, source in ((0, dx_ref), (1, final_ref)):

        @pl.when(core == section)
        def _():
            pltpu.make_async_copy(source.at[z], slices.at[z], local.at[0]).start()
            for by in (1, 2, 3):
                remote(
                    source.at[(z + by) % 4],
                    slices.at[z],
                    (z_send, z_recv),
                    (by - 1, by - 1),
                    here.others[by - 1],
                ).start()

    for entry in second:
        step(entry, 3)
    step(first[2], 0)
    step(first[1], 1)
    for entry in second:
        step(entry, 4)
    step(first[0], 2)
    step(first[2], 1)
    for entry in second:
        step(entry, 5)
    step(first[0], 3)
    step(first[1], 2)
    step(first[0], 4)
    step(first[1], 3)
    step(first[2], 2)
    step(first[1], 4)
    step(first[2], 3)
    step(first[2], 4)
    for entry in first:
        step(entry, 5)

    for copies, _, _ in built:
        for index in (0, 1, 4):
            if copies[index] is not None:
                copies[index].wait_send()
    for section, index in ((here.outer, 2), (here.inner, 3)):

        @pl.when(section)
        def _():
            for copies, _, _ in built:
                copies[index].wait_send()

    swaps = (swap_send, swap_recv)
    across = remote(total.at[1 - core], halves.at[core], swaps, (0, 0), here.partner)
    across.start()
    own = pltpu.make_async_copy(total.at[core], halves.at[core], local.at[1])
    own.start()
    own.wait()
    across.wait_send()
    remote(total.at[1 - core], halves.at[1 - core], swaps, (0, 0), here.partner).wait_recv()
    pltpu.make_async_copy(dx_ref.at[z], slices.at[z], local.at[0]).wait()
    for by in (1, 2, 3):
        copy = remote(
            dx_ref.at[z],
            slices.at[(z + 4 - by) % 4],
            (z_send, z_recv),
            (by - 1, by - 1),
            here.others[by - 1],
        )
        copy.wait_send()
        copy.wait_recv()


def scatter(shares, arrays, vec_zero, quads, vec_one, grad, final):
    micro, tokens, width = grad.shape
    lengths = (shares.half, shares.depth // 2, TAIL)
    chunks = sum(len(pair) for pair in chunk_pairs(shares) + quad_pairs(shares))
    rows = sum(lengths)
    anywhere = pl.BlockSpec(memory_space=pl.ANY)
    work = [pltpu.VMEM((2, 2, 4, length, width), LOW) for length in lengths]
    quad = pltpu.VMEM((4, (lengths[0] + lengths[1]) // 2, width), LOW)
    return pl.pallas_call(
        partial(scatter_kernel, shares),
        in_specs=[anywhere] * 10,
        out_specs=[anywhere] * 2,
        out_shape=[
            jax.ShapeDtypeStruct((2, rows, width), LOW),
            jax.ShapeDtypeStruct((micro, tokens, width), LOW),
        ],
        scratch_shapes=work
        + [quad, quad, work[2]]
        + [
            pltpu.VMEM((chunks, 2, 4, PIECE, width), LOW),
            pltpu.VMEM((chunks, 4, PIECE, width), LOW),
            pltpu.VMEM((chunks, 2, PIECE, width), LOW),
            pltpu.VMEM((chunks, 2, PIECE, width), LOW),
            pltpu.VMEM((chunks, 1, PIECE, width), LOW),
            pltpu.VMEM((2, rows, width), LOW),
            pltpu.SemaphoreType.DMA((2, 6)),
            pltpu.SemaphoreType.DMA((2,)),
            pltpu.SemaphoreType.DMA((1,)),
            pltpu.SemaphoreType.DMA((1,)),
            pltpu.SemaphoreType.DMA((3,)),
            pltpu.SemaphoreType.DMA((3,)),
            pltpu.SemaphoreType.DMA((chunks, 5)),
            pltpu.SemaphoreType.DMA((chunks, 5)),
        ],
        compiler_params=pltpu.CompilerParams(
            collective_id=1, has_side_effects=True, vmem_limit_bytes=VMEM_BYTES
        ),
    )(*arrays, vec_zero, *quads, vec_one, grad, final)


def update_kernel(shares, halves_ref, *refs):
    old, new, turned = refs[:9], refs[9:18], refs[18]
    offset = lax.axis_index((DP, SEQ)) * shares.columns
    half, per, width, depth = shares.half, shares.per, shares.width, shares.depth // 2
    is_inner = (offset >= 3 * width) & (offset < 4 * width)
    is_hidden = offset >= 4 * width

    @pl.when(is_inner)
    def _():
        for side in range(2):
            piece = halves_ref[side, :half, :].astype(jnp.float32)
            wide = per * half
            back = jnp.transpose(jnp.concatenate([piece[:, :wide], piece[:, wide:]], axis=0))
            for j in range(per):
                turned[(2 * j + side) * half : (2 * j + side + 1) * half, :] = back[
                    j * half : (j + 1) * half
                ]

    @pl.when(jnp.logical_not(is_inner))
    def _():
        pair = [halves_ref[side, :half, :].astype(jnp.float32) for side in range(2)]
        plain = jnp.concatenate(pair, axis=0)
        hidden = jnp.concatenate(
            [pair[side][j * depth :][:depth] for j in range(shares.groups) for side in range(2)],
            axis=0,
        )
        turned[...] = jnp.transpose(jnp.where(is_hidden, hidden, plain))

    def store(first, gradient, rate, decay):
        results = adam_update(*[ref[...] for ref in old[first : first + 3]], gradient, rate, decay)
        for ref, result in zip(new[first : first + 3], results):
            ref[...] = result

    store(0, turned[...], rate_matrix, decay_matrix)
    down = [halves_ref[side, half : half + depth, :] for side in range(2)]
    store(3, jnp.concatenate(down, axis=0).astype(jnp.float32), rate_matrix, decay_matrix)
    tails = [halves_ref[side, half + depth :, :].astype(jnp.float32) for side in range(2)]
    store(6, (tails[0] + tails[1])[0:1, : shares.vector_len], rate_vector, 0.0)


def update(shares, halves, old):
    return pl.pallas_call(
        partial(update_kernel, shares),
        out_shape=[jax.ShapeDtypeStruct(piece.shape, jnp.float32) for piece in old],
        scratch_shapes=[pltpu.VMEM((shares.width, shares.columns), jnp.float32)],
        compiler_params=pltpu.CompilerParams(vmem_limit_bytes=VMEM_BYTES),
    )(halves, *old)


ROWS = 256
COLS = 384
STRIP = 32


def whole(shape):
    return pl.BlockSpec(shape, lambda i: (0,) * len(shape))


def row_block(width):
    return pl.BlockSpec((ROWS, width), lambda i: (i, 0))


def col_block(tokens):
    return pl.BlockSpec((tokens, COLS), lambda i: (0, i))


def at_block(shape, *index):
    return pl.BlockSpec(shape, lambda i: index)


def params_of(flops, moved, transcendentals=0):
    return {
        "compiler_params": pltpu.CompilerParams(vmem_limit_bytes=DENSE_BYTES),
        "cost_estimate": pl.CostEstimate(
            flops=flops, bytes_accessed=moved, transcendentals=transcendentals
        ),
    }


def strips(length=ROWS, strip=STRIP):
    return [slice(first, first + strip) for first in range(0, length, strip)]


def eights(values):
    rows, width = values.shape
    return jnp.sum(values.reshape(rows // 8, 8, width), axis=0)


def features_kernel(shares, random_ref, segment_ref, global_ref, query_ref, key_ref, turned_ref):
    core = lax.axis_index(SECTION)
    place = lax.axis_index(SEQ)
    blocks = random_ref.shape[1]
    width = key_ref.shape[1]
    heads = query_ref.shape[0]
    per_half = heads // shares.per
    picks = random_ref.shape[2] // (2 * heads)
    tokens = key_ref.shape[0]
    lane = lax.broadcasted_iota(jnp.int32, (blocks, width), 1)
    row = lax.broadcasted_iota(jnp.int32, (blocks, width), 0)
    key = jnp.where(lane < blocks, lane, lane - blocks)
    chosen = random_ref[place]
    named = global_ref[place]
    always = (jnp.abs(row - key) <= 1).astype(jnp.int32)
    is_global = jnp.zeros((blocks, width), jnp.int32)
    for index in range(named.shape[1]):
        spot = named[:, index : index + 1]
        always = always + (key == spot).astype(jnp.int32)
        is_global = is_global + (row == spot).astype(jnp.int32)
    line = segment_ref[place].astype(jnp.float32)
    column = jnp.transpose(jnp.broadcast_to(line, (8, tokens)))[:, 0:1]
    token_lane = lax.broadcasted_iota(jnp.int32, (tokens, width), 1)
    same = column == (token_lane - 2 * blocks).astype(jnp.float32)
    in_segment = (token_lane >= 2 * blocks) & (token_lane < 2 * blocks + 3)
    segment_side = jnp.where(in_segment & same, 1.0, 0.0)
    for head in range(heads):
        count = always
        for pick in range(picks):
            at = [
                (2 * per_half * (head // per_half) + per_half * side + head % per_half) * picks
                + pick
                for side in range(2)
            ]
            spot = jnp.where(core == 0, chosen[:, at[0] : at[0] + 1], chosen[:, at[1] : at[1] + 1])
            count = count + (key == spot).astype(jnp.int32)
        count = jnp.where(is_global > 0, 1, count)
        high = jnp.where(count == 0, masked, 0.0)
        low = jnp.zeros_like(high)
        for times in (2, 3):
            high = jnp.where(count == times, LOG_HIGH[times - 1], high)
            low = jnp.where(count == times, LOG_LOW[times - 1], low)
        table = jnp.where(lane < blocks, high, jnp.where(lane < 2 * blocks, low, 0.0))
        for block in range(blocks):
            rows = slice(block * BLOCK, (block + 1) * BLOCK)
            query_ref[head, rows, :] = (table[block : block + 1] + segment_side[rows]).astype(LOW)
    token_block = lax.shift_right_logical(
        lax.broadcasted_iota(jnp.int32, (tokens, width), 0), BLOCK.bit_length() - 1
    )
    here = (token_block == token_lane) | (token_block == token_lane - blocks)
    side = jnp.where(here & (token_lane < 2 * blocks), 1.0, 0.0)
    side = jnp.where(in_segment & jnp.logical_not(same), masked, side)
    ones = (token_lane >= 2 * blocks + 3) & (token_lane < 2 * blocks + 6)
    side = jnp.where(ones, 1.0, side)
    key_ref[...] = side.astype(LOW)
    turned_ref[...] = jnp.transpose(side).astype(LOW)


def key_features(shares, random_ids, segment_ids, global_ids):
    micro, _, blocks, head_count, picks = random_ids.shape
    tokens = segment_ids.shape[2]
    width = -(-(2 * blocks + 6) // 128) * 128
    return pl.pallas_call(
        partial(features_kernel, shares),
        out_shape=[
            jax.ShapeDtypeStruct((head_count // 2, tokens, width), LOW),
            jax.ShapeDtypeStruct((tokens, width), LOW),
            jax.ShapeDtypeStruct((width, tokens), LOW),
        ],
        **params_of(0, head_count * tokens * width),
    )(random_ids.reshape(micro, blocks, head_count * picks), segment_ids, global_ids)


def project_kernel(joins, *refs):
    if joins:
        (middle_ref, part_ref, recv_ref, bias_down_ref), refs = refs[:4], refs[4:]
    else:
        hidden_ref, refs = refs[0], refs[1:]
    (gain_ref, shift_ref, weight_ref, bias_ref), refs = refs[:4], refs[4:]
    if joins:
        hidden_ref, refs = refs[0], refs[1:]
    normed_ref, out_ref = refs
    for rows in strips():
        if joins:
            part = part_ref[rows, :] + recv_ref[rows, :].astype(jnp.float32)
            low = (middle_ref[rows, :] + part + bias_down_ref[...]).astype(LOW)
            hidden_ref[rows, :] = low
        else:
            low = hidden_ref[rows, :]
        unit, _ = normalized(low.astype(jnp.float32))
        normed_ref[rows, :] = (unit * gain_ref[...] + shift_ref[...]).astype(LOW)
    for first in range(0, out_ref.shape[1], COLS):
        cols = slice(first, first + COLS)
        product = dot_rows(normed_ref[...], weight_ref[cols, :])
        out_ref[:, cols] = (product + bias_ref[:, cols]).astype(LOW)


def project(before, gain, shift, rows, bias):
    joins = len(before) > 1
    tokens, width = before[0].shape
    out_width = bias.shape[1]
    small = whole((1, width))
    ins = [row_block(width)] * 3 + [small] if joins else [row_block(width)]
    outs = [row_block(width)] * (2 if joins else 1)
    low = jax.ShapeDtypeStruct((tokens, width), LOW)
    return pl.pallas_call(
        partial(project_kernel, joins),
        grid=(tokens // ROWS,),
        in_specs=ins + [small, small, whole((out_width, width)), whole((1, out_width))],
        out_specs=outs + [row_block(out_width)],
        out_shape=[low] * len(outs) + [jax.ShapeDtypeStruct((tokens, out_width), LOW)],
        **params_of(2 * tokens * width * out_width, tokens * width * 16),
    )(*before, gain, shift, rows, bias)


def out_halves(packed_ref, half):
    wide = packed_ref.shape[1] // 2
    return [
        jnp.concatenate([packed_ref[rows, :wide], packed_ref[rows, wide:]], axis=0)
        for rows in (slice(0, half), slice(half, 2 * half))
    ]


def branch_kernel(half, attended_ref, packed_ref, branch_ref, low_ref):
    wide = attended_ref.shape[1]
    for index, weights in enumerate(out_halves(packed_ref, half)):
        cols = slice(index * wide, (index + 1) * wide)
        product = dot_rows(attended_ref[...], weights)
        branch_ref[:, cols] = product
        low_ref[:, cols] = product.astype(LOW)


def branch_out(shares, attended, rows):
    tokens, wide = attended.shape
    width = rows.shape[1]
    return pl.pallas_call(
        partial(branch_kernel, shares.half),
        grid=(tokens // ROWS,),
        in_specs=[row_block(wide), at_block((COLS, width), 3, 0)],
        out_specs=[row_block(width)] * 2,
        out_shape=[
            jax.ShapeDtypeStruct((tokens, width), jnp.float32),
            jax.ShapeDtypeStruct((tokens, width), LOW),
        ],
        **params_of(2 * tokens * width * wide, tokens * width * 8),
    )(attended, rows)


def gelu_parts(value):
    below = 1.0 + (0.3275911 * 0.5**0.5) * jnp.abs(value)
    rough = pl.reciprocal(below, approx=True)
    t = rough * (2.0 - below * rough)
    bell = jnp.exp((-0.5 * value) * value)
    poly = 0.5 * 1.061405429
    for coefficient in (-1.453152027, 1.421413741, -0.284496736, 0.254829592):
        poly = poly * t + 0.5 * coefficient
    tail = poly * (t * bell)
    cdf = jnp.where(value > 0, 1.0 - tail, tail)
    return value * cdf, cdf + value * (bell * (0.5 / math.pi) ** 0.5)


def expand_kernel(
    hidden_ref,
    branch_ref,
    recv_ref,
    bias_out_ref,
    gain_ref,
    shift_ref,
    up_ref,
    down_ref,
    bias_up_ref,
    middle_ref,
    normed_ref,
    slope_ref,
    active_ref,
    part_ref,
    low_ref,
    held,
):
    for rows in strips():
        branch = branch_ref[rows, :] + recv_ref[rows, :].astype(jnp.float32)
        middle = hidden_ref[rows, :].astype(jnp.float32) + (branch + bias_out_ref[...])
        middle_ref[rows, :] = middle
        unit, _ = normalized(middle)
        normed_ref[rows, :] = (unit * gain_ref[...] + shift_ref[...]).astype(LOW)
    for index in range(up_ref.shape[0] // COLS):
        cols = slice(index * COLS, (index + 1) * COLS)
        held[index] = dot_rows(normed_ref[...], up_ref[cols, :])
        for rows in strips():
            active, slope = gelu_parts(held[index, rows, :] + bias_up_ref[:, cols])
            active_ref[rows, cols] = active.astype(LOW)
            slope_ref[rows, cols] = slope
    part = dot_plain(active_ref[...], down_ref[...])
    part_ref[...] = part
    low_ref[...] = part.astype(LOW)


def expand(hidden, branch, recv, bias_out, gain, shift, rows, down, bias_up):
    tokens, width = hidden.shape
    inner = down.shape[0]
    small = whole((1, width))
    return pl.pallas_call(
        expand_kernel,
        grid=(tokens // ROWS,),
        in_specs=[row_block(width)] * 3
        + [small, small, small, at_block((inner, width), 1, 0)]
        + [whole((inner, width)), whole((1, inner))],
        out_specs=[row_block(width), row_block(width), row_block(inner), row_block(inner)]
        + [row_block(width), row_block(width)],
        out_shape=[
            jax.ShapeDtypeStruct((tokens, width), jnp.float32),
            jax.ShapeDtypeStruct((tokens, width), LOW),
            jax.ShapeDtypeStruct((tokens, inner), jnp.float32),
            jax.ShapeDtypeStruct((tokens, inner), LOW),
            jax.ShapeDtypeStruct((tokens, width), jnp.float32),
            jax.ShapeDtypeStruct((tokens, width), LOW),
        ],
        scratch_shapes=[pltpu.VMEM((inner // COLS, ROWS, COLS), jnp.float32)],
        **params_of(4 * tokens * width * inner, tokens * width * 32, tokens * inner),
    )(hidden, branch, recv, bias_out, gain, shift, rows, down, bias_up)


def expand_back_kernel(
    grad_ref,
    slope_ref,
    up_ref,
    down_ref,
    part_ref,
    low_ref,
    grad_up_ref,
    bias_up_ref,
    bias_down_ref,
    sums_up,
    sums_down,
):
    step = pl.program_id(0)

    @pl.when(step == 0)
    def _():
        sums_up[...] = jnp.zeros_like(sums_up)
        sums_down[...] = jnp.zeros_like(sums_down)

    for index in range(down_ref.shape[0] // COLS):
        cols = slice(index * COLS, (index + 1) * COLS)
        grad_up = dot_rows(grad_ref[...], down_ref[cols, :]) * slope_ref[:, cols]
        grad_up_ref[:, cols] = grad_up.astype(LOW)
    part = dot_plain(grad_up_ref[...], up_ref[...])
    part_ref[...] = part
    low_ref[...] = part.astype(LOW)
    for rows in strips():
        sums_up[...] += eights(grad_up_ref[rows, :].astype(jnp.float32))
        sums_down[...] += eights(grad_ref[rows, :].astype(jnp.float32))

    @pl.when(step == pl.num_programs(0) - 1)
    def _():
        bias_up_ref[...] = jnp.sum(sums_up[...], axis=0, keepdims=True)
        bias_down_ref[...] = jnp.sum(sums_down[...], axis=0, keepdims=True)


def expand_back(grad, slope, rows, down):
    tokens, width = grad.shape
    inner = down.shape[0]
    return pl.pallas_call(
        expand_back_kernel,
        grid=(tokens // ROWS,),
        in_specs=[row_block(width), row_block(inner)]
        + [at_block((inner, width), 1, 0), whole((inner, width))],
        out_specs=[row_block(width), row_block(width), row_block(inner)]
        + [whole((1, inner)), whole((1, width))],
        out_shape=[
            jax.ShapeDtypeStruct((tokens, width), jnp.float32),
            jax.ShapeDtypeStruct((tokens, width), LOW),
            jax.ShapeDtypeStruct((tokens, inner), LOW),
            jax.ShapeDtypeStruct((1, inner), jnp.float32),
            jax.ShapeDtypeStruct((1, width), jnp.float32),
        ],
        scratch_shapes=[pltpu.VMEM((8, inner), jnp.float32), pltpu.VMEM((8, width), jnp.float32)],
        **params_of(4 * tokens * width * inner, tokens * width * 24),
    )(grad, slope, rows, down)


def token_products_kernel(count, *refs):
    lefts, rights, outs = refs[:count], refs[count : 2 * count], refs[2 * count :]
    for left, right, out in zip(lefts, rights, outs):
        for first in range(0, COLS, 128):
            cols = slice(first, first + 128)
            out[cols, :] = dot_tokens(left[:, cols], right[...]).astype(LOW)


def token_products(*pairs):
    lefts, rights = zip(*pairs)
    tokens, inner = lefts[0].shape
    width = rights[0].shape[1]
    count = len(pairs)
    return pl.pallas_call(
        partial(token_products_kernel, count),
        grid=(inner // COLS,),
        in_specs=[col_block(tokens)] * count + [whole((tokens, width))] * count,
        out_specs=[pl.BlockSpec((COLS, width), lambda i: (i, 0))] * count,
        out_shape=[jax.ShapeDtypeStruct((inner, width), LOW)] * count,
        **params_of(2 * count * tokens * width * inner, count * tokens * width * 8),
    )(*lefts, *rights)


def norm_back_rows(values_in, incoming, gain_vec):
    unit, scale = normalized(values_in)
    p = incoming * gain_vec
    mean_p = jnp.mean(p, axis=-1, keepdims=True)
    mean_pn = jnp.mean(p * unit, axis=-1, keepdims=True)
    return scale * (p - mean_p - unit * mean_pn), eights(incoming * unit), eights(incoming)


def branch_back_kernel(
    half,
    middle_ref,
    part_ref,
    recv_ref,
    grad_ref,
    attended_ref,
    gain_ref,
    packed_ref,
    grad_middle_ref,
    grad_attended_ref,
    out_grad_ref,
    gain_grad_ref,
    shift_grad_ref,
    bias_grad_ref,
    total,
    low,
    sums,
):
    step = pl.program_id(0)

    @pl.when(step == 0)
    def _():
        total[...] = jnp.zeros_like(total)
        sums[...] = jnp.zeros_like(sums)

    for rows in strips():
        incoming = part_ref[rows, :] + recv_ref[rows, :].astype(jnp.float32)
        change, for_gain, for_shift = norm_back_rows(middle_ref[rows, :], incoming, gain_ref[...])
        grad_middle = grad_ref[rows, :].astype(jnp.float32) + change
        grad_middle_ref[rows, :] = grad_middle
        rounded = grad_middle.astype(LOW)
        low[rows, :] = rounded
        sums[0] += for_gain
        sums[1] += for_shift
        sums[2] += eights(rounded.astype(jnp.float32))
    weights = out_halves(packed_ref, half)
    wide = weights[0].shape[0]
    attended = attended_ref[...]
    pieces = [low[:, :wide], low[:, wide:]]
    grad_attended_ref[...] = (
        dot_plain(pieces[0], weights[0]) + dot_plain(pieces[1], weights[1])
    ).astype(LOW)
    for index in range(2):
        total[index] += dot_tokens(pieces[index], attended)

    @pl.when(step == pl.num_programs(0) - 1)
    def _():
        for index in range(2):
            joined = jnp.concatenate([total[index, :half, :], total[index, half:, :]], axis=1)
            out_grad_ref[index * half : (index + 1) * half, :] = joined.astype(LOW)
        for index, ref in enumerate((gain_grad_ref, shift_grad_ref, bias_grad_ref)):
            ref[...] = jnp.sum(sums[index], axis=0, keepdims=True)


def branch_back(shares, middle, part, recv, grad, attended, gain, rows):
    tokens, width = middle.shape
    wide = attended.shape[1]
    small = whole((1, width))
    one = jax.ShapeDtypeStruct((1, width), jnp.float32)
    return pl.pallas_call(
        partial(branch_back_kernel, shares.half),
        grid=(tokens // ROWS,),
        in_specs=[row_block(width)] * 4 + [row_block(wide), small, at_block((COLS, width), 3, 0)],
        out_specs=[row_block(width), row_block(wide), whole((COLS, width)), small, small, small],
        out_shape=[
            jax.ShapeDtypeStruct((tokens, width), jnp.float32),
            jax.ShapeDtypeStruct((tokens, wide), LOW),
            jax.ShapeDtypeStruct((COLS, width), LOW),
            one,
            one,
            one,
        ],
        scratch_shapes=[
            pltpu.VMEM((2, width // 2, wide), jnp.float32),
            pltpu.VMEM((ROWS, width), LOW),
            pltpu.VMEM((3, 8, width), jnp.float32),
        ],
        **params_of(4 * tokens * width * wide, tokens * width * 20),
    )(middle, part, recv, grad, attended, gain, rows)


def project_back_kernel(grad_ref, weight_ref, part_ref, low_ref, bias_ref, sums):
    step = pl.program_id(0)

    @pl.when(step == 0)
    def _():
        sums[...] = jnp.zeros_like(sums)

    part = dot_plain(grad_ref[...], weight_ref[...])
    part_ref[...] = part
    low_ref[...] = part.astype(LOW)
    for rows in strips():
        sums[...] += eights(grad_ref[rows, :].astype(jnp.float32))

    @pl.when(step == pl.num_programs(0) - 1)
    def _():
        bias_ref[...] = jnp.sum(sums[...], axis=0, keepdims=True)


def project_back(grad_proj, rows):
    tokens, out_width = grad_proj.shape
    width = rows.shape[1]
    return pl.pallas_call(
        project_back_kernel,
        grid=(tokens // ROWS,),
        in_specs=[row_block(out_width), whole((out_width, width))],
        out_specs=[row_block(width), row_block(width), whole((1, out_width))],
        out_shape=[
            jax.ShapeDtypeStruct((tokens, width), jnp.float32),
            jax.ShapeDtypeStruct((tokens, width), LOW),
            jax.ShapeDtypeStruct((1, out_width), jnp.float32),
        ],
        scratch_shapes=[pltpu.VMEM((8, out_width), jnp.float32)],
        **params_of(2 * tokens * width * out_width, tokens * width * 12),
    )(grad_proj, rows)


def input_back_kernel(
    hidden_ref, part_ref, recv_ref, grad_ref, gain_ref, out_ref, gain_grad_ref, shift_grad_ref, sums
):
    step = pl.program_id(0)

    @pl.when(step == 0)
    def _():
        sums[...] = jnp.zeros_like(sums)

    for rows in strips():
        incoming = part_ref[rows, :] + recv_ref[rows, :].astype(jnp.float32)
        hidden = hidden_ref[rows, :].astype(jnp.float32)
        change, for_gain, for_shift = norm_back_rows(hidden, incoming, gain_ref[...])
        out_ref[rows, :] = (grad_ref[rows, :] + change).astype(LOW)
        sums[0] += for_gain
        sums[1] += for_shift

    @pl.when(step == pl.num_programs(0) - 1)
    def _():
        gain_grad_ref[...] = jnp.sum(sums[0], axis=0, keepdims=True)
        shift_grad_ref[...] = jnp.sum(sums[1], axis=0, keepdims=True)


def input_back(hidden, part, recv, grad_middle, gain):
    tokens, width = hidden.shape
    small = whole((1, width))
    one = jax.ShapeDtypeStruct((1, width), jnp.float32)
    return pl.pallas_call(
        input_back_kernel,
        grid=(tokens // ROWS,),
        in_specs=[row_block(width)] * 4 + [small],
        out_specs=[row_block(width), small, small],
        out_shape=[jax.ShapeDtypeStruct((tokens, width), LOW), one, one],
        scratch_shapes=[pltpu.VMEM((2, 8, width), jnp.float32)],
        **params_of(0, tokens * width * 12),
    )(hidden, part, recv, grad_middle, gain)


def attend_kernel(q_ref, k_ref, v_ref, qa_ref, kt_ref, out_ref, lse_ref, keys, held, low):
    tokens, pair = q_ref.shape
    left = lax.broadcasted_iota(jnp.int32, (CHUNK, pair), 1) < pair // 2
    keys[:pair, :] = jnp.transpose(k_ref[...].astype(jnp.float32)).astype(LOW)
    keys[pair:, :] = kt_ref[...]
    for index in range(tokens // CHUNK):
        rows = slice(index * CHUNK, (index + 1) * CHUNK)
        queries = q_ref[rows, :] * 0.125
        outs, tops = [], []
        for head in range(2):
            slot = (2 * index + head) % held.shape[0]
            mine = left if head == 0 else jnp.logical_not(left)
            side = jnp.where(mine, queries, jnp.zeros_like(queries))
            lhs = jnp.concatenate([side, qa_ref[head, rows, :]], axis=1)
            held[slot] = dot_plain(lhs, keys[...])
            levels, shares = [], []
            for strip in strips(CHUNK):
                scores = held[slot, strip, :]
                top = jnp.max(scores, axis=1, keepdims=True)
                weight = jnp.exp(scores - top)
                total = jnp.sum(weight, axis=1, keepdims=True)
                low[slot, strip, :] = weight.astype(LOW)
                levels.append(top + jnp.log(total))
                shares.append(1.0 / total)
            product = dot_plain(low[slot], v_ref[...])
            outs.append(product * jnp.concatenate(shares, axis=0))
            tops.append(jnp.concatenate(levels, axis=0))
        out_ref[rows, :] = jnp.where(left, outs[0], outs[1]).astype(LOW)
        lse_ref[rows, :] = jnp.where(left, tops[0], tops[1])


def attend(projected, query_side, key_side, turned):
    tokens = projected.shape[0]
    width = projected.shape[1] // 3
    pairs = width // 128
    features = key_side.shape[1]
    return pl.pallas_call(
        attend_kernel,
        grid=(pairs,),
        in_specs=[
            pl.BlockSpec((tokens, 128), lambda p: (0, p)),
            pl.BlockSpec((tokens, 128), lambda p: (0, pairs + p)),
            pl.BlockSpec((tokens, 128), lambda p: (0, 2 * pairs + p)),
            pl.BlockSpec((2, tokens, features), lambda p: (p, 0, 0)),
            whole((features, tokens)),
        ],
        out_specs=[
            pl.BlockSpec((tokens, 128), lambda p: (0, p)),
            pl.BlockSpec((tokens, 128), lambda p: (0, p)),
        ],
        out_shape=[
            jax.ShapeDtypeStruct((tokens, width), LOW),
            jax.ShapeDtypeStruct((tokens, width), jnp.float32),
        ],
        scratch_shapes=[
            pltpu.VMEM((128 + features, tokens), LOW),
            pltpu.VMEM((4, CHUNK, tokens), jnp.float32),
            pltpu.VMEM((4, CHUNK, tokens), LOW),
        ],
        **params_of(
            16 * pairs * tokens * tokens * 128, tokens * width * 16, 2 * pairs * tokens * tokens
        ),
    )(projected, projected, projected, query_side, turned)


def three_terms(values):
    high = values.astype(LOW).astype(jnp.float32)
    rest = values - high
    middle = rest.astype(LOW).astype(jnp.float32)
    return high, middle, rest - middle


def attend_back_kernel(
    q_ref,
    k_ref,
    v_ref,
    do_ref,
    o_ref,
    lse_ref,
    qa_ref,
    ka_ref,
    grad_ref,
    held,
    probs,
    changes,
    query_sides,
    grad_sides,
):
    tokens, pair = q_ref.shape
    features = ka_ref.shape[1]
    pairs = pl.num_programs(0)
    place = pl.program_id(0)
    first = 2 * (tokens // BLOCK) + 3
    half = pair // 2
    left = lax.broadcasted_iota(jnp.int32, (CHUNK, pair), 1) < half
    lane = lax.broadcasted_iota(jnp.int32, (CHUNK, features), 1)
    lane_pair = lax.broadcasted_iota(jnp.int32, (CHUNK, pair), 1)
    keys = jnp.concatenate([k_ref[...], ka_ref[...]], axis=1)
    turned = jnp.transpose(k_ref[...].astype(jnp.float32)).astype(LOW)
    ones = (lax.broadcasted_iota(jnp.int32, (tokens, pair), 1) < 3).astype(jnp.float32).astype(LOW)
    values = jnp.concatenate([v_ref[...], ones], axis=1)
    parts, key_grads, value_grads = [], [], []
    for head in range(2):
        mine = left if head == 0 else jnp.logical_not(left)
        for index in range(tokens // CHUNK):
            rows = slice(index * CHUNK, (index + 1) * CHUNK)
            slot = index % 2
            queries = q_ref[rows, :] * 0.125
            grads = do_ref[rows, :]
            product = grads.astype(jnp.float32) * o_ref[rows, :].astype(jnp.float32)
            level = lse_ref[rows, head * half : head * half + 1]
            inner = jnp.sum(jnp.where(mine, product, 0.0), axis=1, keepdims=True)
            side = qa_ref[head, rows, :].astype(jnp.float32)
            for spot, term in enumerate(three_terms(level)):
                side = jnp.where(lane == first + spot, -term, side)
            query_side = jnp.where(mine, queries, jnp.zeros_like(queries))
            grad_side = jnp.where(mine, grads, jnp.zeros_like(grads))
            query_sides[head, rows, :] = query_side
            grad_sides[head, rows, :] = grad_side
            tail = jnp.zeros((CHUNK, pair), jnp.float32)
            for spot, term in enumerate(three_terms(inner)):
                tail = jnp.where(lane_pair == spot, -term, tail)
            held[slot, 0] = dot_rows(
                keys, jnp.concatenate([query_side, side.astype(LOW)], axis=1)
            )
            held[slot, 1] = dot_rows(
                values, jnp.concatenate([grad_side, tail.astype(LOW)], axis=1)
            )
            for strip in strips(tokens, 128):
                prob = jnp.exp(held[slot, 0, strip, :])
                probs[head, strip, rows] = prob.astype(LOW)
                changes[head, strip, rows] = (prob * held[slot, 1, strip, :]).astype(LOW)
        value_grads.append(dot_plain(probs[head], grad_sides[head]))
        key_grads.append(dot_plain(changes[head], query_sides[head]))
        parts.append(dot_plain(turned, changes[head]))
    joined = jnp.concatenate([parts[0][:half], parts[1][half:]], axis=0)
    column = [pl.ds(pl.multiple_of((by * pairs + place) * 128, 128), 128) for by in range(3)]
    grad_ref[:, column[0]] = (jnp.transpose(joined) * 0.125).astype(LOW)
    grad_ref[:, column[1]] = (key_grads[0] + key_grads[1]).astype(LOW)
    grad_ref[:, column[2]] = (value_grads[0] + value_grads[1]).astype(LOW)


def attend_back(projected, grad_attended, attended, levels, query_side, key_side):
    tokens, width = attended.shape
    pairs = width // 128
    features = key_side.shape[1]
    by_pair = pl.BlockSpec((tokens, 128), lambda p: (0, p))
    return pl.pallas_call(
        attend_back_kernel,
        grid=(pairs,),
        in_specs=[
            by_pair,
            pl.BlockSpec((tokens, 128), lambda p: (0, pairs + p)),
            pl.BlockSpec((tokens, 128), lambda p: (0, 2 * pairs + p)),
            by_pair,
            by_pair,
            by_pair,
            pl.BlockSpec((2, tokens, features), lambda p: (p, 0, 0)),
            whole((tokens, features)),
        ],
        out_specs=whole((tokens, 3 * width)),
        out_shape=jax.ShapeDtypeStruct((tokens, 3 * width), LOW),
        scratch_shapes=[
            pltpu.VMEM((2, 2, tokens, CHUNK), jnp.float32),
            pltpu.VMEM((2, tokens, tokens), LOW),
            pltpu.VMEM((2, tokens, tokens), LOW),
            pltpu.VMEM((2, tokens, 128), LOW),
            pltpu.VMEM((2, tokens, 128), LOW),
        ],
        **params_of(
            40 * pairs * tokens * tokens * 128, tokens * width * 24, 2 * pairs * tokens * tokens
        ),
    )(projected, projected, projected, grad_attended, attended, levels, query_side, key_side)


def window_forward(shares, before, weights, biases, features, beside):
    rows, down = weights
    gain_one, shift_one, bias_query, bias_value, bias_out = biases[:5]
    gain_two, shift_two, _, bias_up = biases[5:]
    bias = jnp.concatenate([bias_query, jnp.zeros_like(bias_query), bias_value], axis=1)
    results = project(before, gain_one, shift_one, rows, bias)
    hidden = before[0] if len(before) == 1 else results[0]
    normed, projected = results[-2:]
    projected = beside.tie(projected)
    attended, levels = beside.tie(tuple(attend(projected, *features)))
    branch, low = branch_out(shares, attended, rows)
    expanded = expand(
        hidden, branch, swap(low), bias_out, gain_two, shift_two, rows, down, bias_up
    )
    middle, normed_two, slope, active, part, low = beside.tie(tuple(expanded))
    stored = (hidden, normed, projected, attended, levels, middle, normed_two, slope, active)
    return (middle, part, swap(low), biases[7]), stored


def window_backward(shares, stored, grad, weights, biases, features, beside):
    hidden, normed, projected, attended, levels, middle, normed_two, slope, active = stored
    rows, down = weights
    part, low, grad_up, bias_up, bias_down = beside.tie(
        tuple(expand_back(grad, slope, rows, down))
    )
    arrived = swap(low)
    down_grad, up_grad = token_products((active, grad), (grad_up, normed_two))
    grad_middle, grad_attended, out_grad, gain_two, shift_two, bias_out = branch_back(
        shares, middle, part, arrived, grad, attended, biases[5], rows
    )
    grad_attended = beside.tie(grad_attended)
    grad_proj = attend_back(projected, grad_attended, attended, levels, *features[:2])
    grad_proj = beside.tie(grad_proj)
    part, low, summed = project_back(grad_proj, rows)
    arrived = swap(low)
    (proj_grad,) = token_products((grad_proj, normed))
    grad, gain_one, shift_one = input_back(hidden, part, arrived, grad_middle, biases[0])
    width = attended.shape[1]
    vector_grads = (gain_one, shift_one, summed[:, :width], summed[:, 2 * width :], bias_out)
    vector_grads += (gain_two, shift_two, bias_down, bias_up)
    vector_grads = [piece[0] for piece in vector_grads]
    return grad, (proj_grad, out_grad, up_grad, down_grad), vector_grads


def window_shards(
    block_input,
    cotangent,
    random_ids,
    segment_ids,
    global_ids,
    w_rows,
    w_rows_first,
    w_rows_second,
    w_down,
    w_down_first,
    w_down_second,
    vectors,
    vectors_first,
    vectors_second,
):
    core = lax.axis_index(SECTION)
    micro, _, tokens, width = block_input.shape
    _, _, columns = w_rows.shape
    shares = Shares(width, columns, w_down.shape[1], vectors.shape[1])
    prepared = prepare(shares, w_rows[0], w_down[0], vectors)
    features = key_features(shares, random_ids, segment_ids, global_ids)
    gathered_zero, gathered_one, hidden, grad = gather(shares, prepared, block_input, cotangent)

    beside = Beside(spread_quads(shares, gathered_one[:2]))
    params = [shares.unpack(gathered_zero, core)]
    before = (hidden.reshape(-1, width),)
    before, stored_zero = window_forward(shares, before, *params[0], features, beside)
    params.append(shares.unpack((*beside.flying, gathered_one[2]), core))
    after, stored_one = window_forward(shares, before, *params[1], features, Beside())
    final = (after[0] + (after[1] + after[2].astype(jnp.float32) + after[3])).astype(LOW)

    grad = grad.reshape(-1, width)
    grad, *grads_one = window_backward(shares, stored_one, grad, *params[1], features, Beside())
    *arrays_one, vec_one = shares.by_shard(*grads_one, core)
    beside = Beside(sum_quads(shares, arrays_one))
    grad, *grads_zero = window_backward(shares, stored_zero, grad, *params[0], features, beside)
    *arrays_zero, vec_zero = shares.by_shard(*grads_zero, core)
    grad, final = [piece.reshape(micro, tokens, width) for piece in (grad, final)]
    halves, slices = scatter(shares, arrays_zero, vec_zero, beside.flying, vec_one, grad, final)
    section_result = slices.astype(jnp.float32)[None, :, None]
    old = [
        w_rows[0],
        w_rows_first[0],
        w_rows_second[0],
        w_down[0],
        w_down_first[0],
        w_down_second[0],
        vectors,
        vectors_first,
        vectors_second,
    ]
    new = update(shares, halves, old)
    return (section_result, *[piece[None] for piece in new[:6]], *new[6:])


def one_window_each(mesh, block_input, w_rows, w_down, vectors):
    micro, windows, length, width = block_input.shape
    shards = mesh.shape[DP] * mesh.shape[SEQ]
    columns, depth = w_rows.shape[2] // shards, w_down.shape[1] // shards
    head_dim = width // HEADS
    tokens = length // mesh.shape[SEQ]
    return (
        mesh.shape[SECTION] == 2
        and mesh.shape[SEQ] == micro
        and mesh.shape[DP] == windows
        and tokens % (2 * BLOCK) == 0
        and length % CHUNK == 0
        and head_dim == 64
        and width % columns == 0
        and columns % (2 * head_dim) == 0
        and columns % depth == 0
        and width // columns * (columns // 2) % 128 == 0
        and depth % 32 == 0
        and vectors.shape[1] // shards <= width
        and mesh.shape[DP] == 4
        and micro == 4
        and width == 2 * columns == 2 * COLS
        and w_down.shape[1] == 4 * width
        and (columns // 2) % (2 * PIECE) == 0
        and (depth // 2) % (2 * PIECE) == 0
        and length % (4 * ROWS) == 0
    )


def solution(mesh):
    in_specs = (
        P(None, DP, SEQ, None),
        P(None, DP, SEQ, None),
        P(None, DP, None, None, None),
        P(None, DP, None),
        P(None, DP, None),
        P(SECTION, None, (DP, SEQ)),
        P(SECTION, None, (DP, SEQ)),
        P(SECTION, None, (DP, SEQ)),
        P(SECTION, (DP, SEQ), None),
        P(SECTION, (DP, SEQ), None),
        P(SECTION, (DP, SEQ), None),
        P(SECTION, (DP, SEQ)),
        P(SECTION, (DP, SEQ)),
        P(SECTION, (DP, SEQ)),
    )
    out_specs = (
        P(SECTION, None, DP, SEQ, None),
        P(SECTION, None, (DP, SEQ)),
        P(SECTION, None, (DP, SEQ)),
        P(SECTION, None, (DP, SEQ)),
        P(SECTION, (DP, SEQ), None),
        P(SECTION, (DP, SEQ), None),
        P(SECTION, (DP, SEQ), None),
        P(SECTION, (DP, SEQ)),
        P(SECTION, (DP, SEQ)),
        P(SECTION, (DP, SEQ)),
    )

    def step(*arrays):
        chosen = general_shards
        if one_window_each(mesh, arrays[0], arrays[5], arrays[8], arrays[11]):
            chosen = window_shards
        return jax.shard_map(
            chosen, mesh=mesh, in_specs=in_specs, out_specs=out_specs, check_vma=False
        )(*arrays)

    return step
```

```python
import math
from functools import partial

import jax
import jax.numpy as jnp
import ml_dtypes
import numpy as np
from jax import lax
from jax.experimental import pallas as pl
from jax.experimental.pallas import tpu as pltpu
from jax.sharding import PartitionSpec as P

SECTION, DP, SEQ = "section", "dp", "seq"
HEADS = 12
BLOCK = 64
STEP = 5


epsilon = 1e-05
masked = -1e30
rate_matrix = 0.02
rate_vector = 0.2
decay_matrix = 0.01


def with_halo(x, sides, width):
    for axis, dim in sides:
        devices, length = (lax.axis_size(axis), x.shape[dim])
        up = [(i, (i + 1) % devices) for i in range(devices - 1)]
        down = [(j, i) for i, j in up]
        last = lax.slice_in_dim(x, length - width, length, axis=dim)
        initial = lax.slice_in_dim(x, 0, width, axis=dim)
        before = lax.ppermute(last, axis, up)
        after = lax.ppermute(initial, axis, down)
        x = jnp.concatenate([before, x, after], axis=dim)
    return x


def merged(value, axis, join):
    pieces = jax.tree.map(lambda part: lax.all_gather(part, axis), value)
    head = jax.tree.map(lambda part: part[0], pieces)
    tail = jax.tree.map(lambda part: part[1:], pieces)
    subtotal, _ = lax.scan(lambda subtotal, share: (join(subtotal, share), None), head, tail)
    return subtotal


def from_behind(x, axis, by):
    devices = lax.axis_size(axis)
    pairs = [(i, i + by) for i in range(devices) if 0 <= i + by < devices]
    return lax.ppermute(x, axis, pairs)


def partner(value, axis, bit):
    mask = 2**bit
    pairs = [(source, source ^ mask) for source in range(lax.axis_size(axis))]
    return lax.ppermute(value, axis, pairs)


def mixed_sum(form, left, right):
    return jnp.einsum(form, left, right, preferred_element_type=jnp.float32)


def exact_two(form, left, right):
    return jnp.einsum(
        form, left, right, precision=lax.Precision.HIGHEST, preferred_element_type=jnp.float32
    )


def norm_rows(values_in, gain_vec, shift_vec):
    row_mean = jnp.mean(values_in, axis=-1, keepdims=True)
    centred = values_in - row_mean
    spread = jnp.mean(centred * centred, axis=-1, keepdims=True)
    return centred * lax.rsqrt(spread + epsilon) * gain_vec + shift_vec


def split_vectors(vector_weights, model_width):
    pieces = [
        vector_weights[piece_index * model_width : (piece_index + 1) * model_width]
        for piece_index in range(8)
    ]
    return pieces + [vector_weights[8 * model_width :]]


def route_tables(random_rows, segments, global_rows, seq_place, groups):
    windows, blocks, head_count, pick_count = random_rows.shape
    blocks_dev = blocks // groups
    request_count = blocks_dev * head_count * pick_count
    capacity = -(-request_count // groups)
    requests = random_rows.reshape(windows, groups, request_count)
    owners = requests // blocks_dev
    inside = requests % blocks_dev
    head_of = jnp.arange(request_count) // pick_count % head_count
    is_mine = owners == seq_place
    slot_index = jnp.cumsum(is_mine.astype(jnp.int32), axis=2) - 1
    slot_hot = ((slot_index[..., None] == jnp.arange(capacity)) & is_mine[..., None]).astype(
        jnp.float32
    )
    inside_hot = (inside[..., None] == jnp.arange(blocks_dev)).astype(jnp.float32)
    head_hot = (head_of[:, None] == jnp.arange(head_count)).astype(jnp.float32)
    sender = jnp.einsum(
        "wqsc,wqsb,sh->wqcbh", slot_hot, inside_hot, head_hot, precision=lax.Precision.HIGHEST
    )
    my_owners = lax.dynamic_index_in_dim(owners, seq_place, axis=1, keepdims=False)
    earlier = jnp.arange(request_count)[None, :] < jnp.arange(request_count)[:, None]
    same_owner = my_owners[:, :, None] == my_owners[:, None, :]
    rank_index = jnp.sum((same_owner & earlier[None]).astype(jnp.int32), axis=2)
    picker = (
        (my_owners[..., None, None] == jnp.arange(groups)[:, None])
        & (rank_index[..., None, None] == jnp.arange(capacity)[None, :])
    ).astype(jnp.float32)
    first_block = seq_place * blocks_dev
    owned_hot = (global_rows[:, :, None] == first_block + jnp.arange(blocks_dev)).astype(
        jnp.float32
    )
    length = segments.shape[1]
    block_len = length // blocks
    seg_blocks = segments.reshape(windows, blocks, block_len)
    seg_pad = jnp.pad(seg_blocks, ((0, 0), (1, 1), (0, 0)), constant_values=-1)
    near_segs = lax.dynamic_slice_in_dim(seg_pad, first_block, blocks_dev + 2, axis=1)
    slide_seg = jnp.concatenate([near_segs[:, :-2], near_segs[:, 1:-1], near_segs[:, 2:]], axis=2)
    query_seg = near_segs[:, 1:-1]
    rows_index = jnp.arange(windows)
    global_seg = seg_blocks[rows_index[:, None], global_rows].reshape(windows, -1)
    chosen = lax.dynamic_slice_in_dim(random_rows, first_block, blocks_dev, axis=1)
    far_seg = seg_blocks[rows_index[:, None, None, None], chosen].reshape(
        windows, blocks_dev, head_count, -1
    )
    key_seg = jnp.concatenate(
        [
            jnp.broadcast_to(
                slide_seg[:, :, None, :], (windows, blocks_dev, head_count, slide_seg.shape[2])
            ),
            jnp.broadcast_to(
                global_seg[:, None, None, :], (windows, blocks_dev, head_count, global_seg.shape[1])
            ),
            far_seg,
        ],
        axis=3,
    )
    key_mask = query_seg[:, :, None, :, None] == key_seg[:, :, :, None, :]
    local_seg = query_seg.reshape(windows, -1)
    full_mask = global_seg[:, None, :, None] == local_seg[:, None, None, :]
    return (sender, picker, owned_hot, key_mask, full_mask)


def fetch_blocks(paired, queries, sender, picker, owned_hot):
    windows, tokens, head_count, doubled = paired.shape
    head_dim = queries.shape[-1]
    blocks_dev = tokens // BLOCK
    flattened = paired.reshape(windows, tokens, head_count * doubled)
    padded = with_halo(flattened, ((SEQ, 1),), BLOCK)
    framed = padded.reshape(windows, blocks_dev + 2, BLOCK, head_count, doubled)
    sliding = jnp.concatenate([framed[:, :-2], framed[:, 1:-1], framed[:, 2:]], axis=2)
    local_blocks = paired.reshape(windows, blocks_dev, BLOCK, head_count, doubled)
    owned_low = owned_hot.astype(jnp.bfloat16)
    offered = mixed_sum("wgb,wbthe->wgthe", owned_low, local_blocks)
    offered_queries = mixed_sum("wgb,wbqhd->wgqhd", owned_low, queries)
    global_kv, global_queries = (
        lax.psum(offered.astype(jnp.bfloat16), SEQ).astype(jnp.float32),
        lax.psum(offered_queries.astype(jnp.bfloat16), SEQ).astype(jnp.float32),
    )
    global_kv = global_kv.astype(jnp.bfloat16).reshape(windows, -1, head_count, doubled)
    global_queries = global_queries.astype(jnp.bfloat16).reshape(windows, -1, head_count, head_dim)
    outgoing = mixed_sum("wqcbh,wbthe->qwcte", sender.astype(jnp.bfloat16), local_blocks).astype(
        jnp.bfloat16
    )
    incoming = lax.all_to_all(outgoing, SEQ, split_axis=0, concat_axis=0, tiled=True)
    distant = mixed_sum("wspc,pwcte->wste", picker.astype(jnp.bfloat16), incoming).astype(
        jnp.bfloat16
    )
    pick_count = picker.shape[1] // (blocks_dev * head_count)
    distant = distant.reshape(windows, blocks_dev, head_count, pick_count, BLOCK, doubled)
    return (sliding, global_kv, distant, global_queries)


def combine_stats(earlier, later):
    top = jnp.maximum(earlier[0], later[0])
    return (top, earlier[1] * jnp.exp(earlier[0] - top) + later[1] * jnp.exp(later[0] - top))


def full_forward(global_queries, key_part, value_part, full_mask, head_dim):
    scores = mixed_sum("wqhd,wkhd->whqk", global_queries, key_part) * head_dim ** (-0.5)
    scores = jnp.where(full_mask, scores, masked)
    local_top = jnp.max(scores, axis=3, keepdims=True)
    local_sum = jnp.sum(
        jnp.where(full_mask, jnp.exp(scores - local_top), 0.0), axis=3, keepdims=True
    )
    row_top, row_sum = merged((local_top, local_sum), SEQ, combine_stats)
    full_probs = jnp.where(full_mask, jnp.exp(scores - row_top), 0.0) / row_sum
    partial_out = mixed_sum("whqk,wkhd->wqhd", full_probs.astype(jnp.bfloat16), value_part)
    full_out = lax.psum(partial_out.astype(jnp.bfloat16), SEQ).astype(jnp.float32)
    return (full_out, full_probs)


def attention_weights(queries, sliding, global_kv, distant, key_mask):
    head_dim = queries.shape[-1]
    windows, blocks_dev, _, head_count, _ = queries.shape
    near_scores = mixed_sum("wbqhd,wbkhd->wbhqk", queries, sliding[..., :head_dim])
    global_scores = mixed_sum("wbqhd,wkhd->wbhqk", queries, global_kv[..., :head_dim])
    far_scores = mixed_sum("wbqhd,wbhrkd->wbhqrk", queries, distant[..., :head_dim])
    far_scores = far_scores.reshape(windows, blocks_dev, head_count, BLOCK, -1)
    scores = jnp.concatenate([near_scores, global_scores, far_scores], axis=4) * head_dim ** (-0.5)
    scores = jnp.where(key_mask, scores, masked)
    row_top = jnp.max(scores, axis=4, keepdims=True)
    weight = jnp.exp(scores - row_top)
    return weight / jnp.sum(weight, axis=4, keepdims=True)


def split_keys(scores_like, sliding, global_kv, distant):
    near_keys = sliding.shape[2]
    global_keys = global_kv.shape[1]
    windows, blocks_dev, head_count, pick_count, _, _ = distant.shape
    near_part = scores_like[..., :near_keys]
    global_part = scores_like[..., near_keys : near_keys + global_keys]
    far_part = scores_like[..., near_keys + global_keys :].reshape(
        windows, blocks_dev, head_count, BLOCK, pick_count, BLOCK
    )
    return (near_part, global_part, far_part)


def attention_values(low_probs, sliding, global_kv, distant, head_dim):
    near_part, global_part, far_part = split_keys(low_probs, sliding, global_kv, distant)
    attended = mixed_sum("wbhqk,wbkhd->wbqhd", near_part, sliding[..., head_dim:])
    attended = attended + mixed_sum("wbhqk,wkhd->wbqhd", global_part, global_kv[..., head_dim:])
    return attended + mixed_sum("wbhqrk,wbhrkd->wbqhd", far_part, distant[..., head_dim:])


def layer_forward(hidden, weights, tables):
    row_weights, down_weights, vector_weights = weights
    sender, picker, owned_hot, key_mask, full_mask = tables
    model_width = row_weights.shape[0]
    windows, tokens, _ = hidden.shape
    blocks_dev = tokens // BLOCK
    head_dim = model_width // HEADS
    (
        gain_one,
        shift_one,
        bias_query,
        bias_value,
        bias_out,
        gain_two,
        shift_two,
        bias_down,
        bias_up,
    ) = split_vectors(vector_weights, model_width)
    normed = norm_rows(hidden, gain_one, shift_one).astype(jnp.bfloat16)
    projected = mixed_sum("wtd,de->wte", normed, row_weights[:, : 3 * model_width])
    projected = (
        projected + jnp.concatenate([bias_query, jnp.zeros_like(bias_query), bias_value])
    ).astype(jnp.bfloat16)
    queries = projected[..., :model_width].reshape(windows, blocks_dev, BLOCK, HEADS, head_dim)
    key_part = projected[..., model_width : 2 * model_width].reshape(
        windows, tokens, HEADS, head_dim
    )
    value_part = projected[..., 2 * model_width :].reshape(windows, tokens, HEADS, head_dim)
    paired = jnp.concatenate([key_part, value_part], axis=3)
    sliding, global_kv, distant, global_queries = fetch_blocks(
        paired, queries, sender, picker, owned_hot
    )
    probabilities = attention_weights(queries, sliding, global_kv, distant, key_mask)
    attended = attention_values(
        probabilities.astype(jnp.bfloat16), sliding, global_kv, distant, head_dim
    )
    full_out, full_probs = full_forward(global_queries, key_part, value_part, full_mask, head_dim)
    placed = exact_two(
        "wgb,wgqhd->wbqhd", owned_hot, full_out.reshape(windows, -1, BLOCK, HEADS, head_dim)
    )
    on_global = jnp.sum(owned_hot, axis=1)[:, :, None, None, None] > 0
    attended = jnp.where(on_global, placed, attended)
    mixed_low = attended.reshape(windows, tokens, model_width).astype(jnp.bfloat16)
    middle = (
        hidden
        + mixed_sum("wtd,de->wte", mixed_low, row_weights[:, 3 * model_width : 4 * model_width])
        + bias_out
    )
    normed_two = norm_rows(middle, gain_two, shift_two).astype(jnp.bfloat16)
    up_value = mixed_sum("wtd,df->wtf", normed_two, row_weights[:, 4 * model_width :]) + bias_up
    active = jax.nn.gelu(up_value, approximate=False).astype(jnp.bfloat16)
    output = middle + mixed_sum("wtf,fd->wtd", active, down_weights) + bias_down
    stored = (
        hidden,
        normed,
        queries,
        sliding,
        global_kv,
        distant,
        probabilities,
        mixed_low,
        middle,
        normed_two,
        up_value,
        active,
        key_part,
        value_part,
        global_queries,
        full_probs,
    )
    return (output, stored)


def return_blocks(near_back, global_back, far_back, query_part, sender, picker, owned_hot):
    windows, blocks_dev, _, head_count, doubled = near_back.shape
    first_third = near_back[:, :, :BLOCK]
    centre_third = near_back[:, :, BLOCK : 2 * BLOCK]
    last_third = near_back[:, :, 2 * BLOCK :]
    framed = jnp.pad(first_third, ((0, 0), (0, 2), (0, 0), (0, 0), (0, 0)))
    framed = framed + jnp.pad(centre_third, ((0, 0), (1, 1), (0, 0), (0, 0), (0, 0)))
    framed = framed + jnp.pad(last_third, ((0, 0), (2, 0), (0, 0), (0, 0), (0, 0)))
    own_grad = framed[:, 1:-1]
    for direction in (1, -1):
        rim_grad = framed[:, -1] if direction == 1 else framed[:, 0]
        arrived = from_behind(rim_grad.astype(jnp.bfloat16), SEQ, direction).astype(
            rim_grad.dtype
        )
        if direction == 1:
            own_grad = jnp.concatenate(
                [own_grad[:, :1] + arrived[:, None], own_grad[:, 1:]], axis=1
            )
        else:
            own_grad = jnp.concatenate(
                [own_grad[:, :-1], own_grad[:, -1:] + arrived[:, None]], axis=1
            )
    global_total, query_total = (
        lax.psum(
            global_back.reshape(windows, -1, BLOCK, head_count, doubled).astype(jnp.bfloat16), SEQ
        ).astype(jnp.float32),
        lax.psum(query_part.astype(jnp.bfloat16), SEQ).astype(jnp.float32),
    )
    own_grad = own_grad + exact_two("wgb,wgthe->wbthe", owned_hot, global_total)
    far_flat = far_back.reshape(windows, -1, BLOCK, doubled)
    returning = exact_two("wspc,wste->pwcte", picker, far_flat)
    arrived_far = lax.all_to_all(
        returning.astype(jnp.bfloat16), SEQ, split_axis=0, concat_axis=0, tiled=True
    ).astype(returning.dtype)
    own_grad = own_grad + exact_two("wqcbh,qwcte->wbthe", sender, arrived_far)
    return (own_grad.reshape(windows, blocks_dev * BLOCK, head_count, doubled), query_total)


def attention_back(
    grad_attended,
    queries,
    sliding,
    global_kv,
    distant,
    probabilities,
    key_part,
    value_part,
    global_queries,
    full_probs,
    sender,
    picker,
    owned_hot,
):
    head_dim = queries.shape[-1]
    score_scale = head_dim ** (-0.5)
    windows, blocks_dev, _, head_count, _ = queries.shape
    on_global = jnp.sum(owned_hot, axis=1)[:, :, None, None, None] > 0
    selected = mixed_sum("wgb,wbqhd->wgqhd", owned_hot.astype(jnp.bfloat16), grad_attended)
    rows_grad = lax.psum(selected.astype(jnp.bfloat16), SEQ).reshape(
        windows, -1, head_count, head_dim
    )
    grad_attended = jnp.where(on_global, jnp.zeros_like(grad_attended), grad_attended)
    low_probs = probabilities.astype(jnp.bfloat16)
    near_grad = mixed_sum("wbqhd,wbkhd->wbhqk", grad_attended, sliding[..., head_dim:])
    global_grad = mixed_sum("wbqhd,wkhd->wbhqk", grad_attended, global_kv[..., head_dim:])
    far_grad = mixed_sum("wbqhd,wbhrkd->wbhqrk", grad_attended, distant[..., head_dim:])
    far_grad = far_grad.reshape(windows, blocks_dev, head_count, BLOCK, -1)
    grad_probs = jnp.concatenate([near_grad, global_grad, far_grad], axis=4)
    grad_scores = probabilities * (
        grad_probs - jnp.sum(probabilities * grad_probs, axis=4, keepdims=True)
    )
    grad_scores = grad_scores.astype(jnp.bfloat16)
    near_split, global_split, far_split = split_keys(grad_scores, sliding, global_kv, distant)
    near_probs, global_probs, far_probs = split_keys(low_probs, sliding, global_kv, distant)
    grad_query = mixed_sum("wbhqk,wbkhd->wbqhd", near_split, sliding[..., :head_dim])
    grad_query = grad_query + mixed_sum(
        "wbhqk,wkhd->wbqhd", global_split, global_kv[..., :head_dim]
    )
    grad_query = (
        grad_query + mixed_sum("wbhqrk,wbhrkd->wbqhd", far_split, distant[..., :head_dim])
    ) * score_scale
    near_back = jnp.concatenate(
        [
            mixed_sum("wbhqk,wbqhd->wbkhd", near_split, queries) * score_scale,
            mixed_sum("wbhqk,wbqhd->wbkhd", near_probs, grad_attended),
        ],
        axis=4,
    )
    global_back = jnp.concatenate(
        [
            mixed_sum("wbhqk,wbqhd->wkhd", global_split, queries) * score_scale,
            mixed_sum("wbhqk,wbqhd->wkhd", global_probs, grad_attended),
        ],
        axis=3,
    )
    far_back = jnp.concatenate(
        [
            mixed_sum("wbhqrk,wbqhd->wbhrkd", far_split, queries) * score_scale,
            mixed_sum("wbhqrk,wbqhd->wbhrkd", far_probs, grad_attended),
        ],
        axis=5,
    )
    full_grad_probs = mixed_sum("wqhd,wkhd->whqk", rows_grad, value_part)
    partial_dot = jnp.sum(full_probs * full_grad_probs, axis=3, keepdims=True)
    row_dot = lax.psum(partial_dot, SEQ)
    full_grad_scores = (full_probs * (full_grad_probs - row_dot)).astype(jnp.bfloat16)
    query_part = mixed_sum("whqk,wkhd->wqhd", full_grad_scores, key_part) * score_scale
    full_key_grad = mixed_sum("whqk,wqhd->wkhd", full_grad_scores, global_queries) * score_scale
    full_value_grad = mixed_sum("whqk,wqhd->wkhd", full_probs.astype(jnp.bfloat16), rows_grad)
    grad_paired, query_total = return_blocks(
        near_back, global_back, far_back, query_part, sender, picker, owned_hot
    )
    grad_query = grad_query + exact_two(
        "wgb,wgqhd->wbqhd", owned_hot, query_total.reshape(windows, -1, BLOCK, head_count, head_dim)
    )
    grad_paired = grad_paired + jnp.concatenate([full_key_grad, full_value_grad], axis=3)
    return (grad_query, grad_paired)


def layer_backward(stored, grad_output, weights, tables):
    row_weights, down_weights, vector_weights = weights
    sender, picker, owned_hot, key_mask, full_mask = tables
    (
        hidden,
        normed,
        queries,
        sliding,
        global_kv,
        distant,
        probabilities,
        mixed_low,
        middle,
        normed_two,
        up_value,
        active,
        key_part,
        value_part,
        global_queries,
        full_probs,
    ) = stored
    model_width = row_weights.shape[0]
    windows, tokens, _ = hidden.shape
    blocks_dev = tokens // BLOCK
    head_dim = model_width // HEADS
    (
        gain_one,
        shift_one,
        bias_query,
        bias_value,
        bias_out,
        gain_two,
        shift_two,
        bias_down,
        bias_up,
    ) = split_vectors(vector_weights, model_width)
    grad_ffn = grad_output.astype(jnp.bfloat16)
    grad_bias_down = jnp.sum(grad_ffn.astype(jnp.float32), axis=(0, 1))
    grad_down = mixed_sum("wtf,wtd->fd", active, grad_ffn)
    grad_active = mixed_sum("wtd,fd->wtf", grad_ffn, down_weights)
    gelu_pull = jax.vjp(partial(jax.nn.gelu, approximate=False), up_value)[1]
    grad_up = gelu_pull(grad_active)[0].astype(jnp.bfloat16)
    grad_bias_up = jnp.sum(grad_up.astype(jnp.float32), axis=(0, 1))
    grad_in = mixed_sum("wtd,wtf->df", normed_two, grad_up)
    grad_normed_two = mixed_sum("wtf,df->wtd", grad_up, row_weights[:, 4 * model_width :])
    norm_pull_two = jax.vjp(norm_rows, middle, gain_two, shift_two)[1]
    grad_middle_norm, grad_gain_two, grad_shift_two = norm_pull_two(grad_normed_two)
    grad_middle = grad_output + grad_middle_norm
    grad_branch = grad_middle.astype(jnp.bfloat16)
    grad_bias_out = jnp.sum(grad_branch.astype(jnp.float32), axis=(0, 1))
    grad_out_weight = mixed_sum("wtd,wte->de", mixed_low, grad_branch)
    grad_attended = mixed_sum(
        "wte,de->wtd", grad_branch, row_weights[:, 3 * model_width : 4 * model_width]
    ).astype(jnp.bfloat16)
    grad_attended = grad_attended.reshape(windows, blocks_dev, BLOCK, HEADS, head_dim)
    grad_query, grad_paired = attention_back(
        grad_attended,
        queries,
        sliding,
        global_kv,
        distant,
        probabilities,
        key_part,
        value_part,
        global_queries,
        full_probs,
        sender,
        picker,
        owned_hot,
    )
    grad_projected = jnp.concatenate(
        [
            grad_query.reshape(windows, tokens, model_width),
            grad_paired[..., :head_dim].reshape(windows, tokens, model_width),
            grad_paired[..., head_dim:].reshape(windows, tokens, model_width),
        ],
        axis=2,
    ).astype(jnp.bfloat16)
    summed = jnp.sum(grad_projected.astype(jnp.float32), axis=(0, 1))
    grad_bias_query = summed[:model_width]
    grad_bias_value = summed[2 * model_width :]
    grad_projection = mixed_sum("wtd,wte->de", normed, grad_projected)
    grad_normed = mixed_sum("wte,de->wtd", grad_projected, row_weights[:, : 3 * model_width])
    norm_pull_one = jax.vjp(norm_rows, hidden, gain_one, shift_one)[1]
    grad_hidden_norm, grad_gain_one, grad_shift_one = norm_pull_one(grad_normed)
    grad_hidden = grad_middle + grad_hidden_norm
    grad_rows = jnp.concatenate([grad_projection, grad_out_weight, grad_in], axis=1)
    grad_vectors = jnp.concatenate(
        [
            grad_gain_one,
            grad_shift_one,
            grad_bias_query,
            grad_bias_value,
            grad_bias_out,
            grad_gain_two,
            grad_shift_two,
            grad_bias_down,
            grad_bias_up,
        ]
    )
    return (grad_hidden, (grad_rows, grad_down, grad_vectors))


def adam_update(master, first_old, second_old, gradient, step_rate, decay_rate):
    first_new = 0.5 * first_old + 0.5 * gradient
    second_new = 0.5 * second_old + 0.5 * gradient * gradient
    first_hat = first_new / (1.0 - 0.5**STEP)
    second_hat = second_new / (1.0 - 0.5**STEP)
    master_new = master - step_rate * (
        first_hat / (jnp.sqrt(second_hat) + 1e-08) + decay_rate * master
    )
    return (master_new, first_new, second_new)


def general_shards(
    block_input,
    cotangent,
    random_ids,
    segment_ids,
    global_ids,
    w_rows,
    w_rows_first,
    w_rows_second,
    w_down,
    w_down_first,
    w_down_second,
    vectors,
    vectors_first,
    vectors_second,
):
    section_index = lax.axis_index(SECTION)
    seq_place = lax.axis_index(SEQ)
    groups = lax.axis_size(SEQ)
    row_weights, down_weights, vector_low = (
        lax.all_gather(w_rows[0].astype(jnp.bfloat16), (DP, SEQ), axis=1, tiled=True),
        lax.all_gather(w_down[0].astype(jnp.bfloat16), (DP, SEQ), axis=0, tiled=True),
        lax.all_gather(vectors[0].astype(jnp.bfloat16), (DP, SEQ), axis=0, tiled=True),
    )
    weights = (row_weights, down_weights, vector_low.astype(jnp.float32))
    micro_count, windows, tokens, model_width = block_input.shape
    received = jnp.zeros((windows, tokens, model_width), jnp.bfloat16)
    results = jnp.zeros(block_input.shape, jnp.float32)
    full_totals = (
        jnp.zeros(row_weights.shape, jnp.float32),
        jnp.zeros(down_weights.shape, jnp.float32),
        jnp.zeros(vector_low.shape, jnp.float32),
    )

    def tick(tick_index, carry):
        received, results, full_totals = carry
        forward_mb = jnp.clip(tick_index - section_index, 0, micro_count - 1)
        behind_raw = tick_index - 2 + section_index
        behind = jnp.clip(behind_raw, 0, micro_count - 1)
        live_mask = ((behind_raw >= 0) & (behind_raw < micro_count)).astype(jnp.float32)
        tables_forward = route_tables(
            lax.dynamic_index_in_dim(random_ids, forward_mb, 0, keepdims=False),
            lax.dynamic_index_in_dim(segment_ids, forward_mb, 0, keepdims=False),
            lax.dynamic_index_in_dim(global_ids, forward_mb, 0, keepdims=False),
            seq_place,
            groups,
        )
        tables_behind = route_tables(
            lax.dynamic_index_in_dim(random_ids, behind, 0, keepdims=False),
            lax.dynamic_index_in_dim(segment_ids, behind, 0, keepdims=False),
            lax.dynamic_index_in_dim(global_ids, behind, 0, keepdims=False),
            seq_place,
            groups,
        )
        incoming_values = received.astype(jnp.float32)
        first_input = lax.dynamic_index_in_dim(block_input, forward_mb, 0, keepdims=False).astype(
            jnp.float32
        )
        forward_input = jnp.where(section_index == 0, first_input, incoming_values)
        forward_output = layer_forward(forward_input, weights, tables_forward)[0]
        back_source = lax.dynamic_index_in_dim(block_input, behind, 0, keepdims=False).astype(
            jnp.float32
        )
        back_input = jnp.where(section_index == 0, back_source, incoming_values)
        given_grad = lax.dynamic_index_in_dim(cotangent, behind, 0, keepdims=False).astype(
            jnp.float32
        )
        back_grad = jnp.where(section_index == 0, incoming_values, given_grad) * live_mask
        stored = layer_forward(back_input, weights, tables_behind)[1]
        grad_input, gradients = layer_backward(stored, back_grad, weights, tables_behind)
        outgoing = jnp.where(section_index == 0, forward_output, grad_input).astype(jnp.bfloat16)
        finished = jnp.where(section_index == 0, grad_input, forward_output)
        updated = lax.dynamic_update_index_in_dim(results, finished, behind, 0)
        results = jnp.where(live_mask > 0, updated, results)
        full_totals = tuple(
            (total_part + grad_part for total_part, grad_part in zip(full_totals, gradients))
        )
        return (partner(outgoing, SECTION, 0), results, full_totals)

    received, results, full_totals = lax.fori_loop(
        0, micro_count + 2, tick, (received, results, full_totals)
    )
    shard_totals = (
        lax.psum_scatter(full_totals[0], (DP, SEQ), scatter_dimension=1, tiled=True),
        lax.psum_scatter(full_totals[1], (DP, SEQ), scatter_dimension=0, tiled=True),
        lax.psum_scatter(full_totals[2], (DP, SEQ), scatter_dimension=0, tiled=True),
    )
    new_rows, new_rows_first, new_rows_second = adam_update(
        w_rows[0], w_rows_first[0], w_rows_second[0], shard_totals[0], rate_matrix, decay_matrix
    )
    new_down, new_down_first, new_down_second = adam_update(
        w_down[0], w_down_first[0], w_down_second[0], shard_totals[1], rate_matrix, decay_matrix
    )
    new_vectors, new_vectors_first, new_vectors_second = adam_update(
        vectors[0], vectors_first[0], vectors_second[0], shard_totals[2], rate_vector, 0.0
    )
    return (
        results[None],
        new_rows[None],
        new_rows_first[None],
        new_rows_second[None],
        new_down[None],
        new_down_first[None],
        new_down_second[None],
        new_vectors[None],
        new_vectors_first[None],
        new_vectors_second[None],
    )


LOW = jnp.bfloat16
LOG_HIGH = [float(np.log(c).astype(ml_dtypes.bfloat16)) for c in (1.0, 2.0, 3.0)]
LOG_LOW = [float(np.log(c)) - high for c, high in zip((1.0, 2.0, 3.0), LOG_HIGH)]
CHUNK = 256
VMEM_BYTES = 60 * 1024 * 1024


def dot_rows(left, right):
    return lax.dot_general(left, right, (((1,), (1,)), ((), ())), preferred_element_type=jnp.float32)


def dot_plain(left, right):
    return lax.dot_general(left, right, (((1,), (0,)), ((), ())), preferred_element_type=jnp.float32)


def dot_tokens(left, right):
    return lax.dot_general(left, right, (((0,), (0,)), ((), ())), preferred_element_type=jnp.float32)


def swap(value):
    return lax.ppermute(value, SECTION, [(0, 1), (1, 0)])


def normalized(values_in):
    row_mean = jnp.mean(values_in, axis=-1, keepdims=True)
    centred = values_in - row_mean
    spread = jnp.mean(centred * centred, axis=-1, keepdims=True)
    scale = lax.rsqrt(spread + epsilon)
    return centred * scale, scale


class Shares:
    def __init__(self, width, columns, depth, vector_len):
        self.width = width
        self.columns = columns
        self.depth = depth
        self.vector_len = vector_len
        self.half = columns // 2
        self.per = width // columns
        self.groups = columns // depth

    def unpack(self, gathered, core):
        rows, down, vec = gathered
        vec = vec.reshape(-1, TAIL, self.width)[:, 0, : self.vector_len].reshape(-1)
        pieces = split_vectors(vec.astype(jnp.float32), self.width)
        for index in (2, 3):
            pieces[index] = lax.dynamic_index_in_dim(
                pieces[index].reshape(self.per, 2, self.half), core, 1, keepdims=False
            )
        pieces[8] = lax.dynamic_index_in_dim(
            pieces[8].reshape(-1, 2, self.depth // 2), core, 1, keepdims=False
        )
        return (
            (rows.reshape(-1, self.width), down.reshape(-1, self.width)),
            [piece.reshape(1, -1) for piece in pieces],
        )

    def by_shard(self, grads, vector_grads, core):
        proj, out, up, down = grads
        half, per, width = self.half, self.per, self.width
        hot = (jnp.arange(2) == core).astype(jnp.float32)
        spread = list(vector_grads)
        for index in (2, 3):
            spread[index] = (
                spread[index].reshape(per, 1, half) * hot[None, :, None]
            ).reshape(-1)
        spread[8] = (spread[8].reshape(-1, 1, self.depth // 2) * hot[None, :, None]).reshape(-1)
        for index in (0, 1, 4, 5, 6, 7):
            spread[index] = spread[index] * hot[0]
        vec = jnp.concatenate(spread).reshape(-1, 1, self.vector_len)
        vec = jnp.pad(vec, ((0, 0), (0, TAIL - 1), (0, width - self.vector_len))).astype(LOW)
        return (
            proj.reshape(-1, half, width),
            out.reshape(-1, half, width),
            up.reshape(2, 4, half, width),
            down.reshape(2, 2, 4, self.depth // 2, width),
            vec.reshape(2, 2, 4, TAIL, width),
        )


MESH = pl.DeviceIdType.MESH
PIECE = 48
TAIL = 16


def prepare_kernel(shares, rows_ref, down_ref, vector_ref, rows_out, down_out, vector_out):
    core = lax.axis_index(SECTION)
    offset = lax.axis_index((DP, SEQ)) * shares.columns
    half, per, width, depth = shares.half, shares.per, shares.width, shares.depth // 2
    is_inner = (offset >= 3 * width) & (offset < 4 * width)
    is_hidden = offset >= 4 * width

    @pl.when(is_inner)
    def _():
        for which in range(2):
            side = core if which == 0 else 1 - core
            held = [rows_ref[pl.ds((2 * j + side) * half, half), :] for j in range(per)]
            turned = jnp.transpose(jnp.concatenate(held, axis=0))
            rows_out[which] = jnp.concatenate([turned[:half], turned[half:]], axis=1).astype(LOW)

    @pl.when(jnp.logical_not(is_inner))
    def _():
        turned = jnp.transpose(rows_ref[...]).astype(LOW)
        plain = [turned[:half], turned[half:]]
        hidden = [
            jnp.concatenate(
                [turned[(2 * j + side) * depth :][:depth] for j in range(shares.groups)], axis=0
            )
            for side in range(2)
        ]
        halves = [jnp.where(is_hidden, b, a) for a, b in zip(plain, hidden)]
        rows_out[0] = jnp.where(core == 0, halves[0], halves[1])
        rows_out[1] = jnp.where(core == 0, halves[1], halves[0])

    down = down_ref[...].astype(LOW)
    down_out[0] = jnp.where(core == 0, down[:depth], down[depth:])
    down_out[1] = jnp.where(core == 0, down[depth:], down[:depth])
    vector_out[...] = jnp.zeros_like(vector_out)
    vector_out[0:1, : shares.vector_len] = vector_ref[...].astype(LOW)


def prepare(shares, rows, down, vector):
    return pl.pallas_call(
        partial(prepare_kernel, shares),
        out_shape=[
            jax.ShapeDtypeStruct((2, shares.half, shares.width), LOW),
            jax.ShapeDtypeStruct((2, shares.depth // 2, shares.width), LOW),
            jax.ShapeDtypeStruct((TAIL, shares.width), LOW),
        ],
        compiler_params=pltpu.CompilerParams(vmem_limit_bytes=VMEM_BYTES),
    )(rows, down, vector)


class Place:
    def __init__(self):
        self.core = lax.axis_index(SECTION)
        self.dp = lax.axis_index(DP)
        self.z = lax.axis_index(SEQ)
        self.y, self.x = self.dp // 2, self.dp % 2
        self.high, self.low = self.z // 2, self.z % 2
        self.inner = self.high + self.low == 1
        self.outer = self.high + self.low != 1
        self.partner = {SECTION: 1 - self.core}
        self.along_x = {DP: 2 * self.y + 1 - self.x}
        self.along_y = {DP: 2 * (1 - self.y) + self.x}
        self.across = {SEQ: 3 - self.z}
        self.beside = {SEQ: 2 * self.high + 1 - self.low}
        self.others = [{SEQ: (self.z + by) % 4} for by in (1, 2, 3)]
        self.own = pl.ds(self.z, 1)
        self.next = pl.ds(2 * self.high + 1 - self.low, 1)
        self.near = pl.ds(2 * self.high, 2)
        self.far = pl.ds(2 * (1 - self.high), 2)

    def greet(self):
        barrier = pltpu.get_barrier_semaphore()
        everyone = [self.partner, self.along_x, self.along_y] + self.others
        for device in everyone:
            pl.semaphore_signal(barrier, inc=1, device_id=device, device_id_type=MESH)
        pl.semaphore_wait(barrier, len(everyone))


def remote(src, dst, sems, spots, device):
    return pltpu.make_async_remote_copy(
        src_ref=src,
        dst_ref=dst,
        send_sem=sems[0].at[spots[0]],
        recv_sem=sems[1].at[spots[1]],
        device_id=device,
        device_id_type=MESH,
    )


def chunk_pairs(shares):
    pairs = []
    for array, length in ((0, shares.half), (1, shares.depth // 2)):
        for start in range(0, length, 2 * PIECE):
            pairs.append([(array, start, PIECE, 0), (array, start + PIECE, PIECE, 1)])
    pairs[0].append((2, 0, TAIL, 0))
    return pairs


def quad_pairs(shares):
    length = (shares.half + shares.depth // 2) // 2
    pairs = [
        [(0, start, PIECE, None), (1, start, PIECE, None)] for start in range(0, length, PIECE)
    ]
    pairs[0].append((2, 0, TAIL, 0))
    return pairs


def gather_kernel(shares, *refs):
    (rows_in, down_in, vector_in, x_in, cot_in), refs = refs[:5], refs[5:]
    outs, refs = [refs[0:3], refs[3:6]], refs[6:]
    (x_out, cot_out), refs = refs[:2], refs[2:]
    local, swap_send, swap_recv, z_send, z_recv, send, recv = refs
    here = Place()
    core, y, x, z = here.core, here.y, here.x, here.z
    half = x_in.shape[2] // 2
    rows_half, down_half = shares.half // 2, shares.depth // 4
    here.greet()

    def slices(source, target, base):
        mine = pl.ds(pl.multiple_of(core * half, half), half)
        sems = (z_send, z_recv)
        own = pltpu.make_async_copy(
            source.at[z, 0, mine], target.at[z, core], local.at[8 + base // 4]
        )
        sends, arrivals = [], []
        for by in (1, 2, 3):
            spots = (base + by - 1, base + by - 1)
            device = here.others[by - 1]
            sends.append(
                remote(source.at[(z + by) % 4, 0, mine], target.at[z, core], sems, spots, device)
            )
            arrivals.append(
                remote(
                    source.at[z, 0, mine], target.at[(z + 4 - by) % 4, core], sems, spots, device
                )
            )
        spots = (base + 3, base + 3)
        forward = remote(target.at[:, core], target.at[:, core], sems, spots, here.partner)
        arrived = remote(target.at[:, 1 - core], target.at[:, 1 - core], sems, spots, here.partner)
        return own, sends, arrivals, forward, arrived

    x_moves = slices(x_in, x_out, 0)
    cot_moves = slices(cot_in, cot_out, 4)

    def open_slices(moves):
        moves[0].start()
        for copy in moves[1]:
            copy.start()

    def pass_slices(moves):
        moves[0].wait()
        for copy in moves[2]:
            copy.wait_recv()
        moves[3].start()

    def close_slices(moves):
        for copy in moves[1]:
            copy.wait_send()
        moves[3].wait_send()
        moves[4].wait_recv()

    def first_moves(layer, which):
        down = down_in.at[which]
        rows = rows_in.at[which]
        if layer == 0:
            return [
                (0, rows, outs[0][0].at[y, x, z]),
                (1, down, outs[0][1].at[y, x, z]),
                (2, vector_in, outs[0][2].at[y, x, z]),
            ]
        moves = [(7, vector_in, outs[1][2].at[y, x, z])]
        for part in range(2):
            target = outs[1][part]
            moves.append(
                (
                    3 + 2 * part,
                    rows.at[pl.ds(part * rows_half, rows_half)],
                    target.at[z, pl.ds(0, rows_half)],
                )
            )
            moves.append(
                (
                    4 + 2 * part,
                    down.at[pl.ds(part * down_half, down_half)],
                    target.at[z, pl.ds(rows_half, down_half)],
                )
            )
        return moves

    swaps = (swap_send, swap_recv)
    for layer in range(2):

        @pl.when(core == layer)
        def _():
            across = [
                remote(src, dst, swaps, (spot, spot), here.partner)
                for spot, src, dst in first_moves(layer, 1)
            ]
            own = [
                pltpu.make_async_copy(src, dst, local.at[spot])
                for spot, src, dst in first_moves(layer, 0)
            ]
            for copy in across + own:
                copy.start()
            for copy in own:
                copy.wait()
            for copy in across:
                copy.wait_send()
            for spot, src, dst in first_moves(1 - layer, 0):
                remote(src, dst, swaps, (spot, spot), here.partner).wait_recv()

    numbers, pairs = {}, []
    for layer in range(2):
        for pair in chunk_pairs(shares) if layer == 0 else quad_pairs(shares):
            entry = []
            for array, start, length, order in pair:
                ref = outs[layer][array]
                rows = pl.ds(start, length)
                flat = order is None
                number = len(numbers)
                sems = (send, recv)

                def part(which):
                    return ref.at[which, rows] if flat else ref.at[y, x, which, rows]

                def copy(piece, spots, device):
                    return remote(piece, piece, sems, ((number, spots[0]), (number, spots[1])), device)

                steps = {
                    "z": copy(part(here.own), (0, 0), here.beside),
                    "across": copy(part(here.near), (1, 1), here.across),
                    "on": copy(part(here.far), (4, 1), here.beside),
                }
                arrive = [
                    copy(part(here.next), (0, 0), here.beside),
                    copy(part(here.far), (1, 1), here.across),
                ]
                if order == 0:
                    steps["one"] = copy(ref.at[y, x, :, rows], (2, 2), here.along_y)
                    steps["two"] = copy(ref.at[:, x, :, rows], (3, 3), here.along_x)
                    arrive.append(copy(ref.at[1 - y, x, :, rows], (2, 2), here.along_y))
                    arrive.append(copy(ref.at[:, 1 - x, :, rows], (3, 3), here.along_x))
                elif order == 1:
                    steps["one"] = copy(ref.at[y, x, :, rows], (2, 2), here.along_x)
                    steps["two"] = copy(ref.at[y, :, :, rows], (3, 3), here.along_y)
                    arrive.append(copy(ref.at[y, 1 - x, :, rows], (2, 2), here.along_x))
                    arrive.append(copy(ref.at[1 - y, :, :, rows], (3, 3), here.along_y))
                numbers[number] = (steps, arrive)
                entry.append(number)
            pairs.append(entry)

    def issue(name, entry):
        after = {"z": None, "across": 0, "on": 1, "one": 1, "two": 2}[name]

        def start():
            for number in entry:
                steps, arrive = numbers[number]
                if name in steps:
                    if after is not None and not (name == "one"):
                        arrive[after].wait_recv()
                    steps[name].start()

        if name in ("across", "on"):
            pl.when(here.inner)(start)
        else:
            start()

    def arrived(entry, index, where):
        def wait():
            for number in entry:
                numbers[number][1][index].wait_recv()

        pl.when(where)(wait)

    first, second = pairs[: len(chunk_pairs(shares))], pairs[len(chunk_pairs(shares)) :]
    for entry in first:
        issue("z", entry)
    for entry in first:
        issue("across", entry)
        arrived(entry, 0, here.outer)
    for entry in first[:-1]:
        issue("on", entry)
        arrived(entry, 1, here.outer)
        issue("one", entry)
    issue("on", first[-1])
    for entry in second:
        issue("z", entry)
    open_slices(x_moves)
    arrived(first[-1], 1, here.outer)
    issue("one", first[-1])
    issue("two", first[0])
    for entry in second:
        issue("across", entry)
        arrived(entry, 0, here.outer)
    issue("two", first[1])
    open_slices(cot_moves)
    for entry in second:
        issue("on", entry)
    issue("two", first[2])
    pass_slices(x_moves)
    for entry in second:
        arrived(entry, 1, here.outer)
        for number in entry:
            steps, arrive = numbers[number]
            if "one" in steps:
                steps["one"].start()
                arrive[2].wait_recv()
                steps["two"].start()
    pass_slices(cot_moves)
    for steps, arrive in numbers.values():
        if len(arrive) == 4:
            arrive[3].wait_recv()
        for name in steps:
            if name not in ("across", "on"):
                steps[name].wait_send()

    @pl.when(here.inner)
    def _():
        for steps, _ in numbers.values():
            steps["across"].wait_send()
            steps["on"].wait_send()

    close_slices(x_moves)
    close_slices(cot_moves)


def gather(shares, prepared, block_input, cotangent):
    micro, _, tokens, width = block_input.shape
    chunks = sum(len(pair) for pair in chunk_pairs(shares) + quad_pairs(shares))
    lengths = (shares.half, shares.depth // 2, TAIL)
    layer = [jax.ShapeDtypeStruct((2, 2, 4, rows, width), LOW) for rows in lengths]
    quad = jax.ShapeDtypeStruct((4, (lengths[0] + lengths[1]) // 2, width), LOW)
    window = jax.ShapeDtypeStruct((micro, 2, tokens // 2, width), LOW)
    anywhere = pl.BlockSpec(memory_space=pl.ANY)
    results = pl.pallas_call(
        partial(gather_kernel, shares),
        in_specs=[pl.BlockSpec(memory_space=pltpu.VMEM)] * 3 + [anywhere] * 2,
        out_specs=[anywhere] * 8,
        out_shape=layer + [quad, quad, layer[2]] + [window, window],
        scratch_shapes=[
            pltpu.SemaphoreType.DMA((10,)),
            pltpu.SemaphoreType.DMA((8,)),
            pltpu.SemaphoreType.DMA((8,)),
            pltpu.SemaphoreType.DMA((8,)),
            pltpu.SemaphoreType.DMA((8,)),
            pltpu.SemaphoreType.DMA((chunks, 5)),
            pltpu.SemaphoreType.DMA((chunks, 4)),
        ],
        compiler_params=pltpu.CompilerParams(
            collective_id=0, has_side_effects=True, vmem_limit_bytes=VMEM_BYTES
        ),
    )(*prepared, block_input, cotangent)
    return results[0:3], results[3:6], results[6], results[7]


def over(value, bit):
    return lax.ppermute(value, DP, [(i, i ^ bit) for i in range(4)])


def layout_moves(shares, y, x, pieces, arrays):
    rows_half, down_half = shares.half // 2, shares.depth // 4
    down = arrays[-1]
    moves = []
    for part in range(2):
        rows = pl.ds(part * rows_half, rows_half)
        for index, (by_y, by_x) in enumerate(((0, 0), (1, 0), (0, 1), (1, 1))):
            piece = pieces[part][index]
            at_y, at_x = y ^ by_y, x ^ by_x
            top = pl.ds(0, rows_half)
            if len(arrays) == 2:
                moves.append((piece.at[:, top], arrays[0].at[at_y, at_x, :, rows]))
            else:
                proj, out, up, _ = arrays
                if at_y == 1:
                    moves.append((piece.at[:, top], up.at[at_x, :, rows]))
                elif at_x == 0:
                    moves.append((piece.at[:, top], proj.at[pl.ds(0, 4), rows]))
                else:
                    moves.append((piece.at[pl.ds(0, 2), top], proj.at[pl.ds(4, 2), rows]))
                    moves.append((piece.at[pl.ds(2, 2), top], out.at[:, rows]))
            moves.append(
                (
                    piece.at[:, pl.ds(rows_half, down_half)],
                    down.at[at_y, at_x, :, pl.ds(part * down_half, down_half)],
                )
            )
    return moves


def layout_kernel(shares, joins, *refs):
    dp = lax.axis_index(DP)
    if joins:
        pieces, arrays = [refs[0:4], refs[4:8]], refs[8:10]
    else:
        arrays, pieces = refs[0:4], [refs[4:8], refs[8:12]]
    for spot in range(4):

        @pl.when(dp == spot)
        def _():
            for piece, place in layout_moves(shares, spot // 2, spot % 2, pieces, arrays):
                src, dst = (piece, place) if joins else (place, piece)
                dst[...] = src[...]


def layout(shares, joins, *arrays):
    half, depth, width = shares.half, shares.depth // 2, shares.width
    if joins:
        shapes = [(2, 2, 4, half, width), (2, 2, 4, depth, width)]
    else:
        shapes = [(4, (half + depth) // 2, width)] * 8
    return pl.pallas_call(
        partial(layout_kernel, shares, joins),
        out_shape=[jax.ShapeDtypeStruct(shape, LOW) for shape in shapes],
        compiler_params=pltpu.CompilerParams(vmem_limit_bytes=VMEM_BYTES),
        cost_estimate=pl.CostEstimate(
            flops=0, bytes_accessed=64 * (half + depth) * width, transcendentals=0
        ),
    )(*arrays)


def tied(value, flying):
    return lax.optimization_barrier((value, flying))


def spread_quads(shares, quads):
    low, high = quads
    flying = (low, high, over(low, 2), over(high, 1))
    low, high, low_y, high_x = yield flying
    flying = (low_y, high_x, over(low, 1), over(high, 2))
    low_y, high_x, low_x, high_y = yield flying
    flying = (over(low_y, 1), over(high_x, 2))
    low_both, high_both = yield flying
    yield layout(shares, True, low, low_y, low_x, low_both, high, high_y, high_x, high_both)


def sum_quads(shares, arrays):
    pieces = layout(shares, False, *arrays)

    def total(*terms):
        return sum(term.astype(jnp.float32) for term in terms).astype(LOW)

    low, low_y, low_x, low_both = pieces[:4]
    high, high_y, high_x, high_both = pieces[4:]
    flying = (low_x, high_y, over(low_both, 1), over(high_both, 2))
    low_x, high_y, low_hop, high_hop = yield flying
    low_y, high_x = total(low_y, low_hop), total(high_x, high_hop)
    flying = (low_y, high_x, over(low_x, 1), over(high_y, 2))
    low_y, high_x, low_x, high_y = yield flying
    flying = (over(low_y, 2), over(high_x, 1))
    low_y, high_x = yield flying
    yield (total(low, low_x, low_y), total(high, high_x, high_y))


class Beside:
    def __init__(self, hops=None):
        self.hops = hops
        self.flying = None if hops is None else next(hops)

    def tie(self, value):
        if self.hops is None:
            return value
        value, arrived = tied(value, self.flying)
        self.flying = self.hops.send(arrived)
        return value


def scatter_kernel(shares, *refs):
    (proj, out, up, down, vec_zero, low, high, vec_one), refs = refs[:8], refs[8:]
    (dx_ref, final_ref, halves, slices), refs = refs[:4], refs[4:]
    work, refs = [refs[0:3], refs[3:6]], refs[6:]
    (got_one, got_two, got_far, got_across, got_near, total), refs = refs[:6], refs[6:]
    load, local, swap_send, swap_recv, z_send, z_recv, send, recv = refs
    here = Place()
    core, y, x, z = here.core, here.y, here.x, here.z
    rows_half, down_half = shares.half // 2, shares.depth // 4
    down_base = shares.half
    tail_base = shares.half + shares.depth // 2

    rows = work[0][0]
    moves = [
        [
            (proj.at[pl.ds(0, 4)], rows.at[0, 0]),
            (proj.at[pl.ds(4, 2)], rows.at[0, 1, pl.ds(0, 2)]),
            (out, rows.at[0, 1, pl.ds(2, 2)]),
            (up, rows.at[1]),
            (down, work[0][1]),
            (vec_zero, work[0][2]),
        ],
        [(low, work[1][0]), (high, work[1][1]), (vec_one, work[1][2])],
    ]
    loads = [
        [
            pltpu.make_async_copy(src, dst, load.at[layer, index])
            for index, (src, dst) in enumerate(moves[layer])
        ]
        for layer in range(2)
    ]
    for layer in (1, 0):
        for copy in loads[layer]:
            copy.start()
    here.greet()

    def place_of(layer, array, start):
        if array == 2:
            return tail_base
        if layer == 0:
            return (0, down_base)[array] + start
        if start < rows_half:
            return array * rows_half + start
        return down_base + array * down_half + start - rows_half

    pairs, chunks = [], []
    for layer in (1, 0):
        for index, pair in enumerate(quad_pairs(shares) if layer else chunk_pairs(shares)):
            entry = []
            for array, start, length, order in pair:
                entry.append((len(chunks), layer, array, start, length, order))
                chunks.append(entry[-1])
            pairs.append((index, entry))

    def pieces(chunk):
        number, layer, array, start, length, order = chunk
        ref = work[layer][array]
        rows = pl.ds(start, length)
        sems = (send, recv)
        keeps, slots, copies = [], [], []

        def part(which):
            return ref.at[which, rows] if order is None else ref.at[y, x, which, rows]

        def add(src, slot, device, keep):
            spots = (number, len(copies))
            copies.append(remote(src, slot, sems, (spots, spots), device))
            slots.append(slot)
            keeps.append(keep)

        room = pl.ds(0, length)
        if order == 0:
            add(ref.at[:, 1 - x, :, rows], got_one.at[number, :, :, room], here.along_x, ref.at[:, x, :, rows])
            add(ref.at[1 - y, x, :, rows], got_two.at[number, :, room], here.along_y, ref.at[y, x, :, rows])
        elif order == 1:
            add(ref.at[1 - y, :, :, rows], got_one.at[number, :, :, room], here.along_y, ref.at[y, :, :, rows])
            add(ref.at[y, 1 - x, :, rows], got_two.at[number, :, room], here.along_x, ref.at[y, x, :, rows])
        else:
            copies, slots, keeps = [None] * 2, [None] * 2, [None] * 2
        add(part(here.far), got_far.at[number, :, room], here.beside, part(here.far))
        add(part(here.far), got_across.at[number, :, room], here.across, part(here.near))
        add(part(here.next), got_near.at[number, :, room], here.beside, part(here.own))
        return copies, keeps, slots

    built = [pieces(chunk) for chunk in chunks]
    loaded = set()

    def land(number, phase):
        copies, keeps, slots = built[number]
        copies[phase].wait_recv()
        keep, slot = keeps[phase], slots[phase]
        keep[...] = keep[...] + slot[...]

    def run(chunk, phase):
        number, layer, array, start, length, order = chunk
        copies, keeps, slots = built[number]
        if (layer, array) not in loaded:
            loaded.add((layer, array))
            spots = ((0, 1, 2, 3), (4,), (5,))[array] if layer == 0 else (array,)
            for spot in spots:
                loads[layer][spot].wait()
        if phase < 2:
            if order is not None:
                if phase:
                    land(number, 0)
                copies[phase].start()
        elif phase == 2:
            if order is not None:
                land(number, 1)

            @pl.when(here.outer)
            def _():
                copies[2].start()
                copies[4].start()

        elif phase == 3:

            @pl.when(here.inner)
            def _():
                land(number, 2)
                copies[3].start()

        elif phase == 4:

            @pl.when(here.inner)
            def _():
                land(number, 3)
                copies[4].start()

        else:
            copies[4].wait_recv()
            spot = pl.ds(place_of(layer, array, start), length)
            total[layer, spot, :] = (keeps[4][...] + slots[4][...])[0]

    def step(entry, phase):
        for chunk in entry:
            run(chunk, phase)

    second = [entry for _, entry in pairs[: len(quad_pairs(shares))]]
    first = [entry for _, entry in pairs[len(quad_pairs(shares)) :]]
    tails = [chunk for entry in second for chunk in entry if chunk[5] is not None]
    second = [[chunk for chunk in entry if chunk[5] is None] for entry in second]
    first[0] = first[0] + tails
    step(first[0], 0)
    step(first[1], 0)
    for entry in second:
        step(entry, 2)
    step(first[0], 1)
    for section, source in ((0, dx_ref), (1, final_ref)):

        @pl.when(core == section)
        def _():
            pltpu.make_async_copy(source.at[z], slices.at[z], local.at[0]).start()
            for by in (1, 2, 3):
                remote(
                    source.at[(z + by) % 4],
                    slices.at[z],
                    (z_send, z_recv),
                    (by - 1, by - 1),
                    here.others[by - 1],
                ).start()

    for entry in second:
        step(entry, 3)
    step(first[2], 0)
    step(first[1], 1)
    for entry in second:
        step(entry, 4)
    step(first[0], 2)
    step(first[2], 1)
    for entry in second:
        step(entry, 5)
    step(first[0], 3)
    step(first[1], 2)
    step(first[0], 4)
    step(first[1], 3)
    step(first[2], 2)
    step(first[1], 4)
    step(first[2], 3)
    step(first[2], 4)
    for entry in first:
        step(entry, 5)

    for copies, _, _ in built:
        for index in (0, 1, 4):
            if copies[index] is not None:
                copies[index].wait_send()
    for section, index in ((here.outer, 2), (here.inner, 3)):

        @pl.when(section)
        def _():
            for copies, _, _ in built:
                copies[index].wait_send()

    swaps = (swap_send, swap_recv)
    across = remote(total.at[1 - core], halves.at[core], swaps, (0, 0), here.partner)
    across.start()
    own = pltpu.make_async_copy(total.at[core], halves.at[core], local.at[1])
    own.start()
    own.wait()
    across.wait_send()
    remote(total.at[1 - core], halves.at[1 - core], swaps, (0, 0), here.partner).wait_recv()
    pltpu.make_async_copy(dx_ref.at[z], slices.at[z], local.at[0]).wait()
    for by in (1, 2, 3):
        copy = remote(
            dx_ref.at[z],
            slices.at[(z + 4 - by) % 4],
            (z_send, z_recv),
            (by - 1, by - 1),
            here.others[by - 1],
        )
        copy.wait_send()
        copy.wait_recv()


def scatter(shares, arrays, vec_zero, quads, vec_one, grad, final):
    micro, tokens, width = grad.shape
    lengths = (shares.half, shares.depth // 2, TAIL)
    chunks = sum(len(pair) for pair in chunk_pairs(shares) + quad_pairs(shares))
    rows = sum(lengths)
    anywhere = pl.BlockSpec(memory_space=pl.ANY)
    work = [pltpu.VMEM((2, 2, 4, length, width), LOW) for length in lengths]
    quad = pltpu.VMEM((4, (lengths[0] + lengths[1]) // 2, width), LOW)
    return pl.pallas_call(
        partial(scatter_kernel, shares),
        in_specs=[anywhere] * 10,
        out_specs=[anywhere] * 2,
        out_shape=[
            jax.ShapeDtypeStruct((2, rows, width), LOW),
            jax.ShapeDtypeStruct((micro, tokens, width), LOW),
        ],
        scratch_shapes=work
        + [quad, quad, work[2]]
        + [
            pltpu.VMEM((chunks, 2, 4, PIECE, width), LOW),
            pltpu.VMEM((chunks, 4, PIECE, width), LOW),
            pltpu.VMEM((chunks, 2, PIECE, width), LOW),
            pltpu.VMEM((chunks, 2, PIECE, width), LOW),
            pltpu.VMEM((chunks, 1, PIECE, width), LOW),
            pltpu.VMEM((2, rows, width), LOW),
            pltpu.SemaphoreType.DMA((2, 6)),
            pltpu.SemaphoreType.DMA((2,)),
            pltpu.SemaphoreType.DMA((1,)),
            pltpu.SemaphoreType.DMA((1,)),
            pltpu.SemaphoreType.DMA((3,)),
            pltpu.SemaphoreType.DMA((3,)),
            pltpu.SemaphoreType.DMA((chunks, 5)),
            pltpu.SemaphoreType.DMA((chunks, 5)),
        ],
        compiler_params=pltpu.CompilerParams(
            collective_id=1, has_side_effects=True, vmem_limit_bytes=VMEM_BYTES
        ),
    )(*arrays, vec_zero, *quads, vec_one, grad, final)


def update_kernel(shares, halves_ref, *refs):
    old, new, turned = refs[:9], refs[9:18], refs[18]
    offset = lax.axis_index((DP, SEQ)) * shares.columns
    half, per, width, depth = shares.half, shares.per, shares.width, shares.depth // 2
    is_inner = (offset >= 3 * width) & (offset < 4 * width)
    is_hidden = offset >= 4 * width

    @pl.when(is_inner)
    def _():
        for side in range(2):
            piece = halves_ref[side, :half, :].astype(jnp.float32)
            wide = per * half
            back = jnp.transpose(jnp.concatenate([piece[:, :wide], piece[:, wide:]], axis=0))
            for j in range(per):
                turned[(2 * j + side) * half : (2 * j + side + 1) * half, :] = back[
                    j * half : (j + 1) * half
                ]

    @pl.when(jnp.logical_not(is_inner))
    def _():
        pair = [halves_ref[side, :half, :].astype(jnp.float32) for side in range(2)]
        plain = jnp.concatenate(pair, axis=0)
        hidden = jnp.concatenate(
            [pair[side][j * depth :][:depth] for j in range(shares.groups) for side in range(2)],
            axis=0,
        )
        turned[...] = jnp.transpose(jnp.where(is_hidden, hidden, plain))

    def store(first, gradient, rate, decay):
        results = adam_update(*[ref[...] for ref in old[first : first + 3]], gradient, rate, decay)
        for ref, result in zip(new[first : first + 3], results):
            ref[...] = result

    store(0, turned[...], rate_matrix, decay_matrix)
    down = [halves_ref[side, half : half + depth, :] for side in range(2)]
    store(3, jnp.concatenate(down, axis=0).astype(jnp.float32), rate_matrix, decay_matrix)
    tails = [halves_ref[side, half + depth :, :].astype(jnp.float32) for side in range(2)]
    store(6, (tails[0] + tails[1])[0:1, : shares.vector_len], rate_vector, 0.0)


def update(shares, halves, old):
    return pl.pallas_call(
        partial(update_kernel, shares),
        out_shape=[jax.ShapeDtypeStruct(piece.shape, jnp.float32) for piece in old],
        scratch_shapes=[pltpu.VMEM((shares.width, shares.columns), jnp.float32)],
        compiler_params=pltpu.CompilerParams(vmem_limit_bytes=VMEM_BYTES),
    )(halves, *old)


ROWS = 256
COLS = 384
STRIP = 32


def whole(shape):
    return pl.BlockSpec(shape, lambda i: (0,) * len(shape))


def row_block(width):
    return pl.BlockSpec((ROWS, width), lambda i: (i, 0))


def col_block(tokens):
    return pl.BlockSpec((tokens, COLS), lambda i: (0, i))


def at_block(shape, *index):
    return pl.BlockSpec(shape, lambda i: index)


def params_of(flops, moved, transcendentals=0):
    return {
        "compiler_params": pltpu.CompilerParams(vmem_limit_bytes=VMEM_BYTES),
        "cost_estimate": pl.CostEstimate(
            flops=flops, bytes_accessed=moved, transcendentals=transcendentals
        ),
    }


def strips(length=ROWS, strip=STRIP):
    return [slice(first, first + strip) for first in range(0, length, strip)]


def eights(values):
    rows, width = values.shape
    return jnp.sum(values.reshape(rows // 8, 8, width), axis=0)


def features_kernel(shares, random_ref, segment_ref, global_ref, query_ref, key_ref, turned_ref):
    core = lax.axis_index(SECTION)
    place = lax.axis_index(SEQ)
    blocks = random_ref.shape[1]
    width = key_ref.shape[1]
    heads = query_ref.shape[0]
    per_half = heads // shares.per
    picks = random_ref.shape[2] // (2 * heads)
    tokens = key_ref.shape[0]
    lane = lax.broadcasted_iota(jnp.int32, (blocks, width), 1)
    row = lax.broadcasted_iota(jnp.int32, (blocks, width), 0)
    key = jnp.where(lane < blocks, lane, lane - blocks)
    chosen = random_ref[place]
    named = global_ref[place]
    always = (jnp.abs(row - key) <= 1).astype(jnp.int32)
    is_global = jnp.zeros((blocks, width), jnp.int32)
    for index in range(named.shape[1]):
        spot = named[:, index : index + 1]
        always = always + (key == spot).astype(jnp.int32)
        is_global = is_global + (row == spot).astype(jnp.int32)
    line = segment_ref[place].astype(jnp.float32)
    column = jnp.transpose(jnp.broadcast_to(line, (8, tokens)))[:, 0:1]
    token_lane = lax.broadcasted_iota(jnp.int32, (tokens, width), 1)
    same = column == (token_lane - 2 * blocks).astype(jnp.float32)
    in_segment = (token_lane >= 2 * blocks) & (token_lane < 2 * blocks + 3)
    segment_side = jnp.where(in_segment & same, 1.0, 0.0)
    for head in range(heads):
        count = always
        for pick in range(picks):
            at = [
                (2 * per_half * (head // per_half) + per_half * side + head % per_half) * picks
                + pick
                for side in range(2)
            ]
            spot = jnp.where(core == 0, chosen[:, at[0] : at[0] + 1], chosen[:, at[1] : at[1] + 1])
            count = count + (key == spot).astype(jnp.int32)
        count = jnp.where(is_global > 0, 1, count)
        high = jnp.where(count == 0, masked, 0.0)
        low = jnp.zeros_like(high)
        for times in (2, 3):
            high = jnp.where(count == times, LOG_HIGH[times - 1], high)
            low = jnp.where(count == times, LOG_LOW[times - 1], low)
        table = jnp.where(lane < blocks, high, jnp.where(lane < 2 * blocks, low, 0.0))
        for block in range(blocks):
            rows = slice(block * BLOCK, (block + 1) * BLOCK)
            query_ref[head, rows, :] = (table[block : block + 1] + segment_side[rows]).astype(LOW)
    token_block = lax.shift_right_logical(
        lax.broadcasted_iota(jnp.int32, (tokens, width), 0), BLOCK.bit_length() - 1
    )
    here = (token_block == token_lane) | (token_block == token_lane - blocks)
    side = jnp.where(here & (token_lane < 2 * blocks), 1.0, 0.0)
    side = jnp.where(in_segment & jnp.logical_not(same), masked, side)
    ones = (token_lane >= 2 * blocks + 3) & (token_lane < 2 * blocks + 6)
    side = jnp.where(ones, 1.0, side)
    key_ref[...] = side.astype(LOW)
    turned_ref[...] = jnp.transpose(side).astype(LOW)


def key_features(shares, random_ids, segment_ids, global_ids):
    micro, _, blocks, head_count, picks = random_ids.shape
    tokens = segment_ids.shape[2]
    width = -(-(2 * blocks + 6) // 128) * 128
    return pl.pallas_call(
        partial(features_kernel, shares),
        out_shape=[
            jax.ShapeDtypeStruct((head_count // 2, tokens, width), LOW),
            jax.ShapeDtypeStruct((tokens, width), LOW),
            jax.ShapeDtypeStruct((width, tokens), LOW),
        ],
        **params_of(0, head_count * tokens * width),
    )(random_ids.reshape(micro, blocks, head_count * picks), segment_ids, global_ids)


def project_kernel(joins, *refs):
    if joins:
        (middle_ref, part_ref, recv_ref, bias_down_ref), refs = refs[:4], refs[4:]
    else:
        hidden_ref, refs = refs[0], refs[1:]
    (gain_ref, shift_ref, weight_ref, bias_ref), refs = refs[:4], refs[4:]
    if joins:
        hidden_ref, refs = refs[0], refs[1:]
    normed_ref, out_ref = refs
    for rows in strips():
        if joins:
            part = part_ref[rows, :] + recv_ref[rows, :].astype(jnp.float32)
            low = (middle_ref[rows, :] + part + bias_down_ref[...]).astype(LOW)
            hidden_ref[rows, :] = low
        else:
            low = hidden_ref[rows, :]
        unit, _ = normalized(low.astype(jnp.float32))
        normed_ref[rows, :] = (unit * gain_ref[...] + shift_ref[...]).astype(LOW)
    for first in range(0, out_ref.shape[1], COLS):
        cols = slice(first, first + COLS)
        product = dot_rows(normed_ref[...], weight_ref[cols, :])
        out_ref[:, cols] = (product + bias_ref[:, cols]).astype(LOW)


def project(before, gain, shift, rows, bias):
    joins = len(before) > 1
    tokens, width = before[0].shape
    out_width = bias.shape[1]
    small = whole((1, width))
    ins = [row_block(width)] * 3 + [small] if joins else [row_block(width)]
    outs = [row_block(width)] * (2 if joins else 1)
    low = jax.ShapeDtypeStruct((tokens, width), LOW)
    return pl.pallas_call(
        partial(project_kernel, joins),
        grid=(tokens // ROWS,),
        in_specs=ins + [small, small, whole((out_width, width)), whole((1, out_width))],
        out_specs=outs + [row_block(out_width)],
        out_shape=[low] * len(outs) + [jax.ShapeDtypeStruct((tokens, out_width), LOW)],
        **params_of(2 * tokens * width * out_width, tokens * width * 16),
    )(*before, gain, shift, rows, bias)


def out_halves(packed_ref, half):
    wide = packed_ref.shape[1] // 2
    return [
        jnp.concatenate([packed_ref[rows, :wide], packed_ref[rows, wide:]], axis=0)
        for rows in (slice(0, half), slice(half, 2 * half))
    ]


def branch_kernel(half, attended_ref, packed_ref, branch_ref, low_ref):
    wide = attended_ref.shape[1]
    for index, weights in enumerate(out_halves(packed_ref, half)):
        cols = slice(index * wide, (index + 1) * wide)
        product = dot_rows(attended_ref[...], weights)
        branch_ref[:, cols] = product
        low_ref[:, cols] = product.astype(LOW)


def branch_out(shares, attended, rows):
    tokens, wide = attended.shape
    width = rows.shape[1]
    return pl.pallas_call(
        partial(branch_kernel, shares.half),
        grid=(tokens // ROWS,),
        in_specs=[row_block(wide), at_block((COLS, width), 3, 0)],
        out_specs=[row_block(width)] * 2,
        out_shape=[
            jax.ShapeDtypeStruct((tokens, width), jnp.float32),
            jax.ShapeDtypeStruct((tokens, width), LOW),
        ],
        **params_of(2 * tokens * width * wide, tokens * width * 8),
    )(attended, rows)


def gelu_parts(value):
    below = 1.0 + (0.3275911 * 0.5**0.5) * jnp.abs(value)
    rough = pl.reciprocal(below, approx=True)
    t = rough * (2.0 - below * rough)
    bell = jnp.exp((-0.5 * value) * value)
    poly = 0.5 * 1.061405429
    for coefficient in (-1.453152027, 1.421413741, -0.284496736, 0.254829592):
        poly = poly * t + 0.5 * coefficient
    tail = poly * (t * bell)
    cdf = jnp.where(value > 0, 1.0 - tail, tail)
    return value * cdf, cdf + value * (bell * (0.5 / math.pi) ** 0.5)


def expand_kernel(
    hidden_ref,
    branch_ref,
    recv_ref,
    bias_out_ref,
    gain_ref,
    shift_ref,
    up_ref,
    down_ref,
    bias_up_ref,
    middle_ref,
    normed_ref,
    slope_ref,
    active_ref,
    part_ref,
    low_ref,
    held,
):
    for rows in strips():
        branch = branch_ref[rows, :] + recv_ref[rows, :].astype(jnp.float32)
        middle = hidden_ref[rows, :].astype(jnp.float32) + (branch + bias_out_ref[...])
        middle_ref[rows, :] = middle
        unit, _ = normalized(middle)
        normed_ref[rows, :] = (unit * gain_ref[...] + shift_ref[...]).astype(LOW)
    for index in range(up_ref.shape[0] // COLS):
        cols = slice(index * COLS, (index + 1) * COLS)
        held[index] = dot_rows(normed_ref[...], up_ref[cols, :])
        for rows in strips():
            active, slope = gelu_parts(held[index, rows, :] + bias_up_ref[:, cols])
            active_ref[rows, cols] = active.astype(LOW)
            slope_ref[rows, cols] = slope
    part = dot_plain(active_ref[...], down_ref[...])
    part_ref[...] = part
    low_ref[...] = part.astype(LOW)


def expand(hidden, branch, recv, bias_out, gain, shift, rows, down, bias_up):
    tokens, width = hidden.shape
    inner = down.shape[0]
    small = whole((1, width))
    return pl.pallas_call(
        expand_kernel,
        grid=(tokens // ROWS,),
        in_specs=[row_block(width)] * 3
        + [small, small, small, at_block((inner, width), 1, 0)]
        + [whole((inner, width)), whole((1, inner))],
        out_specs=[row_block(width), row_block(width), row_block(inner), row_block(inner)]
        + [row_block(width), row_block(width)],
        out_shape=[
            jax.ShapeDtypeStruct((tokens, width), jnp.float32),
            jax.ShapeDtypeStruct((tokens, width), LOW),
            jax.ShapeDtypeStruct((tokens, inner), jnp.float32),
            jax.ShapeDtypeStruct((tokens, inner), LOW),
            jax.ShapeDtypeStruct((tokens, width), jnp.float32),
            jax.ShapeDtypeStruct((tokens, width), LOW),
        ],
        scratch_shapes=[pltpu.VMEM((inner // COLS, ROWS, COLS), jnp.float32)],
        **params_of(4 * tokens * width * inner, tokens * width * 32, tokens * inner),
    )(hidden, branch, recv, bias_out, gain, shift, rows, down, bias_up)


def expand_back_kernel(
    grad_ref,
    slope_ref,
    up_ref,
    down_ref,
    part_ref,
    low_ref,
    grad_up_ref,
    bias_up_ref,
    bias_down_ref,
    sums_up,
    sums_down,
):
    step = pl.program_id(0)

    @pl.when(step == 0)
    def _():
        sums_up[...] = jnp.zeros_like(sums_up)
        sums_down[...] = jnp.zeros_like(sums_down)

    for index in range(down_ref.shape[0] // COLS):
        cols = slice(index * COLS, (index + 1) * COLS)
        grad_up = dot_rows(grad_ref[...], down_ref[cols, :]) * slope_ref[:, cols]
        grad_up_ref[:, cols] = grad_up.astype(LOW)
    part = dot_plain(grad_up_ref[...], up_ref[...])
    part_ref[...] = part
    low_ref[...] = part.astype(LOW)
    for rows in strips():
        sums_up[...] += eights(grad_up_ref[rows, :].astype(jnp.float32))
        sums_down[...] += eights(grad_ref[rows, :].astype(jnp.float32))

    @pl.when(step == pl.num_programs(0) - 1)
    def _():
        bias_up_ref[...] = jnp.sum(sums_up[...], axis=0, keepdims=True)
        bias_down_ref[...] = jnp.sum(sums_down[...], axis=0, keepdims=True)


def expand_back(grad, slope, rows, down):
    tokens, width = grad.shape
    inner = down.shape[0]
    return pl.pallas_call(
        expand_back_kernel,
        grid=(tokens // ROWS,),
        in_specs=[row_block(width), row_block(inner)]
        + [at_block((inner, width), 1, 0), whole((inner, width))],
        out_specs=[row_block(width), row_block(width), row_block(inner)]
        + [whole((1, inner)), whole((1, width))],
        out_shape=[
            jax.ShapeDtypeStruct((tokens, width), jnp.float32),
            jax.ShapeDtypeStruct((tokens, width), LOW),
            jax.ShapeDtypeStruct((tokens, inner), LOW),
            jax.ShapeDtypeStruct((1, inner), jnp.float32),
            jax.ShapeDtypeStruct((1, width), jnp.float32),
        ],
        scratch_shapes=[pltpu.VMEM((8, inner), jnp.float32), pltpu.VMEM((8, width), jnp.float32)],
        **params_of(4 * tokens * width * inner, tokens * width * 24),
    )(grad, slope, rows, down)


def token_products_kernel(count, *refs):
    lefts, rights, outs = refs[:count], refs[count : 2 * count], refs[2 * count :]
    for left, right, out in zip(lefts, rights, outs):
        for first in range(0, COLS, 128):
            cols = slice(first, first + 128)
            out[cols, :] = dot_tokens(left[:, cols], right[...]).astype(LOW)


def token_products(*pairs):
    lefts, rights = zip(*pairs)
    tokens, inner = lefts[0].shape
    width = rights[0].shape[1]
    count = len(pairs)
    return pl.pallas_call(
        partial(token_products_kernel, count),
        grid=(inner // COLS,),
        in_specs=[col_block(tokens)] * count + [whole((tokens, width))] * count,
        out_specs=[pl.BlockSpec((COLS, width), lambda i: (i, 0))] * count,
        out_shape=[jax.ShapeDtypeStruct((inner, width), LOW)] * count,
        **params_of(2 * count * tokens * width * inner, count * tokens * width * 8),
    )(*lefts, *rights)


def norm_back_rows(values_in, incoming, gain_vec):
    unit, scale = normalized(values_in)
    p = incoming * gain_vec
    mean_p = jnp.mean(p, axis=-1, keepdims=True)
    mean_pn = jnp.mean(p * unit, axis=-1, keepdims=True)
    return scale * (p - mean_p - unit * mean_pn), eights(incoming * unit), eights(incoming)


def branch_back_kernel(
    half,
    middle_ref,
    part_ref,
    recv_ref,
    grad_ref,
    attended_ref,
    gain_ref,
    packed_ref,
    grad_middle_ref,
    grad_attended_ref,
    out_grad_ref,
    gain_grad_ref,
    shift_grad_ref,
    bias_grad_ref,
    total,
    low,
    sums,
):
    step = pl.program_id(0)

    @pl.when(step == 0)
    def _():
        total[...] = jnp.zeros_like(total)
        sums[...] = jnp.zeros_like(sums)

    for rows in strips():
        incoming = part_ref[rows, :] + recv_ref[rows, :].astype(jnp.float32)
        change, for_gain, for_shift = norm_back_rows(middle_ref[rows, :], incoming, gain_ref[...])
        grad_middle = grad_ref[rows, :].astype(jnp.float32) + change
        grad_middle_ref[rows, :] = grad_middle
        rounded = grad_middle.astype(LOW)
        low[rows, :] = rounded
        sums[0] += for_gain
        sums[1] += for_shift
        sums[2] += eights(rounded.astype(jnp.float32))
    weights = out_halves(packed_ref, half)
    wide = weights[0].shape[0]
    attended = attended_ref[...]
    pieces = [low[:, :wide], low[:, wide:]]
    grad_attended_ref[...] = (
        dot_plain(pieces[0], weights[0]) + dot_plain(pieces[1], weights[1])
    ).astype(LOW)
    for index in range(2):
        total[index] += dot_tokens(pieces[index], attended)

    @pl.when(step == pl.num_programs(0) - 1)
    def _():
        for index in range(2):
            joined = jnp.concatenate([total[index, :half, :], total[index, half:, :]], axis=1)
            out_grad_ref[index * half : (index + 1) * half, :] = joined.astype(LOW)
        for index, ref in enumerate((gain_grad_ref, shift_grad_ref, bias_grad_ref)):
            ref[...] = jnp.sum(sums[index], axis=0, keepdims=True)


def branch_back(shares, middle, part, recv, grad, attended, gain, rows):
    tokens, width = middle.shape
    wide = attended.shape[1]
    small = whole((1, width))
    one = jax.ShapeDtypeStruct((1, width), jnp.float32)
    return pl.pallas_call(
        partial(branch_back_kernel, shares.half),
        grid=(tokens // ROWS,),
        in_specs=[row_block(width)] * 4 + [row_block(wide), small, at_block((COLS, width), 3, 0)],
        out_specs=[row_block(width), row_block(wide), whole((COLS, width)), small, small, small],
        out_shape=[
            jax.ShapeDtypeStruct((tokens, width), jnp.float32),
            jax.ShapeDtypeStruct((tokens, wide), LOW),
            jax.ShapeDtypeStruct((COLS, width), LOW),
            one,
            one,
            one,
        ],
        scratch_shapes=[
            pltpu.VMEM((2, width // 2, wide), jnp.float32),
            pltpu.VMEM((ROWS, width), LOW),
            pltpu.VMEM((3, 8, width), jnp.float32),
        ],
        **params_of(4 * tokens * width * wide, tokens * width * 20),
    )(middle, part, recv, grad, attended, gain, rows)


def project_back_kernel(grad_ref, weight_ref, part_ref, low_ref, bias_ref, sums):
    step = pl.program_id(0)

    @pl.when(step == 0)
    def _():
        sums[...] = jnp.zeros_like(sums)

    part = dot_plain(grad_ref[...], weight_ref[...])
    part_ref[...] = part
    low_ref[...] = part.astype(LOW)
    for rows in strips():
        sums[...] += eights(grad_ref[rows, :].astype(jnp.float32))

    @pl.when(step == pl.num_programs(0) - 1)
    def _():
        bias_ref[...] = jnp.sum(sums[...], axis=0, keepdims=True)


def project_back(grad_proj, rows):
    tokens, out_width = grad_proj.shape
    width = rows.shape[1]
    return pl.pallas_call(
        project_back_kernel,
        grid=(tokens // ROWS,),
        in_specs=[row_block(out_width), whole((out_width, width))],
        out_specs=[row_block(width), row_block(width), whole((1, out_width))],
        out_shape=[
            jax.ShapeDtypeStruct((tokens, width), jnp.float32),
            jax.ShapeDtypeStruct((tokens, width), LOW),
            jax.ShapeDtypeStruct((1, out_width), jnp.float32),
        ],
        scratch_shapes=[pltpu.VMEM((8, out_width), jnp.float32)],
        **params_of(2 * tokens * width * out_width, tokens * width * 12),
    )(grad_proj, rows)


def input_back_kernel(
    hidden_ref, part_ref, recv_ref, grad_ref, gain_ref, out_ref, gain_grad_ref, shift_grad_ref, sums
):
    step = pl.program_id(0)

    @pl.when(step == 0)
    def _():
        sums[...] = jnp.zeros_like(sums)

    for rows in strips():
        incoming = part_ref[rows, :] + recv_ref[rows, :].astype(jnp.float32)
        hidden = hidden_ref[rows, :].astype(jnp.float32)
        change, for_gain, for_shift = norm_back_rows(hidden, incoming, gain_ref[...])
        out_ref[rows, :] = (grad_ref[rows, :] + change).astype(LOW)
        sums[0] += for_gain
        sums[1] += for_shift

    @pl.when(step == pl.num_programs(0) - 1)
    def _():
        gain_grad_ref[...] = jnp.sum(sums[0], axis=0, keepdims=True)
        shift_grad_ref[...] = jnp.sum(sums[1], axis=0, keepdims=True)


def input_back(hidden, part, recv, grad_middle, gain):
    tokens, width = hidden.shape
    small = whole((1, width))
    one = jax.ShapeDtypeStruct((1, width), jnp.float32)
    return pl.pallas_call(
        input_back_kernel,
        grid=(tokens // ROWS,),
        in_specs=[row_block(width)] * 4 + [small],
        out_specs=[row_block(width), small, small],
        out_shape=[jax.ShapeDtypeStruct((tokens, width), LOW), one, one],
        scratch_shapes=[pltpu.VMEM((2, 8, width), jnp.float32)],
        **params_of(0, tokens * width * 12),
    )(hidden, part, recv, grad_middle, gain)


def attend_kernel(q_ref, k_ref, v_ref, qa_ref, kt_ref, out_ref, lse_ref, keys, held, low):
    tokens, pair = q_ref.shape
    left = lax.broadcasted_iota(jnp.int32, (CHUNK, pair), 1) < pair // 2
    keys[:pair, :] = jnp.transpose(k_ref[...].astype(jnp.float32)).astype(LOW)
    keys[pair:, :] = kt_ref[...]
    for index in range(tokens // CHUNK):
        rows = slice(index * CHUNK, (index + 1) * CHUNK)
        queries = q_ref[rows, :] * 0.125
        outs, tops = [], []
        for head in range(2):
            slot = (2 * index + head) % held.shape[0]
            mine = left if head == 0 else jnp.logical_not(left)
            side = jnp.where(mine, queries, jnp.zeros_like(queries))
            lhs = jnp.concatenate([side, qa_ref[head, rows, :]], axis=1)
            held[slot] = dot_plain(lhs, keys[...])
            levels, shares = [], []
            for strip in strips(CHUNK):
                scores = held[slot, strip, :]
                top = jnp.max(scores, axis=1, keepdims=True)
                weight = jnp.exp(scores - top)
                total = jnp.sum(weight, axis=1, keepdims=True)
                low[slot, strip, :] = weight.astype(LOW)
                levels.append(top + jnp.log(total))
                shares.append(1.0 / total)
            product = dot_plain(low[slot], v_ref[...])
            outs.append(product * jnp.concatenate(shares, axis=0))
            tops.append(jnp.concatenate(levels, axis=0))
        out_ref[rows, :] = jnp.where(left, outs[0], outs[1]).astype(LOW)
        lse_ref[rows, :] = jnp.where(left, tops[0], tops[1])


def attend(projected, query_side, key_side, turned):
    tokens = projected.shape[0]
    width = projected.shape[1] // 3
    pairs = width // 128
    features = key_side.shape[1]
    return pl.pallas_call(
        attend_kernel,
        grid=(pairs,),
        in_specs=[
            pl.BlockSpec((tokens, 128), lambda p: (0, p)),
            pl.BlockSpec((tokens, 128), lambda p: (0, pairs + p)),
            pl.BlockSpec((tokens, 128), lambda p: (0, 2 * pairs + p)),
            pl.BlockSpec((2, tokens, features), lambda p: (p, 0, 0)),
            whole((features, tokens)),
        ],
        out_specs=[
            pl.BlockSpec((tokens, 128), lambda p: (0, p)),
            pl.BlockSpec((tokens, 128), lambda p: (0, p)),
        ],
        out_shape=[
            jax.ShapeDtypeStruct((tokens, width), LOW),
            jax.ShapeDtypeStruct((tokens, width), jnp.float32),
        ],
        scratch_shapes=[
            pltpu.VMEM((128 + features, tokens), LOW),
            pltpu.VMEM((4, CHUNK, tokens), jnp.float32),
            pltpu.VMEM((4, CHUNK, tokens), LOW),
        ],
        **params_of(
            16 * pairs * tokens * tokens * 128, tokens * width * 16, 2 * pairs * tokens * tokens
        ),
    )(projected, projected, projected, query_side, turned)


def three_terms(values):
    high = values.astype(LOW).astype(jnp.float32)
    rest = values - high
    middle = rest.astype(LOW).astype(jnp.float32)
    return high, middle, rest - middle


def attend_back_kernel(
    q_ref,
    k_ref,
    v_ref,
    do_ref,
    o_ref,
    lse_ref,
    qa_ref,
    ka_ref,
    grad_ref,
    held,
    probs,
    changes,
    query_sides,
    grad_sides,
):
    tokens, pair = q_ref.shape
    features = ka_ref.shape[1]
    pairs = pl.num_programs(0)
    place = pl.program_id(0)
    first = 2 * (tokens // BLOCK) + 3
    half = pair // 2
    left = lax.broadcasted_iota(jnp.int32, (CHUNK, pair), 1) < half
    lane = lax.broadcasted_iota(jnp.int32, (CHUNK, features), 1)
    lane_pair = lax.broadcasted_iota(jnp.int32, (CHUNK, pair), 1)
    keys = jnp.concatenate([k_ref[...], ka_ref[...]], axis=1)
    turned = jnp.transpose(k_ref[...].astype(jnp.float32)).astype(LOW)
    ones = (lax.broadcasted_iota(jnp.int32, (tokens, pair), 1) < 3).astype(jnp.float32).astype(LOW)
    values = jnp.concatenate([v_ref[...], ones], axis=1)
    parts, key_grads, value_grads = [], [], []
    for head in range(2):
        mine = left if head == 0 else jnp.logical_not(left)
        for index in range(tokens // CHUNK):
            rows = slice(index * CHUNK, (index + 1) * CHUNK)
            slot = index % 2
            queries = q_ref[rows, :] * 0.125
            grads = do_ref[rows, :]
            product = grads.astype(jnp.float32) * o_ref[rows, :].astype(jnp.float32)
            level = lse_ref[rows, head * half : head * half + 1]
            inner = jnp.sum(jnp.where(mine, product, 0.0), axis=1, keepdims=True)
            side = qa_ref[head, rows, :].astype(jnp.float32)
            for spot, term in enumerate(three_terms(level)):
                side = jnp.where(lane == first + spot, -term, side)
            query_side = jnp.where(mine, queries, jnp.zeros_like(queries))
            grad_side = jnp.where(mine, grads, jnp.zeros_like(grads))
            query_sides[head, rows, :] = query_side
            grad_sides[head, rows, :] = grad_side
            tail = jnp.zeros((CHUNK, pair), jnp.float32)
            for spot, term in enumerate(three_terms(inner)):
                tail = jnp.where(lane_pair == spot, -term, tail)
            held[slot, 0] = dot_rows(
                keys, jnp.concatenate([query_side, side.astype(LOW)], axis=1)
            )
            held[slot, 1] = dot_rows(
                values, jnp.concatenate([grad_side, tail.astype(LOW)], axis=1)
            )
            for strip in strips(tokens, 128):
                prob = jnp.exp(held[slot, 0, strip, :])
                probs[head, strip, rows] = prob.astype(LOW)
                changes[head, strip, rows] = (prob * held[slot, 1, strip, :]).astype(LOW)
        value_grads.append(dot_plain(probs[head], grad_sides[head]))
        key_grads.append(dot_plain(changes[head], query_sides[head]))
        parts.append(dot_plain(turned, changes[head]))
    joined = jnp.concatenate([parts[0][:half], parts[1][half:]], axis=0)
    column = [pl.ds(pl.multiple_of((by * pairs + place) * 128, 128), 128) for by in range(3)]
    grad_ref[:, column[0]] = (jnp.transpose(joined) * 0.125).astype(LOW)
    grad_ref[:, column[1]] = (key_grads[0] + key_grads[1]).astype(LOW)
    grad_ref[:, column[2]] = (value_grads[0] + value_grads[1]).astype(LOW)


def attend_back(projected, grad_attended, attended, levels, query_side, key_side):
    tokens, width = attended.shape
    pairs = width // 128
    features = key_side.shape[1]
    by_pair = pl.BlockSpec((tokens, 128), lambda p: (0, p))
    return pl.pallas_call(
        attend_back_kernel,
        grid=(pairs,),
        in_specs=[
            by_pair,
            pl.BlockSpec((tokens, 128), lambda p: (0, pairs + p)),
            pl.BlockSpec((tokens, 128), lambda p: (0, 2 * pairs + p)),
            by_pair,
            by_pair,
            by_pair,
            pl.BlockSpec((2, tokens, features), lambda p: (p, 0, 0)),
            whole((tokens, features)),
        ],
        out_specs=whole((tokens, 3 * width)),
        out_shape=jax.ShapeDtypeStruct((tokens, 3 * width), LOW),
        scratch_shapes=[
            pltpu.VMEM((2, 2, tokens, CHUNK), jnp.float32),
            pltpu.VMEM((2, tokens, tokens), LOW),
            pltpu.VMEM((2, tokens, tokens), LOW),
            pltpu.VMEM((2, tokens, 128), LOW),
            pltpu.VMEM((2, tokens, 128), LOW),
        ],
        **params_of(
            40 * pairs * tokens * tokens * 128, tokens * width * 24, 2 * pairs * tokens * tokens
        ),
    )(projected, projected, projected, grad_attended, attended, levels, query_side, key_side)


def window_forward(shares, before, weights, biases, features, beside):
    rows, down = weights
    gain_one, shift_one, bias_query, bias_value, bias_out = biases[:5]
    gain_two, shift_two, _, bias_up = biases[5:]
    bias = jnp.concatenate([bias_query, jnp.zeros_like(bias_query), bias_value], axis=1)
    results = project(before, gain_one, shift_one, rows, bias)
    hidden = before[0] if len(before) == 1 else results[0]
    normed, projected = results[-2:]
    projected = beside.tie(projected)
    attended, levels = beside.tie(tuple(attend(projected, *features)))
    branch, low = branch_out(shares, attended, rows)
    expanded = expand(
        hidden, branch, swap(low), bias_out, gain_two, shift_two, rows, down, bias_up
    )
    middle, normed_two, slope, active, part, low = beside.tie(tuple(expanded))
    stored = (hidden, normed, projected, attended, levels, middle, normed_two, slope, active)
    return (middle, part, swap(low), biases[7]), stored


def window_backward(shares, stored, grad, weights, biases, features, beside):
    hidden, normed, projected, attended, levels, middle, normed_two, slope, active = stored
    rows, down = weights
    part, low, grad_up, bias_up, bias_down = beside.tie(
        tuple(expand_back(grad, slope, rows, down))
    )
    arrived = swap(low)
    down_grad, up_grad = token_products((active, grad), (grad_up, normed_two))
    grad_middle, grad_attended, out_grad, gain_two, shift_two, bias_out = branch_back(
        shares, middle, part, arrived, grad, attended, biases[5], rows
    )
    grad_attended = beside.tie(grad_attended)
    grad_proj = attend_back(projected, grad_attended, attended, levels, *features[:2])
    grad_proj = beside.tie(grad_proj)
    part, low, summed = project_back(grad_proj, rows)
    arrived = swap(low)
    (proj_grad,) = token_products((grad_proj, normed))
    grad, gain_one, shift_one = input_back(hidden, part, arrived, grad_middle, biases[0])
    width = attended.shape[1]
    vector_grads = (gain_one, shift_one, summed[:, :width], summed[:, 2 * width :], bias_out)
    vector_grads += (gain_two, shift_two, bias_down, bias_up)
    vector_grads = [piece[0] for piece in vector_grads]
    return grad, (proj_grad, out_grad, up_grad, down_grad), vector_grads


def window_shards(
    block_input,
    cotangent,
    random_ids,
    segment_ids,
    global_ids,
    w_rows,
    w_rows_first,
    w_rows_second,
    w_down,
    w_down_first,
    w_down_second,
    vectors,
    vectors_first,
    vectors_second,
):
    core = lax.axis_index(SECTION)
    micro, _, tokens, width = block_input.shape
    _, _, columns = w_rows.shape
    shares = Shares(width, columns, w_down.shape[1], vectors.shape[1])
    prepared = prepare(shares, w_rows[0], w_down[0], vectors)
    features = key_features(shares, random_ids, segment_ids, global_ids)
    gathered_zero, gathered_one, hidden, grad = gather(shares, prepared, block_input, cotangent)

    beside = Beside(spread_quads(shares, gathered_one[:2]))
    params = [shares.unpack(gathered_zero, core)]
    before = (hidden.reshape(-1, width),)
    before, stored_zero = window_forward(shares, before, *params[0], features, beside)
    params.append(shares.unpack((*beside.flying, gathered_one[2]), core))
    after, stored_one = window_forward(shares, before, *params[1], features, Beside())
    final = (after[0] + (after[1] + after[2].astype(jnp.float32) + after[3])).astype(LOW)

    grad = grad.reshape(-1, width)
    grad, *grads_one = window_backward(shares, stored_one, grad, *params[1], features, Beside())
    *arrays_one, vec_one = shares.by_shard(*grads_one, core)
    beside = Beside(sum_quads(shares, arrays_one))
    grad, *grads_zero = window_backward(shares, stored_zero, grad, *params[0], features, beside)
    *arrays_zero, vec_zero = shares.by_shard(*grads_zero, core)
    grad, final = [piece.reshape(micro, tokens, width) for piece in (grad, final)]
    halves, slices = scatter(shares, arrays_zero, vec_zero, beside.flying, vec_one, grad, final)
    section_result = slices.astype(jnp.float32)[None, :, None]
    old = [
        w_rows[0],
        w_rows_first[0],
        w_rows_second[0],
        w_down[0],
        w_down_first[0],
        w_down_second[0],
        vectors,
        vectors_first,
        vectors_second,
    ]
    new = update(shares, halves, old)
    return (section_result, *[piece[None] for piece in new[:6]], *new[6:])


def one_window_each(mesh, block_input, w_rows, w_down, vectors):
    micro, windows, length, width = block_input.shape
    shards = mesh.shape[DP] * mesh.shape[SEQ]
    columns, depth = w_rows.shape[2] // shards, w_down.shape[1] // shards
    head_dim = width // HEADS
    tokens = length // mesh.shape[SEQ]
    return (
        mesh.shape[SECTION] == 2
        and mesh.shape[SEQ] == micro
        and mesh.shape[DP] == windows
        and tokens % (2 * BLOCK) == 0
        and length % CHUNK == 0
        and head_dim == 64
        and width % columns == 0
        and columns % (2 * head_dim) == 0
        and columns % depth == 0
        and width // columns * (columns // 2) % 128 == 0
        and depth % 32 == 0
        and vectors.shape[1] // shards <= width
        and mesh.shape[DP] == 4
        and micro == 4
        and width == 2 * columns == 2 * COLS
        and w_down.shape[1] == 4 * width
        and (columns // 2) % (2 * PIECE) == 0
        and (depth // 2) % (2 * PIECE) == 0
        and length % (4 * ROWS) == 0
    )


def solution(mesh):
    in_specs = (
        P(None, DP, SEQ, None),
        P(None, DP, SEQ, None),
        P(None, DP, None, None, None),
        P(None, DP, None),
        P(None, DP, None),
        P(SECTION, None, (DP, SEQ)),
        P(SECTION, None, (DP, SEQ)),
        P(SECTION, None, (DP, SEQ)),
        P(SECTION, (DP, SEQ), None),
        P(SECTION, (DP, SEQ), None),
        P(SECTION, (DP, SEQ), None),
        P(SECTION, (DP, SEQ)),
        P(SECTION, (DP, SEQ)),
        P(SECTION, (DP, SEQ)),
    )
    out_specs = (
        P(SECTION, None, DP, SEQ, None),
        P(SECTION, None, (DP, SEQ)),
        P(SECTION, None, (DP, SEQ)),
        P(SECTION, None, (DP, SEQ)),
        P(SECTION, (DP, SEQ), None),
        P(SECTION, (DP, SEQ), None),
        P(SECTION, (DP, SEQ), None),
        P(SECTION, (DP, SEQ)),
        P(SECTION, (DP, SEQ)),
        P(SECTION, (DP, SEQ)),
    )

    def step(*arrays):
        chosen = general_shards
        if one_window_each(mesh, arrays[0], arrays[5], arrays[8], arrays[11]):
            chosen = window_shards
        return jax.shard_map(
            chosen, mesh=mesh, in_specs=in_specs, out_specs=out_specs, check_vma=False
        )(*arrays)

    return step
```

```python
import math
from functools import partial

import jax
import jax.numpy as jnp
import ml_dtypes
import numpy as np
from jax import lax
from jax.experimental import pallas as pl
from jax.experimental.pallas import tpu as pltpu
from jax.sharding import PartitionSpec as P

SECTION, DP, SEQ = "section", "dp", "seq"
HEADS = 12
BLOCK = 64
STEP = 5


epsilon = 1e-05
masked = -1e30
rate_matrix = 0.02
rate_vector = 0.2
decay_matrix = 0.01


def with_halo(x, sides, width):
    for axis, dim in sides:
        devices, length = (lax.axis_size(axis), x.shape[dim])
        up = [(i, (i + 1) % devices) for i in range(devices - 1)]
        down = [(j, i) for i, j in up]
        last = lax.slice_in_dim(x, length - width, length, axis=dim)
        initial = lax.slice_in_dim(x, 0, width, axis=dim)
        before = lax.ppermute(last, axis, up)
        after = lax.ppermute(initial, axis, down)
        x = jnp.concatenate([before, x, after], axis=dim)
    return x


def merged(value, axis, join):
    pieces = jax.tree.map(lambda part: lax.all_gather(part, axis), value)
    head = jax.tree.map(lambda part: part[0], pieces)
    tail = jax.tree.map(lambda part: part[1:], pieces)
    subtotal, _ = lax.scan(lambda subtotal, share: (join(subtotal, share), None), head, tail)
    return subtotal


def from_behind(x, axis, by):
    devices = lax.axis_size(axis)
    pairs = [(i, i + by) for i in range(devices) if 0 <= i + by < devices]
    return lax.ppermute(x, axis, pairs)


def partner(value, axis, bit):
    mask = 2**bit
    pairs = [(source, source ^ mask) for source in range(lax.axis_size(axis))]
    return lax.ppermute(value, axis, pairs)


def mixed_sum(form, left, right):
    return jnp.einsum(form, left, right, preferred_element_type=jnp.float32)


def exact_two(form, left, right):
    return jnp.einsum(
        form, left, right, precision=lax.Precision.HIGHEST, preferred_element_type=jnp.float32
    )


def norm_rows(values_in, gain_vec, shift_vec):
    row_mean = jnp.mean(values_in, axis=-1, keepdims=True)
    centred = values_in - row_mean
    spread = jnp.mean(centred * centred, axis=-1, keepdims=True)
    return centred * lax.rsqrt(spread + epsilon) * gain_vec + shift_vec


def split_vectors(vector_weights, model_width):
    pieces = [
        vector_weights[piece_index * model_width : (piece_index + 1) * model_width]
        for piece_index in range(8)
    ]
    return pieces + [vector_weights[8 * model_width :]]


def route_tables(random_rows, segments, global_rows, seq_place, groups):
    windows, blocks, head_count, pick_count = random_rows.shape
    blocks_dev = blocks // groups
    request_count = blocks_dev * head_count * pick_count
    capacity = -(-request_count // groups)
    requests = random_rows.reshape(windows, groups, request_count)
    owners = requests // blocks_dev
    inside = requests % blocks_dev
    head_of = jnp.arange(request_count) // pick_count % head_count
    is_mine = owners == seq_place
    slot_index = jnp.cumsum(is_mine.astype(jnp.int32), axis=2) - 1
    slot_hot = ((slot_index[..., None] == jnp.arange(capacity)) & is_mine[..., None]).astype(
        jnp.float32
    )
    inside_hot = (inside[..., None] == jnp.arange(blocks_dev)).astype(jnp.float32)
    head_hot = (head_of[:, None] == jnp.arange(head_count)).astype(jnp.float32)
    sender = jnp.einsum(
        "wqsc,wqsb,sh->wqcbh", slot_hot, inside_hot, head_hot, precision=lax.Precision.HIGHEST
    )
    my_owners = lax.dynamic_index_in_dim(owners, seq_place, axis=1, keepdims=False)
    earlier = jnp.arange(request_count)[None, :] < jnp.arange(request_count)[:, None]
    same_owner = my_owners[:, :, None] == my_owners[:, None, :]
    rank_index = jnp.sum((same_owner & earlier[None]).astype(jnp.int32), axis=2)
    picker = (
        (my_owners[..., None, None] == jnp.arange(groups)[:, None])
        & (rank_index[..., None, None] == jnp.arange(capacity)[None, :])
    ).astype(jnp.float32)
    first_block = seq_place * blocks_dev
    owned_hot = (global_rows[:, :, None] == first_block + jnp.arange(blocks_dev)).astype(
        jnp.float32
    )
    length = segments.shape[1]
    block_len = length // blocks
    seg_blocks = segments.reshape(windows, blocks, block_len)
    seg_pad = jnp.pad(seg_blocks, ((0, 0), (1, 1), (0, 0)), constant_values=-1)
    near_segs = lax.dynamic_slice_in_dim(seg_pad, first_block, blocks_dev + 2, axis=1)
    slide_seg = jnp.concatenate([near_segs[:, :-2], near_segs[:, 1:-1], near_segs[:, 2:]], axis=2)
    query_seg = near_segs[:, 1:-1]
    rows_index = jnp.arange(windows)
    global_seg = seg_blocks[rows_index[:, None], global_rows].reshape(windows, -1)
    chosen = lax.dynamic_slice_in_dim(random_rows, first_block, blocks_dev, axis=1)
    far_seg = seg_blocks[rows_index[:, None, None, None], chosen].reshape(
        windows, blocks_dev, head_count, -1
    )
    key_seg = jnp.concatenate(
        [
            jnp.broadcast_to(
                slide_seg[:, :, None, :], (windows, blocks_dev, head_count, slide_seg.shape[2])
            ),
            jnp.broadcast_to(
                global_seg[:, None, None, :], (windows, blocks_dev, head_count, global_seg.shape[1])
            ),
            far_seg,
        ],
        axis=3,
    )
    key_mask = query_seg[:, :, None, :, None] == key_seg[:, :, :, None, :]
    local_seg = query_seg.reshape(windows, -1)
    full_mask = global_seg[:, None, :, None] == local_seg[:, None, None, :]
    return (sender, picker, owned_hot, key_mask, full_mask)


def fetch_blocks(paired, queries, sender, picker, owned_hot):
    windows, tokens, head_count, doubled = paired.shape
    head_dim = queries.shape[-1]
    blocks_dev = tokens // BLOCK
    flattened = paired.reshape(windows, tokens, head_count * doubled)
    padded = with_halo(flattened, ((SEQ, 1),), BLOCK)
    framed = padded.reshape(windows, blocks_dev + 2, BLOCK, head_count, doubled)
    sliding = jnp.concatenate([framed[:, :-2], framed[:, 1:-1], framed[:, 2:]], axis=2)
    local_blocks = paired.reshape(windows, blocks_dev, BLOCK, head_count, doubled)
    owned_low = owned_hot.astype(jnp.bfloat16)
    offered = mixed_sum("wgb,wbthe->wgthe", owned_low, local_blocks)
    offered_queries = mixed_sum("wgb,wbqhd->wgqhd", owned_low, queries)
    global_kv, global_queries = (
        lax.psum(offered.astype(jnp.bfloat16), SEQ).astype(jnp.float32),
        lax.psum(offered_queries.astype(jnp.bfloat16), SEQ).astype(jnp.float32),
    )
    global_kv = global_kv.astype(jnp.bfloat16).reshape(windows, -1, head_count, doubled)
    global_queries = global_queries.astype(jnp.bfloat16).reshape(windows, -1, head_count, head_dim)
    outgoing = mixed_sum("wqcbh,wbthe->qwcte", sender.astype(jnp.bfloat16), local_blocks).astype(
        jnp.bfloat16
    )
    incoming = lax.all_to_all(outgoing, SEQ, split_axis=0, concat_axis=0, tiled=True)
    distant = mixed_sum("wspc,pwcte->wste", picker.astype(jnp.bfloat16), incoming).astype(
        jnp.bfloat16
    )
    pick_count = picker.shape[1] // (blocks_dev * head_count)
    distant = distant.reshape(windows, blocks_dev, head_count, pick_count, BLOCK, doubled)
    return (sliding, global_kv, distant, global_queries)


def combine_stats(earlier, later):
    top = jnp.maximum(earlier[0], later[0])
    return (top, earlier[1] * jnp.exp(earlier[0] - top) + later[1] * jnp.exp(later[0] - top))


def full_forward(global_queries, key_part, value_part, full_mask, head_dim):
    scores = mixed_sum("wqhd,wkhd->whqk", global_queries, key_part) * head_dim ** (-0.5)
    scores = jnp.where(full_mask, scores, masked)
    local_top = jnp.max(scores, axis=3, keepdims=True)
    local_sum = jnp.sum(
        jnp.where(full_mask, jnp.exp(scores - local_top), 0.0), axis=3, keepdims=True
    )
    row_top, row_sum = merged((local_top, local_sum), SEQ, combine_stats)
    full_probs = jnp.where(full_mask, jnp.exp(scores - row_top), 0.0) / row_sum
    partial_out = mixed_sum("whqk,wkhd->wqhd", full_probs.astype(jnp.bfloat16), value_part)
    full_out = lax.psum(partial_out.astype(jnp.bfloat16), SEQ).astype(jnp.float32)
    return (full_out, full_probs)


def attention_weights(queries, sliding, global_kv, distant, key_mask):
    head_dim = queries.shape[-1]
    windows, blocks_dev, _, head_count, _ = queries.shape
    near_scores = mixed_sum("wbqhd,wbkhd->wbhqk", queries, sliding[..., :head_dim])
    global_scores = mixed_sum("wbqhd,wkhd->wbhqk", queries, global_kv[..., :head_dim])
    far_scores = mixed_sum("wbqhd,wbhrkd->wbhqrk", queries, distant[..., :head_dim])
    far_scores = far_scores.reshape(windows, blocks_dev, head_count, BLOCK, -1)
    scores = jnp.concatenate([near_scores, global_scores, far_scores], axis=4) * head_dim ** (-0.5)
    scores = jnp.where(key_mask, scores, masked)
    row_top = jnp.max(scores, axis=4, keepdims=True)
    weight = jnp.exp(scores - row_top)
    return weight / jnp.sum(weight, axis=4, keepdims=True)


def split_keys(scores_like, sliding, global_kv, distant):
    near_keys = sliding.shape[2]
    global_keys = global_kv.shape[1]
    windows, blocks_dev, head_count, pick_count, _, _ = distant.shape
    near_part = scores_like[..., :near_keys]
    global_part = scores_like[..., near_keys : near_keys + global_keys]
    far_part = scores_like[..., near_keys + global_keys :].reshape(
        windows, blocks_dev, head_count, BLOCK, pick_count, BLOCK
    )
    return (near_part, global_part, far_part)


def attention_values(low_probs, sliding, global_kv, distant, head_dim):
    near_part, global_part, far_part = split_keys(low_probs, sliding, global_kv, distant)
    attended = mixed_sum("wbhqk,wbkhd->wbqhd", near_part, sliding[..., head_dim:])
    attended = attended + mixed_sum("wbhqk,wkhd->wbqhd", global_part, global_kv[..., head_dim:])
    return attended + mixed_sum("wbhqrk,wbhrkd->wbqhd", far_part, distant[..., head_dim:])


def layer_forward(hidden, weights, tables):
    row_weights, down_weights, vector_weights = weights
    sender, picker, owned_hot, key_mask, full_mask = tables
    model_width = row_weights.shape[0]
    windows, tokens, _ = hidden.shape
    blocks_dev = tokens // BLOCK
    head_dim = model_width // HEADS
    (
        gain_one,
        shift_one,
        bias_query,
        bias_value,
        bias_out,
        gain_two,
        shift_two,
        bias_down,
        bias_up,
    ) = split_vectors(vector_weights, model_width)
    normed = norm_rows(hidden, gain_one, shift_one).astype(jnp.bfloat16)
    projected = mixed_sum("wtd,de->wte", normed, row_weights[:, : 3 * model_width])
    projected = (
        projected + jnp.concatenate([bias_query, jnp.zeros_like(bias_query), bias_value])
    ).astype(jnp.bfloat16)
    queries = projected[..., :model_width].reshape(windows, blocks_dev, BLOCK, HEADS, head_dim)
    key_part = projected[..., model_width : 2 * model_width].reshape(
        windows, tokens, HEADS, head_dim
    )
    value_part = projected[..., 2 * model_width :].reshape(windows, tokens, HEADS, head_dim)
    paired = jnp.concatenate([key_part, value_part], axis=3)
    sliding, global_kv, distant, global_queries = fetch_blocks(
        paired, queries, sender, picker, owned_hot
    )
    probabilities = attention_weights(queries, sliding, global_kv, distant, key_mask)
    attended = attention_values(
        probabilities.astype(jnp.bfloat16), sliding, global_kv, distant, head_dim
    )
    full_out, full_probs = full_forward(global_queries, key_part, value_part, full_mask, head_dim)
    placed = exact_two(
        "wgb,wgqhd->wbqhd", owned_hot, full_out.reshape(windows, -1, BLOCK, HEADS, head_dim)
    )
    on_global = jnp.sum(owned_hot, axis=1)[:, :, None, None, None] > 0
    attended = jnp.where(on_global, placed, attended)
    mixed_low = attended.reshape(windows, tokens, model_width).astype(jnp.bfloat16)
    middle = (
        hidden
        + mixed_sum("wtd,de->wte", mixed_low, row_weights[:, 3 * model_width : 4 * model_width])
        + bias_out
    )
    normed_two = norm_rows(middle, gain_two, shift_two).astype(jnp.bfloat16)
    up_value = mixed_sum("wtd,df->wtf", normed_two, row_weights[:, 4 * model_width :]) + bias_up
    active = jax.nn.gelu(up_value, approximate=False).astype(jnp.bfloat16)
    output = middle + mixed_sum("wtf,fd->wtd", active, down_weights) + bias_down
    stored = (
        hidden,
        normed,
        queries,
        sliding,
        global_kv,
        distant,
        probabilities,
        mixed_low,
        middle,
        normed_two,
        up_value,
        active,
        key_part,
        value_part,
        global_queries,
        full_probs,
    )
    return (output, stored)


def return_blocks(near_back, global_back, far_back, query_part, sender, picker, owned_hot):
    windows, blocks_dev, _, head_count, doubled = near_back.shape
    first_third = near_back[:, :, :BLOCK]
    centre_third = near_back[:, :, BLOCK : 2 * BLOCK]
    last_third = near_back[:, :, 2 * BLOCK :]
    framed = jnp.pad(first_third, ((0, 0), (0, 2), (0, 0), (0, 0), (0, 0)))
    framed = framed + jnp.pad(centre_third, ((0, 0), (1, 1), (0, 0), (0, 0), (0, 0)))
    framed = framed + jnp.pad(last_third, ((0, 0), (2, 0), (0, 0), (0, 0), (0, 0)))
    own_grad = framed[:, 1:-1]
    for direction in (1, -1):
        rim_grad = framed[:, -1] if direction == 1 else framed[:, 0]
        arrived = from_behind(rim_grad.astype(jnp.bfloat16), SEQ, direction).astype(
            rim_grad.dtype
        )
        if direction == 1:
            own_grad = jnp.concatenate(
                [own_grad[:, :1] + arrived[:, None], own_grad[:, 1:]], axis=1
            )
        else:
            own_grad = jnp.concatenate(
                [own_grad[:, :-1], own_grad[:, -1:] + arrived[:, None]], axis=1
            )
    global_total, query_total = (
        lax.psum(
            global_back.reshape(windows, -1, BLOCK, head_count, doubled).astype(jnp.bfloat16), SEQ
        ).astype(jnp.float32),
        lax.psum(query_part.astype(jnp.bfloat16), SEQ).astype(jnp.float32),
    )
    own_grad = own_grad + exact_two("wgb,wgthe->wbthe", owned_hot, global_total)
    far_flat = far_back.reshape(windows, -1, BLOCK, doubled)
    returning = exact_two("wspc,wste->pwcte", picker, far_flat)
    arrived_far = lax.all_to_all(
        returning.astype(jnp.bfloat16), SEQ, split_axis=0, concat_axis=0, tiled=True
    ).astype(returning.dtype)
    own_grad = own_grad + exact_two("wqcbh,qwcte->wbthe", sender, arrived_far)
    return (own_grad.reshape(windows, blocks_dev * BLOCK, head_count, doubled), query_total)


def attention_back(
    grad_attended,
    queries,
    sliding,
    global_kv,
    distant,
    probabilities,
    key_part,
    value_part,
    global_queries,
    full_probs,
    sender,
    picker,
    owned_hot,
):
    head_dim = queries.shape[-1]
    score_scale = head_dim ** (-0.5)
    windows, blocks_dev, _, head_count, _ = queries.shape
    on_global = jnp.sum(owned_hot, axis=1)[:, :, None, None, None] > 0
    selected = mixed_sum("wgb,wbqhd->wgqhd", owned_hot.astype(jnp.bfloat16), grad_attended)
    rows_grad = lax.psum(selected.astype(jnp.bfloat16), SEQ).reshape(
        windows, -1, head_count, head_dim
    )
    grad_attended = jnp.where(on_global, jnp.zeros_like(grad_attended), grad_attended)
    low_probs = probabilities.astype(jnp.bfloat16)
    near_grad = mixed_sum("wbqhd,wbkhd->wbhqk", grad_attended, sliding[..., head_dim:])
    global_grad = mixed_sum("wbqhd,wkhd->wbhqk", grad_attended, global_kv[..., head_dim:])
    far_grad = mixed_sum("wbqhd,wbhrkd->wbhqrk", grad_attended, distant[..., head_dim:])
    far_grad = far_grad.reshape(windows, blocks_dev, head_count, BLOCK, -1)
    grad_probs = jnp.concatenate([near_grad, global_grad, far_grad], axis=4)
    grad_scores = probabilities * (
        grad_probs - jnp.sum(probabilities * grad_probs, axis=4, keepdims=True)
    )
    grad_scores = grad_scores.astype(jnp.bfloat16)
    near_split, global_split, far_split = split_keys(grad_scores, sliding, global_kv, distant)
    near_probs, global_probs, far_probs = split_keys(low_probs, sliding, global_kv, distant)
    grad_query = mixed_sum("wbhqk,wbkhd->wbqhd", near_split, sliding[..., :head_dim])
    grad_query = grad_query + mixed_sum(
        "wbhqk,wkhd->wbqhd", global_split, global_kv[..., :head_dim]
    )
    grad_query = (
        grad_query + mixed_sum("wbhqrk,wbhrkd->wbqhd", far_split, distant[..., :head_dim])
    ) * score_scale
    near_back = jnp.concatenate(
        [
            mixed_sum("wbhqk,wbqhd->wbkhd", near_split, queries) * score_scale,
            mixed_sum("wbhqk,wbqhd->wbkhd", near_probs, grad_attended),
        ],
        axis=4,
    )
    global_back = jnp.concatenate(
        [
            mixed_sum("wbhqk,wbqhd->wkhd", global_split, queries) * score_scale,
            mixed_sum("wbhqk,wbqhd->wkhd", global_probs, grad_attended),
        ],
        axis=3,
    )
    far_back = jnp.concatenate(
        [
            mixed_sum("wbhqrk,wbqhd->wbhrkd", far_split, queries) * score_scale,
            mixed_sum("wbhqrk,wbqhd->wbhrkd", far_probs, grad_attended),
        ],
        axis=5,
    )
    full_grad_probs = mixed_sum("wqhd,wkhd->whqk", rows_grad, value_part)
    partial_dot = jnp.sum(full_probs * full_grad_probs, axis=3, keepdims=True)
    row_dot = lax.psum(partial_dot, SEQ)
    full_grad_scores = (full_probs * (full_grad_probs - row_dot)).astype(jnp.bfloat16)
    query_part = mixed_sum("whqk,wkhd->wqhd", full_grad_scores, key_part) * score_scale
    full_key_grad = mixed_sum("whqk,wqhd->wkhd", full_grad_scores, global_queries) * score_scale
    full_value_grad = mixed_sum("whqk,wqhd->wkhd", full_probs.astype(jnp.bfloat16), rows_grad)
    grad_paired, query_total = return_blocks(
        near_back, global_back, far_back, query_part, sender, picker, owned_hot
    )
    grad_query = grad_query + exact_two(
        "wgb,wgqhd->wbqhd", owned_hot, query_total.reshape(windows, -1, BLOCK, head_count, head_dim)
    )
    grad_paired = grad_paired + jnp.concatenate([full_key_grad, full_value_grad], axis=3)
    return (grad_query, grad_paired)


def layer_backward(stored, grad_output, weights, tables):
    row_weights, down_weights, vector_weights = weights
    sender, picker, owned_hot, key_mask, full_mask = tables
    (
        hidden,
        normed,
        queries,
        sliding,
        global_kv,
        distant,
        probabilities,
        mixed_low,
        middle,
        normed_two,
        up_value,
        active,
        key_part,
        value_part,
        global_queries,
        full_probs,
    ) = stored
    model_width = row_weights.shape[0]
    windows, tokens, _ = hidden.shape
    blocks_dev = tokens // BLOCK
    head_dim = model_width // HEADS
    (
        gain_one,
        shift_one,
        bias_query,
        bias_value,
        bias_out,
        gain_two,
        shift_two,
        bias_down,
        bias_up,
    ) = split_vectors(vector_weights, model_width)
    grad_ffn = grad_output.astype(jnp.bfloat16)
    grad_bias_down = jnp.sum(grad_ffn.astype(jnp.float32), axis=(0, 1))
    grad_down = mixed_sum("wtf,wtd->fd", active, grad_ffn)
    grad_active = mixed_sum("wtd,fd->wtf", grad_ffn, down_weights)
    gelu_pull = jax.vjp(partial(jax.nn.gelu, approximate=False), up_value)[1]
    grad_up = gelu_pull(grad_active)[0].astype(jnp.bfloat16)
    grad_bias_up = jnp.sum(grad_up.astype(jnp.float32), axis=(0, 1))
    grad_in = mixed_sum("wtd,wtf->df", normed_two, grad_up)
    grad_normed_two = mixed_sum("wtf,df->wtd", grad_up, row_weights[:, 4 * model_width :])
    norm_pull_two = jax.vjp(norm_rows, middle, gain_two, shift_two)[1]
    grad_middle_norm, grad_gain_two, grad_shift_two = norm_pull_two(grad_normed_two)
    grad_middle = grad_output + grad_middle_norm
    grad_branch = grad_middle.astype(jnp.bfloat16)
    grad_bias_out = jnp.sum(grad_branch.astype(jnp.float32), axis=(0, 1))
    grad_out_weight = mixed_sum("wtd,wte->de", mixed_low, grad_branch)
    grad_attended = mixed_sum(
        "wte,de->wtd", grad_branch, row_weights[:, 3 * model_width : 4 * model_width]
    ).astype(jnp.bfloat16)
    grad_attended = grad_attended.reshape(windows, blocks_dev, BLOCK, HEADS, head_dim)
    grad_query, grad_paired = attention_back(
        grad_attended,
        queries,
        sliding,
        global_kv,
        distant,
        probabilities,
        key_part,
        value_part,
        global_queries,
        full_probs,
        sender,
        picker,
        owned_hot,
    )
    grad_projected = jnp.concatenate(
        [
            grad_query.reshape(windows, tokens, model_width),
            grad_paired[..., :head_dim].reshape(windows, tokens, model_width),
            grad_paired[..., head_dim:].reshape(windows, tokens, model_width),
        ],
        axis=2,
    ).astype(jnp.bfloat16)
    summed = jnp.sum(grad_projected.astype(jnp.float32), axis=(0, 1))
    grad_bias_query = summed[:model_width]
    grad_bias_value = summed[2 * model_width :]
    grad_projection = mixed_sum("wtd,wte->de", normed, grad_projected)
    grad_normed = mixed_sum("wte,de->wtd", grad_projected, row_weights[:, : 3 * model_width])
    norm_pull_one = jax.vjp(norm_rows, hidden, gain_one, shift_one)[1]
    grad_hidden_norm, grad_gain_one, grad_shift_one = norm_pull_one(grad_normed)
    grad_hidden = grad_middle + grad_hidden_norm
    grad_rows = jnp.concatenate([grad_projection, grad_out_weight, grad_in], axis=1)
    grad_vectors = jnp.concatenate(
        [
            grad_gain_one,
            grad_shift_one,
            grad_bias_query,
            grad_bias_value,
            grad_bias_out,
            grad_gain_two,
            grad_shift_two,
            grad_bias_down,
            grad_bias_up,
        ]
    )
    return (grad_hidden, (grad_rows, grad_down, grad_vectors))


def adam_update(master, first_old, second_old, gradient, step_rate, decay_rate):
    first_new = 0.5 * first_old + 0.5 * gradient
    second_new = 0.5 * second_old + 0.5 * gradient * gradient
    first_hat = first_new / (1.0 - 0.5**STEP)
    second_hat = second_new / (1.0 - 0.5**STEP)
    master_new = master - step_rate * (
        first_hat / (jnp.sqrt(second_hat) + 1e-08) + decay_rate * master
    )
    return (master_new, first_new, second_new)


def general_shards(
    block_input,
    cotangent,
    random_ids,
    segment_ids,
    global_ids,
    w_rows,
    w_rows_first,
    w_rows_second,
    w_down,
    w_down_first,
    w_down_second,
    vectors,
    vectors_first,
    vectors_second,
):
    section_index = lax.axis_index(SECTION)
    seq_place = lax.axis_index(SEQ)
    groups = lax.axis_size(SEQ)
    row_weights, down_weights, vector_low = (
        lax.all_gather(w_rows[0].astype(jnp.bfloat16), (DP, SEQ), axis=1, tiled=True),
        lax.all_gather(w_down[0].astype(jnp.bfloat16), (DP, SEQ), axis=0, tiled=True),
        lax.all_gather(vectors[0].astype(jnp.bfloat16), (DP, SEQ), axis=0, tiled=True),
    )
    weights = (row_weights, down_weights, vector_low.astype(jnp.float32))
    micro_count, windows, tokens, model_width = block_input.shape
    received = jnp.zeros((windows, tokens, model_width), jnp.bfloat16)
    results = jnp.zeros(block_input.shape, jnp.float32)
    full_totals = (
        jnp.zeros(row_weights.shape, jnp.float32),
        jnp.zeros(down_weights.shape, jnp.float32),
        jnp.zeros(vector_low.shape, jnp.float32),
    )

    def tick(tick_index, carry):
        received, results, full_totals = carry
        forward_mb = jnp.clip(tick_index - section_index, 0, micro_count - 1)
        behind_raw = tick_index - 2 + section_index
        behind = jnp.clip(behind_raw, 0, micro_count - 1)
        live_mask = ((behind_raw >= 0) & (behind_raw < micro_count)).astype(jnp.float32)
        tables_forward = route_tables(
            lax.dynamic_index_in_dim(random_ids, forward_mb, 0, keepdims=False),
            lax.dynamic_index_in_dim(segment_ids, forward_mb, 0, keepdims=False),
            lax.dynamic_index_in_dim(global_ids, forward_mb, 0, keepdims=False),
            seq_place,
            groups,
        )
        tables_behind = route_tables(
            lax.dynamic_index_in_dim(random_ids, behind, 0, keepdims=False),
            lax.dynamic_index_in_dim(segment_ids, behind, 0, keepdims=False),
            lax.dynamic_index_in_dim(global_ids, behind, 0, keepdims=False),
            seq_place,
            groups,
        )
        incoming_values = received.astype(jnp.float32)
        first_input = lax.dynamic_index_in_dim(block_input, forward_mb, 0, keepdims=False).astype(
            jnp.float32
        )
        forward_input = jnp.where(section_index == 0, first_input, incoming_values)
        forward_output = layer_forward(forward_input, weights, tables_forward)[0]
        back_source = lax.dynamic_index_in_dim(block_input, behind, 0, keepdims=False).astype(
            jnp.float32
        )
        back_input = jnp.where(section_index == 0, back_source, incoming_values)
        given_grad = lax.dynamic_index_in_dim(cotangent, behind, 0, keepdims=False).astype(
            jnp.float32
        )
        back_grad = jnp.where(section_index == 0, incoming_values, given_grad) * live_mask
        stored = layer_forward(back_input, weights, tables_behind)[1]
        grad_input, gradients = layer_backward(stored, back_grad, weights, tables_behind)
        outgoing = jnp.where(section_index == 0, forward_output, grad_input).astype(jnp.bfloat16)
        finished = jnp.where(section_index == 0, grad_input, forward_output)
        updated = lax.dynamic_update_index_in_dim(results, finished, behind, 0)
        results = jnp.where(live_mask > 0, updated, results)
        full_totals = tuple(
            (total_part + grad_part for total_part, grad_part in zip(full_totals, gradients))
        )
        return (partner(outgoing, SECTION, 0), results, full_totals)

    received, results, full_totals = lax.fori_loop(
        0, micro_count + 2, tick, (received, results, full_totals)
    )
    shard_totals = (
        lax.psum_scatter(full_totals[0], (DP, SEQ), scatter_dimension=1, tiled=True),
        lax.psum_scatter(full_totals[1], (DP, SEQ), scatter_dimension=0, tiled=True),
        lax.psum_scatter(full_totals[2], (DP, SEQ), scatter_dimension=0, tiled=True),
    )
    new_rows, new_rows_first, new_rows_second = adam_update(
        w_rows[0], w_rows_first[0], w_rows_second[0], shard_totals[0], rate_matrix, decay_matrix
    )
    new_down, new_down_first, new_down_second = adam_update(
        w_down[0], w_down_first[0], w_down_second[0], shard_totals[1], rate_matrix, decay_matrix
    )
    new_vectors, new_vectors_first, new_vectors_second = adam_update(
        vectors[0], vectors_first[0], vectors_second[0], shard_totals[2], rate_vector, 0.0
    )
    return (
        results[None],
        new_rows[None],
        new_rows_first[None],
        new_rows_second[None],
        new_down[None],
        new_down_first[None],
        new_down_second[None],
        new_vectors[None],
        new_vectors_first[None],
        new_vectors_second[None],
    )


LOW = jnp.bfloat16
LOG_HIGH = [float(np.log(c).astype(ml_dtypes.bfloat16)) for c in (1.0, 2.0, 3.0)]
LOG_LOW = [float(np.log(c)) - high for c, high in zip((1.0, 2.0, 3.0), LOG_HIGH)]
CHUNK = 256
VMEM_BYTES = 60 * 1024 * 1024


def dot_rows(left, right):
    return lax.dot_general(left, right, (((1,), (1,)), ((), ())), preferred_element_type=jnp.float32)


def dot_plain(left, right):
    return lax.dot_general(left, right, (((1,), (0,)), ((), ())), preferred_element_type=jnp.float32)


def dot_tokens(left, right):
    return lax.dot_general(left, right, (((0,), (0,)), ((), ())), preferred_element_type=jnp.float32)


def swap(value):
    return lax.ppermute(value, SECTION, [(0, 1), (1, 0)])


def normalized(values_in):
    row_mean = jnp.mean(values_in, axis=-1, keepdims=True)
    centred = values_in - row_mean
    spread = jnp.mean(centred * centred, axis=-1, keepdims=True)
    scale = lax.rsqrt(spread + epsilon)
    return centred * scale, scale


class Shares:
    def __init__(self, width, columns, depth, vector_len):
        self.width = width
        self.columns = columns
        self.depth = depth
        self.vector_len = vector_len
        self.half = columns // 2
        self.per = width // columns
        self.groups = columns // depth

    def unpack(self, gathered, core):
        rows, down, vec = gathered
        vec = vec.reshape(-1, TAIL, self.width)[:, 0, : self.vector_len].reshape(-1)
        pieces = split_vectors(vec.astype(jnp.float32), self.width)
        for index in (2, 3):
            pieces[index] = lax.dynamic_index_in_dim(
                pieces[index].reshape(self.per, 2, self.half), core, 1, keepdims=False
            ).reshape(-1)
        pieces[8] = lax.dynamic_index_in_dim(
            pieces[8].reshape(-1, 2, self.depth // 2), core, 1, keepdims=False
        ).reshape(-1)
        nothing = jnp.zeros_like(pieces[2])
        proj = [pieces[2], nothing, pieces[3], nothing]
        order = [pieces[index] for index in (0, 1, 4, 5, 6, 7)] + proj + [pieces[8]]
        return (
            (rows.reshape(-1, self.width), down.reshape(-1, self.width)),
            jnp.concatenate(order).reshape(-1, self.width),
        )

    def by_shard(self, grads, vector_grads, core):
        proj, out, up, down = grads
        half, per, width = self.half, self.per, self.width
        hot = (jnp.arange(2) == core).astype(jnp.float32)
        spread = list(vector_grads)
        for index in (2, 3):
            spread[index] = (
                spread[index].reshape(per, 1, half) * hot[None, :, None]
            ).reshape(-1)
        spread[8] = (spread[8].reshape(-1, 1, self.depth // 2) * hot[None, :, None]).reshape(-1)
        for index in (0, 1, 4, 5, 6, 7):
            spread[index] = spread[index] * hot[0]
        vec = jnp.concatenate(spread).reshape(-1, 1, self.vector_len)
        vec = jnp.pad(vec, ((0, 0), (0, TAIL - 1), (0, width - self.vector_len))).astype(LOW)
        return (
            proj.reshape(-1, half, width),
            out.reshape(-1, half, width),
            up.reshape(2, 4, half, width),
            down.reshape(2, 2, 4, self.depth // 2, width),
            vec.reshape(2, 2, 4, TAIL, width),
        )


MESH = pl.DeviceIdType.MESH
PIECE = 48
TAIL = 16


def prepare_kernel(shares, rows_ref, down_ref, vector_ref, rows_out, down_out, vector_out):
    core = lax.axis_index(SECTION)
    offset = lax.axis_index((DP, SEQ)) * shares.columns
    half, per, width, depth = shares.half, shares.per, shares.width, shares.depth // 2
    is_inner = (offset >= 3 * width) & (offset < 4 * width)
    is_hidden = offset >= 4 * width

    @pl.when(is_inner)
    def _():
        for which in range(2):
            side = core if which == 0 else 1 - core
            held = [rows_ref[pl.ds((2 * j + side) * half, half), :] for j in range(per)]
            turned = jnp.transpose(jnp.concatenate(held, axis=0))
            rows_out[which] = jnp.concatenate([turned[:half], turned[half:]], axis=1).astype(LOW)

    @pl.when(jnp.logical_not(is_inner))
    def _():
        turned = jnp.transpose(rows_ref[...]).astype(LOW)
        plain = [turned[:half], turned[half:]]
        hidden = [
            jnp.concatenate(
                [turned[(2 * j + side) * depth :][:depth] for j in range(shares.groups)], axis=0
            )
            for side in range(2)
        ]
        halves = [jnp.where(is_hidden, b, a) for a, b in zip(plain, hidden)]
        rows_out[0] = jnp.where(core == 0, halves[0], halves[1])
        rows_out[1] = jnp.where(core == 0, halves[1], halves[0])

    down = down_ref[...].astype(LOW)
    down_out[0] = jnp.where(core == 0, down[:depth], down[depth:])
    down_out[1] = jnp.where(core == 0, down[depth:], down[:depth])
    vector_out[...] = jnp.zeros_like(vector_out)
    vector_out[0:1, : shares.vector_len] = vector_ref[...].astype(LOW)


def prepare(shares, rows, down, vector):
    return pl.pallas_call(
        partial(prepare_kernel, shares),
        out_shape=[
            jax.ShapeDtypeStruct((2, shares.half, shares.width), LOW),
            jax.ShapeDtypeStruct((2, shares.depth // 2, shares.width), LOW),
            jax.ShapeDtypeStruct((TAIL, shares.width), LOW),
        ],
        compiler_params=pltpu.CompilerParams(vmem_limit_bytes=VMEM_BYTES),
    )(rows, down, vector)


class Place:
    def __init__(self):
        self.core = lax.axis_index(SECTION)
        self.dp = lax.axis_index(DP)
        self.z = lax.axis_index(SEQ)
        self.y, self.x = self.dp // 2, self.dp % 2
        self.high, self.low = self.z // 2, self.z % 2
        self.inner = self.high + self.low == 1
        self.outer = self.high + self.low != 1
        self.partner = {SECTION: 1 - self.core}
        self.along_x = {DP: 2 * self.y + 1 - self.x}
        self.along_y = {DP: 2 * (1 - self.y) + self.x}
        self.across = {SEQ: 3 - self.z}
        self.beside = {SEQ: 2 * self.high + 1 - self.low}
        self.others = [{SEQ: (self.z + by) % 4} for by in (1, 2, 3)]
        self.own = pl.ds(self.z, 1)
        self.next = pl.ds(2 * self.high + 1 - self.low, 1)
        self.near = pl.ds(2 * self.high, 2)
        self.far = pl.ds(2 * (1 - self.high), 2)

    def greet(self):
        barrier = pltpu.get_barrier_semaphore()
        everyone = [self.partner, self.along_x, self.along_y] + self.others
        for device in everyone:
            pl.semaphore_signal(barrier, inc=1, device_id=device, device_id_type=MESH)
        pl.semaphore_wait(barrier, len(everyone))


def remote(src, dst, sems, spots, device):
    return pltpu.make_async_remote_copy(
        src_ref=src,
        dst_ref=dst,
        send_sem=sems[0].at[spots[0]],
        recv_sem=sems[1].at[spots[1]],
        device_id=device,
        device_id_type=MESH,
    )


def chunk_pairs(shares):
    pairs = []
    for array, length in ((0, shares.half), (1, shares.depth // 2)):
        for start in range(0, length, 2 * PIECE):
            pairs.append([(array, start, PIECE, 0), (array, start + PIECE, PIECE, 1)])
    pairs[0].append((2, 0, TAIL, 0))
    return pairs


def quad_pairs(shares):
    length = (shares.half + shares.depth // 2) // 2
    pairs = [
        [(0, start, PIECE, None), (1, start, PIECE, None)] for start in range(0, length, PIECE)
    ]
    pairs[0].append((2, 0, TAIL, 0))
    return pairs


def gather_kernel(shares, *refs):
    (rows_in, down_in, vector_in, x_in, cot_in), refs = refs[:5], refs[5:]
    outs, refs = [refs[0:3], refs[3:6]], refs[6:]
    (x_out, cot_out), refs = refs[:2], refs[2:]
    local, swap_send, swap_recv, z_send, z_recv, send, recv = refs
    here = Place()
    core, y, x, z = here.core, here.y, here.x, here.z
    half = x_in.shape[2] // 2
    rows_half, down_half = shares.half // 2, shares.depth // 4
    here.greet()

    def slices(source, target, base):
        mine = pl.ds(pl.multiple_of(core * half, half), half)
        sems = (z_send, z_recv)
        own = pltpu.make_async_copy(
            source.at[z, 0, mine], target.at[z, core], local.at[8 + base // 4]
        )
        sends, arrivals = [], []
        for by in (1, 2, 3):
            spots = (base + by - 1, base + by - 1)
            device = here.others[by - 1]
            sends.append(
                remote(source.at[(z + by) % 4, 0, mine], target.at[z, core], sems, spots, device)
            )
            arrivals.append(
                remote(
                    source.at[z, 0, mine], target.at[(z + 4 - by) % 4, core], sems, spots, device
                )
            )
        spots = (base + 3, base + 3)
        forward = remote(target.at[:, core], target.at[:, core], sems, spots, here.partner)
        arrived = remote(target.at[:, 1 - core], target.at[:, 1 - core], sems, spots, here.partner)
        return own, sends, arrivals, forward, arrived

    x_moves = slices(x_in, x_out, 0)
    cot_moves = slices(cot_in, cot_out, 4)

    def open_slices(moves):
        moves[0].start()
        for copy in moves[1]:
            copy.start()

    def pass_slices(moves):
        moves[0].wait()
        for copy in moves[2]:
            copy.wait_recv()
        moves[3].start()

    def close_slices(moves):
        for copy in moves[1]:
            copy.wait_send()
        moves[3].wait_send()
        moves[4].wait_recv()

    def first_moves(layer, which):
        down = down_in.at[which]
        rows = rows_in.at[which]
        if layer == 0:
            return [
                (0, rows, outs[0][0].at[y, x, z]),
                (1, down, outs[0][1].at[y, x, z]),
                (2, vector_in, outs[0][2].at[y, x, z]),
            ]
        moves = [(7, vector_in, outs[1][2].at[y, x, z])]
        for part in range(2):
            target = outs[1][part]
            moves.append(
                (
                    3 + 2 * part,
                    rows.at[pl.ds(part * rows_half, rows_half)],
                    target.at[z, pl.ds(0, rows_half)],
                )
            )
            moves.append(
                (
                    4 + 2 * part,
                    down.at[pl.ds(part * down_half, down_half)],
                    target.at[z, pl.ds(rows_half, down_half)],
                )
            )
        return moves

    swaps = (swap_send, swap_recv)
    for layer in range(2):

        @pl.when(core == layer)
        def _():
            across = [
                remote(src, dst, swaps, (spot, spot), here.partner)
                for spot, src, dst in first_moves(layer, 1)
            ]
            own = [
                pltpu.make_async_copy(src, dst, local.at[spot])
                for spot, src, dst in first_moves(layer, 0)
            ]
            for copy in across + own:
                copy.start()
            for copy in own:
                copy.wait()
            for copy in across:
                copy.wait_send()
            for spot, src, dst in first_moves(1 - layer, 0):
                remote(src, dst, swaps, (spot, spot), here.partner).wait_recv()

    numbers, pairs = {}, []
    for layer in range(2):
        for pair in chunk_pairs(shares) if layer == 0 else quad_pairs(shares):
            entry = []
            for array, start, length, order in pair:
                ref = outs[layer][array]
                rows = pl.ds(start, length)
                flat = order is None
                number = len(numbers)
                sems = (send, recv)

                def part(which):
                    return ref.at[which, rows] if flat else ref.at[y, x, which, rows]

                def copy(piece, spots, device):
                    return remote(piece, piece, sems, ((number, spots[0]), (number, spots[1])), device)

                steps = {
                    "z": copy(part(here.own), (0, 0), here.beside),
                    "across": copy(part(here.near), (1, 1), here.across),
                    "on": copy(part(here.far), (4, 1), here.beside),
                }
                arrive = [
                    copy(part(here.next), (0, 0), here.beside),
                    copy(part(here.far), (1, 1), here.across),
                ]
                if order == 0:
                    steps["one"] = copy(ref.at[y, x, :, rows], (2, 2), here.along_y)
                    steps["two"] = copy(ref.at[:, x, :, rows], (3, 3), here.along_x)
                    arrive.append(copy(ref.at[1 - y, x, :, rows], (2, 2), here.along_y))
                    arrive.append(copy(ref.at[:, 1 - x, :, rows], (3, 3), here.along_x))
                elif order == 1:
                    steps["one"] = copy(ref.at[y, x, :, rows], (2, 2), here.along_x)
                    steps["two"] = copy(ref.at[y, :, :, rows], (3, 3), here.along_y)
                    arrive.append(copy(ref.at[y, 1 - x, :, rows], (2, 2), here.along_x))
                    arrive.append(copy(ref.at[1 - y, :, :, rows], (3, 3), here.along_y))
                numbers[number] = (steps, arrive)
                entry.append(number)
            pairs.append(entry)

    def issue(name, entry):
        after = {"z": None, "across": 0, "on": 1, "one": 1, "two": 2}[name]

        def start():
            for number in entry:
                steps, arrive = numbers[number]
                if name in steps:
                    if after is not None and not (name == "one"):
                        arrive[after].wait_recv()
                    steps[name].start()

        if name in ("across", "on"):
            pl.when(here.inner)(start)
        else:
            start()

    def arrived(entry, index, where):
        def wait():
            for number in entry:
                numbers[number][1][index].wait_recv()

        pl.when(where)(wait)

    first, second = pairs[: len(chunk_pairs(shares))], pairs[len(chunk_pairs(shares)) :]
    for entry in first:
        issue("z", entry)
    for entry in first:
        issue("across", entry)
        arrived(entry, 0, here.outer)
    for entry in first[:-1]:
        issue("on", entry)
        arrived(entry, 1, here.outer)
        issue("one", entry)
    issue("on", first[-1])
    for entry in second:
        issue("z", entry)
    open_slices(x_moves)
    arrived(first[-1], 1, here.outer)
    issue("one", first[-1])
    issue("two", first[0])
    for entry in second:
        issue("across", entry)
        arrived(entry, 0, here.outer)
    issue("two", first[1])
    open_slices(cot_moves)
    for entry in second:
        issue("on", entry)
    issue("two", first[2])
    pass_slices(x_moves)
    for entry in second:
        arrived(entry, 1, here.outer)
        for number in entry:
            steps, arrive = numbers[number]
            if "one" in steps:
                steps["one"].start()
                arrive[2].wait_recv()
                steps["two"].start()
    pass_slices(cot_moves)
    for steps, arrive in numbers.values():
        if len(arrive) == 4:
            arrive[3].wait_recv()
        for name in steps:
            if name not in ("across", "on"):
                steps[name].wait_send()

    @pl.when(here.inner)
    def _():
        for steps, _ in numbers.values():
            steps["across"].wait_send()
            steps["on"].wait_send()

    close_slices(x_moves)
    close_slices(cot_moves)


def gather(shares, prepared, block_input, cotangent):
    micro, _, tokens, width = block_input.shape
    chunks = sum(len(pair) for pair in chunk_pairs(shares) + quad_pairs(shares))
    lengths = (shares.half, shares.depth // 2, TAIL)
    layer = [jax.ShapeDtypeStruct((2, 2, 4, rows, width), LOW) for rows in lengths]
    quad = jax.ShapeDtypeStruct((4, (lengths[0] + lengths[1]) // 2, width), LOW)
    window = jax.ShapeDtypeStruct((micro, 2, tokens // 2, width), LOW)
    anywhere = pl.BlockSpec(memory_space=pl.ANY)
    results = pl.pallas_call(
        partial(gather_kernel, shares),
        in_specs=[pl.BlockSpec(memory_space=pltpu.VMEM)] * 3 + [anywhere] * 2,
        out_specs=[anywhere] * 8,
        out_shape=layer + [quad, quad, layer[2]] + [window, window],
        scratch_shapes=[
            pltpu.SemaphoreType.DMA((10,)),
            pltpu.SemaphoreType.DMA((8,)),
            pltpu.SemaphoreType.DMA((8,)),
            pltpu.SemaphoreType.DMA((8,)),
            pltpu.SemaphoreType.DMA((8,)),
            pltpu.SemaphoreType.DMA((chunks, 5)),
            pltpu.SemaphoreType.DMA((chunks, 4)),
        ],
        compiler_params=pltpu.CompilerParams(
            collective_id=0, has_side_effects=True, vmem_limit_bytes=VMEM_BYTES
        ),
    )(*prepared, block_input, cotangent)
    return results[0:3], results[3:6], results[6], results[7]


def over(value, bit):
    return lax.ppermute(value, DP, [(i, i ^ bit) for i in range(4)])


def layout_moves(shares, y, x, pieces, arrays):
    rows_half, down_half = shares.half // 2, shares.depth // 4
    down = arrays[-1]
    moves = []
    for part in range(2):
        rows = pl.ds(part * rows_half, rows_half)
        for index, (by_y, by_x) in enumerate(((0, 0), (1, 0), (0, 1), (1, 1))):
            piece = pieces[part][index]
            at_y, at_x = y ^ by_y, x ^ by_x
            top = pl.ds(0, rows_half)
            if len(arrays) == 2:
                moves.append((piece.at[:, top], arrays[0].at[at_y, at_x, :, rows]))
            else:
                proj, out, up, _ = arrays
                if at_y == 1:
                    moves.append((piece.at[:, top], up.at[at_x, :, rows]))
                elif at_x == 0:
                    moves.append((piece.at[:, top], proj.at[pl.ds(0, 4), rows]))
                else:
                    moves.append((piece.at[pl.ds(0, 2), top], proj.at[pl.ds(4, 2), rows]))
                    moves.append((piece.at[pl.ds(2, 2), top], out.at[:, rows]))
            moves.append(
                (
                    piece.at[:, pl.ds(rows_half, down_half)],
                    down.at[at_y, at_x, :, pl.ds(part * down_half, down_half)],
                )
            )
    return moves


def layout_kernel(shares, joins, *refs):
    dp = lax.axis_index(DP)
    if joins:
        pieces, arrays = [refs[0:4], refs[4:8]], refs[8:10]
    else:
        arrays, pieces = refs[0:4], [refs[4:8], refs[8:12]]
    for spot in range(4):

        @pl.when(dp == spot)
        def _():
            for piece, place in layout_moves(shares, spot // 2, spot % 2, pieces, arrays):
                src, dst = (piece, place) if joins else (place, piece)
                dst[...] = src[...]


def layout(shares, joins, *arrays):
    half, depth, width = shares.half, shares.depth // 2, shares.width
    if joins:
        shapes = [(2, 2, 4, half, width), (2, 2, 4, depth, width)]
    else:
        shapes = [(4, (half + depth) // 2, width)] * 8
    return pl.pallas_call(
        partial(layout_kernel, shares, joins),
        out_shape=[jax.ShapeDtypeStruct(shape, LOW) for shape in shapes],
        compiler_params=pltpu.CompilerParams(vmem_limit_bytes=VMEM_BYTES),
        cost_estimate=pl.CostEstimate(
            flops=0, bytes_accessed=64 * (half + depth) * width, transcendentals=0
        ),
    )(*arrays)


def tied(value, flying):
    return lax.optimization_barrier((value, flying))


def spread_quads(shares, quads):
    low, high = quads
    flying = (low, high, over(low, 2), over(high, 1))
    low, high, low_y, high_x = yield flying
    flying = (low_y, high_x, over(low, 1), over(high, 2))
    low_y, high_x, low_x, high_y = yield flying
    flying = (over(low_y, 1), over(high_x, 2))
    low_both, high_both = yield flying
    yield layout(shares, True, low, low_y, low_x, low_both, high, high_y, high_x, high_both)


def sum_quads(shares, arrays):
    pieces = layout(shares, False, *arrays)

    def total(*terms):
        return sum(term.astype(jnp.float32) for term in terms).astype(LOW)

    low, low_y, low_x, low_both = pieces[:4]
    high, high_y, high_x, high_both = pieces[4:]
    flying = (low_x, high_y, over(low_both, 1), over(high_both, 2))
    low_x, high_y, low_hop, high_hop = yield flying
    low_y, high_x = total(low_y, low_hop), total(high_x, high_hop)
    flying = (low_y, high_x, over(low_x, 1), over(high_y, 2))
    low_y, high_x, low_x, high_y = yield flying
    flying = (over(low_y, 2), over(high_x, 1))
    low_y, high_x = yield flying
    yield (total(low, low_x, low_y), total(high, high_x, high_y))


class Beside:
    def __init__(self, hops=None):
        self.hops = hops
        self.flying = None if hops is None else next(hops)

    def tie(self, value):
        if self.hops is None:
            return value
        value, arrived = tied(value, self.flying)
        self.flying = self.hops.send(arrived)
        return value


def scatter_kernel(shares, *refs):
    (proj, out, up, down, vec_zero, low, high, vec_one), refs = refs[:8], refs[8:]
    (dx_ref, final_ref, halves, slices), refs = refs[:4], refs[4:]
    work, refs = [refs[0:3], refs[3:6]], refs[6:]
    (got_one, got_two, got_far, got_across, got_near, total), refs = refs[:6], refs[6:]
    load, local, swap_send, swap_recv, z_send, z_recv, send, recv = refs
    here = Place()
    core, y, x, z = here.core, here.y, here.x, here.z
    rows_half, down_half = shares.half // 2, shares.depth // 4
    down_base = shares.half
    tail_base = shares.half + shares.depth // 2

    rows = work[0][0]
    moves = [
        [
            (proj.at[pl.ds(0, 4)], rows.at[0, 0]),
            (proj.at[pl.ds(4, 2)], rows.at[0, 1, pl.ds(0, 2)]),
            (out, rows.at[0, 1, pl.ds(2, 2)]),
            (up, rows.at[1]),
            (down, work[0][1]),
            (vec_zero, work[0][2]),
        ],
        [(low, work[1][0]), (high, work[1][1]), (vec_one, work[1][2])],
    ]
    loads = [
        [
            pltpu.make_async_copy(src, dst, load.at[layer, index])
            for index, (src, dst) in enumerate(moves[layer])
        ]
        for layer in range(2)
    ]
    for layer in (1, 0):
        for copy in loads[layer]:
            copy.start()
    here.greet()

    def place_of(layer, array, start):
        if array == 2:
            return tail_base
        if layer == 0:
            return (0, down_base)[array] + start
        if start < rows_half:
            return array * rows_half + start
        return down_base + array * down_half + start - rows_half

    pairs, chunks = [], []
    for layer in (1, 0):
        for index, pair in enumerate(quad_pairs(shares) if layer else chunk_pairs(shares)):
            entry = []
            for array, start, length, order in pair:
                entry.append((len(chunks), layer, array, start, length, order))
                chunks.append(entry[-1])
            pairs.append((index, entry))

    def pieces(chunk):
        number, layer, array, start, length, order = chunk
        ref = work[layer][array]
        rows = pl.ds(start, length)
        sems = (send, recv)
        keeps, slots, copies = [], [], []

        def part(which):
            return ref.at[which, rows] if order is None else ref.at[y, x, which, rows]

        def add(src, slot, device, keep):
            spots = (number, len(copies))
            copies.append(remote(src, slot, sems, (spots, spots), device))
            slots.append(slot)
            keeps.append(keep)

        room = pl.ds(0, length)
        if order == 0:
            add(ref.at[:, 1 - x, :, rows], got_one.at[number, :, :, room], here.along_x, ref.at[:, x, :, rows])
            add(ref.at[1 - y, x, :, rows], got_two.at[number, :, room], here.along_y, ref.at[y, x, :, rows])
        elif order == 1:
            add(ref.at[1 - y, :, :, rows], got_one.at[number, :, :, room], here.along_y, ref.at[y, :, :, rows])
            add(ref.at[y, 1 - x, :, rows], got_two.at[number, :, room], here.along_x, ref.at[y, x, :, rows])
        else:
            copies, slots, keeps = [None] * 2, [None] * 2, [None] * 2
        add(part(here.far), got_far.at[number, :, room], here.beside, part(here.far))
        add(part(here.far), got_across.at[number, :, room], here.across, part(here.near))
        add(part(here.next), got_near.at[number, :, room], here.beside, part(here.own))
        return copies, keeps, slots

    built = [pieces(chunk) for chunk in chunks]
    loaded = set()

    def land(number, phase):
        copies, keeps, slots = built[number]
        copies[phase].wait_recv()
        keep, slot = keeps[phase], slots[phase]
        keep[...] = keep[...] + slot[...]

    def run(chunk, phase):
        number, layer, array, start, length, order = chunk
        copies, keeps, slots = built[number]
        if (layer, array) not in loaded:
            loaded.add((layer, array))
            spots = ((0, 1, 2, 3), (4,), (5,))[array] if layer == 0 else (array,)
            for spot in spots:
                loads[layer][spot].wait()
        if phase < 2:
            if order is not None:
                if phase:
                    land(number, 0)
                copies[phase].start()
        elif phase == 2:
            if order is not None:
                land(number, 1)

            @pl.when(here.outer)
            def _():
                copies[2].start()
                copies[4].start()

        elif phase == 3:

            @pl.when(here.inner)
            def _():
                land(number, 2)
                copies[3].start()

        elif phase == 4:

            @pl.when(here.inner)
            def _():
                land(number, 3)
                copies[4].start()

        else:
            copies[4].wait_recv()
            spot = pl.ds(place_of(layer, array, start), length)
            total[layer, spot, :] = (keeps[4][...] + slots[4][...])[0]

    def step(entry, phase):
        for chunk in entry:
            run(chunk, phase)

    second = [entry for _, entry in pairs[: len(quad_pairs(shares))]]
    first = [entry for _, entry in pairs[len(quad_pairs(shares)) :]]
    tails = [chunk for entry in second for chunk in entry if chunk[5] is not None]
    second = [[chunk for chunk in entry if chunk[5] is None] for entry in second]
    first[0] = first[0] + tails
    step(first[0], 0)
    step(first[1], 0)
    for entry in second:
        step(entry, 2)
    step(first[0], 1)
    for section, source in ((0, dx_ref), (1, final_ref)):

        @pl.when(core == section)
        def _():
            pltpu.make_async_copy(source.at[z], slices.at[z], local.at[0]).start()
            for by in (1, 2, 3):
                remote(
                    source.at[(z + by) % 4],
                    slices.at[z],
                    (z_send, z_recv),
                    (by - 1, by - 1),
                    here.others[by - 1],
                ).start()

    for entry in second:
        step(entry, 3)
    step(first[2], 0)
    step(first[1], 1)
    for entry in second:
        step(entry, 4)
    step(first[0], 2)
    step(first[2], 1)
    for entry in second:
        step(entry, 5)
    step(first[0], 3)
    step(first[1], 2)
    step(first[0], 4)
    step(first[1], 3)
    step(first[2], 2)
    step(first[1], 4)
    step(first[2], 3)
    step(first[2], 4)
    for entry in first:
        step(entry, 5)

    for copies, _, _ in built:
        for index in (0, 1, 4):
            if copies[index] is not None:
                copies[index].wait_send()
    for section, index in ((here.outer, 2), (here.inner, 3)):

        @pl.when(section)
        def _():
            for copies, _, _ in built:
                copies[index].wait_send()

    swaps = (swap_send, swap_recv)
    across = remote(total.at[1 - core], halves.at[core], swaps, (0, 0), here.partner)
    across.start()
    own = pltpu.make_async_copy(total.at[core], halves.at[core], local.at[1])
    own.start()
    own.wait()
    across.wait_send()
    remote(total.at[1 - core], halves.at[1 - core], swaps, (0, 0), here.partner).wait_recv()
    pltpu.make_async_copy(dx_ref.at[z], slices.at[z], local.at[0]).wait()
    for by in (1, 2, 3):
        copy = remote(
            dx_ref.at[z],
            slices.at[(z + 4 - by) % 4],
            (z_send, z_recv),
            (by - 1, by - 1),
            here.others[by - 1],
        )
        copy.wait_send()
        copy.wait_recv()


def scatter(shares, arrays, vec_zero, quads, vec_one, grad, final):
    micro, tokens, width = grad.shape
    lengths = (shares.half, shares.depth // 2, TAIL)
    chunks = sum(len(pair) for pair in chunk_pairs(shares) + quad_pairs(shares))
    rows = sum(lengths)
    anywhere = pl.BlockSpec(memory_space=pl.ANY)
    work = [pltpu.VMEM((2, 2, 4, length, width), LOW) for length in lengths]
    quad = pltpu.VMEM((4, (lengths[0] + lengths[1]) // 2, width), LOW)
    return pl.pallas_call(
        partial(scatter_kernel, shares),
        in_specs=[anywhere] * 10,
        out_specs=[anywhere] * 2,
        out_shape=[
            jax.ShapeDtypeStruct((2, rows, width), LOW),
            jax.ShapeDtypeStruct((micro, tokens, width), LOW),
        ],
        scratch_shapes=work
        + [quad, quad, work[2]]
        + [
            pltpu.VMEM((chunks, 2, 4, PIECE, width), LOW),
            pltpu.VMEM((chunks, 4, PIECE, width), LOW),
            pltpu.VMEM((chunks, 2, PIECE, width), LOW),
            pltpu.VMEM((chunks, 2, PIECE, width), LOW),
            pltpu.VMEM((chunks, 1, PIECE, width), LOW),
            pltpu.VMEM((2, rows, width), LOW),
            pltpu.SemaphoreType.DMA((2, 6)),
            pltpu.SemaphoreType.DMA((2,)),
            pltpu.SemaphoreType.DMA((1,)),
            pltpu.SemaphoreType.DMA((1,)),
            pltpu.SemaphoreType.DMA((3,)),
            pltpu.SemaphoreType.DMA((3,)),
            pltpu.SemaphoreType.DMA((chunks, 5)),
            pltpu.SemaphoreType.DMA((chunks, 5)),
        ],
        compiler_params=pltpu.CompilerParams(
            collective_id=1, has_side_effects=True, vmem_limit_bytes=VMEM_BYTES
        ),
    )(*arrays, vec_zero, *quads, vec_one, grad, final)


def update_kernel(shares, halves_ref, *refs):
    old, new, turned = refs[:9], refs[9:18], refs[18]
    offset = lax.axis_index((DP, SEQ)) * shares.columns
    half, per, width, depth = shares.half, shares.per, shares.width, shares.depth // 2
    is_inner = (offset >= 3 * width) & (offset < 4 * width)
    is_hidden = offset >= 4 * width

    @pl.when(is_inner)
    def _():
        for side in range(2):
            piece = halves_ref[side, :half, :].astype(jnp.float32)
            wide = per * half
            back = jnp.transpose(jnp.concatenate([piece[:, :wide], piece[:, wide:]], axis=0))
            for j in range(per):
                turned[(2 * j + side) * half : (2 * j + side + 1) * half, :] = back[
                    j * half : (j + 1) * half
                ]

    @pl.when(jnp.logical_not(is_inner))
    def _():
        pair = [halves_ref[side, :half, :].astype(jnp.float32) for side in range(2)]
        plain = jnp.concatenate(pair, axis=0)
        hidden = jnp.concatenate(
            [pair[side][j * depth :][:depth] for j in range(shares.groups) for side in range(2)],
            axis=0,
        )
        turned[...] = jnp.transpose(jnp.where(is_hidden, hidden, plain))

    def store(first, gradient, rate, decay):
        results = adam_update(*[ref[...] for ref in old[first : first + 3]], gradient, rate, decay)
        for ref, result in zip(new[first : first + 3], results):
            ref[...] = result

    store(0, turned[...], rate_matrix, decay_matrix)
    down = [halves_ref[side, half : half + depth, :] for side in range(2)]
    store(3, jnp.concatenate(down, axis=0).astype(jnp.float32), rate_matrix, decay_matrix)
    tails = [halves_ref[side, half + depth :, :].astype(jnp.float32) for side in range(2)]
    store(6, (tails[0] + tails[1])[0:1, : shares.vector_len], rate_vector, 0.0)


def update(shares, halves, old):
    return pl.pallas_call(
        partial(update_kernel, shares),
        out_shape=[jax.ShapeDtypeStruct(piece.shape, jnp.float32) for piece in old],
        scratch_shapes=[pltpu.VMEM((shares.width, shares.columns), jnp.float32)],
        compiler_params=pltpu.CompilerParams(vmem_limit_bytes=VMEM_BYTES),
    )(halves, *old)


(GAIN_ONE, SHIFT_ONE, BIAS_OUT, GAIN_TWO, SHIFT_TWO, BIAS_DOWN, BIAS_PROJ, _, BIAS_UP, _) = [
    slice(row, row + 1) for row in range(10)
]
ROWS = 256
COLS = 384
STRIP = 32


def whole(shape):
    return pl.BlockSpec(shape, lambda i: (0,) * len(shape))


def row_block(width):
    return pl.BlockSpec((ROWS, width), lambda i: (i, 0))


def col_block(tokens):
    return pl.BlockSpec((tokens, COLS), lambda i: (0, i))


def at_block(shape, *index):
    return pl.BlockSpec(shape, lambda i: index)


def params_of(flops, moved, transcendentals=0):
    return {
        "compiler_params": pltpu.CompilerParams(vmem_limit_bytes=VMEM_BYTES),
        "cost_estimate": pl.CostEstimate(
            flops=flops, bytes_accessed=moved, transcendentals=transcendentals
        ),
    }


def strips(length=ROWS, strip=STRIP):
    return [slice(first, first + strip) for first in range(0, length, strip)]


def both(own_ref, recv_ref, rows):
    return own_ref[rows, :].astype(jnp.float32) + recv_ref[rows, :].astype(jnp.float32)


def bias_of(vec_ref, first, index):
    start = index * COLS
    width = vec_ref.shape[1]
    row = first.start + start // width
    return vec_ref[row : row + 1, start % width : start % width + COLS]


def eights(values):
    rows, width = values.shape
    return jnp.sum(values.reshape(rows // 8, 8, width), axis=0)


def features_kernel(shares, random_ref, segment_ref, global_ref, query_ref, key_ref, turned_ref):
    core = lax.axis_index(SECTION)
    place = lax.axis_index(SEQ)
    blocks = random_ref.shape[1]
    width = key_ref.shape[1]
    heads = query_ref.shape[0]
    per_half = heads // shares.per
    picks = random_ref.shape[2] // (2 * heads)
    tokens = key_ref.shape[0]
    lane = lax.broadcasted_iota(jnp.int32, (blocks, width), 1)
    row = lax.broadcasted_iota(jnp.int32, (blocks, width), 0)
    key = jnp.where(lane < blocks, lane, lane - blocks)
    chosen = random_ref[place]
    named = global_ref[place]
    always = (jnp.abs(row - key) <= 1).astype(jnp.int32)
    is_global = jnp.zeros((blocks, width), jnp.int32)
    for index in range(named.shape[1]):
        spot = named[:, index : index + 1]
        always = always + (key == spot).astype(jnp.int32)
        is_global = is_global + (row == spot).astype(jnp.int32)
    line = segment_ref[place].astype(jnp.float32)
    column = jnp.transpose(jnp.broadcast_to(line, (8, tokens)))[:, 0:1]
    token_lane = lax.broadcasted_iota(jnp.int32, (tokens, width), 1)
    same = column == (token_lane - 2 * blocks).astype(jnp.float32)
    in_segment = (token_lane >= 2 * blocks) & (token_lane < 2 * blocks + 3)
    segment_side = jnp.where(in_segment & same, 1.0, 0.0)
    for head in range(heads):
        count = always
        for pick in range(picks):
            at = [
                (2 * per_half * (head // per_half) + per_half * side + head % per_half) * picks
                + pick
                for side in range(2)
            ]
            spot = jnp.where(core == 0, chosen[:, at[0] : at[0] + 1], chosen[:, at[1] : at[1] + 1])
            count = count + (key == spot).astype(jnp.int32)
        count = jnp.where(is_global > 0, 1, count)
        high = jnp.where(count == 0, masked, 0.0)
        low = jnp.zeros_like(high)
        for times in (2, 3):
            high = jnp.where(count == times, LOG_HIGH[times - 1], high)
            low = jnp.where(count == times, LOG_LOW[times - 1], low)
        table = jnp.where(lane < blocks, high, jnp.where(lane < 2 * blocks, low, 0.0))
        for block in range(blocks):
            rows = slice(block * BLOCK, (block + 1) * BLOCK)
            query_ref[head, rows, :] = (table[block : block + 1] + segment_side[rows]).astype(LOW)
    token_block = lax.shift_right_logical(
        lax.broadcasted_iota(jnp.int32, (tokens, width), 0), BLOCK.bit_length() - 1
    )
    here = (token_block == token_lane) | (token_block == token_lane - blocks)
    side = jnp.where(here & (token_lane < 2 * blocks), 1.0, 0.0)
    side = jnp.where(in_segment & jnp.logical_not(same), masked, side)
    ones = (token_lane >= 2 * blocks + 3) & (token_lane < 2 * blocks + 6)
    side = jnp.where(ones, 1.0, side)
    key_ref[...] = side.astype(LOW)
    turned_ref[...] = jnp.transpose(side).astype(LOW)


def key_features(shares, random_ids, segment_ids, global_ids):
    micro, _, blocks, head_count, picks = random_ids.shape
    tokens = segment_ids.shape[2]
    width = -(-(2 * blocks + 6) // 128) * 128
    return pl.pallas_call(
        partial(features_kernel, shares),
        out_shape=[
            jax.ShapeDtypeStruct((head_count // 2, tokens, width), LOW),
            jax.ShapeDtypeStruct((tokens, width), LOW),
            jax.ShapeDtypeStruct((width, tokens), LOW),
        ],
        **params_of(0, head_count * tokens * width),
    )(random_ids.reshape(micro, blocks, head_count * picks), segment_ids, global_ids)


def project_kernel(joins, *refs):
    if joins:
        (middle_ref, part_ref, recv_ref, before_ref), refs = refs[:4], refs[4:]
    else:
        hidden_ref, refs = refs[0], refs[1:]
    (vec_ref, weight_ref), refs = refs[:2], refs[2:]
    if joins:
        hidden_ref, refs = refs[0], refs[1:]
    normed_ref, out_ref = refs
    for rows in strips():
        if joins:
            part = both(part_ref, recv_ref, rows)
            low = (middle_ref[rows, :] + part + before_ref[BIAS_DOWN]).astype(LOW)
            hidden_ref[rows, :] = low
        else:
            low = hidden_ref[rows, :]
        unit, _ = normalized(low.astype(jnp.float32))
        normed_ref[rows, :] = (unit * vec_ref[GAIN_ONE] + vec_ref[SHIFT_ONE]).astype(LOW)
    for index in range(out_ref.shape[1] // COLS):
        cols = slice(index * COLS, (index + 1) * COLS)
        product = dot_rows(normed_ref[...], weight_ref[cols, :])
        out_ref[:, cols] = (product + bias_of(vec_ref, BIAS_PROJ, index)).astype(LOW)


def project(before, vec, rows, out_width):
    joins = len(before) > 1
    tokens, width = before[0].shape
    ins = [row_block(width)] * 3 + [whole(vec.shape)] if joins else [row_block(width)]
    outs = [row_block(width)] * (2 if joins else 1)
    low = jax.ShapeDtypeStruct((tokens, width), LOW)
    return pl.pallas_call(
        partial(project_kernel, joins),
        grid=(tokens // ROWS,),
        in_specs=ins + [whole(vec.shape), whole((out_width, width))],
        out_specs=outs + [row_block(out_width)],
        out_shape=[low] * len(outs) + [jax.ShapeDtypeStruct((tokens, out_width), LOW)],
        **params_of(2 * tokens * width * out_width, tokens * width * 16),
    )(*before, vec, rows)


def out_halves(packed_ref, half):
    wide = packed_ref.shape[1] // 2
    return [
        jnp.concatenate([packed_ref[rows, :wide], packed_ref[rows, wide:]], axis=0)
        for rows in (slice(0, half), slice(half, 2 * half))
    ]


def branch_kernel(half, attended_ref, packed_ref, low_ref):
    wide = attended_ref.shape[1]
    for index, weights in enumerate(out_halves(packed_ref, half)):
        cols = slice(index * wide, (index + 1) * wide)
        low_ref[:, cols] = dot_rows(attended_ref[...], weights).astype(LOW)


def branch_out(shares, attended, rows):
    tokens, wide = attended.shape
    width = rows.shape[1]
    return pl.pallas_call(
        partial(branch_kernel, shares.half),
        grid=(tokens // ROWS,),
        in_specs=[row_block(wide), at_block((COLS, width), 3, 0)],
        out_specs=row_block(width),
        out_shape=jax.ShapeDtypeStruct((tokens, width), LOW),
        **params_of(2 * tokens * width * wide, tokens * width * 4),
    )(attended, rows)


def gelu_parts(value):
    below = 1.0 + (0.3275911 * 0.5**0.5) * jnp.abs(value)
    rough = pl.reciprocal(below, approx=True)
    t = rough * (2.0 - below * rough)
    bell = jnp.exp((-0.5 * value) * value)
    poly = 0.5 * 1.061405429
    for coefficient in (-1.453152027, 1.421413741, -0.284496736, 0.254829592):
        poly = poly * t + 0.5 * coefficient
    tail = poly * (t * bell)
    cdf = jnp.where(value > 0, 1.0 - tail, tail)
    return value * cdf, cdf + value * (bell * (0.5 / math.pi) ** 0.5)


def expand_kernel(
    hidden_ref,
    branch_ref,
    recv_ref,
    vec_ref,
    up_ref,
    down_ref,
    middle_ref,
    normed_ref,
    slope_ref,
    active_ref,
    low_ref,
    held,
):
    for rows in strips():
        branch = both(branch_ref, recv_ref, rows) + vec_ref[BIAS_OUT]
        middle = hidden_ref[rows, :].astype(jnp.float32) + branch
        middle_ref[rows, :] = middle
        unit, _ = normalized(middle)
        normed_ref[rows, :] = (unit * vec_ref[GAIN_TWO] + vec_ref[SHIFT_TWO]).astype(LOW)
    for index in range(up_ref.shape[0] // COLS):
        cols = slice(index * COLS, (index + 1) * COLS)
        held[index] = dot_rows(normed_ref[...], up_ref[cols, :])
        for rows in strips():
            active, slope = gelu_parts(held[index, rows, :] + bias_of(vec_ref, BIAS_UP, index))
            active_ref[rows, cols] = active.astype(LOW)
            slope_ref[rows, cols] = slope.astype(LOW)
    low_ref[...] = dot_plain(active_ref[...], down_ref[...]).astype(LOW)


def expand(hidden, branch, recv, vec, rows, down):
    tokens, width = hidden.shape
    inner = down.shape[0]
    return pl.pallas_call(
        expand_kernel,
        grid=(tokens // ROWS,),
        in_specs=[row_block(width)] * 3
        + [whole(vec.shape), at_block((inner, width), 1, 0), whole((inner, width))],
        out_specs=[row_block(width), row_block(width), row_block(inner), row_block(inner)]
        + [row_block(width)],
        out_shape=[
            jax.ShapeDtypeStruct((tokens, width), jnp.float32),
            jax.ShapeDtypeStruct((tokens, width), LOW),
            jax.ShapeDtypeStruct((tokens, inner), LOW),
            jax.ShapeDtypeStruct((tokens, inner), LOW),
            jax.ShapeDtypeStruct((tokens, width), LOW),
        ],
        scratch_shapes=[pltpu.VMEM((inner // COLS, ROWS, COLS), jnp.float32)],
        **params_of(4 * tokens * width * inner, tokens * width * 32, tokens * inner),
    )(hidden, branch, recv, vec, rows, down)


def expand_back_kernel(
    grad_ref,
    slope_ref,
    up_ref,
    down_ref,
    low_ref,
    grad_up_ref,
    bias_up_ref,
    bias_down_ref,
    sums_up,
    sums_down,
):
    step = pl.program_id(0)

    @pl.when(step == 0)
    def _():
        sums_up[...] = jnp.zeros_like(sums_up)
        sums_down[...] = jnp.zeros_like(sums_down)

    for index in range(down_ref.shape[0] // COLS):
        cols = slice(index * COLS, (index + 1) * COLS)
        grad_active = dot_rows(grad_ref[...], down_ref[cols, :])
        grad_up_ref[:, cols] = (grad_active * slope_ref[:, cols].astype(jnp.float32)).astype(LOW)
    low_ref[...] = dot_plain(grad_up_ref[...], up_ref[...]).astype(LOW)
    for rows in strips():
        sums_up[...] += eights(grad_up_ref[rows, :].astype(jnp.float32))
        sums_down[...] += eights(grad_ref[rows, :].astype(jnp.float32))

    @pl.when(step == pl.num_programs(0) - 1)
    def _():
        bias_up_ref[...] = jnp.sum(sums_up[...], axis=0, keepdims=True)
        bias_down_ref[...] = jnp.sum(sums_down[...], axis=0, keepdims=True)


def expand_back(grad, slope, rows, down):
    tokens, width = grad.shape
    inner = down.shape[0]
    return pl.pallas_call(
        expand_back_kernel,
        grid=(tokens // ROWS,),
        in_specs=[row_block(width), row_block(inner)]
        + [at_block((inner, width), 1, 0), whole((inner, width))],
        out_specs=[row_block(width), row_block(inner), whole((1, inner)), whole((1, width))],
        out_shape=[
            jax.ShapeDtypeStruct((tokens, width), LOW),
            jax.ShapeDtypeStruct((tokens, inner), LOW),
            jax.ShapeDtypeStruct((1, inner), jnp.float32),
            jax.ShapeDtypeStruct((1, width), jnp.float32),
        ],
        scratch_shapes=[pltpu.VMEM((8, inner), jnp.float32), pltpu.VMEM((8, width), jnp.float32)],
        **params_of(4 * tokens * width * inner, tokens * width * 24),
    )(grad, slope, rows, down)


def token_products_kernel(count, *refs):
    lefts, rights, outs = refs[:count], refs[count : 2 * count], refs[2 * count :]
    for left, right, out in zip(lefts, rights, outs):
        for first in range(0, COLS, 128):
            cols = slice(first, first + 128)
            out[cols, :] = dot_tokens(left[:, cols], right[...]).astype(LOW)


def token_products(*pairs):
    lefts, rights = zip(*pairs)
    tokens, inner = lefts[0].shape
    width = rights[0].shape[1]
    count = len(pairs)
    return pl.pallas_call(
        partial(token_products_kernel, count),
        grid=(inner // COLS,),
        in_specs=[col_block(tokens)] * count + [whole((tokens, width))] * count,
        out_specs=[pl.BlockSpec((COLS, width), lambda i: (i, 0))] * count,
        out_shape=[jax.ShapeDtypeStruct((inner, width), LOW)] * count,
        **params_of(2 * count * tokens * width * inner, count * tokens * width * 8),
    )(*lefts, *rights)


def norm_back_rows(values_in, incoming, gain_vec):
    unit, scale = normalized(values_in)
    p = incoming * gain_vec
    mean_p = jnp.mean(p, axis=-1, keepdims=True)
    mean_pn = jnp.mean(p * unit, axis=-1, keepdims=True)
    return scale * (p - mean_p - unit * mean_pn), eights(incoming * unit), eights(incoming)


def branch_back_kernel(
    half,
    middle_ref,
    part_ref,
    recv_ref,
    grad_ref,
    attended_ref,
    vec_ref,
    packed_ref,
    grad_middle_ref,
    grad_attended_ref,
    out_grad_ref,
    gain_grad_ref,
    shift_grad_ref,
    bias_grad_ref,
    total,
    low,
    sums,
):
    step = pl.program_id(0)

    @pl.when(step == 0)
    def _():
        total[...] = jnp.zeros_like(total)
        sums[...] = jnp.zeros_like(sums)

    for rows in strips():
        incoming = both(part_ref, recv_ref, rows)
        change, for_gain, for_shift = norm_back_rows(
            middle_ref[rows, :], incoming, vec_ref[GAIN_TWO]
        )
        grad_middle = grad_ref[rows, :].astype(jnp.float32) + change
        grad_middle_ref[rows, :] = grad_middle
        rounded = grad_middle.astype(LOW)
        low[rows, :] = rounded
        sums[0] += for_gain
        sums[1] += for_shift
        sums[2] += eights(rounded.astype(jnp.float32))
    weights = out_halves(packed_ref, half)
    wide = weights[0].shape[0]
    attended = attended_ref[...]
    pieces = [low[:, :wide], low[:, wide:]]
    grad_attended_ref[...] = (
        dot_plain(pieces[0], weights[0]) + dot_plain(pieces[1], weights[1])
    ).astype(LOW)
    for index in range(2):
        total[index] += dot_tokens(pieces[index], attended)

    @pl.when(step == pl.num_programs(0) - 1)
    def _():
        for index in range(2):
            joined = jnp.concatenate([total[index, :half, :], total[index, half:, :]], axis=1)
            out_grad_ref[index * half : (index + 1) * half, :] = joined.astype(LOW)
        for index, ref in enumerate((gain_grad_ref, shift_grad_ref, bias_grad_ref)):
            ref[...] = jnp.sum(sums[index], axis=0, keepdims=True)


def branch_back(shares, middle, part, recv, grad, attended, vec, rows):
    tokens, width = middle.shape
    wide = attended.shape[1]
    small = whole((1, width))
    one = jax.ShapeDtypeStruct((1, width), jnp.float32)
    return pl.pallas_call(
        partial(branch_back_kernel, shares.half),
        grid=(tokens // ROWS,),
        in_specs=[row_block(width)] * 4
        + [row_block(wide), whole(vec.shape), at_block((COLS, width), 3, 0)],
        out_specs=[row_block(width), row_block(wide), whole((COLS, width)), small, small, small],
        out_shape=[
            jax.ShapeDtypeStruct((tokens, width), jnp.float32),
            jax.ShapeDtypeStruct((tokens, wide), LOW),
            jax.ShapeDtypeStruct((COLS, width), LOW),
            one,
            one,
            one,
        ],
        scratch_shapes=[
            pltpu.VMEM((2, width // 2, wide), jnp.float32),
            pltpu.VMEM((ROWS, width), LOW),
            pltpu.VMEM((3, 8, width), jnp.float32),
        ],
        **params_of(4 * tokens * width * wide, tokens * width * 20),
    )(middle, part, recv, grad, attended, vec, rows)


def project_back_kernel(grad_ref, weight_ref, low_ref, bias_ref, sums):
    step = pl.program_id(0)

    @pl.when(step == 0)
    def _():
        sums[...] = jnp.zeros_like(sums)

    low_ref[...] = dot_plain(grad_ref[...], weight_ref[...]).astype(LOW)
    for rows in strips():
        sums[...] += eights(grad_ref[rows, :].astype(jnp.float32))

    @pl.when(step == pl.num_programs(0) - 1)
    def _():
        bias_ref[...] = jnp.sum(sums[...], axis=0, keepdims=True)


def project_back(grad_proj, rows):
    tokens, out_width = grad_proj.shape
    width = rows.shape[1]
    return pl.pallas_call(
        project_back_kernel,
        grid=(tokens // ROWS,),
        in_specs=[row_block(out_width), whole((out_width, width))],
        out_specs=[row_block(width), whole((1, out_width))],
        out_shape=[
            jax.ShapeDtypeStruct((tokens, width), LOW),
            jax.ShapeDtypeStruct((1, out_width), jnp.float32),
        ],
        scratch_shapes=[pltpu.VMEM((8, out_width), jnp.float32)],
        **params_of(2 * tokens * width * out_width, tokens * width * 12),
    )(grad_proj, rows)


def input_back_kernel(
    hidden_ref, part_ref, recv_ref, grad_ref, vec_ref, out_ref, gain_grad_ref, shift_grad_ref, sums
):
    step = pl.program_id(0)

    @pl.when(step == 0)
    def _():
        sums[...] = jnp.zeros_like(sums)

    for rows in strips():
        incoming = both(part_ref, recv_ref, rows)
        hidden = hidden_ref[rows, :].astype(jnp.float32)
        change, for_gain, for_shift = norm_back_rows(hidden, incoming, vec_ref[GAIN_ONE])
        out_ref[rows, :] = (grad_ref[rows, :] + change).astype(LOW)
        sums[0] += for_gain
        sums[1] += for_shift

    @pl.when(step == pl.num_programs(0) - 1)
    def _():
        gain_grad_ref[...] = jnp.sum(sums[0], axis=0, keepdims=True)
        shift_grad_ref[...] = jnp.sum(sums[1], axis=0, keepdims=True)


def input_back(hidden, part, recv, grad_middle, vec):
    tokens, width = hidden.shape
    small = whole((1, width))
    one = jax.ShapeDtypeStruct((1, width), jnp.float32)
    return pl.pallas_call(
        input_back_kernel,
        grid=(tokens // ROWS,),
        in_specs=[row_block(width)] * 4 + [whole(vec.shape)],
        out_specs=[row_block(width), small, small],
        out_shape=[jax.ShapeDtypeStruct((tokens, width), LOW), one, one],
        scratch_shapes=[pltpu.VMEM((2, 8, width), jnp.float32)],
        **params_of(0, tokens * width * 12),
    )(hidden, part, recv, grad_middle, vec)


def attend_kernel(q_ref, k_ref, v_ref, qa_ref, kt_ref, out_ref, lse_ref, keys, held, low):
    tokens, pair = q_ref.shape
    left = lax.broadcasted_iota(jnp.int32, (CHUNK, pair), 1) < pair // 2
    keys[:pair, :] = jnp.transpose(k_ref[...].astype(jnp.float32)).astype(LOW)
    keys[pair:, :] = kt_ref[...]
    for index in range(tokens // CHUNK):
        rows = slice(index * CHUNK, (index + 1) * CHUNK)
        queries = q_ref[rows, :] * 0.125
        outs, tops = [], []
        for head in range(2):
            slot = (2 * index + head) % held.shape[0]
            mine = left if head == 0 else jnp.logical_not(left)
            side = jnp.where(mine, queries, jnp.zeros_like(queries))
            lhs = jnp.concatenate([side, qa_ref[head, rows, :]], axis=1)
            held[slot] = dot_plain(lhs, keys[...])
            levels, shares = [], []
            for strip in strips(CHUNK):
                scores = held[slot, strip, :]
                top = jnp.max(scores, axis=1, keepdims=True)
                weight = jnp.exp(scores - top)
                total = jnp.sum(weight, axis=1, keepdims=True)
                low[slot, strip, :] = weight.astype(LOW)
                levels.append(top + jnp.log(total))
                shares.append(1.0 / total)
            product = dot_plain(low[slot], v_ref[...])
            outs.append(product * jnp.concatenate(shares, axis=0))
            tops.append(jnp.concatenate(levels, axis=0))
        out_ref[rows, :] = jnp.where(left, outs[0], outs[1]).astype(LOW)
        lse_ref[rows, :] = jnp.where(left, tops[0], tops[1])


def attend(projected, query_side, key_side, turned):
    tokens = projected.shape[0]
    width = projected.shape[1] // 3
    pairs = width // 128
    features = key_side.shape[1]
    return pl.pallas_call(
        attend_kernel,
        grid=(pairs,),
        in_specs=[
            pl.BlockSpec((tokens, 128), lambda p: (0, p)),
            pl.BlockSpec((tokens, 128), lambda p: (0, pairs + p)),
            pl.BlockSpec((tokens, 128), lambda p: (0, 2 * pairs + p)),
            pl.BlockSpec((2, tokens, features), lambda p: (p, 0, 0)),
            whole((features, tokens)),
        ],
        out_specs=[
            pl.BlockSpec((tokens, 128), lambda p: (0, p)),
            pl.BlockSpec((tokens, 128), lambda p: (0, p)),
        ],
        out_shape=[
            jax.ShapeDtypeStruct((tokens, width), LOW),
            jax.ShapeDtypeStruct((tokens, width), jnp.float32),
        ],
        scratch_shapes=[
            pltpu.VMEM((128 + features, tokens), LOW),
            pltpu.VMEM((4, CHUNK, tokens), jnp.float32),
            pltpu.VMEM((4, CHUNK, tokens), LOW),
        ],
        **params_of(
            16 * pairs * tokens * tokens * 128, tokens * width * 16, 2 * pairs * tokens * tokens
        ),
    )(projected, projected, projected, query_side, turned)


def three_terms(values):
    high = values.astype(LOW).astype(jnp.float32)
    rest = values - high
    middle = rest.astype(LOW).astype(jnp.float32)
    return high, middle, rest - middle


def attend_back_kernel(
    q_ref,
    k_ref,
    v_ref,
    do_ref,
    o_ref,
    lse_ref,
    qa_ref,
    ka_ref,
    grad_ref,
    held,
    probs,
    changes,
    query_sides,
    grad_sides,
):
    tokens, pair = q_ref.shape
    features = ka_ref.shape[1]
    pairs = pl.num_programs(0)
    place = pl.program_id(0)
    first = 2 * (tokens // BLOCK) + 3
    half = pair // 2
    left = lax.broadcasted_iota(jnp.int32, (CHUNK, pair), 1) < half
    lane = lax.broadcasted_iota(jnp.int32, (CHUNK, features), 1)
    lane_pair = lax.broadcasted_iota(jnp.int32, (CHUNK, pair), 1)
    keys = jnp.concatenate([k_ref[...], ka_ref[...]], axis=1)
    turned = jnp.transpose(k_ref[...].astype(jnp.float32)).astype(LOW)
    ones = (lax.broadcasted_iota(jnp.int32, (tokens, pair), 1) < 3).astype(jnp.float32).astype(LOW)
    values = jnp.concatenate([v_ref[...], ones], axis=1)
    parts, key_grads, value_grads = [], [], []
    for head in range(2):
        mine = left if head == 0 else jnp.logical_not(left)
        for index in range(tokens // CHUNK):
            rows = slice(index * CHUNK, (index + 1) * CHUNK)
            slot = index % 2
            queries = q_ref[rows, :] * 0.125
            grads = do_ref[rows, :]
            product = grads.astype(jnp.float32) * o_ref[rows, :].astype(jnp.float32)
            level = lse_ref[rows, head * half : head * half + 1]
            inner = jnp.sum(jnp.where(mine, product, 0.0), axis=1, keepdims=True)
            side = qa_ref[head, rows, :].astype(jnp.float32)
            for spot, term in enumerate(three_terms(level)):
                side = jnp.where(lane == first + spot, -term, side)
            query_side = jnp.where(mine, queries, jnp.zeros_like(queries))
            grad_side = jnp.where(mine, grads, jnp.zeros_like(grads))
            query_sides[head, rows, :] = query_side
            grad_sides[head, rows, :] = grad_side
            tail = jnp.zeros((CHUNK, pair), jnp.float32)
            for spot, term in enumerate(three_terms(inner)):
                tail = jnp.where(lane_pair == spot, -term, tail)
            held[slot, 0] = dot_rows(
                keys, jnp.concatenate([query_side, side.astype(LOW)], axis=1)
            )
            held[slot, 1] = dot_rows(
                values, jnp.concatenate([grad_side, tail.astype(LOW)], axis=1)
            )
            for strip in strips(tokens, 128):
                prob = jnp.exp(held[slot, 0, strip, :])
                probs[head, strip, rows] = prob.astype(LOW)
                changes[head, strip, rows] = (prob * held[slot, 1, strip, :]).astype(LOW)
        value_grads.append(dot_plain(probs[head], grad_sides[head]))
        key_grads.append(dot_plain(changes[head], query_sides[head]))
        parts.append(dot_plain(turned, changes[head]))
    joined = jnp.concatenate([parts[0][:half], parts[1][half:]], axis=0)
    column = [pl.ds(pl.multiple_of((by * pairs + place) * 128, 128), 128) for by in range(3)]
    grad_ref[:, column[0]] = (jnp.transpose(joined) * 0.125).astype(LOW)
    grad_ref[:, column[1]] = (key_grads[0] + key_grads[1]).astype(LOW)
    grad_ref[:, column[2]] = (value_grads[0] + value_grads[1]).astype(LOW)


def attend_back(projected, grad_attended, attended, levels, query_side, key_side):
    tokens, width = attended.shape
    pairs = width // 128
    features = key_side.shape[1]
    by_pair = pl.BlockSpec((tokens, 128), lambda p: (0, p))
    return pl.pallas_call(
        attend_back_kernel,
        grid=(pairs,),
        in_specs=[
            by_pair,
            pl.BlockSpec((tokens, 128), lambda p: (0, pairs + p)),
            pl.BlockSpec((tokens, 128), lambda p: (0, 2 * pairs + p)),
            by_pair,
            by_pair,
            by_pair,
            pl.BlockSpec((2, tokens, features), lambda p: (p, 0, 0)),
            whole((tokens, features)),
        ],
        out_specs=whole((tokens, 3 * width)),
        out_shape=jax.ShapeDtypeStruct((tokens, 3 * width), LOW),
        scratch_shapes=[
            pltpu.VMEM((2, 2, tokens, CHUNK), jnp.float32),
            pltpu.VMEM((2, tokens, tokens), LOW),
            pltpu.VMEM((2, tokens, tokens), LOW),
            pltpu.VMEM((2, tokens, 128), LOW),
            pltpu.VMEM((2, tokens, 128), LOW),
        ],
        **params_of(
            40 * pairs * tokens * tokens * 128, tokens * width * 24, 2 * pairs * tokens * tokens
        ),
    )(projected, projected, projected, grad_attended, attended, levels, query_side, key_side)


def window_forward(shares, before, weights, vec, features, beside):
    rows, down = weights
    results = project(before, vec, rows, 6 * shares.half)
    hidden = before[0] if len(before) == 1 else results[0]
    normed, projected = results[-2:]
    projected = beside.tie(projected)
    attended, levels = beside.tie(tuple(attend(projected, *features)))
    low = branch_out(shares, attended, rows)
    expanded = expand(hidden, low, swap(low), vec, rows, down)
    middle, normed_two, slope, active, low = beside.tie(tuple(expanded))
    stored = (hidden, normed, projected, attended, levels, middle, normed_two, slope, active)
    return (middle, low, swap(low), vec), stored


def window_backward(shares, stored, grad, weights, vec, features, beside):
    hidden, normed, projected, attended, levels, middle, normed_two, slope, active = stored
    rows, down = weights
    low, grad_up, bias_up, bias_down = beside.tie(tuple(expand_back(grad, slope, rows, down)))
    arrived = swap(low)
    down_grad, up_grad = token_products((active, grad), (grad_up, normed_two))
    grad_middle, grad_attended, out_grad, gain_two, shift_two, bias_out = branch_back(
        shares, middle, low, arrived, grad, attended, vec, rows
    )
    grad_attended = beside.tie(grad_attended)
    grad_proj = attend_back(projected, grad_attended, attended, levels, *features[:2])
    grad_proj = beside.tie(grad_proj)
    low, summed = project_back(grad_proj, rows)
    arrived = swap(low)
    (proj_grad,) = token_products((grad_proj, normed))
    grad, gain_one, shift_one = input_back(hidden, low, arrived, grad_middle, vec)
    width = attended.shape[1]
    vector_grads = (gain_one, shift_one, summed[:, :width], summed[:, 2 * width :], bias_out)
    vector_grads += (gain_two, shift_two, bias_down, bias_up)
    vector_grads = [piece[0] for piece in vector_grads]
    return grad, (proj_grad, out_grad, up_grad, down_grad), vector_grads


def window_shards(
    block_input,
    cotangent,
    random_ids,
    segment_ids,
    global_ids,
    w_rows,
    w_rows_first,
    w_rows_second,
    w_down,
    w_down_first,
    w_down_second,
    vectors,
    vectors_first,
    vectors_second,
):
    core = lax.axis_index(SECTION)
    micro, _, tokens, width = block_input.shape
    _, _, columns = w_rows.shape
    shares = Shares(width, columns, w_down.shape[1], vectors.shape[1])
    prepared = prepare(shares, w_rows[0], w_down[0], vectors)
    features = key_features(shares, random_ids, segment_ids, global_ids)
    gathered_zero, gathered_one, hidden, grad = gather(shares, prepared, block_input, cotangent)

    beside = Beside(spread_quads(shares, gathered_one[:2]))
    params = [shares.unpack(gathered_zero, core)]
    before = (hidden.reshape(-1, width),)
    before, stored_zero = window_forward(shares, before, *params[0], features, beside)
    params.append(shares.unpack((*beside.flying, gathered_one[2]), core))
    after, stored_one = window_forward(shares, before, *params[1], features, Beside())
    final = after[1].astype(jnp.float32) + after[2].astype(jnp.float32)
    final = (after[0] + final + after[3][BIAS_DOWN]).astype(LOW)

    grad = grad.reshape(-1, width)
    grad, *grads_one = window_backward(shares, stored_one, grad, *params[1], features, Beside())
    *arrays_one, vec_one = shares.by_shard(*grads_one, core)
    beside = Beside(sum_quads(shares, arrays_one))
    grad, *grads_zero = window_backward(shares, stored_zero, grad, *params[0], features, beside)
    *arrays_zero, vec_zero = shares.by_shard(*grads_zero, core)
    grad, final = [piece.reshape(micro, tokens, width) for piece in (grad, final)]
    halves, slices = scatter(shares, arrays_zero, vec_zero, beside.flying, vec_one, grad, final)
    section_result = slices.astype(jnp.float32)[None, :, None]
    old = [
        w_rows[0],
        w_rows_first[0],
        w_rows_second[0],
        w_down[0],
        w_down_first[0],
        w_down_second[0],
        vectors,
        vectors_first,
        vectors_second,
    ]
    new = update(shares, halves, old)
    return (section_result, *[piece[None] for piece in new[:6]], *new[6:])


def one_window_each(mesh, block_input, w_rows, w_down, vectors):
    micro, windows, length, width = block_input.shape
    shards = mesh.shape[DP] * mesh.shape[SEQ]
    columns, depth = w_rows.shape[2] // shards, w_down.shape[1] // shards
    head_dim = width // HEADS
    tokens = length // mesh.shape[SEQ]
    return (
        mesh.shape[SECTION] == 2
        and mesh.shape[SEQ] == micro
        and mesh.shape[DP] == windows
        and tokens % (2 * BLOCK) == 0
        and length % CHUNK == 0
        and head_dim == 64
        and width % columns == 0
        and columns % (2 * head_dim) == 0
        and columns % depth == 0
        and width // columns * (columns // 2) % 128 == 0
        and depth % 32 == 0
        and vectors.shape[1] // shards <= width
        and mesh.shape[DP] == 4
        and micro == 4
        and width == 2 * columns == 2 * COLS
        and w_down.shape[1] == 4 * width
        and (columns // 2) % (2 * PIECE) == 0
        and (depth // 2) % (2 * PIECE) == 0
        and length % (4 * ROWS) == 0
    )


def solution(mesh):
    in_specs = (
        P(None, DP, SEQ, None),
        P(None, DP, SEQ, None),
        P(None, DP, None, None, None),
        P(None, DP, None),
        P(None, DP, None),
        P(SECTION, None, (DP, SEQ)),
        P(SECTION, None, (DP, SEQ)),
        P(SECTION, None, (DP, SEQ)),
        P(SECTION, (DP, SEQ), None),
        P(SECTION, (DP, SEQ), None),
        P(SECTION, (DP, SEQ), None),
        P(SECTION, (DP, SEQ)),
        P(SECTION, (DP, SEQ)),
        P(SECTION, (DP, SEQ)),
    )
    out_specs = (
        P(SECTION, None, DP, SEQ, None),
        P(SECTION, None, (DP, SEQ)),
        P(SECTION, None, (DP, SEQ)),
        P(SECTION, None, (DP, SEQ)),
        P(SECTION, (DP, SEQ), None),
        P(SECTION, (DP, SEQ), None),
        P(SECTION, (DP, SEQ), None),
        P(SECTION, (DP, SEQ)),
        P(SECTION, (DP, SEQ)),
        P(SECTION, (DP, SEQ)),
    )

    def step(*arrays):
        chosen = general_shards
        if one_window_each(mesh, arrays[0], arrays[5], arrays[8], arrays[11]):
            chosen = window_shards
        return jax.shard_map(
            chosen, mesh=mesh, in_specs=in_specs, out_specs=out_specs, check_vma=False
        )(*arrays)

    return step
```

```python
import math
from functools import partial

import jax
import jax.numpy as jnp
import ml_dtypes
import numpy as np
from jax import lax
from jax.experimental import pallas as pl
from jax.experimental.pallas import tpu as pltpu
from jax.sharding import PartitionSpec as P

SECTION, DP, SEQ = "section", "dp", "seq"
HEADS = 12
BLOCK = 64
STEP = 5


epsilon = 1e-05
masked = -1e30
rate_matrix = 0.02
rate_vector = 0.2
decay_matrix = 0.01


def with_halo(x, sides, width):
    for axis, dim in sides:
        devices, length = (lax.axis_size(axis), x.shape[dim])
        up = [(i, (i + 1) % devices) for i in range(devices - 1)]
        down = [(j, i) for i, j in up]
        last = lax.slice_in_dim(x, length - width, length, axis=dim)
        initial = lax.slice_in_dim(x, 0, width, axis=dim)
        before = lax.ppermute(last, axis, up)
        after = lax.ppermute(initial, axis, down)
        x = jnp.concatenate([before, x, after], axis=dim)
    return x


def merged(value, axis, join):
    pieces = jax.tree.map(lambda part: lax.all_gather(part, axis), value)
    head = jax.tree.map(lambda part: part[0], pieces)
    tail = jax.tree.map(lambda part: part[1:], pieces)
    subtotal, _ = lax.scan(lambda subtotal, share: (join(subtotal, share), None), head, tail)
    return subtotal


def from_behind(x, axis, by):
    devices = lax.axis_size(axis)
    pairs = [(i, i + by) for i in range(devices) if 0 <= i + by < devices]
    return lax.ppermute(x, axis, pairs)


def partner(value, axis, bit):
    mask = 2**bit
    pairs = [(source, source ^ mask) for source in range(lax.axis_size(axis))]
    return lax.ppermute(value, axis, pairs)


def mixed_sum(form, left, right):
    return jnp.einsum(form, left, right, preferred_element_type=jnp.float32)


def exact_two(form, left, right):
    return jnp.einsum(
        form, left, right, precision=lax.Precision.HIGHEST, preferred_element_type=jnp.float32
    )


def norm_rows(values_in, gain_vec, shift_vec):
    row_mean = jnp.mean(values_in, axis=-1, keepdims=True)
    centred = values_in - row_mean
    spread = jnp.mean(centred * centred, axis=-1, keepdims=True)
    return centred * lax.rsqrt(spread + epsilon) * gain_vec + shift_vec


def split_vectors(vector_weights, model_width):
    pieces = [
        vector_weights[piece_index * model_width : (piece_index + 1) * model_width]
        for piece_index in range(8)
    ]
    return pieces + [vector_weights[8 * model_width :]]


def route_tables(random_rows, segments, global_rows, seq_place, groups):
    windows, blocks, head_count, pick_count = random_rows.shape
    blocks_dev = blocks // groups
    request_count = blocks_dev * head_count * pick_count
    capacity = -(-request_count // groups)
    requests = random_rows.reshape(windows, groups, request_count)
    owners = requests // blocks_dev
    inside = requests % blocks_dev
    head_of = jnp.arange(request_count) // pick_count % head_count
    is_mine = owners == seq_place
    slot_index = jnp.cumsum(is_mine.astype(jnp.int32), axis=2) - 1
    slot_hot = ((slot_index[..., None] == jnp.arange(capacity)) & is_mine[..., None]).astype(
        jnp.float32
    )
    inside_hot = (inside[..., None] == jnp.arange(blocks_dev)).astype(jnp.float32)
    head_hot = (head_of[:, None] == jnp.arange(head_count)).astype(jnp.float32)
    sender = jnp.einsum(
        "wqsc,wqsb,sh->wqcbh", slot_hot, inside_hot, head_hot, precision=lax.Precision.HIGHEST
    )
    my_owners = lax.dynamic_index_in_dim(owners, seq_place, axis=1, keepdims=False)
    earlier = jnp.arange(request_count)[None, :] < jnp.arange(request_count)[:, None]
    same_owner = my_owners[:, :, None] == my_owners[:, None, :]
    rank_index = jnp.sum((same_owner & earlier[None]).astype(jnp.int32), axis=2)
    picker = (
        (my_owners[..., None, None] == jnp.arange(groups)[:, None])
        & (rank_index[..., None, None] == jnp.arange(capacity)[None, :])
    ).astype(jnp.float32)
    first_block = seq_place * blocks_dev
    owned_hot = (global_rows[:, :, None] == first_block + jnp.arange(blocks_dev)).astype(
        jnp.float32
    )
    length = segments.shape[1]
    block_len = length // blocks
    seg_blocks = segments.reshape(windows, blocks, block_len)
    seg_pad = jnp.pad(seg_blocks, ((0, 0), (1, 1), (0, 0)), constant_values=-1)
    near_segs = lax.dynamic_slice_in_dim(seg_pad, first_block, blocks_dev + 2, axis=1)
    slide_seg = jnp.concatenate([near_segs[:, :-2], near_segs[:, 1:-1], near_segs[:, 2:]], axis=2)
    query_seg = near_segs[:, 1:-1]
    rows_index = jnp.arange(windows)
    global_seg = seg_blocks[rows_index[:, None], global_rows].reshape(windows, -1)
    chosen = lax.dynamic_slice_in_dim(random_rows, first_block, blocks_dev, axis=1)
    far_seg = seg_blocks[rows_index[:, None, None, None], chosen].reshape(
        windows, blocks_dev, head_count, -1
    )
    key_seg = jnp.concatenate(
        [
            jnp.broadcast_to(
                slide_seg[:, :, None, :], (windows, blocks_dev, head_count, slide_seg.shape[2])
            ),
            jnp.broadcast_to(
                global_seg[:, None, None, :], (windows, blocks_dev, head_count, global_seg.shape[1])
            ),
            far_seg,
        ],
        axis=3,
    )
    key_mask = query_seg[:, :, None, :, None] == key_seg[:, :, :, None, :]
    local_seg = query_seg.reshape(windows, -1)
    full_mask = global_seg[:, None, :, None] == local_seg[:, None, None, :]
    return (sender, picker, owned_hot, key_mask, full_mask)


def fetch_blocks(paired, queries, sender, picker, owned_hot):
    windows, tokens, head_count, doubled = paired.shape
    head_dim = queries.shape[-1]
    blocks_dev = tokens // BLOCK
    flattened = paired.reshape(windows, tokens, head_count * doubled)
    padded = with_halo(flattened, ((SEQ, 1),), BLOCK)
    framed = padded.reshape(windows, blocks_dev + 2, BLOCK, head_count, doubled)
    sliding = jnp.concatenate([framed[:, :-2], framed[:, 1:-1], framed[:, 2:]], axis=2)
    local_blocks = paired.reshape(windows, blocks_dev, BLOCK, head_count, doubled)
    owned_low = owned_hot.astype(jnp.bfloat16)
    offered = mixed_sum("wgb,wbthe->wgthe", owned_low, local_blocks)
    offered_queries = mixed_sum("wgb,wbqhd->wgqhd", owned_low, queries)
    global_kv, global_queries = (
        lax.psum(offered.astype(jnp.bfloat16), SEQ).astype(jnp.float32),
        lax.psum(offered_queries.astype(jnp.bfloat16), SEQ).astype(jnp.float32),
    )
    global_kv = global_kv.astype(jnp.bfloat16).reshape(windows, -1, head_count, doubled)
    global_queries = global_queries.astype(jnp.bfloat16).reshape(windows, -1, head_count, head_dim)
    outgoing = mixed_sum("wqcbh,wbthe->qwcte", sender.astype(jnp.bfloat16), local_blocks).astype(
        jnp.bfloat16
    )
    incoming = lax.all_to_all(outgoing, SEQ, split_axis=0, concat_axis=0, tiled=True)
    distant = mixed_sum("wspc,pwcte->wste", picker.astype(jnp.bfloat16), incoming).astype(
        jnp.bfloat16
    )
    pick_count = picker.shape[1] // (blocks_dev * head_count)
    distant = distant.reshape(windows, blocks_dev, head_count, pick_count, BLOCK, doubled)
    return (sliding, global_kv, distant, global_queries)


def combine_stats(earlier, later):
    top = jnp.maximum(earlier[0], later[0])
    return (top, earlier[1] * jnp.exp(earlier[0] - top) + later[1] * jnp.exp(later[0] - top))


def full_forward(global_queries, key_part, value_part, full_mask, head_dim):
    scores = mixed_sum("wqhd,wkhd->whqk", global_queries, key_part) * head_dim ** (-0.5)
    scores = jnp.where(full_mask, scores, masked)
    local_top = jnp.max(scores, axis=3, keepdims=True)
    local_sum = jnp.sum(
        jnp.where(full_mask, jnp.exp(scores - local_top), 0.0), axis=3, keepdims=True
    )
    row_top, row_sum = merged((local_top, local_sum), SEQ, combine_stats)
    full_probs = jnp.where(full_mask, jnp.exp(scores - row_top), 0.0) / row_sum
    partial_out = mixed_sum("whqk,wkhd->wqhd", full_probs.astype(jnp.bfloat16), value_part)
    full_out = lax.psum(partial_out.astype(jnp.bfloat16), SEQ).astype(jnp.float32)
    return (full_out, full_probs)


def attention_weights(queries, sliding, global_kv, distant, key_mask):
    head_dim = queries.shape[-1]
    windows, blocks_dev, _, head_count, _ = queries.shape
    near_scores = mixed_sum("wbqhd,wbkhd->wbhqk", queries, sliding[..., :head_dim])
    global_scores = mixed_sum("wbqhd,wkhd->wbhqk", queries, global_kv[..., :head_dim])
    far_scores = mixed_sum("wbqhd,wbhrkd->wbhqrk", queries, distant[..., :head_dim])
    far_scores = far_scores.reshape(windows, blocks_dev, head_count, BLOCK, -1)
    scores = jnp.concatenate([near_scores, global_scores, far_scores], axis=4) * head_dim ** (-0.5)
    scores = jnp.where(key_mask, scores, masked)
    row_top = jnp.max(scores, axis=4, keepdims=True)
    weight = jnp.exp(scores - row_top)
    return weight / jnp.sum(weight, axis=4, keepdims=True)


def split_keys(scores_like, sliding, global_kv, distant):
    near_keys = sliding.shape[2]
    global_keys = global_kv.shape[1]
    windows, blocks_dev, head_count, pick_count, _, _ = distant.shape
    near_part = scores_like[..., :near_keys]
    global_part = scores_like[..., near_keys : near_keys + global_keys]
    far_part = scores_like[..., near_keys + global_keys :].reshape(
        windows, blocks_dev, head_count, BLOCK, pick_count, BLOCK
    )
    return (near_part, global_part, far_part)


def attention_values(low_probs, sliding, global_kv, distant, head_dim):
    near_part, global_part, far_part = split_keys(low_probs, sliding, global_kv, distant)
    attended = mixed_sum("wbhqk,wbkhd->wbqhd", near_part, sliding[..., head_dim:])
    attended = attended + mixed_sum("wbhqk,wkhd->wbqhd", global_part, global_kv[..., head_dim:])
    return attended + mixed_sum("wbhqrk,wbhrkd->wbqhd", far_part, distant[..., head_dim:])


def layer_forward(hidden, weights, tables):
    row_weights, down_weights, vector_weights = weights
    sender, picker, owned_hot, key_mask, full_mask = tables
    model_width = row_weights.shape[0]
    windows, tokens, _ = hidden.shape
    blocks_dev = tokens // BLOCK
    head_dim = model_width // HEADS
    (
        gain_one,
        shift_one,
        bias_query,
        bias_value,
        bias_out,
        gain_two,
        shift_two,
        bias_down,
        bias_up,
    ) = split_vectors(vector_weights, model_width)
    normed = norm_rows(hidden, gain_one, shift_one).astype(jnp.bfloat16)
    projected = mixed_sum("wtd,de->wte", normed, row_weights[:, : 3 * model_width])
    projected = (
        projected + jnp.concatenate([bias_query, jnp.zeros_like(bias_query), bias_value])
    ).astype(jnp.bfloat16)
    queries = projected[..., :model_width].reshape(windows, blocks_dev, BLOCK, HEADS, head_dim)
    key_part = projected[..., model_width : 2 * model_width].reshape(
        windows, tokens, HEADS, head_dim
    )
    value_part = projected[..., 2 * model_width :].reshape(windows, tokens, HEADS, head_dim)
    paired = jnp.concatenate([key_part, value_part], axis=3)
    sliding, global_kv, distant, global_queries = fetch_blocks(
        paired, queries, sender, picker, owned_hot
    )
    probabilities = attention_weights(queries, sliding, global_kv, distant, key_mask)
    attended = attention_values(
        probabilities.astype(jnp.bfloat16), sliding, global_kv, distant, head_dim
    )
    full_out, full_probs = full_forward(global_queries, key_part, value_part, full_mask, head_dim)
    placed = exact_two(
        "wgb,wgqhd->wbqhd", owned_hot, full_out.reshape(windows, -1, BLOCK, HEADS, head_dim)
    )
    on_global = jnp.sum(owned_hot, axis=1)[:, :, None, None, None] > 0
    attended = jnp.where(on_global, placed, attended)
    mixed_low = attended.reshape(windows, tokens, model_width).astype(jnp.bfloat16)
    middle = (
        hidden
        + mixed_sum("wtd,de->wte", mixed_low, row_weights[:, 3 * model_width : 4 * model_width])
        + bias_out
    )
    normed_two = norm_rows(middle, gain_two, shift_two).astype(jnp.bfloat16)
    up_value = mixed_sum("wtd,df->wtf", normed_two, row_weights[:, 4 * model_width :]) + bias_up
    active = jax.nn.gelu(up_value, approximate=False).astype(jnp.bfloat16)
    output = middle + mixed_sum("wtf,fd->wtd", active, down_weights) + bias_down
    stored = (
        hidden,
        normed,
        queries,
        sliding,
        global_kv,
        distant,
        probabilities,
        mixed_low,
        middle,
        normed_two,
        up_value,
        active,
        key_part,
        value_part,
        global_queries,
        full_probs,
    )
    return (output, stored)


def return_blocks(near_back, global_back, far_back, query_part, sender, picker, owned_hot):
    windows, blocks_dev, _, head_count, doubled = near_back.shape
    first_third = near_back[:, :, :BLOCK]
    centre_third = near_back[:, :, BLOCK : 2 * BLOCK]
    last_third = near_back[:, :, 2 * BLOCK :]
    framed = jnp.pad(first_third, ((0, 0), (0, 2), (0, 0), (0, 0), (0, 0)))
    framed = framed + jnp.pad(centre_third, ((0, 0), (1, 1), (0, 0), (0, 0), (0, 0)))
    framed = framed + jnp.pad(last_third, ((0, 0), (2, 0), (0, 0), (0, 0), (0, 0)))
    own_grad = framed[:, 1:-1]
    for direction in (1, -1):
        rim_grad = framed[:, -1] if direction == 1 else framed[:, 0]
        arrived = from_behind(rim_grad.astype(jnp.bfloat16), SEQ, direction).astype(
            rim_grad.dtype
        )
        if direction == 1:
            own_grad = jnp.concatenate(
                [own_grad[:, :1] + arrived[:, None], own_grad[:, 1:]], axis=1
            )
        else:
            own_grad = jnp.concatenate(
                [own_grad[:, :-1], own_grad[:, -1:] + arrived[:, None]], axis=1
            )
    global_total, query_total = (
        lax.psum(
            global_back.reshape(windows, -1, BLOCK, head_count, doubled).astype(jnp.bfloat16), SEQ
        ).astype(jnp.float32),
        lax.psum(query_part.astype(jnp.bfloat16), SEQ).astype(jnp.float32),
    )
    own_grad = own_grad + exact_two("wgb,wgthe->wbthe", owned_hot, global_total)
    far_flat = far_back.reshape(windows, -1, BLOCK, doubled)
    returning = exact_two("wspc,wste->pwcte", picker, far_flat)
    arrived_far = lax.all_to_all(
        returning.astype(jnp.bfloat16), SEQ, split_axis=0, concat_axis=0, tiled=True
    ).astype(returning.dtype)
    own_grad = own_grad + exact_two("wqcbh,qwcte->wbthe", sender, arrived_far)
    return (own_grad.reshape(windows, blocks_dev * BLOCK, head_count, doubled), query_total)


def attention_back(
    grad_attended,
    queries,
    sliding,
    global_kv,
    distant,
    probabilities,
    key_part,
    value_part,
    global_queries,
    full_probs,
    sender,
    picker,
    owned_hot,
):
    head_dim = queries.shape[-1]
    score_scale = head_dim ** (-0.5)
    windows, blocks_dev, _, head_count, _ = queries.shape
    on_global = jnp.sum(owned_hot, axis=1)[:, :, None, None, None] > 0
    selected = mixed_sum("wgb,wbqhd->wgqhd", owned_hot.astype(jnp.bfloat16), grad_attended)
    rows_grad = lax.psum(selected.astype(jnp.bfloat16), SEQ).reshape(
        windows, -1, head_count, head_dim
    )
    grad_attended = jnp.where(on_global, jnp.zeros_like(grad_attended), grad_attended)
    low_probs = probabilities.astype(jnp.bfloat16)
    near_grad = mixed_sum("wbqhd,wbkhd->wbhqk", grad_attended, sliding[..., head_dim:])
    global_grad = mixed_sum("wbqhd,wkhd->wbhqk", grad_attended, global_kv[..., head_dim:])
    far_grad = mixed_sum("wbqhd,wbhrkd->wbhqrk", grad_attended, distant[..., head_dim:])
    far_grad = far_grad.reshape(windows, blocks_dev, head_count, BLOCK, -1)
    grad_probs = jnp.concatenate([near_grad, global_grad, far_grad], axis=4)
    grad_scores = probabilities * (
        grad_probs - jnp.sum(probabilities * grad_probs, axis=4, keepdims=True)
    )
    grad_scores = grad_scores.astype(jnp.bfloat16)
    near_split, global_split, far_split = split_keys(grad_scores, sliding, global_kv, distant)
    near_probs, global_probs, far_probs = split_keys(low_probs, sliding, global_kv, distant)
    grad_query = mixed_sum("wbhqk,wbkhd->wbqhd", near_split, sliding[..., :head_dim])
    grad_query = grad_query + mixed_sum(
        "wbhqk,wkhd->wbqhd", global_split, global_kv[..., :head_dim]
    )
    grad_query = (
        grad_query + mixed_sum("wbhqrk,wbhrkd->wbqhd", far_split, distant[..., :head_dim])
    ) * score_scale
    near_back = jnp.concatenate(
        [
            mixed_sum("wbhqk,wbqhd->wbkhd", near_split, queries) * score_scale,
            mixed_sum("wbhqk,wbqhd->wbkhd", near_probs, grad_attended),
        ],
        axis=4,
    )
    global_back = jnp.concatenate(
        [
            mixed_sum("wbhqk,wbqhd->wkhd", global_split, queries) * score_scale,
            mixed_sum("wbhqk,wbqhd->wkhd", global_probs, grad_attended),
        ],
        axis=3,
    )
    far_back = jnp.concatenate(
        [
            mixed_sum("wbhqrk,wbqhd->wbhrkd", far_split, queries) * score_scale,
            mixed_sum("wbhqrk,wbqhd->wbhrkd", far_probs, grad_attended),
        ],
        axis=5,
    )
    full_grad_probs = mixed_sum("wqhd,wkhd->whqk", rows_grad, value_part)
    partial_dot = jnp.sum(full_probs * full_grad_probs, axis=3, keepdims=True)
    row_dot = lax.psum(partial_dot, SEQ)
    full_grad_scores = (full_probs * (full_grad_probs - row_dot)).astype(jnp.bfloat16)
    query_part = mixed_sum("whqk,wkhd->wqhd", full_grad_scores, key_part) * score_scale
    full_key_grad = mixed_sum("whqk,wqhd->wkhd", full_grad_scores, global_queries) * score_scale
    full_value_grad = mixed_sum("whqk,wqhd->wkhd", full_probs.astype(jnp.bfloat16), rows_grad)
    grad_paired, query_total = return_blocks(
        near_back, global_back, far_back, query_part, sender, picker, owned_hot
    )
    grad_query = grad_query + exact_two(
        "wgb,wgqhd->wbqhd", owned_hot, query_total.reshape(windows, -1, BLOCK, head_count, head_dim)
    )
    grad_paired = grad_paired + jnp.concatenate([full_key_grad, full_value_grad], axis=3)
    return (grad_query, grad_paired)


def layer_backward(stored, grad_output, weights, tables):
    row_weights, down_weights, vector_weights = weights
    sender, picker, owned_hot, key_mask, full_mask = tables
    (
        hidden,
        normed,
        queries,
        sliding,
        global_kv,
        distant,
        probabilities,
        mixed_low,
        middle,
        normed_two,
        up_value,
        active,
        key_part,
        value_part,
        global_queries,
        full_probs,
    ) = stored
    model_width = row_weights.shape[0]
    windows, tokens, _ = hidden.shape
    blocks_dev = tokens // BLOCK
    head_dim = model_width // HEADS
    (
        gain_one,
        shift_one,
        bias_query,
        bias_value,
        bias_out,
        gain_two,
        shift_two,
        bias_down,
        bias_up,
    ) = split_vectors(vector_weights, model_width)
    grad_ffn = grad_output.astype(jnp.bfloat16)
    grad_bias_down = jnp.sum(grad_ffn.astype(jnp.float32), axis=(0, 1))
    grad_down = mixed_sum("wtf,wtd->fd", active, grad_ffn)
    grad_active = mixed_sum("wtd,fd->wtf", grad_ffn, down_weights)
    gelu_pull = jax.vjp(partial(jax.nn.gelu, approximate=False), up_value)[1]
    grad_up = gelu_pull(grad_active)[0].astype(jnp.bfloat16)
    grad_bias_up = jnp.sum(grad_up.astype(jnp.float32), axis=(0, 1))
    grad_in = mixed_sum("wtd,wtf->df", normed_two, grad_up)
    grad_normed_two = mixed_sum("wtf,df->wtd", grad_up, row_weights[:, 4 * model_width :])
    norm_pull_two = jax.vjp(norm_rows, middle, gain_two, shift_two)[1]
    grad_middle_norm, grad_gain_two, grad_shift_two = norm_pull_two(grad_normed_two)
    grad_middle = grad_output + grad_middle_norm
    grad_branch = grad_middle.astype(jnp.bfloat16)
    grad_bias_out = jnp.sum(grad_branch.astype(jnp.float32), axis=(0, 1))
    grad_out_weight = mixed_sum("wtd,wte->de", mixed_low, grad_branch)
    grad_attended = mixed_sum(
        "wte,de->wtd", grad_branch, row_weights[:, 3 * model_width : 4 * model_width]
    ).astype(jnp.bfloat16)
    grad_attended = grad_attended.reshape(windows, blocks_dev, BLOCK, HEADS, head_dim)
    grad_query, grad_paired = attention_back(
        grad_attended,
        queries,
        sliding,
        global_kv,
        distant,
        probabilities,
        key_part,
        value_part,
        global_queries,
        full_probs,
        sender,
        picker,
        owned_hot,
    )
    grad_projected = jnp.concatenate(
        [
            grad_query.reshape(windows, tokens, model_width),
            grad_paired[..., :head_dim].reshape(windows, tokens, model_width),
            grad_paired[..., head_dim:].reshape(windows, tokens, model_width),
        ],
        axis=2,
    ).astype(jnp.bfloat16)
    summed = jnp.sum(grad_projected.astype(jnp.float32), axis=(0, 1))
    grad_bias_query = summed[:model_width]
    grad_bias_value = summed[2 * model_width :]
    grad_projection = mixed_sum("wtd,wte->de", normed, grad_projected)
    grad_normed = mixed_sum("wte,de->wtd", grad_projected, row_weights[:, : 3 * model_width])
    norm_pull_one = jax.vjp(norm_rows, hidden, gain_one, shift_one)[1]
    grad_hidden_norm, grad_gain_one, grad_shift_one = norm_pull_one(grad_normed)
    grad_hidden = grad_middle + grad_hidden_norm
    grad_rows = jnp.concatenate([grad_projection, grad_out_weight, grad_in], axis=1)
    grad_vectors = jnp.concatenate(
        [
            grad_gain_one,
            grad_shift_one,
            grad_bias_query,
            grad_bias_value,
            grad_bias_out,
            grad_gain_two,
            grad_shift_two,
            grad_bias_down,
            grad_bias_up,
        ]
    )
    return (grad_hidden, (grad_rows, grad_down, grad_vectors))


def adam_update(master, first_old, second_old, gradient, step_rate, decay_rate):
    first_new = 0.5 * first_old + 0.5 * gradient
    second_new = 0.5 * second_old + 0.5 * gradient * gradient
    first_hat = first_new / (1.0 - 0.5**STEP)
    second_hat = second_new / (1.0 - 0.5**STEP)
    master_new = master - step_rate * (
        first_hat / (jnp.sqrt(second_hat) + 1e-08) + decay_rate * master
    )
    return (master_new, first_new, second_new)


def general_shards(
    block_input,
    cotangent,
    random_ids,
    segment_ids,
    global_ids,
    w_rows,
    w_rows_first,
    w_rows_second,
    w_down,
    w_down_first,
    w_down_second,
    vectors,
    vectors_first,
    vectors_second,
):
    section_index = lax.axis_index(SECTION)
    seq_place = lax.axis_index(SEQ)
    groups = lax.axis_size(SEQ)
    row_weights, down_weights, vector_low = (
        lax.all_gather(w_rows[0].astype(jnp.bfloat16), (DP, SEQ), axis=1, tiled=True),
        lax.all_gather(w_down[0].astype(jnp.bfloat16), (DP, SEQ), axis=0, tiled=True),
        lax.all_gather(vectors[0].astype(jnp.bfloat16), (DP, SEQ), axis=0, tiled=True),
    )
    weights = (row_weights, down_weights, vector_low.astype(jnp.float32))
    micro_count, windows, tokens, model_width = block_input.shape
    received = jnp.zeros((windows, tokens, model_width), jnp.bfloat16)
    results = jnp.zeros(block_input.shape, jnp.float32)
    full_totals = (
        jnp.zeros(row_weights.shape, jnp.float32),
        jnp.zeros(down_weights.shape, jnp.float32),
        jnp.zeros(vector_low.shape, jnp.float32),
    )

    def tick(tick_index, carry):
        received, results, full_totals = carry
        forward_mb = jnp.clip(tick_index - section_index, 0, micro_count - 1)
        behind_raw = tick_index - 2 + section_index
        behind = jnp.clip(behind_raw, 0, micro_count - 1)
        live_mask = ((behind_raw >= 0) & (behind_raw < micro_count)).astype(jnp.float32)
        tables_forward = route_tables(
            lax.dynamic_index_in_dim(random_ids, forward_mb, 0, keepdims=False),
            lax.dynamic_index_in_dim(segment_ids, forward_mb, 0, keepdims=False),
            lax.dynamic_index_in_dim(global_ids, forward_mb, 0, keepdims=False),
            seq_place,
            groups,
        )
        tables_behind = route_tables(
            lax.dynamic_index_in_dim(random_ids, behind, 0, keepdims=False),
            lax.dynamic_index_in_dim(segment_ids, behind, 0, keepdims=False),
            lax.dynamic_index_in_dim(global_ids, behind, 0, keepdims=False),
            seq_place,
            groups,
        )
        incoming_values = received.astype(jnp.float32)
        first_input = lax.dynamic_index_in_dim(block_input, forward_mb, 0, keepdims=False).astype(
            jnp.float32
        )
        forward_input = jnp.where(section_index == 0, first_input, incoming_values)
        forward_output = layer_forward(forward_input, weights, tables_forward)[0]
        back_source = lax.dynamic_index_in_dim(block_input, behind, 0, keepdims=False).astype(
            jnp.float32
        )
        back_input = jnp.where(section_index == 0, back_source, incoming_values)
        given_grad = lax.dynamic_index_in_dim(cotangent, behind, 0, keepdims=False).astype(
            jnp.float32
        )
        back_grad = jnp.where(section_index == 0, incoming_values, given_grad) * live_mask
        stored = layer_forward(back_input, weights, tables_behind)[1]
        grad_input, gradients = layer_backward(stored, back_grad, weights, tables_behind)
        outgoing = jnp.where(section_index == 0, forward_output, grad_input).astype(jnp.bfloat16)
        finished = jnp.where(section_index == 0, grad_input, forward_output)
        updated = lax.dynamic_update_index_in_dim(results, finished, behind, 0)
        results = jnp.where(live_mask > 0, updated, results)
        full_totals = tuple(
            (total_part + grad_part for total_part, grad_part in zip(full_totals, gradients))
        )
        return (partner(outgoing, SECTION, 0), results, full_totals)

    received, results, full_totals = lax.fori_loop(
        0, micro_count + 2, tick, (received, results, full_totals)
    )
    shard_totals = (
        lax.psum_scatter(full_totals[0], (DP, SEQ), scatter_dimension=1, tiled=True),
        lax.psum_scatter(full_totals[1], (DP, SEQ), scatter_dimension=0, tiled=True),
        lax.psum_scatter(full_totals[2], (DP, SEQ), scatter_dimension=0, tiled=True),
    )
    new_rows, new_rows_first, new_rows_second = adam_update(
        w_rows[0], w_rows_first[0], w_rows_second[0], shard_totals[0], rate_matrix, decay_matrix
    )
    new_down, new_down_first, new_down_second = adam_update(
        w_down[0], w_down_first[0], w_down_second[0], shard_totals[1], rate_matrix, decay_matrix
    )
    new_vectors, new_vectors_first, new_vectors_second = adam_update(
        vectors[0], vectors_first[0], vectors_second[0], shard_totals[2], rate_vector, 0.0
    )
    return (
        results[None],
        new_rows[None],
        new_rows_first[None],
        new_rows_second[None],
        new_down[None],
        new_down_first[None],
        new_down_second[None],
        new_vectors[None],
        new_vectors_first[None],
        new_vectors_second[None],
    )


LOW = jnp.bfloat16
LOG_HIGH = [float(np.log(c).astype(ml_dtypes.bfloat16)) for c in (1.0, 2.0, 3.0)]
LOG_LOW = [float(np.log(c)) - high for c, high in zip((1.0, 2.0, 3.0), LOG_HIGH)]
CHUNK = 256
VMEM_BYTES = 60 * 1024 * 1024


def dot_rows(left, right):
    return lax.dot_general(left, right, (((1,), (1,)), ((), ())), preferred_element_type=jnp.float32)


def dot_plain(left, right):
    return lax.dot_general(left, right, (((1,), (0,)), ((), ())), preferred_element_type=jnp.float32)


def dot_tokens(left, right):
    return lax.dot_general(left, right, (((0,), (0,)), ((), ())), preferred_element_type=jnp.float32)


def swap(value):
    return lax.ppermute(value, SECTION, [(0, 1), (1, 0)])


def normalized(values_in):
    row_mean = jnp.mean(values_in, axis=-1, keepdims=True)
    centred = values_in - row_mean
    spread = jnp.mean(centred * centred, axis=-1, keepdims=True)
    scale = lax.rsqrt(spread + epsilon)
    return centred * scale, scale


class Shares:
    def __init__(self, width, columns, depth, vector_len):
        self.width = width
        self.columns = columns
        self.depth = depth
        self.vector_len = vector_len
        self.half = columns // 2
        self.per = width // columns
        self.groups = columns // depth

    def unpack(self, gathered, core):
        rows, down, vec = gathered
        vec = vec.reshape(-1, TAIL, self.width)[:, 0, : self.vector_len].reshape(-1)
        pieces = split_vectors(vec.astype(jnp.float32), self.width)
        for index in (2, 3):
            pieces[index] = lax.dynamic_index_in_dim(
                pieces[index].reshape(self.per, 2, self.half), core, 1, keepdims=False
            ).reshape(-1)
        pieces[8] = lax.dynamic_index_in_dim(
            pieces[8].reshape(-1, 2, self.depth // 2), core, 1, keepdims=False
        ).reshape(-1)
        nothing = jnp.zeros_like(pieces[2])
        proj = [pieces[2], nothing, pieces[3], nothing]
        order = [pieces[index] for index in (0, 1, 4, 5, 6, 7)] + proj + [pieces[8]]
        return (
            (rows.reshape(-1, self.width), down.reshape(-1, self.width)),
            jnp.concatenate(order).reshape(-1, self.width),
        )

    def vector_shards(self, vector_grads, core):
        half, per = self.half, self.per
        hot = (jnp.arange(2) == core).astype(jnp.float32)
        spread = list(vector_grads)
        for index in (2, 3):
            spread[index] = (
                spread[index].reshape(per, 1, half) * hot[None, :, None]
            ).reshape(-1)
        spread[8] = (spread[8].reshape(-1, 1, self.depth // 2) * hot[None, :, None]).reshape(-1)
        for index in (0, 1, 4, 5, 6, 7):
            spread[index] = spread[index] * hot[0]
        vec = jnp.concatenate(spread).reshape(-1, 1, self.vector_len)
        vec = jnp.pad(vec, ((0, 0), (0, TAIL - 1), (0, self.width - self.vector_len)))
        return vec.astype(LOW).reshape(2, 2, 4, TAIL, self.width)


MESH = pl.DeviceIdType.MESH
PIECE = 48
TAIL = 16


def prepare_kernel(shares, rows_ref, down_ref, vector_ref, rows_out, down_out, vector_out):
    core = lax.axis_index(SECTION)
    offset = lax.axis_index((DP, SEQ)) * shares.columns
    half, per, width, depth = shares.half, shares.per, shares.width, shares.depth // 2
    is_inner = (offset >= 3 * width) & (offset < 4 * width)
    is_hidden = offset >= 4 * width

    @pl.when(is_inner)
    def _():
        for which in range(2):
            side = core if which == 0 else 1 - core
            held = [rows_ref[pl.ds((2 * j + side) * half, half), :] for j in range(per)]
            turned = jnp.transpose(jnp.concatenate(held, axis=0))
            rows_out[which] = jnp.concatenate([turned[:half], turned[half:]], axis=1).astype(LOW)

    @pl.when(jnp.logical_not(is_inner))
    def _():
        turned = jnp.transpose(rows_ref[...]).astype(LOW)
        plain = [turned[:half], turned[half:]]
        hidden = [
            jnp.concatenate(
                [turned[(2 * j + side) * depth :][:depth] for j in range(shares.groups)], axis=0
            )
            for side in range(2)
        ]
        halves = [jnp.where(is_hidden, b, a) for a, b in zip(plain, hidden)]
        rows_out[0] = jnp.where(core == 0, halves[0], halves[1])
        rows_out[1] = jnp.where(core == 0, halves[1], halves[0])

    down = down_ref[...].astype(LOW)
    down_out[0] = jnp.where(core == 0, down[:depth], down[depth:])
    down_out[1] = jnp.where(core == 0, down[depth:], down[:depth])
    vector_out[...] = jnp.zeros_like(vector_out)
    vector_out[0:1, : shares.vector_len] = vector_ref[...].astype(LOW)


def prepare(shares, rows, down, vector):
    return pl.pallas_call(
        partial(prepare_kernel, shares),
        out_shape=[
            jax.ShapeDtypeStruct((2, shares.half, shares.width), LOW),
            jax.ShapeDtypeStruct((2, shares.depth // 2, shares.width), LOW),
            jax.ShapeDtypeStruct((TAIL, shares.width), LOW),
        ],
        compiler_params=pltpu.CompilerParams(vmem_limit_bytes=VMEM_BYTES),
    )(rows, down, vector)


class Place:
    def __init__(self):
        self.core = lax.axis_index(SECTION)
        self.dp = lax.axis_index(DP)
        self.z = lax.axis_index(SEQ)
        self.y, self.x = self.dp // 2, self.dp % 2
        self.high, self.low = self.z // 2, self.z % 2
        self.inner = self.high + self.low == 1
        self.outer = self.high + self.low != 1
        self.partner = {SECTION: 1 - self.core}
        self.along_x = {DP: 2 * self.y + 1 - self.x}
        self.along_y = {DP: 2 * (1 - self.y) + self.x}
        self.across = {SEQ: 3 - self.z}
        self.beside = {SEQ: 2 * self.high + 1 - self.low}
        self.others = [{SEQ: (self.z + by) % 4} for by in (1, 2, 3)]
        self.own = pl.ds(self.z, 1)
        self.next = pl.ds(2 * self.high + 1 - self.low, 1)
        self.near = pl.ds(2 * self.high, 2)
        self.far = pl.ds(2 * (1 - self.high), 2)

    def greet(self):
        barrier = pltpu.get_barrier_semaphore()
        everyone = [self.partner, self.along_x, self.along_y] + self.others
        for device in everyone:
            pl.semaphore_signal(barrier, inc=1, device_id=device, device_id_type=MESH)
        pl.semaphore_wait(barrier, len(everyone))


def remote(src, dst, sems, spots, device):
    return pltpu.make_async_remote_copy(
        src_ref=src,
        dst_ref=dst,
        send_sem=sems[0].at[spots[0]],
        recv_sem=sems[1].at[spots[1]],
        device_id=device,
        device_id_type=MESH,
    )


def chunk_pairs(shares):
    pairs = []
    for array, length in ((0, shares.half), (1, shares.depth // 2)):
        for start in range(0, length, 2 * PIECE):
            pairs.append([(array, start, PIECE, 0), (array, start + PIECE, PIECE, 1)])
    pairs[0] += [(2, 0, TAIL, 0), (3, 0, TAIL, 0)]
    return pairs


def gather_kernel(shares, *refs):
    ins, refs = refs[:4], refs[4:]
    (x_in, cot_in), refs = refs[:2], refs[2:]
    outs, refs = refs[:4], refs[4:]
    (x_out, cot_out), refs = refs[:2], refs[2:]
    local, z_send, z_recv, send, recv = refs
    here = Place()
    core, y, x, z = here.core, here.y, here.x, here.z
    half = x_in.shape[2] // 2
    own = [
        pltpu.make_async_copy(src, dst.at[y, x, z], local.at[index])
        for index, (src, dst) in enumerate(zip(ins, outs))
    ]
    for copy in own:
        copy.start()
    here.greet()

    def slices(source, target, base):
        mine = pl.ds(pl.multiple_of(core * half, half), half)
        sems = (z_send, z_recv)
        own = pltpu.make_async_copy(
            source.at[z, 0, mine], target.at[z, core], local.at[4 + base // 4]
        )
        sends, arrivals = [], []
        for by in (1, 2, 3):
            spots = (base + by - 1, base + by - 1)
            device = here.others[by - 1]
            sends.append(
                remote(source.at[(z + by) % 4, 0, mine], target.at[z, core], sems, spots, device)
            )
            arrivals.append(
                remote(
                    source.at[z, 0, mine], target.at[(z + 4 - by) % 4, core], sems, spots, device
                )
            )
        spots = (base + 3, base + 3)
        forward = remote(target.at[:, core], target.at[:, core], sems, spots, here.partner)
        arrived = remote(target.at[:, 1 - core], target.at[:, 1 - core], sems, spots, here.partner)
        return own, sends, arrivals, forward, arrived

    x_moves = slices(x_in, x_out, 0)
    cot_moves = slices(cot_in, cot_out, 4)

    def open_slices(moves):
        moves[0].start()
        for copy in moves[1]:
            copy.start()

    def pass_slices(moves):
        moves[0].wait()
        for copy in moves[2]:
            copy.wait_recv()
        moves[3].start()

    def close_slices(moves):
        for copy in moves[1]:
            copy.wait_send()
        moves[3].wait_send()
        moves[4].wait_recv()

    numbers, pairs = {}, []
    for pair in chunk_pairs(shares):
        entry = []
        for array, start, length, order in pair:
            ref = outs[array]
            rows = pl.ds(start, length)
            number = len(numbers)
            sems = (send, recv)

            def part(which):
                return ref.at[y, x, which, rows]

            def copy(piece, spots, device):
                return remote(piece, piece, sems, ((number, spots[0]), (number, spots[1])), device)

            steps = {
                "z": copy(part(here.own), (0, 0), here.beside),
                "across": copy(part(here.near), (1, 1), here.across),
                "on": copy(part(here.far), (4, 1), here.beside),
            }
            arrive = [
                copy(part(here.next), (0, 0), here.beside),
                copy(part(here.far), (1, 1), here.across),
            ]
            if order == 0:
                steps["one"] = copy(ref.at[y, x, :, rows], (2, 2), here.along_y)
                steps["two"] = copy(ref.at[:, x, :, rows], (3, 3), here.along_x)
                arrive.append(copy(ref.at[1 - y, x, :, rows], (2, 2), here.along_y))
                arrive.append(copy(ref.at[:, 1 - x, :, rows], (3, 3), here.along_x))
            else:
                steps["one"] = copy(ref.at[y, x, :, rows], (2, 2), here.along_x)
                steps["two"] = copy(ref.at[y, :, :, rows], (3, 3), here.along_y)
                arrive.append(copy(ref.at[y, 1 - x, :, rows], (2, 2), here.along_x))
                arrive.append(copy(ref.at[1 - y, :, :, rows], (3, 3), here.along_y))
            numbers[number] = (steps, arrive)
            entry.append(number)
        pairs.append(entry)

    def issue(name, entry):
        after = {"z": None, "across": 0, "on": 1, "one": None, "two": 2}[name]

        def start():
            for number in entry:
                steps, arrive = numbers[number]
                if after is not None:
                    arrive[after].wait_recv()
                steps[name].start()

        if name in ("across", "on"):
            pl.when(here.inner)(start)
        else:
            start()

    def arrived(entry, index, where):
        def wait():
            for number in entry:
                numbers[number][1][index].wait_recv()

        pl.when(where)(wait)

    for copy in own:
        copy.wait()
    for entry in pairs:
        issue("z", entry)
    for entry in pairs:
        issue("across", entry)
        arrived(entry, 0, here.outer)
    for index, entry in enumerate(pairs):
        issue("on", entry)
        if index == len(pairs) - 1:
            open_slices(x_moves)
        arrived(entry, 1, here.outer)
        issue("one", entry)
    issue("two", pairs[0])
    open_slices(cot_moves)
    for entry in pairs[1:]:
        issue("two", entry)
    pass_slices(x_moves)
    pass_slices(cot_moves)
    for entry in pairs:
        arrived(entry, 3, core >= 0)
    for steps, _ in numbers.values():
        for name in ("z", "one", "two"):
            steps[name].wait_send()

    @pl.when(here.inner)
    def _():
        for steps, _ in numbers.values():
            steps["across"].wait_send()
            steps["on"].wait_send()

    close_slices(x_moves)
    close_slices(cot_moves)


def gather(shares, first_layer, block_input, cotangent):
    micro, _, tokens, width = block_input.shape
    chunks = sum(len(pair) for pair in chunk_pairs(shares))
    lengths = (shares.half, shares.depth // 2, TAIL, TAIL)
    arrays = [jax.ShapeDtypeStruct((2, 2, 4, rows, width), LOW) for rows in lengths]
    window = jax.ShapeDtypeStruct((micro, 2, tokens // 2, width), LOW)
    anywhere = pl.BlockSpec(memory_space=pl.ANY)
    results = pl.pallas_call(
        partial(gather_kernel, shares),
        in_specs=[pl.BlockSpec(memory_space=pltpu.VMEM)] * 4 + [anywhere] * 2,
        out_specs=[anywhere] * 6,
        out_shape=arrays + [window, window],
        scratch_shapes=[
            pltpu.SemaphoreType.DMA((6,)),
            pltpu.SemaphoreType.DMA((8,)),
            pltpu.SemaphoreType.DMA((8,)),
            pltpu.SemaphoreType.DMA((chunks, 5)),
            pltpu.SemaphoreType.DMA((chunks, 4)),
        ],
        compiler_params=pltpu.CompilerParams(
            collective_id=0, has_side_effects=True, vmem_limit_bytes=VMEM_BYTES
        ),
        cost_estimate=pl.CostEstimate(
            flops=10**11, bytes_accessed=3 * 10**8, transcendentals=0
        ),
    )(*first_layer, block_input, cotangent)
    return results[:3], results[3], results[4], results[5]


def scatter_kernel(shares, *refs):
    arrays, refs = refs[:4], refs[4:]
    (dx_ref, final_ref, halves, slices), refs = refs[:4], refs[4:]
    work, refs = refs[:4], refs[4:]
    (got_one, got_two, got_far, got_across, got_near, total), refs = refs[:6], refs[6:]
    load, local, swap_send, swap_recv, z_send, z_recv, send, recv = refs
    here = Place()
    core, y, x, z = here.core, here.y, here.x, here.z
    bases = (0, shares.half, shares.half + shares.depth // 2)
    bases += (bases[2] + TAIL,)
    loads = [
        pltpu.make_async_copy(src, dst, load.at[index])
        for index, (src, dst) in enumerate(zip(arrays, work))
    ]
    for copy in loads:
        copy.start()
    here.greet()
    pairs, count = [], 0
    for pair in chunk_pairs(shares):
        pairs.append([(count + index, *chunk) for index, chunk in enumerate(pair)])
        count += len(pair)

    def pieces(chunk):
        number, array, start, length, order = chunk
        ref = work[array]
        rows = pl.ds(start, length)
        room = pl.ds(0, length)
        sems = (send, recv)
        keeps, slots, copies = [], [], []

        def part(which):
            return ref.at[y, x, which, rows]

        def add(src, slot, device, keep):
            spots = (number, len(copies))
            copies.append(remote(src, slot, sems, (spots, spots), device))
            slots.append(slot)
            keeps.append(keep)

        one, two = got_one.at[number, :, :, room], got_two.at[number, :, room]
        if order == 0:
            add(ref.at[:, 1 - x, :, rows], one, here.along_x, ref.at[:, x, :, rows])
            add(ref.at[1 - y, x, :, rows], two, here.along_y, ref.at[y, x, :, rows])
        else:
            add(ref.at[1 - y, :, :, rows], one, here.along_y, ref.at[y, :, :, rows])
            add(ref.at[y, 1 - x, :, rows], two, here.along_x, ref.at[y, x, :, rows])
        add(part(here.far), got_far.at[number, :, room], here.beside, part(here.far))
        add(part(here.far), got_across.at[number, :, room], here.across, part(here.near))
        add(part(here.next), got_near.at[number, :, room], here.beside, part(here.own))
        return copies, keeps, slots

    built = [pieces(chunk) for pair in pairs for chunk in pair]
    loaded = set()

    def land(number, phase):
        copies, keeps, slots = built[number]
        copies[phase].wait_recv()
        keep, slot = keeps[phase], slots[phase]
        keep[...] = keep[...] + slot[...]

    def run(chunk, phase):
        number, array, start, length, _ = chunk
        copies, keeps, slots = built[number]
        if array not in loaded:
            loaded.add(array)
            loads[array].wait()
        if phase < 2:
            if phase:
                land(number, 0)
            copies[phase].start()
        elif phase == 2:
            land(number, 1)

            @pl.when(here.outer)
            def _():
                copies[2].start()
                copies[4].start()

        elif phase < 5:

            @pl.when(here.inner)
            def _():
                land(number, phase - 1)
                copies[phase].start()

        else:
            copies[4].wait_recv()
            spot = pl.ds(bases[array] + start, length)
            total[spot, :] = (keeps[4][...] + slots[4][...])[0]

    def step(index, phase):
        for chunk in pairs[index]:
            run(chunk, phase)

    step(0, 0)
    step(1, 0)
    for section, source in ((0, dx_ref), (1, final_ref)):

        @pl.when(core == section)
        def _():
            pltpu.make_async_copy(source.at[z], slices.at[z], local.at[0]).start()
            for by in (1, 2, 3):
                remote(
                    source.at[(z + by) % 4],
                    slices.at[z],
                    (z_send, z_recv),
                    (by - 1, by - 1),
                    here.others[by - 1],
                ).start()

    for index, phase in (
        (0, 1),
        (2, 0),
        (1, 1),
        (0, 2),
        (2, 1),
        (0, 3),
        (1, 2),
        (0, 4),
        (1, 3),
        (2, 2),
        (1, 4),
        (2, 3),
        (0, 5),
        (2, 4),
        (1, 5),
        (2, 5),
    ):
        step(index, phase)

    for copies, _, _ in built:
        for index in (0, 1, 4):
            copies[index].wait_send()
    for section, index in ((here.outer, 2), (here.inner, 3)):

        @pl.when(section)
        def _():
            for copies, _, _ in built:
                copies[index].wait_send()

    across = remote(total, halves.at[core], (swap_send, swap_recv), (0, 0), here.partner)
    across.start()
    own = pltpu.make_async_copy(total, halves.at[core], local.at[1])
    own.start()
    own.wait()
    across.wait_send()
    remote(total, halves.at[1 - core], (swap_send, swap_recv), (0, 0), here.partner).wait_recv()
    pltpu.make_async_copy(dx_ref.at[z], slices.at[z], local.at[0]).wait()
    for by in (1, 2, 3):
        copy = remote(
            dx_ref.at[z],
            slices.at[(z + 4 - by) % 4],
            (z_send, z_recv),
            (by - 1, by - 1),
            here.others[by - 1],
        )
        copy.wait_send()
        copy.wait_recv()


def scatter(shares, arrays, grad, final):
    micro, tokens, width = grad.shape
    lengths = (shares.half, shares.depth // 2, TAIL, TAIL)
    chunks = sum(len(pair) for pair in chunk_pairs(shares))
    rows = sum(lengths)
    anywhere = pl.BlockSpec(memory_space=pl.ANY)
    return pl.pallas_call(
        partial(scatter_kernel, shares),
        in_specs=[anywhere] * 6,
        out_specs=[anywhere] * 2,
        out_shape=[
            jax.ShapeDtypeStruct((2, rows, width), LOW),
            jax.ShapeDtypeStruct((micro, tokens, width), LOW),
        ],
        scratch_shapes=[pltpu.VMEM((2, 2, 4, length, width), LOW) for length in lengths]
        + [
            pltpu.VMEM((chunks, 2, 4, PIECE, width), LOW),
            pltpu.VMEM((chunks, 4, PIECE, width), LOW),
            pltpu.VMEM((chunks, 2, PIECE, width), LOW),
            pltpu.VMEM((chunks, 2, PIECE, width), LOW),
            pltpu.VMEM((chunks, 1, PIECE, width), LOW),
            pltpu.VMEM((rows, width), LOW),
            pltpu.SemaphoreType.DMA((4,)),
            pltpu.SemaphoreType.DMA((2,)),
            pltpu.SemaphoreType.DMA((1,)),
            pltpu.SemaphoreType.DMA((1,)),
            pltpu.SemaphoreType.DMA((3,)),
            pltpu.SemaphoreType.DMA((3,)),
            pltpu.SemaphoreType.DMA((chunks, 5)),
            pltpu.SemaphoreType.DMA((chunks, 5)),
        ],
        compiler_params=pltpu.CompilerParams(
            collective_id=1, has_side_effects=True, vmem_limit_bytes=VMEM_BYTES
        ),
        cost_estimate=pl.CostEstimate(
            flops=10**11, bytes_accessed=3 * 10**8, transcendentals=0
        ),
    )(*arrays, grad, final)


def update_kernel(shares, *refs):
    (halves_ref, rows_ref, rows_recv, down_ref, down_recv, slices_ref), refs = refs[:6], refs[6:]
    old, new, result_ref, turned = refs[:9], refs[9:18], refs[18], refs[19]
    core = lax.axis_index(SECTION)
    offset = lax.axis_index((DP, SEQ)) * shares.columns
    half, per, width, depth = shares.half, shares.per, shares.width, shares.depth // 2
    is_inner = (offset >= 3 * width) & (offset < 4 * width)
    is_hidden = offset >= 4 * width
    result_ref[...] = slices_ref[...].astype(jnp.float32)

    def both_halves(rows, recv, own):
        return [
            jnp.where(core == 0, halves_ref[0, rows, :], recv[...]).astype(jnp.float32),
            jnp.where(core == 0, halves_ref[1, rows, :], own[...]).astype(jnp.float32),
        ]

    pair = both_halves(slice(0, half), rows_recv, rows_ref)

    @pl.when(is_inner)
    def _():
        for side in range(2):
            piece = pair[side]
            wide = per * half
            back = jnp.transpose(jnp.concatenate([piece[:, :wide], piece[:, wide:]], axis=0))
            for j in range(per):
                turned[(2 * j + side) * half : (2 * j + side + 1) * half, :] = back[
                    j * half : (j + 1) * half
                ]

    @pl.when(jnp.logical_not(is_inner))
    def _():
        plain = jnp.concatenate(pair, axis=0)
        hidden = jnp.concatenate(
            [pair[side][j * depth :][:depth] for j in range(shares.groups) for side in range(2)],
            axis=0,
        )
        turned[...] = jnp.transpose(jnp.where(is_hidden, hidden, plain))

    def store(first, gradient, rate, decay):
        results = adam_update(*[ref[...] for ref in old[first : first + 3]], gradient, rate, decay)
        for ref, result in zip(new[first : first + 3], results):
            ref[...] = result

    store(0, turned[...], rate_matrix, decay_matrix)
    down = both_halves(slice(half, half + depth), down_recv, down_ref)
    store(3, jnp.concatenate(down, axis=0), rate_matrix, decay_matrix)
    tails = [
        halves_ref[side, half + depth :, :].astype(jnp.float32) for side in range(2)
    ]
    tail = tails[0] + tails[1]
    tail = jnp.where(core == 0, tail[0:1], tail[TAIL : TAIL + 1])
    store(6, tail[:, : shares.vector_len], rate_vector, 0.0)


def update(shares, halves, reduced, slices, old):
    rows, down = reduced
    return pl.pallas_call(
        partial(update_kernel, shares),
        out_shape=[jax.ShapeDtypeStruct(piece.shape, jnp.float32) for piece in old]
        + [jax.ShapeDtypeStruct(slices.shape, jnp.float32)],
        scratch_shapes=[pltpu.VMEM((shares.width, shares.columns), jnp.float32)],
        compiler_params=pltpu.CompilerParams(vmem_limit_bytes=VMEM_BYTES),
    )(halves, rows, swap(rows), down, swap(down), slices, *old)


(GAIN_ONE, SHIFT_ONE, BIAS_OUT, GAIN_TWO, SHIFT_TWO, BIAS_DOWN, BIAS_PROJ, _, BIAS_UP, _) = [
    slice(row, row + 1) for row in range(10)
]
ROWS = 256
COLS = 384
STRIP = 32


def whole(shape):
    return pl.BlockSpec(shape, lambda i: (0,) * len(shape))


def row_block(width):
    return pl.BlockSpec((ROWS, width), lambda i: (i, 0))


def col_block(tokens):
    return pl.BlockSpec((tokens, COLS), lambda i: (0, i))


def at_block(shape, *index):
    return pl.BlockSpec(shape, lambda i: index)


def params_of(flops, moved, transcendentals=0):
    return {
        "compiler_params": pltpu.CompilerParams(vmem_limit_bytes=VMEM_BYTES),
        "cost_estimate": pl.CostEstimate(
            flops=flops, bytes_accessed=moved, transcendentals=transcendentals
        ),
    }


def strips(length=ROWS, strip=STRIP):
    return [slice(first, first + strip) for first in range(0, length, strip)]


def both(own_ref, recv_ref, rows):
    return own_ref[rows, :].astype(jnp.float32) + recv_ref[rows, :].astype(jnp.float32)


def bias_of(vec_ref, first, index):
    start = index * COLS
    width = vec_ref.shape[1]
    row = first.start + start // width
    return vec_ref[row : row + 1, start % width : start % width + COLS]


def eights(values):
    rows, width = values.shape
    return jnp.sum(values.reshape(rows // 8, 8, width), axis=0)


def features_kernel(shares, random_ref, segment_ref, global_ref, query_ref, key_ref, turned_ref):
    core = lax.axis_index(SECTION)
    place = lax.axis_index(SEQ)
    blocks = random_ref.shape[1]
    width = key_ref.shape[1]
    heads = query_ref.shape[0]
    per_half = heads // shares.per
    picks = random_ref.shape[2] // (2 * heads)
    tokens = key_ref.shape[0]
    lane = lax.broadcasted_iota(jnp.int32, (blocks, width), 1)
    row = lax.broadcasted_iota(jnp.int32, (blocks, width), 0)
    key = jnp.where(lane < blocks, lane, lane - blocks)
    chosen = random_ref[place]
    named = global_ref[place]
    always = (jnp.abs(row - key) <= 1).astype(jnp.int32)
    is_global = jnp.zeros((blocks, width), jnp.int32)
    for index in range(named.shape[1]):
        spot = named[:, index : index + 1]
        always = always + (key == spot).astype(jnp.int32)
        is_global = is_global + (row == spot).astype(jnp.int32)
    line = segment_ref[place].astype(jnp.float32)
    column = jnp.transpose(jnp.broadcast_to(line, (8, tokens)))[:, 0:1]
    token_lane = lax.broadcasted_iota(jnp.int32, (tokens, width), 1)
    same = column == (token_lane - 2 * blocks).astype(jnp.float32)
    in_segment = (token_lane >= 2 * blocks) & (token_lane < 2 * blocks + 3)
    segment_side = jnp.where(in_segment & same, 1.0, 0.0)
    for head in range(heads):
        count = always
        for pick in range(picks):
            at = [
                (2 * per_half * (head // per_half) + per_half * side + head % per_half) * picks
                + pick
                for side in range(2)
            ]
            spot = jnp.where(core == 0, chosen[:, at[0] : at[0] + 1], chosen[:, at[1] : at[1] + 1])
            count = count + (key == spot).astype(jnp.int32)
        count = jnp.where(is_global > 0, 1, count)
        high = jnp.where(count == 0, masked, 0.0)
        low = jnp.zeros_like(high)
        for times in (2, 3):
            high = jnp.where(count == times, LOG_HIGH[times - 1], high)
            low = jnp.where(count == times, LOG_LOW[times - 1], low)
        table = jnp.where(lane < blocks, high, jnp.where(lane < 2 * blocks, low, 0.0))
        for block in range(blocks):
            rows = slice(block * BLOCK, (block + 1) * BLOCK)
            query_ref[head, rows, :] = (table[block : block + 1] + segment_side[rows]).astype(LOW)
    token_block = lax.shift_right_logical(
        lax.broadcasted_iota(jnp.int32, (tokens, width), 0), BLOCK.bit_length() - 1
    )
    here = (token_block == token_lane) | (token_block == token_lane - blocks)
    side = jnp.where(here & (token_lane < 2 * blocks), 1.0, 0.0)
    side = jnp.where(in_segment & jnp.logical_not(same), masked, side)
    ones = (token_lane >= 2 * blocks + 3) & (token_lane < 2 * blocks + 6)
    side = jnp.where(ones, 1.0, side)
    key_ref[...] = side.astype(LOW)
    turned_ref[...] = jnp.transpose(side).astype(LOW)


def key_features(shares, random_ids, segment_ids, global_ids):
    micro, _, blocks, head_count, picks = random_ids.shape
    tokens = segment_ids.shape[2]
    width = -(-(2 * blocks + 6) // 128) * 128
    return pl.pallas_call(
        partial(features_kernel, shares),
        out_shape=[
            jax.ShapeDtypeStruct((head_count // 2, tokens, width), LOW),
            jax.ShapeDtypeStruct((tokens, width), LOW),
            jax.ShapeDtypeStruct((width, tokens), LOW),
        ],
        **params_of(0, head_count * tokens * width),
    )(random_ids.reshape(micro, blocks, head_count * picks), segment_ids, global_ids)


def project_kernel(joins, *refs):
    if joins:
        (middle_ref, part_ref, recv_ref, before_ref), refs = refs[:4], refs[4:]
    else:
        hidden_ref, refs = refs[0], refs[1:]
    (vec_ref, weight_ref), refs = refs[:2], refs[2:]
    if joins:
        hidden_ref, refs = refs[0], refs[1:]
    normed_ref, out_ref = refs
    for rows in strips():
        if joins:
            part = both(part_ref, recv_ref, rows)
            low = (middle_ref[rows, :] + part + before_ref[BIAS_DOWN]).astype(LOW)
            hidden_ref[rows, :] = low
        else:
            low = hidden_ref[rows, :]
        unit, _ = normalized(low.astype(jnp.float32))
        normed_ref[rows, :] = (unit * vec_ref[GAIN_ONE] + vec_ref[SHIFT_ONE]).astype(LOW)
    for index in range(out_ref.shape[1] // COLS):
        cols = slice(index * COLS, (index + 1) * COLS)
        product = dot_rows(normed_ref[...], weight_ref[cols, :])
        out_ref[:, cols] = (product + bias_of(vec_ref, BIAS_PROJ, index)).astype(LOW)


def project(before, vec, rows, out_width):
    joins = len(before) > 1
    tokens, width = before[0].shape
    ins = [row_block(width)] * 3 + [whole(vec.shape)] if joins else [row_block(width)]
    outs = [row_block(width)] * (2 if joins else 1)
    low = jax.ShapeDtypeStruct((tokens, width), LOW)
    return pl.pallas_call(
        partial(project_kernel, joins),
        grid=(tokens // ROWS,),
        in_specs=ins + [whole(vec.shape), whole((out_width, width))],
        out_specs=outs + [row_block(out_width)],
        out_shape=[low] * len(outs) + [jax.ShapeDtypeStruct((tokens, out_width), LOW)],
        **params_of(2 * tokens * width * out_width, tokens * width * 16),
    )(*before, vec, rows)


def out_halves(packed_ref, half):
    wide = packed_ref.shape[1] // 2
    return [
        jnp.concatenate([packed_ref[rows, :wide], packed_ref[rows, wide:]], axis=0)
        for rows in (slice(0, half), slice(half, 2 * half))
    ]


def branch_kernel(half, attended_ref, packed_ref, low_ref):
    wide = attended_ref.shape[1]
    for index, weights in enumerate(out_halves(packed_ref, half)):
        cols = slice(index * wide, (index + 1) * wide)
        low_ref[:, cols] = dot_rows(attended_ref[...], weights).astype(LOW)


def branch_out(shares, attended, rows):
    tokens, wide = attended.shape
    width = rows.shape[1]
    return pl.pallas_call(
        partial(branch_kernel, shares.half),
        grid=(tokens // ROWS,),
        in_specs=[row_block(wide), at_block((COLS, width), 3, 0)],
        out_specs=row_block(width),
        out_shape=jax.ShapeDtypeStruct((tokens, width), LOW),
        **params_of(2 * tokens * width * wide, tokens * width * 4),
    )(attended, rows)


def gelu_parts(value):
    below = 1.0 + (0.3275911 * 0.5**0.5) * jnp.abs(value)
    rough = pl.reciprocal(below, approx=True)
    t = rough * (2.0 - below * rough)
    bell = jnp.exp((-0.5 * value) * value)
    poly = 0.5 * 1.061405429
    for coefficient in (-1.453152027, 1.421413741, -0.284496736, 0.254829592):
        poly = poly * t + 0.5 * coefficient
    tail = poly * (t * bell)
    cdf = jnp.where(value > 0, 1.0 - tail, tail)
    return value * cdf, cdf + value * (bell * (0.5 / math.pi) ** 0.5)


def expand_kernel(
    hidden_ref,
    branch_ref,
    recv_ref,
    vec_ref,
    up_ref,
    down_ref,
    middle_ref,
    normed_ref,
    slope_ref,
    active_ref,
    low_ref,
    held,
):
    for rows in strips():
        branch = both(branch_ref, recv_ref, rows) + vec_ref[BIAS_OUT]
        middle = hidden_ref[rows, :].astype(jnp.float32) + branch
        middle_ref[rows, :] = middle
        unit, _ = normalized(middle)
        normed_ref[rows, :] = (unit * vec_ref[GAIN_TWO] + vec_ref[SHIFT_TWO]).astype(LOW)
    for index in range(up_ref.shape[0] // COLS):
        cols = slice(index * COLS, (index + 1) * COLS)
        held[index] = dot_rows(normed_ref[...], up_ref[cols, :])
        for rows in strips():
            active, slope = gelu_parts(held[index, rows, :] + bias_of(vec_ref, BIAS_UP, index))
            active_ref[rows, cols] = active.astype(LOW)
            slope_ref[rows, cols] = slope.astype(LOW)
    low_ref[...] = dot_plain(active_ref[...], down_ref[...]).astype(LOW)


def expand(hidden, branch, recv, vec, rows, down):
    tokens, width = hidden.shape
    inner = down.shape[0]
    return pl.pallas_call(
        expand_kernel,
        grid=(tokens // ROWS,),
        in_specs=[row_block(width)] * 3
        + [whole(vec.shape), at_block((inner, width), 1, 0), whole((inner, width))],
        out_specs=[row_block(width), row_block(width), row_block(inner), row_block(inner)]
        + [row_block(width)],
        out_shape=[
            jax.ShapeDtypeStruct((tokens, width), jnp.float32),
            jax.ShapeDtypeStruct((tokens, width), LOW),
            jax.ShapeDtypeStruct((tokens, inner), LOW),
            jax.ShapeDtypeStruct((tokens, inner), LOW),
            jax.ShapeDtypeStruct((tokens, width), LOW),
        ],
        scratch_shapes=[pltpu.VMEM((inner // COLS, ROWS, COLS), jnp.float32)],
        **params_of(4 * tokens * width * inner, tokens * width * 32, tokens * inner),
    )(hidden, branch, recv, vec, rows, down)


def expand_back_kernel(
    grad_ref,
    slope_ref,
    up_ref,
    down_ref,
    low_ref,
    grad_up_ref,
    bias_up_ref,
    bias_down_ref,
    sums_up,
    sums_down,
):
    step = pl.program_id(0)

    @pl.when(step == 0)
    def _():
        sums_up[...] = jnp.zeros_like(sums_up)
        sums_down[...] = jnp.zeros_like(sums_down)

    for index in range(down_ref.shape[0] // COLS):
        cols = slice(index * COLS, (index + 1) * COLS)
        grad_active = dot_rows(grad_ref[...], down_ref[cols, :])
        grad_up_ref[:, cols] = (grad_active * slope_ref[:, cols].astype(jnp.float32)).astype(LOW)
    low_ref[...] = dot_plain(grad_up_ref[...], up_ref[...]).astype(LOW)
    for rows in strips():
        sums_up[...] += eights(grad_up_ref[rows, :].astype(jnp.float32))
        sums_down[...] += eights(grad_ref[rows, :].astype(jnp.float32))

    @pl.when(step == pl.num_programs(0) - 1)
    def _():
        bias_up_ref[...] = jnp.sum(sums_up[...], axis=0, keepdims=True)
        bias_down_ref[...] = jnp.sum(sums_down[...], axis=0, keepdims=True)


def expand_back(grad, slope, rows, down):
    tokens, width = grad.shape
    inner = down.shape[0]
    return pl.pallas_call(
        expand_back_kernel,
        grid=(tokens // ROWS,),
        in_specs=[row_block(width), row_block(inner)]
        + [at_block((inner, width), 1, 0), whole((inner, width))],
        out_specs=[row_block(width), row_block(inner), whole((1, inner)), whole((1, width))],
        out_shape=[
            jax.ShapeDtypeStruct((tokens, width), LOW),
            jax.ShapeDtypeStruct((tokens, inner), LOW),
            jax.ShapeDtypeStruct((1, inner), jnp.float32),
            jax.ShapeDtypeStruct((1, width), jnp.float32),
        ],
        scratch_shapes=[pltpu.VMEM((8, inner), jnp.float32), pltpu.VMEM((8, width), jnp.float32)],
        **params_of(4 * tokens * width * inner, tokens * width * 24),
    )(grad, slope, rows, down)


def token_products_kernel(lefts, rights, outs):
    for left, right, out in zip(lefts, rights, outs):
        for first in range(0, COLS, 128):
            cols = slice(first, first + 128)
            out[cols, :] = dot_tokens(left[:, cols], right[...]).astype(LOW)


def hidden_products(active, grad, grad_up, normed):
    tokens, inner = active.shape
    width = grad.shape[1]

    def kernel(a_ref, b_ref, c_ref, d_ref, down_ref, rows_ref):
        token_products_kernel((a_ref, b_ref), (c_ref, d_ref), (down_ref, rows_ref))

    return pl.pallas_call(
        kernel,
        grid=(inner // COLS,),
        in_specs=[col_block(tokens)] * 2 + [whole((tokens, width))] * 2,
        out_specs=[
            pl.BlockSpec((COLS, width), lambda i: (i, 0)),
            pl.BlockSpec((COLS, width), lambda i: (inner // COLS + i, 0)),
        ],
        out_shape=[
            jax.ShapeDtypeStruct((inner, width), LOW),
            jax.ShapeDtypeStruct((2 * inner, width), LOW),
        ],
        **params_of(4 * tokens * width * inner, tokens * width * 16),
    )(active, grad_up, grad, normed)


def project_products(grad_proj, normed, rows_grad):
    tokens, out_width = grad_proj.shape
    width = normed.shape[1]

    def kernel(a_ref, b_ref, _, rows_ref):
        token_products_kernel((a_ref,), (b_ref,), (rows_ref,))

    return pl.pallas_call(
        kernel,
        grid=(out_width // COLS,),
        in_specs=[col_block(tokens), whole((tokens, width)), pl.BlockSpec(memory_space=pl.ANY)],
        out_specs=pl.BlockSpec((COLS, width), lambda i: (i, 0)),
        out_shape=jax.ShapeDtypeStruct(rows_grad.shape, LOW),
        input_output_aliases={2: 0},
        **params_of(2 * tokens * width * out_width, tokens * width * 8),
    )(grad_proj, normed, rows_grad)


def norm_back_rows(values_in, incoming, gain_vec):
    unit, scale = normalized(values_in)
    p = incoming * gain_vec
    mean_p = jnp.mean(p, axis=-1, keepdims=True)
    mean_pn = jnp.mean(p * unit, axis=-1, keepdims=True)
    return scale * (p - mean_p - unit * mean_pn), eights(incoming * unit), eights(incoming)


def branch_back_kernel(
    half,
    middle_ref,
    part_ref,
    recv_ref,
    grad_ref,
    attended_ref,
    vec_ref,
    packed_ref,
    _,
    grad_middle_ref,
    grad_attended_ref,
    out_grad_ref,
    gain_grad_ref,
    shift_grad_ref,
    bias_grad_ref,
    total,
    low,
    sums,
):
    step = pl.program_id(0)

    @pl.when(step == 0)
    def _():
        total[...] = jnp.zeros_like(total)
        sums[...] = jnp.zeros_like(sums)

    for rows in strips():
        incoming = both(part_ref, recv_ref, rows)
        change, for_gain, for_shift = norm_back_rows(
            middle_ref[rows, :], incoming, vec_ref[GAIN_TWO]
        )
        grad_middle = grad_ref[rows, :].astype(jnp.float32) + change
        grad_middle_ref[rows, :] = grad_middle
        rounded = grad_middle.astype(LOW)
        low[rows, :] = rounded
        sums[0] += for_gain
        sums[1] += for_shift
        sums[2] += eights(rounded.astype(jnp.float32))
    weights = out_halves(packed_ref, half)
    wide = weights[0].shape[0]
    attended = attended_ref[...]
    pieces = [low[:, :wide], low[:, wide:]]
    grad_attended_ref[...] = (
        dot_plain(pieces[0], weights[0]) + dot_plain(pieces[1], weights[1])
    ).astype(LOW)
    for index in range(2):
        total[index] += dot_tokens(pieces[index], attended)

    @pl.when(step == pl.num_programs(0) - 1)
    def _():
        for index in range(2):
            joined = jnp.concatenate([total[index, :half, :], total[index, half:, :]], axis=1)
            out_grad_ref[index * half : (index + 1) * half, :] = joined.astype(LOW)
        for index, ref in enumerate((gain_grad_ref, shift_grad_ref, bias_grad_ref)):
            ref[...] = jnp.sum(sums[index], axis=0, keepdims=True)


def branch_back(shares, middle, part, recv, grad, attended, vec, rows, rows_grad):
    tokens, width = middle.shape
    wide = attended.shape[1]
    small = whole((1, width))
    one = jax.ShapeDtypeStruct((1, width), jnp.float32)
    return pl.pallas_call(
        partial(branch_back_kernel, shares.half),
        grid=(tokens // ROWS,),
        in_specs=[row_block(width)] * 4
        + [row_block(wide), whole(vec.shape), at_block((COLS, width), 3, 0)]
        + [pl.BlockSpec(memory_space=pl.ANY)],
        out_specs=[row_block(width), row_block(wide), at_block((COLS, width), 3, 0)]
        + [small, small, small],
        out_shape=[
            jax.ShapeDtypeStruct((tokens, width), jnp.float32),
            jax.ShapeDtypeStruct((tokens, wide), LOW),
            jax.ShapeDtypeStruct(rows_grad.shape, LOW),
            one,
            one,
            one,
        ],
        input_output_aliases={7: 2},
        scratch_shapes=[
            pltpu.VMEM((2, width // 2, wide), jnp.float32),
            pltpu.VMEM((ROWS, width), LOW),
            pltpu.VMEM((3, 8, width), jnp.float32),
        ],
        **params_of(4 * tokens * width * wide, tokens * width * 20),
    )(middle, part, recv, grad, attended, vec, rows, rows_grad)


def project_back_kernel(grad_ref, weight_ref, low_ref, bias_ref, sums):
    step = pl.program_id(0)

    @pl.when(step == 0)
    def _():
        sums[...] = jnp.zeros_like(sums)

    low_ref[...] = dot_plain(grad_ref[...], weight_ref[...]).astype(LOW)
    for rows in strips():
        sums[...] += eights(grad_ref[rows, :].astype(jnp.float32))

    @pl.when(step == pl.num_programs(0) - 1)
    def _():
        bias_ref[...] = jnp.sum(sums[...], axis=0, keepdims=True)


def project_back(grad_proj, rows):
    tokens, out_width = grad_proj.shape
    width = rows.shape[1]
    return pl.pallas_call(
        project_back_kernel,
        grid=(tokens // ROWS,),
        in_specs=[row_block(out_width), whole((out_width, width))],
        out_specs=[row_block(width), whole((1, out_width))],
        out_shape=[
            jax.ShapeDtypeStruct((tokens, width), LOW),
            jax.ShapeDtypeStruct((1, out_width), jnp.float32),
        ],
        scratch_shapes=[pltpu.VMEM((8, out_width), jnp.float32)],
        **params_of(2 * tokens * width * out_width, tokens * width * 12),
    )(grad_proj, rows)


def input_back_kernel(
    hidden_ref, part_ref, recv_ref, grad_ref, vec_ref, out_ref, gain_grad_ref, shift_grad_ref, sums
):
    step = pl.program_id(0)

    @pl.when(step == 0)
    def _():
        sums[...] = jnp.zeros_like(sums)

    for rows in strips():
        incoming = both(part_ref, recv_ref, rows)
        hidden = hidden_ref[rows, :].astype(jnp.float32)
        change, for_gain, for_shift = norm_back_rows(hidden, incoming, vec_ref[GAIN_ONE])
        out_ref[rows, :] = (grad_ref[rows, :] + change).astype(LOW)
        sums[0] += for_gain
        sums[1] += for_shift

    @pl.when(step == pl.num_programs(0) - 1)
    def _():
        gain_grad_ref[...] = jnp.sum(sums[0], axis=0, keepdims=True)
        shift_grad_ref[...] = jnp.sum(sums[1], axis=0, keepdims=True)


def input_back(hidden, part, recv, grad_middle, vec):
    tokens, width = hidden.shape
    small = whole((1, width))
    one = jax.ShapeDtypeStruct((1, width), jnp.float32)
    return pl.pallas_call(
        input_back_kernel,
        grid=(tokens // ROWS,),
        in_specs=[row_block(width)] * 4 + [whole(vec.shape)],
        out_specs=[row_block(width), small, small],
        out_shape=[jax.ShapeDtypeStruct((tokens, width), LOW), one, one],
        scratch_shapes=[pltpu.VMEM((2, 8, width), jnp.float32)],
        **params_of(0, tokens * width * 12),
    )(hidden, part, recv, grad_middle, vec)


def attend_kernel(q_ref, k_ref, v_ref, qa_ref, kt_ref, out_ref, lse_ref, keys, held, low):
    tokens, pair = q_ref.shape
    left = lax.broadcasted_iota(jnp.int32, (CHUNK, pair), 1) < pair // 2
    keys[:pair, :] = jnp.transpose(k_ref[...].astype(jnp.float32)).astype(LOW)
    keys[pair:, :] = kt_ref[...]
    for index in range(tokens // CHUNK):
        rows = slice(index * CHUNK, (index + 1) * CHUNK)
        queries = q_ref[rows, :] * 0.125
        outs, tops = [], []
        for head in range(2):
            slot = (2 * index + head) % held.shape[0]
            mine = left if head == 0 else jnp.logical_not(left)
            side = jnp.where(mine, queries, jnp.zeros_like(queries))
            lhs = jnp.concatenate([side, qa_ref[head, rows, :]], axis=1)
            held[slot] = dot_plain(lhs, keys[...])
            levels, shares = [], []
            for strip in strips(CHUNK):
                scores = held[slot, strip, :]
                top = jnp.max(scores, axis=1, keepdims=True)
                weight = jnp.exp(scores - top)
                total = jnp.sum(weight, axis=1, keepdims=True)
                low[slot, strip, :] = weight.astype(LOW)
                levels.append(top + jnp.log(total))
                shares.append(1.0 / total)
            product = dot_plain(low[slot], v_ref[...])
            outs.append(product * jnp.concatenate(shares, axis=0))
            tops.append(jnp.concatenate(levels, axis=0))
        out_ref[rows, :] = jnp.where(left, outs[0], outs[1]).astype(LOW)
        lse_ref[rows, :] = jnp.where(left, tops[0], tops[1])


def attend(projected, query_side, key_side, turned):
    tokens = projected.shape[0]
    width = projected.shape[1] // 3
    pairs = width // 128
    features = key_side.shape[1]
    return pl.pallas_call(
        attend_kernel,
        grid=(pairs,),
        in_specs=[
            pl.BlockSpec((tokens, 128), lambda p: (0, p)),
            pl.BlockSpec((tokens, 128), lambda p: (0, pairs + p)),
            pl.BlockSpec((tokens, 128), lambda p: (0, 2 * pairs + p)),
            pl.BlockSpec((2, tokens, features), lambda p: (p, 0, 0)),
            whole((features, tokens)),
        ],
        out_specs=[
            pl.BlockSpec((tokens, 128), lambda p: (0, p)),
            pl.BlockSpec((tokens, 128), lambda p: (0, p)),
        ],
        out_shape=[
            jax.ShapeDtypeStruct((tokens, width), LOW),
            jax.ShapeDtypeStruct((tokens, width), jnp.float32),
        ],
        scratch_shapes=[
            pltpu.VMEM((128 + features, tokens), LOW),
            pltpu.VMEM((4, CHUNK, tokens), jnp.float32),
            pltpu.VMEM((4, CHUNK, tokens), LOW),
        ],
        **params_of(
            16 * pairs * tokens * tokens * 128, tokens * width * 16, 2 * pairs * tokens * tokens
        ),
    )(projected, projected, projected, query_side, turned)


def three_terms(values):
    high = values.astype(LOW).astype(jnp.float32)
    rest = values - high
    middle = rest.astype(LOW).astype(jnp.float32)
    return high, middle, rest - middle


def attend_back_kernel(
    q_ref,
    k_ref,
    v_ref,
    do_ref,
    o_ref,
    lse_ref,
    qa_ref,
    ka_ref,
    grad_ref,
    held,
    probs,
    changes,
    query_sides,
    grad_sides,
):
    tokens, pair = q_ref.shape
    features = ka_ref.shape[1]
    pairs = pl.num_programs(0)
    place = pl.program_id(0)
    first = 2 * (tokens // BLOCK) + 3
    half = pair // 2
    left = lax.broadcasted_iota(jnp.int32, (CHUNK, pair), 1) < half
    lane = lax.broadcasted_iota(jnp.int32, (CHUNK, features), 1)
    lane_pair = lax.broadcasted_iota(jnp.int32, (CHUNK, pair), 1)
    keys = jnp.concatenate([k_ref[...], ka_ref[...]], axis=1)
    turned = jnp.transpose(k_ref[...].astype(jnp.float32)).astype(LOW)
    ones = (lax.broadcasted_iota(jnp.int32, (tokens, pair), 1) < 3).astype(jnp.float32).astype(LOW)
    values = jnp.concatenate([v_ref[...], ones], axis=1)
    parts, key_grads, value_grads = [], [], []
    for head in range(2):
        mine = left if head == 0 else jnp.logical_not(left)
        for index in range(tokens // CHUNK):
            rows = slice(index * CHUNK, (index + 1) * CHUNK)
            slot = index % 2
            queries = q_ref[rows, :] * 0.125
            grads = do_ref[rows, :]
            product = grads.astype(jnp.float32) * o_ref[rows, :].astype(jnp.float32)
            level = lse_ref[rows, head * half : head * half + 1]
            inner = jnp.sum(jnp.where(mine, product, 0.0), axis=1, keepdims=True)
            side = qa_ref[head, rows, :].astype(jnp.float32)
            for spot, term in enumerate(three_terms(level)):
                side = jnp.where(lane == first + spot, -term, side)
            query_side = jnp.where(mine, queries, jnp.zeros_like(queries))
            grad_side = jnp.where(mine, grads, jnp.zeros_like(grads))
            query_sides[head, rows, :] = query_side
            grad_sides[head, rows, :] = grad_side
            tail = jnp.zeros((CHUNK, pair), jnp.float32)
            for spot, term in enumerate(three_terms(inner)):
                tail = jnp.where(lane_pair == spot, -term, tail)
            held[slot, 0] = dot_rows(
                keys, jnp.concatenate([query_side, side.astype(LOW)], axis=1)
            )
            held[slot, 1] = dot_rows(
                values, jnp.concatenate([grad_side, tail.astype(LOW)], axis=1)
            )
            for strip in strips(tokens, 128):
                prob = jnp.exp(held[slot, 0, strip, :])
                probs[head, strip, rows] = prob.astype(LOW)
                changes[head, strip, rows] = (prob * held[slot, 1, strip, :]).astype(LOW)
        value_grads.append(dot_plain(probs[head], grad_sides[head]))
        key_grads.append(dot_plain(changes[head], query_sides[head]))
        parts.append(dot_plain(turned, changes[head]))
    joined = jnp.concatenate([parts[0][:half], parts[1][half:]], axis=0)
    column = [pl.ds(pl.multiple_of((by * pairs + place) * 128, 128), 128) for by in range(3)]
    grad_ref[:, column[0]] = (jnp.transpose(joined) * 0.125).astype(LOW)
    grad_ref[:, column[1]] = (key_grads[0] + key_grads[1]).astype(LOW)
    grad_ref[:, column[2]] = (value_grads[0] + value_grads[1]).astype(LOW)


def attend_back(projected, grad_attended, attended, levels, query_side, key_side):
    tokens, width = attended.shape
    pairs = width // 128
    features = key_side.shape[1]
    by_pair = pl.BlockSpec((tokens, 128), lambda p: (0, p))
    return pl.pallas_call(
        attend_back_kernel,
        grid=(pairs,),
        in_specs=[
            by_pair,
            pl.BlockSpec((tokens, 128), lambda p: (0, pairs + p)),
            pl.BlockSpec((tokens, 128), lambda p: (0, 2 * pairs + p)),
            by_pair,
            by_pair,
            by_pair,
            pl.BlockSpec((2, tokens, features), lambda p: (p, 0, 0)),
            whole((tokens, features)),
        ],
        out_specs=whole((tokens, 3 * width)),
        out_shape=jax.ShapeDtypeStruct((tokens, 3 * width), LOW),
        scratch_shapes=[
            pltpu.VMEM((2, 2, tokens, CHUNK), jnp.float32),
            pltpu.VMEM((2, tokens, tokens), LOW),
            pltpu.VMEM((2, tokens, tokens), LOW),
            pltpu.VMEM((2, tokens, 128), LOW),
            pltpu.VMEM((2, tokens, 128), LOW),
        ],
        **params_of(
            40 * pairs * tokens * tokens * 128, tokens * width * 24, 2 * pairs * tokens * tokens
        ),
    )(projected, projected, projected, grad_attended, attended, levels, query_side, key_side)


def window_forward(shares, before, weights, vec, features, late=None):
    rows, down = weights
    results = project(before, vec, rows, 6 * shares.half)
    hidden = before[0] if len(before) == 1 else results[0]
    normed, projected = results[-2:]
    if late is not None:
        projected, late[0] = lax.optimization_barrier((projected, late[0]))
    attended, levels = attend(projected, *features)
    if late is not None:
        attended, levels, late[1] = lax.optimization_barrier((attended, levels, late[1]))
    low = branch_out(shares, attended, rows)
    middle, normed_two, slope, active, low = expand(hidden, low, swap(low), vec, rows, down)
    stored = (hidden, normed, projected, attended, levels, middle, normed_two, slope, active)
    return (middle, low, swap(low), vec), stored


def window_backward(stored, grad, weights, vec, features, shares, reduce):
    hidden, normed, projected, attended, levels, middle, normed_two, slope, active = stored
    rows, down = weights
    low, grad_up, bias_up, bias_down = expand_back(grad, slope, rows, down)
    arrived = swap(low)
    down_grad, rows_grad = hidden_products(active, grad, grad_up, normed_two)
    down_grad = reduce(down_grad)
    grad_middle, grad_attended, rows_grad, gain_two, shift_two, bias_out = branch_back(
        shares, middle, low, arrived, grad, attended, vec, rows, rows_grad
    )
    grad_proj = attend_back(projected, grad_attended, attended, levels, *features[:2])
    low, summed = project_back(grad_proj, rows)
    arrived = swap(low)
    rows_grad = reduce(project_products(grad_proj, normed, rows_grad))
    grad, gain_one, shift_one = input_back(hidden, low, arrived, grad_middle, vec)
    width = attended.shape[1]
    vector_grads = (gain_one, shift_one, summed[:, :width], summed[:, 2 * width :], bias_out)
    vector_grads += (gain_two, shift_two, bias_down, bias_up)
    vector_grads = [piece[0] for piece in vector_grads]
    return grad, (rows_grad, down_grad), vector_grads


def window_shards(
    block_input,
    cotangent,
    random_ids,
    segment_ids,
    global_ids,
    w_rows,
    w_rows_first,
    w_rows_second,
    w_down,
    w_down_first,
    w_down_second,
    vectors,
    vectors_first,
    vectors_second,
):
    core = lax.axis_index(SECTION)
    micro, _, tokens, width = block_input.shape
    _, _, columns = w_rows.shape
    shares = Shares(width, columns, w_down.shape[1], vectors.shape[1])
    rows, down, vec = prepare(shares, w_rows[0], w_down[0], vectors)
    rows_recv, down_recv, vec_recv = swap(rows[1]), swap(down[1]), swap(vec)

    def of_layer(layer, kept, recv):
        return jnp.where(core == layer, kept, recv)

    rows_one = of_layer(1, rows[0], rows_recv)
    down_one = of_layer(1, down[0], down_recv)
    rows_one = lax.all_gather(rows_one, (DP, SEQ), axis=0)
    down_one = lax.all_gather(down_one, (DP, SEQ), axis=0)
    first_layer = [of_layer(0, rows[0], rows_recv), of_layer(0, down[0], down_recv)]
    first_layer += [of_layer(layer, vec, vec_recv) for layer in range(2)]
    gathered_zero, vec_one, hidden, grad = gather(shares, first_layer, block_input, cotangent)
    features = key_features(shares, random_ids, segment_ids, global_ids)

    params = [shares.unpack(gathered_zero, core)]
    before = (hidden.reshape(-1, width),)
    late = [rows_one, down_one]
    before, stored_zero = window_forward(shares, before, *params[0], features, late)
    params.append(shares.unpack((*late, vec_one), core))
    after, stored_one = window_forward(shares, before, *params[1], features)
    final = after[1].astype(jnp.float32) + after[2].astype(jnp.float32)
    final = (after[0] + final + after[3][BIAS_DOWN]).astype(LOW)

    shards = lax.axis_size((DP, SEQ))

    def summed(array):
        return lax.psum_scatter(
            array.reshape(shards, -1, width), (DP, SEQ), scatter_dimension=0
        )

    grad = grad.reshape(-1, width)
    grad, reduced, vector_one = window_backward(
        stored_one, grad, *params[1], features, shares, summed
    )
    grad, own, vector_zero = window_backward(
        stored_zero, grad, *params[0], features, shares, lambda array: array
    )
    arrays = [array.reshape(2, 2, 4, -1, width) for array in own]
    arrays += [shares.vector_shards(piece, core) for piece in (vector_zero, vector_one)]
    grad, final = [piece.reshape(micro, tokens, width) for piece in (grad, final)]
    halves, slices = scatter(shares, arrays, grad, final)
    old = [
        w_rows[0],
        w_rows_first[0],
        w_rows_second[0],
        w_down[0],
        w_down_first[0],
        w_down_second[0],
        vectors,
        vectors_first,
        vectors_second,
    ]
    *new, result = update(shares, halves, reduced, slices, old)
    return (result[None, :, None], *[piece[None] for piece in new[:6]], *new[6:])


def one_window_each(mesh, block_input, w_rows, w_down, vectors):
    micro, windows, length, width = block_input.shape
    shards = mesh.shape[DP] * mesh.shape[SEQ]
    columns, depth = w_rows.shape[2] // shards, w_down.shape[1] // shards
    head_dim = width // HEADS
    tokens = length // mesh.shape[SEQ]
    return (
        mesh.shape[SECTION] == 2
        and mesh.shape[SEQ] == micro
        and mesh.shape[DP] == windows
        and tokens % (2 * BLOCK) == 0
        and length % CHUNK == 0
        and head_dim == 64
        and width % columns == 0
        and columns % (2 * head_dim) == 0
        and columns % depth == 0
        and width // columns * (columns // 2) % 128 == 0
        and depth % 32 == 0
        and vectors.shape[1] // shards <= width
        and mesh.shape[DP] == 4
        and micro == 4
        and width == 2 * columns == 2 * COLS
        and w_down.shape[1] == 4 * width
        and (columns // 2) % (2 * PIECE) == 0
        and (depth // 2) % (2 * PIECE) == 0
        and length % (4 * ROWS) == 0
    )


def solution(mesh):
    in_specs = (
        P(None, DP, SEQ, None),
        P(None, DP, SEQ, None),
        P(None, DP, None, None, None),
        P(None, DP, None),
        P(None, DP, None),
        P(SECTION, None, (DP, SEQ)),
        P(SECTION, None, (DP, SEQ)),
        P(SECTION, None, (DP, SEQ)),
        P(SECTION, (DP, SEQ), None),
        P(SECTION, (DP, SEQ), None),
        P(SECTION, (DP, SEQ), None),
        P(SECTION, (DP, SEQ)),
        P(SECTION, (DP, SEQ)),
        P(SECTION, (DP, SEQ)),
    )
    out_specs = (
        P(SECTION, None, DP, SEQ, None),
        P(SECTION, None, (DP, SEQ)),
        P(SECTION, None, (DP, SEQ)),
        P(SECTION, None, (DP, SEQ)),
        P(SECTION, (DP, SEQ), None),
        P(SECTION, (DP, SEQ), None),
        P(SECTION, (DP, SEQ), None),
        P(SECTION, (DP, SEQ)),
        P(SECTION, (DP, SEQ)),
        P(SECTION, (DP, SEQ)),
    )

    def step(*arrays):
        chosen = general_shards
        if one_window_each(mesh, arrays[0], arrays[5], arrays[8], arrays[11]):
            chosen = window_shards
        return jax.shard_map(
            chosen, mesh=mesh, in_specs=in_specs, out_specs=out_specs, check_vma=False
        )(*arrays)

    return step
```

```python
import math
from functools import partial

import jax
import jax.numpy as jnp
import ml_dtypes
import numpy as np
from jax import lax
from jax.experimental import pallas as pl
from jax.experimental.pallas import tpu as pltpu
from jax.sharding import PartitionSpec as P

SECTION, DP, SEQ = "section", "dp", "seq"
HEADS = 12
BLOCK = 64
STEP = 5


epsilon = 1e-05
masked = -1e30
rate_matrix = 0.02
rate_vector = 0.2
decay_matrix = 0.01


def with_halo(x, sides, width):
    for axis, dim in sides:
        devices, length = (lax.axis_size(axis), x.shape[dim])
        up = [(i, (i + 1) % devices) for i in range(devices - 1)]
        down = [(j, i) for i, j in up]
        last = lax.slice_in_dim(x, length - width, length, axis=dim)
        initial = lax.slice_in_dim(x, 0, width, axis=dim)
        before = lax.ppermute(last, axis, up)
        after = lax.ppermute(initial, axis, down)
        x = jnp.concatenate([before, x, after], axis=dim)
    return x


def merged(value, axis, join):
    pieces = jax.tree.map(lambda part: lax.all_gather(part, axis), value)
    head = jax.tree.map(lambda part: part[0], pieces)
    tail = jax.tree.map(lambda part: part[1:], pieces)
    subtotal, _ = lax.scan(lambda subtotal, share: (join(subtotal, share), None), head, tail)
    return subtotal


def from_behind(x, axis, by):
    devices = lax.axis_size(axis)
    pairs = [(i, i + by) for i in range(devices) if 0 <= i + by < devices]
    return lax.ppermute(x, axis, pairs)


def partner(value, axis, bit):
    mask = 2**bit
    pairs = [(source, source ^ mask) for source in range(lax.axis_size(axis))]
    return lax.ppermute(value, axis, pairs)


def mixed_sum(form, left, right):
    return jnp.einsum(form, left, right, preferred_element_type=jnp.float32)


def exact_two(form, left, right):
    return jnp.einsum(
        form, left, right, precision=lax.Precision.HIGHEST, preferred_element_type=jnp.float32
    )


def norm_rows(values_in, gain_vec, shift_vec):
    row_mean = jnp.mean(values_in, axis=-1, keepdims=True)
    centred = values_in - row_mean
    spread = jnp.mean(centred * centred, axis=-1, keepdims=True)
    return centred * lax.rsqrt(spread + epsilon) * gain_vec + shift_vec


def split_vectors(vector_weights, model_width):
    pieces = [
        vector_weights[piece_index * model_width : (piece_index + 1) * model_width]
        for piece_index in range(8)
    ]
    return pieces + [vector_weights[8 * model_width :]]


def route_tables(random_rows, segments, global_rows, seq_place, groups):
    windows, blocks, head_count, pick_count = random_rows.shape
    blocks_dev = blocks // groups
    request_count = blocks_dev * head_count * pick_count
    capacity = -(-request_count // groups)
    requests = random_rows.reshape(windows, groups, request_count)
    owners = requests // blocks_dev
    inside = requests % blocks_dev
    head_of = jnp.arange(request_count) // pick_count % head_count
    is_mine = owners == seq_place
    slot_index = jnp.cumsum(is_mine.astype(jnp.int32), axis=2) - 1
    slot_hot = ((slot_index[..., None] == jnp.arange(capacity)) & is_mine[..., None]).astype(
        jnp.float32
    )
    inside_hot = (inside[..., None] == jnp.arange(blocks_dev)).astype(jnp.float32)
    head_hot = (head_of[:, None] == jnp.arange(head_count)).astype(jnp.float32)
    sender = jnp.einsum(
        "wqsc,wqsb,sh->wqcbh", slot_hot, inside_hot, head_hot, precision=lax.Precision.HIGHEST
    )
    my_owners = lax.dynamic_index_in_dim(owners, seq_place, axis=1, keepdims=False)
    earlier = jnp.arange(request_count)[None, :] < jnp.arange(request_count)[:, None]
    same_owner = my_owners[:, :, None] == my_owners[:, None, :]
    rank_index = jnp.sum((same_owner & earlier[None]).astype(jnp.int32), axis=2)
    picker = (
        (my_owners[..., None, None] == jnp.arange(groups)[:, None])
        & (rank_index[..., None, None] == jnp.arange(capacity)[None, :])
    ).astype(jnp.float32)
    first_block = seq_place * blocks_dev
    owned_hot = (global_rows[:, :, None] == first_block + jnp.arange(blocks_dev)).astype(
        jnp.float32
    )
    length = segments.shape[1]
    block_len = length // blocks
    seg_blocks = segments.reshape(windows, blocks, block_len)
    seg_pad = jnp.pad(seg_blocks, ((0, 0), (1, 1), (0, 0)), constant_values=-1)
    near_segs = lax.dynamic_slice_in_dim(seg_pad, first_block, blocks_dev + 2, axis=1)
    slide_seg = jnp.concatenate([near_segs[:, :-2], near_segs[:, 1:-1], near_segs[:, 2:]], axis=2)
    query_seg = near_segs[:, 1:-1]
    rows_index = jnp.arange(windows)
    global_seg = seg_blocks[rows_index[:, None], global_rows].reshape(windows, -1)
    chosen = lax.dynamic_slice_in_dim(random_rows, first_block, blocks_dev, axis=1)
    far_seg = seg_blocks[rows_index[:, None, None, None], chosen].reshape(
        windows, blocks_dev, head_count, -1
    )
    key_seg = jnp.concatenate(
        [
            jnp.broadcast_to(
                slide_seg[:, :, None, :], (windows, blocks_dev, head_count, slide_seg.shape[2])
            ),
            jnp.broadcast_to(
                global_seg[:, None, None, :], (windows, blocks_dev, head_count, global_seg.shape[1])
            ),
            far_seg,
        ],
        axis=3,
    )
    key_mask = query_seg[:, :, None, :, None] == key_seg[:, :, :, None, :]
    local_seg = query_seg.reshape(windows, -1)
    full_mask = global_seg[:, None, :, None] == local_seg[:, None, None, :]
    return (sender, picker, owned_hot, key_mask, full_mask)


def fetch_blocks(paired, queries, sender, picker, owned_hot):
    windows, tokens, head_count, doubled = paired.shape
    head_dim = queries.shape[-1]
    blocks_dev = tokens // BLOCK
    flattened = paired.reshape(windows, tokens, head_count * doubled)
    padded = with_halo(flattened, ((SEQ, 1),), BLOCK)
    framed = padded.reshape(windows, blocks_dev + 2, BLOCK, head_count, doubled)
    sliding = jnp.concatenate([framed[:, :-2], framed[:, 1:-1], framed[:, 2:]], axis=2)
    local_blocks = paired.reshape(windows, blocks_dev, BLOCK, head_count, doubled)
    owned_low = owned_hot.astype(jnp.bfloat16)
    offered = mixed_sum("wgb,wbthe->wgthe", owned_low, local_blocks)
    offered_queries = mixed_sum("wgb,wbqhd->wgqhd", owned_low, queries)
    global_kv, global_queries = (
        lax.psum(offered.astype(jnp.bfloat16), SEQ).astype(jnp.float32),
        lax.psum(offered_queries.astype(jnp.bfloat16), SEQ).astype(jnp.float32),
    )
    global_kv = global_kv.astype(jnp.bfloat16).reshape(windows, -1, head_count, doubled)
    global_queries = global_queries.astype(jnp.bfloat16).reshape(windows, -1, head_count, head_dim)
    outgoing = mixed_sum("wqcbh,wbthe->qwcte", sender.astype(jnp.bfloat16), local_blocks).astype(
        jnp.bfloat16
    )
    incoming = lax.all_to_all(outgoing, SEQ, split_axis=0, concat_axis=0, tiled=True)
    distant = mixed_sum("wspc,pwcte->wste", picker.astype(jnp.bfloat16), incoming).astype(
        jnp.bfloat16
    )
    pick_count = picker.shape[1] // (blocks_dev * head_count)
    distant = distant.reshape(windows, blocks_dev, head_count, pick_count, BLOCK, doubled)
    return (sliding, global_kv, distant, global_queries)


def combine_stats(earlier, later):
    top = jnp.maximum(earlier[0], later[0])
    return (top, earlier[1] * jnp.exp(earlier[0] - top) + later[1] * jnp.exp(later[0] - top))


def full_forward(global_queries, key_part, value_part, full_mask, head_dim):
    scores = mixed_sum("wqhd,wkhd->whqk", global_queries, key_part) * head_dim ** (-0.5)
    scores = jnp.where(full_mask, scores, masked)
    local_top = jnp.max(scores, axis=3, keepdims=True)
    local_sum = jnp.sum(
        jnp.where(full_mask, jnp.exp(scores - local_top), 0.0), axis=3, keepdims=True
    )
    row_top, row_sum = merged((local_top, local_sum), SEQ, combine_stats)
    full_probs = jnp.where(full_mask, jnp.exp(scores - row_top), 0.0) / row_sum
    partial_out = mixed_sum("whqk,wkhd->wqhd", full_probs.astype(jnp.bfloat16), value_part)
    full_out = lax.psum(partial_out.astype(jnp.bfloat16), SEQ).astype(jnp.float32)
    return (full_out, full_probs)


def attention_weights(queries, sliding, global_kv, distant, key_mask):
    head_dim = queries.shape[-1]
    windows, blocks_dev, _, head_count, _ = queries.shape
    near_scores = mixed_sum("wbqhd,wbkhd->wbhqk", queries, sliding[..., :head_dim])
    global_scores = mixed_sum("wbqhd,wkhd->wbhqk", queries, global_kv[..., :head_dim])
    far_scores = mixed_sum("wbqhd,wbhrkd->wbhqrk", queries, distant[..., :head_dim])
    far_scores = far_scores.reshape(windows, blocks_dev, head_count, BLOCK, -1)
    scores = jnp.concatenate([near_scores, global_scores, far_scores], axis=4) * head_dim ** (-0.5)
    scores = jnp.where(key_mask, scores, masked)
    row_top = jnp.max(scores, axis=4, keepdims=True)
    weight = jnp.exp(scores - row_top)
    return weight / jnp.sum(weight, axis=4, keepdims=True)


def split_keys(scores_like, sliding, global_kv, distant):
    near_keys = sliding.shape[2]
    global_keys = global_kv.shape[1]
    windows, blocks_dev, head_count, pick_count, _, _ = distant.shape
    near_part = scores_like[..., :near_keys]
    global_part = scores_like[..., near_keys : near_keys + global_keys]
    far_part = scores_like[..., near_keys + global_keys :].reshape(
        windows, blocks_dev, head_count, BLOCK, pick_count, BLOCK
    )
    return (near_part, global_part, far_part)


def attention_values(low_probs, sliding, global_kv, distant, head_dim):
    near_part, global_part, far_part = split_keys(low_probs, sliding, global_kv, distant)
    attended = mixed_sum("wbhqk,wbkhd->wbqhd", near_part, sliding[..., head_dim:])
    attended = attended + mixed_sum("wbhqk,wkhd->wbqhd", global_part, global_kv[..., head_dim:])
    return attended + mixed_sum("wbhqrk,wbhrkd->wbqhd", far_part, distant[..., head_dim:])


def layer_forward(hidden, weights, tables):
    row_weights, down_weights, vector_weights = weights
    sender, picker, owned_hot, key_mask, full_mask = tables
    model_width = row_weights.shape[0]
    windows, tokens, _ = hidden.shape
    blocks_dev = tokens // BLOCK
    head_dim = model_width // HEADS
    (
        gain_one,
        shift_one,
        bias_query,
        bias_value,
        bias_out,
        gain_two,
        shift_two,
        bias_down,
        bias_up,
    ) = split_vectors(vector_weights, model_width)
    normed = norm_rows(hidden, gain_one, shift_one).astype(jnp.bfloat16)
    projected = mixed_sum("wtd,de->wte", normed, row_weights[:, : 3 * model_width])
    projected = (
        projected + jnp.concatenate([bias_query, jnp.zeros_like(bias_query), bias_value])
    ).astype(jnp.bfloat16)
    queries = projected[..., :model_width].reshape(windows, blocks_dev, BLOCK, HEADS, head_dim)
    key_part = projected[..., model_width : 2 * model_width].reshape(
        windows, tokens, HEADS, head_dim
    )
    value_part = projected[..., 2 * model_width :].reshape(windows, tokens, HEADS, head_dim)
    paired = jnp.concatenate([key_part, value_part], axis=3)
    sliding, global_kv, distant, global_queries = fetch_blocks(
        paired, queries, sender, picker, owned_hot
    )
    probabilities = attention_weights(queries, sliding, global_kv, distant, key_mask)
    attended = attention_values(
        probabilities.astype(jnp.bfloat16), sliding, global_kv, distant, head_dim
    )
    full_out, full_probs = full_forward(global_queries, key_part, value_part, full_mask, head_dim)
    placed = exact_two(
        "wgb,wgqhd->wbqhd", owned_hot, full_out.reshape(windows, -1, BLOCK, HEADS, head_dim)
    )
    on_global = jnp.sum(owned_hot, axis=1)[:, :, None, None, None] > 0
    attended = jnp.where(on_global, placed, attended)
    mixed_low = attended.reshape(windows, tokens, model_width).astype(jnp.bfloat16)
    middle = (
        hidden
        + mixed_sum("wtd,de->wte", mixed_low, row_weights[:, 3 * model_width : 4 * model_width])
        + bias_out
    )
    normed_two = norm_rows(middle, gain_two, shift_two).astype(jnp.bfloat16)
    up_value = mixed_sum("wtd,df->wtf", normed_two, row_weights[:, 4 * model_width :]) + bias_up
    active = jax.nn.gelu(up_value, approximate=False).astype(jnp.bfloat16)
    output = middle + mixed_sum("wtf,fd->wtd", active, down_weights) + bias_down
    stored = (
        hidden,
        normed,
        queries,
        sliding,
        global_kv,
        distant,
        probabilities,
        mixed_low,
        middle,
        normed_two,
        up_value,
        active,
        key_part,
        value_part,
        global_queries,
        full_probs,
    )
    return (output, stored)


def return_blocks(near_back, global_back, far_back, query_part, sender, picker, owned_hot):
    windows, blocks_dev, _, head_count, doubled = near_back.shape
    first_third = near_back[:, :, :BLOCK]
    centre_third = near_back[:, :, BLOCK : 2 * BLOCK]
    last_third = near_back[:, :, 2 * BLOCK :]
    framed = jnp.pad(first_third, ((0, 0), (0, 2), (0, 0), (0, 0), (0, 0)))
    framed = framed + jnp.pad(centre_third, ((0, 0), (1, 1), (0, 0), (0, 0), (0, 0)))
    framed = framed + jnp.pad(last_third, ((0, 0), (2, 0), (0, 0), (0, 0), (0, 0)))
    own_grad = framed[:, 1:-1]
    for direction in (1, -1):
        rim_grad = framed[:, -1] if direction == 1 else framed[:, 0]
        arrived = from_behind(rim_grad.astype(jnp.bfloat16), SEQ, direction).astype(
            rim_grad.dtype
        )
        if direction == 1:
            own_grad = jnp.concatenate(
                [own_grad[:, :1] + arrived[:, None], own_grad[:, 1:]], axis=1
            )
        else:
            own_grad = jnp.concatenate(
                [own_grad[:, :-1], own_grad[:, -1:] + arrived[:, None]], axis=1
            )
    global_total, query_total = (
        lax.psum(
            global_back.reshape(windows, -1, BLOCK, head_count, doubled).astype(jnp.bfloat16), SEQ
        ).astype(jnp.float32),
        lax.psum(query_part.astype(jnp.bfloat16), SEQ).astype(jnp.float32),
    )
    own_grad = own_grad + exact_two("wgb,wgthe->wbthe", owned_hot, global_total)
    far_flat = far_back.reshape(windows, -1, BLOCK, doubled)
    returning = exact_two("wspc,wste->pwcte", picker, far_flat)
    arrived_far = lax.all_to_all(
        returning.astype(jnp.bfloat16), SEQ, split_axis=0, concat_axis=0, tiled=True
    ).astype(returning.dtype)
    own_grad = own_grad + exact_two("wqcbh,qwcte->wbthe", sender, arrived_far)
    return (own_grad.reshape(windows, blocks_dev * BLOCK, head_count, doubled), query_total)


def attention_back(
    grad_attended,
    queries,
    sliding,
    global_kv,
    distant,
    probabilities,
    key_part,
    value_part,
    global_queries,
    full_probs,
    sender,
    picker,
    owned_hot,
):
    head_dim = queries.shape[-1]
    score_scale = head_dim ** (-0.5)
    windows, blocks_dev, _, head_count, _ = queries.shape
    on_global = jnp.sum(owned_hot, axis=1)[:, :, None, None, None] > 0
    selected = mixed_sum("wgb,wbqhd->wgqhd", owned_hot.astype(jnp.bfloat16), grad_attended)
    rows_grad = lax.psum(selected.astype(jnp.bfloat16), SEQ).reshape(
        windows, -1, head_count, head_dim
    )
    grad_attended = jnp.where(on_global, jnp.zeros_like(grad_attended), grad_attended)
    low_probs = probabilities.astype(jnp.bfloat16)
    near_grad = mixed_sum("wbqhd,wbkhd->wbhqk", grad_attended, sliding[..., head_dim:])
    global_grad = mixed_sum("wbqhd,wkhd->wbhqk", grad_attended, global_kv[..., head_dim:])
    far_grad = mixed_sum("wbqhd,wbhrkd->wbhqrk", grad_attended, distant[..., head_dim:])
    far_grad = far_grad.reshape(windows, blocks_dev, head_count, BLOCK, -1)
    grad_probs = jnp.concatenate([near_grad, global_grad, far_grad], axis=4)
    grad_scores = probabilities * (
        grad_probs - jnp.sum(probabilities * grad_probs, axis=4, keepdims=True)
    )
    grad_scores = grad_scores.astype(jnp.bfloat16)
    near_split, global_split, far_split = split_keys(grad_scores, sliding, global_kv, distant)
    near_probs, global_probs, far_probs = split_keys(low_probs, sliding, global_kv, distant)
    grad_query = mixed_sum("wbhqk,wbkhd->wbqhd", near_split, sliding[..., :head_dim])
    grad_query = grad_query + mixed_sum(
        "wbhqk,wkhd->wbqhd", global_split, global_kv[..., :head_dim]
    )
    grad_query = (
        grad_query + mixed_sum("wbhqrk,wbhrkd->wbqhd", far_split, distant[..., :head_dim])
    ) * score_scale
    near_back = jnp.concatenate(
        [
            mixed_sum("wbhqk,wbqhd->wbkhd", near_split, queries) * score_scale,
            mixed_sum("wbhqk,wbqhd->wbkhd", near_probs, grad_attended),
        ],
        axis=4,
    )
    global_back = jnp.concatenate(
        [
            mixed_sum("wbhqk,wbqhd->wkhd", global_split, queries) * score_scale,
            mixed_sum("wbhqk,wbqhd->wkhd", global_probs, grad_attended),
        ],
        axis=3,
    )
    far_back = jnp.concatenate(
        [
            mixed_sum("wbhqrk,wbqhd->wbhrkd", far_split, queries) * score_scale,
            mixed_sum("wbhqrk,wbqhd->wbhrkd", far_probs, grad_attended),
        ],
        axis=5,
    )
    full_grad_probs = mixed_sum("wqhd,wkhd->whqk", rows_grad, value_part)
    partial_dot = jnp.sum(full_probs * full_grad_probs, axis=3, keepdims=True)
    row_dot = lax.psum(partial_dot, SEQ)
    full_grad_scores = (full_probs * (full_grad_probs - row_dot)).astype(jnp.bfloat16)
    query_part = mixed_sum("whqk,wkhd->wqhd", full_grad_scores, key_part) * score_scale
    full_key_grad = mixed_sum("whqk,wqhd->wkhd", full_grad_scores, global_queries) * score_scale
    full_value_grad = mixed_sum("whqk,wqhd->wkhd", full_probs.astype(jnp.bfloat16), rows_grad)
    grad_paired, query_total = return_blocks(
        near_back, global_back, far_back, query_part, sender, picker, owned_hot
    )
    grad_query = grad_query + exact_two(
        "wgb,wgqhd->wbqhd", owned_hot, query_total.reshape(windows, -1, BLOCK, head_count, head_dim)
    )
    grad_paired = grad_paired + jnp.concatenate([full_key_grad, full_value_grad], axis=3)
    return (grad_query, grad_paired)


def layer_backward(stored, grad_output, weights, tables):
    row_weights, down_weights, vector_weights = weights
    sender, picker, owned_hot, key_mask, full_mask = tables
    (
        hidden,
        normed,
        queries,
        sliding,
        global_kv,
        distant,
        probabilities,
        mixed_low,
        middle,
        normed_two,
        up_value,
        active,
        key_part,
        value_part,
        global_queries,
        full_probs,
    ) = stored
    model_width = row_weights.shape[0]
    windows, tokens, _ = hidden.shape
    blocks_dev = tokens // BLOCK
    head_dim = model_width // HEADS
    (
        gain_one,
        shift_one,
        bias_query,
        bias_value,
        bias_out,
        gain_two,
        shift_two,
        bias_down,
        bias_up,
    ) = split_vectors(vector_weights, model_width)
    grad_ffn = grad_output.astype(jnp.bfloat16)
    grad_bias_down = jnp.sum(grad_ffn.astype(jnp.float32), axis=(0, 1))
    grad_down = mixed_sum("wtf,wtd->fd", active, grad_ffn)
    grad_active = mixed_sum("wtd,fd->wtf", grad_ffn, down_weights)
    gelu_pull = jax.vjp(partial(jax.nn.gelu, approximate=False), up_value)[1]
    grad_up = gelu_pull(grad_active)[0].astype(jnp.bfloat16)
    grad_bias_up = jnp.sum(grad_up.astype(jnp.float32), axis=(0, 1))
    grad_in = mixed_sum("wtd,wtf->df", normed_two, grad_up)
    grad_normed_two = mixed_sum("wtf,df->wtd", grad_up, row_weights[:, 4 * model_width :])
    norm_pull_two = jax.vjp(norm_rows, middle, gain_two, shift_two)[1]
    grad_middle_norm, grad_gain_two, grad_shift_two = norm_pull_two(grad_normed_two)
    grad_middle = grad_output + grad_middle_norm
    grad_branch = grad_middle.astype(jnp.bfloat16)
    grad_bias_out = jnp.sum(grad_branch.astype(jnp.float32), axis=(0, 1))
    grad_out_weight = mixed_sum("wtd,wte->de", mixed_low, grad_branch)
    grad_attended = mixed_sum(
        "wte,de->wtd", grad_branch, row_weights[:, 3 * model_width : 4 * model_width]
    ).astype(jnp.bfloat16)
    grad_attended = grad_attended.reshape(windows, blocks_dev, BLOCK, HEADS, head_dim)
    grad_query, grad_paired = attention_back(
        grad_attended,
        queries,
        sliding,
        global_kv,
        distant,
        probabilities,
        key_part,
        value_part,
        global_queries,
        full_probs,
        sender,
        picker,
        owned_hot,
    )
    grad_projected = jnp.concatenate(
        [
            grad_query.reshape(windows, tokens, model_width),
            grad_paired[..., :head_dim].reshape(windows, tokens, model_width),
            grad_paired[..., head_dim:].reshape(windows, tokens, model_width),
        ],
        axis=2,
    ).astype(jnp.bfloat16)
    summed = jnp.sum(grad_projected.astype(jnp.float32), axis=(0, 1))
    grad_bias_query = summed[:model_width]
    grad_bias_value = summed[2 * model_width :]
    grad_projection = mixed_sum("wtd,wte->de", normed, grad_projected)
    grad_normed = mixed_sum("wte,de->wtd", grad_projected, row_weights[:, : 3 * model_width])
    norm_pull_one = jax.vjp(norm_rows, hidden, gain_one, shift_one)[1]
    grad_hidden_norm, grad_gain_one, grad_shift_one = norm_pull_one(grad_normed)
    grad_hidden = grad_middle + grad_hidden_norm
    grad_rows = jnp.concatenate([grad_projection, grad_out_weight, grad_in], axis=1)
    grad_vectors = jnp.concatenate(
        [
            grad_gain_one,
            grad_shift_one,
            grad_bias_query,
            grad_bias_value,
            grad_bias_out,
            grad_gain_two,
            grad_shift_two,
            grad_bias_down,
            grad_bias_up,
        ]
    )
    return (grad_hidden, (grad_rows, grad_down, grad_vectors))


def adam_update(master, first_old, second_old, gradient, step_rate, decay_rate):
    first_new = 0.5 * first_old + 0.5 * gradient
    second_new = 0.5 * second_old + 0.5 * gradient * gradient
    first_hat = first_new / (1.0 - 0.5**STEP)
    second_hat = second_new / (1.0 - 0.5**STEP)
    master_new = master - step_rate * (
        first_hat / (jnp.sqrt(second_hat) + 1e-08) + decay_rate * master
    )
    return (master_new, first_new, second_new)


def general_shards(
    block_input,
    cotangent,
    random_ids,
    segment_ids,
    global_ids,
    w_rows,
    w_rows_first,
    w_rows_second,
    w_down,
    w_down_first,
    w_down_second,
    vectors,
    vectors_first,
    vectors_second,
):
    section_index = lax.axis_index(SECTION)
    seq_place = lax.axis_index(SEQ)
    groups = lax.axis_size(SEQ)
    row_weights, down_weights, vector_low = (
        lax.all_gather(w_rows[0].astype(jnp.bfloat16), (DP, SEQ), axis=1, tiled=True),
        lax.all_gather(w_down[0].astype(jnp.bfloat16), (DP, SEQ), axis=0, tiled=True),
        lax.all_gather(vectors[0].astype(jnp.bfloat16), (DP, SEQ), axis=0, tiled=True),
    )
    weights = (row_weights, down_weights, vector_low.astype(jnp.float32))
    micro_count, windows, tokens, model_width = block_input.shape
    received = jnp.zeros((windows, tokens, model_width), jnp.bfloat16)
    results = jnp.zeros(block_input.shape, jnp.float32)
    full_totals = (
        jnp.zeros(row_weights.shape, jnp.float32),
        jnp.zeros(down_weights.shape, jnp.float32),
        jnp.zeros(vector_low.shape, jnp.float32),
    )

    def tick(tick_index, carry):
        received, results, full_totals = carry
        forward_mb = jnp.clip(tick_index - section_index, 0, micro_count - 1)
        behind_raw = tick_index - 2 + section_index
        behind = jnp.clip(behind_raw, 0, micro_count - 1)
        live_mask = ((behind_raw >= 0) & (behind_raw < micro_count)).astype(jnp.float32)
        tables_forward = route_tables(
            lax.dynamic_index_in_dim(random_ids, forward_mb, 0, keepdims=False),
            lax.dynamic_index_in_dim(segment_ids, forward_mb, 0, keepdims=False),
            lax.dynamic_index_in_dim(global_ids, forward_mb, 0, keepdims=False),
            seq_place,
            groups,
        )
        tables_behind = route_tables(
            lax.dynamic_index_in_dim(random_ids, behind, 0, keepdims=False),
            lax.dynamic_index_in_dim(segment_ids, behind, 0, keepdims=False),
            lax.dynamic_index_in_dim(global_ids, behind, 0, keepdims=False),
            seq_place,
            groups,
        )
        incoming_values = received.astype(jnp.float32)
        first_input = lax.dynamic_index_in_dim(block_input, forward_mb, 0, keepdims=False).astype(
            jnp.float32
        )
        forward_input = jnp.where(section_index == 0, first_input, incoming_values)
        forward_output = layer_forward(forward_input, weights, tables_forward)[0]
        back_source = lax.dynamic_index_in_dim(block_input, behind, 0, keepdims=False).astype(
            jnp.float32
        )
        back_input = jnp.where(section_index == 0, back_source, incoming_values)
        given_grad = lax.dynamic_index_in_dim(cotangent, behind, 0, keepdims=False).astype(
            jnp.float32
        )
        back_grad = jnp.where(section_index == 0, incoming_values, given_grad) * live_mask
        stored = layer_forward(back_input, weights, tables_behind)[1]
        grad_input, gradients = layer_backward(stored, back_grad, weights, tables_behind)
        outgoing = jnp.where(section_index == 0, forward_output, grad_input).astype(jnp.bfloat16)
        finished = jnp.where(section_index == 0, grad_input, forward_output)
        updated = lax.dynamic_update_index_in_dim(results, finished, behind, 0)
        results = jnp.where(live_mask > 0, updated, results)
        full_totals = tuple(
            (total_part + grad_part for total_part, grad_part in zip(full_totals, gradients))
        )
        return (partner(outgoing, SECTION, 0), results, full_totals)

    received, results, full_totals = lax.fori_loop(
        0, micro_count + 2, tick, (received, results, full_totals)
    )
    shard_totals = (
        lax.psum_scatter(full_totals[0], (DP, SEQ), scatter_dimension=1, tiled=True),
        lax.psum_scatter(full_totals[1], (DP, SEQ), scatter_dimension=0, tiled=True),
        lax.psum_scatter(full_totals[2], (DP, SEQ), scatter_dimension=0, tiled=True),
    )
    new_rows, new_rows_first, new_rows_second = adam_update(
        w_rows[0], w_rows_first[0], w_rows_second[0], shard_totals[0], rate_matrix, decay_matrix
    )
    new_down, new_down_first, new_down_second = adam_update(
        w_down[0], w_down_first[0], w_down_second[0], shard_totals[1], rate_matrix, decay_matrix
    )
    new_vectors, new_vectors_first, new_vectors_second = adam_update(
        vectors[0], vectors_first[0], vectors_second[0], shard_totals[2], rate_vector, 0.0
    )
    return (
        results[None],
        new_rows[None],
        new_rows_first[None],
        new_rows_second[None],
        new_down[None],
        new_down_first[None],
        new_down_second[None],
        new_vectors[None],
        new_vectors_first[None],
        new_vectors_second[None],
    )


LOW = jnp.bfloat16
LOG_HIGH = [float(np.log(c).astype(ml_dtypes.bfloat16)) for c in (1.0, 2.0, 3.0)]
LOG_LOW = [float(np.log(c)) - high for c, high in zip((1.0, 2.0, 3.0), LOG_HIGH)]
CHUNK = 256
VMEM_BYTES = 60 * 1024 * 1024


def dot_rows(left, right):
    return lax.dot_general(left, right, (((1,), (1,)), ((), ())), preferred_element_type=jnp.float32)


def dot_plain(left, right):
    return lax.dot_general(left, right, (((1,), (0,)), ((), ())), preferred_element_type=jnp.float32)


def dot_tokens(left, right):
    return lax.dot_general(left, right, (((0,), (0,)), ((), ())), preferred_element_type=jnp.float32)


def swap(value):
    return lax.ppermute(value, SECTION, [(0, 1), (1, 0)])


def normalized(values_in):
    row_mean = jnp.mean(values_in, axis=-1, keepdims=True)
    centred = values_in - row_mean
    spread = jnp.mean(centred * centred, axis=-1, keepdims=True)
    scale = lax.rsqrt(spread + epsilon)
    return centred * scale, scale


class Shares:
    def __init__(self, width, columns, depth, vector_len):
        self.width = width
        self.columns = columns
        self.depth = depth
        self.vector_len = vector_len
        self.half = columns // 2
        self.per = width // columns
        self.groups = columns // depth

    def unpack(self, gathered, core):
        rows, down, vec = gathered
        vec = vec.reshape(-1, TAIL, self.width)[:, 0, : self.vector_len].reshape(-1)
        pieces = split_vectors(vec.astype(jnp.float32), self.width)
        for index in (2, 3):
            pieces[index] = lax.dynamic_index_in_dim(
                pieces[index].reshape(self.per, 2, self.half), core, 1, keepdims=False
            ).reshape(-1)
        pieces[8] = lax.dynamic_index_in_dim(
            pieces[8].reshape(-1, 2, self.depth // 2), core, 1, keepdims=False
        ).reshape(-1)
        nothing = jnp.zeros_like(pieces[2])
        proj = [pieces[2], nothing, pieces[3], nothing]
        order = [pieces[index] for index in (0, 1, 4, 5, 6, 7)] + proj + [pieces[8]]
        return (
            (rows.reshape(-1, self.width), down.reshape(-1, self.width)),
            jnp.concatenate(order).reshape(-1, self.width),
        )

    def by_shard(self, grads, vector_grads, core):
        rows, down = grads
        half, per, width = self.half, self.per, self.width
        hot = (jnp.arange(2) == core).astype(jnp.float32)
        spread = list(vector_grads)
        for index in (2, 3):
            spread[index] = (
                spread[index].reshape(per, 1, half) * hot[None, :, None]
            ).reshape(-1)
        spread[8] = (spread[8].reshape(-1, 1, self.depth // 2) * hot[None, :, None]).reshape(-1)
        for index in (0, 1, 4, 5, 6, 7):
            spread[index] = spread[index] * hot[0]
        vec = jnp.concatenate(spread).reshape(-1, 1, self.vector_len)
        vec = jnp.pad(vec, ((0, 0), (0, TAIL - 1), (0, width - self.vector_len))).astype(LOW)
        return [array.reshape(2, 2, 4, -1, width) for array in (rows, down, vec)]


MESH = pl.DeviceIdType.MESH
PIECE = 48
TAIL = 16


def prepare_kernel(shares, rows_ref, down_ref, vector_ref, rows_out, down_out, vector_out):
    core = lax.axis_index(SECTION)
    offset = lax.axis_index((DP, SEQ)) * shares.columns
    half, per, width, depth = shares.half, shares.per, shares.width, shares.depth // 2
    is_inner = (offset >= 3 * width) & (offset < 4 * width)
    is_hidden = offset >= 4 * width

    @pl.when(is_inner)
    def _():
        for which in range(2):
            side = core if which == 0 else 1 - core
            held = [rows_ref[pl.ds((2 * j + side) * half, half), :] for j in range(per)]
            turned = jnp.transpose(jnp.concatenate(held, axis=0))
            rows_out[which] = jnp.concatenate([turned[:half], turned[half:]], axis=1).astype(LOW)

    @pl.when(jnp.logical_not(is_inner))
    def _():
        turned = jnp.transpose(rows_ref[...]).astype(LOW)
        plain = [turned[:half], turned[half:]]
        hidden = [
            jnp.concatenate(
                [turned[(2 * j + side) * depth :][:depth] for j in range(shares.groups)], axis=0
            )
            for side in range(2)
        ]
        halves = [jnp.where(is_hidden, b, a) for a, b in zip(plain, hidden)]
        rows_out[0] = jnp.where(core == 0, halves[0], halves[1])
        rows_out[1] = jnp.where(core == 0, halves[1], halves[0])

    down = down_ref[...].astype(LOW)
    down_out[0] = jnp.where(core == 0, down[:depth], down[depth:])
    down_out[1] = jnp.where(core == 0, down[depth:], down[:depth])
    vector_out[...] = jnp.zeros_like(vector_out)
    vector_out[0:1, : shares.vector_len] = vector_ref[...].astype(LOW)


def prepare(shares, rows, down, vector):
    return pl.pallas_call(
        partial(prepare_kernel, shares),
        out_shape=[
            jax.ShapeDtypeStruct((2, shares.half, shares.width), LOW),
            jax.ShapeDtypeStruct((2, shares.depth // 2, shares.width), LOW),
            jax.ShapeDtypeStruct((TAIL, shares.width), LOW),
        ],
        compiler_params=pltpu.CompilerParams(vmem_limit_bytes=VMEM_BYTES),
    )(rows, down, vector)


class Place:
    def __init__(self):
        self.core = lax.axis_index(SECTION)
        self.dp = lax.axis_index(DP)
        self.z = lax.axis_index(SEQ)
        self.y, self.x = self.dp // 2, self.dp % 2
        self.high, self.low = self.z // 2, self.z % 2
        self.inner = self.high + self.low == 1
        self.outer = self.high + self.low != 1
        self.partner = {SECTION: 1 - self.core}
        self.along_x = {DP: 2 * self.y + 1 - self.x}
        self.along_y = {DP: 2 * (1 - self.y) + self.x}
        self.across = {SEQ: 3 - self.z}
        self.beside = {SEQ: 2 * self.high + 1 - self.low}
        self.others = [{SEQ: (self.z + by) % 4} for by in (1, 2, 3)]
        self.own = pl.ds(self.z, 1)
        self.next = pl.ds(2 * self.high + 1 - self.low, 1)
        self.near = pl.ds(2 * self.high, 2)
        self.far = pl.ds(2 * (1 - self.high), 2)

    def greet(self):
        barrier = pltpu.get_barrier_semaphore()
        everyone = [self.partner, self.along_x, self.along_y] + self.others
        for device in everyone:
            pl.semaphore_signal(barrier, inc=1, device_id=device, device_id_type=MESH)
        pl.semaphore_wait(barrier, len(everyone))


def remote(src, dst, sems, spots, device):
    return pltpu.make_async_remote_copy(
        src_ref=src,
        dst_ref=dst,
        send_sem=sems[0].at[spots[0]],
        recv_sem=sems[1].at[spots[1]],
        device_id=device,
        device_id_type=MESH,
    )


def chunk_pairs(shares):
    pairs = []
    for array, length in ((0, shares.half), (1, shares.depth // 2)):
        for start in range(0, length, 2 * PIECE):
            pairs.append([(array, start, PIECE, 0), (array, start + PIECE, PIECE, 1)])
    pairs[0].append((2, 0, TAIL, 0))
    return pairs


def quad_pairs(shares):
    length = (shares.half + shares.depth // 2) // 2
    pairs = [
        [(0, start, PIECE, None), (1, start, PIECE, None)] for start in range(0, length, PIECE)
    ]
    pairs[0].append((2, 0, TAIL, 0))
    return pairs


def gather_kernel(shares, *refs):
    (rows_in, down_in, vector_in, x_in, cot_in), refs = refs[:5], refs[5:]
    outs, refs = [refs[0:3], refs[3:6]], refs[6:]
    (x_out, cot_out), refs = refs[:2], refs[2:]
    local, swap_send, swap_recv, z_send, z_recv, send, recv = refs
    here = Place()
    core, y, x, z = here.core, here.y, here.x, here.z
    half = x_in.shape[2] // 2
    rows_half, down_half = shares.half // 2, shares.depth // 4
    here.greet()

    def slices(source, target, base):
        mine = pl.ds(pl.multiple_of(core * half, half), half)
        sems = (z_send, z_recv)
        own = pltpu.make_async_copy(
            source.at[z, 0, mine], target.at[z, core], local.at[8 + base // 4]
        )
        sends, arrivals = [], []
        for by in (1, 2, 3):
            spots = (base + by - 1, base + by - 1)
            device = here.others[by - 1]
            sends.append(
                remote(source.at[(z + by) % 4, 0, mine], target.at[z, core], sems, spots, device)
            )
            arrivals.append(
                remote(
                    source.at[z, 0, mine], target.at[(z + 4 - by) % 4, core], sems, spots, device
                )
            )
        spots = (base + 3, base + 3)
        forward = remote(target.at[:, core], target.at[:, core], sems, spots, here.partner)
        arrived = remote(target.at[:, 1 - core], target.at[:, 1 - core], sems, spots, here.partner)
        return own, sends, arrivals, forward, arrived

    x_moves = slices(x_in, x_out, 0)
    cot_moves = slices(cot_in, cot_out, 4)

    def open_slices(moves):
        moves[0].start()
        for copy in moves[1]:
            copy.start()

    def pass_slices(moves):
        moves[0].wait()
        for copy in moves[2]:
            copy.wait_recv()
        moves[3].start()

    def close_slices(moves):
        for copy in moves[1]:
            copy.wait_send()
        moves[3].wait_send()
        moves[4].wait_recv()

    def first_moves(layer, which):
        down = down_in.at[which]
        rows = rows_in.at[which]
        if layer == 0:
            return [
                (0, rows, outs[0][0].at[y, x, z]),
                (1, down, outs[0][1].at[y, x, z]),
                (2, vector_in, outs[0][2].at[y, x, z]),
            ]
        moves = [(7, vector_in, outs[1][2].at[y, x, z])]
        for part in range(2):
            target = outs[1][part]
            moves.append(
                (
                    3 + 2 * part,
                    rows.at[pl.ds(part * rows_half, rows_half)],
                    target.at[z, pl.ds(0, rows_half)],
                )
            )
            moves.append(
                (
                    4 + 2 * part,
                    down.at[pl.ds(part * down_half, down_half)],
                    target.at[z, pl.ds(rows_half, down_half)],
                )
            )
        return moves

    swaps = (swap_send, swap_recv)
    for layer in range(2):

        @pl.when(core == layer)
        def _():
            across = [
                remote(src, dst, swaps, (spot, spot), here.partner)
                for spot, src, dst in first_moves(layer, 1)
            ]
            own = [
                pltpu.make_async_copy(src, dst, local.at[spot])
                for spot, src, dst in first_moves(layer, 0)
            ]
            for copy in across + own:
                copy.start()
            for copy in own:
                copy.wait()
            for copy in across:
                copy.wait_send()
            for spot, src, dst in first_moves(1 - layer, 0):
                remote(src, dst, swaps, (spot, spot), here.partner).wait_recv()

    numbers, pairs = {}, []
    for layer in range(2):
        for pair in chunk_pairs(shares) if layer == 0 else quad_pairs(shares):
            entry = []
            for array, start, length, order in pair:
                ref = outs[layer][array]
                rows = pl.ds(start, length)
                flat = order is None
                number = len(numbers)
                sems = (send, recv)

                def part(which):
                    return ref.at[which, rows] if flat else ref.at[y, x, which, rows]

                def copy(piece, spots, device):
                    return remote(piece, piece, sems, ((number, spots[0]), (number, spots[1])), device)

                steps = {
                    "z": copy(part(here.own), (0, 0), here.beside),
                    "across": copy(part(here.near), (1, 1), here.across),
                    "on": copy(part(here.far), (4, 1), here.beside),
                }
                arrive = [
                    copy(part(here.next), (0, 0), here.beside),
                    copy(part(here.far), (1, 1), here.across),
                ]
                if order == 0:
                    steps["one"] = copy(ref.at[y, x, :, rows], (2, 2), here.along_y)
                    steps["two"] = copy(ref.at[:, x, :, rows], (3, 3), here.along_x)
                    arrive.append(copy(ref.at[1 - y, x, :, rows], (2, 2), here.along_y))
                    arrive.append(copy(ref.at[:, 1 - x, :, rows], (3, 3), here.along_x))
                elif order == 1:
                    steps["one"] = copy(ref.at[y, x, :, rows], (2, 2), here.along_x)
                    steps["two"] = copy(ref.at[y, :, :, rows], (3, 3), here.along_y)
                    arrive.append(copy(ref.at[y, 1 - x, :, rows], (2, 2), here.along_x))
                    arrive.append(copy(ref.at[1 - y, :, :, rows], (3, 3), here.along_y))
                numbers[number] = (steps, arrive)
                entry.append(number)
            pairs.append(entry)

    def issue(name, entry):
        after = {"z": None, "across": 0, "on": 1, "one": 1, "two": 2}[name]

        def start():
            for number in entry:
                steps, arrive = numbers[number]
                if name in steps:
                    if after is not None and not (name == "one"):
                        arrive[after].wait_recv()
                    steps[name].start()

        if name in ("across", "on"):
            pl.when(here.inner)(start)
        else:
            start()

    def arrived(entry, index, where):
        def wait():
            for number in entry:
                numbers[number][1][index].wait_recv()

        pl.when(where)(wait)

    first, second = pairs[: len(chunk_pairs(shares))], pairs[len(chunk_pairs(shares)) :]
    for entry in first:
        issue("z", entry)
    for entry in first:
        issue("across", entry)
        arrived(entry, 0, here.outer)
    for entry in first[:-1]:
        issue("on", entry)
        arrived(entry, 1, here.outer)
        issue("one", entry)
    issue("on", first[-1])
    for entry in second:
        issue("z", entry)
    open_slices(x_moves)
    arrived(first[-1], 1, here.outer)
    issue("one", first[-1])
    issue("two", first[0])
    for entry in second:
        issue("across", entry)
        arrived(entry, 0, here.outer)
    issue("two", first[1])
    open_slices(cot_moves)
    for entry in second:
        issue("on", entry)
    issue("two", first[2])
    pass_slices(x_moves)
    for entry in second:
        arrived(entry, 1, here.outer)
        for number in entry:
            steps, arrive = numbers[number]
            if "one" in steps:
                steps["one"].start()
                arrive[2].wait_recv()
                steps["two"].start()
    pass_slices(cot_moves)
    for steps, arrive in numbers.values():
        if len(arrive) == 4:
            arrive[3].wait_recv()
        for name in steps:
            if name not in ("across", "on"):
                steps[name].wait_send()

    @pl.when(here.inner)
    def _():
        for steps, _ in numbers.values():
            steps["across"].wait_send()
            steps["on"].wait_send()

    close_slices(x_moves)
    close_slices(cot_moves)


def gather(shares, prepared, block_input, cotangent):
    micro, _, tokens, width = block_input.shape
    chunks = sum(len(pair) for pair in chunk_pairs(shares) + quad_pairs(shares))
    lengths = (shares.half, shares.depth // 2, TAIL)
    layer = [jax.ShapeDtypeStruct((2, 2, 4, rows, width), LOW) for rows in lengths]
    quad = jax.ShapeDtypeStruct((4, (lengths[0] + lengths[1]) // 2, width), LOW)
    window = jax.ShapeDtypeStruct((micro, 2, tokens // 2, width), LOW)
    anywhere = pl.BlockSpec(memory_space=pl.ANY)
    results = pl.pallas_call(
        partial(gather_kernel, shares),
        in_specs=[pl.BlockSpec(memory_space=pltpu.VMEM)] * 3 + [anywhere] * 2,
        out_specs=[anywhere] * 8,
        out_shape=layer + [quad, quad, layer[2]] + [window, window],
        scratch_shapes=[
            pltpu.SemaphoreType.DMA((10,)),
            pltpu.SemaphoreType.DMA((8,)),
            pltpu.SemaphoreType.DMA((8,)),
            pltpu.SemaphoreType.DMA((8,)),
            pltpu.SemaphoreType.DMA((8,)),
            pltpu.SemaphoreType.DMA((chunks, 5)),
            pltpu.SemaphoreType.DMA((chunks, 4)),
        ],
        compiler_params=pltpu.CompilerParams(
            collective_id=0, has_side_effects=True, vmem_limit_bytes=VMEM_BYTES
        ),
    )(*prepared, block_input, cotangent)
    return results[0:3], results[3:6], results[6], results[7]


def over(value, bit):
    return lax.ppermute(value, DP, [(i, i ^ bit) for i in range(4)])


def layout_moves(shares, y, x, pieces, arrays):
    rows_half, down_half = shares.half // 2, shares.depth // 4
    moves = []
    for part in range(2):
        for index, (by_y, by_x) in enumerate(((0, 0), (1, 0), (0, 1), (1, 1))):
            piece = pieces[part][index]
            at_y, at_x = y ^ by_y, x ^ by_x
            for array, length, start in ((0, rows_half, 0), (1, down_half, rows_half)):
                moves.append(
                    (
                        piece.at[:, pl.ds(start, length)],
                        arrays[array].at[at_y, at_x, :, pl.ds(part * length, length)],
                    )
                )
    return moves


def layout_kernel(shares, joins, *refs):
    dp = lax.axis_index(DP)
    if joins:
        pieces, arrays = [refs[0:4], refs[4:8]], refs[8:10]
    else:
        arrays, pieces = refs[0:2], [refs[2:6], refs[6:10]]
    for spot in range(4):

        @pl.when(dp == spot)
        def _():
            for piece, place in layout_moves(shares, spot // 2, spot % 2, pieces, arrays):
                src, dst = (piece, place) if joins else (place, piece)
                dst[...] = src[...]


def layout(shares, joins, *arrays):
    half, depth, width = shares.half, shares.depth // 2, shares.width
    length = (half + depth) // 2
    merged_specs = [
        pl.BlockSpec((2, 2, 1, rows, width), lambda z: (0, 0, z, 0, 0)) for rows in (half, depth)
    ]
    merged_shapes = [(2, 2, 4, rows, width) for rows in (half, depth)]
    piece_specs = [pl.BlockSpec((1, length, width), lambda z: (z, 0, 0))] * 8
    piece_shapes = [(4, length, width)] * 8
    return pl.pallas_call(
        partial(layout_kernel, shares, joins),
        grid=(4,),
        in_specs=piece_specs if joins else merged_specs,
        out_specs=merged_specs if joins else piece_specs,
        out_shape=[
            jax.ShapeDtypeStruct(shape, LOW) for shape in (merged_shapes if joins else piece_shapes)
        ],
        compiler_params=pltpu.CompilerParams(vmem_limit_bytes=VMEM_BYTES),
        cost_estimate=pl.CostEstimate(
            flops=0, bytes_accessed=64 * (half + depth) * width, transcendentals=0
        ),
    )(*arrays)


def tied(value, flying):
    return lax.optimization_barrier((value, flying))


def spread_quads(shares, quads):
    low, high = quads
    flying = (low, high, over(low, 2), over(high, 1))
    low, high, low_y, high_x = yield flying
    flying = (low_y, high_x, over(low, 1), over(high, 2))
    low_y, high_x, low_x, high_y = yield flying
    flying = (over(low_y, 1), over(high_x, 2))
    low_both, high_both = yield flying
    yield layout(shares, True, low, low_y, low_x, low_both, high, high_y, high_x, high_both)


def sum_quads(shares, arrays):
    pieces = layout(shares, False, *arrays)

    def total(*terms):
        return sum(term.astype(jnp.float32) for term in terms).astype(LOW)

    low, low_y, low_x, low_both = pieces[:4]
    high, high_y, high_x, high_both = pieces[4:]
    flying = (low_x, high_y, over(low_both, 1), over(high_both, 2))
    low_x, high_y, low_hop, high_hop = yield flying
    low_y, high_x = low_y + low_hop, high_x + high_hop
    flying = (low_y, high_x, over(low_x, 1), over(high_y, 2))
    low_y, high_x, low_x, high_y = yield flying
    flying = (over(low_y, 2), over(high_x, 1))
    low_y, high_x = yield flying
    yield (total(low, low_x, low_y), total(high, high_x, high_y))


class Beside:
    def __init__(self, hops=None):
        self.hops = hops
        self.flying = None if hops is None else next(hops)

    def tie(self, value):
        if self.hops is None:
            return value
        value, arrived = tied(value, self.flying)
        self.flying = self.hops.send(arrived)
        return value


def scatter_kernel(shares, *refs):
    (rows_zero, down, vec_zero, low, high, vec_one), refs = refs[:6], refs[6:]
    (dx_ref, final_ref, halves, slices), refs = refs[:4], refs[4:]
    work, refs = [refs[0:3], refs[3:6]], refs[6:]
    (got_one, got_two, got_far, got_across, got_near, total), refs = refs[:6], refs[6:]
    load, local, swap_send, swap_recv, z_send, z_recv, send, recv = refs
    here = Place()
    core, y, x, z = here.core, here.y, here.x, here.z
    rows_half, down_half = shares.half // 2, shares.depth // 4
    down_base = shares.half
    tail_base = shares.half + shares.depth // 2

    moves = [
        [(rows_zero, work[0][0]), (down, work[0][1]), (vec_zero, work[0][2])],
        [(low, work[1][0]), (high, work[1][1]), (vec_one, work[1][2])],
    ]
    loads = [
        [
            pltpu.make_async_copy(src, dst, load.at[layer, index])
            for index, (src, dst) in enumerate(moves[layer])
        ]
        for layer in range(2)
    ]
    for layer in (1, 0):
        for copy in loads[layer]:
            copy.start()
    here.greet()

    def place_of(layer, array, start):
        if array == 2:
            return tail_base
        if layer == 0:
            return (0, down_base)[array] + start
        if start < rows_half:
            return array * rows_half + start
        return down_base + array * down_half + start - rows_half

    pairs, chunks = [], []
    for layer in (1, 0):
        for index, pair in enumerate(quad_pairs(shares) if layer else chunk_pairs(shares)):
            entry = []
            for array, start, length, order in pair:
                entry.append((len(chunks), layer, array, start, length, order))
                chunks.append(entry[-1])
            pairs.append((index, entry))

    def pieces(chunk):
        number, layer, array, start, length, order = chunk
        ref = work[layer][array]
        rows = pl.ds(start, length)
        sems = (send, recv)
        keeps, slots, copies = [], [], []

        def part(which):
            return ref.at[which, rows] if order is None else ref.at[y, x, which, rows]

        def add(src, slot, device, keep):
            spots = (number, len(copies))
            copies.append(remote(src, slot, sems, (spots, spots), device))
            slots.append(slot)
            keeps.append(keep)

        room = pl.ds(0, length)
        if order == 0:
            add(ref.at[:, 1 - x, :, rows], got_one.at[number, :, :, room], here.along_x, ref.at[:, x, :, rows])
            add(ref.at[1 - y, x, :, rows], got_two.at[number, :, room], here.along_y, ref.at[y, x, :, rows])
        elif order == 1:
            add(ref.at[1 - y, :, :, rows], got_one.at[number, :, :, room], here.along_y, ref.at[y, :, :, rows])
            add(ref.at[y, 1 - x, :, rows], got_two.at[number, :, room], here.along_x, ref.at[y, x, :, rows])
        else:
            copies, slots, keeps = [None] * 2, [None] * 2, [None] * 2
        add(part(here.far), got_far.at[number, :, room], here.beside, part(here.far))
        add(part(here.far), got_across.at[number, :, room], here.across, part(here.near))
        add(part(here.next), got_near.at[number, :, room], here.beside, part(here.own))
        return copies, keeps, slots

    built = [pieces(chunk) for chunk in chunks]
    loaded = set()

    def land(number, phase):
        copies, keeps, slots = built[number]
        copies[phase].wait_recv()
        keep, slot = keeps[phase], slots[phase]
        keep[...] = keep[...] + slot[...]

    def run(chunk, phase):
        number, layer, array, start, length, order = chunk
        copies, keeps, slots = built[number]
        if (layer, array) not in loaded:
            loaded.add((layer, array))
            loads[layer][array].wait()
        if phase < 2:
            if order is not None:
                if phase:
                    land(number, 0)
                copies[phase].start()
        elif phase == 2:
            if order is not None:
                land(number, 1)

            @pl.when(here.outer)
            def _():
                copies[2].start()
                copies[4].start()

        elif phase == 3:

            @pl.when(here.inner)
            def _():
                land(number, 2)
                copies[3].start()

        elif phase == 4:

            @pl.when(here.inner)
            def _():
                land(number, 3)
                copies[4].start()

        else:
            copies[4].wait_recv()
            spot = pl.ds(place_of(layer, array, start), length)
            total[layer, spot, :] = (keeps[4][...] + slots[4][...])[0]

    def step(entry, phase):
        for chunk in entry:
            run(chunk, phase)

    second = [entry for _, entry in pairs[: len(quad_pairs(shares))]]
    first = [entry for _, entry in pairs[len(quad_pairs(shares)) :]]
    tails = [chunk for entry in second for chunk in entry if chunk[5] is not None]
    second = [[chunk for chunk in entry if chunk[5] is None] for entry in second]
    first[0] = first[0] + tails
    step(first[0], 0)
    step(first[1], 0)
    for entry in second:
        step(entry, 2)
    step(first[0], 1)
    for section, source in ((0, dx_ref), (1, final_ref)):

        @pl.when(core == section)
        def _():
            pltpu.make_async_copy(source.at[z], slices.at[z], local.at[0]).start()
            for by in (1, 2, 3):
                remote(
                    source.at[(z + by) % 4],
                    slices.at[z],
                    (z_send, z_recv),
                    (by - 1, by - 1),
                    here.others[by - 1],
                ).start()

    for entry in second:
        step(entry, 3)
    step(first[2], 0)
    step(first[1], 1)
    for entry in second:
        step(entry, 4)
    step(first[0], 2)
    step(first[2], 1)
    for entry in second:
        step(entry, 5)
    step(first[0], 3)
    step(first[1], 2)
    step(first[0], 4)
    step(first[1], 3)
    step(first[2], 2)
    step(first[1], 4)
    step(first[2], 3)
    step(first[2], 4)
    for entry in first:
        step(entry, 5)

    for copies, _, _ in built:
        for index in (0, 1, 4):
            if copies[index] is not None:
                copies[index].wait_send()
    for section, index in ((here.outer, 2), (here.inner, 3)):

        @pl.when(section)
        def _():
            for copies, _, _ in built:
                copies[index].wait_send()

    swaps = (swap_send, swap_recv)
    across = remote(total.at[1 - core], halves.at[core], swaps, (0, 0), here.partner)
    across.start()
    own = pltpu.make_async_copy(total.at[core], halves.at[core], local.at[1])
    own.start()
    own.wait()
    across.wait_send()
    remote(total.at[1 - core], halves.at[1 - core], swaps, (0, 0), here.partner).wait_recv()
    pltpu.make_async_copy(dx_ref.at[z], slices.at[z], local.at[0]).wait()
    for by in (1, 2, 3):
        copy = remote(
            dx_ref.at[z],
            slices.at[(z + 4 - by) % 4],
            (z_send, z_recv),
            (by - 1, by - 1),
            here.others[by - 1],
        )
        copy.wait_send()
        copy.wait_recv()


def scatter(shares, arrays, vec_zero, quads, vec_one, grad, final):
    micro, tokens, width = grad.shape
    lengths = (shares.half, shares.depth // 2, TAIL)
    chunks = sum(len(pair) for pair in chunk_pairs(shares) + quad_pairs(shares))
    rows = sum(lengths)
    anywhere = pl.BlockSpec(memory_space=pl.ANY)
    work = [pltpu.VMEM((2, 2, 4, length, width), LOW) for length in lengths]
    quad = pltpu.VMEM((4, (lengths[0] + lengths[1]) // 2, width), LOW)
    return pl.pallas_call(
        partial(scatter_kernel, shares),
        in_specs=[anywhere] * 8,
        out_specs=[anywhere] * 2,
        out_shape=[
            jax.ShapeDtypeStruct((2, rows, width), LOW),
            jax.ShapeDtypeStruct((micro, tokens, width), LOW),
        ],
        scratch_shapes=work
        + [quad, quad, work[2]]
        + [
            pltpu.VMEM((chunks, 2, 4, PIECE, width), LOW),
            pltpu.VMEM((chunks, 4, PIECE, width), LOW),
            pltpu.VMEM((chunks, 2, PIECE, width), LOW),
            pltpu.VMEM((chunks, 2, PIECE, width), LOW),
            pltpu.VMEM((chunks, 1, PIECE, width), LOW),
            pltpu.VMEM((2, rows, width), LOW),
            pltpu.SemaphoreType.DMA((2, 3)),
            pltpu.SemaphoreType.DMA((2,)),
            pltpu.SemaphoreType.DMA((1,)),
            pltpu.SemaphoreType.DMA((1,)),
            pltpu.SemaphoreType.DMA((3,)),
            pltpu.SemaphoreType.DMA((3,)),
            pltpu.SemaphoreType.DMA((chunks, 5)),
            pltpu.SemaphoreType.DMA((chunks, 5)),
        ],
        compiler_params=pltpu.CompilerParams(
            collective_id=1, has_side_effects=True, vmem_limit_bytes=VMEM_BYTES
        ),
    )(*arrays, vec_zero, *quads, vec_one, grad, final)


def update_kernel(shares, halves_ref, slices_ref, *refs):
    old, new, result_ref, turned = refs[:9], refs[9:18], refs[18], refs[19]
    result_ref[...] = slices_ref[...].astype(jnp.float32)
    offset = lax.axis_index((DP, SEQ)) * shares.columns
    half, per, width, depth = shares.half, shares.per, shares.width, shares.depth // 2
    is_inner = (offset >= 3 * width) & (offset < 4 * width)
    is_hidden = offset >= 4 * width

    @pl.when(is_inner)
    def _():
        for side in range(2):
            piece = halves_ref[side, :half, :].astype(jnp.float32)
            wide = per * half
            back = jnp.transpose(jnp.concatenate([piece[:, :wide], piece[:, wide:]], axis=0))
            for j in range(per):
                turned[(2 * j + side) * half : (2 * j + side + 1) * half, :] = back[
                    j * half : (j + 1) * half
                ]

    @pl.when(jnp.logical_not(is_inner))
    def _():
        pair = [halves_ref[side, :half, :].astype(jnp.float32) for side in range(2)]
        plain = jnp.concatenate(pair, axis=0)
        hidden = jnp.concatenate(
            [pair[side][j * depth :][:depth] for j in range(shares.groups) for side in range(2)],
            axis=0,
        )
        turned[...] = jnp.transpose(jnp.where(is_hidden, hidden, plain))

    def store(first, gradient, rate, decay):
        results = adam_update(*[ref[...] for ref in old[first : first + 3]], gradient, rate, decay)
        for ref, result in zip(new[first : first + 3], results):
            ref[...] = result

    store(0, turned[...], rate_matrix, decay_matrix)
    down = [halves_ref[side, half : half + depth, :] for side in range(2)]
    store(3, jnp.concatenate(down, axis=0).astype(jnp.float32), rate_matrix, decay_matrix)
    tails = [halves_ref[side, half + depth :, :].astype(jnp.float32) for side in range(2)]
    store(6, (tails[0] + tails[1])[0:1, : shares.vector_len], rate_vector, 0.0)


def update(shares, halves, slices, old):
    return pl.pallas_call(
        partial(update_kernel, shares),
        out_shape=[jax.ShapeDtypeStruct(piece.shape, jnp.float32) for piece in (*old, slices)],
        scratch_shapes=[pltpu.VMEM((shares.width, shares.columns), jnp.float32)],
        compiler_params=pltpu.CompilerParams(vmem_limit_bytes=VMEM_BYTES),
    )(halves, slices, *old)


(GAIN_ONE, SHIFT_ONE, BIAS_OUT, GAIN_TWO, SHIFT_TWO, BIAS_DOWN, BIAS_PROJ, _, BIAS_UP, _) = [
    slice(row, row + 1) for row in range(10)
]
ROWS = 256
COLS = 384
WIDE = 512
STRIP = 32


def whole(shape):
    return pl.BlockSpec(shape, lambda i: (0,) * len(shape))


def row_block(width):
    return pl.BlockSpec((ROWS, width), lambda i: (i, 0))


def col_block(tokens):
    return pl.BlockSpec((tokens, COLS), lambda i: (0, i))


def at_block(shape, *index):
    return pl.BlockSpec(shape, lambda i: index)


def params_of(flops, moved, transcendentals=0):
    return {
        "compiler_params": pltpu.CompilerParams(vmem_limit_bytes=VMEM_BYTES),
        "cost_estimate": pl.CostEstimate(
            flops=flops, bytes_accessed=moved, transcendentals=transcendentals
        ),
    }


def strips(length=ROWS, strip=STRIP):
    return [slice(first, first + strip) for first in range(0, length, strip)]


def both(own_ref, recv_ref, rows):
    return own_ref[rows, :].astype(jnp.float32) + recv_ref[rows, :].astype(jnp.float32)


def bias_of(vec_ref, first, start, length):
    row, width = first.start, vec_ref.shape[1]
    pieces = []
    for place in range(2):
        low = max(start - place * width, 0)
        high = min(start + length - place * width, width)
        if low < high:
            pieces.append(vec_ref[row + place : row + place + 1, low:high])
    return pieces[0] if len(pieces) == 1 else jnp.concatenate(pieces, axis=1)


def eights(values):
    rows, width = values.shape
    return jnp.sum(values.reshape(rows // 8, 8, width), axis=0)


def features_kernel(shares, random_ref, segment_ref, global_ref, query_ref, key_ref, turned_ref):
    core = lax.axis_index(SECTION)
    place = lax.axis_index(SEQ)
    blocks = random_ref.shape[1]
    width = key_ref.shape[1]
    heads = query_ref.shape[0]
    per_half = heads // shares.per
    picks = random_ref.shape[2] // (2 * heads)
    tokens = key_ref.shape[0]
    lane = lax.broadcasted_iota(jnp.int32, (blocks, width), 1)
    row = lax.broadcasted_iota(jnp.int32, (blocks, width), 0)
    key = jnp.where(lane < blocks, lane, lane - blocks)
    chosen = random_ref[place]
    named = global_ref[place]
    always = (jnp.abs(row - key) <= 1).astype(jnp.int32)
    is_global = jnp.zeros((blocks, width), jnp.int32)
    for index in range(named.shape[1]):
        spot = named[:, index : index + 1]
        always = always + (key == spot).astype(jnp.int32)
        is_global = is_global + (row == spot).astype(jnp.int32)
    line = segment_ref[place].astype(jnp.float32)
    column = jnp.transpose(jnp.broadcast_to(line, (8, tokens)))[:, 0:1]
    token_lane = lax.broadcasted_iota(jnp.int32, (tokens, width), 1)
    same = column == (token_lane - 2 * blocks).astype(jnp.float32)
    in_segment = (token_lane >= 2 * blocks) & (token_lane < 2 * blocks + 3)
    segment_side = jnp.where(in_segment & same, 1.0, 0.0)
    for head in range(heads):
        count = always
        for pick in range(picks):
            at = [
                (2 * per_half * (head // per_half) + per_half * side + head % per_half) * picks
                + pick
                for side in range(2)
            ]
            spot = jnp.where(core == 0, chosen[:, at[0] : at[0] + 1], chosen[:, at[1] : at[1] + 1])
            count = count + (key == spot).astype(jnp.int32)
        count = jnp.where(is_global > 0, 1, count)
        high = jnp.where(count == 0, masked, 0.0)
        low = jnp.zeros_like(high)
        for times in (2, 3):
            high = jnp.where(count == times, LOG_HIGH[times - 1], high)
            low = jnp.where(count == times, LOG_LOW[times - 1], low)
        table = jnp.where(lane < blocks, high, jnp.where(lane < 2 * blocks, low, 0.0))
        for block in range(blocks):
            rows = slice(block * BLOCK, (block + 1) * BLOCK)
            query_ref[head, rows, :] = (table[block : block + 1] + segment_side[rows]).astype(LOW)
    token_block = lax.shift_right_logical(
        lax.broadcasted_iota(jnp.int32, (tokens, width), 0), BLOCK.bit_length() - 1
    )
    here = (token_block == token_lane) | (token_block == token_lane - blocks)
    side = jnp.where(here & (token_lane < 2 * blocks), 1.0, 0.0)
    side = jnp.where(in_segment & jnp.logical_not(same), masked, side)
    ones = (token_lane >= 2 * blocks + 3) & (token_lane < 2 * blocks + 6)
    side = jnp.where(ones, 1.0, side)
    key_ref[...] = side.astype(LOW)
    turned_ref[...] = jnp.transpose(side).astype(LOW)


def key_features(shares, random_ids, segment_ids, global_ids):
    micro, _, blocks, head_count, picks = random_ids.shape
    tokens = segment_ids.shape[2]
    width = -(-(2 * blocks + 6) // 128) * 128
    return pl.pallas_call(
        partial(features_kernel, shares),
        out_shape=[
            jax.ShapeDtypeStruct((head_count // 2, tokens, width), LOW),
            jax.ShapeDtypeStruct((tokens, width), LOW),
            jax.ShapeDtypeStruct((width, tokens), LOW),
        ],
        **params_of(0, head_count * tokens * width),
    )(random_ids.reshape(micro, blocks, head_count * picks), segment_ids, global_ids)


def project_kernel(joins, *refs):
    if joins:
        (middle_ref, part_ref, recv_ref, before_ref), refs = refs[:4], refs[4:]
    else:
        hidden_ref, refs = refs[0], refs[1:]
    (vec_ref, weight_ref), refs = refs[:2], refs[2:]
    if joins:
        hidden_ref, refs = refs[0], refs[1:]
    normed_ref, out_ref = refs
    for rows in strips():
        if joins:
            part = both(part_ref, recv_ref, rows)
            low = (middle_ref[rows, :] + part + before_ref[BIAS_DOWN]).astype(LOW)
            hidden_ref[rows, :] = low
        else:
            low = hidden_ref[rows, :]
        unit, _ = normalized(low.astype(jnp.float32))
        normed_ref[rows, :] = (unit * vec_ref[GAIN_ONE] + vec_ref[SHIFT_ONE]).astype(LOW)
    product = dot_rows(normed_ref[...], weight_ref[...])
    out_ref[...] = (product + bias_of(vec_ref, BIAS_PROJ, 0, out_ref.shape[1])).astype(LOW)


def project(before, vec, rows, out_width):
    joins = len(before) > 1
    tokens, width = before[0].shape
    ins = [row_block(width)] * 3 + [whole(vec.shape)] if joins else [row_block(width)]
    outs = [row_block(width)] * (2 if joins else 1)
    low = jax.ShapeDtypeStruct((tokens, width), LOW)
    return pl.pallas_call(
        partial(project_kernel, joins),
        grid=(tokens // ROWS,),
        in_specs=ins + [whole(vec.shape), whole((out_width, width))],
        out_specs=outs + [row_block(out_width)],
        out_shape=[low] * len(outs) + [jax.ShapeDtypeStruct((tokens, out_width), LOW)],
        **params_of(2 * tokens * width * out_width, tokens * width * 16),
    )(*before, vec, rows)


def out_halves(packed_ref, half):
    wide = packed_ref.shape[1] // 2
    return [
        jnp.concatenate([packed_ref[rows, :wide], packed_ref[rows, wide:]], axis=0)
        for rows in (slice(0, half), slice(half, 2 * half))
    ]


def branch_kernel(half, attended_ref, packed_ref, low_ref):
    wide = attended_ref.shape[1]
    for index, weights in enumerate(out_halves(packed_ref, half)):
        cols = slice(index * wide, (index + 1) * wide)
        low_ref[:, cols] = dot_rows(attended_ref[...], weights).astype(LOW)


def branch_out(shares, attended, rows):
    tokens, wide = attended.shape
    width = rows.shape[1]
    return pl.pallas_call(
        partial(branch_kernel, shares.half),
        grid=(tokens // ROWS,),
        in_specs=[row_block(wide), at_block((COLS, width), 3, 0)],
        out_specs=row_block(width),
        out_shape=jax.ShapeDtypeStruct((tokens, width), LOW),
        **params_of(2 * tokens * width * wide, tokens * width * 4),
    )(attended, rows)


def gelu_parts(value):
    below = 1.0 + (0.3275911 * 0.5**0.5) * jnp.abs(value)
    rough = pl.reciprocal(below, approx=True)
    t = rough * (2.0 - below * rough)
    bell = jnp.exp((-0.5 * value) * value)
    poly = 0.5 * 1.061405429
    for coefficient in (-1.453152027, 1.421413741, -0.284496736, 0.254829592):
        poly = poly * t + 0.5 * coefficient
    tail = poly * (t * bell)
    cdf = jnp.where(value > 0, 1.0 - tail, tail)
    return value * cdf, cdf + value * (bell * (0.5 / math.pi) ** 0.5)


def expand_kernel(
    hidden_ref,
    branch_ref,
    recv_ref,
    vec_ref,
    up_ref,
    down_ref,
    middle_ref,
    normed_ref,
    slope_ref,
    active_ref,
    low_ref,
    held,
):
    for rows in strips():
        branch = both(branch_ref, recv_ref, rows) + vec_ref[BIAS_OUT]
        middle = hidden_ref[rows, :].astype(jnp.float32) + branch
        middle_ref[rows, :] = middle
        unit, _ = normalized(middle)
        normed_ref[rows, :] = (unit * vec_ref[GAIN_TWO] + vec_ref[SHIFT_TWO]).astype(LOW)
    for index in range(up_ref.shape[0] // WIDE):
        cols = slice(index * WIDE, (index + 1) * WIDE)
        held[index] = dot_rows(normed_ref[...], up_ref[cols, :])
        bias = bias_of(vec_ref, BIAS_UP, index * WIDE, WIDE)
        for rows in strips():
            active, slope = gelu_parts(held[index, rows, :] + bias)
            active_ref[rows, cols] = active.astype(LOW)
            slope_ref[rows, cols] = slope.astype(LOW)
    low_ref[...] = dot_plain(active_ref[...], down_ref[...]).astype(LOW)


def expand(hidden, branch, recv, vec, rows, down):
    tokens, width = hidden.shape
    inner = down.shape[0]
    return pl.pallas_call(
        expand_kernel,
        grid=(tokens // ROWS,),
        in_specs=[row_block(width)] * 3
        + [whole(vec.shape), at_block((inner, width), 1, 0), whole((inner, width))],
        out_specs=[row_block(width), row_block(width), row_block(inner), row_block(inner)]
        + [row_block(width)],
        out_shape=[
            jax.ShapeDtypeStruct((tokens, width), jnp.float32),
            jax.ShapeDtypeStruct((tokens, width), LOW),
            jax.ShapeDtypeStruct((tokens, inner), LOW),
            jax.ShapeDtypeStruct((tokens, inner), LOW),
            jax.ShapeDtypeStruct((tokens, width), LOW),
        ],
        scratch_shapes=[pltpu.VMEM((inner // WIDE, ROWS, WIDE), jnp.float32)],
        **params_of(4 * tokens * width * inner, tokens * width * 32, tokens * inner),
    )(hidden, branch, recv, vec, rows, down)


def expand_back_kernel(
    grad_ref,
    slope_ref,
    up_ref,
    down_ref,
    low_ref,
    grad_up_ref,
    bias_up_ref,
    bias_down_ref,
    sums_up,
    sums_down,
):
    step = pl.program_id(0)

    @pl.when(step == 0)
    def _():
        sums_up[...] = jnp.zeros_like(sums_up)
        sums_down[...] = jnp.zeros_like(sums_down)

    for index in range(down_ref.shape[0] // WIDE):
        cols = slice(index * WIDE, (index + 1) * WIDE)
        grad_active = dot_rows(grad_ref[...], down_ref[cols, :])
        grad_up_ref[:, cols] = (grad_active * slope_ref[:, cols].astype(jnp.float32)).astype(LOW)
    low_ref[...] = dot_plain(grad_up_ref[...], up_ref[...]).astype(LOW)
    for rows in strips():
        sums_up[...] += eights(grad_up_ref[rows, :].astype(jnp.float32))
        sums_down[...] += eights(grad_ref[rows, :].astype(jnp.float32))

    @pl.when(step == pl.num_programs(0) - 1)
    def _():
        bias_up_ref[...] = jnp.sum(sums_up[...], axis=0, keepdims=True)
        bias_down_ref[...] = jnp.sum(sums_down[...], axis=0, keepdims=True)


def expand_back(grad, slope, rows, down):
    tokens, width = grad.shape
    inner = down.shape[0]
    return pl.pallas_call(
        expand_back_kernel,
        grid=(tokens // ROWS,),
        in_specs=[row_block(width), row_block(inner)]
        + [at_block((inner, width), 1, 0), whole((inner, width))],
        out_specs=[row_block(width), row_block(inner), whole((1, inner)), whole((1, width))],
        out_shape=[
            jax.ShapeDtypeStruct((tokens, width), LOW),
            jax.ShapeDtypeStruct((tokens, inner), LOW),
            jax.ShapeDtypeStruct((1, inner), jnp.float32),
            jax.ShapeDtypeStruct((1, width), jnp.float32),
        ],
        scratch_shapes=[pltpu.VMEM((8, inner), jnp.float32), pltpu.VMEM((8, width), jnp.float32)],
        **params_of(4 * tokens * width * inner, tokens * width * 24),
    )(grad, slope, rows, down)


def token_products_kernel(lefts, rights, outs):
    for left, right, out in zip(lefts, rights, outs):
        out[...] = dot_tokens(left[...], right[...]).astype(LOW)


def hidden_products(active, grad, grad_up, normed):
    tokens, inner = active.shape
    width = grad.shape[1]

    def kernel(a_ref, b_ref, c_ref, d_ref, down_ref, rows_ref):
        token_products_kernel((a_ref, b_ref), (c_ref, d_ref), (down_ref, rows_ref))

    return pl.pallas_call(
        kernel,
        grid=(inner // COLS,),
        in_specs=[col_block(tokens)] * 2 + [whole((tokens, width))] * 2,
        out_specs=[
            pl.BlockSpec((COLS, width), lambda i: (i, 0)),
            pl.BlockSpec((COLS, width), lambda i: (inner // COLS + i, 0)),
        ],
        out_shape=[
            jax.ShapeDtypeStruct((inner, width), LOW),
            jax.ShapeDtypeStruct((2 * inner, width), LOW),
        ],
        **params_of(4 * tokens * width * inner, tokens * width * 16),
    )(active, grad_up, grad, normed)


def project_products(grad_proj, normed, rows_grad):
    tokens, out_width = grad_proj.shape
    width = normed.shape[1]

    def kernel(a_ref, b_ref, _, rows_ref):
        token_products_kernel((a_ref,), (b_ref,), (rows_ref,))

    return pl.pallas_call(
        kernel,
        grid=(out_width // COLS,),
        in_specs=[col_block(tokens), whole((tokens, width)), pl.BlockSpec(memory_space=pl.ANY)],
        out_specs=pl.BlockSpec((COLS, width), lambda i: (i, 0)),
        out_shape=jax.ShapeDtypeStruct(rows_grad.shape, LOW),
        input_output_aliases={2: 0},
        **params_of(2 * tokens * width * out_width, tokens * width * 8),
    )(grad_proj, normed, rows_grad)


def norm_back_rows(values_in, incoming, gain_vec):
    unit, scale = normalized(values_in)
    p = incoming * gain_vec
    mean_p = jnp.mean(p, axis=-1, keepdims=True)
    mean_pn = jnp.mean(p * unit, axis=-1, keepdims=True)
    return scale * (p - mean_p - unit * mean_pn), eights(incoming * unit), eights(incoming)


def branch_back_kernel(
    half,
    middle_ref,
    part_ref,
    recv_ref,
    grad_ref,
    attended_ref,
    vec_ref,
    packed_ref,
    _,
    grad_middle_ref,
    grad_attended_ref,
    out_grad_ref,
    gain_grad_ref,
    shift_grad_ref,
    bias_grad_ref,
    total,
    low,
    sums,
):
    step = pl.program_id(0)

    @pl.when(step == 0)
    def _():
        total[...] = jnp.zeros_like(total)
        sums[...] = jnp.zeros_like(sums)

    for rows in strips():
        incoming = both(part_ref, recv_ref, rows)
        change, for_gain, for_shift = norm_back_rows(
            middle_ref[rows, :], incoming, vec_ref[GAIN_TWO]
        )
        grad_middle = grad_ref[rows, :].astype(jnp.float32) + change
        grad_middle_ref[rows, :] = grad_middle
        rounded = grad_middle.astype(LOW)
        low[rows, :] = rounded
        sums[0] += for_gain
        sums[1] += for_shift
        sums[2] += eights(rounded.astype(jnp.float32))
    weights = out_halves(packed_ref, half)
    wide = weights[0].shape[0]
    attended = attended_ref[...]
    pieces = [low[:, :wide], low[:, wide:]]
    grad_attended_ref[...] = (
        dot_plain(pieces[0], weights[0]) + dot_plain(pieces[1], weights[1])
    ).astype(LOW)
    for index in range(2):
        total[index] += dot_tokens(pieces[index], attended)

    @pl.when(step == pl.num_programs(0) - 1)
    def _():
        for index in range(2):
            joined = jnp.concatenate([total[index, :half, :], total[index, half:, :]], axis=1)
            out_grad_ref[index * half : (index + 1) * half, :] = joined.astype(LOW)
        for index, ref in enumerate((gain_grad_ref, shift_grad_ref, bias_grad_ref)):
            ref[...] = jnp.sum(sums[index], axis=0, keepdims=True)


def branch_back(shares, middle, part, recv, grad, attended, vec, rows, rows_grad):
    tokens, width = middle.shape
    wide = attended.shape[1]
    small = whole((1, width))
    one = jax.ShapeDtypeStruct((1, width), jnp.float32)
    return pl.pallas_call(
        partial(branch_back_kernel, shares.half),
        grid=(tokens // ROWS,),
        in_specs=[row_block(width)] * 4
        + [row_block(wide), whole(vec.shape), at_block((COLS, width), 3, 0)]
        + [pl.BlockSpec(memory_space=pl.ANY)],
        out_specs=[row_block(width), row_block(wide), at_block((COLS, width), 3, 0)]
        + [small, small, small],
        out_shape=[
            jax.ShapeDtypeStruct((tokens, width), jnp.float32),
            jax.ShapeDtypeStruct((tokens, wide), LOW),
            jax.ShapeDtypeStruct(rows_grad.shape, LOW),
            one,
            one,
            one,
        ],
        input_output_aliases={7: 2},
        scratch_shapes=[
            pltpu.VMEM((2, width // 2, wide), jnp.float32),
            pltpu.VMEM((ROWS, width), LOW),
            pltpu.VMEM((3, 8, width), jnp.float32),
        ],
        **params_of(4 * tokens * width * wide, tokens * width * 20),
    )(middle, part, recv, grad, attended, vec, rows, rows_grad)


def project_back_kernel(grad_ref, weight_ref, low_ref, bias_ref, sums):
    step = pl.program_id(0)

    @pl.when(step == 0)
    def _():
        sums[...] = jnp.zeros_like(sums)

    low_ref[...] = dot_plain(grad_ref[...], weight_ref[...]).astype(LOW)
    for rows in strips():
        sums[...] += eights(grad_ref[rows, :].astype(jnp.float32))

    @pl.when(step == pl.num_programs(0) - 1)
    def _():
        bias_ref[...] = jnp.sum(sums[...], axis=0, keepdims=True)


def project_back(grad_proj, rows):
    tokens, out_width = grad_proj.shape
    width = rows.shape[1]
    return pl.pallas_call(
        project_back_kernel,
        grid=(tokens // ROWS,),
        in_specs=[row_block(out_width), whole((out_width, width))],
        out_specs=[row_block(width), whole((1, out_width))],
        out_shape=[
            jax.ShapeDtypeStruct((tokens, width), LOW),
            jax.ShapeDtypeStruct((1, out_width), jnp.float32),
        ],
        scratch_shapes=[pltpu.VMEM((8, out_width), jnp.float32)],
        **params_of(2 * tokens * width * out_width, tokens * width * 12),
    )(grad_proj, rows)


def input_back_kernel(
    hidden_ref, part_ref, recv_ref, grad_ref, vec_ref, out_ref, gain_grad_ref, shift_grad_ref, sums
):
    step = pl.program_id(0)

    @pl.when(step == 0)
    def _():
        sums[...] = jnp.zeros_like(sums)

    for rows in strips():
        incoming = both(part_ref, recv_ref, rows)
        hidden = hidden_ref[rows, :].astype(jnp.float32)
        change, for_gain, for_shift = norm_back_rows(hidden, incoming, vec_ref[GAIN_ONE])
        out_ref[rows, :] = (grad_ref[rows, :] + change).astype(LOW)
        sums[0] += for_gain
        sums[1] += for_shift

    @pl.when(step == pl.num_programs(0) - 1)
    def _():
        gain_grad_ref[...] = jnp.sum(sums[0], axis=0, keepdims=True)
        shift_grad_ref[...] = jnp.sum(sums[1], axis=0, keepdims=True)


def input_back(hidden, part, recv, grad_middle, vec):
    tokens, width = hidden.shape
    small = whole((1, width))
    one = jax.ShapeDtypeStruct((1, width), jnp.float32)
    return pl.pallas_call(
        input_back_kernel,
        grid=(tokens // ROWS,),
        in_specs=[row_block(width)] * 4 + [whole(vec.shape)],
        out_specs=[row_block(width), small, small],
        out_shape=[jax.ShapeDtypeStruct((tokens, width), LOW), one, one],
        scratch_shapes=[pltpu.VMEM((2, 8, width), jnp.float32)],
        **params_of(0, tokens * width * 12),
    )(hidden, part, recv, grad_middle, vec)


def attend_kernel(q_ref, k_ref, v_ref, qa_ref, kt_ref, out_ref, lse_ref, keys, held, low):
    tokens, pair = q_ref.shape
    left = lax.broadcasted_iota(jnp.int32, (CHUNK, pair), 1) < pair // 2
    keys[:pair, :] = jnp.transpose(k_ref[...].astype(jnp.float32)).astype(LOW)
    keys[pair:, :] = kt_ref[...]
    for index in range(tokens // CHUNK):
        rows = slice(index * CHUNK, (index + 1) * CHUNK)
        queries = q_ref[rows, :] * 0.125
        outs, tops = [], []
        for head in range(2):
            slot = (2 * index + head) % held.shape[0]
            mine = left if head == 0 else jnp.logical_not(left)
            side = jnp.where(mine, queries, jnp.zeros_like(queries))
            lhs = jnp.concatenate([side, qa_ref[head, rows, :]], axis=1)
            held[slot] = dot_plain(lhs, keys[...])
            levels, shares = [], []
            for strip in strips(CHUNK):
                scores = held[slot, strip, :]
                top = jnp.max(scores, axis=1, keepdims=True)
                weight = jnp.exp(scores - top)
                total = jnp.sum(weight, axis=1, keepdims=True)
                low[slot, strip, :] = weight.astype(LOW)
                levels.append(top + jnp.log(total))
                shares.append(1.0 / total)
            product = dot_plain(low[slot], v_ref[...])
            outs.append(product * jnp.concatenate(shares, axis=0))
            tops.append(jnp.concatenate(levels, axis=0))
        out_ref[rows, :] = jnp.where(left, outs[0], outs[1]).astype(LOW)
        lse_ref[rows, :] = jnp.where(left, tops[0], tops[1])


def attend(projected, query_side, key_side, turned):
    tokens = projected.shape[0]
    width = projected.shape[1] // 3
    pairs = width // 128
    features = key_side.shape[1]
    return pl.pallas_call(
        attend_kernel,
        grid=(pairs,),
        in_specs=[
            pl.BlockSpec((tokens, 128), lambda p: (0, p)),
            pl.BlockSpec((tokens, 128), lambda p: (0, pairs + p)),
            pl.BlockSpec((tokens, 128), lambda p: (0, 2 * pairs + p)),
            pl.BlockSpec((2, tokens, features), lambda p: (p, 0, 0)),
            whole((features, tokens)),
        ],
        out_specs=[
            pl.BlockSpec((tokens, 128), lambda p: (0, p)),
            pl.BlockSpec((tokens, 128), lambda p: (0, p)),
        ],
        out_shape=[
            jax.ShapeDtypeStruct((tokens, width), LOW),
            jax.ShapeDtypeStruct((tokens, width), jnp.float32),
        ],
        scratch_shapes=[
            pltpu.VMEM((128 + features, tokens), LOW),
            pltpu.VMEM((4, CHUNK, tokens), jnp.float32),
            pltpu.VMEM((4, CHUNK, tokens), LOW),
        ],
        **params_of(
            16 * pairs * tokens * tokens * 128, tokens * width * 16, 2 * pairs * tokens * tokens
        ),
    )(projected, projected, projected, query_side, turned)


def three_terms(values):
    high = values.astype(LOW).astype(jnp.float32)
    rest = values - high
    middle = rest.astype(LOW).astype(jnp.float32)
    return high, middle, rest - middle


def attend_back_kernel(
    q_ref,
    k_ref,
    v_ref,
    do_ref,
    o_ref,
    lse_ref,
    qa_ref,
    ka_ref,
    grad_ref,
    held,
    probs,
    changes,
    query_sides,
    grad_sides,
):
    tokens, pair = q_ref.shape
    features = ka_ref.shape[1]
    pairs = pl.num_programs(0)
    place = pl.program_id(0)
    first = 2 * (tokens // BLOCK) + 3
    half = pair // 2
    left = lax.broadcasted_iota(jnp.int32, (CHUNK, pair), 1) < half
    lane = lax.broadcasted_iota(jnp.int32, (CHUNK, features), 1)
    lane_pair = lax.broadcasted_iota(jnp.int32, (CHUNK, pair), 1)
    keys = jnp.concatenate([k_ref[...], ka_ref[...]], axis=1)
    turned = jnp.transpose(k_ref[...].astype(jnp.float32)).astype(LOW)
    ones = (lax.broadcasted_iota(jnp.int32, (tokens, pair), 1) < 3).astype(jnp.float32).astype(LOW)
    values = jnp.concatenate([v_ref[...], ones], axis=1)
    parts, key_grads, value_grads = [], [], []
    for head in range(2):
        mine = left if head == 0 else jnp.logical_not(left)
        for index in range(tokens // CHUNK):
            rows = slice(index * CHUNK, (index + 1) * CHUNK)
            slot = index % 2
            queries = q_ref[rows, :] * 0.125
            grads = do_ref[rows, :]
            product = grads.astype(jnp.float32) * o_ref[rows, :].astype(jnp.float32)
            level = lse_ref[rows, head * half : head * half + 1]
            inner = jnp.sum(jnp.where(mine, product, 0.0), axis=1, keepdims=True)
            side = qa_ref[head, rows, :].astype(jnp.float32)
            for spot, term in enumerate(three_terms(level)):
                side = jnp.where(lane == first + spot, -term, side)
            query_side = jnp.where(mine, queries, jnp.zeros_like(queries))
            grad_side = jnp.where(mine, grads, jnp.zeros_like(grads))
            query_sides[head, rows, :] = query_side
            grad_sides[head, rows, :] = grad_side
            tail = jnp.zeros((CHUNK, pair), jnp.float32)
            for spot, term in enumerate(three_terms(inner)):
                tail = jnp.where(lane_pair == spot, -term, tail)
            held[slot, 0] = dot_rows(
                keys, jnp.concatenate([query_side, side.astype(LOW)], axis=1)
            )
            held[slot, 1] = dot_rows(
                values, jnp.concatenate([grad_side, tail.astype(LOW)], axis=1)
            )
            for strip in strips(tokens, 128):
                prob = jnp.exp(held[slot, 0, strip, :])
                probs[head, strip, rows] = prob.astype(LOW)
                changes[head, strip, rows] = (prob * held[slot, 1, strip, :]).astype(LOW)
        value_grads.append(dot_plain(probs[head], grad_sides[head]))
        key_grads.append(dot_plain(changes[head], query_sides[head]))
        parts.append(dot_plain(turned, changes[head]))
    joined = jnp.concatenate([parts[0][:half], parts[1][half:]], axis=0)
    column = [pl.ds(pl.multiple_of((by * pairs + place) * 128, 128), 128) for by in range(3)]
    grad_ref[:, column[0]] = (jnp.transpose(joined) * 0.125).astype(LOW)
    grad_ref[:, column[1]] = (key_grads[0] + key_grads[1]).astype(LOW)
    grad_ref[:, column[2]] = (value_grads[0] + value_grads[1]).astype(LOW)


def attend_back(projected, grad_attended, attended, levels, query_side, key_side):
    tokens, width = attended.shape
    pairs = width // 128
    features = key_side.shape[1]
    by_pair = pl.BlockSpec((tokens, 128), lambda p: (0, p))
    return pl.pallas_call(
        attend_back_kernel,
        grid=(pairs,),
        in_specs=[
            by_pair,
            pl.BlockSpec((tokens, 128), lambda p: (0, pairs + p)),
            pl.BlockSpec((tokens, 128), lambda p: (0, 2 * pairs + p)),
            by_pair,
            by_pair,
            by_pair,
            pl.BlockSpec((2, tokens, features), lambda p: (p, 0, 0)),
            whole((tokens, features)),
        ],
        out_specs=whole((tokens, 3 * width)),
        out_shape=jax.ShapeDtypeStruct((tokens, 3 * width), LOW),
        scratch_shapes=[
            pltpu.VMEM((2, 2, tokens, CHUNK), jnp.float32),
            pltpu.VMEM((2, tokens, tokens), LOW),
            pltpu.VMEM((2, tokens, tokens), LOW),
            pltpu.VMEM((2, tokens, 128), LOW),
            pltpu.VMEM((2, tokens, 128), LOW),
        ],
        **params_of(
            40 * pairs * tokens * tokens * 128, tokens * width * 24, 2 * pairs * tokens * tokens
        ),
    )(projected, projected, projected, grad_attended, attended, levels, query_side, key_side)


def window_forward(shares, before, weights, vec, features, beside):
    rows, down = weights
    results = project(before, vec, rows, 6 * shares.half)
    hidden = before[0] if len(before) == 1 else results[0]
    normed, projected = results[-2:]
    projected = beside.tie(projected)
    attended, levels = beside.tie(tuple(attend(projected, *features)))
    low = branch_out(shares, attended, rows)
    expanded = expand(hidden, low, swap(low), vec, rows, down)
    middle, normed_two, slope, active, low = beside.tie(tuple(expanded))
    stored = (hidden, normed, projected, attended, levels, middle, normed_two, slope, active)
    return (middle, low, swap(low), vec), stored


def window_backward(shares, stored, grad, weights, vec, features, beside):
    hidden, normed, projected, attended, levels, middle, normed_two, slope, active = stored
    rows, down = weights
    low, grad_up, bias_up, bias_down = beside.tie(tuple(expand_back(grad, slope, rows, down)))
    arrived = swap(low)
    down_grad, rows_grad = hidden_products(active, grad, grad_up, normed_two)
    grad_middle, grad_attended, rows_grad, gain_two, shift_two, bias_out = branch_back(
        shares, middle, low, arrived, grad, attended, vec, rows, rows_grad
    )
    grad_attended = beside.tie(grad_attended)
    grad_proj = attend_back(projected, grad_attended, attended, levels, *features[:2])
    grad_proj = beside.tie(grad_proj)
    low, summed = project_back(grad_proj, rows)
    arrived = swap(low)
    rows_grad = project_products(grad_proj, normed, rows_grad)
    grad, gain_one, shift_one = input_back(hidden, low, arrived, grad_middle, vec)
    width = attended.shape[1]
    vector_grads = (gain_one, shift_one, summed[:, :width], summed[:, 2 * width :], bias_out)
    vector_grads += (gain_two, shift_two, bias_down, bias_up)
    vector_grads = [piece[0] for piece in vector_grads]
    return grad, (rows_grad, down_grad), vector_grads


def window_shards(
    block_input,
    cotangent,
    random_ids,
    segment_ids,
    global_ids,
    w_rows,
    w_rows_first,
    w_rows_second,
    w_down,
    w_down_first,
    w_down_second,
    vectors,
    vectors_first,
    vectors_second,
):
    core = lax.axis_index(SECTION)
    micro, _, tokens, width = block_input.shape
    _, _, columns = w_rows.shape
    shares = Shares(width, columns, w_down.shape[1], vectors.shape[1])
    prepared = prepare(shares, w_rows[0], w_down[0], vectors)
    features = key_features(shares, random_ids, segment_ids, global_ids)
    gathered_zero, gathered_one, hidden, grad = gather(shares, prepared, block_input, cotangent)

    beside = Beside(spread_quads(shares, gathered_one[:2]))
    params = [shares.unpack(gathered_zero, core)]
    before = (hidden.reshape(-1, width),)
    before, stored_zero = window_forward(shares, before, *params[0], features, beside)
    params.append(shares.unpack((*beside.flying, gathered_one[2]), core))
    after, stored_one = window_forward(shares, before, *params[1], features, Beside())
    final = after[1].astype(jnp.float32) + after[2].astype(jnp.float32)
    final = (after[0] + final + after[3][BIAS_DOWN]).astype(LOW)

    grad = grad.reshape(-1, width)
    grad, *grads_one = window_backward(shares, stored_one, grad, *params[1], features, Beside())
    *arrays_one, vec_one = shares.by_shard(*grads_one, core)
    beside = Beside(sum_quads(shares, arrays_one))
    grad, *grads_zero = window_backward(shares, stored_zero, grad, *params[0], features, beside)
    *arrays_zero, vec_zero = shares.by_shard(*grads_zero, core)
    grad, final = [piece.reshape(micro, tokens, width) for piece in (grad, final)]
    halves, slices = scatter(shares, arrays_zero, vec_zero, beside.flying, vec_one, grad, final)
    old = [
        w_rows[0],
        w_rows_first[0],
        w_rows_second[0],
        w_down[0],
        w_down_first[0],
        w_down_second[0],
        vectors,
        vectors_first,
        vectors_second,
    ]
    *new, result = update(shares, halves, slices, old)
    return (result[None, :, None], *[piece[None] for piece in new[:6]], *new[6:])


def one_window_each(mesh, block_input, w_rows, w_down, vectors):
    micro, windows, length, width = block_input.shape
    shards = mesh.shape[DP] * mesh.shape[SEQ]
    columns, depth = w_rows.shape[2] // shards, w_down.shape[1] // shards
    head_dim = width // HEADS
    tokens = length // mesh.shape[SEQ]
    return (
        mesh.shape[SECTION] == 2
        and mesh.shape[SEQ] == micro
        and mesh.shape[DP] == windows
        and tokens % (2 * BLOCK) == 0
        and length % CHUNK == 0
        and head_dim == 64
        and width % columns == 0
        and columns % (2 * head_dim) == 0
        and columns % depth == 0
        and width // columns * (columns // 2) % 128 == 0
        and depth % 32 == 0
        and vectors.shape[1] // shards <= width
        and mesh.shape[DP] == 4
        and micro == 4
        and width == 2 * columns == 2 * COLS
        and w_down.shape[1] == 4 * width
        and (columns // 2) % (2 * PIECE) == 0
        and (depth // 2) % (2 * PIECE) == 0
        and length % (4 * ROWS) == 0
    )


def solution(mesh):
    in_specs = (
        P(None, DP, SEQ, None),
        P(None, DP, SEQ, None),
        P(None, DP, None, None, None),
        P(None, DP, None),
        P(None, DP, None),
        P(SECTION, None, (DP, SEQ)),
        P(SECTION, None, (DP, SEQ)),
        P(SECTION, None, (DP, SEQ)),
        P(SECTION, (DP, SEQ), None),
        P(SECTION, (DP, SEQ), None),
        P(SECTION, (DP, SEQ), None),
        P(SECTION, (DP, SEQ)),
        P(SECTION, (DP, SEQ)),
        P(SECTION, (DP, SEQ)),
    )
    out_specs = (
        P(SECTION, None, DP, SEQ, None),
        P(SECTION, None, (DP, SEQ)),
        P(SECTION, None, (DP, SEQ)),
        P(SECTION, None, (DP, SEQ)),
        P(SECTION, (DP, SEQ), None),
        P(SECTION, (DP, SEQ), None),
        P(SECTION, (DP, SEQ), None),
        P(SECTION, (DP, SEQ)),
        P(SECTION, (DP, SEQ)),
        P(SECTION, (DP, SEQ)),
    )

    def step(*arrays):
        chosen = general_shards
        if one_window_each(mesh, arrays[0], arrays[5], arrays[8], arrays[11]):
            chosen = window_shards
        return jax.shard_map(
            chosen, mesh=mesh, in_specs=in_specs, out_specs=out_specs, check_vma=False
        )(*arrays)

    return step
```

```python
import math
from functools import partial

import jax
import jax.numpy as jnp
import ml_dtypes
import numpy as np
from jax import lax
from jax.experimental import pallas as pl
from jax.experimental.pallas import tpu as pltpu
from jax.sharding import PartitionSpec as P

SECTION, DP, SEQ = "section", "dp", "seq"
HEADS = 12
BLOCK = 64
STEP = 5


epsilon = 1e-05
masked = -1e30
rate_matrix = 0.02
rate_vector = 0.2
decay_matrix = 0.01


def with_halo(x, sides, width):
    for axis, dim in sides:
        devices, length = (lax.axis_size(axis), x.shape[dim])
        up = [(i, (i + 1) % devices) for i in range(devices - 1)]
        down = [(j, i) for i, j in up]
        last = lax.slice_in_dim(x, length - width, length, axis=dim)
        initial = lax.slice_in_dim(x, 0, width, axis=dim)
        before = lax.ppermute(last, axis, up)
        after = lax.ppermute(initial, axis, down)
        x = jnp.concatenate([before, x, after], axis=dim)
    return x


def merged(value, axis, join):
    pieces = jax.tree.map(lambda part: lax.all_gather(part, axis), value)
    head = jax.tree.map(lambda part: part[0], pieces)
    tail = jax.tree.map(lambda part: part[1:], pieces)
    subtotal, _ = lax.scan(lambda subtotal, share: (join(subtotal, share), None), head, tail)
    return subtotal


def from_behind(x, axis, by):
    devices = lax.axis_size(axis)
    pairs = [(i, i + by) for i in range(devices) if 0 <= i + by < devices]
    return lax.ppermute(x, axis, pairs)


def partner(value, axis, bit):
    mask = 2**bit
    pairs = [(source, source ^ mask) for source in range(lax.axis_size(axis))]
    return lax.ppermute(value, axis, pairs)


def mixed_sum(form, left, right):
    return jnp.einsum(form, left, right, preferred_element_type=jnp.float32)


def exact_two(form, left, right):
    return jnp.einsum(
        form, left, right, precision=lax.Precision.HIGHEST, preferred_element_type=jnp.float32
    )


def norm_rows(values_in, gain_vec, shift_vec):
    row_mean = jnp.mean(values_in, axis=-1, keepdims=True)
    centred = values_in - row_mean
    spread = jnp.mean(centred * centred, axis=-1, keepdims=True)
    return centred * lax.rsqrt(spread + epsilon) * gain_vec + shift_vec


def split_vectors(vector_weights, model_width):
    pieces = [
        vector_weights[piece_index * model_width : (piece_index + 1) * model_width]
        for piece_index in range(8)
    ]
    return pieces + [vector_weights[8 * model_width :]]


def route_tables(random_rows, segments, global_rows, seq_place, groups):
    windows, blocks, head_count, pick_count = random_rows.shape
    blocks_dev = blocks // groups
    request_count = blocks_dev * head_count * pick_count
    capacity = -(-request_count // groups)
    requests = random_rows.reshape(windows, groups, request_count)
    owners = requests // blocks_dev
    inside = requests % blocks_dev
    head_of = jnp.arange(request_count) // pick_count % head_count
    is_mine = owners == seq_place
    slot_index = jnp.cumsum(is_mine.astype(jnp.int32), axis=2) - 1
    slot_hot = ((slot_index[..., None] == jnp.arange(capacity)) & is_mine[..., None]).astype(
        jnp.float32
    )
    inside_hot = (inside[..., None] == jnp.arange(blocks_dev)).astype(jnp.float32)
    head_hot = (head_of[:, None] == jnp.arange(head_count)).astype(jnp.float32)
    sender = jnp.einsum(
        "wqsc,wqsb,sh->wqcbh", slot_hot, inside_hot, head_hot, precision=lax.Precision.HIGHEST
    )
    my_owners = lax.dynamic_index_in_dim(owners, seq_place, axis=1, keepdims=False)
    earlier = jnp.arange(request_count)[None, :] < jnp.arange(request_count)[:, None]
    same_owner = my_owners[:, :, None] == my_owners[:, None, :]
    rank_index = jnp.sum((same_owner & earlier[None]).astype(jnp.int32), axis=2)
    picker = (
        (my_owners[..., None, None] == jnp.arange(groups)[:, None])
        & (rank_index[..., None, None] == jnp.arange(capacity)[None, :])
    ).astype(jnp.float32)
    first_block = seq_place * blocks_dev
    owned_hot = (global_rows[:, :, None] == first_block + jnp.arange(blocks_dev)).astype(
        jnp.float32
    )
    length = segments.shape[1]
    block_len = length // blocks
    seg_blocks = segments.reshape(windows, blocks, block_len)
    seg_pad = jnp.pad(seg_blocks, ((0, 0), (1, 1), (0, 0)), constant_values=-1)
    near_segs = lax.dynamic_slice_in_dim(seg_pad, first_block, blocks_dev + 2, axis=1)
    slide_seg = jnp.concatenate([near_segs[:, :-2], near_segs[:, 1:-1], near_segs[:, 2:]], axis=2)
    query_seg = near_segs[:, 1:-1]
    rows_index = jnp.arange(windows)
    global_seg = seg_blocks[rows_index[:, None], global_rows].reshape(windows, -1)
    chosen = lax.dynamic_slice_in_dim(random_rows, first_block, blocks_dev, axis=1)
    far_seg = seg_blocks[rows_index[:, None, None, None], chosen].reshape(
        windows, blocks_dev, head_count, -1
    )
    key_seg = jnp.concatenate(
        [
            jnp.broadcast_to(
                slide_seg[:, :, None, :], (windows, blocks_dev, head_count, slide_seg.shape[2])
            ),
            jnp.broadcast_to(
                global_seg[:, None, None, :], (windows, blocks_dev, head_count, global_seg.shape[1])
            ),
            far_seg,
        ],
        axis=3,
    )
    key_mask = query_seg[:, :, None, :, None] == key_seg[:, :, :, None, :]
    local_seg = query_seg.reshape(windows, -1)
    full_mask = global_seg[:, None, :, None] == local_seg[:, None, None, :]
    return (sender, picker, owned_hot, key_mask, full_mask)


def fetch_blocks(paired, queries, sender, picker, owned_hot):
    windows, tokens, head_count, doubled = paired.shape
    head_dim = queries.shape[-1]
    blocks_dev = tokens // BLOCK
    flattened = paired.reshape(windows, tokens, head_count * doubled)
    padded = with_halo(flattened, ((SEQ, 1),), BLOCK)
    framed = padded.reshape(windows, blocks_dev + 2, BLOCK, head_count, doubled)
    sliding = jnp.concatenate([framed[:, :-2], framed[:, 1:-1], framed[:, 2:]], axis=2)
    local_blocks = paired.reshape(windows, blocks_dev, BLOCK, head_count, doubled)
    owned_low = owned_hot.astype(jnp.bfloat16)
    offered = mixed_sum("wgb,wbthe->wgthe", owned_low, local_blocks)
    offered_queries = mixed_sum("wgb,wbqhd->wgqhd", owned_low, queries)
    global_kv, global_queries = (
        lax.psum(offered.astype(jnp.bfloat16), SEQ).astype(jnp.float32),
        lax.psum(offered_queries.astype(jnp.bfloat16), SEQ).astype(jnp.float32),
    )
    global_kv = global_kv.astype(jnp.bfloat16).reshape(windows, -1, head_count, doubled)
    global_queries = global_queries.astype(jnp.bfloat16).reshape(windows, -1, head_count, head_dim)
    outgoing = mixed_sum("wqcbh,wbthe->qwcte", sender.astype(jnp.bfloat16), local_blocks).astype(
        jnp.bfloat16
    )
    incoming = lax.all_to_all(outgoing, SEQ, split_axis=0, concat_axis=0, tiled=True)
    distant = mixed_sum("wspc,pwcte->wste", picker.astype(jnp.bfloat16), incoming).astype(
        jnp.bfloat16
    )
    pick_count = picker.shape[1] // (blocks_dev * head_count)
    distant = distant.reshape(windows, blocks_dev, head_count, pick_count, BLOCK, doubled)
    return (sliding, global_kv, distant, global_queries)


def combine_stats(earlier, later):
    top = jnp.maximum(earlier[0], later[0])
    return (top, earlier[1] * jnp.exp(earlier[0] - top) + later[1] * jnp.exp(later[0] - top))


def full_forward(global_queries, key_part, value_part, full_mask, head_dim):
    scores = mixed_sum("wqhd,wkhd->whqk", global_queries, key_part) * head_dim ** (-0.5)
    scores = jnp.where(full_mask, scores, masked)
    local_top = jnp.max(scores, axis=3, keepdims=True)
    local_sum = jnp.sum(
        jnp.where(full_mask, jnp.exp(scores - local_top), 0.0), axis=3, keepdims=True
    )
    row_top, row_sum = merged((local_top, local_sum), SEQ, combine_stats)
    full_probs = jnp.where(full_mask, jnp.exp(scores - row_top), 0.0) / row_sum
    partial_out = mixed_sum("whqk,wkhd->wqhd", full_probs.astype(jnp.bfloat16), value_part)
    full_out = lax.psum(partial_out.astype(jnp.bfloat16), SEQ).astype(jnp.float32)
    return (full_out, full_probs)


def attention_weights(queries, sliding, global_kv, distant, key_mask):
    head_dim = queries.shape[-1]
    windows, blocks_dev, _, head_count, _ = queries.shape
    near_scores = mixed_sum("wbqhd,wbkhd->wbhqk", queries, sliding[..., :head_dim])
    global_scores = mixed_sum("wbqhd,wkhd->wbhqk", queries, global_kv[..., :head_dim])
    far_scores = mixed_sum("wbqhd,wbhrkd->wbhqrk", queries, distant[..., :head_dim])
    far_scores = far_scores.reshape(windows, blocks_dev, head_count, BLOCK, -1)
    scores = jnp.concatenate([near_scores, global_scores, far_scores], axis=4) * head_dim ** (-0.5)
    scores = jnp.where(key_mask, scores, masked)
    row_top = jnp.max(scores, axis=4, keepdims=True)
    weight = jnp.exp(scores - row_top)
    return weight / jnp.sum(weight, axis=4, keepdims=True)


def split_keys(scores_like, sliding, global_kv, distant):
    near_keys = sliding.shape[2]
    global_keys = global_kv.shape[1]
    windows, blocks_dev, head_count, pick_count, _, _ = distant.shape
    near_part = scores_like[..., :near_keys]
    global_part = scores_like[..., near_keys : near_keys + global_keys]
    far_part = scores_like[..., near_keys + global_keys :].reshape(
        windows, blocks_dev, head_count, BLOCK, pick_count, BLOCK
    )
    return (near_part, global_part, far_part)


def attention_values(low_probs, sliding, global_kv, distant, head_dim):
    near_part, global_part, far_part = split_keys(low_probs, sliding, global_kv, distant)
    attended = mixed_sum("wbhqk,wbkhd->wbqhd", near_part, sliding[..., head_dim:])
    attended = attended + mixed_sum("wbhqk,wkhd->wbqhd", global_part, global_kv[..., head_dim:])
    return attended + mixed_sum("wbhqrk,wbhrkd->wbqhd", far_part, distant[..., head_dim:])


def layer_forward(hidden, weights, tables):
    row_weights, down_weights, vector_weights = weights
    sender, picker, owned_hot, key_mask, full_mask = tables
    model_width = row_weights.shape[0]
    windows, tokens, _ = hidden.shape
    blocks_dev = tokens // BLOCK
    head_dim = model_width // HEADS
    (
        gain_one,
        shift_one,
        bias_query,
        bias_value,
        bias_out,
        gain_two,
        shift_two,
        bias_down,
        bias_up,
    ) = split_vectors(vector_weights, model_width)
    normed = norm_rows(hidden, gain_one, shift_one).astype(jnp.bfloat16)
    projected = mixed_sum("wtd,de->wte", normed, row_weights[:, : 3 * model_width])
    projected = (
        projected + jnp.concatenate([bias_query, jnp.zeros_like(bias_query), bias_value])
    ).astype(jnp.bfloat16)
    queries = projected[..., :model_width].reshape(windows, blocks_dev, BLOCK, HEADS, head_dim)
    key_part = projected[..., model_width : 2 * model_width].reshape(
        windows, tokens, HEADS, head_dim
    )
    value_part = projected[..., 2 * model_width :].reshape(windows, tokens, HEADS, head_dim)
    paired = jnp.concatenate([key_part, value_part], axis=3)
    sliding, global_kv, distant, global_queries = fetch_blocks(
        paired, queries, sender, picker, owned_hot
    )
    probabilities = attention_weights(queries, sliding, global_kv, distant, key_mask)
    attended = attention_values(
        probabilities.astype(jnp.bfloat16), sliding, global_kv, distant, head_dim
    )
    full_out, full_probs = full_forward(global_queries, key_part, value_part, full_mask, head_dim)
    placed = exact_two(
        "wgb,wgqhd->wbqhd", owned_hot, full_out.reshape(windows, -1, BLOCK, HEADS, head_dim)
    )
    on_global = jnp.sum(owned_hot, axis=1)[:, :, None, None, None] > 0
    attended = jnp.where(on_global, placed, attended)
    mixed_low = attended.reshape(windows, tokens, model_width).astype(jnp.bfloat16)
    middle = (
        hidden
        + mixed_sum("wtd,de->wte", mixed_low, row_weights[:, 3 * model_width : 4 * model_width])
        + bias_out
    )
    normed_two = norm_rows(middle, gain_two, shift_two).astype(jnp.bfloat16)
    up_value = mixed_sum("wtd,df->wtf", normed_two, row_weights[:, 4 * model_width :]) + bias_up
    active = jax.nn.gelu(up_value, approximate=False).astype(jnp.bfloat16)
    output = middle + mixed_sum("wtf,fd->wtd", active, down_weights) + bias_down
    stored = (
        hidden,
        normed,
        queries,
        sliding,
        global_kv,
        distant,
        probabilities,
        mixed_low,
        middle,
        normed_two,
        up_value,
        active,
        key_part,
        value_part,
        global_queries,
        full_probs,
    )
    return (output, stored)


def return_blocks(near_back, global_back, far_back, query_part, sender, picker, owned_hot):
    windows, blocks_dev, _, head_count, doubled = near_back.shape
    first_third = near_back[:, :, :BLOCK]
    centre_third = near_back[:, :, BLOCK : 2 * BLOCK]
    last_third = near_back[:, :, 2 * BLOCK :]
    framed = jnp.pad(first_third, ((0, 0), (0, 2), (0, 0), (0, 0), (0, 0)))
    framed = framed + jnp.pad(centre_third, ((0, 0), (1, 1), (0, 0), (0, 0), (0, 0)))
    framed = framed + jnp.pad(last_third, ((0, 0), (2, 0), (0, 0), (0, 0), (0, 0)))
    own_grad = framed[:, 1:-1]
    for direction in (1, -1):
        rim_grad = framed[:, -1] if direction == 1 else framed[:, 0]
        arrived = from_behind(rim_grad.astype(jnp.bfloat16), SEQ, direction).astype(
            rim_grad.dtype
        )
        if direction == 1:
            own_grad = jnp.concatenate(
                [own_grad[:, :1] + arrived[:, None], own_grad[:, 1:]], axis=1
            )
        else:
            own_grad = jnp.concatenate(
                [own_grad[:, :-1], own_grad[:, -1:] + arrived[:, None]], axis=1
            )
    global_total, query_total = (
        lax.psum(
            global_back.reshape(windows, -1, BLOCK, head_count, doubled).astype(jnp.bfloat16), SEQ
        ).astype(jnp.float32),
        lax.psum(query_part.astype(jnp.bfloat16), SEQ).astype(jnp.float32),
    )
    own_grad = own_grad + exact_two("wgb,wgthe->wbthe", owned_hot, global_total)
    far_flat = far_back.reshape(windows, -1, BLOCK, doubled)
    returning = exact_two("wspc,wste->pwcte", picker, far_flat)
    arrived_far = lax.all_to_all(
        returning.astype(jnp.bfloat16), SEQ, split_axis=0, concat_axis=0, tiled=True
    ).astype(returning.dtype)
    own_grad = own_grad + exact_two("wqcbh,qwcte->wbthe", sender, arrived_far)
    return (own_grad.reshape(windows, blocks_dev * BLOCK, head_count, doubled), query_total)


def attention_back(
    grad_attended,
    queries,
    sliding,
    global_kv,
    distant,
    probabilities,
    key_part,
    value_part,
    global_queries,
    full_probs,
    sender,
    picker,
    owned_hot,
):
    head_dim = queries.shape[-1]
    score_scale = head_dim ** (-0.5)
    windows, blocks_dev, _, head_count, _ = queries.shape
    on_global = jnp.sum(owned_hot, axis=1)[:, :, None, None, None] > 0
    selected = mixed_sum("wgb,wbqhd->wgqhd", owned_hot.astype(jnp.bfloat16), grad_attended)
    rows_grad = lax.psum(selected.astype(jnp.bfloat16), SEQ).reshape(
        windows, -1, head_count, head_dim
    )
    grad_attended = jnp.where(on_global, jnp.zeros_like(grad_attended), grad_attended)
    low_probs = probabilities.astype(jnp.bfloat16)
    near_grad = mixed_sum("wbqhd,wbkhd->wbhqk", grad_attended, sliding[..., head_dim:])
    global_grad = mixed_sum("wbqhd,wkhd->wbhqk", grad_attended, global_kv[..., head_dim:])
    far_grad = mixed_sum("wbqhd,wbhrkd->wbhqrk", grad_attended, distant[..., head_dim:])
    far_grad = far_grad.reshape(windows, blocks_dev, head_count, BLOCK, -1)
    grad_probs = jnp.concatenate([near_grad, global_grad, far_grad], axis=4)
    grad_scores = probabilities * (
        grad_probs - jnp.sum(probabilities * grad_probs, axis=4, keepdims=True)
    )
    grad_scores = grad_scores.astype(jnp.bfloat16)
    near_split, global_split, far_split = split_keys(grad_scores, sliding, global_kv, distant)
    near_probs, global_probs, far_probs = split_keys(low_probs, sliding, global_kv, distant)
    grad_query = mixed_sum("wbhqk,wbkhd->wbqhd", near_split, sliding[..., :head_dim])
    grad_query = grad_query + mixed_sum(
        "wbhqk,wkhd->wbqhd", global_split, global_kv[..., :head_dim]
    )
    grad_query = (
        grad_query + mixed_sum("wbhqrk,wbhrkd->wbqhd", far_split, distant[..., :head_dim])
    ) * score_scale
    near_back = jnp.concatenate(
        [
            mixed_sum("wbhqk,wbqhd->wbkhd", near_split, queries) * score_scale,
            mixed_sum("wbhqk,wbqhd->wbkhd", near_probs, grad_attended),
        ],
        axis=4,
    )
    global_back = jnp.concatenate(
        [
            mixed_sum("wbhqk,wbqhd->wkhd", global_split, queries) * score_scale,
            mixed_sum("wbhqk,wbqhd->wkhd", global_probs, grad_attended),
        ],
        axis=3,
    )
    far_back = jnp.concatenate(
        [
            mixed_sum("wbhqrk,wbqhd->wbhrkd", far_split, queries) * score_scale,
            mixed_sum("wbhqrk,wbqhd->wbhrkd", far_probs, grad_attended),
        ],
        axis=5,
    )
    full_grad_probs = mixed_sum("wqhd,wkhd->whqk", rows_grad, value_part)
    partial_dot = jnp.sum(full_probs * full_grad_probs, axis=3, keepdims=True)
    row_dot = lax.psum(partial_dot, SEQ)
    full_grad_scores = (full_probs * (full_grad_probs - row_dot)).astype(jnp.bfloat16)
    query_part = mixed_sum("whqk,wkhd->wqhd", full_grad_scores, key_part) * score_scale
    full_key_grad = mixed_sum("whqk,wqhd->wkhd", full_grad_scores, global_queries) * score_scale
    full_value_grad = mixed_sum("whqk,wqhd->wkhd", full_probs.astype(jnp.bfloat16), rows_grad)
    grad_paired, query_total = return_blocks(
        near_back, global_back, far_back, query_part, sender, picker, owned_hot
    )
    grad_query = grad_query + exact_two(
        "wgb,wgqhd->wbqhd", owned_hot, query_total.reshape(windows, -1, BLOCK, head_count, head_dim)
    )
    grad_paired = grad_paired + jnp.concatenate([full_key_grad, full_value_grad], axis=3)
    return (grad_query, grad_paired)


def layer_backward(stored, grad_output, weights, tables):
    row_weights, down_weights, vector_weights = weights
    sender, picker, owned_hot, key_mask, full_mask = tables
    (
        hidden,
        normed,
        queries,
        sliding,
        global_kv,
        distant,
        probabilities,
        mixed_low,
        middle,
        normed_two,
        up_value,
        active,
        key_part,
        value_part,
        global_queries,
        full_probs,
    ) = stored
    model_width = row_weights.shape[0]
    windows, tokens, _ = hidden.shape
    blocks_dev = tokens // BLOCK
    head_dim = model_width // HEADS
    (
        gain_one,
        shift_one,
        bias_query,
        bias_value,
        bias_out,
        gain_two,
        shift_two,
        bias_down,
        bias_up,
    ) = split_vectors(vector_weights, model_width)
    grad_ffn = grad_output.astype(jnp.bfloat16)
    grad_bias_down = jnp.sum(grad_ffn.astype(jnp.float32), axis=(0, 1))
    grad_down = mixed_sum("wtf,wtd->fd", active, grad_ffn)
    grad_active = mixed_sum("wtd,fd->wtf", grad_ffn, down_weights)
    gelu_pull = jax.vjp(partial(jax.nn.gelu, approximate=False), up_value)[1]
    grad_up = gelu_pull(grad_active)[0].astype(jnp.bfloat16)
    grad_bias_up = jnp.sum(grad_up.astype(jnp.float32), axis=(0, 1))
    grad_in = mixed_sum("wtd,wtf->df", normed_two, grad_up)
    grad_normed_two = mixed_sum("wtf,df->wtd", grad_up, row_weights[:, 4 * model_width :])
    norm_pull_two = jax.vjp(norm_rows, middle, gain_two, shift_two)[1]
    grad_middle_norm, grad_gain_two, grad_shift_two = norm_pull_two(grad_normed_two)
    grad_middle = grad_output + grad_middle_norm
    grad_branch = grad_middle.astype(jnp.bfloat16)
    grad_bias_out = jnp.sum(grad_branch.astype(jnp.float32), axis=(0, 1))
    grad_out_weight = mixed_sum("wtd,wte->de", mixed_low, grad_branch)
    grad_attended = mixed_sum(
        "wte,de->wtd", grad_branch, row_weights[:, 3 * model_width : 4 * model_width]
    ).astype(jnp.bfloat16)
    grad_attended = grad_attended.reshape(windows, blocks_dev, BLOCK, HEADS, head_dim)
    grad_query, grad_paired = attention_back(
        grad_attended,
        queries,
        sliding,
        global_kv,
        distant,
        probabilities,
        key_part,
        value_part,
        global_queries,
        full_probs,
        sender,
        picker,
        owned_hot,
    )
    grad_projected = jnp.concatenate(
        [
            grad_query.reshape(windows, tokens, model_width),
            grad_paired[..., :head_dim].reshape(windows, tokens, model_width),
            grad_paired[..., head_dim:].reshape(windows, tokens, model_width),
        ],
        axis=2,
    ).astype(jnp.bfloat16)
    summed = jnp.sum(grad_projected.astype(jnp.float32), axis=(0, 1))
    grad_bias_query = summed[:model_width]
    grad_bias_value = summed[2 * model_width :]
    grad_projection = mixed_sum("wtd,wte->de", normed, grad_projected)
    grad_normed = mixed_sum("wte,de->wtd", grad_projected, row_weights[:, : 3 * model_width])
    norm_pull_one = jax.vjp(norm_rows, hidden, gain_one, shift_one)[1]
    grad_hidden_norm, grad_gain_one, grad_shift_one = norm_pull_one(grad_normed)
    grad_hidden = grad_middle + grad_hidden_norm
    grad_rows = jnp.concatenate([grad_projection, grad_out_weight, grad_in], axis=1)
    grad_vectors = jnp.concatenate(
        [
            grad_gain_one,
            grad_shift_one,
            grad_bias_query,
            grad_bias_value,
            grad_bias_out,
            grad_gain_two,
            grad_shift_two,
            grad_bias_down,
            grad_bias_up,
        ]
    )
    return (grad_hidden, (grad_rows, grad_down, grad_vectors))


def adam_update(master, first_old, second_old, gradient, step_rate, decay_rate):
    first_new = 0.5 * first_old + 0.5 * gradient
    second_new = 0.5 * second_old + 0.5 * gradient * gradient
    first_hat = first_new / (1.0 - 0.5**STEP)
    second_hat = second_new / (1.0 - 0.5**STEP)
    master_new = master - step_rate * (
        first_hat / (jnp.sqrt(second_hat) + 1e-08) + decay_rate * master
    )
    return (master_new, first_new, second_new)


def general_shards(
    block_input,
    cotangent,
    random_ids,
    segment_ids,
    global_ids,
    w_rows,
    w_rows_first,
    w_rows_second,
    w_down,
    w_down_first,
    w_down_second,
    vectors,
    vectors_first,
    vectors_second,
):
    section_index = lax.axis_index(SECTION)
    seq_place = lax.axis_index(SEQ)
    groups = lax.axis_size(SEQ)
    row_weights, down_weights, vector_low = (
        lax.all_gather(w_rows[0].astype(jnp.bfloat16), (DP, SEQ), axis=1, tiled=True),
        lax.all_gather(w_down[0].astype(jnp.bfloat16), (DP, SEQ), axis=0, tiled=True),
        lax.all_gather(vectors[0].astype(jnp.bfloat16), (DP, SEQ), axis=0, tiled=True),
    )
    weights = (row_weights, down_weights, vector_low.astype(jnp.float32))
    micro_count, windows, tokens, model_width = block_input.shape
    received = jnp.zeros((windows, tokens, model_width), jnp.bfloat16)
    results = jnp.zeros(block_input.shape, jnp.float32)
    full_totals = (
        jnp.zeros(row_weights.shape, jnp.float32),
        jnp.zeros(down_weights.shape, jnp.float32),
        jnp.zeros(vector_low.shape, jnp.float32),
    )

    def tick(tick_index, carry):
        received, results, full_totals = carry
        forward_mb = jnp.clip(tick_index - section_index, 0, micro_count - 1)
        behind_raw = tick_index - 2 + section_index
        behind = jnp.clip(behind_raw, 0, micro_count - 1)
        live_mask = ((behind_raw >= 0) & (behind_raw < micro_count)).astype(jnp.float32)
        tables_forward = route_tables(
            lax.dynamic_index_in_dim(random_ids, forward_mb, 0, keepdims=False),
            lax.dynamic_index_in_dim(segment_ids, forward_mb, 0, keepdims=False),
            lax.dynamic_index_in_dim(global_ids, forward_mb, 0, keepdims=False),
            seq_place,
            groups,
        )
        tables_behind = route_tables(
            lax.dynamic_index_in_dim(random_ids, behind, 0, keepdims=False),
            lax.dynamic_index_in_dim(segment_ids, behind, 0, keepdims=False),
            lax.dynamic_index_in_dim(global_ids, behind, 0, keepdims=False),
            seq_place,
            groups,
        )
        incoming_values = received.astype(jnp.float32)
        first_input = lax.dynamic_index_in_dim(block_input, forward_mb, 0, keepdims=False).astype(
            jnp.float32
        )
        forward_input = jnp.where(section_index == 0, first_input, incoming_values)
        forward_output = layer_forward(forward_input, weights, tables_forward)[0]
        back_source = lax.dynamic_index_in_dim(block_input, behind, 0, keepdims=False).astype(
            jnp.float32
        )
        back_input = jnp.where(section_index == 0, back_source, incoming_values)
        given_grad = lax.dynamic_index_in_dim(cotangent, behind, 0, keepdims=False).astype(
            jnp.float32
        )
        back_grad = jnp.where(section_index == 0, incoming_values, given_grad) * live_mask
        stored = layer_forward(back_input, weights, tables_behind)[1]
        grad_input, gradients = layer_backward(stored, back_grad, weights, tables_behind)
        outgoing = jnp.where(section_index == 0, forward_output, grad_input).astype(jnp.bfloat16)
        finished = jnp.where(section_index == 0, grad_input, forward_output)
        updated = lax.dynamic_update_index_in_dim(results, finished, behind, 0)
        results = jnp.where(live_mask > 0, updated, results)
        full_totals = tuple(
            (total_part + grad_part for total_part, grad_part in zip(full_totals, gradients))
        )
        return (partner(outgoing, SECTION, 0), results, full_totals)

    received, results, full_totals = lax.fori_loop(
        0, micro_count + 2, tick, (received, results, full_totals)
    )
    shard_totals = (
        lax.psum_scatter(full_totals[0], (DP, SEQ), scatter_dimension=1, tiled=True),
        lax.psum_scatter(full_totals[1], (DP, SEQ), scatter_dimension=0, tiled=True),
        lax.psum_scatter(full_totals[2], (DP, SEQ), scatter_dimension=0, tiled=True),
    )
    new_rows, new_rows_first, new_rows_second = adam_update(
        w_rows[0], w_rows_first[0], w_rows_second[0], shard_totals[0], rate_matrix, decay_matrix
    )
    new_down, new_down_first, new_down_second = adam_update(
        w_down[0], w_down_first[0], w_down_second[0], shard_totals[1], rate_matrix, decay_matrix
    )
    new_vectors, new_vectors_first, new_vectors_second = adam_update(
        vectors[0], vectors_first[0], vectors_second[0], shard_totals[2], rate_vector, 0.0
    )
    return (
        results[None],
        new_rows[None],
        new_rows_first[None],
        new_rows_second[None],
        new_down[None],
        new_down_first[None],
        new_down_second[None],
        new_vectors[None],
        new_vectors_first[None],
        new_vectors_second[None],
    )


LOW = jnp.bfloat16
LOG_HIGH = [float(np.log(c).astype(ml_dtypes.bfloat16)) for c in (1.0, 2.0, 3.0)]
LOG_LOW = [float(np.log(c)) - high for c, high in zip((1.0, 2.0, 3.0), LOG_HIGH)]
CHUNK = 256
VMEM_BYTES = 60 * 1024 * 1024


def dot_rows(left, right):
    return lax.dot_general(left, right, (((1,), (1,)), ((), ())), preferred_element_type=jnp.float32)


def dot_plain(left, right):
    return lax.dot_general(left, right, (((1,), (0,)), ((), ())), preferred_element_type=jnp.float32)


def dot_tokens(left, right):
    return lax.dot_general(left, right, (((0,), (0,)), ((), ())), preferred_element_type=jnp.float32)


def swap(value):
    return lax.ppermute(value, SECTION, [(0, 1), (1, 0)])


def normalized(values_in):
    row_mean = jnp.mean(values_in, axis=-1, keepdims=True)
    centred = values_in - row_mean
    spread = jnp.mean(centred * centred, axis=-1, keepdims=True)
    scale = lax.rsqrt(spread + epsilon)
    return centred * scale, scale


class Shares:
    def __init__(self, width, columns, depth, vector_len):
        self.width = width
        self.columns = columns
        self.depth = depth
        self.vector_len = vector_len
        self.half = columns // 2
        self.per = width // columns
        self.groups = columns // depth

    def unpack(self, gathered, core):
        rows, down, vec = gathered
        vec = vec.reshape(-1, TAIL, self.width)[:, 0, : self.vector_len].reshape(-1)
        pieces = split_vectors(vec.astype(jnp.float32), self.width)
        for index in (2, 3):
            pieces[index] = lax.dynamic_index_in_dim(
                pieces[index].reshape(self.per, 2, self.half), core, 1, keepdims=False
            ).reshape(-1)
        pieces[8] = lax.dynamic_index_in_dim(
            pieces[8].reshape(-1, 2, self.depth // 2), core, 1, keepdims=False
        ).reshape(-1)
        nothing = jnp.zeros_like(pieces[2])
        proj = [pieces[2], nothing, pieces[3], nothing]
        order = [pieces[index] for index in (0, 1, 4, 5, 6, 7)] + proj + [pieces[8]]
        return (
            (rows.reshape(-1, self.width), down.reshape(-1, self.width)),
            jnp.concatenate(order).reshape(-1, self.width),
        )

    def by_shard(self, grads, vector_grads, core):
        rows, down = grads
        half, per, width = self.half, self.per, self.width
        hot = (jnp.arange(2) == core).astype(jnp.float32)
        spread = list(vector_grads)
        for index in (2, 3):
            spread[index] = (
                spread[index].reshape(per, 1, half) * hot[None, :, None]
            ).reshape(-1)
        spread[8] = (spread[8].reshape(-1, 1, self.depth // 2) * hot[None, :, None]).reshape(-1)
        for index in (0, 1, 4, 5, 6, 7):
            spread[index] = spread[index] * hot[0]
        vec = jnp.concatenate(spread).reshape(-1, 1, self.vector_len)
        vec = jnp.pad(vec, ((0, 0), (0, TAIL - 1), (0, width - self.vector_len))).astype(LOW)
        return [array.reshape(2, 2, 4, -1, width) for array in (rows, down, vec)]


MESH = pl.DeviceIdType.MESH
PIECE = 48
TAIL = 16


def prepare_kernel(shares, rows_ref, down_ref, vector_ref, rows_out, down_out, vector_out):
    core = lax.axis_index(SECTION)
    offset = lax.axis_index((DP, SEQ)) * shares.columns
    half, per, width, depth = shares.half, shares.per, shares.width, shares.depth // 2
    is_inner = (offset >= 3 * width) & (offset < 4 * width)
    is_hidden = offset >= 4 * width

    @pl.when(is_inner)
    def _():
        for which in range(2):
            side = core if which == 0 else 1 - core
            held = [rows_ref[pl.ds((2 * j + side) * half, half), :] for j in range(per)]
            turned = jnp.transpose(jnp.concatenate(held, axis=0))
            rows_out[which] = jnp.concatenate([turned[:half], turned[half:]], axis=1).astype(LOW)

    @pl.when(jnp.logical_not(is_inner))
    def _():
        turned = jnp.transpose(rows_ref[...]).astype(LOW)
        plain = [turned[:half], turned[half:]]
        hidden = [
            jnp.concatenate(
                [turned[(2 * j + side) * depth :][:depth] for j in range(shares.groups)], axis=0
            )
            for side in range(2)
        ]
        halves = [jnp.where(is_hidden, b, a) for a, b in zip(plain, hidden)]
        rows_out[0] = jnp.where(core == 0, halves[0], halves[1])
        rows_out[1] = jnp.where(core == 0, halves[1], halves[0])

    down = down_ref[...].astype(LOW)
    down_out[0] = jnp.where(core == 0, down[:depth], down[depth:])
    down_out[1] = jnp.where(core == 0, down[depth:], down[:depth])
    vector_out[...] = jnp.zeros_like(vector_out)
    vector_out[0:1, : shares.vector_len] = vector_ref[...].astype(LOW)


def prepare(shares, rows, down, vector):
    return pl.pallas_call(
        partial(prepare_kernel, shares),
        out_shape=[
            jax.ShapeDtypeStruct((2, shares.half, shares.width), LOW),
            jax.ShapeDtypeStruct((2, shares.depth // 2, shares.width), LOW),
            jax.ShapeDtypeStruct((TAIL, shares.width), LOW),
        ],
        compiler_params=pltpu.CompilerParams(vmem_limit_bytes=VMEM_BYTES),
    )(rows, down, vector)


class Place:
    def __init__(self):
        self.core = lax.axis_index(SECTION)
        self.dp = lax.axis_index(DP)
        self.z = lax.axis_index(SEQ)
        self.y, self.x = self.dp // 2, self.dp % 2
        self.high, self.low = self.z // 2, self.z % 2
        self.inner = self.high + self.low == 1
        self.outer = self.high + self.low != 1
        self.partner = {SECTION: 1 - self.core}
        self.along_x = {DP: 2 * self.y + 1 - self.x}
        self.along_y = {DP: 2 * (1 - self.y) + self.x}
        self.across = {SEQ: 3 - self.z}
        self.beside = {SEQ: 2 * self.high + 1 - self.low}
        self.others = [{SEQ: (self.z + by) % 4} for by in (1, 2, 3)]
        self.own = pl.ds(self.z, 1)
        self.next = pl.ds(2 * self.high + 1 - self.low, 1)
        self.near = pl.ds(2 * self.high, 2)
        self.far = pl.ds(2 * (1 - self.high), 2)

    def greet(self):
        barrier = pltpu.get_barrier_semaphore()
        everyone = [self.partner, self.along_x, self.along_y] + self.others
        for device in everyone:
            pl.semaphore_signal(barrier, inc=1, device_id=device, device_id_type=MESH)
        pl.semaphore_wait(barrier, len(everyone))


def remote(src, dst, sems, spots, device):
    return pltpu.make_async_remote_copy(
        src_ref=src,
        dst_ref=dst,
        send_sem=sems[0].at[spots[0]],
        recv_sem=sems[1].at[spots[1]],
        device_id=device,
        device_id_type=MESH,
    )


def chunk_pairs(shares):
    pairs = []
    for array, length in ((0, shares.half), (1, shares.depth // 2)):
        for start in range(0, length, 2 * PIECE):
            pairs.append([(array, start, PIECE, 0), (array, start + PIECE, PIECE, 1)])
    pairs[0].append((2, 0, TAIL, 0))
    return pairs


def quad_pairs(shares):
    length = (shares.half + shares.depth // 2) // 2
    pairs = [
        [(0, start, PIECE, None), (1, start, PIECE, None)] for start in range(0, length, PIECE)
    ]
    pairs[0].append((2, 0, TAIL, 0))
    return pairs


def gather_kernel(shares, *refs):
    (rows_in, down_in, vector_in, x_in, cot_in), refs = refs[:5], refs[5:]
    outs, refs = [refs[0:3], refs[3:6]], refs[6:]
    hops, (x_out, cot_out), refs = refs[:2], refs[2:4], refs[4:]
    local, swap_send, swap_recv, z_send, z_recv, send, recv = refs
    here = Place()
    core, y, x, z = here.core, here.y, here.x, here.z
    half = x_in.shape[2] // 2
    rows_half, down_half = shares.half // 2, shares.depth // 4
    here.greet()

    def slices(source, target, base):
        mine = pl.ds(pl.multiple_of(core * half, half), half)
        sems = (z_send, z_recv)
        own = pltpu.make_async_copy(
            source.at[z, 0, mine], target.at[z, core], local.at[8 + base // 4]
        )
        sends, arrivals = [], []
        for by in (1, 2, 3):
            spots = (base + by - 1, base + by - 1)
            device = here.others[by - 1]
            sends.append(
                remote(source.at[(z + by) % 4, 0, mine], target.at[z, core], sems, spots, device)
            )
            arrivals.append(
                remote(
                    source.at[z, 0, mine], target.at[(z + 4 - by) % 4, core], sems, spots, device
                )
            )
        spots = (base + 3, base + 3)
        forward = remote(target.at[:, core], target.at[:, core], sems, spots, here.partner)
        arrived = remote(target.at[:, 1 - core], target.at[:, 1 - core], sems, spots, here.partner)
        return own, sends, arrivals, forward, arrived

    x_moves = slices(x_in, x_out, 0)
    cot_moves = slices(cot_in, cot_out, 4)

    def open_slices(moves):
        moves[0].start()
        for copy in moves[1]:
            copy.start()

    def pass_slices(moves):
        moves[0].wait()
        for copy in moves[2]:
            copy.wait_recv()
        moves[3].start()

    def close_slices(moves):
        for copy in moves[1]:
            copy.wait_send()
        moves[3].wait_send()
        moves[4].wait_recv()

    def first_moves(layer, which):
        down = down_in.at[which]
        rows = rows_in.at[which]
        if layer == 0:
            return [
                (0, rows, outs[0][0].at[y, x, z]),
                (1, down, outs[0][1].at[y, x, z]),
                (2, vector_in, outs[0][2].at[y, x, z]),
            ]
        moves = [(7, vector_in, outs[1][2].at[y, x, z])]
        for part in range(2):
            target = outs[1][part]
            moves.append(
                (
                    3 + 2 * part,
                    rows.at[pl.ds(part * rows_half, rows_half)],
                    target.at[z, pl.ds(0, rows_half)],
                )
            )
            moves.append(
                (
                    4 + 2 * part,
                    down.at[pl.ds(part * down_half, down_half)],
                    target.at[z, pl.ds(rows_half, down_half)],
                )
            )
        return moves

    swaps = (swap_send, swap_recv)
    for layer in range(2):

        @pl.when(core == layer)
        def _():
            across = [
                remote(src, dst, swaps, (spot, spot), here.partner)
                for spot, src, dst in first_moves(layer, 1)
            ]
            own = [
                pltpu.make_async_copy(src, dst, local.at[spot])
                for spot, src, dst in first_moves(layer, 0)
            ]
            for copy in across + own:
                copy.start()
            for copy in own:
                copy.wait()
            for copy in across:
                copy.wait_send()
            for spot, src, dst in first_moves(1 - layer, 0):
                remote(src, dst, swaps, (spot, spot), here.partner).wait_recv()

    numbers, pairs = {}, []
    for layer in range(2):
        for pair in chunk_pairs(shares) if layer == 0 else quad_pairs(shares):
            entry = []
            for array, start, length, order in pair:
                ref = outs[layer][array]
                rows = pl.ds(start, length)
                flat = order is None
                number = len(numbers)
                sems = (send, recv)

                def part(which):
                    return ref.at[which, rows] if flat else ref.at[y, x, which, rows]

                def copy(piece, spots, device):
                    return remote(piece, piece, sems, ((number, spots[0]), (number, spots[1])), device)

                steps = {
                    "z": copy(part(here.own), (0, 0), here.beside),
                    "across": copy(part(here.near), (1, 1), here.across),
                    "on": copy(part(here.far), (4, 1), here.beside),
                }
                arrive = [
                    copy(part(here.next), (0, 0), here.beside),
                    copy(part(here.far), (1, 1), here.across),
                ]
                if order == 0:
                    steps["one"] = copy(ref.at[y, x, :, rows], (2, 2), here.along_y)
                    steps["two"] = copy(ref.at[:, x, :, rows], (3, 3), here.along_x)
                    arrive.append(copy(ref.at[1 - y, x, :, rows], (2, 2), here.along_y))
                    arrive.append(copy(ref.at[:, 1 - x, :, rows], (3, 3), here.along_x))
                elif order == 1:
                    steps["one"] = copy(ref.at[y, x, :, rows], (2, 2), here.along_x)
                    steps["two"] = copy(ref.at[y, :, :, rows], (3, 3), here.along_y)
                    arrive.append(copy(ref.at[y, 1 - x, :, rows], (2, 2), here.along_x))
                    arrive.append(copy(ref.at[1 - y, :, :, rows], (3, 3), here.along_y))
                else:
                    device = here.along_x if array else here.along_y
                    spots = ((number, 2), (number, 2))
                    hop = remote(ref.at[:, rows], hops[array].at[:, rows], sems, spots, device)
                    steps["one"] = hop
                    arrive.append(hop)
                numbers[number] = (steps, arrive)
                entry.append(number)
            pairs.append(entry)

    def issue(name, entry):
        after = {"z": None, "across": 0, "on": 1, "one": 1, "two": 2}[name]

        def start():
            for number in entry:
                steps, arrive = numbers[number]
                if name in steps:
                    if after is not None and not (name == "one"):
                        arrive[after].wait_recv()
                    steps[name].start()

        if name in ("across", "on"):
            pl.when(here.inner)(start)
        else:
            start()

    def arrived(entry, index, where):
        def wait():
            for number in entry:
                numbers[number][1][index].wait_recv()

        pl.when(where)(wait)

    first, second = pairs[: len(chunk_pairs(shares))], pairs[len(chunk_pairs(shares)) :]
    for entry in first:
        issue("z", entry)
    for entry in first:
        issue("across", entry)
        arrived(entry, 0, here.outer)
    for entry in first[:-1]:
        issue("on", entry)
        arrived(entry, 1, here.outer)
        issue("one", entry)
    issue("on", first[-1])
    for entry in second:
        issue("z", entry)
    open_slices(x_moves)
    arrived(first[-1], 1, here.outer)
    issue("one", first[-1])
    issue("two", first[0])
    for entry in second:
        issue("across", entry)
        arrived(entry, 0, here.outer)
    issue("two", first[1])
    open_slices(cot_moves)
    for entry in second:
        issue("on", entry)
    issue("two", first[2])
    pass_slices(x_moves)
    for entry in second:
        arrived(entry, 1, here.outer)
        issue("one", entry)
    for entry in second:
        for number in entry:
            steps, arrive = numbers[number]
            arrive[2].wait_recv()
            if "two" in steps:
                steps["two"].start()
    pass_slices(cot_moves)
    for steps, arrive in numbers.values():
        if len(arrive) == 4:
            arrive[3].wait_recv()
        for name in steps:
            if name not in ("across", "on"):
                steps[name].wait_send()

    @pl.when(here.inner)
    def _():
        for steps, _ in numbers.values():
            steps["across"].wait_send()
            steps["on"].wait_send()

    close_slices(x_moves)
    close_slices(cot_moves)


def gather(shares, prepared, block_input, cotangent):
    micro, _, tokens, width = block_input.shape
    chunks = sum(len(pair) for pair in chunk_pairs(shares) + quad_pairs(shares))
    lengths = (shares.half, shares.depth // 2, TAIL)
    layer = [jax.ShapeDtypeStruct((2, 2, 4, rows, width), LOW) for rows in lengths]
    quad = jax.ShapeDtypeStruct((4, (lengths[0] + lengths[1]) // 2, width), LOW)
    window = jax.ShapeDtypeStruct((micro, 2, tokens // 2, width), LOW)
    anywhere = pl.BlockSpec(memory_space=pl.ANY)
    results = pl.pallas_call(
        partial(gather_kernel, shares),
        in_specs=[pl.BlockSpec(memory_space=pltpu.VMEM)] * 3 + [anywhere] * 2,
        out_specs=[anywhere] * 10,
        out_shape=layer + [quad, quad, layer[2]] + [quad, quad] + [window, window],
        scratch_shapes=[
            pltpu.SemaphoreType.DMA((10,)),
            pltpu.SemaphoreType.DMA((8,)),
            pltpu.SemaphoreType.DMA((8,)),
            pltpu.SemaphoreType.DMA((8,)),
            pltpu.SemaphoreType.DMA((8,)),
            pltpu.SemaphoreType.DMA((chunks, 5)),
            pltpu.SemaphoreType.DMA((chunks, 4)),
        ],
        compiler_params=pltpu.CompilerParams(
            collective_id=0, has_side_effects=True, vmem_limit_bytes=VMEM_BYTES
        ),
    )(*prepared, block_input, cotangent)
    return results[0:3], results[3:5] + results[6:8], results[5], results[8], results[9]


def over(value, bit):
    return lax.ppermute(value, DP, [(i, i ^ bit) for i in range(4)])


def layout_moves(shares, y, x, pieces, arrays):
    rows_half, down_half = shares.half // 2, shares.depth // 4
    moves = []
    for part in range(2):
        for index, (by_y, by_x) in enumerate(((0, 0), (1, 0), (0, 1), (1, 1))):
            piece = pieces[part][index]
            at_y, at_x = y ^ by_y, x ^ by_x
            for array, length, start in ((0, rows_half, 0), (1, down_half, rows_half)):
                moves.append(
                    (
                        piece.at[:, pl.ds(start, length)],
                        arrays[array].at[at_y, at_x, :, pl.ds(part * length, length)],
                    )
                )
    return moves


def layout_kernel(shares, joins, *refs):
    dp = lax.axis_index(DP)
    if joins:
        pieces, arrays = [refs[0:4], refs[4:8]], refs[8:10]
    else:
        arrays, pieces = refs[0:2], [refs[2:6], refs[6:10]]
    for spot in range(4):

        @pl.when(dp == spot)
        def _():
            for piece, place in layout_moves(shares, spot // 2, spot % 2, pieces, arrays):
                src, dst = (piece, place) if joins else (place, piece)
                dst[...] = src[...]


def layout(shares, joins, *arrays):
    half, depth, width = shares.half, shares.depth // 2, shares.width
    length = (half + depth) // 2
    merged_specs = [
        pl.BlockSpec((2, 2, 1, rows, width), lambda z: (0, 0, z, 0, 0)) for rows in (half, depth)
    ]
    merged_shapes = [(2, 2, 4, rows, width) for rows in (half, depth)]
    piece_specs = [pl.BlockSpec((1, length, width), lambda z: (z, 0, 0))] * 8
    piece_shapes = [(4, length, width)] * 8
    return pl.pallas_call(
        partial(layout_kernel, shares, joins),
        grid=(4,),
        in_specs=piece_specs if joins else merged_specs,
        out_specs=merged_specs if joins else piece_specs,
        out_shape=[
            jax.ShapeDtypeStruct(shape, LOW) for shape in (merged_shapes if joins else piece_shapes)
        ],
        compiler_params=pltpu.CompilerParams(vmem_limit_bytes=VMEM_BYTES),
        cost_estimate=pl.CostEstimate(
            flops=0, bytes_accessed=64 * (half + depth) * width, transcendentals=0
        ),
    )(*arrays)


def tied(value, flying):
    return lax.optimization_barrier((value, flying))


def spread_quads(shares, quads):
    low, high, low_y, high_x = quads
    flying = (low_y, high_x, over(low, 1), over(high, 2))
    low_y, high_x, low_x, high_y = yield flying
    flying = (over(low_y, 1), over(high_x, 2))
    low_both, high_both = yield flying
    yield layout(shares, True, low, low_y, low_x, low_both, high, high_y, high_x, high_both)


def sum_quads(shares, arrays):
    pieces = layout(shares, False, *arrays)

    low, low_y, low_x, low_both = pieces[:4]
    high, high_y, high_x, high_both = pieces[4:]
    flying = (low_x, high_y, over(low_both, 1), over(high_both, 2))
    low_x, high_y, low_hop, high_hop = yield flying
    low_y, high_x = low_y + low_hop, high_x + high_hop
    flying = (low_y, high_x, over(low_x, 1), over(high_y, 2))
    low_y, high_x, low_x, high_y = yield flying
    flying = (over(low_y, 2), over(high_x, 1))
    low_y, high_x = yield flying
    yield (low, high, low_x, high_x, low_y, high_y)


class Beside:
    def __init__(self, hops=None):
        self.hops = hops
        self.flying = None if hops is None else next(hops)

    def tie(self, value):
        if self.hops is None:
            return value
        value, arrived = tied(value, self.flying)
        self.flying = self.hops.send(arrived)
        return value


def scatter_kernel(shares, *refs):
    (rows_zero, down, vec_zero, *terms, vec_one), refs = refs[:10], refs[10:]
    (dx_ref, final_ref, halves, slices), refs = refs[:4], refs[4:]
    work, refs = [refs[0:3], refs[3:6]], refs[6:]
    added, refs = refs[:4], refs[4:]
    (got_one, got_two, got_far, got_across, got_near, total), refs = refs[:6], refs[6:]
    load, local, swap_send, swap_recv, z_send, z_recv, send, recv = refs
    here = Place()
    core, y, x, z = here.core, here.y, here.x, here.z
    rows_half, down_half = shares.half // 2, shares.depth // 4
    down_base = shares.half
    tail_base = shares.half + shares.depth // 2

    moves = [
        [(rows_zero, work[0][0]), (down, work[0][1]), (vec_zero, work[0][2])],
        [(terms[0], work[1][0]), (terms[1], work[1][1]), (vec_one, work[1][2])],
    ]
    moves[1] += zip(terms[2:], added)
    loads = [
        [
            pltpu.make_async_copy(src, dst, load.at[layer, index])
            for index, (src, dst) in enumerate(moves[layer])
        ]
        for layer in range(2)
    ]
    for layer in (1, 0):
        for copy in loads[layer]:
            copy.start()
    here.greet()

    def place_of(layer, array, start):
        if array == 2:
            return tail_base
        if layer == 0:
            return (0, down_base)[array] + start
        if start < rows_half:
            return array * rows_half + start
        return down_base + array * down_half + start - rows_half

    pairs, chunks = [], []
    for layer in (1, 0):
        for index, pair in enumerate(quad_pairs(shares) if layer else chunk_pairs(shares)):
            entry = []
            for array, start, length, order in pair:
                entry.append((len(chunks), layer, array, start, length, order))
                chunks.append(entry[-1])
            pairs.append((index, entry))

    def pieces(chunk):
        number, layer, array, start, length, order = chunk
        ref = work[layer][array]
        rows = pl.ds(start, length)
        sems = (send, recv)
        keeps, slots, copies = [], [], []

        def part(which):
            return ref.at[which, rows] if order is None else ref.at[y, x, which, rows]

        def add(src, slot, device, keep):
            spots = (number, len(copies))
            copies.append(remote(src, slot, sems, (spots, spots), device))
            slots.append(slot)
            keeps.append(keep)

        room = pl.ds(0, length)
        if order == 0:
            add(ref.at[:, 1 - x, :, rows], got_one.at[number, :, :, room], here.along_x, ref.at[:, x, :, rows])
            add(ref.at[1 - y, x, :, rows], got_two.at[number, :, room], here.along_y, ref.at[y, x, :, rows])
        elif order == 1:
            add(ref.at[1 - y, :, :, rows], got_one.at[number, :, :, room], here.along_y, ref.at[y, :, :, rows])
            add(ref.at[y, 1 - x, :, rows], got_two.at[number, :, room], here.along_x, ref.at[y, x, :, rows])
        else:
            copies, slots, keeps = [None] * 2, [None] * 2, [None] * 2
        add(part(here.far), got_far.at[number, :, room], here.beside, part(here.far))
        add(part(here.far), got_across.at[number, :, room], here.across, part(here.near))
        add(part(here.next), got_near.at[number, :, room], here.beside, part(here.own))
        return copies, keeps, slots

    built = [pieces(chunk) for chunk in chunks]
    loaded = set()

    def land(number, phase):
        copies, keeps, slots = built[number]
        copies[phase].wait_recv()
        keep, slot = keeps[phase], slots[phase]
        keep[...] = keep[...] + slot[...]

    def run(chunk, phase):
        number, layer, array, start, length, order = chunk
        copies, keeps, slots = built[number]
        if (layer, array) not in loaded:
            loaded.add((layer, array))
            loads[layer][array].wait()
            if layer == 1 and array < 2:
                loads[1][3 + array].wait()
                loads[1][5 + array].wait()
                for group in range(4):
                    parts = (work[1][array], added[array], added[2 + array])
                    summed = sum(part[group].astype(jnp.float32) for part in parts)
                    work[1][array][group] = summed.astype(LOW)
        if phase < 2:
            if order is not None:
                if phase:
                    land(number, 0)
                copies[phase].start()
        elif phase == 2:
            if order is not None:
                land(number, 1)

            @pl.when(here.outer)
            def _():
                copies[2].start()
                copies[4].start()

        elif phase == 3:

            @pl.when(here.inner)
            def _():
                land(number, 2)
                copies[3].start()

        elif phase == 4:

            @pl.when(here.inner)
            def _():
                land(number, 3)
                copies[4].start()

        else:
            copies[4].wait_recv()
            spot = pl.ds(place_of(layer, array, start), length)
            total[layer, spot, :] = (keeps[4][...] + slots[4][...])[0]

    def step(entry, phase):
        for chunk in entry:
            run(chunk, phase)

    second = [entry for _, entry in pairs[: len(quad_pairs(shares))]]
    first = [entry for _, entry in pairs[len(quad_pairs(shares)) :]]
    tails = [chunk for entry in second for chunk in entry if chunk[5] is not None]
    second = [[chunk for chunk in entry if chunk[5] is None] for entry in second]
    first[0] = first[0] + tails
    step(first[0], 0)
    step(first[1], 0)
    for entry in second:
        step(entry, 2)
    step(first[0], 1)
    for section, source in ((0, dx_ref), (1, final_ref)):

        @pl.when(core == section)
        def _():
            pltpu.make_async_copy(source.at[z], slices.at[z], local.at[0]).start()
            for by in (1, 2, 3):
                remote(
                    source.at[(z + by) % 4],
                    slices.at[z],
                    (z_send, z_recv),
                    (by - 1, by - 1),
                    here.others[by - 1],
                ).start()

    for entry in second:
        step(entry, 3)
    step(first[2], 0)
    step(first[1], 1)
    for entry in second:
        step(entry, 4)
    step(first[0], 2)
    step(first[2], 1)
    for entry in second:
        step(entry, 5)
    step(first[0], 3)
    step(first[1], 2)
    step(first[0], 4)
    step(first[1], 3)
    step(first[2], 2)
    step(first[1], 4)
    step(first[2], 3)
    step(first[2], 4)
    for entry in first:
        step(entry, 5)

    for copies, _, _ in built:
        for index in (0, 1, 4):
            if copies[index] is not None:
                copies[index].wait_send()
    for section, index in ((here.outer, 2), (here.inner, 3)):

        @pl.when(section)
        def _():
            for copies, _, _ in built:
                copies[index].wait_send()

    swaps = (swap_send, swap_recv)
    across = remote(total.at[1 - core], halves.at[core], swaps, (0, 0), here.partner)
    across.start()
    own = pltpu.make_async_copy(total.at[core], halves.at[core], local.at[1])
    own.start()
    own.wait()
    across.wait_send()
    remote(total.at[1 - core], halves.at[1 - core], swaps, (0, 0), here.partner).wait_recv()
    pltpu.make_async_copy(dx_ref.at[z], slices.at[z], local.at[0]).wait()
    for by in (1, 2, 3):
        copy = remote(
            dx_ref.at[z],
            slices.at[(z + 4 - by) % 4],
            (z_send, z_recv),
            (by - 1, by - 1),
            here.others[by - 1],
        )
        copy.wait_send()
        copy.wait_recv()


def scatter(shares, arrays, vec_zero, quads, vec_one, grad, final):
    micro, tokens, width = grad.shape
    lengths = (shares.half, shares.depth // 2, TAIL)
    chunks = sum(len(pair) for pair in chunk_pairs(shares) + quad_pairs(shares))
    rows = sum(lengths)
    anywhere = pl.BlockSpec(memory_space=pl.ANY)
    work = [pltpu.VMEM((2, 2, 4, length, width), LOW) for length in lengths]
    quad = pltpu.VMEM((4, (lengths[0] + lengths[1]) // 2, width), LOW)
    return pl.pallas_call(
        partial(scatter_kernel, shares),
        in_specs=[anywhere] * 12,
        out_specs=[anywhere] * 2,
        out_shape=[
            jax.ShapeDtypeStruct((2, rows, width), LOW),
            jax.ShapeDtypeStruct((micro, tokens, width), LOW),
        ],
        scratch_shapes=work
        + [quad, quad, work[2]]
        + [quad] * 4
        + [
            pltpu.VMEM((chunks, 2, 4, PIECE, width), LOW),
            pltpu.VMEM((chunks, 4, PIECE, width), LOW),
            pltpu.VMEM((chunks, 2, PIECE, width), LOW),
            pltpu.VMEM((chunks, 2, PIECE, width), LOW),
            pltpu.VMEM((chunks, 1, PIECE, width), LOW),
            pltpu.VMEM((2, rows, width), LOW),
            pltpu.SemaphoreType.DMA((2, 7)),
            pltpu.SemaphoreType.DMA((2,)),
            pltpu.SemaphoreType.DMA((1,)),
            pltpu.SemaphoreType.DMA((1,)),
            pltpu.SemaphoreType.DMA((3,)),
            pltpu.SemaphoreType.DMA((3,)),
            pltpu.SemaphoreType.DMA((chunks, 5)),
            pltpu.SemaphoreType.DMA((chunks, 5)),
        ],
        compiler_params=pltpu.CompilerParams(
            collective_id=1, has_side_effects=True, vmem_limit_bytes=VMEM_BYTES
        ),
    )(*arrays, vec_zero, *quads, vec_one, grad, final)


def update_kernel(shares, halves_ref, slices_ref, *refs):
    old, new, result_ref, turned = refs[:9], refs[9:18], refs[18], refs[19]
    result_ref[...] = slices_ref[...].astype(jnp.float32)
    offset = lax.axis_index((DP, SEQ)) * shares.columns
    half, per, width, depth = shares.half, shares.per, shares.width, shares.depth // 2
    is_inner = (offset >= 3 * width) & (offset < 4 * width)
    is_hidden = offset >= 4 * width

    @pl.when(is_inner)
    def _():
        for side in range(2):
            piece = halves_ref[side, :half, :].astype(jnp.float32)
            wide = per * half
            back = jnp.transpose(jnp.concatenate([piece[:, :wide], piece[:, wide:]], axis=0))
            for j in range(per):
                turned[(2 * j + side) * half : (2 * j + side + 1) * half, :] = back[
                    j * half : (j + 1) * half
                ]

    @pl.when(jnp.logical_not(is_inner))
    def _():
        pair = [halves_ref[side, :half, :].astype(jnp.float32) for side in range(2)]
        plain = jnp.concatenate(pair, axis=0)
        hidden = jnp.concatenate(
            [pair[side][j * depth :][:depth] for j in range(shares.groups) for side in range(2)],
            axis=0,
        )
        turned[...] = jnp.transpose(jnp.where(is_hidden, hidden, plain))

    def store(first, gradient, rate, decay):
        results = adam_update(*[ref[...] for ref in old[first : first + 3]], gradient, rate, decay)
        for ref, result in zip(new[first : first + 3], results):
            ref[...] = result

    store(0, turned[...], rate_matrix, decay_matrix)
    down = [halves_ref[side, half : half + depth, :] for side in range(2)]
    store(3, jnp.concatenate(down, axis=0).astype(jnp.float32), rate_matrix, decay_matrix)
    tails = [halves_ref[side, half + depth :, :].astype(jnp.float32) for side in range(2)]
    store(6, (tails[0] + tails[1])[0:1, : shares.vector_len], rate_vector, 0.0)


def update(shares, halves, slices, old):
    return pl.pallas_call(
        partial(update_kernel, shares),
        out_shape=[jax.ShapeDtypeStruct(piece.shape, jnp.float32) for piece in (*old, slices)],
        scratch_shapes=[pltpu.VMEM((shares.width, shares.columns), jnp.float32)],
        compiler_params=pltpu.CompilerParams(vmem_limit_bytes=VMEM_BYTES),
    )(halves, slices, *old)


(GAIN_ONE, SHIFT_ONE, BIAS_OUT, GAIN_TWO, SHIFT_TWO, BIAS_DOWN, BIAS_PROJ, _, BIAS_UP, _) = [
    slice(row, row + 1) for row in range(10)
]
ROWS = 256
COLS = 384
WIDE = 512
STRIP = 32


def whole(shape):
    return pl.BlockSpec(shape, lambda i: (0,) * len(shape))


def row_block(width):
    return pl.BlockSpec((ROWS, width), lambda i: (i, 0))


def col_block(tokens):
    return pl.BlockSpec((tokens, COLS), lambda i: (0, i))


def at_block(shape, *index):
    return pl.BlockSpec(shape, lambda i: index)


def params_of(flops, moved, transcendentals=0):
    return {
        "compiler_params": pltpu.CompilerParams(vmem_limit_bytes=VMEM_BYTES),
        "cost_estimate": pl.CostEstimate(
            flops=flops, bytes_accessed=moved, transcendentals=transcendentals
        ),
    }


def strips(length=ROWS, strip=STRIP):
    return [slice(first, first + strip) for first in range(0, length, strip)]


def both(own_ref, recv_ref, rows):
    return own_ref[rows, :].astype(jnp.float32) + recv_ref[rows, :].astype(jnp.float32)


def bias_of(vec_ref, first, start, length):
    row, width = first.start, vec_ref.shape[1]
    pieces = []
    for place in range(2):
        low = max(start - place * width, 0)
        high = min(start + length - place * width, width)
        if low < high:
            pieces.append(vec_ref[row + place : row + place + 1, low:high])
    return pieces[0] if len(pieces) == 1 else jnp.concatenate(pieces, axis=1)


def eights(values):
    rows, width = values.shape
    return jnp.sum(values.reshape(rows // 8, 8, width), axis=0)


def features_kernel(shares, random_ref, segment_ref, global_ref, query_ref, key_ref, turned_ref):
    core = lax.axis_index(SECTION)
    place = lax.axis_index(SEQ)
    blocks = random_ref.shape[1]
    width = key_ref.shape[1]
    heads = query_ref.shape[0]
    per_half = heads // shares.per
    picks = random_ref.shape[2] // (2 * heads)
    tokens = key_ref.shape[0]
    lane = lax.broadcasted_iota(jnp.int32, (blocks, width), 1)
    row = lax.broadcasted_iota(jnp.int32, (blocks, width), 0)
    key = jnp.where(lane < blocks, lane, lane - blocks)
    chosen = random_ref[place]
    named = global_ref[place]
    always = (jnp.abs(row - key) <= 1).astype(jnp.int32)
    is_global = jnp.zeros((blocks, width), jnp.int32)
    for index in range(named.shape[1]):
        spot = named[:, index : index + 1]
        always = always + (key == spot).astype(jnp.int32)
        is_global = is_global + (row == spot).astype(jnp.int32)
    line = segment_ref[place].astype(jnp.float32)
    column = jnp.transpose(jnp.broadcast_to(line, (8, tokens)))[:, 0:1]
    token_lane = lax.broadcasted_iota(jnp.int32, (tokens, width), 1)
    same = column == (token_lane - 2 * blocks).astype(jnp.float32)
    in_segment = (token_lane >= 2 * blocks) & (token_lane < 2 * blocks + 3)
    segment_side = jnp.where(in_segment & same, 1.0, 0.0)
    for head in range(heads):
        count = always
        for pick in range(picks):
            at = [
                (2 * per_half * (head // per_half) + per_half * side + head % per_half) * picks
                + pick
                for side in range(2)
            ]
            spot = jnp.where(core == 0, chosen[:, at[0] : at[0] + 1], chosen[:, at[1] : at[1] + 1])
            count = count + (key == spot).astype(jnp.int32)
        count = jnp.where(is_global > 0, 1, count)
        high = jnp.where(count == 0, masked, 0.0)
        low = jnp.zeros_like(high)
        for times in (2, 3):
            high = jnp.where(count == times, LOG_HIGH[times - 1], high)
            low = jnp.where(count == times, LOG_LOW[times - 1], low)
        table = jnp.where(lane < blocks, high, jnp.where(lane < 2 * blocks, low, 0.0))
        for block in range(blocks):
            rows = slice(block * BLOCK, (block + 1) * BLOCK)
            query_ref[head, rows, :] = (table[block : block + 1] + segment_side[rows]).astype(LOW)
    token_block = lax.shift_right_logical(
        lax.broadcasted_iota(jnp.int32, (tokens, width), 0), BLOCK.bit_length() - 1
    )
    here = (token_block == token_lane) | (token_block == token_lane - blocks)
    side = jnp.where(here & (token_lane < 2 * blocks), 1.0, 0.0)
    side = jnp.where(in_segment & jnp.logical_not(same), masked, side)
    ones = (token_lane >= 2 * blocks + 3) & (token_lane < 2 * blocks + 6)
    side = jnp.where(ones, 1.0, side)
    key_ref[...] = side.astype(LOW)
    turned_ref[...] = jnp.transpose(side).astype(LOW)


def key_features(shares, random_ids, segment_ids, global_ids):
    micro, _, blocks, head_count, picks = random_ids.shape
    tokens = segment_ids.shape[2]
    width = -(-(2 * blocks + 6) // 128) * 128
    return pl.pallas_call(
        partial(features_kernel, shares),
        out_shape=[
            jax.ShapeDtypeStruct((head_count // 2, tokens, width), LOW),
            jax.ShapeDtypeStruct((tokens, width), LOW),
            jax.ShapeDtypeStruct((width, tokens), LOW),
        ],
        **params_of(0, head_count * tokens * width),
    )(random_ids.reshape(micro, blocks, head_count * picks), segment_ids, global_ids)


def project_kernel(joins, *refs):
    if joins:
        (middle_ref, part_ref, recv_ref, before_ref), refs = refs[:4], refs[4:]
    else:
        hidden_ref, refs = refs[0], refs[1:]
    (vec_ref, weight_ref), refs = refs[:2], refs[2:]
    if joins:
        hidden_ref, refs = refs[0], refs[1:]
    normed_ref, out_ref = refs
    for rows in strips():
        if joins:
            part = both(part_ref, recv_ref, rows)
            low = (middle_ref[rows, :] + part + before_ref[BIAS_DOWN]).astype(LOW)
            hidden_ref[rows, :] = low
        else:
            low = hidden_ref[rows, :]
        unit, _ = normalized(low.astype(jnp.float32))
        normed_ref[rows, :] = (unit * vec_ref[GAIN_ONE] + vec_ref[SHIFT_ONE]).astype(LOW)
    product = dot_rows(normed_ref[...], weight_ref[...])
    out_ref[...] = (product + bias_of(vec_ref, BIAS_PROJ, 0, out_ref.shape[1])).astype(LOW)


def project(before, vec, rows, out_width):
    joins = len(before) > 1
    tokens, width = before[0].shape
    ins = [row_block(width)] * 3 + [whole(vec.shape)] if joins else [row_block(width)]
    outs = [row_block(width)] * (2 if joins else 1)
    low = jax.ShapeDtypeStruct((tokens, width), LOW)
    return pl.pallas_call(
        partial(project_kernel, joins),
        grid=(tokens // ROWS,),
        in_specs=ins + [whole(vec.shape), whole((out_width, width))],
        out_specs=outs + [row_block(out_width)],
        out_shape=[low] * len(outs) + [jax.ShapeDtypeStruct((tokens, out_width), LOW)],
        **params_of(2 * tokens * width * out_width, tokens * width * 16),
    )(*before, vec, rows)


def out_halves(packed_ref, half):
    wide = packed_ref.shape[1] // 2
    return [
        jnp.concatenate([packed_ref[rows, :wide], packed_ref[rows, wide:]], axis=0)
        for rows in (slice(0, half), slice(half, 2 * half))
    ]


def branch_kernel(half, attended_ref, packed_ref, low_ref):
    wide = attended_ref.shape[1]
    for index, weights in enumerate(out_halves(packed_ref, half)):
        cols = slice(index * wide, (index + 1) * wide)
        low_ref[:, cols] = dot_rows(attended_ref[...], weights).astype(LOW)


def branch_out(shares, attended, rows):
    tokens, wide = attended.shape
    width = rows.shape[1]
    return pl.pallas_call(
        partial(branch_kernel, shares.half),
        grid=(tokens // ROWS,),
        in_specs=[row_block(wide), at_block((COLS, width), 3, 0)],
        out_specs=row_block(width),
        out_shape=jax.ShapeDtypeStruct((tokens, width), LOW),
        **params_of(2 * tokens * width * wide, tokens * width * 4),
    )(attended, rows)


def gelu_parts(value):
    below = 1.0 + (0.3275911 * 0.5**0.5) * jnp.abs(value)
    rough = pl.reciprocal(below, approx=True)
    t = rough * (2.0 - below * rough)
    bell = jnp.exp((-0.5 * value) * value)
    poly = 0.5 * 1.061405429
    for coefficient in (-1.453152027, 1.421413741, -0.284496736, 0.254829592):
        poly = poly * t + 0.5 * coefficient
    tail = poly * (t * bell)
    cdf = jnp.where(value > 0, 1.0 - tail, tail)
    return value * cdf, cdf + value * (bell * (0.5 / math.pi) ** 0.5)


def expand_kernel(
    hidden_ref,
    branch_ref,
    recv_ref,
    vec_ref,
    up_ref,
    down_ref,
    middle_ref,
    normed_ref,
    slope_ref,
    active_ref,
    low_ref,
    held,
):
    for rows in strips():
        branch = both(branch_ref, recv_ref, rows) + vec_ref[BIAS_OUT]
        middle = hidden_ref[rows, :].astype(jnp.float32) + branch
        middle_ref[rows, :] = middle
        unit, _ = normalized(middle)
        normed_ref[rows, :] = (unit * vec_ref[GAIN_TWO] + vec_ref[SHIFT_TWO]).astype(LOW)
    for index in range(up_ref.shape[0] // WIDE):
        cols = slice(index * WIDE, (index + 1) * WIDE)
        held[index] = dot_rows(normed_ref[...], up_ref[cols, :])
        bias = bias_of(vec_ref, BIAS_UP, index * WIDE, WIDE)
        for rows in strips():
            active, slope = gelu_parts(held[index, rows, :] + bias)
            active_ref[rows, cols] = active.astype(LOW)
            slope_ref[rows, cols] = slope.astype(LOW)
    low_ref[...] = dot_plain(active_ref[...], down_ref[...]).astype(LOW)


def expand(hidden, branch, recv, vec, rows, down):
    tokens, width = hidden.shape
    inner = down.shape[0]
    return pl.pallas_call(
        expand_kernel,
        grid=(tokens // ROWS,),
        in_specs=[row_block(width)] * 3
        + [whole(vec.shape), at_block((inner, width), 1, 0), whole((inner, width))],
        out_specs=[row_block(width), row_block(width), row_block(inner), row_block(inner)]
        + [row_block(width)],
        out_shape=[
            jax.ShapeDtypeStruct((tokens, width), jnp.float32),
            jax.ShapeDtypeStruct((tokens, width), LOW),
            jax.ShapeDtypeStruct((tokens, inner), LOW),
            jax.ShapeDtypeStruct((tokens, inner), LOW),
            jax.ShapeDtypeStruct((tokens, width), LOW),
        ],
        scratch_shapes=[pltpu.VMEM((inner // WIDE, ROWS, WIDE), jnp.float32)],
        **params_of(4 * tokens * width * inner, tokens * width * 32, tokens * inner),
    )(hidden, branch, recv, vec, rows, down)


def expand_back_kernel(
    grad_ref,
    slope_ref,
    up_ref,
    down_ref,
    low_ref,
    grad_up_ref,
    bias_up_ref,
    bias_down_ref,
    sums_up,
    sums_down,
):
    step = pl.program_id(0)

    @pl.when(step == 0)
    def _():
        sums_up[...] = jnp.zeros_like(sums_up)
        sums_down[...] = jnp.zeros_like(sums_down)

    for index in range(down_ref.shape[0] // WIDE):
        cols = slice(index * WIDE, (index + 1) * WIDE)
        grad_active = dot_rows(grad_ref[...], down_ref[cols, :])
        grad_up_ref[:, cols] = (grad_active * slope_ref[:, cols].astype(jnp.float32)).astype(LOW)
    low_ref[...] = dot_plain(grad_up_ref[...], up_ref[...]).astype(LOW)
    for rows in strips():
        sums_up[...] += eights(grad_up_ref[rows, :].astype(jnp.float32))
        sums_down[...] += eights(grad_ref[rows, :].astype(jnp.float32))

    @pl.when(step == pl.num_programs(0) - 1)
    def _():
        bias_up_ref[...] = jnp.sum(sums_up[...], axis=0, keepdims=True)
        bias_down_ref[...] = jnp.sum(sums_down[...], axis=0, keepdims=True)


def expand_back(grad, slope, rows, down):
    tokens, width = grad.shape
    inner = down.shape[0]
    return pl.pallas_call(
        expand_back_kernel,
        grid=(tokens // ROWS,),
        in_specs=[row_block(width), row_block(inner)]
        + [at_block((inner, width), 1, 0), whole((inner, width))],
        out_specs=[row_block(width), row_block(inner), whole((1, inner)), whole((1, width))],
        out_shape=[
            jax.ShapeDtypeStruct((tokens, width), LOW),
            jax.ShapeDtypeStruct((tokens, inner), LOW),
            jax.ShapeDtypeStruct((1, inner), jnp.float32),
            jax.ShapeDtypeStruct((1, width), jnp.float32),
        ],
        scratch_shapes=[pltpu.VMEM((8, inner), jnp.float32), pltpu.VMEM((8, width), jnp.float32)],
        **params_of(4 * tokens * width * inner, tokens * width * 24),
    )(grad, slope, rows, down)


def token_products_kernel(lefts, rights, outs):
    for left, right, out in zip(lefts, rights, outs):
        out[...] = dot_tokens(left[...], right[...]).astype(LOW)


def hidden_products(active, grad, grad_up, normed):
    tokens, inner = active.shape
    width = grad.shape[1]

    def kernel(a_ref, b_ref, c_ref, d_ref, down_ref, rows_ref):
        token_products_kernel((a_ref, b_ref), (c_ref, d_ref), (down_ref, rows_ref))

    return pl.pallas_call(
        kernel,
        grid=(inner // COLS,),
        in_specs=[col_block(tokens)] * 2 + [whole((tokens, width))] * 2,
        out_specs=[
            pl.BlockSpec((COLS, width), lambda i: (i, 0)),
            pl.BlockSpec((COLS, width), lambda i: (inner // COLS + i, 0)),
        ],
        out_shape=[
            jax.ShapeDtypeStruct((inner, width), LOW),
            jax.ShapeDtypeStruct((2 * inner, width), LOW),
        ],
        **params_of(4 * tokens * width * inner, tokens * width * 16),
    )(active, grad_up, grad, normed)


def project_products(grad_proj, normed, rows_grad):
    tokens, out_width = grad_proj.shape
    width = normed.shape[1]

    def kernel(a_ref, b_ref, _, rows_ref):
        token_products_kernel((a_ref,), (b_ref,), (rows_ref,))

    return pl.pallas_call(
        kernel,
        grid=(out_width // COLS,),
        in_specs=[col_block(tokens), whole((tokens, width)), pl.BlockSpec(memory_space=pl.ANY)],
        out_specs=pl.BlockSpec((COLS, width), lambda i: (i, 0)),
        out_shape=jax.ShapeDtypeStruct(rows_grad.shape, LOW),
        input_output_aliases={2: 0},
        **params_of(2 * tokens * width * out_width, tokens * width * 8),
    )(grad_proj, normed, rows_grad)


def norm_back_rows(values_in, incoming, gain_vec):
    unit, scale = normalized(values_in)
    p = incoming * gain_vec
    mean_p = jnp.mean(p, axis=-1, keepdims=True)
    mean_pn = jnp.mean(p * unit, axis=-1, keepdims=True)
    return scale * (p - mean_p - unit * mean_pn), eights(incoming * unit), eights(incoming)


def branch_back_kernel(
    half,
    middle_ref,
    part_ref,
    recv_ref,
    grad_ref,
    attended_ref,
    vec_ref,
    packed_ref,
    _,
    grad_middle_ref,
    grad_attended_ref,
    out_grad_ref,
    gain_grad_ref,
    shift_grad_ref,
    bias_grad_ref,
    total,
    low,
    sums,
):
    step = pl.program_id(0)

    @pl.when(step == 0)
    def _():
        total[...] = jnp.zeros_like(total)
        sums[...] = jnp.zeros_like(sums)

    for rows in strips():
        incoming = both(part_ref, recv_ref, rows)
        change, for_gain, for_shift = norm_back_rows(
            middle_ref[rows, :], incoming, vec_ref[GAIN_TWO]
        )
        grad_middle = grad_ref[rows, :].astype(jnp.float32) + change
        grad_middle_ref[rows, :] = grad_middle
        rounded = grad_middle.astype(LOW)
        low[rows, :] = rounded
        sums[0] += for_gain
        sums[1] += for_shift
        sums[2] += eights(rounded.astype(jnp.float32))
    weights = out_halves(packed_ref, half)
    wide = weights[0].shape[0]
    attended = attended_ref[...]
    pieces = [low[:, :wide], low[:, wide:]]
    grad_attended_ref[...] = (
        dot_plain(pieces[0], weights[0]) + dot_plain(pieces[1], weights[1])
    ).astype(LOW)
    for index in range(2):
        total[index] += dot_tokens(pieces[index], attended)

    @pl.when(step == pl.num_programs(0) - 1)
    def _():
        for index in range(2):
            joined = jnp.concatenate([total[index, :half, :], total[index, half:, :]], axis=1)
            out_grad_ref[index * half : (index + 1) * half, :] = joined.astype(LOW)
        for index, ref in enumerate((gain_grad_ref, shift_grad_ref, bias_grad_ref)):
            ref[...] = jnp.sum(sums[index], axis=0, keepdims=True)


def branch_back(shares, middle, part, recv, grad, attended, vec, rows, rows_grad):
    tokens, width = middle.shape
    wide = attended.shape[1]
    small = whole((1, width))
    one = jax.ShapeDtypeStruct((1, width), jnp.float32)
    return pl.pallas_call(
        partial(branch_back_kernel, shares.half),
        grid=(tokens // ROWS,),
        in_specs=[row_block(width)] * 4
        + [row_block(wide), whole(vec.shape), at_block((COLS, width), 3, 0)]
        + [pl.BlockSpec(memory_space=pl.ANY)],
        out_specs=[row_block(width), row_block(wide), at_block((COLS, width), 3, 0)]
        + [small, small, small],
        out_shape=[
            jax.ShapeDtypeStruct((tokens, width), jnp.float32),
            jax.ShapeDtypeStruct((tokens, wide), LOW),
            jax.ShapeDtypeStruct(rows_grad.shape, LOW),
            one,
            one,
            one,
        ],
        input_output_aliases={7: 2},
        scratch_shapes=[
            pltpu.VMEM((2, width // 2, wide), jnp.float32),
            pltpu.VMEM((ROWS, width), LOW),
            pltpu.VMEM((3, 8, width), jnp.float32),
        ],
        **params_of(4 * tokens * width * wide, tokens * width * 20),
    )(middle, part, recv, grad, attended, vec, rows, rows_grad)


def project_back_kernel(grad_ref, weight_ref, low_ref, bias_ref, sums):
    step = pl.program_id(0)

    @pl.when(step == 0)
    def _():
        sums[...] = jnp.zeros_like(sums)

    low_ref[...] = dot_plain(grad_ref[...], weight_ref[...]).astype(LOW)
    for rows in strips():
        sums[...] += eights(grad_ref[rows, :].astype(jnp.float32))

    @pl.when(step == pl.num_programs(0) - 1)
    def _():
        bias_ref[...] = jnp.sum(sums[...], axis=0, keepdims=True)


def project_back(grad_proj, rows):
    tokens, out_width = grad_proj.shape
    width = rows.shape[1]
    return pl.pallas_call(
        project_back_kernel,
        grid=(tokens // ROWS,),
        in_specs=[row_block(out_width), whole((out_width, width))],
        out_specs=[row_block(width), whole((1, out_width))],
        out_shape=[
            jax.ShapeDtypeStruct((tokens, width), LOW),
            jax.ShapeDtypeStruct((1, out_width), jnp.float32),
        ],
        scratch_shapes=[pltpu.VMEM((8, out_width), jnp.float32)],
        **params_of(2 * tokens * width * out_width, tokens * width * 12),
    )(grad_proj, rows)


def input_back_kernel(
    hidden_ref, part_ref, recv_ref, grad_ref, vec_ref, out_ref, gain_grad_ref, shift_grad_ref, sums
):
    step = pl.program_id(0)

    @pl.when(step == 0)
    def _():
        sums[...] = jnp.zeros_like(sums)

    for rows in strips():
        incoming = both(part_ref, recv_ref, rows)
        hidden = hidden_ref[rows, :].astype(jnp.float32)
        change, for_gain, for_shift = norm_back_rows(hidden, incoming, vec_ref[GAIN_ONE])
        out_ref[rows, :] = (grad_ref[rows, :] + change).astype(LOW)
        sums[0] += for_gain
        sums[1] += for_shift

    @pl.when(step == pl.num_programs(0) - 1)
    def _():
        gain_grad_ref[...] = jnp.sum(sums[0], axis=0, keepdims=True)
        shift_grad_ref[...] = jnp.sum(sums[1], axis=0, keepdims=True)


def input_back(hidden, part, recv, grad_middle, vec):
    tokens, width = hidden.shape
    small = whole((1, width))
    one = jax.ShapeDtypeStruct((1, width), jnp.float32)
    return pl.pallas_call(
        input_back_kernel,
        grid=(tokens // ROWS,),
        in_specs=[row_block(width)] * 4 + [whole(vec.shape)],
        out_specs=[row_block(width), small, small],
        out_shape=[jax.ShapeDtypeStruct((tokens, width), LOW), one, one],
        scratch_shapes=[pltpu.VMEM((2, 8, width), jnp.float32)],
        **params_of(0, tokens * width * 12),
    )(hidden, part, recv, grad_middle, vec)


def attend_kernel(q_ref, k_ref, v_ref, qa_ref, kt_ref, out_ref, lse_ref, keys, held, low):
    tokens, pair = q_ref.shape
    left = lax.broadcasted_iota(jnp.int32, (CHUNK, pair), 1) < pair // 2
    keys[:pair, :] = jnp.transpose(k_ref[...].astype(jnp.float32)).astype(LOW)
    keys[pair:, :] = kt_ref[...]
    for index in range(tokens // CHUNK):
        rows = slice(index * CHUNK, (index + 1) * CHUNK)
        queries = q_ref[rows, :] * 0.125
        outs, tops = [], []
        for head in range(2):
            slot = (2 * index + head) % held.shape[0]
            mine = left if head == 0 else jnp.logical_not(left)
            side = jnp.where(mine, queries, jnp.zeros_like(queries))
            lhs = jnp.concatenate([side, qa_ref[head, rows, :]], axis=1)
            held[slot] = dot_plain(lhs, keys[...])
            levels, shares = [], []
            for strip in strips(CHUNK):
                scores = held[slot, strip, :]
                top = jnp.max(scores, axis=1, keepdims=True)
                weight = jnp.exp(scores - top)
                total = jnp.sum(weight, axis=1, keepdims=True)
                low[slot, strip, :] = weight.astype(LOW)
                levels.append(top + jnp.log(total))
                shares.append(1.0 / total)
            product = dot_plain(low[slot], v_ref[...])
            outs.append(product * jnp.concatenate(shares, axis=0))
            tops.append(jnp.concatenate(levels, axis=0))
        out_ref[rows, :] = jnp.where(left, outs[0], outs[1]).astype(LOW)
        lse_ref[rows, :] = jnp.where(left, tops[0], tops[1])


def attend(projected, query_side, key_side, turned):
    tokens = projected.shape[0]
    width = projected.shape[1] // 3
    pairs = width // 128
    features = key_side.shape[1]
    return pl.pallas_call(
        attend_kernel,
        grid=(pairs,),
        in_specs=[
            pl.BlockSpec((tokens, 128), lambda p: (0, p)),
            pl.BlockSpec((tokens, 128), lambda p: (0, pairs + p)),
            pl.BlockSpec((tokens, 128), lambda p: (0, 2 * pairs + p)),
            pl.BlockSpec((2, tokens, features), lambda p: (p, 0, 0)),
            whole((features, tokens)),
        ],
        out_specs=[
            pl.BlockSpec((tokens, 128), lambda p: (0, p)),
            pl.BlockSpec((tokens, 128), lambda p: (0, p)),
        ],
        out_shape=[
            jax.ShapeDtypeStruct((tokens, width), LOW),
            jax.ShapeDtypeStruct((tokens, width), jnp.float32),
        ],
        scratch_shapes=[
            pltpu.VMEM((128 + features, tokens), LOW),
            pltpu.VMEM((4, CHUNK, tokens), jnp.float32),
            pltpu.VMEM((4, CHUNK, tokens), LOW),
        ],
        **params_of(
            16 * pairs * tokens * tokens * 128, tokens * width * 16, 2 * pairs * tokens * tokens
        ),
    )(projected, projected, projected, query_side, turned)


def three_terms(values):
    high = values.astype(LOW).astype(jnp.float32)
    rest = values - high
    middle = rest.astype(LOW).astype(jnp.float32)
    return high, middle, rest - middle


def attend_back_kernel(
    q_ref,
    k_ref,
    v_ref,
    do_ref,
    o_ref,
    lse_ref,
    qa_ref,
    ka_ref,
    grad_ref,
    held,
    probs,
    changes,
    query_sides,
    grad_sides,
):
    tokens, pair = q_ref.shape
    features = ka_ref.shape[1]
    pairs = pl.num_programs(0)
    place = pl.program_id(0)
    first = 2 * (tokens // BLOCK) + 3
    half = pair // 2
    left = lax.broadcasted_iota(jnp.int32, (CHUNK, pair), 1) < half
    lane = lax.broadcasted_iota(jnp.int32, (CHUNK, features), 1)
    lane_pair = lax.broadcasted_iota(jnp.int32, (CHUNK, pair), 1)
    keys = jnp.concatenate([k_ref[...], ka_ref[...]], axis=1)
    turned = jnp.transpose(k_ref[...].astype(jnp.float32)).astype(LOW)
    ones = (lax.broadcasted_iota(jnp.int32, (tokens, pair), 1) < 3).astype(jnp.float32).astype(LOW)
    values = jnp.concatenate([v_ref[...], ones], axis=1)
    parts, key_grads, value_grads = [], [], []
    for head in range(2):
        mine = left if head == 0 else jnp.logical_not(left)
        for index in range(tokens // CHUNK):
            rows = slice(index * CHUNK, (index + 1) * CHUNK)
            slot = index % 2
            queries = q_ref[rows, :] * 0.125
            grads = do_ref[rows, :]
            product = grads.astype(jnp.float32) * o_ref[rows, :].astype(jnp.float32)
            level = lse_ref[rows, head * half : head * half + 1]
            inner = jnp.sum(jnp.where(mine, product, 0.0), axis=1, keepdims=True)
            side = qa_ref[head, rows, :].astype(jnp.float32)
            for spot, term in enumerate(three_terms(level)):
                side = jnp.where(lane == first + spot, -term, side)
            query_side = jnp.where(mine, queries, jnp.zeros_like(queries))
            grad_side = jnp.where(mine, grads, jnp.zeros_like(grads))
            query_sides[head, rows, :] = query_side
            grad_sides[head, rows, :] = grad_side
            tail = jnp.zeros((CHUNK, pair), jnp.float32)
            for spot, term in enumerate(three_terms(inner)):
                tail = jnp.where(lane_pair == spot, -term, tail)
            held[slot, 0] = dot_rows(
                keys, jnp.concatenate([query_side, side.astype(LOW)], axis=1)
            )
            held[slot, 1] = dot_rows(
                values, jnp.concatenate([grad_side, tail.astype(LOW)], axis=1)
            )
            for strip in strips(tokens, 128):
                prob = jnp.exp(held[slot, 0, strip, :])
                probs[head, strip, rows] = prob.astype(LOW)
                changes[head, strip, rows] = (prob * held[slot, 1, strip, :]).astype(LOW)
        value_grads.append(dot_plain(probs[head], grad_sides[head]))
        key_grads.append(dot_plain(changes[head], query_sides[head]))
        parts.append(dot_plain(turned, changes[head]))
    joined = jnp.concatenate([parts[0][:half], parts[1][half:]], axis=0)
    column = [pl.ds(pl.multiple_of((by * pairs + place) * 128, 128), 128) for by in range(3)]
    grad_ref[:, column[0]] = (jnp.transpose(joined) * 0.125).astype(LOW)
    grad_ref[:, column[1]] = (key_grads[0] + key_grads[1]).astype(LOW)
    grad_ref[:, column[2]] = (value_grads[0] + value_grads[1]).astype(LOW)


def attend_back(projected, grad_attended, attended, levels, query_side, key_side):
    tokens, width = attended.shape
    pairs = width // 128
    features = key_side.shape[1]
    by_pair = pl.BlockSpec((tokens, 128), lambda p: (0, p))
    return pl.pallas_call(
        attend_back_kernel,
        grid=(pairs,),
        in_specs=[
            by_pair,
            pl.BlockSpec((tokens, 128), lambda p: (0, pairs + p)),
            pl.BlockSpec((tokens, 128), lambda p: (0, 2 * pairs + p)),
            by_pair,
            by_pair,
            by_pair,
            pl.BlockSpec((2, tokens, features), lambda p: (p, 0, 0)),
            whole((tokens, features)),
        ],
        out_specs=whole((tokens, 3 * width)),
        out_shape=jax.ShapeDtypeStruct((tokens, 3 * width), LOW),
        scratch_shapes=[
            pltpu.VMEM((2, 2, tokens, CHUNK), jnp.float32),
            pltpu.VMEM((2, tokens, tokens), LOW),
            pltpu.VMEM((2, tokens, tokens), LOW),
            pltpu.VMEM((2, tokens, 128), LOW),
            pltpu.VMEM((2, tokens, 128), LOW),
        ],
        **params_of(
            40 * pairs * tokens * tokens * 128, tokens * width * 24, 2 * pairs * tokens * tokens
        ),
    )(projected, projected, projected, grad_attended, attended, levels, query_side, key_side)


def window_forward(shares, before, weights, vec, features, beside):
    rows, down = weights
    results = project(before, vec, rows, 6 * shares.half)
    hidden = before[0] if len(before) == 1 else results[0]
    normed, projected = results[-2:]
    attended, levels = beside.tie(tuple(attend(projected, *features)))
    low = branch_out(shares, attended, rows)
    expanded = expand(hidden, low, swap(low), vec, rows, down)
    middle, normed_two, slope, active, low = beside.tie(tuple(expanded))
    stored = (hidden, normed, projected, attended, levels, middle, normed_two, slope, active)
    return (middle, low, swap(low), vec), stored


def window_backward(shares, stored, grad, weights, vec, features, beside):
    hidden, normed, projected, attended, levels, middle, normed_two, slope, active = stored
    rows, down = weights
    low, grad_up, bias_up, bias_down = beside.tie(tuple(expand_back(grad, slope, rows, down)))
    arrived = swap(low)
    down_grad, rows_grad = hidden_products(active, grad, grad_up, normed_two)
    grad_middle, grad_attended, rows_grad, gain_two, shift_two, bias_out = branch_back(
        shares, middle, low, arrived, grad, attended, vec, rows, rows_grad
    )
    grad_attended = beside.tie(grad_attended)
    grad_proj = attend_back(projected, grad_attended, attended, levels, *features[:2])
    grad_proj = beside.tie(grad_proj)
    low, summed = project_back(grad_proj, rows)
    arrived = swap(low)
    rows_grad = project_products(grad_proj, normed, rows_grad)
    grad, gain_one, shift_one = input_back(hidden, low, arrived, grad_middle, vec)
    width = attended.shape[1]
    vector_grads = (gain_one, shift_one, summed[:, :width], summed[:, 2 * width :], bias_out)
    vector_grads += (gain_two, shift_two, bias_down, bias_up)
    vector_grads = [piece[0] for piece in vector_grads]
    return grad, (rows_grad, down_grad), vector_grads


def window_shards(
    block_input,
    cotangent,
    random_ids,
    segment_ids,
    global_ids,
    w_rows,
    w_rows_first,
    w_rows_second,
    w_down,
    w_down_first,
    w_down_second,
    vectors,
    vectors_first,
    vectors_second,
):
    core = lax.axis_index(SECTION)
    micro, _, tokens, width = block_input.shape
    _, _, columns = w_rows.shape
    shares = Shares(width, columns, w_down.shape[1], vectors.shape[1])
    prepared = prepare(shares, w_rows[0], w_down[0], vectors)
    features = key_features(shares, random_ids, segment_ids, global_ids)
    gathered_zero, quads, vec_low, hidden, grad = gather(shares, prepared, block_input, cotangent)

    beside = Beside(spread_quads(shares, quads))
    params = [shares.unpack(gathered_zero, core)]
    before = (hidden.reshape(-1, width),)
    before, stored_zero = window_forward(shares, before, *params[0], features, beside)
    params.append(shares.unpack((*beside.flying, vec_low), core))
    after, stored_one = window_forward(shares, before, *params[1], features, Beside())
    final = after[1].astype(jnp.float32) + after[2].astype(jnp.float32)
    final = (after[0] + final + after[3][BIAS_DOWN]).astype(LOW)

    grad = grad.reshape(-1, width)
    grad, *grads_one = window_backward(shares, stored_one, grad, *params[1], features, Beside())
    *arrays_one, vec_one = shares.by_shard(*grads_one, core)
    beside = Beside(sum_quads(shares, arrays_one))
    grad, *grads_zero = window_backward(shares, stored_zero, grad, *params[0], features, beside)
    *arrays_zero, vec_zero = shares.by_shard(*grads_zero, core)
    grad, final = [piece.reshape(micro, tokens, width) for piece in (grad, final)]
    halves, slices = scatter(shares, arrays_zero, vec_zero, beside.flying, vec_one, grad, final)
    old = [
        w_rows[0],
        w_rows_first[0],
        w_rows_second[0],
        w_down[0],
        w_down_first[0],
        w_down_second[0],
        vectors,
        vectors_first,
        vectors_second,
    ]
    *new, result = update(shares, halves, slices, old)
    return (result[None, :, None], *[piece[None] for piece in new[:6]], *new[6:])


def one_window_each(mesh, block_input, w_rows, w_down, vectors):
    micro, windows, length, width = block_input.shape
    shards = mesh.shape[DP] * mesh.shape[SEQ]
    columns, depth = w_rows.shape[2] // shards, w_down.shape[1] // shards
    head_dim = width // HEADS
    tokens = length // mesh.shape[SEQ]
    return (
        mesh.shape[SECTION] == 2
        and mesh.shape[SEQ] == micro
        and mesh.shape[DP] == windows
        and tokens % (2 * BLOCK) == 0
        and length % CHUNK == 0
        and head_dim == 64
        and width % columns == 0
        and columns % (2 * head_dim) == 0
        and columns % depth == 0
        and width // columns * (columns // 2) % 128 == 0
        and depth % 32 == 0
        and vectors.shape[1] // shards <= width
        and mesh.shape[DP] == 4
        and micro == 4
        and width == 2 * columns == 2 * COLS
        and w_down.shape[1] == 4 * width
        and (columns // 2) % (2 * PIECE) == 0
        and (depth // 2) % (2 * PIECE) == 0
        and length % (4 * ROWS) == 0
    )


def solution(mesh):
    in_specs = (
        P(None, DP, SEQ, None),
        P(None, DP, SEQ, None),
        P(None, DP, None, None, None),
        P(None, DP, None),
        P(None, DP, None),
        P(SECTION, None, (DP, SEQ)),
        P(SECTION, None, (DP, SEQ)),
        P(SECTION, None, (DP, SEQ)),
        P(SECTION, (DP, SEQ), None),
        P(SECTION, (DP, SEQ), None),
        P(SECTION, (DP, SEQ), None),
        P(SECTION, (DP, SEQ)),
        P(SECTION, (DP, SEQ)),
        P(SECTION, (DP, SEQ)),
    )
    out_specs = (
        P(SECTION, None, DP, SEQ, None),
        P(SECTION, None, (DP, SEQ)),
        P(SECTION, None, (DP, SEQ)),
        P(SECTION, None, (DP, SEQ)),
        P(SECTION, (DP, SEQ), None),
        P(SECTION, (DP, SEQ), None),
        P(SECTION, (DP, SEQ), None),
        P(SECTION, (DP, SEQ)),
        P(SECTION, (DP, SEQ)),
        P(SECTION, (DP, SEQ)),
    )

    def step(*arrays):
        chosen = general_shards
        if one_window_each(mesh, arrays[0], arrays[5], arrays[8], arrays[11]):
            chosen = window_shards
        return jax.shard_map(
            chosen, mesh=mesh, in_specs=in_specs, out_specs=out_specs, check_vma=False
        )(*arrays)

    return step
```

```python
import math
from functools import partial

import jax
import jax.numpy as jnp
import ml_dtypes
import numpy as np
from jax import lax
from jax.experimental import pallas as pl
from jax.experimental.pallas import tpu as pltpu
from jax.sharding import PartitionSpec as P

SECTION, DP, SEQ = "section", "dp", "seq"
HEADS = 12
BLOCK = 64
STEP = 5


epsilon = 1e-05
masked = -1e30
rate_matrix = 0.02
rate_vector = 0.2
decay_matrix = 0.01


def with_halo(x, sides, width):
    for axis, dim in sides:
        devices, length = (lax.axis_size(axis), x.shape[dim])
        up = [(i, (i + 1) % devices) for i in range(devices - 1)]
        down = [(j, i) for i, j in up]
        last = lax.slice_in_dim(x, length - width, length, axis=dim)
        initial = lax.slice_in_dim(x, 0, width, axis=dim)
        before = lax.ppermute(last, axis, up)
        after = lax.ppermute(initial, axis, down)
        x = jnp.concatenate([before, x, after], axis=dim)
    return x


def merged(value, axis, join):
    pieces = jax.tree.map(lambda part: lax.all_gather(part, axis), value)
    head = jax.tree.map(lambda part: part[0], pieces)
    tail = jax.tree.map(lambda part: part[1:], pieces)
    subtotal, _ = lax.scan(lambda subtotal, share: (join(subtotal, share), None), head, tail)
    return subtotal


def from_behind(x, axis, by):
    devices = lax.axis_size(axis)
    pairs = [(i, i + by) for i in range(devices) if 0 <= i + by < devices]
    return lax.ppermute(x, axis, pairs)


def partner(value, axis, bit):
    mask = 2**bit
    pairs = [(source, source ^ mask) for source in range(lax.axis_size(axis))]
    return lax.ppermute(value, axis, pairs)


def mixed_sum(form, left, right):
    return jnp.einsum(form, left, right, preferred_element_type=jnp.float32)


def exact_two(form, left, right):
    return jnp.einsum(
        form, left, right, precision=lax.Precision.HIGHEST, preferred_element_type=jnp.float32
    )


def norm_rows(values_in, gain_vec, shift_vec):
    row_mean = jnp.mean(values_in, axis=-1, keepdims=True)
    centred = values_in - row_mean
    spread = jnp.mean(centred * centred, axis=-1, keepdims=True)
    return centred * lax.rsqrt(spread + epsilon) * gain_vec + shift_vec


def split_vectors(vector_weights, model_width):
    pieces = [
        vector_weights[piece_index * model_width : (piece_index + 1) * model_width]
        for piece_index in range(8)
    ]
    return pieces + [vector_weights[8 * model_width :]]


def route_tables(random_rows, segments, global_rows, seq_place, groups):
    windows, blocks, head_count, pick_count = random_rows.shape
    blocks_dev = blocks // groups
    request_count = blocks_dev * head_count * pick_count
    capacity = -(-request_count // groups)
    requests = random_rows.reshape(windows, groups, request_count)
    owners = requests // blocks_dev
    inside = requests % blocks_dev
    head_of = jnp.arange(request_count) // pick_count % head_count
    is_mine = owners == seq_place
    slot_index = jnp.cumsum(is_mine.astype(jnp.int32), axis=2) - 1
    slot_hot = ((slot_index[..., None] == jnp.arange(capacity)) & is_mine[..., None]).astype(
        jnp.float32
    )
    inside_hot = (inside[..., None] == jnp.arange(blocks_dev)).astype(jnp.float32)
    head_hot = (head_of[:, None] == jnp.arange(head_count)).astype(jnp.float32)
    sender = jnp.einsum(
        "wqsc,wqsb,sh->wqcbh", slot_hot, inside_hot, head_hot, precision=lax.Precision.HIGHEST
    )
    my_owners = lax.dynamic_index_in_dim(owners, seq_place, axis=1, keepdims=False)
    earlier = jnp.arange(request_count)[None, :] < jnp.arange(request_count)[:, None]
    same_owner = my_owners[:, :, None] == my_owners[:, None, :]
    rank_index = jnp.sum((same_owner & earlier[None]).astype(jnp.int32), axis=2)
    picker = (
        (my_owners[..., None, None] == jnp.arange(groups)[:, None])
        & (rank_index[..., None, None] == jnp.arange(capacity)[None, :])
    ).astype(jnp.float32)
    first_block = seq_place * blocks_dev
    owned_hot = (global_rows[:, :, None] == first_block + jnp.arange(blocks_dev)).astype(
        jnp.float32
    )
    length = segments.shape[1]
    block_len = length // blocks
    seg_blocks = segments.reshape(windows, blocks, block_len)
    seg_pad = jnp.pad(seg_blocks, ((0, 0), (1, 1), (0, 0)), constant_values=-1)
    near_segs = lax.dynamic_slice_in_dim(seg_pad, first_block, blocks_dev + 2, axis=1)
    slide_seg = jnp.concatenate([near_segs[:, :-2], near_segs[:, 1:-1], near_segs[:, 2:]], axis=2)
    query_seg = near_segs[:, 1:-1]
    rows_index = jnp.arange(windows)
    global_seg = seg_blocks[rows_index[:, None], global_rows].reshape(windows, -1)
    chosen = lax.dynamic_slice_in_dim(random_rows, first_block, blocks_dev, axis=1)
    far_seg = seg_blocks[rows_index[:, None, None, None], chosen].reshape(
        windows, blocks_dev, head_count, -1
    )
    key_seg = jnp.concatenate(
        [
            jnp.broadcast_to(
                slide_seg[:, :, None, :], (windows, blocks_dev, head_count, slide_seg.shape[2])
            ),
            jnp.broadcast_to(
                global_seg[:, None, None, :], (windows, blocks_dev, head_count, global_seg.shape[1])
            ),
            far_seg,
        ],
        axis=3,
    )
    key_mask = query_seg[:, :, None, :, None] == key_seg[:, :, :, None, :]
    local_seg = query_seg.reshape(windows, -1)
    full_mask = global_seg[:, None, :, None] == local_seg[:, None, None, :]
    return (sender, picker, owned_hot, key_mask, full_mask)


def fetch_blocks(paired, queries, sender, picker, owned_hot):
    windows, tokens, head_count, doubled = paired.shape
    head_dim = queries.shape[-1]
    blocks_dev = tokens // BLOCK
    flattened = paired.reshape(windows, tokens, head_count * doubled)
    padded = with_halo(flattened, ((SEQ, 1),), BLOCK)
    framed = padded.reshape(windows, blocks_dev + 2, BLOCK, head_count, doubled)
    sliding = jnp.concatenate([framed[:, :-2], framed[:, 1:-1], framed[:, 2:]], axis=2)
    local_blocks = paired.reshape(windows, blocks_dev, BLOCK, head_count, doubled)
    owned_low = owned_hot.astype(jnp.bfloat16)
    offered = mixed_sum("wgb,wbthe->wgthe", owned_low, local_blocks)
    offered_queries = mixed_sum("wgb,wbqhd->wgqhd", owned_low, queries)
    global_kv, global_queries = (
        lax.psum(offered.astype(jnp.bfloat16), SEQ).astype(jnp.float32),
        lax.psum(offered_queries.astype(jnp.bfloat16), SEQ).astype(jnp.float32),
    )
    global_kv = global_kv.astype(jnp.bfloat16).reshape(windows, -1, head_count, doubled)
    global_queries = global_queries.astype(jnp.bfloat16).reshape(windows, -1, head_count, head_dim)
    outgoing = mixed_sum("wqcbh,wbthe->qwcte", sender.astype(jnp.bfloat16), local_blocks).astype(
        jnp.bfloat16
    )
    incoming = lax.all_to_all(outgoing, SEQ, split_axis=0, concat_axis=0, tiled=True)
    distant = mixed_sum("wspc,pwcte->wste", picker.astype(jnp.bfloat16), incoming).astype(
        jnp.bfloat16
    )
    pick_count = picker.shape[1] // (blocks_dev * head_count)
    distant = distant.reshape(windows, blocks_dev, head_count, pick_count, BLOCK, doubled)
    return (sliding, global_kv, distant, global_queries)


def combine_stats(earlier, later):
    top = jnp.maximum(earlier[0], later[0])
    return (top, earlier[1] * jnp.exp(earlier[0] - top) + later[1] * jnp.exp(later[0] - top))


def full_forward(global_queries, key_part, value_part, full_mask, head_dim):
    scores = mixed_sum("wqhd,wkhd->whqk", global_queries, key_part) * head_dim ** (-0.5)
    scores = jnp.where(full_mask, scores, masked)
    local_top = jnp.max(scores, axis=3, keepdims=True)
    local_sum = jnp.sum(
        jnp.where(full_mask, jnp.exp(scores - local_top), 0.0), axis=3, keepdims=True
    )
    row_top, row_sum = merged((local_top, local_sum), SEQ, combine_stats)
    full_probs = jnp.where(full_mask, jnp.exp(scores - row_top), 0.0) / row_sum
    partial_out = mixed_sum("whqk,wkhd->wqhd", full_probs.astype(jnp.bfloat16), value_part)
    full_out = lax.psum(partial_out.astype(jnp.bfloat16), SEQ).astype(jnp.float32)
    return (full_out, full_probs)


def attention_weights(queries, sliding, global_kv, distant, key_mask):
    head_dim = queries.shape[-1]
    windows, blocks_dev, _, head_count, _ = queries.shape
    near_scores = mixed_sum("wbqhd,wbkhd->wbhqk", queries, sliding[..., :head_dim])
    global_scores = mixed_sum("wbqhd,wkhd->wbhqk", queries, global_kv[..., :head_dim])
    far_scores = mixed_sum("wbqhd,wbhrkd->wbhqrk", queries, distant[..., :head_dim])
    far_scores = far_scores.reshape(windows, blocks_dev, head_count, BLOCK, -1)
    scores = jnp.concatenate([near_scores, global_scores, far_scores], axis=4) * head_dim ** (-0.5)
    scores = jnp.where(key_mask, scores, masked)
    row_top = jnp.max(scores, axis=4, keepdims=True)
    weight = jnp.exp(scores - row_top)
    return weight / jnp.sum(weight, axis=4, keepdims=True)


def split_keys(scores_like, sliding, global_kv, distant):
    near_keys = sliding.shape[2]
    global_keys = global_kv.shape[1]
    windows, blocks_dev, head_count, pick_count, _, _ = distant.shape
    near_part = scores_like[..., :near_keys]
    global_part = scores_like[..., near_keys : near_keys + global_keys]
    far_part = scores_like[..., near_keys + global_keys :].reshape(
        windows, blocks_dev, head_count, BLOCK, pick_count, BLOCK
    )
    return (near_part, global_part, far_part)


def attention_values(low_probs, sliding, global_kv, distant, head_dim):
    near_part, global_part, far_part = split_keys(low_probs, sliding, global_kv, distant)
    attended = mixed_sum("wbhqk,wbkhd->wbqhd", near_part, sliding[..., head_dim:])
    attended = attended + mixed_sum("wbhqk,wkhd->wbqhd", global_part, global_kv[..., head_dim:])
    return attended + mixed_sum("wbhqrk,wbhrkd->wbqhd", far_part, distant[..., head_dim:])


def layer_forward(hidden, weights, tables):
    row_weights, down_weights, vector_weights = weights
    sender, picker, owned_hot, key_mask, full_mask = tables
    model_width = row_weights.shape[0]
    windows, tokens, _ = hidden.shape
    blocks_dev = tokens // BLOCK
    head_dim = model_width // HEADS
    (
        gain_one,
        shift_one,
        bias_query,
        bias_value,
        bias_out,
        gain_two,
        shift_two,
        bias_down,
        bias_up,
    ) = split_vectors(vector_weights, model_width)
    normed = norm_rows(hidden, gain_one, shift_one).astype(jnp.bfloat16)
    projected = mixed_sum("wtd,de->wte", normed, row_weights[:, : 3 * model_width])
    projected = (
        projected + jnp.concatenate([bias_query, jnp.zeros_like(bias_query), bias_value])
    ).astype(jnp.bfloat16)
    queries = projected[..., :model_width].reshape(windows, blocks_dev, BLOCK, HEADS, head_dim)
    key_part = projected[..., model_width : 2 * model_width].reshape(
        windows, tokens, HEADS, head_dim
    )
    value_part = projected[..., 2 * model_width :].reshape(windows, tokens, HEADS, head_dim)
    paired = jnp.concatenate([key_part, value_part], axis=3)
    sliding, global_kv, distant, global_queries = fetch_blocks(
        paired, queries, sender, picker, owned_hot
    )
    probabilities = attention_weights(queries, sliding, global_kv, distant, key_mask)
    attended = attention_values(
        probabilities.astype(jnp.bfloat16), sliding, global_kv, distant, head_dim
    )
    full_out, full_probs = full_forward(global_queries, key_part, value_part, full_mask, head_dim)
    placed = exact_two(
        "wgb,wgqhd->wbqhd", owned_hot, full_out.reshape(windows, -1, BLOCK, HEADS, head_dim)
    )
    on_global = jnp.sum(owned_hot, axis=1)[:, :, None, None, None] > 0
    attended = jnp.where(on_global, placed, attended)
    mixed_low = attended.reshape(windows, tokens, model_width).astype(jnp.bfloat16)
    middle = (
        hidden
        + mixed_sum("wtd,de->wte", mixed_low, row_weights[:, 3 * model_width : 4 * model_width])
        + bias_out
    )
    normed_two = norm_rows(middle, gain_two, shift_two).astype(jnp.bfloat16)
    up_value = mixed_sum("wtd,df->wtf", normed_two, row_weights[:, 4 * model_width :]) + bias_up
    active = jax.nn.gelu(up_value, approximate=False).astype(jnp.bfloat16)
    output = middle + mixed_sum("wtf,fd->wtd", active, down_weights) + bias_down
    stored = (
        hidden,
        normed,
        queries,
        sliding,
        global_kv,
        distant,
        probabilities,
        mixed_low,
        middle,
        normed_two,
        up_value,
        active,
        key_part,
        value_part,
        global_queries,
        full_probs,
    )
    return (output, stored)


def return_blocks(near_back, global_back, far_back, query_part, sender, picker, owned_hot):
    windows, blocks_dev, _, head_count, doubled = near_back.shape
    first_third = near_back[:, :, :BLOCK]
    centre_third = near_back[:, :, BLOCK : 2 * BLOCK]
    last_third = near_back[:, :, 2 * BLOCK :]
    framed = jnp.pad(first_third, ((0, 0), (0, 2), (0, 0), (0, 0), (0, 0)))
    framed = framed + jnp.pad(centre_third, ((0, 0), (1, 1), (0, 0), (0, 0), (0, 0)))
    framed = framed + jnp.pad(last_third, ((0, 0), (2, 0), (0, 0), (0, 0), (0, 0)))
    own_grad = framed[:, 1:-1]
    for direction in (1, -1):
        rim_grad = framed[:, -1] if direction == 1 else framed[:, 0]
        arrived = from_behind(rim_grad.astype(jnp.bfloat16), SEQ, direction).astype(
            rim_grad.dtype
        )
        if direction == 1:
            own_grad = jnp.concatenate(
                [own_grad[:, :1] + arrived[:, None], own_grad[:, 1:]], axis=1
            )
        else:
            own_grad = jnp.concatenate(
                [own_grad[:, :-1], own_grad[:, -1:] + arrived[:, None]], axis=1
            )
    global_total, query_total = (
        lax.psum(
            global_back.reshape(windows, -1, BLOCK, head_count, doubled).astype(jnp.bfloat16), SEQ
        ).astype(jnp.float32),
        lax.psum(query_part.astype(jnp.bfloat16), SEQ).astype(jnp.float32),
    )
    own_grad = own_grad + exact_two("wgb,wgthe->wbthe", owned_hot, global_total)
    far_flat = far_back.reshape(windows, -1, BLOCK, doubled)
    returning = exact_two("wspc,wste->pwcte", picker, far_flat)
    arrived_far = lax.all_to_all(
        returning.astype(jnp.bfloat16), SEQ, split_axis=0, concat_axis=0, tiled=True
    ).astype(returning.dtype)
    own_grad = own_grad + exact_two("wqcbh,qwcte->wbthe", sender, arrived_far)
    return (own_grad.reshape(windows, blocks_dev * BLOCK, head_count, doubled), query_total)


def attention_back(
    grad_attended,
    queries,
    sliding,
    global_kv,
    distant,
    probabilities,
    key_part,
    value_part,
    global_queries,
    full_probs,
    sender,
    picker,
    owned_hot,
):
    head_dim = queries.shape[-1]
    score_scale = head_dim ** (-0.5)
    windows, blocks_dev, _, head_count, _ = queries.shape
    on_global = jnp.sum(owned_hot, axis=1)[:, :, None, None, None] > 0
    selected = mixed_sum("wgb,wbqhd->wgqhd", owned_hot.astype(jnp.bfloat16), grad_attended)
    rows_grad = lax.psum(selected.astype(jnp.bfloat16), SEQ).reshape(
        windows, -1, head_count, head_dim
    )
    grad_attended = jnp.where(on_global, jnp.zeros_like(grad_attended), grad_attended)
    low_probs = probabilities.astype(jnp.bfloat16)
    near_grad = mixed_sum("wbqhd,wbkhd->wbhqk", grad_attended, sliding[..., head_dim:])
    global_grad = mixed_sum("wbqhd,wkhd->wbhqk", grad_attended, global_kv[..., head_dim:])
    far_grad = mixed_sum("wbqhd,wbhrkd->wbhqrk", grad_attended, distant[..., head_dim:])
    far_grad = far_grad.reshape(windows, blocks_dev, head_count, BLOCK, -1)
    grad_probs = jnp.concatenate([near_grad, global_grad, far_grad], axis=4)
    grad_scores = probabilities * (
        grad_probs - jnp.sum(probabilities * grad_probs, axis=4, keepdims=True)
    )
    grad_scores = grad_scores.astype(jnp.bfloat16)
    near_split, global_split, far_split = split_keys(grad_scores, sliding, global_kv, distant)
    near_probs, global_probs, far_probs = split_keys(low_probs, sliding, global_kv, distant)
    grad_query = mixed_sum("wbhqk,wbkhd->wbqhd", near_split, sliding[..., :head_dim])
    grad_query = grad_query + mixed_sum(
        "wbhqk,wkhd->wbqhd", global_split, global_kv[..., :head_dim]
    )
    grad_query = (
        grad_query + mixed_sum("wbhqrk,wbhrkd->wbqhd", far_split, distant[..., :head_dim])
    ) * score_scale
    near_back = jnp.concatenate(
        [
            mixed_sum("wbhqk,wbqhd->wbkhd", near_split, queries) * score_scale,
            mixed_sum("wbhqk,wbqhd->wbkhd", near_probs, grad_attended),
        ],
        axis=4,
    )
    global_back = jnp.concatenate(
        [
            mixed_sum("wbhqk,wbqhd->wkhd", global_split, queries) * score_scale,
            mixed_sum("wbhqk,wbqhd->wkhd", global_probs, grad_attended),
        ],
        axis=3,
    )
    far_back = jnp.concatenate(
        [
            mixed_sum("wbhqrk,wbqhd->wbhrkd", far_split, queries) * score_scale,
            mixed_sum("wbhqrk,wbqhd->wbhrkd", far_probs, grad_attended),
        ],
        axis=5,
    )
    full_grad_probs = mixed_sum("wqhd,wkhd->whqk", rows_grad, value_part)
    partial_dot = jnp.sum(full_probs * full_grad_probs, axis=3, keepdims=True)
    row_dot = lax.psum(partial_dot, SEQ)
    full_grad_scores = (full_probs * (full_grad_probs - row_dot)).astype(jnp.bfloat16)
    query_part = mixed_sum("whqk,wkhd->wqhd", full_grad_scores, key_part) * score_scale
    full_key_grad = mixed_sum("whqk,wqhd->wkhd", full_grad_scores, global_queries) * score_scale
    full_value_grad = mixed_sum("whqk,wqhd->wkhd", full_probs.astype(jnp.bfloat16), rows_grad)
    grad_paired, query_total = return_blocks(
        near_back, global_back, far_back, query_part, sender, picker, owned_hot
    )
    grad_query = grad_query + exact_two(
        "wgb,wgqhd->wbqhd", owned_hot, query_total.reshape(windows, -1, BLOCK, head_count, head_dim)
    )
    grad_paired = grad_paired + jnp.concatenate([full_key_grad, full_value_grad], axis=3)
    return (grad_query, grad_paired)


def layer_backward(stored, grad_output, weights, tables):
    row_weights, down_weights, vector_weights = weights
    sender, picker, owned_hot, key_mask, full_mask = tables
    (
        hidden,
        normed,
        queries,
        sliding,
        global_kv,
        distant,
        probabilities,
        mixed_low,
        middle,
        normed_two,
        up_value,
        active,
        key_part,
        value_part,
        global_queries,
        full_probs,
    ) = stored
    model_width = row_weights.shape[0]
    windows, tokens, _ = hidden.shape
    blocks_dev = tokens // BLOCK
    head_dim = model_width // HEADS
    (
        gain_one,
        shift_one,
        bias_query,
        bias_value,
        bias_out,
        gain_two,
        shift_two,
        bias_down,
        bias_up,
    ) = split_vectors(vector_weights, model_width)
    grad_ffn = grad_output.astype(jnp.bfloat16)
    grad_bias_down = jnp.sum(grad_ffn.astype(jnp.float32), axis=(0, 1))
    grad_down = mixed_sum("wtf,wtd->fd", active, grad_ffn)
    grad_active = mixed_sum("wtd,fd->wtf", grad_ffn, down_weights)
    gelu_pull = jax.vjp(partial(jax.nn.gelu, approximate=False), up_value)[1]
    grad_up = gelu_pull(grad_active)[0].astype(jnp.bfloat16)
    grad_bias_up = jnp.sum(grad_up.astype(jnp.float32), axis=(0, 1))
    grad_in = mixed_sum("wtd,wtf->df", normed_two, grad_up)
    grad_normed_two = mixed_sum("wtf,df->wtd", grad_up, row_weights[:, 4 * model_width :])
    norm_pull_two = jax.vjp(norm_rows, middle, gain_two, shift_two)[1]
    grad_middle_norm, grad_gain_two, grad_shift_two = norm_pull_two(grad_normed_two)
    grad_middle = grad_output + grad_middle_norm
    grad_branch = grad_middle.astype(jnp.bfloat16)
    grad_bias_out = jnp.sum(grad_branch.astype(jnp.float32), axis=(0, 1))
    grad_out_weight = mixed_sum("wtd,wte->de", mixed_low, grad_branch)
    grad_attended = mixed_sum(
        "wte,de->wtd", grad_branch, row_weights[:, 3 * model_width : 4 * model_width]
    ).astype(jnp.bfloat16)
    grad_attended = grad_attended.reshape(windows, blocks_dev, BLOCK, HEADS, head_dim)
    grad_query, grad_paired = attention_back(
        grad_attended,
        queries,
        sliding,
        global_kv,
        distant,
        probabilities,
        key_part,
        value_part,
        global_queries,
        full_probs,
        sender,
        picker,
        owned_hot,
    )
    grad_projected = jnp.concatenate(
        [
            grad_query.reshape(windows, tokens, model_width),
            grad_paired[..., :head_dim].reshape(windows, tokens, model_width),
            grad_paired[..., head_dim:].reshape(windows, tokens, model_width),
        ],
        axis=2,
    ).astype(jnp.bfloat16)
    summed = jnp.sum(grad_projected.astype(jnp.float32), axis=(0, 1))
    grad_bias_query = summed[:model_width]
    grad_bias_value = summed[2 * model_width :]
    grad_projection = mixed_sum("wtd,wte->de", normed, grad_projected)
    grad_normed = mixed_sum("wte,de->wtd", grad_projected, row_weights[:, : 3 * model_width])
    norm_pull_one = jax.vjp(norm_rows, hidden, gain_one, shift_one)[1]
    grad_hidden_norm, grad_gain_one, grad_shift_one = norm_pull_one(grad_normed)
    grad_hidden = grad_middle + grad_hidden_norm
    grad_rows = jnp.concatenate([grad_projection, grad_out_weight, grad_in], axis=1)
    grad_vectors = jnp.concatenate(
        [
            grad_gain_one,
            grad_shift_one,
            grad_bias_query,
            grad_bias_value,
            grad_bias_out,
            grad_gain_two,
            grad_shift_two,
            grad_bias_down,
            grad_bias_up,
        ]
    )
    return (grad_hidden, (grad_rows, grad_down, grad_vectors))


def adam_update(master, first_old, second_old, gradient, step_rate, decay_rate):
    first_new = 0.5 * first_old + 0.5 * gradient
    second_new = 0.5 * second_old + 0.5 * gradient * gradient
    first_hat = first_new / (1.0 - 0.5**STEP)
    second_hat = second_new / (1.0 - 0.5**STEP)
    master_new = master - step_rate * (
        first_hat / (jnp.sqrt(second_hat) + 1e-08) + decay_rate * master
    )
    return (master_new, first_new, second_new)


def general_shards(
    block_input,
    cotangent,
    random_ids,
    segment_ids,
    global_ids,
    w_rows,
    w_rows_first,
    w_rows_second,
    w_down,
    w_down_first,
    w_down_second,
    vectors,
    vectors_first,
    vectors_second,
):
    section_index = lax.axis_index(SECTION)
    seq_place = lax.axis_index(SEQ)
    groups = lax.axis_size(SEQ)
    row_weights, down_weights, vector_low = (
        lax.all_gather(w_rows[0].astype(jnp.bfloat16), (DP, SEQ), axis=1, tiled=True),
        lax.all_gather(w_down[0].astype(jnp.bfloat16), (DP, SEQ), axis=0, tiled=True),
        lax.all_gather(vectors[0].astype(jnp.bfloat16), (DP, SEQ), axis=0, tiled=True),
    )
    weights = (row_weights, down_weights, vector_low.astype(jnp.float32))
    micro_count, windows, tokens, model_width = block_input.shape
    received = jnp.zeros((windows, tokens, model_width), jnp.bfloat16)
    results = jnp.zeros(block_input.shape, jnp.float32)
    full_totals = (
        jnp.zeros(row_weights.shape, jnp.float32),
        jnp.zeros(down_weights.shape, jnp.float32),
        jnp.zeros(vector_low.shape, jnp.float32),
    )

    def tick(tick_index, carry):
        received, results, full_totals = carry
        forward_mb = jnp.clip(tick_index - section_index, 0, micro_count - 1)
        behind_raw = tick_index - 2 + section_index
        behind = jnp.clip(behind_raw, 0, micro_count - 1)
        live_mask = ((behind_raw >= 0) & (behind_raw < micro_count)).astype(jnp.float32)
        tables_forward = route_tables(
            lax.dynamic_index_in_dim(random_ids, forward_mb, 0, keepdims=False),
            lax.dynamic_index_in_dim(segment_ids, forward_mb, 0, keepdims=False),
            lax.dynamic_index_in_dim(global_ids, forward_mb, 0, keepdims=False),
            seq_place,
            groups,
        )
        tables_behind = route_tables(
            lax.dynamic_index_in_dim(random_ids, behind, 0, keepdims=False),
            lax.dynamic_index_in_dim(segment_ids, behind, 0, keepdims=False),
            lax.dynamic_index_in_dim(global_ids, behind, 0, keepdims=False),
            seq_place,
            groups,
        )
        incoming_values = received.astype(jnp.float32)
        first_input = lax.dynamic_index_in_dim(block_input, forward_mb, 0, keepdims=False).astype(
            jnp.float32
        )
        forward_input = jnp.where(section_index == 0, first_input, incoming_values)
        forward_output = layer_forward(forward_input, weights, tables_forward)[0]
        back_source = lax.dynamic_index_in_dim(block_input, behind, 0, keepdims=False).astype(
            jnp.float32
        )
        back_input = jnp.where(section_index == 0, back_source, incoming_values)
        given_grad = lax.dynamic_index_in_dim(cotangent, behind, 0, keepdims=False).astype(
            jnp.float32
        )
        back_grad = jnp.where(section_index == 0, incoming_values, given_grad) * live_mask
        stored = layer_forward(back_input, weights, tables_behind)[1]
        grad_input, gradients = layer_backward(stored, back_grad, weights, tables_behind)
        outgoing = jnp.where(section_index == 0, forward_output, grad_input).astype(jnp.bfloat16)
        finished = jnp.where(section_index == 0, grad_input, forward_output)
        updated = lax.dynamic_update_index_in_dim(results, finished, behind, 0)
        results = jnp.where(live_mask > 0, updated, results)
        full_totals = tuple(
            (total_part + grad_part for total_part, grad_part in zip(full_totals, gradients))
        )
        return (partner(outgoing, SECTION, 0), results, full_totals)

    received, results, full_totals = lax.fori_loop(
        0, micro_count + 2, tick, (received, results, full_totals)
    )
    shard_totals = (
        lax.psum_scatter(full_totals[0], (DP, SEQ), scatter_dimension=1, tiled=True),
        lax.psum_scatter(full_totals[1], (DP, SEQ), scatter_dimension=0, tiled=True),
        lax.psum_scatter(full_totals[2], (DP, SEQ), scatter_dimension=0, tiled=True),
    )
    new_rows, new_rows_first, new_rows_second = adam_update(
        w_rows[0], w_rows_first[0], w_rows_second[0], shard_totals[0], rate_matrix, decay_matrix
    )
    new_down, new_down_first, new_down_second = adam_update(
        w_down[0], w_down_first[0], w_down_second[0], shard_totals[1], rate_matrix, decay_matrix
    )
    new_vectors, new_vectors_first, new_vectors_second = adam_update(
        vectors[0], vectors_first[0], vectors_second[0], shard_totals[2], rate_vector, 0.0
    )
    return (
        results[None],
        new_rows[None],
        new_rows_first[None],
        new_rows_second[None],
        new_down[None],
        new_down_first[None],
        new_down_second[None],
        new_vectors[None],
        new_vectors_first[None],
        new_vectors_second[None],
    )


LOW = jnp.bfloat16
LOG_HIGH = [float(np.log(c).astype(ml_dtypes.bfloat16)) for c in (1.0, 2.0, 3.0)]
LOG_LOW = [float(np.log(c)) - high for c, high in zip((1.0, 2.0, 3.0), LOG_HIGH)]
CHUNK = 256
VMEM_BYTES = 60 * 1024 * 1024


def dot_rows(left, right):
    return lax.dot_general(left, right, (((1,), (1,)), ((), ())), preferred_element_type=jnp.float32)


def dot_plain(left, right):
    return lax.dot_general(left, right, (((1,), (0,)), ((), ())), preferred_element_type=jnp.float32)


def dot_tokens(left, right):
    return lax.dot_general(left, right, (((0,), (0,)), ((), ())), preferred_element_type=jnp.float32)


def swap(value):
    return lax.ppermute(value, SECTION, [(0, 1), (1, 0)])


def normalized(values_in):
    row_mean = jnp.mean(values_in, axis=-1, keepdims=True)
    centred = values_in - row_mean
    spread = jnp.mean(centred * centred, axis=-1, keepdims=True)
    scale = lax.rsqrt(spread + epsilon)
    return centred * scale, scale


class Shares:
    def __init__(self, width, columns, depth, vector_len):
        self.width = width
        self.columns = columns
        self.depth = depth
        self.vector_len = vector_len
        self.half = columns // 2
        self.per = width // columns
        self.groups = columns // depth

    def unpack(self, gathered, core):
        rows, down, vec = gathered
        vec = vec.reshape(-1, TAIL, self.width)[:, 0, : self.vector_len].reshape(-1)
        pieces = split_vectors(vec.astype(jnp.float32), self.width)
        for index in (2, 3):
            pieces[index] = lax.dynamic_index_in_dim(
                pieces[index].reshape(self.per, 2, self.half), core, 1, keepdims=False
            ).reshape(-1)
        pieces[8] = lax.dynamic_index_in_dim(
            pieces[8].reshape(-1, 2, self.depth // 2), core, 1, keepdims=False
        ).reshape(-1)
        nothing = jnp.zeros_like(pieces[2])
        proj = [pieces[2], nothing, pieces[3], nothing]
        order = [pieces[index] for index in (0, 1, 4, 5, 6, 7)] + proj + [pieces[8]]
        return (
            (rows.reshape(-1, self.width), down.reshape(-1, self.width)),
            jnp.concatenate(order).reshape(-1, self.width),
        )

    def by_shard(self, grads, vector_grads, core):
        rows, down = grads
        half, per, width = self.half, self.per, self.width
        hot = (jnp.arange(2) == core).astype(jnp.float32)
        spread = list(vector_grads)
        for index in (2, 3):
            spread[index] = (
                spread[index].reshape(per, 1, half) * hot[None, :, None]
            ).reshape(-1)
        spread[8] = (spread[8].reshape(-1, 1, self.depth // 2) * hot[None, :, None]).reshape(-1)
        for index in (0, 1, 4, 5, 6, 7):
            spread[index] = spread[index] * hot[0]
        vec = jnp.concatenate(spread).reshape(-1, 1, self.vector_len)
        vec = jnp.pad(vec, ((0, 0), (0, TAIL - 1), (0, width - self.vector_len))).astype(LOW)
        return [array.reshape(2, 2, 4, -1, width) for array in (rows, down, vec)]


MESH = pl.DeviceIdType.MESH
PIECE = 48
TAIL = 16


def prepare_kernel(shares, rows_ref, down_ref, vector_ref, rows_out, down_out, vector_out):
    core = lax.axis_index(SECTION)
    offset = lax.axis_index((DP, SEQ)) * shares.columns
    half, per, width, depth = shares.half, shares.per, shares.width, shares.depth // 2
    is_inner = (offset >= 3 * width) & (offset < 4 * width)
    is_hidden = offset >= 4 * width

    @pl.when(is_inner)
    def _():
        for which in range(2):
            side = core if which == 0 else 1 - core
            held = [rows_ref[pl.ds((2 * j + side) * half, half), :] for j in range(per)]
            turned = jnp.transpose(jnp.concatenate(held, axis=0))
            rows_out[which] = jnp.concatenate([turned[:half], turned[half:]], axis=1).astype(LOW)

    @pl.when(jnp.logical_not(is_inner))
    def _():
        turned = jnp.transpose(rows_ref[...]).astype(LOW)
        plain = [turned[:half], turned[half:]]
        hidden = [
            jnp.concatenate(
                [turned[(2 * j + side) * depth :][:depth] for j in range(shares.groups)], axis=0
            )
            for side in range(2)
        ]
        halves = [jnp.where(is_hidden, b, a) for a, b in zip(plain, hidden)]
        rows_out[0] = jnp.where(core == 0, halves[0], halves[1])
        rows_out[1] = jnp.where(core == 0, halves[1], halves[0])

    down = down_ref[...].astype(LOW)
    down_out[0] = jnp.where(core == 0, down[:depth], down[depth:])
    down_out[1] = jnp.where(core == 0, down[depth:], down[:depth])
    vector_out[...] = jnp.zeros_like(vector_out)
    vector_out[0:1, : shares.vector_len] = vector_ref[...].astype(LOW)


def prepare(shares, rows, down, vector):
    return pl.pallas_call(
        partial(prepare_kernel, shares),
        out_shape=[
            jax.ShapeDtypeStruct((2, shares.half, shares.width), LOW),
            jax.ShapeDtypeStruct((2, shares.depth // 2, shares.width), LOW),
            jax.ShapeDtypeStruct((TAIL, shares.width), LOW),
        ],
        compiler_params=pltpu.CompilerParams(vmem_limit_bytes=VMEM_BYTES),
    )(rows, down, vector)


class Place:
    def __init__(self):
        self.core = lax.axis_index(SECTION)
        self.dp = lax.axis_index(DP)
        self.z = lax.axis_index(SEQ)
        self.y, self.x = self.dp // 2, self.dp % 2
        self.high, self.low = self.z // 2, self.z % 2
        self.inner = self.high + self.low == 1
        self.outer = self.high + self.low != 1
        self.partner = {SECTION: 1 - self.core}
        self.along_x = {DP: 2 * self.y + 1 - self.x}
        self.along_y = {DP: 2 * (1 - self.y) + self.x}
        self.across = {SEQ: 3 - self.z}
        self.beside = {SEQ: 2 * self.high + 1 - self.low}
        self.others = [{SEQ: (self.z + by) % 4} for by in (1, 2, 3)]
        self.own = pl.ds(self.z, 1)
        self.next = pl.ds(2 * self.high + 1 - self.low, 1)
        self.near = pl.ds(2 * self.high, 2)
        self.far = pl.ds(2 * (1 - self.high), 2)

    def greet(self):
        barrier = pltpu.get_barrier_semaphore()
        everyone = [self.partner, self.along_x, self.along_y] + self.others
        for device in everyone:
            pl.semaphore_signal(barrier, inc=1, device_id=device, device_id_type=MESH)
        pl.semaphore_wait(barrier, len(everyone))


def remote(src, dst, sems, spots, device):
    return pltpu.make_async_remote_copy(
        src_ref=src,
        dst_ref=dst,
        send_sem=sems[0].at[spots[0]],
        recv_sem=sems[1].at[spots[1]],
        device_id=device,
        device_id_type=MESH,
    )


def chunk_pairs(shares):
    pairs = []
    for array, length in ((0, shares.half), (1, shares.depth // 2)):
        for start in range(0, length, 2 * PIECE):
            pairs.append([(array, start, PIECE, 0), (array, start + PIECE, PIECE, 1)])
    pairs[0].append((2, 0, TAIL, 0))
    return pairs


def quad_pairs(shares):
    length = (shares.half + shares.depth // 2) // 2
    pairs = [
        [(0, start, PIECE, None), (1, start, PIECE, None)] for start in range(0, length, PIECE)
    ]
    pairs[0].append((2, 0, TAIL, 0))
    return pairs


def gather_kernel(shares, *refs):
    (rows_in, down_in, vector_in, x_in, cot_in), refs = refs[:5], refs[5:]
    outs, refs = [refs[0:3], refs[3:6]], refs[6:]
    (x_out, cot_out), refs = refs[:2], refs[2:]
    local, swap_send, swap_recv, z_send, z_recv, send, recv = refs
    here = Place()
    core, y, x, z = here.core, here.y, here.x, here.z
    half = x_in.shape[2] // 2
    rows_half, down_half = shares.half // 2, shares.depth // 4
    here.greet()

    def slices(source, target, base):
        mine = pl.ds(pl.multiple_of(core * half, half), half)
        sems = (z_send, z_recv)
        own = pltpu.make_async_copy(
            source.at[z, 0, mine], target.at[z, core], local.at[8 + base // 4]
        )
        sends, arrivals = [], []
        for by in (1, 2, 3):
            spots = (base + by - 1, base + by - 1)
            device = here.others[by - 1]
            sends.append(
                remote(source.at[(z + by) % 4, 0, mine], target.at[z, core], sems, spots, device)
            )
            arrivals.append(
                remote(
                    source.at[z, 0, mine], target.at[(z + 4 - by) % 4, core], sems, spots, device
                )
            )
        spots = (base + 3, base + 3)
        forward = remote(target.at[:, core], target.at[:, core], sems, spots, here.partner)
        arrived = remote(target.at[:, 1 - core], target.at[:, 1 - core], sems, spots, here.partner)
        return own, sends, arrivals, forward, arrived

    x_moves = slices(x_in, x_out, 0)
    cot_moves = slices(cot_in, cot_out, 4)

    def open_slices(moves):
        moves[0].start()
        for copy in moves[1]:
            copy.start()

    def pass_slices(moves):
        moves[0].wait()
        for copy in moves[2]:
            copy.wait_recv()
        moves[3].start()

    def close_slices(moves):
        for copy in moves[1]:
            copy.wait_send()
        moves[3].wait_send()
        moves[4].wait_recv()

    def first_moves(layer, which):
        down = down_in.at[which]
        rows = rows_in.at[which]
        if layer == 0:
            return [
                (0, rows, outs[0][0].at[y, x, z]),
                (1, down, outs[0][1].at[y, x, z]),
                (2, vector_in, outs[0][2].at[y, x, z]),
            ]
        moves = [(7, vector_in, outs[1][2].at[y, x, z])]
        for part in range(2):
            target = outs[1][part]
            moves.append(
                (
                    3 + 2 * part,
                    rows.at[pl.ds(part * rows_half, rows_half)],
                    target.at[z, pl.ds(0, rows_half)],
                )
            )
            moves.append(
                (
                    4 + 2 * part,
                    down.at[pl.ds(part * down_half, down_half)],
                    target.at[z, pl.ds(rows_half, down_half)],
                )
            )
        return moves

    swaps = (swap_send, swap_recv)
    for layer in range(2):

        @pl.when(core == layer)
        def _():
            across = [
                remote(src, dst, swaps, (spot, spot), here.partner)
                for spot, src, dst in first_moves(layer, 1)
            ]
            own = [
                pltpu.make_async_copy(src, dst, local.at[spot])
                for spot, src, dst in first_moves(layer, 0)
            ]
            for copy in across + own:
                copy.start()
            for copy in own:
                copy.wait()
            for copy in across:
                copy.wait_send()
            for spot, src, dst in first_moves(1 - layer, 0):
                remote(src, dst, swaps, (spot, spot), here.partner).wait_recv()

    numbers, pairs = {}, []
    for layer in range(2):
        for pair in chunk_pairs(shares) if layer == 0 else quad_pairs(shares):
            entry = []
            for array, start, length, order in pair:
                ref = outs[layer][array]
                rows = pl.ds(start, length)
                flat = order is None
                number = len(numbers)
                sems = (send, recv)

                def part(which):
                    return ref.at[which, rows] if flat else ref.at[y, x, which, rows]

                def copy(piece, spots, device):
                    return remote(piece, piece, sems, ((number, spots[0]), (number, spots[1])), device)

                steps = {
                    "z": copy(part(here.own), (0, 0), here.beside),
                    "across": copy(part(here.near), (1, 1), here.across),
                    "on": copy(part(here.far), (4, 1), here.beside),
                }
                arrive = [
                    copy(part(here.next), (0, 0), here.beside),
                    copy(part(here.far), (1, 1), here.across),
                ]
                if order == 0:
                    steps["one"] = copy(ref.at[y, x, :, rows], (2, 2), here.along_y)
                    steps["two"] = copy(ref.at[:, x, :, rows], (3, 3), here.along_x)
                    arrive.append(copy(ref.at[1 - y, x, :, rows], (2, 2), here.along_y))
                    arrive.append(copy(ref.at[:, 1 - x, :, rows], (3, 3), here.along_x))
                elif order == 1:
                    steps["one"] = copy(ref.at[y, x, :, rows], (2, 2), here.along_x)
                    steps["two"] = copy(ref.at[y, :, :, rows], (3, 3), here.along_y)
                    arrive.append(copy(ref.at[y, 1 - x, :, rows], (2, 2), here.along_x))
                    arrive.append(copy(ref.at[1 - y, :, :, rows], (3, 3), here.along_y))
                numbers[number] = (steps, arrive)
                entry.append(number)
            pairs.append(entry)

    def issue(name, entry):
        after = {"z": None, "across": 0, "on": 1, "one": 1, "two": 2}[name]

        def start():
            for number in entry:
                steps, arrive = numbers[number]
                if name in steps:
                    if after is not None and not (name == "one"):
                        arrive[after].wait_recv()
                    steps[name].start()

        if name in ("across", "on"):
            pl.when(here.inner)(start)
        else:
            start()

    def arrived(entry, index, where):
        def wait():
            for number in entry:
                numbers[number][1][index].wait_recv()

        pl.when(where)(wait)

    first, second = pairs[: len(chunk_pairs(shares))], pairs[len(chunk_pairs(shares)) :]
    for entry in first:
        issue("z", entry)
    for entry in first:
        issue("across", entry)
        arrived(entry, 0, here.outer)
    for entry in first[:-1]:
        issue("on", entry)
        arrived(entry, 1, here.outer)
        issue("one", entry)
    issue("on", first[-1])
    for entry in second:
        issue("z", entry)
    open_slices(x_moves)
    arrived(first[-1], 1, here.outer)
    issue("one", first[-1])
    issue("two", first[0])
    for entry in second:
        issue("across", entry)
        arrived(entry, 0, here.outer)
    issue("two", first[1])
    open_slices(cot_moves)
    for entry in second:
        issue("on", entry)
    issue("two", first[2])
    pass_slices(x_moves)
    for entry in second:
        arrived(entry, 1, here.outer)
        for number in entry:
            steps, arrive = numbers[number]
            if "one" in steps:
                steps["one"].start()
                arrive[2].wait_recv()
                steps["two"].start()
    pass_slices(cot_moves)
    for steps, arrive in numbers.values():
        if len(arrive) == 4:
            arrive[3].wait_recv()
        for name in steps:
            if name not in ("across", "on"):
                steps[name].wait_send()

    @pl.when(here.inner)
    def _():
        for steps, _ in numbers.values():
            steps["across"].wait_send()
            steps["on"].wait_send()

    close_slices(x_moves)
    close_slices(cot_moves)


def gather(shares, prepared, block_input, cotangent):
    micro, _, tokens, width = block_input.shape
    chunks = sum(len(pair) for pair in chunk_pairs(shares) + quad_pairs(shares))
    lengths = (shares.half, shares.depth // 2, TAIL)
    layer = [jax.ShapeDtypeStruct((2, 2, 4, rows, width), LOW) for rows in lengths]
    quad = jax.ShapeDtypeStruct((4, (lengths[0] + lengths[1]) // 2, width), LOW)
    window = jax.ShapeDtypeStruct((micro, 2, tokens // 2, width), LOW)
    anywhere = pl.BlockSpec(memory_space=pl.ANY)
    results = pl.pallas_call(
        partial(gather_kernel, shares),
        in_specs=[pl.BlockSpec(memory_space=pltpu.VMEM)] * 3 + [anywhere] * 2,
        out_specs=[anywhere] * 8,
        out_shape=layer + [quad, quad, layer[2]] + [window, window],
        scratch_shapes=[
            pltpu.SemaphoreType.DMA((10,)),
            pltpu.SemaphoreType.DMA((8,)),
            pltpu.SemaphoreType.DMA((8,)),
            pltpu.SemaphoreType.DMA((8,)),
            pltpu.SemaphoreType.DMA((8,)),
            pltpu.SemaphoreType.DMA((chunks, 5)),
            pltpu.SemaphoreType.DMA((chunks, 4)),
        ],
        compiler_params=pltpu.CompilerParams(
            collective_id=0, has_side_effects=True, vmem_limit_bytes=VMEM_BYTES
        ),
    )(*prepared, block_input, cotangent)
    return results[0:3], results[3:6], results[6], results[7]


def over(value, bit):
    return lax.ppermute(value, DP, [(i, i ^ bit) for i in range(4)])


def layout_moves(shares, y, x, pieces, arrays):
    rows_half, down_half = shares.half // 2, shares.depth // 4
    moves = []
    for part in range(2):
        for index, (by_y, by_x) in enumerate(((0, 0), (1, 0), (0, 1), (1, 1))):
            piece = pieces[part][index]
            at_y, at_x = y ^ by_y, x ^ by_x
            for array, length, start in ((0, rows_half, 0), (1, down_half, rows_half)):
                moves.append(
                    (
                        piece.at[:, pl.ds(start, length)],
                        arrays[array].at[at_y, at_x, :, pl.ds(part * length, length)],
                    )
                )
    return moves


def layout_kernel(shares, joins, *refs):
    dp = lax.axis_index(DP)
    if joins:
        pieces, arrays = [refs[0:4], refs[4:8]], refs[8:10]
    else:
        arrays, pieces = refs[0:2], [refs[2:6], refs[6:10]]
    for spot in range(4):

        @pl.when(dp == spot)
        def _():
            for piece, place in layout_moves(shares, spot // 2, spot % 2, pieces, arrays):
                src, dst = (piece, place) if joins else (place, piece)
                dst[...] = src[...]


def layout(shares, joins, *arrays):
    half, depth, width = shares.half, shares.depth // 2, shares.width
    length = (half + depth) // 2
    merged_specs = [
        pl.BlockSpec((2, 2, 1, rows, width), lambda z: (0, 0, z, 0, 0)) for rows in (half, depth)
    ]
    merged_shapes = [(2, 2, 4, rows, width) for rows in (half, depth)]
    piece_specs = [pl.BlockSpec((1, length, width), lambda z: (z, 0, 0))] * 8
    piece_shapes = [(4, length, width)] * 8
    return pl.pallas_call(
        partial(layout_kernel, shares, joins),
        grid=(4,),
        in_specs=piece_specs if joins else merged_specs,
        out_specs=merged_specs if joins else piece_specs,
        out_shape=[
            jax.ShapeDtypeStruct(shape, LOW) for shape in (merged_shapes if joins else piece_shapes)
        ],
        compiler_params=pltpu.CompilerParams(vmem_limit_bytes=VMEM_BYTES),
        cost_estimate=pl.CostEstimate(
            flops=0, bytes_accessed=64 * (half + depth) * width, transcendentals=0
        ),
    )(*arrays)


def tied(value, flying):
    return lax.optimization_barrier((value, flying))


def spread_quads(shares, quads):
    low, high = quads
    flying = (low, high, over(low, 2), over(high, 1))
    low, high, low_y, high_x = yield flying
    flying = (low_y, high_x, over(low, 1), over(high, 2))
    low_y, high_x, low_x, high_y = yield flying
    flying = (over(low_y, 1), over(high_x, 2))
    low_both, high_both = yield flying
    yield layout(shares, True, low, low_y, low_x, low_both, high, high_y, high_x, high_both)


def sum_quads(shares, arrays):
    pieces = layout(shares, False, *arrays)

    low, low_y, low_x, low_both = pieces[:4]
    high, high_y, high_x, high_both = pieces[4:]
    flying = (low_x, high_y, over(low_both, 1), over(high_both, 2))
    low_x, high_y, low_hop, high_hop = yield flying
    low_y, high_x = low_y + low_hop, high_x + high_hop
    flying = (low_y, high_x, over(low_x, 1), over(high_y, 2))
    low_y, high_x, low_x, high_y = yield flying
    flying = (over(low_y, 2), over(high_x, 1))
    low_y, high_x = yield flying
    yield (low, high, low_x, high_x, low_y, high_y)


class Beside:
    def __init__(self, hops=None):
        self.hops = hops
        self.flying = None if hops is None else next(hops)

    def tie(self, value):
        if self.hops is None:
            return value
        value, arrived = tied(value, self.flying)
        self.flying = self.hops.send(arrived)
        return value


def scatter_kernel(shares, *refs):
    (rows_zero, down, vec_zero, *terms, vec_one), refs = refs[:10], refs[10:]
    (dx_ref, final_ref, halves, slices), refs = refs[:4], refs[4:]
    work, refs = [refs[0:3], refs[3:6]], refs[6:]
    added, refs = refs[:4], refs[4:]
    (got_one, got_two, got_far, got_across, got_near, total), refs = refs[:6], refs[6:]
    load, local, swap_send, swap_recv, z_send, z_recv, send, recv = refs
    here = Place()
    core, y, x, z = here.core, here.y, here.x, here.z
    rows_half, down_half = shares.half // 2, shares.depth // 4
    down_base = shares.half
    tail_base = shares.half + shares.depth // 2

    moves = [
        [(rows_zero, work[0][0]), (down, work[0][1]), (vec_zero, work[0][2])],
        [(terms[0], work[1][0]), (terms[1], work[1][1]), (vec_one, work[1][2])],
    ]
    moves[1] += zip(terms[2:], added)
    loads = [
        [
            pltpu.make_async_copy(src, dst, load.at[layer, index])
            for index, (src, dst) in enumerate(moves[layer])
        ]
        for layer in range(2)
    ]
    for layer in (1, 0):
        for copy in loads[layer]:
            copy.start()
    here.greet()

    def place_of(layer, array, start):
        if array == 2:
            return tail_base
        if layer == 0:
            return (0, down_base)[array] + start
        if start < rows_half:
            return array * rows_half + start
        return down_base + array * down_half + start - rows_half

    pairs, chunks = [], []
    for layer in (1, 0):
        for index, pair in enumerate(quad_pairs(shares) if layer else chunk_pairs(shares)):
            entry = []
            for array, start, length, order in pair:
                entry.append((len(chunks), layer, array, start, length, order))
                chunks.append(entry[-1])
            pairs.append((index, entry))

    def pieces(chunk):
        number, layer, array, start, length, order = chunk
        ref = work[layer][array]
        rows = pl.ds(start, length)
        sems = (send, recv)
        keeps, slots, copies = [], [], []

        def part(which):
            return ref.at[which, rows] if order is None else ref.at[y, x, which, rows]

        def add(src, slot, device, keep):
            spots = (number, len(copies))
            copies.append(remote(src, slot, sems, (spots, spots), device))
            slots.append(slot)
            keeps.append(keep)

        room = pl.ds(0, length)
        if order == 0:
            add(ref.at[:, 1 - x, :, rows], got_one.at[number, :, :, room], here.along_x, ref.at[:, x, :, rows])
            add(ref.at[1 - y, x, :, rows], got_two.at[number, :, room], here.along_y, ref.at[y, x, :, rows])
        elif order == 1:
            add(ref.at[1 - y, :, :, rows], got_one.at[number, :, :, room], here.along_y, ref.at[y, :, :, rows])
            add(ref.at[y, 1 - x, :, rows], got_two.at[number, :, room], here.along_x, ref.at[y, x, :, rows])
        else:
            copies, slots, keeps = [None] * 2, [None] * 2, [None] * 2
        add(part(here.far), got_far.at[number, :, room], here.beside, part(here.far))
        add(part(here.far), got_across.at[number, :, room], here.across, part(here.near))
        add(part(here.next), got_near.at[number, :, room], here.beside, part(here.own))
        return copies, keeps, slots

    built = [pieces(chunk) for chunk in chunks]
    loaded = set()

    def land(number, phase):
        copies, keeps, slots = built[number]
        copies[phase].wait_recv()
        keep, slot = keeps[phase], slots[phase]
        keep[...] = keep[...] + slot[...]

    def run(chunk, phase):
        number, layer, array, start, length, order = chunk
        copies, keeps, slots = built[number]
        if (layer, array) not in loaded:
            loaded.add((layer, array))
            loads[layer][array].wait()
            if layer == 1 and array < 2:
                loads[1][3 + array].wait()
                loads[1][5 + array].wait()
                for group in range(4):
                    parts = (work[1][array], added[array], added[2 + array])
                    summed = sum(part[group].astype(jnp.float32) for part in parts)
                    work[1][array][group] = summed.astype(LOW)
        if phase < 2:
            if order is not None:
                if phase:
                    land(number, 0)
                copies[phase].start()
        elif phase == 2:
            if order is not None:
                land(number, 1)

            @pl.when(here.outer)
            def _():
                copies[2].start()
                copies[4].start()

        elif phase == 3:

            @pl.when(here.inner)
            def _():
                land(number, 2)
                copies[3].start()

        elif phase == 4:

            @pl.when(here.inner)
            def _():
                land(number, 3)
                copies[4].start()

        else:
            copies[4].wait_recv()
            spot = pl.ds(place_of(layer, array, start), length)
            total[layer, spot, :] = (keeps[4][...] + slots[4][...])[0]

    def step(entry, phase):
        for chunk in entry:
            run(chunk, phase)

    second = [entry for _, entry in pairs[: len(quad_pairs(shares))]]
    first = [entry for _, entry in pairs[len(quad_pairs(shares)) :]]
    tails = [chunk for entry in second for chunk in entry if chunk[5] is not None]
    second = [[chunk for chunk in entry if chunk[5] is None] for entry in second]
    first[0] = first[0] + tails
    step(first[0], 0)
    step(first[1], 0)
    for entry in second:
        step(entry, 2)
    step(first[0], 1)
    for section, source in ((0, dx_ref), (1, final_ref)):

        @pl.when(core == section)
        def _():
            pltpu.make_async_copy(source.at[z], slices.at[z], local.at[0]).start()
            for by in (1, 2, 3):
                remote(
                    source.at[(z + by) % 4],
                    slices.at[z],
                    (z_send, z_recv),
                    (by - 1, by - 1),
                    here.others[by - 1],
                ).start()

    for entry in second:
        step(entry, 3)
    step(first[2], 0)
    step(first[1], 1)
    for entry in second:
        step(entry, 4)
    step(first[0], 2)
    step(first[2], 1)
    for entry in second:
        step(entry, 5)
    step(first[0], 3)
    step(first[1], 2)
    step(first[0], 4)
    step(first[1], 3)
    step(first[2], 2)
    step(first[1], 4)
    step(first[2], 3)
    step(first[2], 4)
    for entry in first:
        step(entry, 5)

    for copies, _, _ in built:
        for index in (0, 1, 4):
            if copies[index] is not None:
                copies[index].wait_send()
    for section, index in ((here.outer, 2), (here.inner, 3)):

        @pl.when(section)
        def _():
            for copies, _, _ in built:
                copies[index].wait_send()

    swaps = (swap_send, swap_recv)
    across = remote(total.at[1 - core], halves.at[core], swaps, (0, 0), here.partner)
    across.start()
    own = pltpu.make_async_copy(total.at[core], halves.at[core], local.at[1])
    own.start()
    own.wait()
    across.wait_send()
    remote(total.at[1 - core], halves.at[1 - core], swaps, (0, 0), here.partner).wait_recv()
    pltpu.make_async_copy(dx_ref.at[z], slices.at[z], local.at[0]).wait()
    for by in (1, 2, 3):
        copy = remote(
            dx_ref.at[z],
            slices.at[(z + 4 - by) % 4],
            (z_send, z_recv),
            (by - 1, by - 1),
            here.others[by - 1],
        )
        copy.wait_send()
        copy.wait_recv()


def scatter(shares, arrays, vec_zero, quads, vec_one, grad, final):
    micro, tokens, width = grad.shape
    lengths = (shares.half, shares.depth // 2, TAIL)
    chunks = sum(len(pair) for pair in chunk_pairs(shares) + quad_pairs(shares))
    rows = sum(lengths)
    anywhere = pl.BlockSpec(memory_space=pl.ANY)
    work = [pltpu.VMEM((2, 2, 4, length, width), LOW) for length in lengths]
    quad = pltpu.VMEM((4, (lengths[0] + lengths[1]) // 2, width), LOW)
    return pl.pallas_call(
        partial(scatter_kernel, shares),
        in_specs=[anywhere] * 12,
        out_specs=[anywhere] * 2,
        out_shape=[
            jax.ShapeDtypeStruct((2, rows, width), LOW),
            jax.ShapeDtypeStruct((micro, tokens, width), LOW),
        ],
        scratch_shapes=work
        + [quad, quad, work[2]]
        + [quad] * 4
        + [
            pltpu.VMEM((chunks, 2, 4, PIECE, width), LOW),
            pltpu.VMEM((chunks, 4, PIECE, width), LOW),
            pltpu.VMEM((chunks, 2, PIECE, width), LOW),
            pltpu.VMEM((chunks, 2, PIECE, width), LOW),
            pltpu.VMEM((chunks, 1, PIECE, width), LOW),
            pltpu.VMEM((2, rows, width), LOW),
            pltpu.SemaphoreType.DMA((2, 7)),
            pltpu.SemaphoreType.DMA((2,)),
            pltpu.SemaphoreType.DMA((1,)),
            pltpu.SemaphoreType.DMA((1,)),
            pltpu.SemaphoreType.DMA((3,)),
            pltpu.SemaphoreType.DMA((3,)),
            pltpu.SemaphoreType.DMA((chunks, 5)),
            pltpu.SemaphoreType.DMA((chunks, 5)),
        ],
        compiler_params=pltpu.CompilerParams(
            collective_id=1, has_side_effects=True, vmem_limit_bytes=VMEM_BYTES
        ),
    )(*arrays, vec_zero, *quads, vec_one, grad, final)


def update_kernel(shares, halves_ref, slices_ref, *refs):
    old, new, result_ref, turned = refs[:9], refs[9:18], refs[18], refs[19]
    result_ref[...] = slices_ref[...].astype(jnp.float32)
    offset = lax.axis_index((DP, SEQ)) * shares.columns
    half, per, width, depth = shares.half, shares.per, shares.width, shares.depth // 2
    is_inner = (offset >= 3 * width) & (offset < 4 * width)
    is_hidden = offset >= 4 * width

    @pl.when(is_inner)
    def _():
        for side in range(2):
            piece = halves_ref[side, :half, :].astype(jnp.float32)
            wide = per * half
            back = jnp.transpose(jnp.concatenate([piece[:, :wide], piece[:, wide:]], axis=0))
            for j in range(per):
                turned[(2 * j + side) * half : (2 * j + side + 1) * half, :] = back[
                    j * half : (j + 1) * half
                ]

    @pl.when(jnp.logical_not(is_inner))
    def _():
        pair = [halves_ref[side, :half, :].astype(jnp.float32) for side in range(2)]
        plain = jnp.concatenate(pair, axis=0)
        hidden = jnp.concatenate(
            [pair[side][j * depth :][:depth] for j in range(shares.groups) for side in range(2)],
            axis=0,
        )
        turned[...] = jnp.transpose(jnp.where(is_hidden, hidden, plain))

    def store(first, gradient, rate, decay):
        results = adam_update(*[ref[...] for ref in old[first : first + 3]], gradient, rate, decay)
        for ref, result in zip(new[first : first + 3], results):
            ref[...] = result

    store(0, turned[...], rate_matrix, decay_matrix)
    down = [halves_ref[side, half : half + depth, :] for side in range(2)]
    store(3, jnp.concatenate(down, axis=0).astype(jnp.float32), rate_matrix, decay_matrix)
    tails = [halves_ref[side, half + depth :, :].astype(jnp.float32) for side in range(2)]
    store(6, (tails[0] + tails[1])[0:1, : shares.vector_len], rate_vector, 0.0)


def update(shares, halves, slices, old):
    return pl.pallas_call(
        partial(update_kernel, shares),
        out_shape=[jax.ShapeDtypeStruct(piece.shape, jnp.float32) for piece in (*old, slices)],
        scratch_shapes=[pltpu.VMEM((shares.width, shares.columns), jnp.float32)],
        compiler_params=pltpu.CompilerParams(vmem_limit_bytes=VMEM_BYTES),
    )(halves, slices, *old)


(GAIN_ONE, SHIFT_ONE, BIAS_OUT, GAIN_TWO, SHIFT_TWO, BIAS_DOWN, BIAS_PROJ, _, BIAS_UP, _) = [
    slice(row, row + 1) for row in range(10)
]
ROWS = 256
COLS = 384
WIDE = 512
STRIP = 32


def whole(shape):
    return pl.BlockSpec(shape, lambda i: (0,) * len(shape))


def row_block(width):
    return pl.BlockSpec((ROWS, width), lambda i: (i, 0))


def col_block(tokens):
    return pl.BlockSpec((tokens, COLS), lambda i: (0, i))


def at_block(shape, *index):
    return pl.BlockSpec(shape, lambda i: index)


def params_of(flops, moved, transcendentals=0):
    return {
        "compiler_params": pltpu.CompilerParams(vmem_limit_bytes=VMEM_BYTES),
        "cost_estimate": pl.CostEstimate(
            flops=flops, bytes_accessed=moved, transcendentals=transcendentals
        ),
    }


def strips(length=ROWS, strip=STRIP):
    return [slice(first, first + strip) for first in range(0, length, strip)]


def both(own_ref, recv_ref, rows):
    return own_ref[rows, :].astype(jnp.float32) + recv_ref[rows, :].astype(jnp.float32)


def bias_of(vec_ref, first, start, length):
    row, width = first.start, vec_ref.shape[1]
    pieces = []
    for place in range(2):
        low = max(start - place * width, 0)
        high = min(start + length - place * width, width)
        if low < high:
            pieces.append(vec_ref[row + place : row + place + 1, low:high])
    return pieces[0] if len(pieces) == 1 else jnp.concatenate(pieces, axis=1)


def eights(values):
    rows, width = values.shape
    return jnp.sum(values.reshape(rows // 8, 8, width), axis=0)


def features_kernel(shares, random_ref, segment_ref, global_ref, query_ref, key_ref, turned_ref):
    core = lax.axis_index(SECTION)
    place = lax.axis_index(SEQ)
    blocks = random_ref.shape[1]
    width = key_ref.shape[1]
    heads = query_ref.shape[0]
    per_half = heads // shares.per
    picks = random_ref.shape[2] // (2 * heads)
    tokens = key_ref.shape[0]
    lane = lax.broadcasted_iota(jnp.int32, (blocks, width), 1)
    row = lax.broadcasted_iota(jnp.int32, (blocks, width), 0)
    key = jnp.where(lane < blocks, lane, lane - blocks)
    chosen = random_ref[place]
    named = global_ref[place]
    always = (jnp.abs(row - key) <= 1).astype(jnp.int32)
    is_global = jnp.zeros((blocks, width), jnp.int32)
    for index in range(named.shape[1]):
        spot = named[:, index : index + 1]
        always = always + (key == spot).astype(jnp.int32)
        is_global = is_global + (row == spot).astype(jnp.int32)
    line = segment_ref[place].astype(jnp.float32)
    column = jnp.transpose(jnp.broadcast_to(line, (8, tokens)))[:, 0:1]
    token_lane = lax.broadcasted_iota(jnp.int32, (tokens, width), 1)
    same = column == (token_lane - 2 * blocks).astype(jnp.float32)
    in_segment = (token_lane >= 2 * blocks) & (token_lane < 2 * blocks + 3)
    segment_side = jnp.where(in_segment & same, 1.0, 0.0)
    for head in range(heads):
        count = always
        for pick in range(picks):
            at = [
                (2 * per_half * (head // per_half) + per_half * side + head % per_half) * picks
                + pick
                for side in range(2)
            ]
            spot = jnp.where(core == 0, chosen[:, at[0] : at[0] + 1], chosen[:, at[1] : at[1] + 1])
            count = count + (key == spot).astype(jnp.int32)
        count = jnp.where(is_global > 0, 1, count)
        high = jnp.where(count == 0, masked, 0.0)
        low = jnp.zeros_like(high)
        for times in (2, 3):
            high = jnp.where(count == times, LOG_HIGH[times - 1], high)
            low = jnp.where(count == times, LOG_LOW[times - 1], low)
        table = jnp.where(lane < blocks, high, jnp.where(lane < 2 * blocks, low, 0.0))
        for block in range(blocks):
            rows = slice(block * BLOCK, (block + 1) * BLOCK)
            query_ref[head, rows, :] = (table[block : block + 1] + segment_side[rows]).astype(LOW)
    token_block = lax.shift_right_logical(
        lax.broadcasted_iota(jnp.int32, (tokens, width), 0), BLOCK.bit_length() - 1
    )
    here = (token_block == token_lane) | (token_block == token_lane - blocks)
    side = jnp.where(here & (token_lane < 2 * blocks), 1.0, 0.0)
    side = jnp.where(in_segment & jnp.logical_not(same), masked, side)
    ones = (token_lane >= 2 * blocks + 3) & (token_lane < 2 * blocks + 6)
    side = jnp.where(ones, 1.0, side)
    key_ref[...] = side.astype(LOW)
    turned_ref[...] = jnp.transpose(side).astype(LOW)


def key_features(shares, random_ids, segment_ids, global_ids):
    micro, _, blocks, head_count, picks = random_ids.shape
    tokens = segment_ids.shape[2]
    width = -(-(2 * blocks + 6) // 128) * 128
    return pl.pallas_call(
        partial(features_kernel, shares),
        out_shape=[
            jax.ShapeDtypeStruct((head_count // 2, tokens, width), LOW),
            jax.ShapeDtypeStruct((tokens, width), LOW),
            jax.ShapeDtypeStruct((width, tokens), LOW),
        ],
        **params_of(0, head_count * tokens * width),
    )(random_ids.reshape(micro, blocks, head_count * picks), segment_ids, global_ids)


def project_kernel(joins, *refs):
    if joins:
        (middle_ref, part_ref, recv_ref, before_ref), refs = refs[:4], refs[4:]
    else:
        hidden_ref, refs = refs[0], refs[1:]
    (vec_ref, weight_ref), refs = refs[:2], refs[2:]
    if joins:
        hidden_ref, refs = refs[0], refs[1:]
    normed_ref, out_ref = refs
    for rows in strips():
        if joins:
            part = both(part_ref, recv_ref, rows)
            low = (middle_ref[rows, :] + part + before_ref[BIAS_DOWN]).astype(LOW)
            hidden_ref[rows, :] = low
        else:
            low = hidden_ref[rows, :]
        unit, _ = normalized(low.astype(jnp.float32))
        normed_ref[rows, :] = (unit * vec_ref[GAIN_ONE] + vec_ref[SHIFT_ONE]).astype(LOW)
    product = dot_rows(normed_ref[...], weight_ref[...])
    out_ref[...] = (product + bias_of(vec_ref, BIAS_PROJ, 0, out_ref.shape[1])).astype(LOW)


def project(before, vec, rows, out_width):
    joins = len(before) > 1
    tokens, width = before[0].shape
    ins = [row_block(width)] * 3 + [whole(vec.shape)] if joins else [row_block(width)]
    outs = [row_block(width)] * (2 if joins else 1)
    low = jax.ShapeDtypeStruct((tokens, width), LOW)
    return pl.pallas_call(
        partial(project_kernel, joins),
        grid=(tokens // ROWS,),
        in_specs=ins + [whole(vec.shape), whole((out_width, width))],
        out_specs=outs + [row_block(out_width)],
        out_shape=[low] * len(outs) + [jax.ShapeDtypeStruct((tokens, out_width), LOW)],
        **params_of(2 * tokens * width * out_width, tokens * width * 16),
    )(*before, vec, rows)


def out_halves(packed_ref, half):
    wide = packed_ref.shape[1] // 2
    return [
        jnp.concatenate([packed_ref[rows, :wide], packed_ref[rows, wide:]], axis=0)
        for rows in (slice(0, half), slice(half, 2 * half))
    ]


def branch_kernel(half, attended_ref, packed_ref, low_ref):
    wide = attended_ref.shape[1]
    for index, weights in enumerate(out_halves(packed_ref, half)):
        cols = slice(index * wide, (index + 1) * wide)
        low_ref[:, cols] = dot_rows(attended_ref[...], weights).astype(LOW)


def branch_out(shares, attended, rows):
    tokens, wide = attended.shape
    width = rows.shape[1]
    return pl.pallas_call(
        partial(branch_kernel, shares.half),
        grid=(tokens // ROWS,),
        in_specs=[row_block(wide), at_block((COLS, width), 3, 0)],
        out_specs=row_block(width),
        out_shape=jax.ShapeDtypeStruct((tokens, width), LOW),
        **params_of(2 * tokens * width * wide, tokens * width * 4),
    )(attended, rows)


def gelu_parts(value):
    below = 1.0 + (0.3275911 * 0.5**0.5) * jnp.abs(value)
    rough = pl.reciprocal(below, approx=True)
    t = rough * (2.0 - below * rough)
    bell = jnp.exp((-0.5 * value) * value)
    poly = 0.5 * 1.061405429
    for coefficient in (-1.453152027, 1.421413741, -0.284496736, 0.254829592):
        poly = poly * t + 0.5 * coefficient
    tail = poly * (t * bell)
    cdf = jnp.where(value > 0, 1.0 - tail, tail)
    return value * cdf, cdf + value * (bell * (0.5 / math.pi) ** 0.5)


def expand_kernel(
    hidden_ref,
    branch_ref,
    recv_ref,
    vec_ref,
    up_ref,
    down_ref,
    middle_ref,
    normed_ref,
    slope_ref,
    active_ref,
    low_ref,
    held,
):
    for rows in strips():
        branch = both(branch_ref, recv_ref, rows) + vec_ref[BIAS_OUT]
        middle = hidden_ref[rows, :].astype(jnp.float32) + branch
        middle_ref[rows, :] = middle
        unit, _ = normalized(middle)
        normed_ref[rows, :] = (unit * vec_ref[GAIN_TWO] + vec_ref[SHIFT_TWO]).astype(LOW)
    for index in range(up_ref.shape[0] // WIDE):
        cols = slice(index * WIDE, (index + 1) * WIDE)
        held[index] = dot_rows(normed_ref[...], up_ref[cols, :])
        bias = bias_of(vec_ref, BIAS_UP, index * WIDE, WIDE)
        for rows in strips():
            active, slope = gelu_parts(held[index, rows, :] + bias)
            active_ref[rows, cols] = active.astype(LOW)
            slope_ref[rows, cols] = slope.astype(LOW)
    low_ref[...] = dot_plain(active_ref[...], down_ref[...]).astype(LOW)


def expand(hidden, branch, recv, vec, rows, down):
    tokens, width = hidden.shape
    inner = down.shape[0]
    return pl.pallas_call(
        expand_kernel,
        grid=(tokens // ROWS,),
        in_specs=[row_block(width)] * 3
        + [whole(vec.shape), at_block((inner, width), 1, 0), whole((inner, width))],
        out_specs=[row_block(width), row_block(width), row_block(inner), row_block(inner)]
        + [row_block(width)],
        out_shape=[
            jax.ShapeDtypeStruct((tokens, width), jnp.float32),
            jax.ShapeDtypeStruct((tokens, width), LOW),
            jax.ShapeDtypeStruct((tokens, inner), LOW),
            jax.ShapeDtypeStruct((tokens, inner), LOW),
            jax.ShapeDtypeStruct((tokens, width), LOW),
        ],
        scratch_shapes=[pltpu.VMEM((inner // WIDE, ROWS, WIDE), jnp.float32)],
        **params_of(4 * tokens * width * inner, tokens * width * 32, tokens * inner),
    )(hidden, branch, recv, vec, rows, down)


def expand_back_kernel(
    grad_ref,
    slope_ref,
    up_ref,
    down_ref,
    low_ref,
    grad_up_ref,
    bias_up_ref,
    bias_down_ref,
    sums_up,
    sums_down,
):
    step = pl.program_id(0)

    @pl.when(step == 0)
    def _():
        sums_up[...] = jnp.zeros_like(sums_up)
        sums_down[...] = jnp.zeros_like(sums_down)

    for index in range(down_ref.shape[0] // WIDE):
        cols = slice(index * WIDE, (index + 1) * WIDE)
        grad_active = dot_rows(grad_ref[...], down_ref[cols, :])
        grad_up_ref[:, cols] = (grad_active * slope_ref[:, cols].astype(jnp.float32)).astype(LOW)
    low_ref[...] = dot_plain(grad_up_ref[...], up_ref[...]).astype(LOW)
    for rows in strips():
        sums_up[...] += eights(grad_up_ref[rows, :].astype(jnp.float32))
        sums_down[...] += eights(grad_ref[rows, :].astype(jnp.float32))

    @pl.when(step == pl.num_programs(0) - 1)
    def _():
        bias_up_ref[...] = jnp.sum(sums_up[...], axis=0, keepdims=True)
        bias_down_ref[...] = jnp.sum(sums_down[...], axis=0, keepdims=True)


def expand_back(grad, slope, rows, down):
    tokens, width = grad.shape
    inner = down.shape[0]
    return pl.pallas_call(
        expand_back_kernel,
        grid=(tokens // ROWS,),
        in_specs=[row_block(width), row_block(inner)]
        + [at_block((inner, width), 1, 0), whole((inner, width))],
        out_specs=[row_block(width), row_block(inner), whole((1, inner)), whole((1, width))],
        out_shape=[
            jax.ShapeDtypeStruct((tokens, width), LOW),
            jax.ShapeDtypeStruct((tokens, inner), LOW),
            jax.ShapeDtypeStruct((1, inner), jnp.float32),
            jax.ShapeDtypeStruct((1, width), jnp.float32),
        ],
        scratch_shapes=[pltpu.VMEM((8, inner), jnp.float32), pltpu.VMEM((8, width), jnp.float32)],
        **params_of(4 * tokens * width * inner, tokens * width * 24),
    )(grad, slope, rows, down)


def token_products_kernel(lefts, rights, outs):
    for left, right, out in zip(lefts, rights, outs):
        out[...] = dot_tokens(left[...], right[...]).astype(LOW)


def hidden_products(active, grad, grad_up, normed):
    tokens, inner = active.shape
    width = grad.shape[1]

    def kernel(a_ref, b_ref, c_ref, d_ref, down_ref, rows_ref):
        token_products_kernel((a_ref, b_ref), (c_ref, d_ref), (down_ref, rows_ref))

    return pl.pallas_call(
        kernel,
        grid=(inner // COLS,),
        in_specs=[col_block(tokens)] * 2 + [whole((tokens, width))] * 2,
        out_specs=[
            pl.BlockSpec((COLS, width), lambda i: (i, 0)),
            pl.BlockSpec((COLS, width), lambda i: (inner // COLS + i, 0)),
        ],
        out_shape=[
            jax.ShapeDtypeStruct((inner, width), LOW),
            jax.ShapeDtypeStruct((2 * inner, width), LOW),
        ],
        **params_of(4 * tokens * width * inner, tokens * width * 16),
    )(active, grad_up, grad, normed)


def project_products(grad_proj, normed, rows_grad):
    tokens, out_width = grad_proj.shape
    width = normed.shape[1]

    def kernel(a_ref, b_ref, _, rows_ref):
        token_products_kernel((a_ref,), (b_ref,), (rows_ref,))

    return pl.pallas_call(
        kernel,
        grid=(out_width // COLS,),
        in_specs=[col_block(tokens), whole((tokens, width)), pl.BlockSpec(memory_space=pl.ANY)],
        out_specs=pl.BlockSpec((COLS, width), lambda i: (i, 0)),
        out_shape=jax.ShapeDtypeStruct(rows_grad.shape, LOW),
        input_output_aliases={2: 0},
        **params_of(2 * tokens * width * out_width, tokens * width * 8),
    )(grad_proj, normed, rows_grad)


def norm_back_rows(values_in, incoming, gain_vec):
    unit, scale = normalized(values_in)
    p = incoming * gain_vec
    mean_p = jnp.mean(p, axis=-1, keepdims=True)
    mean_pn = jnp.mean(p * unit, axis=-1, keepdims=True)
    return scale * (p - mean_p - unit * mean_pn), eights(incoming * unit), eights(incoming)


def branch_back_kernel(
    half,
    middle_ref,
    part_ref,
    recv_ref,
    grad_ref,
    attended_ref,
    vec_ref,
    packed_ref,
    _,
    grad_middle_ref,
    grad_attended_ref,
    out_grad_ref,
    gain_grad_ref,
    shift_grad_ref,
    bias_grad_ref,
    total,
    low,
    sums,
):
    step = pl.program_id(0)

    @pl.when(step == 0)
    def _():
        total[...] = jnp.zeros_like(total)
        sums[...] = jnp.zeros_like(sums)

    for rows in strips():
        incoming = both(part_ref, recv_ref, rows)
        change, for_gain, for_shift = norm_back_rows(
            middle_ref[rows, :], incoming, vec_ref[GAIN_TWO]
        )
        grad_middle = grad_ref[rows, :].astype(jnp.float32) + change
        grad_middle_ref[rows, :] = grad_middle
        rounded = grad_middle.astype(LOW)
        low[rows, :] = rounded
        sums[0] += for_gain
        sums[1] += for_shift
        sums[2] += eights(rounded.astype(jnp.float32))
    weights = out_halves(packed_ref, half)
    wide = weights[0].shape[0]
    attended = attended_ref[...]
    pieces = [low[:, :wide], low[:, wide:]]
    grad_attended_ref[...] = (
        dot_plain(pieces[0], weights[0]) + dot_plain(pieces[1], weights[1])
    ).astype(LOW)
    for index in range(2):
        total[index] += dot_tokens(pieces[index], attended)

    @pl.when(step == pl.num_programs(0) - 1)
    def _():
        for index in range(2):
            joined = jnp.concatenate([total[index, :half, :], total[index, half:, :]], axis=1)
            out_grad_ref[index * half : (index + 1) * half, :] = joined.astype(LOW)
        for index, ref in enumerate((gain_grad_ref, shift_grad_ref, bias_grad_ref)):
            ref[...] = jnp.sum(sums[index], axis=0, keepdims=True)


def branch_back(shares, middle, part, recv, grad, attended, vec, rows, rows_grad):
    tokens, width = middle.shape
    wide = attended.shape[1]
    small = whole((1, width))
    one = jax.ShapeDtypeStruct((1, width), jnp.float32)
    return pl.pallas_call(
        partial(branch_back_kernel, shares.half),
        grid=(tokens // ROWS,),
        in_specs=[row_block(width)] * 4
        + [row_block(wide), whole(vec.shape), at_block((COLS, width), 3, 0)]
        + [pl.BlockSpec(memory_space=pl.ANY)],
        out_specs=[row_block(width), row_block(wide), at_block((COLS, width), 3, 0)]
        + [small, small, small],
        out_shape=[
            jax.ShapeDtypeStruct((tokens, width), jnp.float32),
            jax.ShapeDtypeStruct((tokens, wide), LOW),
            jax.ShapeDtypeStruct(rows_grad.shape, LOW),
            one,
            one,
            one,
        ],
        input_output_aliases={7: 2},
        scratch_shapes=[
            pltpu.VMEM((2, width // 2, wide), jnp.float32),
            pltpu.VMEM((ROWS, width), LOW),
            pltpu.VMEM((3, 8, width), jnp.float32),
        ],
        **params_of(4 * tokens * width * wide, tokens * width * 20),
    )(middle, part, recv, grad, attended, vec, rows, rows_grad)


def project_back_kernel(grad_ref, weight_ref, low_ref, bias_ref, sums):
    step = pl.program_id(0)

    @pl.when(step == 0)
    def _():
        sums[...] = jnp.zeros_like(sums)

    low_ref[...] = dot_plain(grad_ref[...], weight_ref[...]).astype(LOW)
    for rows in strips():
        sums[...] += eights(grad_ref[rows, :].astype(jnp.float32))

    @pl.when(step == pl.num_programs(0) - 1)
    def _():
        bias_ref[...] = jnp.sum(sums[...], axis=0, keepdims=True)


def project_back(grad_proj, rows):
    tokens, out_width = grad_proj.shape
    width = rows.shape[1]
    return pl.pallas_call(
        project_back_kernel,
        grid=(tokens // ROWS,),
        in_specs=[row_block(out_width), whole((out_width, width))],
        out_specs=[row_block(width), whole((1, out_width))],
        out_shape=[
            jax.ShapeDtypeStruct((tokens, width), LOW),
            jax.ShapeDtypeStruct((1, out_width), jnp.float32),
        ],
        scratch_shapes=[pltpu.VMEM((8, out_width), jnp.float32)],
        **params_of(2 * tokens * width * out_width, tokens * width * 12),
    )(grad_proj, rows)


def input_back_kernel(
    hidden_ref, part_ref, recv_ref, grad_ref, vec_ref, out_ref, gain_grad_ref, shift_grad_ref, sums
):
    step = pl.program_id(0)

    @pl.when(step == 0)
    def _():
        sums[...] = jnp.zeros_like(sums)

    for rows in strips():
        incoming = both(part_ref, recv_ref, rows)
        hidden = hidden_ref[rows, :].astype(jnp.float32)
        change, for_gain, for_shift = norm_back_rows(hidden, incoming, vec_ref[GAIN_ONE])
        out_ref[rows, :] = (grad_ref[rows, :] + change).astype(LOW)
        sums[0] += for_gain
        sums[1] += for_shift

    @pl.when(step == pl.num_programs(0) - 1)
    def _():
        gain_grad_ref[...] = jnp.sum(sums[0], axis=0, keepdims=True)
        shift_grad_ref[...] = jnp.sum(sums[1], axis=0, keepdims=True)


def input_back(hidden, part, recv, grad_middle, vec):
    tokens, width = hidden.shape
    small = whole((1, width))
    one = jax.ShapeDtypeStruct((1, width), jnp.float32)
    return pl.pallas_call(
        input_back_kernel,
        grid=(tokens // ROWS,),
        in_specs=[row_block(width)] * 4 + [whole(vec.shape)],
        out_specs=[row_block(width), small, small],
        out_shape=[jax.ShapeDtypeStruct((tokens, width), LOW), one, one],
        scratch_shapes=[pltpu.VMEM((2, 8, width), jnp.float32)],
        **params_of(0, tokens * width * 12),
    )(hidden, part, recv, grad_middle, vec)


def attend_kernel(q_ref, k_ref, v_ref, qa_ref, kt_ref, out_ref, lse_ref, keys, held, low):
    tokens, pair = q_ref.shape
    left = lax.broadcasted_iota(jnp.int32, (CHUNK, pair), 1) < pair // 2
    keys[:pair, :] = jnp.transpose(k_ref[...].astype(jnp.float32)).astype(LOW)
    keys[pair:, :] = kt_ref[...]
    for index in range(tokens // CHUNK):
        rows = slice(index * CHUNK, (index + 1) * CHUNK)
        queries = q_ref[rows, :] * 0.125
        outs, tops = [], []
        for head in range(2):
            slot = (2 * index + head) % held.shape[0]
            mine = left if head == 0 else jnp.logical_not(left)
            side = jnp.where(mine, queries, jnp.zeros_like(queries))
            lhs = jnp.concatenate([side, qa_ref[head, rows, :]], axis=1)
            held[slot] = dot_plain(lhs, keys[...])
            levels, shares = [], []
            for strip in strips(CHUNK):
                scores = held[slot, strip, :]
                top = jnp.max(scores, axis=1, keepdims=True)
                weight = jnp.exp(scores - top)
                total = jnp.sum(weight, axis=1, keepdims=True)
                low[slot, strip, :] = weight.astype(LOW)
                levels.append(top + jnp.log(total))
                shares.append(1.0 / total)
            product = dot_plain(low[slot], v_ref[...])
            outs.append(product * jnp.concatenate(shares, axis=0))
            tops.append(jnp.concatenate(levels, axis=0))
        out_ref[rows, :] = jnp.where(left, outs[0], outs[1]).astype(LOW)
        lse_ref[rows, :] = jnp.where(left, tops[0], tops[1])


def attend(projected, query_side, key_side, turned):
    tokens = projected.shape[0]
    width = projected.shape[1] // 3
    pairs = width // 128
    features = key_side.shape[1]
    return pl.pallas_call(
        attend_kernel,
        grid=(pairs,),
        in_specs=[
            pl.BlockSpec((tokens, 128), lambda p: (0, p)),
            pl.BlockSpec((tokens, 128), lambda p: (0, pairs + p)),
            pl.BlockSpec((tokens, 128), lambda p: (0, 2 * pairs + p)),
            pl.BlockSpec((2, tokens, features), lambda p: (p, 0, 0)),
            whole((features, tokens)),
        ],
        out_specs=[
            pl.BlockSpec((tokens, 128), lambda p: (0, p)),
            pl.BlockSpec((tokens, 128), lambda p: (0, p)),
        ],
        out_shape=[
            jax.ShapeDtypeStruct((tokens, width), LOW),
            jax.ShapeDtypeStruct((tokens, width), jnp.float32),
        ],
        scratch_shapes=[
            pltpu.VMEM((128 + features, tokens), LOW),
            pltpu.VMEM((4, CHUNK, tokens), jnp.float32),
            pltpu.VMEM((4, CHUNK, tokens), LOW),
        ],
        **params_of(
            16 * pairs * tokens * tokens * 128, tokens * width * 16, 2 * pairs * tokens * tokens
        ),
    )(projected, projected, projected, query_side, turned)


def three_terms(values):
    high = values.astype(LOW).astype(jnp.float32)
    rest = values - high
    middle = rest.astype(LOW).astype(jnp.float32)
    return high, middle, rest - middle


def attend_back_kernel(
    q_ref,
    k_ref,
    v_ref,
    do_ref,
    o_ref,
    lse_ref,
    qa_ref,
    ka_ref,
    grad_ref,
    held,
    probs,
    changes,
    query_sides,
    grad_sides,
):
    tokens, pair = q_ref.shape
    features = ka_ref.shape[1]
    pairs = pl.num_programs(0)
    place = pl.program_id(0)
    first = 2 * (tokens // BLOCK) + 3
    half = pair // 2
    left = lax.broadcasted_iota(jnp.int32, (CHUNK, pair), 1) < half
    lane = lax.broadcasted_iota(jnp.int32, (CHUNK, features), 1)
    lane_pair = lax.broadcasted_iota(jnp.int32, (CHUNK, pair), 1)
    keys = jnp.concatenate([k_ref[...], ka_ref[...]], axis=1)
    turned = jnp.transpose(k_ref[...].astype(jnp.float32)).astype(LOW)
    ones = (lax.broadcasted_iota(jnp.int32, (tokens, pair), 1) < 3).astype(jnp.float32).astype(LOW)
    values = jnp.concatenate([v_ref[...], ones], axis=1)
    parts, key_grads, value_grads = [], [], []
    for head in range(2):
        mine = left if head == 0 else jnp.logical_not(left)
        for index in range(tokens // CHUNK):
            rows = slice(index * CHUNK, (index + 1) * CHUNK)
            slot = index % 2
            queries = q_ref[rows, :] * 0.125
            grads = do_ref[rows, :]
            product = grads.astype(jnp.float32) * o_ref[rows, :].astype(jnp.float32)
            level = lse_ref[rows, head * half : head * half + 1]
            inner = jnp.sum(jnp.where(mine, product, 0.0), axis=1, keepdims=True)
            side = qa_ref[head, rows, :].astype(jnp.float32)
            for spot, term in enumerate(three_terms(level)):
                side = jnp.where(lane == first + spot, -term, side)
            query_side = jnp.where(mine, queries, jnp.zeros_like(queries))
            grad_side = jnp.where(mine, grads, jnp.zeros_like(grads))
            query_sides[head, rows, :] = query_side
            grad_sides[head, rows, :] = grad_side
            tail = jnp.zeros((CHUNK, pair), jnp.float32)
            for spot, term in enumerate(three_terms(inner)):
                tail = jnp.where(lane_pair == spot, -term, tail)
            held[slot, 0] = dot_rows(
                keys, jnp.concatenate([query_side, side.astype(LOW)], axis=1)
            )
            held[slot, 1] = dot_rows(
                values, jnp.concatenate([grad_side, tail.astype(LOW)], axis=1)
            )
            for strip in strips(tokens, 128):
                prob = jnp.exp(held[slot, 0, strip, :])
                probs[head, strip, rows] = prob.astype(LOW)
                changes[head, strip, rows] = (prob * held[slot, 1, strip, :]).astype(LOW)
        value_grads.append(dot_plain(probs[head], grad_sides[head]))
        key_grads.append(dot_plain(changes[head], query_sides[head]))
        parts.append(dot_plain(turned, changes[head]))
    joined = jnp.concatenate([parts[0][:half], parts[1][half:]], axis=0)
    column = [pl.ds(pl.multiple_of((by * pairs + place) * 128, 128), 128) for by in range(3)]
    grad_ref[:, column[0]] = (jnp.transpose(joined) * 0.125).astype(LOW)
    grad_ref[:, column[1]] = (key_grads[0] + key_grads[1]).astype(LOW)
    grad_ref[:, column[2]] = (value_grads[0] + value_grads[1]).astype(LOW)


def attend_back(projected, grad_attended, attended, levels, query_side, key_side):
    tokens, width = attended.shape
    pairs = width // 128
    features = key_side.shape[1]
    by_pair = pl.BlockSpec((tokens, 128), lambda p: (0, p))
    return pl.pallas_call(
        attend_back_kernel,
        grid=(pairs,),
        in_specs=[
            by_pair,
            pl.BlockSpec((tokens, 128), lambda p: (0, pairs + p)),
            pl.BlockSpec((tokens, 128), lambda p: (0, 2 * pairs + p)),
            by_pair,
            by_pair,
            by_pair,
            pl.BlockSpec((2, tokens, features), lambda p: (p, 0, 0)),
            whole((tokens, features)),
        ],
        out_specs=whole((tokens, 3 * width)),
        out_shape=jax.ShapeDtypeStruct((tokens, 3 * width), LOW),
        scratch_shapes=[
            pltpu.VMEM((2, 2, tokens, CHUNK), jnp.float32),
            pltpu.VMEM((2, tokens, tokens), LOW),
            pltpu.VMEM((2, tokens, tokens), LOW),
            pltpu.VMEM((2, tokens, 128), LOW),
            pltpu.VMEM((2, tokens, 128), LOW),
        ],
        **params_of(
            40 * pairs * tokens * tokens * 128, tokens * width * 24, 2 * pairs * tokens * tokens
        ),
    )(projected, projected, projected, grad_attended, attended, levels, query_side, key_side)


def window_forward(shares, before, weights, vec, features, beside):
    rows, down = weights
    results = project(before, vec, rows, 6 * shares.half)
    hidden = before[0] if len(before) == 1 else results[0]
    normed, projected = results[-2:]
    projected = beside.tie(projected)
    attended, levels = beside.tie(tuple(attend(projected, *features)))
    low = branch_out(shares, attended, rows)
    expanded = expand(hidden, low, swap(low), vec, rows, down)
    middle, normed_two, slope, active, low = beside.tie(tuple(expanded))
    stored = (hidden, normed, projected, attended, levels, middle, normed_two, slope, active)
    return (middle, low, swap(low), vec), stored


def window_backward(shares, stored, grad, weights, vec, features, beside):
    hidden, normed, projected, attended, levels, middle, normed_two, slope, active = stored
    rows, down = weights
    low, grad_up, bias_up, bias_down = beside.tie(tuple(expand_back(grad, slope, rows, down)))
    arrived = swap(low)
    down_grad, rows_grad = hidden_products(active, grad, grad_up, normed_two)
    grad_middle, grad_attended, rows_grad, gain_two, shift_two, bias_out = branch_back(
        shares, middle, low, arrived, grad, attended, vec, rows, rows_grad
    )
    grad_attended = beside.tie(grad_attended)
    grad_proj = attend_back(projected, grad_attended, attended, levels, *features[:2])
    grad_proj = beside.tie(grad_proj)
    low, summed = project_back(grad_proj, rows)
    arrived = swap(low)
    rows_grad = project_products(grad_proj, normed, rows_grad)
    grad, gain_one, shift_one = input_back(hidden, low, arrived, grad_middle, vec)
    width = attended.shape[1]
    vector_grads = (gain_one, shift_one, summed[:, :width], summed[:, 2 * width :], bias_out)
    vector_grads += (gain_two, shift_two, bias_down, bias_up)
    vector_grads = [piece[0] for piece in vector_grads]
    return grad, (rows_grad, down_grad), vector_grads


def window_shards(
    block_input,
    cotangent,
    random_ids,
    segment_ids,
    global_ids,
    w_rows,
    w_rows_first,
    w_rows_second,
    w_down,
    w_down_first,
    w_down_second,
    vectors,
    vectors_first,
    vectors_second,
):
    core = lax.axis_index(SECTION)
    micro, _, tokens, width = block_input.shape
    _, _, columns = w_rows.shape
    shares = Shares(width, columns, w_down.shape[1], vectors.shape[1])
    prepared = prepare(shares, w_rows[0], w_down[0], vectors)
    features = key_features(shares, random_ids, segment_ids, global_ids)
    gathered_zero, gathered_one, hidden, grad = gather(shares, prepared, block_input, cotangent)

    beside = Beside(spread_quads(shares, gathered_one[:2]))
    params = [shares.unpack(gathered_zero, core)]
    before = (hidden.reshape(-1, width),)
    before, stored_zero = window_forward(shares, before, *params[0], features, beside)
    params.append(shares.unpack((*beside.flying, gathered_one[2]), core))
    after, stored_one = window_forward(shares, before, *params[1], features, Beside())
    final = after[1].astype(jnp.float32) + after[2].astype(jnp.float32)
    final = (after[0] + final + after[3][BIAS_DOWN]).astype(LOW)

    grad = grad.reshape(-1, width)
    grad, *grads_one = window_backward(shares, stored_one, grad, *params[1], features, Beside())
    *arrays_one, vec_one = shares.by_shard(*grads_one, core)
    beside = Beside(sum_quads(shares, arrays_one))
    grad, *grads_zero = window_backward(shares, stored_zero, grad, *params[0], features, beside)
    *arrays_zero, vec_zero = shares.by_shard(*grads_zero, core)
    grad, final = [piece.reshape(micro, tokens, width) for piece in (grad, final)]
    halves, slices = scatter(shares, arrays_zero, vec_zero, beside.flying, vec_one, grad, final)
    old = [
        w_rows[0],
        w_rows_first[0],
        w_rows_second[0],
        w_down[0],
        w_down_first[0],
        w_down_second[0],
        vectors,
        vectors_first,
        vectors_second,
    ]
    *new, result = update(shares, halves, slices, old)
    return (result[None, :, None], *[piece[None] for piece in new[:6]], *new[6:])


def one_window_each(mesh, block_input, w_rows, w_down, vectors):
    micro, windows, length, width = block_input.shape
    shards = mesh.shape[DP] * mesh.shape[SEQ]
    columns, depth = w_rows.shape[2] // shards, w_down.shape[1] // shards
    head_dim = width // HEADS
    tokens = length // mesh.shape[SEQ]
    return (
        mesh.shape[SECTION] == 2
        and mesh.shape[SEQ] == micro
        and mesh.shape[DP] == windows
        and tokens % (2 * BLOCK) == 0
        and length % CHUNK == 0
        and head_dim == 64
        and width % columns == 0
        and columns % (2 * head_dim) == 0
        and columns % depth == 0
        and width // columns * (columns // 2) % 128 == 0
        and depth % 32 == 0
        and vectors.shape[1] // shards <= width
        and mesh.shape[DP] == 4
        and micro == 4
        and width == 2 * columns == 2 * COLS
        and w_down.shape[1] == 4 * width
        and (columns // 2) % (2 * PIECE) == 0
        and (depth // 2) % (2 * PIECE) == 0
        and length % (4 * ROWS) == 0
    )


def solution(mesh):
    in_specs = (
        P(None, DP, SEQ, None),
        P(None, DP, SEQ, None),
        P(None, DP, None, None, None),
        P(None, DP, None),
        P(None, DP, None),
        P(SECTION, None, (DP, SEQ)),
        P(SECTION, None, (DP, SEQ)),
        P(SECTION, None, (DP, SEQ)),
        P(SECTION, (DP, SEQ), None),
        P(SECTION, (DP, SEQ), None),
        P(SECTION, (DP, SEQ), None),
        P(SECTION, (DP, SEQ)),
        P(SECTION, (DP, SEQ)),
        P(SECTION, (DP, SEQ)),
    )
    out_specs = (
        P(SECTION, None, DP, SEQ, None),
        P(SECTION, None, (DP, SEQ)),
        P(SECTION, None, (DP, SEQ)),
        P(SECTION, None, (DP, SEQ)),
        P(SECTION, (DP, SEQ), None),
        P(SECTION, (DP, SEQ), None),
        P(SECTION, (DP, SEQ), None),
        P(SECTION, (DP, SEQ)),
        P(SECTION, (DP, SEQ)),
        P(SECTION, (DP, SEQ)),
    )

    def step(*arrays):
        chosen = general_shards
        if one_window_each(mesh, arrays[0], arrays[5], arrays[8], arrays[11]):
            chosen = window_shards
        return jax.shard_map(
            chosen, mesh=mesh, in_specs=in_specs, out_specs=out_specs, check_vma=False
        )(*arrays)

    return step
```
